32 devices in a mesh: ep: 4 (over z), dp: 8 (over y, x, core).
Axes of the slice: x: 2, y: 2, z: 4, core: 2. Of those that a mesh axis runs over, the one named last changes fastest.
Arguments:
- tokens: bfloat16 [2, 4096, 1024], P(None, ('ep', 'dp')), may hold values from -6 to 6
- segments: int32 [2, 4, 1024], P(None, 'ep', 'dp'), may hold values from 0 to 3, never falling along the last dimension, each value on 1 to 512 neighbouring positions
- routes: int32 [2, 4096, 8], P(None, ('ep', 'dp')), may hold values from 0 to 31, all different within a row; in each aligned block of 128 rows (0 to 127, 128 to 255, ..., all dimensions but the last counted through in order) at most 64 rows name the same one
- first_gain: float32 [1024], replicated, may hold values from 0.1 to 1.9
- w_query: bfloat16 [1024, 1024], replicated, may hold values from -0.1875 to 0.1875
- w_key: bfloat16 [1024, 512], replicated, may hold values from -0.1875 to 0.1875
- w_value: bfloat16 [1024, 512], replicated, may hold values from -0.1875 to 0.1875
- w_out: bfloat16 [1024, 1024], replicated, may hold values from -3 to 3
- second_gain: float32 [1024], replicated, may hold values from 0.1 to 1.9
- w_router: bfloat16 [1024, 32], replicated, may hold values from -0.09375 to 0.09375
- w_gate: bfloat16 [32, 1024, 512], P('ep'), may hold values from -0.1875 to 0.1875
- w_up: bfloat16 [32, 1024, 512], P('ep'), may hold values from -0.1875 to 0.1875
- w_down: bfloat16 [32, 512, 1024], P('ep'), may hold values from -0.75 to 0.75
- cotangent: bfloat16 [2, 4096, 1024], P(None, ('ep', 'dp')), may hold values from -6 to 6
Outputs:
- output: bfloat16 [2, 4096, 1024], P(None, ('ep', 'dp'))
- grad_tokens: float32 [2, 4096, 1024], P(None, ('ep', 'dp'))
- grad_first_gain: float32 [1024], P(('ep', 'dp'))
- grad_w_query: float32 [1024, 1024], P(('ep', 'dp'))
- grad_w_key: float32 [1024, 512], P(('ep', 'dp'))
- grad_w_value: float32 [1024, 512], P(('ep', 'dp'))
- grad_w_out: float32 [1024, 1024], P(('ep', 'dp'))
- grad_second_gain: float32 [1024], P(('ep', 'dp'))
- grad_w_router: float32 [1024, 32], P(('ep', 'dp'))
- grad_w_gate: float32 [32, 1024, 512], P('ep', 'dp')
- grad_w_up: float32 [32, 1024, 512], P('ep', 'dp')
- grad_w_down: float32 [32, 512, 1024], P('ep', 'dp')
The draws below stay inside these ranges and needn't reach their ends.
Inputs may be any that keep to these rules, and one draw needn't show every extreme that they name: `routes`: the 8 experts of a token are distinct. In the 128 token rows that one device holds in one micro-batch (aligned blocks), no expert is named more than 64 times, and in some blocks one expert is named exactly 64 times. `segments`: along each sequence the ids never fall; every id from 0 to 3 labels a run of consecutive tokens, the longest run being half of the sequence's 1024 tokens.
All inputs are finite; a program needn't handle non-finite values.
Results may differ from the reference program's by a relative error of at most 0.015.
The reference program's roundings to bfloat16 on the way count: a program that leaves them out, or rounds other values in their place, can miss the bound.
Values may be sent and summed in bfloat16 or wider, within the bound.
A program may use at most 256 MiB of HBM per device.

```python
import math
import jax
import jax.numpy as jnp
import numpy as np
from jax import lax

D = 1024
HEADS = 16
KV_HEADS = 8
HEAD_DIM = 64
FFE = 512
EXPERTS = 32
TOP = 8
MICRO = 2
MB_TOK = 128
LEN = 1024
SEQS = 4
TOKENS_MB = 4096
CAP = 64


def spiked(values, key, source, target, parts, factor):
    def block_of(position):
        return (jnp.arange(values.shape[position]) // (values.shape[position] // parts)).reshape((-1,) + (1,) * (values.ndim - 1 - position))

    first = jax.random.permutation(key, parts)[block_of(target)]
    second = (block_of(target) + parts // 2) % parts
    return jnp.where((block_of(source) == first) | (block_of(source) == second), factor * values, values)


def levels(own_key, dims, shards, low, largest):
    factor_of, own = 1.0, jax.random.fold_in(own_key, 6)
    for position, shards_of in shards:
        steps = jnp.exp(jax.random.uniform(jax.random.fold_in(own, position), (shards_of,), jnp.float32, low / len(shards), largest / len(shards)))
        factor_of = factor_of * jnp.repeat(steps, dims[position] // shards_of).reshape([-1 if axis == position else 1 for axis in range(len(dims))])
    return factor_of


def split_up(number_of, total, limit, skew):
    loads = [(1 << 20) // math.isqrt(standing ** skew) + 1 for standing in range(2, number_of + 1)]
    spare, counts = total - limit - (number_of - 1), [1] * (number_of - 1)
    while spare > 0:
        candidates = [i for i in range(number_of - 1) if counts[i] < limit]
        pool, left = sum([loads[i] for i in candidates]), spare
        for i in candidates:
            extra = min(limit - counts[i], max(1, left * loads[i] // pool), spare)
            counts[i] = counts[i] + extra
            spare = spare - extra
    return np.array([limit] + counts)


def uneven(stream_key, amount, total, reach, lean):
    if amount == 2:
        one = jax.random.randint(stream_key, (), max(1, total - reach), min(reach, total - 1) + 1)
        return jnp.stack([one, total - one])
    sizes = jnp.asarray(split_up(amount, total, reach, lean), jnp.int32)
    twos = (amount - 1) // 2
    source_of, sink = sizes[1:1 + 2 * twos:2], sizes[2:2 + 2 * twos:2]
    slack = jnp.minimum(source_of - 1, reach - sink)
    passed = jax.random.randint(jax.random.fold_in(stream_key, 1), (twos,), 0, 1 << 20) % (slack + 1)
    sizes = sizes.at[1:1 + 2 * twos:2].set(source_of - passed).at[2:2 + 2 * twos:2].set(sink + passed)
    return sizes[jax.random.permutation(jax.random.fold_in(stream_key, 2), amount)]


def routed_block(rng, own, number, rows, amount, top, reach, slope):
    order = jax.random.permutation(rng, amount)
    heavy_load, ordinary = portions_of(amount, rows * top, reach, slope, True), portions_of(amount, rows * top, reach, slope, False)
    places = jnp.arange(amount)

    def named(sizes, offset_by):
        used = int((sizes > 0).sum())
        fixed = max(1, used // 4)
        moved = fixed + (places - fixed + offset_by * (used - fixed)) % max(1, amount - fixed)
        return jnp.zeros((amount,), jnp.int32).at[order[jnp.where(places < fixed, places, moved)]].set(jnp.asarray(sizes, jnp.int32))

    sizes = jnp.where(number % 4 == 0, named(heavy_load, number // 4), named(ordinary, number - number // 4 - 1))
    mixed = jax.random.permutation(jax.random.fold_in(own, 3), amount)
    giver, receiver = mixed[0:amount // 2 * 2:2], mixed[1:amount // 2 * 2:2]
    margin = jnp.minimum(sizes[giver] - 1, reach - sizes[receiver]) // 2
    margin = jnp.where((giver == order[0]) | (receiver == order[0]) | (sizes[receiver] == 0), 0, jnp.maximum(margin, 0))
    moved = jax.random.randint(jax.random.fold_in(own, 4), (amount // 2,), 0, 1 << 20) % (margin + 1)
    sizes = sizes.at[giver].add(-moved).at[receiver].add(moved)
    labels = jnp.searchsorted(jnp.cumsum(sizes), jnp.arange(rows * top), side="right").astype(jnp.int32)
    listing = labels.reshape(top, rows).T
    listing = listing[jax.random.permutation(jax.random.fold_in(own, 1), rows)]
    offset_by = jax.random.randint(jax.random.fold_in(own, 2), (rows, 1), 0, top)
    return jnp.take_along_axis(listing, (jnp.arange(top)[None, :] + offset_by) % top, axis=1)


def portions_of(amount, total, reach, lean, full):
    loads = [(1 << 20) // math.isqrt(grade ** lean) + 1 for grade in range(1, amount + 1)]
    largest = reach if full else min(reach, max(-(-total // amount), total * loads[0] // sum(loads)))
    least = 1 if total - largest >= amount - 1 else 0
    given, rest = [largest] + [least] * (amount - 1), total - largest - least * (amount - 1)
    while rest > 0:
        free = [i for i in range(1, amount) if given[i] < largest] or [i for i in range(1, amount) if given[i] < reach]
        whole, left = sum([loads[i] for i in free]), rest
        for i in free:
            extra = min(reach - given[i], max(1, left * loads[i] // whole), rest)
            given[i] = given[i] + extra
            rest = rest - extra
    return np.array(given)


def centred(rng, extent, scale, reach, pieces=(), kind=jnp.bfloat16):
    values = jax.random.normal(rng, extent, jnp.float32) * scale
    if len(pieces) > 0:
        values = levels(rng, extent, pieces, -0.22, 0.18) * values
    return jnp.clip(values, min=-reach, max=reach).astype(kind)


def gaussian_with(stream_key, extent, deviation, limit, pieces, heavy, kind=jnp.bfloat16):
    entries = deviation * jax.random.normal(stream_key, extent, jnp.float32)
    if pieces:
        entries = entries * levels(stream_key, extent, pieces, -0.22, 0.18)
    return jnp.clip(spiked(entries, jax.random.fold_in(stream_key, 3), *heavy), -limit, limit).astype(kind)


def setup_inputs(seed: int = 0) -> dict:
    key_of = jax.random.split(jax.random.key(seed), 15)
    tokens = centred(key_of[0], (MICRO, TOKENS_MB, D), 1.0, 6.0, ((1, 32),))
    segments = jax.vmap(lambda own: jnp.searchsorted(jnp.cumsum(uneven(own, 4, LEN, LEN // 2, 2)), jnp.arange(LEN), side="right"))(jax.random.split(key_of[1], MICRO * SEQS)).reshape((MICRO, SEQS, LEN)).astype(jnp.int32)
    routes_keys = jax.random.split(jax.random.fold_in(key_of[2], 1), MICRO * TOKENS_MB // MB_TOK)
    routes_turns = jax.random.permutation(jax.random.fold_in(key_of[2], 3), MICRO * TOKENS_MB // MB_TOK)
    routes = jax.vmap(lambda own, number: routed_block(jax.random.fold_in(key_of[2], 2), own, number, MB_TOK, EXPERTS, TOP, CAP, 2))(routes_keys, routes_turns).reshape((MICRO, TOKENS_MB, TOP))
    first_gain = jnp.clip(1.0 + 0.18 * jax.random.normal(key_of[3], (D,), jnp.float32), 0.1, 1.9)
    w_query = centred(key_of[4], (D, HEADS * HEAD_DIM), D ** -0.5, 0.1875)
    w_key = centred(key_of[5], (D, KV_HEADS * HEAD_DIM), D ** -0.5, 0.1875)
    w_value = centred(key_of[6], (D, KV_HEADS * HEAD_DIM), D ** -0.5, 0.1875)
    w_out = centred(key_of[7], (HEADS * HEAD_DIM, D), 4 ** -0.5, 3.0)
    second_gain = jnp.clip(1.0 + 0.18 * jax.random.normal(key_of[8], (D,), jnp.float32), 0.1, 1.9)
    w_router = centred(key_of[9], (D, EXPERTS), (4 * D) ** -0.5, 0.09375)
    w_gate = centred(key_of[10], (EXPERTS, D, FFE), D ** -0.5, 0.1875, ((0, 4),))
    w_up = centred(key_of[11], (EXPERTS, D, FFE), D ** -0.5, 0.1875, ((0, 4),))
    w_down = centred(key_of[12], (EXPERTS, FFE, D), (FFE // 8) ** -0.5, 0.75, ((0, 4),))
    cotangent = gaussian_with(key_of[13], (MICRO, TOKENS_MB, D), 1.0, 6.0, ((1, 32),), (1, 2, 32, 2.75))
    return dict(tokens=tokens, segments=segments, routes=routes, first_gain=first_gain, w_query=w_query, w_key=w_key, w_value=w_value, w_out=w_out, second_gain=second_gain, w_router=w_router, w_gate=w_gate, w_up=w_up, w_down=w_down, cotangent=cotangent)


@jax.custom_vjp
def low(v):
    return lax.optimization_barrier(v.astype(jnp.bfloat16)).astype(jnp.float32)

@jax.custom_vjp
def low_back(v):
    return v

def low_keep(v):
    return (low(v), None)

def low_pass(kept, grad):
    return (grad,)

def back_keep(v):
    return (v, None)

def back_low(kept, grad):
    return (low(grad),)
low.defvjp(low_keep, low_pass)
low_back.defvjp(back_keep, back_low)
EPSILON = 1e-06
ROPE_BASE = 10000.0
MASKED = -1e+30
HIGHEST = lax.Precision.HIGHEST

def rms_norm(values, gain):
    return values * lax.rsqrt(lax.optimization_barrier(jnp.mean(values * values, axis=-1, keepdims=True)) + EPSILON) * gain

def rope_tables(positions, head_size):
    halfway = head_size // 2
    frequency = ROPE_BASE ** (-(jnp.arange(halfway, dtype=jnp.float32) * 2.0 / head_size))
    angles = positions.astype(jnp.float32)[:, None] * frequency[None, :]
    return (jnp.cos(angles), jnp.sin(angles))

def rotate(values, cosine, sine_table):
    halfway = values.shape[-1] // 2
    first_part = values[..., :halfway]
    second_part = values[..., halfway:]
    cosine_wide = cosine[:, None, :]
    sine_wide = sine_table[:, None, :]
    return jnp.concatenate([first_part * cosine_wide - second_part * sine_wide, second_part * cosine_wide + first_part * sine_wide], axis=-1)

def positions_of(seg_ids):
    length = seg_ids.shape[-1]
    starts = jax.vmap(lambda seg_row: jnp.searchsorted(seg_row, seg_row, side='left'))(seg_ids).astype(jnp.int32)
    return (jnp.arange(length, dtype=jnp.int32)[None, :] - starts).reshape(-1).astype(jnp.int32)

def slot_tables(routing):
    token_count = routing.shape[0]
    sources = token_count // MB_TOK
    flat_expert = routing.reshape(sources, MB_TOK * TOP)
    hit_table = (flat_expert[:, :, None] == jnp.arange(EXPERTS, dtype=jnp.int32)[None, None, :]).astype(jnp.int32)
    slot_rank = lax.optimization_barrier(jnp.sum((jnp.cumsum(hit_table, axis=1) - hit_table) * hit_table, axis=2)).astype(jnp.int32)
    source_ids = jnp.broadcast_to(jnp.arange(sources, dtype=jnp.int32)[:, None], slot_rank.shape)
    pair_ids = jnp.arange(token_count * TOP, dtype=jnp.int32).reshape(sources, MB_TOK * TOP)
    empty_table = jnp.full((EXPERTS, sources, CAP), -1, jnp.int32)
    tok_table = empty_table.at[flat_expert, source_ids, slot_rank].set(pair_ids // TOP, mode='drop')
    pair_table = empty_table.at[flat_expert, source_ids, slot_rank].set(pair_ids, mode='drop')
    return (tok_table.reshape(EXPERTS, sources * CAP), pair_table.reshape(EXPERTS, sources * CAP))

def attend_sequence(queries, key_rows, value_rows, seg_ids):
    length = seg_ids.shape[0]
    block_size = min(512, length)
    score_scale = queries.shape[-1] ** (-0.5)
    key_pos = jnp.arange(length, dtype=jnp.int32)

    def one_block(block_start):
        query_block = lax.dynamic_slice_in_dim(queries, block_start, block_size, 0)
        query_pos = block_start + jnp.arange(block_size, dtype=jnp.int32)
        query_seg = lax.dynamic_slice_in_dim(seg_ids, block_start, block_size, 0)
        scores = jnp.einsum('qkgd,nkd->kgqn', query_block, key_rows, precision=HIGHEST) * score_scale
        scores = low_back(scores)
        allowed = (key_pos[None, :] <= query_pos[:, None]) & (seg_ids[None, :] == query_seg[:, None])
        scores = jnp.where(allowed[None, None], scores, MASKED)
        weights = low(jax.nn.softmax(scores, axis=-1))
        return jnp.einsum('kgqn,nkd->qkgd', weights, value_rows, precision=HIGHEST)
    starts = (jnp.arange(length // block_size, dtype=jnp.int32) * block_size).astype(jnp.int32)
    blocks = lax.map(jax.checkpoint(one_block), starts)
    return blocks.reshape(queries.shape)

def layer(inputs, cosine, sine_table, seg_ids, routing, tok_table, pair_table, params):
    first_gain, w_query, w_key, w_value, w_out, second_gain, w_router, w_gate, w_up, w_down = params
    token_count = inputs.shape[0]
    seq_count = seg_ids.shape[0]
    length = seg_ids.shape[1]
    groups = HEADS // KV_HEADS
    normed_one = low(rms_norm(inputs, first_gain))
    query_pre = low_back(jnp.dot(normed_one, w_query, precision=HIGHEST)).reshape(token_count, HEADS, HEAD_DIM)
    queries = low(rotate(query_pre, cosine, sine_table))
    key_pre = low_back(jnp.dot(normed_one, w_key, precision=HIGHEST)).reshape(token_count, KV_HEADS, HEAD_DIM)
    key_rows = low(rotate(key_pre, cosine, sine_table))
    value_rows = low(low_back(jnp.dot(normed_one, w_value, precision=HIGHEST))).reshape(token_count, KV_HEADS, HEAD_DIM)
    attended = lax.map(lambda members: attend_sequence(members[0], members[1], members[2], members[3]), (queries.reshape(seq_count, length, KV_HEADS, groups, HEAD_DIM), key_rows.reshape(seq_count, length, KV_HEADS, HEAD_DIM), value_rows.reshape(seq_count, length, KV_HEADS, HEAD_DIM), seg_ids))
    attn_low = low(low_back(attended.reshape(token_count, HEADS * HEAD_DIM)))
    residual = inputs + low_back(jnp.dot(attn_low, w_out, precision=HIGHEST))
    normed_two = low(rms_norm(residual, second_gain))
    logits = jnp.dot(normed_two, w_router, precision=HIGHEST)
    chosen = jnp.take_along_axis(logits, routing, axis=1)
    gate_probs = jax.nn.softmax(chosen, axis=-1)
    flat_probs = gate_probs.reshape(-1)

    def one_expert(expert_mix, members):
        tok_ids, pair_ids, gate_weight, up_weight, down_weight = members
        is_kept = tok_ids >= 0
        safe_ids = jnp.maximum(tok_ids, 0)
        rows_in = low_back(jnp.where(is_kept[:, None], normed_two[safe_ids], 0.0))
        gate_pre = low_back(jnp.dot(rows_in, gate_weight, precision=HIGHEST))
        up_pre = low_back(jnp.dot(rows_in, up_weight, precision=HIGHEST))
        hidden = low(jax.nn.silu(gate_pre) * up_pre)
        out_rows = low(low_back(jnp.dot(hidden, down_weight, precision=HIGHEST)))
        weight = jnp.where(is_kept, flat_probs[jnp.maximum(pair_ids, 0)], 0.0)
        return (expert_mix.at[safe_ids].add(weight[:, None] * out_rows), None)
    expert_mix, unused = lax.scan(jax.checkpoint(one_expert), jnp.zeros(inputs.shape, jnp.float32), (tok_table, pair_table, w_gate, w_up, w_down))
    return residual + expert_mix

def reference(tokens, segments, routes, first_gain, w_query, w_key, w_value, w_out, second_gain, w_router, w_gate, w_up, w_down, cotangent):
    params = tuple((member.astype(jnp.float32) for member in (first_gain, w_query, w_key, w_value, w_out, second_gain, w_router, w_gate, w_up, w_down)))
    tables = [slot_tables(routes[micro_index]) for micro_index in range(MICRO)]
    rope_parts = [rope_tables(positions_of(segments[micro_index]), HEAD_DIM) for micro_index in range(MICRO)]
    inputs = tokens.astype(jnp.float32)

    def forward(inputs_all, weights_all):
        results = []
        for micro_index in range(MICRO):
            results.append(layer(inputs_all[micro_index], rope_parts[micro_index][0], rope_parts[micro_index][1], segments[micro_index], routes[micro_index], tables[micro_index][0], tables[micro_index][1], weights_all))
        return jnp.stack(results)
    result, pullback = jax.vjp(forward, inputs, params)
    grad_inputs, grad_params = pullback(cotangent.astype(jnp.float32))
    return (result.astype(jnp.bfloat16), grad_inputs, grad_params[0], grad_params[1], grad_params[2], grad_params[3], grad_params[4], grad_params[5], grad_params[6], grad_params[7], grad_params[8], grad_params[9])
```

```python
import functools

import jax
import jax.numpy as jnp
from jax import lax
from jax.experimental import pallas as pl
from jax.experimental.pallas import tpu as pltpu
from jax.sharding import PartitionSpec as P

HEADS = 16
KV_HEADS = 8
HEAD_DIM = 64
EXPERTS = 32
CAP = 64
EPSILON = 1e-06
ROPE_BASE = 10000.0
MASKED = -1e30
HIGHEST = lax.Precision.HIGHEST
MESH = pl.DeviceIdType.MESH
BF16 = jnp.bfloat16
F32 = jnp.float32
VMEM = pl.BlockSpec(memory_space=pltpu.VMEM)
ANY = pl.BlockSpec(memory_space=pl.ANY)
DMA = pltpu.SemaphoreType.DMA


def bit_count(n):
    return n.bit_length() - 1


def masks(bits):
    out = [0]
    for b in bits:
        out = out + [m | (1 << b) for m in out]
    return out


def gather_orders(n):
    bits = list(range(bit_count(n)))
    return (bits[1:] + bits[:1], bits[:0:-1] + bits[:1])


def greet(ep, dp, ne, nd):
    barrier = pltpu.get_barrier_semaphore()
    for k in range(1, ne):
        pl.semaphore_signal(
            barrier, inc=1, device_id={"ep": lax.rem(ep + k, ne)}, device_id_type=MESH
        )
    for b in range(bit_count(nd)):
        pl.semaphore_signal(
            barrier, inc=1, device_id={"dp": jnp.bitwise_xor(dp, 1 << b)}, device_id_type=MESH
        )
    pl.semaphore_wait(barrier, ne - 1 + bit_count(nd))


def remote(src, dst, send, recv, where):
    return pltpu.make_async_remote_copy(
        src_ref=src, dst_ref=dst, send_sem=send, recv_sem=recv, device_id=where, device_id_type=MESH
    )


def gather_body(ne, nd, n_dp, n_ep, *refs):
    n_in = n_dp + n_ep
    ins, outs, sems = refs[:n_in], refs[n_in : 2 * n_in], refs[2 * n_in :]
    ep, dp = lax.axis_index("ep"), lax.axis_index("dp")
    own_sem, dp_send, dp_recv, ep_send, ep_recv = sems
    greet(ep, dp, ne, nd)
    own = []
    for a in range(n_in):
        me = dp if a < n_dp else ep
        copy = pltpu.make_async_copy(ins[a], outs[a].at[me], own_sem.at[a])
        copy.start()
        own.append(copy)

    def dp_step(t):
        copies = []
        for a in range(n_dp):
            order = gather_orders(nd)[a % 2]
            for j, m in enumerate(masks(order[:t])):
                block = jnp.bitwise_xor(dp, m)
                src = ins[a] if m == 0 else outs[a].at[block]
                k = (1 << t) - 1 + j
                copies.append(
                    remote(
                        src,
                        outs[a].at[block],
                        dp_send.at[a, k],
                        dp_recv.at[a, k],
                        {"dp": jnp.bitwise_xor(dp, 1 << order[t])},
                    )
                )
        for c in copies:
            c.start()
        return copies

    def ep_copy(a, s, way):
        shard = lax.rem(ep - way * s + ne, ne)
        src = ins[n_dp + a] if s == 0 else outs[n_dp + a].at[shard]
        k = 0 if way == 1 else 1
        return remote(
            src,
            outs[n_dp + a].at[shard],
            ep_send.at[a, k, s],
            ep_recv.at[a, k, s],
            {"ep": lax.rem(ep + way + ne, ne)},
        )

    def sends(s, way):
        if way == 1:
            return (ep >= s) & (ep < ne - 1)
        return (ep + s <= ne - 1) & (ep >= 1)

    def receives(s, way):
        if way == 1:
            return ep >= 1 + s
        return ep + 1 + s <= ne - 1

    def ep_start(s):
        for a in range(n_ep):
            for way in (1, -1):

                @pl.when(sends(s, way))
                def _(a=a, way=way):
                    ep_copy(a, s, way).start()

    def ep_wait(s):
        for a in range(n_ep):
            for way in (1, -1):

                @pl.when(receives(s, way))
                def _(a=a, way=way):
                    ep_copy(a, s, way).wait_recv()

    dp_steps = bit_count(nd) if n_dp else 0
    ep_steps = ne - 1 if n_ep else 0
    started = []
    for t in range(max(dp_steps, ep_steps) + 1):
        if 0 < t <= dp_steps:
            for c in started[-1]:
                c.wait_recv()
        if t < dp_steps:
            started.append(dp_step(t))
        if 0 < t <= ep_steps:
            ep_wait(t - 1)
        if t < ep_steps:
            ep_start(t)
    for group in started:
        for c in group:
            c.wait_send()
    for s in range(ep_steps):
        for a in range(n_ep):
            for way in (1, -1):

                @pl.when(sends(s, way))
                def _(a=a, s=s, way=way):
                    ep_copy(a, s, way).wait_send()

    for c in own:
        c.wait()


def gather(ne, nd, dp_arrays, ep_arrays, collective):
    arrays = list(dp_arrays) + list(ep_arrays)
    counts = [nd] * len(dp_arrays) + [ne] * len(ep_arrays)
    a, b = max(len(dp_arrays), 1), max(len(ep_arrays), 1)
    return pl.pallas_call(
        functools.partial(gather_body, ne, nd, len(dp_arrays), len(ep_arrays)),
        out_shape=[
            jax.ShapeDtypeStruct((n,) + v.shape, v.dtype) for n, v in zip(counts, arrays)
        ],
        in_specs=[ANY] * len(arrays),
        out_specs=[ANY] * len(arrays),
        scratch_shapes=[
            DMA((len(arrays),)),
            DMA((a, nd - 1)),
            DMA((a, nd - 1)),
            DMA((b, 2, ne - 1)),
            DMA((b, 2, ne - 1)),
        ],
        compiler_params=pltpu.CompilerParams(
            collective_id=collective, has_side_effects=True, vmem_limit_bytes=8 * 2**20
        ),
    )(*arrays)


def reduce_body(ne, nd, n_dp, n_ep, n_swap, *refs):
    n_in = n_dp + n_ep + n_swap
    ins, outs = refs[:n_in], refs[n_in : 2 * n_in]
    rest = refs[2 * n_in :]
    n_sum = n_dp + n_ep
    held = rest[:n_sum]
    landing = rest[n_sum : 2 * n_sum]
    in_sem, dp_send, dp_recv, ep_send, ep_recv, swap_send, swap_recv = rest[2 * n_sum :]
    ep, dp = lax.axis_index("ep"), lax.axis_index("dp")
    loads = []
    for a in range(n_sum):
        copy = pltpu.make_async_copy(ins[a], held[a], in_sem.at[a])
        copy.start()
        loads.append(copy)
    greet(ep, dp, ne, nd)
    swaps = []
    for a in range(n_swap):
        src, dst = ins[n_sum + a], outs[n_sum + a]
        copy = pltpu.make_async_copy(src.at[ep], dst.at[ep], in_sem.at[n_sum + a])
        copy.start()
        loads.append(copy)
        for k in range(1, ne):
            to = lax.rem(ep + k, ne)
            copy = remote(
                src.at[to], dst.at[ep], swap_send.at[a, k - 1], swap_recv.at[a, k - 1], {"ep": to}
            )
            copy.start()
            swaps.append(copy)
    for c in loads:
        c.wait()

    def add(a, block, arrived):
        held[a][block] = (held[a][block].astype(F32) + arrived.astype(F32)).astype(held[a].dtype)

    nb = bit_count(nd)

    def dp_parts(a, t):
        order = gather_orders(nd)[a % 2][::-1]
        bit, left = order[t], order[t + 1 :]
        first = sum(1 << (nb - 1 - i) for i in range(t))
        return bit, [(first + j, m) for j, m in enumerate(masks(left))]

    def dp_copies(a, t):
        bit, parts = dp_parts(a, t)
        partner = jnp.bitwise_xor(dp, 1 << bit)
        return [
            (
                m,
                k,
                remote(
                    held[a].at[jnp.bitwise_xor(partner, m)],
                    landing[a].at[k],
                    dp_send.at[a, k],
                    dp_recv.at[a, k],
                    {"dp": partner},
                ),
            )
            for k, m in parts
        ]

    def ep_copy(a, s, way):
        dest = ne - 1 - s if way == 1 else s
        k = 0 if way == 1 else 1
        return remote(
            held[n_dp + a].at[dest],
            landing[n_dp + a].at[k, s],
            ep_send.at[a, k, s],
            ep_recv.at[a, k, s],
            {"ep": lax.rem(ep + way + ne, ne)},
        )

    def ep_sends(s, way):
        return ep < ne - 1 - s if way == 1 else ep > s

    def ep_gets(s, way):
        return (
            (ep >= 1) & (ep <= ne - 1 - s) if way == 1 else (ep <= ne - 2) & (ep >= s)
        )

    dp_steps = nb if n_dp else 0
    ep_steps = ne - 1 if n_ep else 0
    started = []
    for t in range(max(dp_steps + 1, ep_steps)):
        if t < ep_steps:
            for a in range(n_ep):
                for way in (1, -1):

                    @pl.when(ep_gets(t, way))
                    def _(a=a, way=way):
                        ep_copy(a, t, way).wait_recv()
                        dest = ne - 1 - t if way == 1 else t
                        add(n_dp + a, dest, landing[n_dp + a][0 if way == 1 else 1, t])

                    @pl.when(ep_sends(t, way))
                    def _(a=a, way=way):
                        ep_copy(a, t, way).start()

        if 0 < t <= dp_steps:
            for a, group in started[-1]:
                for m, k, c in group:
                    c.wait_recv()
                    add(a, jnp.bitwise_xor(dp, m), landing[a][k])
        if t < dp_steps:
            started.append([(a, dp_copies(a, t)) for a in range(n_dp)])
            for a, group in started[-1]:
                for m, k, c in group:
                    c.start()
    for a in range(n_dp):
        outs[a][...] = held[a][dp]
    for a in range(n_ep):
        outs[n_dp + a][...] = held[n_dp + a][ep]
    for groups in started:
        for a, group in groups:
            for m, k, c in group:
                c.wait_send()
    for s in range(ep_steps):
        for a in range(n_ep):
            for way in (1, -1):

                @pl.when(ep_sends(s, way))
                def _(a=a, s=s, way=way):
                    ep_copy(a, s, way).wait_send()

    for c in swaps:
        c.wait()


def reduce(ne, nd, dp_arrays, ep_arrays, swap_arrays, collective):
    sums = list(dp_arrays) + list(ep_arrays)
    landing = [(nd - 1,) + v.shape[1:] for v in dp_arrays]
    landing += [(2, ne - 1) + v.shape[1:] for v in ep_arrays]
    a, b, c = (max(len(v), 1) for v in (dp_arrays, ep_arrays, swap_arrays))
    return pl.pallas_call(
        functools.partial(
            reduce_body, ne, nd, len(dp_arrays), len(ep_arrays), len(swap_arrays)
        ),
        out_shape=[jax.ShapeDtypeStruct(v.shape[1:], v.dtype) for v in sums]
        + [jax.ShapeDtypeStruct(v.shape, v.dtype) for v in swap_arrays],
        in_specs=[ANY] * (len(sums) + len(swap_arrays)),
        out_specs=[VMEM] * len(sums) + [ANY] * len(swap_arrays),
        scratch_shapes=[pltpu.VMEM(v.shape, v.dtype) for v in sums]
        + [pltpu.VMEM(s, v.dtype) for s, v in zip(landing, sums)]
        + [
            DMA((len(sums) + len(swap_arrays),)),
            DMA((a, nd - 1)),
            DMA((a, nd - 1)),
            DMA((b, 2, ne - 1)),
            DMA((b, 2, ne - 1)),
            DMA((c, ne - 1)),
            DMA((c, ne - 1)),
        ],
        compiler_params=pltpu.CompilerParams(
            collective_id=collective, has_side_effects=True, vmem_limit_bytes=48 * 2**20
        ),
    )(*sums, *swap_arrays)


def dot(a, b, dims=((1,), (0,))):
    return lax.dot_general(a, b, (dims, ((), ())), preferred_element_type=F32)


def expert_body(
    blocks,
    rows,
    half,
    core_ref,
    normed_ref,
    cot_ref,
    probs_ref,
    gate_ref,
    up_ref,
    down_ref,
    mix_ref,
    grad_ref,
    dots_ref,
    keep_gate,
    send_gate,
    keep_up,
    send_up,
    keep_down,
    send_down,
    rows_in,
    cots_in,
    picks,
    weights,
    first,
    second,
    load_sem,
):
    e = pl.program_id(0)
    count = pl.num_programs(0)

    def block_at(s):
        return pl.ds(pl.multiple_of(s * rows, rows), rows)

    def load(s, k):
        src, dst = ((normed_ref, first), (cot_ref, second))[k]
        return pltpu.make_async_copy(src.at[block_at(s)], dst.at[block_at(s)], load_sem.at[k, s])

    def store(s, k):
        src, dst = ((first, mix_ref), (second, grad_ref))[k]
        return pltpu.make_async_copy(src.at[block_at(s)], dst.at[block_at(s)], load_sem.at[k, s])

    @pl.when(e == 0)
    def _():
        before = lax.broadcasted_iota(jnp.int32, (rows, rows), 0)
        after = lax.broadcasted_iota(jnp.int32, (rows, rows), 1)
        earlier = (before < after).astype(BF16)
        n_exp = rows_in.shape[1]
        slot = lax.broadcasted_iota(jnp.int32, (n_exp, CAP, rows), 1)

        @pl.loop(0, blocks)
        def _(s):
            load(s, 0).start()
            load(s, 1).start()

        @pl.loop(0, blocks)
        def _(s):
            at = block_at(s)
            probs = probs_ref[s]
            hit = probs >= 0.0
            rank = dot(hit.astype(BF16), earlier)
            rank = jnp.where(hit, rank, -1.0).astype(jnp.int32)
            pick = jnp.broadcast_to(rank[:, None, :], (n_exp, CAP, rows)) == slot
            pick_f = pick.astype(F32)
            share = jnp.sum(pick_f * probs[:, None, :], axis=2, keepdims=True)
            weights[s] = share
            flat = pick_f.reshape(n_exp * CAP, rows).astype(BF16)
            picks[s] = flat
            load(s, 0).wait()
            load(s, 1).wait()
            rows_in[s] = (
                dot(flat, first[at, :]).astype(BF16).reshape(n_exp, CAP, normed_ref.shape[1])
            )
            cots_in[s] = (
                dot(flat, second[at, :]).astype(BF16).reshape(n_exp, CAP, cot_ref.shape[1])
            )

    width = normed_ref.shape[1]
    x = rows_in[:, e].reshape(blocks * CAP, width)
    c = cots_in[:, e].reshape(blocks * CAP, width)
    p = weights[:, e].reshape(blocks * CAP, 1)
    w_gate, w_up, w_down = gate_ref[0], up_ref[0], down_ref[0]
    gate_pre = dot(x, w_gate)
    up_pre = dot(x, w_up)
    sigma = jax.nn.sigmoid(gate_pre)
    silu = gate_pre * sigma
    hidden = (silu * up_pre).astype(BF16)
    out = dot(hidden, w_down) * p
    back = dot(c, w_down, ((1,), (1,)))
    wide = hidden.astype(F32)
    pair = jnp.sum(wide * back, axis=1, keepdims=True)
    back = back * p
    grad_up = (back * silu).astype(BF16)
    grad_gate = (back * up_pre * (sigma * (1.0 + gate_pre * (1.0 - sigma)))).astype(BF16)
    scaled = (wide * p).astype(BF16)
    grad_x = dot(grad_gate, w_gate, ((1,), (1,))) + dot(grad_up, w_up, ((1,), (1,)))

    flat = picks[:, pl.ds(pl.multiple_of(e * CAP, CAP), CAP), :].astype(F32)
    dots_ref[0] = jnp.sum(flat * pair.reshape(blocks, CAP, 1), axis=1)

    def split(value, keep, send):
        value = value.astype(BF16)
        n, r = half * 2, value.shape[0] // (half * 2)
        value = value.reshape(n, r, value.shape[1])

        @pl.when(core_ref[0] == 0)
        def _():
            for i in range(half):
                keep[i, 0] = value[2 * i]
                send[i, 0] = value[2 * i + 1]

        @pl.when(core_ref[0] == 1)
        def _():
            for i in range(half):
                keep[i, 0] = value[2 * i + 1]
                send[i, 0] = value[2 * i]

    split(dot(scaled, c, ((0,), (0,))), keep_down, send_down)
    split(dot(x, grad_gate, ((0,), (0,))), keep_gate, send_gate)
    split(dot(x, grad_up, ((0,), (0,))), keep_up, send_up)

    rows_in[:, e] = grad_x.astype(BF16).reshape(blocks, CAP, width)
    cots_in[:, e] = out.astype(BF16).reshape(blocks, CAP, width)

    @pl.when(e == count - 1)
    def _():
        n_exp = rows_in.shape[1]

        @pl.loop(0, blocks)
        def _(s):
            at = block_at(s)
            flat = picks[s]
            first[at, :] = dot(
                flat, cots_in[s].reshape(n_exp * CAP, width), ((0,), (0,))
            ).astype(BF16)
            second[at, :] = dot(
                flat, rows_in[s].reshape(n_exp * CAP, width), ((0,), (0,))
            ).astype(BF16)
            store(s, 0).start()
            store(s, 1).start()

        @pl.loop(0, blocks)
        def _(s):
            store(s, 0).wait()
            store(s, 1).wait()


def experts(normed, cot, probs, w_gate, w_up, w_down, rows, nd, core):
    n_exp, width, inner = w_gate.shape
    blocks = normed.shape[0] // rows
    half = nd // 2
    grads = []
    for a, b in ((width, inner), (width, inner), (inner, width)):
        shape = jax.ShapeDtypeStruct((half, n_exp, a // nd, b), BF16)
        spec = pl.BlockSpec((half, 1, a // nd, b), lambda e, *_: (0, e, 0, 0))
        grads += [(shape, spec)] * 2
    one = pl.Buffered(1)
    full = (blocks * rows, width)
    return pl.pallas_call(
        functools.partial(expert_body, blocks, rows, half),
        grid_spec=pltpu.PrefetchScalarGridSpec(
            num_scalar_prefetch=1,
            grid=(n_exp,),
            in_specs=[
                ANY,
                ANY,
                pl.BlockSpec(probs.shape, lambda e, *_: (0, 0, 0), pipeline_mode=one),
                pl.BlockSpec((1, width, inner), lambda e, *_: (e, 0, 0)),
                pl.BlockSpec((1, width, inner), lambda e, *_: (e, 0, 0)),
                pl.BlockSpec((1, inner, width), lambda e, *_: (e, 0, 0)),
            ],
            out_specs=[
                ANY,
                ANY,
                pl.BlockSpec((1, blocks, rows), lambda e, *_: (e, 0, 0)),
            ]
            + [g[1] for g in grads],
            scratch_shapes=[
                pltpu.VMEM((blocks, n_exp, CAP, width), BF16),
                pltpu.VMEM((blocks, n_exp, CAP, width), BF16),
                pltpu.VMEM((blocks, n_exp * CAP, rows), BF16),
                pltpu.VMEM((blocks, n_exp, CAP, 1), F32),
                pltpu.VMEM(full, BF16),
                pltpu.VMEM(full, BF16),
                DMA((2, blocks)),
            ],
        ),
        out_shape=[
            jax.ShapeDtypeStruct(full, BF16),
            jax.ShapeDtypeStruct(full, BF16),
            jax.ShapeDtypeStruct((n_exp, blocks, rows), F32),
        ]
        + [g[0] for g in grads],
        compiler_params=pltpu.CompilerParams(
            vmem_limit_bytes=60 * 2**20, dimension_semantics=("arbitrary",)
        ),
    )(core, normed, cot, probs, w_gate, w_up, w_down)


def rms_scale(values):
    return lax.rsqrt(jnp.mean(values * values, axis=-1, keepdims=True) + EPSILON)


def rotate(values, cosine, sine):
    half = values.shape[-1] // 2
    a, b = values[..., :half], values[..., half:]
    return jnp.concatenate([a * cosine - b * sine, b * cosine + a * sine], axis=-1)


def attend(queries, keys, values, allowed):
    scale = queries.shape[-1] ** (-0.5)
    scores = jnp.einsum("mqkgd,mnkd->mkgqn", queries, keys, preferred_element_type=F32) * scale
    scores = jnp.where(allowed[:, None, None], scores, MASKED)
    top = jnp.max(scores, axis=-1, keepdims=True)
    terms = jnp.exp(scores - top)
    total = jnp.sum(terms, axis=-1, keepdims=True)
    weights = (terms / total).astype(BF16)
    out = jnp.einsum("mkgqn,mnkd->mqkgd", weights, values, preferred_element_type=F32)
    return out, top + jnp.log(total)


def attend_back(queries, grad, log_total, grad_dot, keys, values, allowed):
    scale = queries.shape[-1] ** (-0.5)
    scores = jnp.einsum("mqkgd,mnkd->mkgqn", queries, keys, preferred_element_type=F32) * scale
    scores = jnp.where(allowed[:, None, None], scores, MASKED)
    probs = jnp.exp(scores - log_total)
    grad_prob = jnp.einsum("mqkgd,mnkd->mkgqn", grad, values, preferred_element_type=F32)
    grad_score = (probs * (grad_prob - grad_dot)).astype(BF16)
    grad_query = (
        jnp.einsum("mkgqn,mnkd->mqkgd", grad_score, keys, preferred_element_type=F32) * scale
    )
    grad_key = (
        jnp.einsum("mkgqn,mqkgd->mnkd", grad_score, queries, preferred_element_type=F32) * scale
    )
    grad_value = jnp.einsum(
        "mkgqn,mqkgd->mnkd", probs.astype(BF16), grad, preferred_element_type=F32
    )
    return grad_query, grad_key, grad_value


def halve(values, dp, orders, nb):
    live = list(range(nb - 1, 0, -1))
    for bit in orders:
        axis = live.index(bit)
        mine = jnp.bitwise_and(lax.shift_right_logical(dp, bit), 1)
        kept = lax.dynamic_index_in_dim(values, mine, axis, keepdims=False)
        sent = lax.dynamic_index_in_dim(values, 1 - mine, axis, keepdims=False)
        n = 1 << nb
        arrived = lax.ppermute(sent, "dp", [(i, i ^ (1 << bit)) for i in range(n)])
        values = (kept.astype(F32) + arrived.astype(F32)).astype(BF16)
        live.remove(bit)
    return values


def reduce_expert(keep, send, dp, nd):
    nb = bit_count(nd)
    arrived = lax.ppermute(send, "dp", [(i, i ^ 1) for i in range(nd)])
    values = (keep.astype(F32) + arrived.astype(F32)).astype(BF16)
    values = values.reshape((2,) * (nb - 1) + values.shape[1:])
    half = keep.shape[1] // 2
    first, second = gather_orders(nd)
    out = []
    for part, order in ((0, first), (1, second)):
        piece = lax.slice_in_dim(values, part * half, (part + 1) * half, axis=nb - 1)
        out.append(halve(piece, dp, order[:-1][::-1], nb))
    return jnp.concatenate(out, axis=0).astype(F32)


def per_device(
    tokens,
    segments,
    routes,
    first_gain,
    w_query,
    w_key,
    w_value,
    w_out,
    second_gain,
    w_router,
    w_gate,
    w_up,
    w_down,
    cotangent,
):
    micro, rows, width = tokens.shape
    ne, nd = lax.axis_size("ep"), lax.axis_size("dp")
    ep, dp = lax.axis_index("ep"), lax.axis_index("dp")
    groups = HEADS // KV_HEADS
    length = rows * nd
    kv_width = KV_HEADS * HEAD_DIM
    every = micro * rows
    inputs = tokens.reshape(every, width).astype(F32)
    grad_output = cotangent.reshape(every, width).astype(F32)

    query_pos = dp * rows + jnp.arange(rows, dtype=jnp.int32)
    halfway = HEAD_DIM // 2
    frequency = ROPE_BASE ** (-(jnp.arange(halfway, dtype=F32) * 2.0 / HEAD_DIM))
    angles = query_pos.astype(F32)[:, None] * frequency[None, :]
    cosine = jnp.tile(jnp.cos(angles), (micro, 1))[:, None, :]
    sine = jnp.tile(jnp.sin(angles), (micro, 1))[:, None, :]

    inv_one = rms_scale(inputs)
    normed_one = (inputs * inv_one * first_gain).astype(BF16)
    query_rot = rotate(
        jnp.dot(normed_one, w_query, preferred_element_type=F32).reshape(every, HEADS, HEAD_DIM),
        cosine,
        sine,
    ).astype(BF16)
    key_rot = (
        rotate(
            jnp.dot(normed_one, w_key, preferred_element_type=F32).reshape(
                every, KV_HEADS, HEAD_DIM
            ),
            cosine,
            sine,
        )
        .astype(BF16)
        .reshape(every, kv_width)
    )
    value_own = jnp.dot(normed_one, w_value, preferred_element_type=F32).astype(BF16)

    ids = jnp.arange(128, dtype=jnp.int32)
    counts = jnp.sum((segments[:, 0, :, None] == ids).astype(F32), axis=1)
    counts = jnp.concatenate([counts, jnp.zeros((8 - micro, 128), F32)], axis=0)

    key_all, value_all, count_all, cot_all = gather(
        ne, nd, (key_rot, value_own, counts), (cotangent.reshape(every, width),), 0
    )

    totals = jnp.sum(count_all[:, :micro], axis=0)
    lower = (ids[None, None, :] < segments[:, 0, :, None]).astype(F32)
    starts = jnp.sum(lower * totals[:, None, :], axis=2).astype(jnp.int32)
    key_pos = jnp.arange(length, dtype=jnp.int32)
    allowed = (key_pos[None, None, :] <= query_pos[None, :, None]) & (
        key_pos[None, None, :] >= starts[:, :, None]
    )

    def sequence(gathered):
        return (
            gathered.reshape(nd, micro, rows, kv_width)
            .transpose(1, 0, 2, 3)
            .reshape(micro, length, KV_HEADS, HEAD_DIM)
        )

    keys, values = sequence(key_all), sequence(value_all)
    queries = query_rot.reshape(micro, rows, KV_HEADS, groups, HEAD_DIM)
    attn_sum, log_total = attend(queries, keys, values, allowed)
    attn_low = attn_sum.reshape(every, HEADS * HEAD_DIM).astype(BF16)
    residual = inputs + jnp.dot(attn_low, w_out, preferred_element_type=F32)
    inv_two = rms_scale(residual)
    normed_two = (residual * inv_two * second_gain).astype(BF16)
    logits = jnp.dot(normed_two, w_router, preferred_element_type=F32)
    routing = routes.reshape(every, routes.shape[2])
    chosen = jnp.any(
        routing[:, :, None] == jnp.arange(EXPERTS, dtype=jnp.int32)[None, None, :], axis=1
    )
    masked = jnp.where(chosen, logits, MASKED)
    terms = jnp.where(chosen, jnp.exp(masked - jnp.max(masked, axis=1, keepdims=True)), 0.0)
    gate_probs = terms / jnp.sum(terms, axis=1, keepdims=True)
    marked = jnp.where(chosen, gate_probs, -1.0).T

    normed_all, marked_all = gather(ne, nd, (), (normed_two, marked), 1)
    here = EXPERTS // ne
    probs_here = lax.dynamic_slice_in_dim(marked_all, ep * here, here, axis=1)
    probs_here = (
        probs_here.reshape(ne, here, micro, rows)
        .transpose(0, 2, 1, 3)
        .reshape(ne * micro, here, rows)
    )
    core = jnp.bitwise_and(dp, 1).reshape(1)
    mix, grad_in, pair_dots, *grads = experts(
        normed_all.reshape(ne * every, width),
        cot_all.reshape(ne * every, width),
        probs_here,
        w_gate,
        w_up,
        w_down,
        rows,
        nd,
        core,
    )
    grad_w_gate = reduce_expert(grads[0], grads[1], dp, nd)
    grad_w_up = reduce_expert(grads[2], grads[3], dp, nd)
    grad_w_down = reduce_expert(grads[4], grads[5], dp, nd)

    pair_dots = pair_dots.reshape(here, ne, every).transpose(1, 0, 2)
    grad_back, dots_all = reduce(
        ne, nd, (), (grad_in.reshape(ne, every, width),), (pair_dots,), 2
    )
    pair_dot = dots_all.reshape(EXPERTS, every).T
    grad_logits = gate_probs * (
        pair_dot - jnp.sum(gate_probs * pair_dot, axis=1, keepdims=True)
    )
    grad_w_router = jnp.einsum(
        "td,te->de", normed_two.astype(F32), grad_logits, precision=HIGHEST
    )
    grad_normed_two = (
        jnp.einsum("te,de->td", grad_logits, w_router.astype(F32), precision=HIGHEST)
        + grad_back.astype(F32)
    )
    scaled_two = grad_normed_two * second_gain
    grad_gain_two = jnp.sum(grad_normed_two * residual * inv_two, axis=0)
    grad_residual = (
        grad_output
        + inv_two * scaled_two
        - residual * inv_two**3 * jnp.mean(scaled_two * residual, axis=-1, keepdims=True)
    )
    residual_low = grad_residual.astype(BF16)
    grad_w_out = jnp.einsum("tf,td->fd", attn_low, residual_low, preferred_element_type=F32)
    grad_attn = jnp.einsum("td,fd->tf", residual_low, w_out, preferred_element_type=F32).astype(
        BF16
    )
    grad_attn = grad_attn.reshape(micro, rows, KV_HEADS, groups, HEAD_DIM)
    grad_dot = jnp.sum(grad_attn.astype(F32) * attn_sum, axis=-1).transpose(0, 2, 3, 1)[..., None]
    grad_query_rot, grad_key_all, grad_value_all = attend_back(
        queries, grad_attn, log_total, grad_dot, keys, values, allowed
    )

    def pieces(summed):
        return (
            summed.reshape(micro, nd, rows, kv_width)
            .transpose(1, 0, 2, 3)
            .reshape(nd, every, kv_width)
            .astype(BF16)
        )

    grad_key, grad_value, mix_own = reduce(
        ne,
        nd,
        (pieces(grad_key_all), pieces(grad_value_all)),
        (mix.reshape(ne, every, width),),
        (),
        3,
    )
    output = (residual + mix_own.astype(F32)).astype(BF16).reshape(tokens.shape)
    grad_query_pre = (
        rotate(grad_query_rot.reshape(every, HEADS, HEAD_DIM), cosine, -sine)
        .astype(BF16)
        .reshape(every, HEADS * HEAD_DIM)
    )
    grad_key_pre = (
        rotate(grad_key.astype(F32).reshape(every, KV_HEADS, HEAD_DIM), cosine, -sine)
        .astype(BF16)
        .reshape(every, kv_width)
    )
    grad_value_pre = grad_value

    def weight_grad(grad):
        return jnp.einsum("td,tf->df", normed_one, grad, preferred_element_type=F32)

    grad_w_query = weight_grad(grad_query_pre)
    grad_w_key = weight_grad(grad_key_pre)
    grad_w_value = weight_grad(grad_value_pre)
    grad_normed_one = (
        jnp.einsum("tf,df->td", grad_query_pre, w_query, preferred_element_type=F32)
        + jnp.einsum("tf,df->td", grad_key_pre, w_key, preferred_element_type=F32)
        + jnp.einsum("tf,df->td", grad_value_pre, w_value, preferred_element_type=F32)
    )
    scaled_one = grad_normed_one * first_gain
    grad_gain_one = jnp.sum(grad_normed_one * inputs * inv_one, axis=0)
    grad_tokens = (
        grad_residual
        + inv_one * scaled_one
        - inputs * inv_one**3 * jnp.mean(scaled_one * inputs, axis=-1, keepdims=True)
    )

    small = jnp.concatenate(
        [
            grad_w_router,
            grad_gain_one[:, None],
            grad_gain_two[:, None],
            jnp.zeros((width, 128 - EXPERTS - 2), F32),
        ],
        axis=1,
    )

    def by_owner(grad):
        share = grad.shape[0] // (ne * nd)
        return (
            grad.astype(BF16)
            .reshape(ne, nd, share, grad.shape[1])
            .transpose(1, 0, 2, 3)
            .reshape(nd, ne * share, grad.shape[1])
        )

    dense = reduce(
        ne,
        nd,
        (
            by_owner(jnp.concatenate([grad_w_query, grad_w_key, small], axis=1)),
            by_owner(jnp.concatenate([grad_w_out, grad_w_value], axis=1)),
        ),
        (),
        (),
        4,
    )
    dense = reduce(ne, nd, (), [v.reshape(ne, -1, v.shape[1]) for v in dense], (), 5)
    first, second = (v.astype(F32) for v in dense)
    model = width + kv_width
    return (
        output,
        grad_tokens.reshape(tokens.shape),
        first[:, model + EXPERTS],
        first[:, :width],
        first[:, width:model],
        second[:, width:],
        second[:, :width],
        first[:, model + EXPERTS + 1],
        first[:, model : model + EXPERTS],
        grad_w_gate,
        grad_w_up,
        grad_w_down,
    )


def solution(mesh):
    in_specs = (
        P(None, ("ep", "dp"), None),
        P(None, "ep", "dp"),
        P(None, ("ep", "dp"), None),
        P(),
        P(),
        P(),
        P(),
        P(),
        P(),
        P(),
        P("ep", None, None),
        P("ep", None, None),
        P("ep", None, None),
        P(None, ("ep", "dp"), None),
    )
    out_specs = (
        P(None, ("ep", "dp"), None),
        P(None, ("ep", "dp"), None),
        P(("ep", "dp")),
        P(("ep", "dp"), None),
        P(("ep", "dp"), None),
        P(("ep", "dp"), None),
        P(("ep", "dp"), None),
        P(("ep", "dp")),
        P(("ep", "dp"), None),
        P("ep", "dp", None),
        P("ep", "dp", None),
        P("ep", "dp", None),
    )
    return jax.shard_map(
        per_device, mesh=mesh, in_specs=in_specs, out_specs=out_specs, check_vma=False
    )
```

```python
import functools

import jax
import jax.numpy as jnp
from jax import lax
from jax.experimental import pallas as pl
from jax.experimental.pallas import tpu as pltpu
from jax.sharding import PartitionSpec as P

HEADS = 16
KV_HEADS = 8
HEAD_DIM = 64
EXPERTS = 32
CAP = 64
EPSILON = 1e-06
ROPE_BASE = 10000.0
MASKED = -1e30
HIGHEST = lax.Precision.HIGHEST
MESH = pl.DeviceIdType.MESH
BF16 = jnp.bfloat16
F32 = jnp.float32
VMEM = pl.BlockSpec(memory_space=pltpu.VMEM)
ANY = pl.BlockSpec(memory_space=pl.ANY)
DMA = pltpu.SemaphoreType.DMA


def bit_count(n):
    return n.bit_length() - 1


def masks(bits):
    out = [0]
    for b in bits:
        out = out + [m | (1 << b) for m in out]
    return out


def gather_orders(n):
    bits = list(range(bit_count(n)))
    return (bits[1:] + bits[:1], bits[:0:-1] + bits[:1])


def greet(ep, dp, ne, nd):
    barrier = pltpu.get_barrier_semaphore()
    for k in range(1, ne):
        pl.semaphore_signal(
            barrier, inc=1, device_id={"ep": lax.rem(ep + k, ne)}, device_id_type=MESH
        )
    for b in range(bit_count(nd)):
        pl.semaphore_signal(
            barrier, inc=1, device_id={"dp": jnp.bitwise_xor(dp, 1 << b)}, device_id_type=MESH
        )
    pl.semaphore_wait(barrier, ne - 1 + bit_count(nd))


def remote(src, dst, send, recv, where):
    return pltpu.make_async_remote_copy(
        src_ref=src, dst_ref=dst, send_sem=send, recv_sem=recv, device_id=where, device_id_type=MESH
    )


def gather_body(ne, nd, n_dp, n_ep, *refs):
    n_in = n_dp + n_ep
    ins, outs, sems = refs[:n_in], refs[n_in : 2 * n_in], refs[2 * n_in :]
    ep, dp = lax.axis_index("ep"), lax.axis_index("dp")
    own_sem, dp_send, dp_recv, ep_send, ep_recv = sems
    greet(ep, dp, ne, nd)
    own = []
    for a in range(n_in):
        me = dp if a < n_dp else ep
        copy = pltpu.make_async_copy(ins[a], outs[a].at[me], own_sem.at[a])
        copy.start()
        own.append(copy)

    def dp_step(t):
        copies = []
        for a in range(n_dp):
            order = gather_orders(nd)[a % 2]
            for j, m in enumerate(masks(order[:t])):
                block = jnp.bitwise_xor(dp, m)
                src = ins[a] if m == 0 else outs[a].at[block]
                k = (1 << t) - 1 + j
                copies.append(
                    remote(
                        src,
                        outs[a].at[block],
                        dp_send.at[a, k],
                        dp_recv.at[a, k],
                        {"dp": jnp.bitwise_xor(dp, 1 << order[t])},
                    )
                )
        for c in copies:
            c.start()
        return copies

    def ep_copy(a, s, way):
        shard = lax.rem(ep - way * s + ne, ne)
        src = ins[n_dp + a] if s == 0 else outs[n_dp + a].at[shard]
        k = 0 if way == 1 else 1
        return remote(
            src,
            outs[n_dp + a].at[shard],
            ep_send.at[a, k, s],
            ep_recv.at[a, k, s],
            {"ep": lax.rem(ep + way + ne, ne)},
        )

    def sends(s, way):
        if way == 1:
            return (ep >= s) & (ep < ne - 1)
        return (ep + s <= ne - 1) & (ep >= 1)

    def receives(s, way):
        if way == 1:
            return ep >= 1 + s
        return ep + 1 + s <= ne - 1

    def ep_start(s):
        for a in range(n_ep):
            for way in (1, -1):

                @pl.when(sends(s, way))
                def _(a=a, way=way):
                    ep_copy(a, s, way).start()

    def ep_wait(s):
        for a in range(n_ep):
            for way in (1, -1):

                @pl.when(receives(s, way))
                def _(a=a, way=way):
                    ep_copy(a, s, way).wait_recv()

    dp_steps = bit_count(nd) if n_dp else 0
    ep_steps = ne - 1 if n_ep else 0
    started = []
    for t in range(max(dp_steps, ep_steps) + 1):
        if 0 < t <= dp_steps:
            for c in started[-1]:
                c.wait_recv()
        if t < dp_steps:
            started.append(dp_step(t))
        if 0 < t <= ep_steps:
            ep_wait(t - 1)
        if t < ep_steps:
            ep_start(t)
    for group in started:
        for c in group:
            c.wait_send()
    for s in range(ep_steps):
        for a in range(n_ep):
            for way in (1, -1):

                @pl.when(sends(s, way))
                def _(a=a, s=s, way=way):
                    ep_copy(a, s, way).wait_send()

    for c in own:
        c.wait()


def cost(us):
    return pl.CostEstimate(flops=0, bytes_accessed=int(us * 3.0e6), transcendentals=0)


def gather(ne, nd, dp_arrays, ep_arrays, collective, us):
    arrays = list(dp_arrays) + list(ep_arrays)
    counts = [nd] * len(dp_arrays) + [ne] * len(ep_arrays)
    a, b = max(len(dp_arrays), 1), max(len(ep_arrays), 1)
    return pl.pallas_call(
        functools.partial(gather_body, ne, nd, len(dp_arrays), len(ep_arrays)),
        out_shape=[
            jax.ShapeDtypeStruct((n,) + v.shape, v.dtype) for n, v in zip(counts, arrays)
        ],
        in_specs=[ANY] * len(arrays),
        out_specs=[ANY] * len(arrays),
        scratch_shapes=[
            DMA((len(arrays),)),
            DMA((a, nd - 1)),
            DMA((a, nd - 1)),
            DMA((b, 2, ne - 1)),
            DMA((b, 2, ne - 1)),
        ],
        compiler_params=pltpu.CompilerParams(
            collective_id=collective, has_side_effects=True, vmem_limit_bytes=8 * 2**20
        ),
        cost_estimate=cost(us),
    )(*arrays)


def reduce_body(ne, nd, n_dp, n_ep, n_swap, *refs):
    n_in = n_dp + n_ep + n_swap
    ins, outs = refs[:n_in], refs[n_in : 2 * n_in]
    rest = refs[2 * n_in :]
    n_sum = n_dp + n_ep
    held = rest[:n_sum]
    landing = rest[n_sum : 2 * n_sum]
    in_sem, dp_send, dp_recv, ep_send, ep_recv, swap_send, swap_recv = rest[2 * n_sum :]
    ep, dp = lax.axis_index("ep"), lax.axis_index("dp")
    loads = []
    for a in range(n_sum):
        copy = pltpu.make_async_copy(ins[a], held[a], in_sem.at[a])
        copy.start()
        loads.append(copy)
    greet(ep, dp, ne, nd)
    swaps = []
    for a in range(n_swap):
        src, dst = ins[n_sum + a], outs[n_sum + a]
        copy = pltpu.make_async_copy(src.at[ep], dst.at[ep], in_sem.at[n_sum + a])
        copy.start()
        loads.append(copy)
        for k in range(1, ne):
            to = lax.rem(ep + k, ne)
            copy = remote(
                src.at[to], dst.at[ep], swap_send.at[a, k - 1], swap_recv.at[a, k - 1], {"ep": to}
            )
            copy.start()
            swaps.append(copy)
    for c in loads:
        c.wait()

    def add(a, block, arrived):
        held[a][block] = (held[a][block].astype(F32) + arrived.astype(F32)).astype(held[a].dtype)

    nb = bit_count(nd)

    def dp_parts(a, t):
        order = gather_orders(nd)[a % 2][::-1]
        bit, left = order[t], order[t + 1 :]
        first = sum(1 << (nb - 1 - i) for i in range(t))
        return bit, [(first + j, m) for j, m in enumerate(masks(left))]

    def dp_copies(a, t):
        bit, parts = dp_parts(a, t)
        partner = jnp.bitwise_xor(dp, 1 << bit)
        return [
            (
                m,
                k,
                remote(
                    held[a].at[jnp.bitwise_xor(partner, m)],
                    landing[a].at[k],
                    dp_send.at[a, k],
                    dp_recv.at[a, k],
                    {"dp": partner},
                ),
            )
            for k, m in parts
        ]

    def ep_copy(a, dest, way):
        k = 0 if way == 1 else 1
        return remote(
            held[n_dp + a].at[dest],
            landing[n_dp + a].at[k, dest],
            ep_send.at[a, k, dest],
            ep_recv.at[a, k, dest],
            {"ep": lax.rem(ep + way + ne, ne)},
        )

    def ep_turn(t, way):
        return ep + ne - 1 - t if way == 1 else ep + t - (ne - 1)

    def ep_has(t, way):
        return ep_turn(t, way) <= ne - 1 if way == 1 else ep_turn(t, way) >= 0

    def ep_inner(way):
        return ep >= 1 if way == 1 else ep <= ne - 2

    def ep_go(t):
        for a in range(n_ep):
            for way in (1, -1):
                dest = ep_turn(t, way)

                @pl.when(ep_has(t, way) & ep_inner(way))
                def _(a=a, way=way, dest=dest):
                    ep_copy(a, dest, way).wait_recv()
                    add(n_dp + a, dest, landing[n_dp + a][0 if way == 1 else 1, dest])

                if t < ne - 1:

                    @pl.when(ep_has(t, way))
                    def _(a=a, way=way, dest=dest):
                        ep_copy(a, dest, way).start()

    dp_steps = nb if n_dp else 0
    ep_steps = ne if n_ep else 0
    started = []
    for t in range(max(dp_steps + 1, ep_steps)):
        if t < ep_steps:
            ep_go(t)

        if 0 < t <= dp_steps:
            for a, group in started[-1]:
                for m, k, c in group:
                    c.wait_recv()
                    add(a, jnp.bitwise_xor(dp, m), landing[a][k])
        if t < dp_steps:
            started.append([(a, dp_copies(a, t)) for a in range(n_dp)])
            for a, group in started[-1]:
                for m, k, c in group:
                    c.start()
    for a in range(n_dp):
        outs[a][...] = held[a][dp]
    for a in range(n_ep):
        outs[n_dp + a][...] = held[n_dp + a][ep]
    for groups in started:
        for a, group in groups:
            for m, k, c in group:
                c.wait_send()
    for t in range(ep_steps - 1):
        for a in range(n_ep):
            for way in (1, -1):
                dest = ep_turn(t, way)

                @pl.when(ep_has(t, way))
                def _(a=a, way=way, dest=dest):
                    ep_copy(a, dest, way).wait_send()

    for c in swaps:
        c.wait()


def reduce(ne, nd, dp_arrays, ep_arrays, swap_arrays, collective, us):
    sums = list(dp_arrays) + list(ep_arrays)
    landing = [(nd - 1,) + v.shape[1:] for v in dp_arrays]
    landing += [(2, ne) + v.shape[1:] for v in ep_arrays]
    a, b, c = (max(len(v), 1) for v in (dp_arrays, ep_arrays, swap_arrays))
    return pl.pallas_call(
        functools.partial(
            reduce_body, ne, nd, len(dp_arrays), len(ep_arrays), len(swap_arrays)
        ),
        out_shape=[jax.ShapeDtypeStruct(v.shape[1:], v.dtype) for v in sums]
        + [jax.ShapeDtypeStruct(v.shape, v.dtype) for v in swap_arrays],
        in_specs=[ANY] * (len(sums) + len(swap_arrays)),
        out_specs=[VMEM] * len(sums) + [ANY] * len(swap_arrays),
        scratch_shapes=[pltpu.VMEM(v.shape, v.dtype) for v in sums]
        + [pltpu.VMEM(s, v.dtype) for s, v in zip(landing, sums)]
        + [
            DMA((len(sums) + len(swap_arrays),)),
            DMA((a, nd - 1)),
            DMA((a, nd - 1)),
            DMA((b, 2, ne)),
            DMA((b, 2, ne)),
            DMA((c, ne - 1)),
            DMA((c, ne - 1)),
        ],
        compiler_params=pltpu.CompilerParams(
            collective_id=collective, has_side_effects=True, vmem_limit_bytes=48 * 2**20
        ),
        cost_estimate=cost(us),
    )(*sums, *swap_arrays)


def dot(a, b, dims=((1,), (0,))):
    return lax.dot_general(a, b, (dims, ((), ())), preferred_element_type=F32)


def expert_body(
    blocks,
    rows,
    half,
    core_ref,
    normed_ref,
    cot_ref,
    probs_ref,
    gate_ref,
    up_ref,
    down_ref,
    mix_ref,
    grad_ref,
    dots_ref,
    keep_gate,
    send_gate,
    keep_up,
    send_up,
    keep_down,
    send_down,
    rows_in,
    cots_in,
    picks,
    weights,
    first,
    second,
    load_sem,
):
    e = pl.program_id(0)
    count = pl.num_programs(0)

    def block_at(s):
        return pl.ds(pl.multiple_of(s * rows, rows), rows)

    def load(s, k):
        src, dst = ((normed_ref, first), (cot_ref, second))[k]
        return pltpu.make_async_copy(src.at[block_at(s)], dst.at[block_at(s)], load_sem.at[k, s])

    def store(s, k):
        src, dst = ((first, mix_ref), (second, grad_ref))[k]
        return pltpu.make_async_copy(src.at[block_at(s)], dst.at[block_at(s)], load_sem.at[k, s])

    @pl.when(e == 0)
    def _():
        before = lax.broadcasted_iota(jnp.int32, (rows, rows), 0)
        after = lax.broadcasted_iota(jnp.int32, (rows, rows), 1)
        earlier = (before < after).astype(BF16)
        n_exp = rows_in.shape[1]
        slot = lax.broadcasted_iota(jnp.int32, (n_exp, CAP, rows), 1)

        @pl.loop(0, blocks)
        def _(s):
            load(s, 0).start()
            load(s, 1).start()

        @pl.loop(0, blocks)
        def _(s):
            at = block_at(s)
            probs = probs_ref[s]
            hit = probs >= 0.0
            rank = dot(hit.astype(BF16), earlier)
            rank = jnp.where(hit, rank, -1.0).astype(jnp.int32)
            pick = jnp.broadcast_to(rank[:, None, :], (n_exp, CAP, rows)) == slot
            pick_f = pick.astype(F32)
            share = jnp.sum(pick_f * probs[:, None, :], axis=2, keepdims=True)
            weights[s] = share
            flat = pick_f.reshape(n_exp * CAP, rows).astype(BF16)
            picks[s] = flat
            load(s, 0).wait()
            load(s, 1).wait()
            rows_in[s] = (
                dot(flat, first[at, :]).astype(BF16).reshape(n_exp, CAP, normed_ref.shape[1])
            )
            cots_in[s] = (
                dot(flat, second[at, :]).astype(BF16).reshape(n_exp, CAP, cot_ref.shape[1])
            )

    width = normed_ref.shape[1]
    x = rows_in[:, e].reshape(blocks * CAP, width)
    c = cots_in[:, e].reshape(blocks * CAP, width)
    p = weights[:, e].reshape(blocks * CAP, 1)
    w_gate, w_up, w_down = gate_ref[0], up_ref[0], down_ref[0]
    gate_pre = dot(x, w_gate)
    up_pre = dot(x, w_up)
    sigma = jax.nn.sigmoid(gate_pre)
    silu = gate_pre * sigma
    hidden = (silu * up_pre).astype(BF16)
    out = dot(hidden, w_down) * p
    back = dot(c, w_down, ((1,), (1,)))
    wide = hidden.astype(F32)
    pair = jnp.sum(wide * back, axis=1, keepdims=True)
    back = back * p
    grad_up = (back * silu).astype(BF16)
    grad_gate = (back * up_pre * (sigma * (1.0 + gate_pre * (1.0 - sigma)))).astype(BF16)
    scaled = (wide * p).astype(BF16)
    grad_x = dot(grad_gate, w_gate, ((1,), (1,))) + dot(grad_up, w_up, ((1,), (1,)))

    flat = picks[:, pl.ds(pl.multiple_of(e * CAP, CAP), CAP), :].astype(F32)
    dots_ref[0] = jnp.sum(flat * pair.reshape(blocks, CAP, 1), axis=1)

    def split(value, keep, send):
        value = value.astype(BF16)
        n, r = half * 2, value.shape[0] // (half * 2)
        value = value.reshape(n, r, value.shape[1])

        @pl.when(core_ref[0] == 0)
        def _():
            for i in range(half):
                keep[i, 0] = value[2 * i]
                send[i, 0] = value[2 * i + 1]

        @pl.when(core_ref[0] == 1)
        def _():
            for i in range(half):
                keep[i, 0] = value[2 * i + 1]
                send[i, 0] = value[2 * i]

    split(dot(scaled, c, ((0,), (0,))), keep_down, send_down)
    split(dot(x, grad_gate, ((0,), (0,))), keep_gate, send_gate)
    split(dot(x, grad_up, ((0,), (0,))), keep_up, send_up)

    rows_in[:, e] = grad_x.astype(BF16).reshape(blocks, CAP, width)
    cots_in[:, e] = out.astype(BF16).reshape(blocks, CAP, width)

    @pl.when(e == count - 1)
    def _():
        n_exp = rows_in.shape[1]

        @pl.loop(0, blocks)
        def _(s):
            at = block_at(s)
            flat = picks[s]
            first[at, :] = dot(
                flat, cots_in[s].reshape(n_exp * CAP, width), ((0,), (0,))
            ).astype(BF16)
            second[at, :] = dot(
                flat, rows_in[s].reshape(n_exp * CAP, width), ((0,), (0,))
            ).astype(BF16)
            store(s, 0).start()
            store(s, 1).start()

        @pl.loop(0, blocks)
        def _(s):
            store(s, 0).wait()
            store(s, 1).wait()


def experts(normed, cot, probs, w_gate, w_up, w_down, rows, nd, core):
    n_exp, width, inner = w_gate.shape
    blocks = normed.shape[0] // rows
    half = nd // 2
    grads = []
    for a, b in ((width, inner), (width, inner), (inner, width)):
        shape = jax.ShapeDtypeStruct((half, n_exp, a // nd, b), BF16)
        spec = pl.BlockSpec((half, 1, a // nd, b), lambda e, *_: (0, e, 0, 0))
        grads += [(shape, spec)] * 2
    one = pl.Buffered(1)
    full = (blocks * rows, width)
    return pl.pallas_call(
        functools.partial(expert_body, blocks, rows, half),
        grid_spec=pltpu.PrefetchScalarGridSpec(
            num_scalar_prefetch=1,
            grid=(n_exp,),
            in_specs=[
                ANY,
                ANY,
                pl.BlockSpec(probs.shape, lambda e, *_: (0, 0, 0), pipeline_mode=one),
                pl.BlockSpec((1, width, inner), lambda e, *_: (e, 0, 0)),
                pl.BlockSpec((1, width, inner), lambda e, *_: (e, 0, 0)),
                pl.BlockSpec((1, inner, width), lambda e, *_: (e, 0, 0)),
            ],
            out_specs=[
                ANY,
                ANY,
                pl.BlockSpec((1, blocks, rows), lambda e, *_: (e, 0, 0)),
            ]
            + [g[1] for g in grads],
            scratch_shapes=[
                pltpu.VMEM((blocks, n_exp, CAP, width), BF16),
                pltpu.VMEM((blocks, n_exp, CAP, width), BF16),
                pltpu.VMEM((blocks, n_exp * CAP, rows), BF16),
                pltpu.VMEM((blocks, n_exp, CAP, 1), F32),
                pltpu.VMEM(full, BF16),
                pltpu.VMEM(full, BF16),
                DMA((2, blocks)),
            ],
        ),
        out_shape=[
            jax.ShapeDtypeStruct(full, BF16),
            jax.ShapeDtypeStruct(full, BF16),
            jax.ShapeDtypeStruct((n_exp, blocks, rows), F32),
        ]
        + [g[0] for g in grads],
        compiler_params=pltpu.CompilerParams(
            vmem_limit_bytes=60 * 2**20, dimension_semantics=("arbitrary",)
        ),
        cost_estimate=cost(65),
    )(core, normed, cot, probs, w_gate, w_up, w_down)


def rms_scale(values):
    return lax.rsqrt(jnp.mean(values * values, axis=-1, keepdims=True) + EPSILON)


def partner(x):
    lane = lax.broadcasted_iota(jnp.int32, x.shape, 1)
    half = HEAD_DIM // 2
    low = lax.rem(lane, HEAD_DIM) < half
    return jnp.where(low, pltpu.roll(x, x.shape[1] - half, 1), pltpu.roll(x, half, 1))


def turn(x, cosine, sine):
    return x * cosine + partner(x) * sine


def project_body(
    tokens_ref, gain_ref, cos_ref, sin_ref, wq_ref, wk_ref, wv_ref, n_ref, q_ref, k_ref, v_ref
):
    x = tokens_ref[...].astype(F32)
    n_ref[...] = (x * rms_scale(x) * gain_ref[...]).astype(BF16)
    normed = n_ref[...]
    cosine, sine = cos_ref[...], sin_ref[...]
    tile = 256
    for w, out, turned in ((wk_ref, k_ref, True), (wv_ref, v_ref, False), (wq_ref, q_ref, True)):
        for c in range(0, w.shape[1], tile):
            y = dot(normed, w[:, c : c + tile])
            if turned:
                for i in range(0, tile, 128):
                    out[:, c + i : c + i + 128] = turn(y[:, i : i + 128], cosine, sine).astype(BF16)
            else:
                out[:, c : c + tile] = y.astype(BF16)


def project(tokens, gain, cosine, sine, w_query, w_key, w_value):
    rows, width = tokens.shape
    shapes = [width, w_query.shape[1], w_key.shape[1], w_value.shape[1]]
    return pl.pallas_call(
        project_body,
        out_shape=[jax.ShapeDtypeStruct((rows, n), BF16) for n in shapes],
        in_specs=[VMEM] * 7,
        out_specs=[VMEM] * 4,
        compiler_params=pltpu.CompilerParams(vmem_limit_bytes=32 * 2**20),
        cost_estimate=cost(5),
    )(tokens, gain, cosine, sine, w_query, w_key, w_value)


def spread(x):
    lane = lax.broadcasted_iota(jnp.int32, (x.shape[0], 128), 1)
    low = lane < HEAD_DIM
    zero = jnp.zeros((), x.dtype)
    first, second = x[:, :128], x[:, 128:]
    return jnp.concatenate(
        [
            jnp.where(low, first, zero),
            jnp.where(low, pltpu.roll(first, HEAD_DIM, 1), zero),
            jnp.where(low, zero, pltpu.roll(second, HEAD_DIM, 1)),
            jnp.where(low, zero, second),
        ],
        axis=0,
    )


def gathered(x, rows):
    lane = lax.broadcasted_iota(jnp.int32, (rows, 128), 1)
    low = lane < HEAD_DIM
    h = [x[i * rows : (i + 1) * rows] for i in range(4)]
    return jnp.concatenate(
        [
            jnp.where(low, h[0], pltpu.roll(h[1], HEAD_DIM, 1)),
            jnp.where(low, pltpu.roll(h[2], HEAD_DIM, 1), h[3]),
        ],
        axis=1,
    )


def window_of(dp, span):
    return jnp.maximum(dp - (span - 1), 0)


def window_scores(dp, span, rows, starts_ref, q, k):
    keys = k.shape[0]
    scores = dot(q, k, ((1,), (1,))).reshape(4, rows, keys)
    key_pos = window_of(dp, span) * rows + lax.broadcasted_iota(jnp.int32, (rows, keys), 1)
    query_pos = dp * rows + lax.broadcasted_iota(jnp.int32, (rows, keys), 0)
    allowed = (key_pos <= query_pos) & (key_pos >= starts_ref[...])
    return jnp.where(allowed[None], scores, MASKED).reshape(4 * rows, keys)


def in_window(ref, dp, span):
    block = ref[pl.ds(window_of(dp, span), span)]
    return block.reshape(span * block.shape[1], block.shape[2])


SCALE = HEAD_DIM ** (-0.5)


def attend_body(span, dp_ref, starts_ref, q_ref, k_ref, v_ref, out_ref, log_ref):
    dp = dp_ref[0]
    rows = q_ref.shape[0]
    q = spread(q_ref[...].astype(F32) * SCALE).astype(BF16)
    scores = window_scores(dp, span, rows, starts_ref, q, in_window(k_ref, dp, span))
    top = jnp.max(scores, axis=1, keepdims=True)
    terms = jnp.exp(scores - top)
    total = jnp.sum(terms, axis=1, keepdims=True)
    log_ref[0, 0] = top + jnp.log(total)
    weights = (terms * (1.0 / total)).astype(BF16)
    out = dot(weights, in_window(v_ref, dp, span))
    out_ref[...] = gathered(out, rows).astype(BF16)


def attention_specs(micro, rows, nd):
    pairs = KV_HEADS // 2
    mine = pl.BlockSpec((rows, 4 * HEAD_DIM), lambda m, h, *_: (m, h))
    theirs = pl.BlockSpec((nd, rows, 2 * HEAD_DIM), lambda m, h, *_: (0, m, h))
    column = pl.BlockSpec((rows, 1), lambda m, h, *_: (m, 0))
    logs = pl.BlockSpec((1, 1, 4 * rows, 1), lambda m, h, *_: (m, h, 0, 0))
    log_shape = jax.ShapeDtypeStruct((micro, pairs, 4 * rows, 1), F32)
    return (micro, pairs), mine, theirs, column, logs, log_shape


def attend(dp, starts, queries, keys, values, micro, rows, nd):
    grid, mine, theirs, column, logs, log_shape = attention_specs(micro, rows, nd)
    return pl.pallas_call(
        functools.partial(attend_body, nd // 2 + 1),
        grid_spec=pltpu.PrefetchScalarGridSpec(
            num_scalar_prefetch=1,
            grid=grid,
            in_specs=[column, mine, theirs, theirs],
            out_specs=[mine, logs],
        ),
        out_shape=[jax.ShapeDtypeStruct(queries.shape, BF16), log_shape],
        compiler_params=pltpu.CompilerParams(vmem_limit_bytes=40 * 2**20),
        cost_estimate=cost(15),
    )(dp.reshape(1), starts, queries, keys, values)


def attend_back_body(
    span, dp_ref, starts_ref, q_ref, k_ref, v_ref, log_ref, g_ref, cos_ref, sin_ref, *outs
):
    dq_ref, dk_ref, dv_ref = outs
    dp = dp_ref[0]
    rows = q_ref.shape[0]
    q = spread(q_ref[...].astype(F32) * SCALE).astype(BF16)
    g = spread(g_ref[...].astype(F32)).astype(BF16)
    k, v = in_window(k_ref, dp, span), in_window(v_ref, dp, span)
    scores = window_scores(dp, span, rows, starts_ref, q, k)
    probs = jnp.exp(scores - log_ref[0, 0])
    grad_probs = dot(g, v, ((1,), (1,)))
    total = jnp.sum(probs * grad_probs, axis=1, keepdims=True)
    grad_scores = (probs * (grad_probs - total)).astype(BF16)
    dq = gathered(dot(grad_scores, k) * SCALE, rows)
    cosine, sine = cos_ref[...], -sin_ref[...]
    for i in range(0, dq.shape[1], 128):
        dq_ref[:, i : i + 128] = turn(dq[:, i : i + 128], cosine, sine).astype(BF16)
    dk_ref[...] = jnp.zeros_like(dk_ref)
    dv_ref[...] = jnp.zeros_like(dv_ref)
    here = pl.ds(window_of(dp, span), span)
    dk = dot(grad_scores, q, ((0,), (0,))).astype(BF16)
    dk_ref[here] = dk.reshape(span, rows, dk.shape[1])
    dv = dot(probs.astype(BF16), g, ((0,), (0,))).astype(BF16)
    dv_ref[here] = dv.reshape(span, rows, dv.shape[1])


def attend_back(dp, starts, queries, keys, values, logs_in, grad, cosine, sine, micro, rows, nd):
    grid, mine, theirs, column, logs, _ = attention_specs(micro, rows, nd)
    table = pl.BlockSpec((rows, 128), lambda m, h, *_: (0, 0))
    return pl.pallas_call(
        functools.partial(attend_back_body, nd // 2 + 1),
        grid_spec=pltpu.PrefetchScalarGridSpec(
            num_scalar_prefetch=1,
            grid=grid,
            in_specs=[column, mine, theirs, theirs, logs, mine, table, table],
            out_specs=[mine, theirs, theirs],
        ),
        out_shape=[
            jax.ShapeDtypeStruct(queries.shape, BF16),
            jax.ShapeDtypeStruct(keys.shape, BF16),
            jax.ShapeDtypeStruct(values.shape, BF16),
        ],
        compiler_params=pltpu.CompilerParams(vmem_limit_bytes=48 * 2**20),
        cost_estimate=cost(25),
    )(dp.reshape(1), starts, queries, keys, values, logs_in, grad, cosine, sine)


def input_body(
    ne,
    nd,
    n_ref,
    dq_ref,
    dk_ref,
    dv_ref,
    cos_ref,
    sin_ref,
    wq_ref,
    wk_ref,
    wv_ref,
    tokens_ref,
    gain_ref,
    res_ref,
    wq_out,
    wk_out,
    wv_out,
    tok_out,
    gain_out,
    dk_turned,
):
    normed = n_ref[...]
    cosine, sine = cos_ref[...], -sin_ref[...]
    for i in range(0, dk_ref.shape[1], 128):
        part = dk_ref[:, i : i + 128].astype(F32)
        dk_turned[:, i : i + 128] = turn(part, cosine, sine).astype(BF16)
    tile = 256
    for grad, out in ((dq_ref, wq_out), (dk_turned, wk_out), (dv_ref, wv_out)):
        share = out.shape[1] // ne
        for c in range(0, grad.shape[1], tile):
            y = dot(normed, grad[:, c : c + tile], ((0,), (0,))).astype(BF16)
            for e in range(ne):
                for d in range(nd):
                    r = (e * nd + d) * share
                    out[d, e * share : (e + 1) * share, c : c + tile] = y[r : r + share]
    back = (
        dot(dq_ref[...], wq_ref[...], ((1,), (1,)))
        + dot(dk_turned[...], wk_ref[...], ((1,), (1,)))
        + dot(dv_ref[...], wv_ref[...], ((1,), (1,)))
    )
    x = tokens_ref[...].astype(F32)
    r = rms_scale(x)
    scaled = back * gain_ref[...]
    gain_out[...] = jnp.sum(back * x * r, axis=0, keepdims=True)
    tok_out[...] = (
        res_ref[...] + r * scaled - x * (r * r * r) * jnp.mean(scaled * x, axis=1, keepdims=True)
    )


def input_grads(ne, nd, normed, dq, dk, dv, cosine, sine, weights, tokens, gain, grad_residual):
    rows, width = tokens.shape
    share = width // (ne * nd)
    return pl.pallas_call(
        functools.partial(input_body, ne, nd),
        out_shape=[jax.ShapeDtypeStruct((nd, ne * share, w.shape[1]), BF16) for w in weights]
        + [
            jax.ShapeDtypeStruct((rows, width), F32),
            jax.ShapeDtypeStruct((1, width), F32),
        ],
        in_specs=[VMEM] * 12,
        out_specs=[VMEM] * 5,
        scratch_shapes=[pltpu.VMEM(dk.shape, BF16)],
        compiler_params=pltpu.CompilerParams(vmem_limit_bytes=48 * 2**20),
        cost_estimate=cost(10),
    )(normed, dq, dk, dv, cosine, sine, *weights, tokens, gain, grad_residual)


def halve(values, dp, orders, nb):
    live = list(range(nb - 1, 0, -1))
    for bit in orders:
        axis = live.index(bit)
        mine = jnp.bitwise_and(lax.shift_right_logical(dp, bit), 1)
        kept = lax.dynamic_index_in_dim(values, mine, axis, keepdims=False)
        sent = lax.dynamic_index_in_dim(values, 1 - mine, axis, keepdims=False)
        n = 1 << nb
        arrived = lax.ppermute(sent, "dp", [(i, i ^ (1 << bit)) for i in range(n)])
        values = (kept.astype(F32) + arrived.astype(F32)).astype(BF16)
        live.remove(bit)
    return values


def reduce_expert(keep, send, dp, nd):
    nb = bit_count(nd)
    arrived = lax.ppermute(send, "dp", [(i, i ^ 1) for i in range(nd)])
    values = (keep.astype(F32) + arrived.astype(F32)).astype(BF16)
    values = values.reshape((2,) * (nb - 1) + values.shape[1:])
    half = keep.shape[1] // 2
    first, second = gather_orders(nd)
    out = []
    for part, order in ((0, first), (1, second)):
        piece = lax.slice_in_dim(values, part * half, (part + 1) * half, axis=nb - 1)
        out.append(halve(piece, dp, order[:-1][::-1], nb))
    return jnp.concatenate(out, axis=0).astype(F32)


def per_device(
    tokens,
    segments,
    routes,
    first_gain,
    w_query,
    w_key,
    w_value,
    w_out,
    second_gain,
    w_router,
    w_gate,
    w_up,
    w_down,
    cotangent,
):
    micro, rows, width = tokens.shape
    ne, nd = lax.axis_size("ep"), lax.axis_size("dp")
    ep, dp = lax.axis_index("ep"), lax.axis_index("dp")
    groups = HEADS // KV_HEADS
    kv_width = KV_HEADS * HEAD_DIM
    every = micro * rows
    inputs = tokens.reshape(every, width).astype(F32)
    grad_output = cotangent.reshape(every, width).astype(F32)

    query_pos = dp * rows + jnp.arange(rows, dtype=jnp.int32)
    halfway = HEAD_DIM // 2
    frequency = ROPE_BASE ** (-(jnp.arange(halfway, dtype=F32) * 2.0 / HEAD_DIM))
    angles = query_pos.astype(F32)[:, None] * frequency[None, :]
    lanes = 2 * HEAD_DIM // halfway
    sign = jnp.where(jnp.arange(2 * HEAD_DIM) % HEAD_DIM < halfway, -1.0, 1.0).astype(F32)
    cosine = jnp.tile(jnp.cos(angles), (micro, lanes))
    sine = jnp.tile(jnp.sin(angles), (micro, lanes)) * sign

    tokens_flat = tokens.reshape(every, width)
    gain_one = first_gain.reshape(1, width)
    normed_one, query_rot, key_rot, value_own = project(
        tokens_flat, gain_one, cosine, sine, w_query, w_key, w_value
    )

    ids = jnp.arange(128, dtype=jnp.int32)
    counts = jnp.sum((segments[:, 0, :, None] == ids).astype(F32), axis=1)
    counts = jnp.concatenate([counts, jnp.zeros((8 - micro, 128), F32)], axis=0)

    key_all, value_all, count_all, cot_all = gather(
        ne, nd, (key_rot, value_own, counts), (cotangent.reshape(every, width),), 0, 40
    )

    totals = jnp.sum(count_all[:, :micro], axis=0)
    lower = (ids[None, None, :] < segments[:, 0, :, None]).astype(F32)
    starts = jnp.sum(lower * totals[:, None, :], axis=2).astype(jnp.int32)
    starts = starts.reshape(every, 1)
    attn_low, logs = attend(dp, starts, query_rot, key_all, value_all, micro, rows, nd)
    residual = inputs + jnp.dot(attn_low, w_out, preferred_element_type=F32)
    inv_two = rms_scale(residual)
    normed_two = (residual * inv_two * second_gain).astype(BF16)
    logits = jnp.dot(normed_two, w_router, preferred_element_type=F32)
    routing = routes.reshape(every, routes.shape[2])
    chosen = jnp.any(
        routing[:, :, None] == jnp.arange(EXPERTS, dtype=jnp.int32)[None, None, :], axis=1
    )
    masked = jnp.where(chosen, logits, MASKED)
    terms = jnp.where(chosen, jnp.exp(masked - jnp.max(masked, axis=1, keepdims=True)), 0.0)
    gate_probs = terms / jnp.sum(terms, axis=1, keepdims=True)
    marked = jnp.where(chosen, gate_probs, -1.0).T

    normed_all, marked_all = gather(ne, nd, (), (normed_two, marked), 1, 38)
    here = EXPERTS // ne
    probs_here = lax.dynamic_slice_in_dim(marked_all, ep * here, here, axis=1)
    probs_here = (
        probs_here.reshape(ne, here, micro, rows)
        .transpose(0, 2, 1, 3)
        .reshape(ne * micro, here, rows)
    )
    core = jnp.bitwise_and(dp, 1).reshape(1)
    mix, grad_in, pair_dots, *grads = experts(
        normed_all.reshape(ne * every, width),
        cot_all.reshape(ne * every, width),
        probs_here,
        w_gate,
        w_up,
        w_down,
        rows,
        nd,
        core,
    )
    grad_w_gate = reduce_expert(grads[0], grads[1], dp, nd)
    grad_w_up = reduce_expert(grads[2], grads[3], dp, nd)
    grad_w_down = reduce_expert(grads[4], grads[5], dp, nd)

    pair_dots = pair_dots.reshape(here, ne, every).transpose(1, 0, 2)
    grad_back, dots_all = reduce(
        ne, nd, (), (grad_in.reshape(ne, every, width),), (pair_dots,), 2, 40
    )
    pair_dot = dots_all.reshape(EXPERTS, every).T
    grad_logits = gate_probs * (
        pair_dot - jnp.sum(gate_probs * pair_dot, axis=1, keepdims=True)
    )
    grad_w_router = jnp.einsum(
        "td,te->de", normed_two.astype(F32), grad_logits, precision=HIGHEST
    )
    grad_normed_two = (
        jnp.einsum("te,de->td", grad_logits, w_router.astype(F32), precision=HIGHEST)
        + grad_back.astype(F32)
    )
    scaled_two = grad_normed_two * second_gain
    grad_gain_two = jnp.sum(grad_normed_two * residual * inv_two, axis=0)
    grad_residual = (
        grad_output
        + inv_two * scaled_two
        - residual * inv_two**3 * jnp.mean(scaled_two * residual, axis=-1, keepdims=True)
    )
    residual_low = grad_residual.astype(BF16)
    grad_w_out = jnp.einsum("tf,td->fd", attn_low, residual_low, preferred_element_type=F32)
    grad_attn = jnp.einsum("td,fd->tf", residual_low, w_out, preferred_element_type=F32).astype(
        BF16
    )
    grad_query, grad_key_all, grad_value_all = attend_back(
        dp,
        starts,
        query_rot,
        key_all,
        value_all,
        logs,
        grad_attn,
        cosine,
        sine,
        micro,
        rows,
        nd,
    )
    grad_key, grad_value, mix_own = reduce(
        ne,
        nd,
        (grad_key_all, grad_value_all),
        (mix.reshape(ne, every, width),),
        (),
        3,
        40,
    )
    output = (residual + mix_own.astype(F32)).astype(BF16).reshape(tokens.shape)
    grad_w_query, grad_w_key, grad_w_value, grad_tokens, grad_gain_one = input_grads(
        ne,
        nd,
        normed_one,
        grad_query,
        grad_key,
        grad_value,
        cosine,
        sine,
        (w_query, w_key, w_value),
        tokens_flat,
        gain_one,
        grad_residual,
    )

    small = jnp.concatenate(
        [
            grad_w_router,
            grad_gain_one.reshape(width, 1),
            grad_gain_two[:, None],
            jnp.zeros((width, 128 - EXPERTS - 2), F32),
        ],
        axis=1,
    )

    def by_owner(grad):
        share = grad.shape[0] // (ne * nd)
        return (
            grad.astype(BF16)
            .reshape(ne, nd, share, grad.shape[1])
            .transpose(1, 0, 2, 3)
            .reshape(nd, ne * share, grad.shape[1])
        )

    dense = reduce(
        ne,
        nd,
        (grad_w_query, by_owner(grad_w_out), grad_w_key, grad_w_value, by_owner(small)),
        (),
        (),
        4,
        45,
    )
    dense = reduce(ne, nd, (), [v.reshape(ne, -1, v.shape[1]) for v in dense], (), 5, 18)
    d_query, d_out, d_key, d_value, d_small = (v.astype(F32) for v in dense)
    return (
        output,
        grad_tokens.reshape(tokens.shape),
        d_small[:, EXPERTS],
        d_query,
        d_key,
        d_value,
        d_out,
        d_small[:, EXPERTS + 1],
        d_small[:, :EXPERTS],
        grad_w_gate,
        grad_w_up,
        grad_w_down,
    )


def solution(mesh):
    in_specs = (
        P(None, ("ep", "dp"), None),
        P(None, "ep", "dp"),
        P(None, ("ep", "dp"), None),
        P(),
        P(),
        P(),
        P(),
        P(),
        P(),
        P(),
        P("ep", None, None),
        P("ep", None, None),
        P("ep", None, None),
        P(None, ("ep", "dp"), None),
    )
    out_specs = (
        P(None, ("ep", "dp"), None),
        P(None, ("ep", "dp"), None),
        P(("ep", "dp")),
        P(("ep", "dp"), None),
        P(("ep", "dp"), None),
        P(("ep", "dp"), None),
        P(("ep", "dp"), None),
        P(("ep", "dp")),
        P(("ep", "dp"), None),
        P("ep", "dp", None),
        P("ep", "dp", None),
        P("ep", "dp", None),
    )
    return jax.shard_map(
        per_device, mesh=mesh, in_specs=in_specs, out_specs=out_specs, check_vma=False
    )
```

```python
import functools

import jax
import jax.numpy as jnp
from jax import lax
from jax.experimental import pallas as pl
from jax.experimental.pallas import tpu as pltpu
from jax.sharding import PartitionSpec as P

HEADS = 16
KV_HEADS = 8
HEAD_DIM = 64
EXPERTS = 32
CAP = 64
EPSILON = 1e-06
ROPE_BASE = 10000.0
MASKED = -1e30
HIGHEST = lax.Precision.HIGHEST
MESH = pl.DeviceIdType.MESH
BF16 = jnp.bfloat16
F32 = jnp.float32
VMEM = pl.BlockSpec(memory_space=pltpu.VMEM)
ANY = pl.BlockSpec(memory_space=pl.ANY)
DMA = pltpu.SemaphoreType.DMA


def bit_count(n):
    return n.bit_length() - 1


def masks(bits):
    out = [0]
    for b in bits:
        out = out + [m | (1 << b) for m in out]
    return out


def gather_orders(n):
    bits = list(range(bit_count(n)))
    return (bits[1:] + bits[:1], bits[:0:-1] + bits[:1])


def greet(ep, dp, ne, nd):
    barrier = pltpu.get_barrier_semaphore()
    for k in range(1, ne):
        pl.semaphore_signal(
            barrier, inc=1, device_id={"ep": lax.rem(ep + k, ne)}, device_id_type=MESH
        )
    for b in range(bit_count(nd)):
        pl.semaphore_signal(
            barrier, inc=1, device_id={"dp": jnp.bitwise_xor(dp, 1 << b)}, device_id_type=MESH
        )
    pl.semaphore_wait(barrier, ne - 1 + bit_count(nd))


def remote(src, dst, send, recv, where):
    return pltpu.make_async_remote_copy(
        src_ref=src, dst_ref=dst, send_sem=send, recv_sem=recv, device_id=where, device_id_type=MESH
    )


def gather_body(ne, nd, n_dp, n_ep, *refs):
    n_in = n_dp + n_ep
    ins, outs, sems = refs[:n_in], refs[n_in : 2 * n_in], refs[2 * n_in :]
    ep, dp = lax.axis_index("ep"), lax.axis_index("dp")
    own_sem, dp_send, dp_recv, ep_send, ep_recv = sems
    greet(ep, dp, ne, nd)
    own = []
    for a in range(n_in):
        me = dp if a < n_dp else ep
        copy = pltpu.make_async_copy(ins[a], outs[a].at[me], own_sem.at[a])
        copy.start()
        own.append(copy)

    def dp_step(t):
        copies = []
        for a in range(n_dp):
            order = gather_orders(nd)[a % 2]
            for j, m in enumerate(masks(order[:t])):
                block = jnp.bitwise_xor(dp, m)
                src = ins[a] if m == 0 else outs[a].at[block]
                k = (1 << t) - 1 + j
                copies.append(
                    remote(
                        src,
                        outs[a].at[block],
                        dp_send.at[a, k],
                        dp_recv.at[a, k],
                        {"dp": jnp.bitwise_xor(dp, 1 << order[t])},
                    )
                )
        for c in copies:
            c.start()
        return copies

    def ep_copy(a, s, way):
        shard = lax.rem(ep - way * s + ne, ne)
        src = ins[n_dp + a] if s == 0 else outs[n_dp + a].at[shard]
        k = 0 if way == 1 else 1
        return remote(
            src,
            outs[n_dp + a].at[shard],
            ep_send.at[a, k, s],
            ep_recv.at[a, k, s],
            {"ep": lax.rem(ep + way + ne, ne)},
        )

    def sends(s, way):
        if way == 1:
            return (ep >= s) & (ep < ne - 1)
        return (ep + s <= ne - 1) & (ep >= 1)

    def receives(s, way):
        if way == 1:
            return ep >= 1 + s
        return ep + 1 + s <= ne - 1

    def ep_start(s):
        for a in range(n_ep):
            for way in (1, -1):

                @pl.when(sends(s, way))
                def _(a=a, way=way):
                    ep_copy(a, s, way).start()

    def ep_wait(s):
        for a in range(n_ep):
            for way in (1, -1):

                @pl.when(receives(s, way))
                def _(a=a, way=way):
                    ep_copy(a, s, way).wait_recv()

    dp_steps = bit_count(nd) if n_dp else 0
    ep_steps = ne - 1 if n_ep else 0
    started = []
    for t in range(max(dp_steps, ep_steps) + 1):
        if 0 < t <= dp_steps:
            for c in started[-1]:
                c.wait_recv()
        if t < dp_steps:
            started.append(dp_step(t))
        if 0 < t <= ep_steps:
            ep_wait(t - 1)
        if t < ep_steps:
            ep_start(t)
    for group in started:
        for c in group:
            c.wait_send()
    for s in range(ep_steps):
        for a in range(n_ep):
            for way in (1, -1):

                @pl.when(sends(s, way))
                def _(a=a, s=s, way=way):
                    ep_copy(a, s, way).wait_send()

    for c in own:
        c.wait()


def cost(us):
    return pl.CostEstimate(flops=0, bytes_accessed=int(us * 3.0e6), transcendentals=0)


def gather(ne, nd, dp_arrays, ep_arrays, collective, us):
    arrays = list(dp_arrays) + list(ep_arrays)
    counts = [nd] * len(dp_arrays) + [ne] * len(ep_arrays)
    a, b = max(len(dp_arrays), 1), max(len(ep_arrays), 1)
    return pl.pallas_call(
        functools.partial(gather_body, ne, nd, len(dp_arrays), len(ep_arrays)),
        out_shape=[
            jax.ShapeDtypeStruct((n,) + v.shape, v.dtype) for n, v in zip(counts, arrays)
        ],
        in_specs=[ANY] * len(arrays),
        out_specs=[ANY] * len(arrays),
        scratch_shapes=[
            DMA((len(arrays),)),
            DMA((a, nd - 1)),
            DMA((a, nd - 1)),
            DMA((b, 2, ne - 1)),
            DMA((b, 2, ne - 1)),
        ],
        compiler_params=pltpu.CompilerParams(
            collective_id=collective, has_side_effects=True, vmem_limit_bytes=8 * 2**20
        ),
        cost_estimate=cost(us),
    )(*arrays)


def reduce_body(ne, nd, n_dp, n_ep, n_swap, *refs):
    n_in = n_dp + n_ep + n_swap
    ins, outs = refs[:n_in], refs[n_in : 2 * n_in]
    rest = refs[2 * n_in :]
    n_sum = n_dp + n_ep
    held = rest[:n_sum]
    landing = rest[n_sum : 2 * n_sum]
    in_sem, dp_send, dp_recv, ep_send, ep_recv, swap_send, swap_recv = rest[2 * n_sum :]
    ep, dp = lax.axis_index("ep"), lax.axis_index("dp")
    loads = []
    for a in range(n_sum):
        copy = pltpu.make_async_copy(ins[a], held[a], in_sem.at[a])
        copy.start()
        loads.append(copy)
    greet(ep, dp, ne, nd)
    swaps = []
    for a in range(n_swap):
        src, dst = ins[n_sum + a], outs[n_sum + a]
        copy = pltpu.make_async_copy(src.at[ep], dst.at[ep], in_sem.at[n_sum + a])
        copy.start()
        loads.append(copy)
        for k in range(1, ne):
            to = lax.rem(ep + k, ne)
            copy = remote(
                src.at[to], dst.at[ep], swap_send.at[a, k - 1], swap_recv.at[a, k - 1], {"ep": to}
            )
            copy.start()
            swaps.append(copy)
    for c in loads:
        c.wait()

    def add(a, block, arrived):
        held[a][block] = (held[a][block].astype(F32) + arrived.astype(F32)).astype(held[a].dtype)

    nb = bit_count(nd)

    def dp_parts(a, t):
        order = gather_orders(nd)[a % 2][::-1]
        bit, left = order[t], order[t + 1 :]
        first = sum(1 << (nb - 1 - i) for i in range(t))
        return bit, [(first + j, m) for j, m in enumerate(masks(left))]

    def dp_copies(a, t):
        bit, parts = dp_parts(a, t)
        partner = jnp.bitwise_xor(dp, 1 << bit)
        return [
            (
                m,
                k,
                remote(
                    held[a].at[jnp.bitwise_xor(partner, m)],
                    landing[a].at[k],
                    dp_send.at[a, k],
                    dp_recv.at[a, k],
                    {"dp": partner},
                ),
            )
            for k, m in parts
        ]

    def ep_copy(a, dest, way):
        k = 0 if way == 1 else 1
        return remote(
            held[n_dp + a].at[dest],
            landing[n_dp + a].at[k, dest],
            ep_send.at[a, k, dest],
            ep_recv.at[a, k, dest],
            {"ep": lax.rem(ep + way + ne, ne)},
        )

    def ep_turn(t, way):
        return ep + ne - 1 - t if way == 1 else ep + t - (ne - 1)

    def ep_has(t, way):
        return ep_turn(t, way) <= ne - 1 if way == 1 else ep_turn(t, way) >= 0

    def ep_inner(way):
        return ep >= 1 if way == 1 else ep <= ne - 2

    def ep_go(t):
        for a in range(n_ep):
            for way in (1, -1):
                dest = ep_turn(t, way)

                @pl.when(ep_has(t, way) & ep_inner(way))
                def _(a=a, way=way, dest=dest):
                    ep_copy(a, dest, way).wait_recv()
                    add(n_dp + a, dest, landing[n_dp + a][0 if way == 1 else 1, dest])

                if t < ne - 1:

                    @pl.when(ep_has(t, way))
                    def _(a=a, way=way, dest=dest):
                        ep_copy(a, dest, way).start()

    dp_steps = nb if n_dp else 0
    ep_steps = ne if n_ep else 0
    started = []
    for t in range(max(dp_steps + 1, ep_steps)):
        if t < ep_steps:
            ep_go(t)

        if 0 < t <= dp_steps:
            for a, group in started[-1]:
                for m, k, c in group:
                    c.wait_recv()
                    add(a, jnp.bitwise_xor(dp, m), landing[a][k])
        if t < dp_steps:
            started.append([(a, dp_copies(a, t)) for a in range(n_dp)])
            for a, group in started[-1]:
                for m, k, c in group:
                    c.start()
    for a in range(n_dp):
        outs[a][...] = held[a][dp]
    for a in range(n_ep):
        outs[n_dp + a][...] = held[n_dp + a][ep]
    for groups in started:
        for a, group in groups:
            for m, k, c in group:
                c.wait_send()
    for t in range(ep_steps - 1):
        for a in range(n_ep):
            for way in (1, -1):
                dest = ep_turn(t, way)

                @pl.when(ep_has(t, way))
                def _(a=a, way=way, dest=dest):
                    ep_copy(a, dest, way).wait_send()

    for c in swaps:
        c.wait()


def reduce(ne, nd, dp_arrays, ep_arrays, swap_arrays, collective, us):
    sums = list(dp_arrays) + list(ep_arrays)
    landing = [(nd - 1,) + v.shape[1:] for v in dp_arrays]
    landing += [(2, ne) + v.shape[1:] for v in ep_arrays]
    a, b, c = (max(len(v), 1) for v in (dp_arrays, ep_arrays, swap_arrays))
    return pl.pallas_call(
        functools.partial(
            reduce_body, ne, nd, len(dp_arrays), len(ep_arrays), len(swap_arrays)
        ),
        out_shape=[jax.ShapeDtypeStruct(v.shape[1:], v.dtype) for v in sums]
        + [jax.ShapeDtypeStruct(v.shape, v.dtype) for v in swap_arrays],
        in_specs=[ANY] * (len(sums) + len(swap_arrays)),
        out_specs=[VMEM] * len(sums) + [ANY] * len(swap_arrays),
        scratch_shapes=[pltpu.VMEM(v.shape, v.dtype) for v in sums]
        + [pltpu.VMEM(s, v.dtype) for s, v in zip(landing, sums)]
        + [
            DMA((len(sums) + len(swap_arrays),)),
            DMA((a, nd - 1)),
            DMA((a, nd - 1)),
            DMA((b, 2, ne)),
            DMA((b, 2, ne)),
            DMA((c, ne - 1)),
            DMA((c, ne - 1)),
        ],
        compiler_params=pltpu.CompilerParams(
            collective_id=collective, has_side_effects=True, vmem_limit_bytes=48 * 2**20
        ),
        cost_estimate=cost(us),
    )(*sums, *swap_arrays)


def dot(a, b, dims=((1,), (0,))):
    return lax.dot_general(a, b, (dims, ((), ())), preferred_element_type=F32)


def expert_body(ne, nd, micro, rows, *refs):
    cots = refs[:ne]
    normed_ref, probs_ref, gate_ref, up_ref, down_ref = refs[ne : ne + 5]
    mix_ref, grad_ref, dots_ref, sums_ref = refs[ne + 5 : ne + 9]
    rows_in, cots_in, picks, weights, first, second, keep, send, arrived = refs[ne + 9 : ne + 18]
    load_sem, store_sem, send_sem, recv_sem, free_sem = refs[ne + 18 :]
    e = pl.program_id(0)
    last = pl.num_programs(0) - 1
    ep, dp = lax.axis_index("ep"), lax.axis_index("dp")
    other = {"dp": jnp.bitwise_xor(dp, 1)}
    every = micro * rows
    blocks = ne * micro
    width = first.shape[1]
    n_exp = rows_in.shape[1]

    def exchange():
        return remote(send, arrived, send_sem, recv_sem, other)

    def loads():
        out = [pltpu.make_async_copy(normed_ref, first, load_sem.at[ne])]
        for k in range(ne):
            at = pl.multiple_of(lax.rem(ep - k + ne, ne) * every, every)
            out.append(
                pltpu.make_async_copy(cots[k], second.at[pl.ds(at, every)], load_sem.at[k])
            )
        return out

    def block_at(s):
        return pl.ds(pl.multiple_of(s * rows, rows), rows)

    def returned(t):
        k, m = t // micro, lax.rem(t, micro)
        return lax.rem(ep + k, ne) * micro + m

    def stores(t):
        s = returned(t)
        return (
            pltpu.make_async_copy(
                first.at[block_at(s)], mix_ref.at[block_at(t)], store_sem.at[0, t]
            ),
            pltpu.make_async_copy(
                second.at[block_at(s)], grad_ref.at[block_at(s)], store_sem.at[1, t]
            ),
        )

    def collect():
        exchange().wait_recv()
        sums_ref[:, 0] = (keep[...].astype(F32) + arrived[...].astype(F32)).astype(BF16)

    @pl.when(e == 0)
    def _():
        for copy in loads():
            copy.start()
        barrier = pltpu.get_barrier_semaphore()
        pl.semaphore_signal(barrier, inc=1, device_id=other, device_id_type=MESH)
        pl.semaphore_wait(barrier, 1)
        before = lax.broadcasted_iota(jnp.int32, (rows, rows), 0)
        after = lax.broadcasted_iota(jnp.int32, (rows, rows), 1)
        earlier = (before < after).astype(BF16)
        slot = lax.broadcasted_iota(jnp.int32, (n_exp, CAP, rows), 1)
        for copy in loads():
            copy.wait()

        @pl.loop(0, blocks)
        def _(s):
            at = block_at(s)
            probs = probs_ref[s]
            hit = probs >= 0.0
            rank = dot(hit.astype(BF16), earlier)
            rank = jnp.where(hit, rank, -1.0).astype(jnp.int32)
            pick = jnp.broadcast_to(rank[:, None, :], (n_exp, CAP, rows)) == slot
            pick_f = pick.astype(F32)
            share = jnp.sum(pick_f * probs[:, None, :], axis=2, keepdims=True)
            weights[s] = share
            flat = pick_f.reshape(n_exp * CAP, rows).astype(BF16)
            picks[s] = flat
            rows_in[s] = dot(flat, first[at, :]).astype(BF16).reshape(n_exp, CAP, width)
            cots_in[s] = dot(flat, second[at, :]).astype(BF16).reshape(n_exp, CAP, width)

    @pl.when(e < last)
    def _():
        x = rows_in[:, e].reshape(blocks * CAP, width)
        c = cots_in[:, e].reshape(blocks * CAP, width)
        p = weights[:, e].reshape(blocks * CAP, 1)
        w_gate, w_up, w_down = gate_ref[0], up_ref[0], down_ref[0]
        gate_pre = dot(x, w_gate)
        up_pre = dot(x, w_up)
        sigma = jax.nn.sigmoid(gate_pre)
        silu = gate_pre * sigma
        hidden = (silu * up_pre).astype(BF16)
        out = dot(hidden, w_down) * p
        back = dot(c, w_down, ((1,), (1,)))
        wide = hidden.astype(F32)
        pair = jnp.sum(wide * back, axis=1, keepdims=True)
        back = back * p
        grad_up = (back * silu).astype(BF16)
        grad_gate = (back * up_pre * (sigma * (1.0 + gate_pre * (1.0 - sigma)))).astype(BF16)
        scaled = (wide * p).astype(BF16)
        grad_x = dot(grad_gate, w_gate, ((1,), (1,))) + dot(grad_up, w_up, ((1,), (1,)))

        flat = picks[:, pl.ds(pl.multiple_of(e * CAP, CAP), CAP), :].astype(F32)
        dots_ref[0] = jnp.sum(flat * pair.reshape(blocks, CAP, 1), axis=1)

        @pl.when(e > 0)
        def _():
            collect()
            pl.semaphore_signal(free_sem, inc=1, device_id=other, device_id_type=MESH)
            exchange().wait_send()
            pl.semaphore_wait(free_sem, 1)

        def split(value, offset):
            value = value.astype(BF16)
            piece, columns = value.shape[0] // nd, keep.shape[2]

            def put(even, odd):
                for i in range(nd):
                    ref = odd if i % 2 else even
                    for j in range(value.shape[1] // columns):
                        at = offset + j * piece
                        ref[i // 2, at : at + piece] = value[
                            i * piece : (i + 1) * piece, j * columns : (j + 1) * columns
                        ]

            @pl.when(jnp.bitwise_and(dp, 1) == 0)
            def _():
                put(keep, send)

            @pl.when(jnp.bitwise_and(dp, 1) == 1)
            def _():
                put(send, keep)

        share = width // nd
        split(dot(scaled, c, ((0,), (0,))), 2 * share)
        split(dot(x, grad_gate, ((0,), (0,))), 0)
        split(dot(x, grad_up, ((0,), (0,))), share)
        exchange().start()

        rows_in[:, e] = grad_x.astype(BF16).reshape(blocks, CAP, width)
        cots_in[:, e] = out.astype(BF16).reshape(blocks, CAP, width)

    @pl.when(e == last)
    def _():
        @pl.loop(0, blocks)
        def _(t):
            s = returned(t)
            at = block_at(s)
            flat = picks[s]
            first[at, :] = dot(
                flat, cots_in[s].reshape(n_exp * CAP, width), ((0,), (0,))
            ).astype(BF16)
            second[at, :] = dot(
                flat, rows_in[s].reshape(n_exp * CAP, width), ((0,), (0,))
            ).astype(BF16)
            for copy in stores(t):
                copy.start()

        collect()
        exchange().wait_send()

        @pl.loop(0, blocks)
        def _(t):
            for copy in stores(t):
                copy.wait()


def experts(normed, cots, probs, w_gate, w_up, w_down, micro, rows, ne, nd, collective):
    n_exp, width, inner = w_gate.shape
    blocks = ne * micro
    half = nd // 2
    packed = 2 * width // nd + (inner // nd) * (width // inner)
    full = (blocks * rows, width)
    one = pl.Buffered(1)
    weight = lambda e: (jnp.minimum(e, n_exp - 1), 0, 0)
    return pl.pallas_call(
        functools.partial(expert_body, ne, nd, micro, rows),
        grid=(n_exp + 1,),
        in_specs=[ANY] * (ne + 1)
        + [
            pl.BlockSpec(probs.shape, lambda e: (0, 0, 0), pipeline_mode=one),
            pl.BlockSpec((1, width, inner), weight),
            pl.BlockSpec((1, width, inner), weight),
            pl.BlockSpec((1, inner, width), weight),
        ],
        out_specs=[
            ANY,
            ANY,
            pl.BlockSpec((1, blocks, rows), weight),
            pl.BlockSpec((half, 1, packed, inner), lambda e: (0, jnp.maximum(e - 1, 0), 0, 0)),
        ],
        scratch_shapes=[
            pltpu.VMEM((blocks, n_exp, CAP, width), BF16),
            pltpu.VMEM((blocks, n_exp, CAP, width), BF16),
            pltpu.VMEM((blocks, n_exp * CAP, rows), BF16),
            pltpu.VMEM((blocks, n_exp, CAP, 1), F32),
            pltpu.VMEM(full, BF16),
            pltpu.VMEM(full, BF16),
            pltpu.VMEM((half, packed, inner), BF16),
            pltpu.VMEM((half, packed, inner), BF16),
            pltpu.VMEM((half, packed, inner), BF16),
            DMA((ne + 1,)),
            DMA((2, blocks)),
            DMA,
            DMA,
            pltpu.SemaphoreType.REGULAR,
        ],
        out_shape=[
            jax.ShapeDtypeStruct(full, BF16),
            jax.ShapeDtypeStruct(full, BF16),
            jax.ShapeDtypeStruct((n_exp, blocks, rows), F32),
            jax.ShapeDtypeStruct((half, n_exp, packed, inner), BF16),
        ],
        compiler_params=pltpu.CompilerParams(
            vmem_limit_bytes=62 * 2**20,
            dimension_semantics=("arbitrary",),
            collective_id=collective,
            has_side_effects=True,
        ),
        cost_estimate=cost(65),
    )(*cots, normed, probs, w_gate, w_up, w_down)


def rms_scale(values):
    return lax.rsqrt(jnp.mean(values * values, axis=-1, keepdims=True) + EPSILON)


def partner(x):
    lane = lax.broadcasted_iota(jnp.int32, x.shape, 1)
    half = HEAD_DIM // 2
    low = lax.rem(lane, HEAD_DIM) < half
    return jnp.where(low, pltpu.roll(x, x.shape[1] - half, 1), pltpu.roll(x, half, 1))


def turn(x, cosine, sine):
    return x * cosine + partner(x) * sine


def project_body(
    tokens_ref, gain_ref, cos_ref, sin_ref, wq_ref, wk_ref, wv_ref, n_ref, q_ref, k_ref, v_ref
):
    x = tokens_ref[...].astype(F32)
    n_ref[...] = (x * rms_scale(x) * gain_ref[...]).astype(BF16)
    normed = n_ref[...]
    cosine, sine = cos_ref[...], sin_ref[...]
    tile = 256
    for w, out, turned in ((wk_ref, k_ref, True), (wv_ref, v_ref, False), (wq_ref, q_ref, True)):
        for c in range(0, w.shape[1], tile):
            y = dot(normed, w[:, c : c + tile])
            if turned:
                for i in range(0, tile, 128):
                    out[:, c + i : c + i + 128] = turn(y[:, i : i + 128], cosine, sine).astype(BF16)
            else:
                out[:, c : c + tile] = y.astype(BF16)


def project(tokens, gain, cosine, sine, w_query, w_key, w_value):
    rows, width = tokens.shape
    shapes = [width, w_query.shape[1], w_key.shape[1], w_value.shape[1]]
    return pl.pallas_call(
        project_body,
        out_shape=[jax.ShapeDtypeStruct((rows, n), BF16) for n in shapes],
        in_specs=[VMEM] * 7,
        out_specs=[VMEM] * 4,
        compiler_params=pltpu.CompilerParams(vmem_limit_bytes=32 * 2**20),
        cost_estimate=cost(5),
    )(tokens, gain, cosine, sine, w_query, w_key, w_value)


def spread(x):
    lane = lax.broadcasted_iota(jnp.int32, (x.shape[0], 128), 1)
    low = lane < HEAD_DIM
    zero = jnp.zeros((), x.dtype)
    first, second = x[:, :128], x[:, 128:]
    return jnp.concatenate(
        [
            jnp.where(low, first, zero),
            jnp.where(low, pltpu.roll(first, HEAD_DIM, 1), zero),
            jnp.where(low, zero, pltpu.roll(second, HEAD_DIM, 1)),
            jnp.where(low, zero, second),
        ],
        axis=0,
    )


def gathered(x, rows):
    lane = lax.broadcasted_iota(jnp.int32, (rows, 128), 1)
    low = lane < HEAD_DIM
    h = [x[i * rows : (i + 1) * rows] for i in range(4)]
    return jnp.concatenate(
        [
            jnp.where(low, h[0], pltpu.roll(h[1], HEAD_DIM, 1)),
            jnp.where(low, pltpu.roll(h[2], HEAD_DIM, 1), h[3]),
        ],
        axis=1,
    )


def window_of(dp, span):
    return jnp.maximum(dp - (span - 1), 0)


def window_scores(dp, span, rows, starts_ref, q, k):
    keys = k.shape[0]
    scores = dot(q, k, ((1,), (1,))).reshape(4, rows, keys)
    key_pos = window_of(dp, span) * rows + lax.broadcasted_iota(jnp.int32, (rows, keys), 1)
    query_pos = dp * rows + lax.broadcasted_iota(jnp.int32, (rows, keys), 0)
    allowed = (key_pos <= query_pos) & (key_pos >= starts_ref[...])
    return jnp.where(allowed[None], scores, MASKED).reshape(4 * rows, keys)


def in_window(ref, dp, span):
    block = ref[pl.ds(window_of(dp, span), span)]
    return block.reshape(span * block.shape[1], block.shape[2])


SCALE = HEAD_DIM ** (-0.5)


def attend_body(span, dp_ref, starts_ref, q_ref, k_ref, v_ref, out_ref, log_ref):
    dp = dp_ref[0]
    rows = q_ref.shape[0]
    q = spread(q_ref[...].astype(F32) * SCALE).astype(BF16)
    scores = window_scores(dp, span, rows, starts_ref, q, in_window(k_ref, dp, span))
    top = jnp.max(scores, axis=1, keepdims=True)
    terms = jnp.exp(scores - top)
    total = jnp.sum(terms, axis=1, keepdims=True)
    log_ref[0, 0] = top + jnp.log(total)
    weights = (terms * (1.0 / total)).astype(BF16)
    out = dot(weights, in_window(v_ref, dp, span))
    out_ref[...] = gathered(out, rows).astype(BF16)


def attention_specs(micro, rows, nd):
    pairs = KV_HEADS // 2
    mine = pl.BlockSpec((rows, 4 * HEAD_DIM), lambda m, h, *_: (m, h))
    theirs = pl.BlockSpec((nd, rows, 2 * HEAD_DIM), lambda m, h, *_: (0, m, h))
    column = pl.BlockSpec((rows, 1), lambda m, h, *_: (m, 0))
    logs = pl.BlockSpec((1, 1, 4 * rows, 1), lambda m, h, *_: (m, h, 0, 0))
    log_shape = jax.ShapeDtypeStruct((micro, pairs, 4 * rows, 1), F32)
    return (micro, pairs), mine, theirs, column, logs, log_shape


def attend(dp, starts, queries, keys, values, micro, rows, nd):
    grid, mine, theirs, column, logs, log_shape = attention_specs(micro, rows, nd)
    return pl.pallas_call(
        functools.partial(attend_body, nd // 2 + 1),
        grid_spec=pltpu.PrefetchScalarGridSpec(
            num_scalar_prefetch=1,
            grid=grid,
            in_specs=[column, mine, theirs, theirs],
            out_specs=[mine, logs],
        ),
        out_shape=[jax.ShapeDtypeStruct(queries.shape, BF16), log_shape],
        compiler_params=pltpu.CompilerParams(vmem_limit_bytes=40 * 2**20),
        cost_estimate=cost(15),
    )(dp.reshape(1), starts, queries, keys, values)


def attend_back_body(
    span, dp_ref, starts_ref, q_ref, k_ref, v_ref, log_ref, g_ref, cos_ref, sin_ref, *outs
):
    dq_ref, dk_ref, dv_ref = outs
    dp = dp_ref[0]
    rows = q_ref.shape[0]
    q = spread(q_ref[...].astype(F32) * SCALE).astype(BF16)
    g = spread(g_ref[...].astype(F32)).astype(BF16)
    k, v = in_window(k_ref, dp, span), in_window(v_ref, dp, span)
    scores = window_scores(dp, span, rows, starts_ref, q, k)
    probs = jnp.exp(scores - log_ref[0, 0])
    grad_probs = dot(g, v, ((1,), (1,)))
    total = jnp.sum(probs * grad_probs, axis=1, keepdims=True)
    grad_scores = (probs * (grad_probs - total)).astype(BF16)
    dq = gathered(dot(grad_scores, k) * SCALE, rows)
    cosine, sine = cos_ref[...], -sin_ref[...]
    for i in range(0, dq.shape[1], 128):
        dq_ref[:, i : i + 128] = turn(dq[:, i : i + 128], cosine, sine).astype(BF16)
    dk_ref[...] = jnp.zeros_like(dk_ref)
    dv_ref[...] = jnp.zeros_like(dv_ref)
    here = pl.ds(window_of(dp, span), span)
    dk = dot(grad_scores, q, ((0,), (0,))).astype(BF16)
    dk_ref[here] = dk.reshape(span, rows, dk.shape[1])
    dv = dot(probs.astype(BF16), g, ((0,), (0,))).astype(BF16)
    dv_ref[here] = dv.reshape(span, rows, dv.shape[1])


def attend_back(dp, starts, queries, keys, values, logs_in, grad, cosine, sine, micro, rows, nd):
    grid, mine, theirs, column, logs, _ = attention_specs(micro, rows, nd)
    table = pl.BlockSpec((rows, 128), lambda m, h, *_: (0, 0))
    return pl.pallas_call(
        functools.partial(attend_back_body, nd // 2 + 1),
        grid_spec=pltpu.PrefetchScalarGridSpec(
            num_scalar_prefetch=1,
            grid=grid,
            in_specs=[column, mine, theirs, theirs, logs, mine, table, table],
            out_specs=[mine, theirs, theirs],
        ),
        out_shape=[
            jax.ShapeDtypeStruct(queries.shape, BF16),
            jax.ShapeDtypeStruct(keys.shape, BF16),
            jax.ShapeDtypeStruct(values.shape, BF16),
        ],
        compiler_params=pltpu.CompilerParams(vmem_limit_bytes=48 * 2**20),
        cost_estimate=cost(25),
    )(dp.reshape(1), starts, queries, keys, values, logs_in, grad, cosine, sine)


def input_body(
    ne,
    nd,
    n_ref,
    dq_ref,
    dk_ref,
    dv_ref,
    cos_ref,
    sin_ref,
    wq_ref,
    wk_ref,
    wv_ref,
    tokens_ref,
    gain_ref,
    res_ref,
    wq_out,
    wk_out,
    wv_out,
    tok_out,
    gain_out,
    dk_turned,
):
    normed = n_ref[...]
    cosine, sine = cos_ref[...], -sin_ref[...]
    for i in range(0, dk_ref.shape[1], 128):
        part = dk_ref[:, i : i + 128].astype(F32)
        dk_turned[:, i : i + 128] = turn(part, cosine, sine).astype(BF16)
    tile = 256
    for grad, out in ((dq_ref, wq_out), (dk_turned, wk_out), (dv_ref, wv_out)):
        share = out.shape[1] // ne
        for c in range(0, grad.shape[1], tile):
            y = dot(normed, grad[:, c : c + tile], ((0,), (0,))).astype(BF16)
            for e in range(ne):
                for d in range(nd):
                    r = (e * nd + d) * share
                    out[d, e * share : (e + 1) * share, c : c + tile] = y[r : r + share]
    back = (
        dot(dq_ref[...], wq_ref[...], ((1,), (1,)))
        + dot(dk_turned[...], wk_ref[...], ((1,), (1,)))
        + dot(dv_ref[...], wv_ref[...], ((1,), (1,)))
    )
    x = tokens_ref[...].astype(F32)
    r = rms_scale(x)
    scaled = back * gain_ref[...]
    gain_out[...] = jnp.sum(back * x * r, axis=0, keepdims=True)
    tok_out[...] = (
        res_ref[...] + r * scaled - x * (r * r * r) * jnp.mean(scaled * x, axis=1, keepdims=True)
    )


def input_grads(ne, nd, normed, dq, dk, dv, cosine, sine, weights, tokens, gain, grad_residual):
    rows, width = tokens.shape
    share = width // (ne * nd)
    return pl.pallas_call(
        functools.partial(input_body, ne, nd),
        out_shape=[jax.ShapeDtypeStruct((nd, ne * share, w.shape[1]), BF16) for w in weights]
        + [
            jax.ShapeDtypeStruct((rows, width), F32),
            jax.ShapeDtypeStruct((1, width), F32),
        ],
        in_specs=[VMEM] * 12,
        out_specs=[VMEM] * 5,
        scratch_shapes=[pltpu.VMEM(dk.shape, BF16)],
        compiler_params=pltpu.CompilerParams(vmem_limit_bytes=48 * 2**20),
        cost_estimate=cost(10),
    )(normed, dq, dk, dv, cosine, sine, *weights, tokens, gain, grad_residual)


def halves(values, dp, axis, bit, part, parts_axis):
    count = values.shape[parts_axis] // 2
    values = lax.slice_in_dim(values, part * count, (part + 1) * count, axis=parts_axis)
    mine = jnp.bitwise_and(lax.shift_right_logical(dp, bit), 1)
    kept = lax.dynamic_index_in_dim(values, mine, axis, keepdims=False)
    sent = lax.dynamic_index_in_dim(values, 1 - mine, axis, keepdims=False)
    return kept, sent


def swap_bit(sent, bit, nd):
    return lax.ppermute(sent, "dp", [(i, i ^ (1 << bit)) for i in range(nd)])


def plus(a, b):
    return (a.astype(F32) + b.astype(F32)).astype(BF16)


def tie(value, *others):
    return lax.optimization_barrier((value,) + others)


def per_device(
    tokens,
    segments,
    routes,
    first_gain,
    w_query,
    w_key,
    w_value,
    w_out,
    second_gain,
    w_router,
    w_gate,
    w_up,
    w_down,
    cotangent,
):
    micro, rows, width = tokens.shape
    ne, nd = lax.axis_size("ep"), lax.axis_size("dp")
    ep, dp = lax.axis_index("ep"), lax.axis_index("dp")
    groups = HEADS // KV_HEADS
    kv_width = KV_HEADS * HEAD_DIM
    every = micro * rows
    inputs = tokens.reshape(every, width).astype(F32)
    grad_output = cotangent.reshape(every, width).astype(F32)

    query_pos = dp * rows + jnp.arange(rows, dtype=jnp.int32)
    halfway = HEAD_DIM // 2
    frequency = ROPE_BASE ** (-(jnp.arange(halfway, dtype=F32) * 2.0 / HEAD_DIM))
    angles = query_pos.astype(F32)[:, None] * frequency[None, :]
    lanes = 2 * HEAD_DIM // halfway
    sign = jnp.where(jnp.arange(2 * HEAD_DIM) % HEAD_DIM < halfway, -1.0, 1.0).astype(F32)
    cosine = jnp.tile(jnp.cos(angles), (micro, lanes))
    sine = jnp.tile(jnp.sin(angles), (micro, lanes)) * sign

    tokens_flat = tokens.reshape(every, width)
    gain_one = first_gain.reshape(1, width)
    normed_one, query_rot, key_rot, value_own = project(
        tokens_flat, gain_one, cosine, sine, w_query, w_key, w_value
    )

    ids = jnp.arange(128, dtype=jnp.int32)
    counts = jnp.sum((segments[:, 0, :, None] == ids).astype(F32), axis=1)
    counts = jnp.concatenate([counts, jnp.zeros((8 - micro, 128), F32)], axis=0)

    cot_own = cotangent.reshape(every, width)

    def around(value, k):
        return lax.ppermute(value, "ep", [(i, (i + k) % ne) for i in range(ne)])

    cots = [cot_own] + [around(cot_own, k) for k in range(1, ne)]
    key_all, value_all, count_all = gather(ne, nd, (key_rot, value_own, counts), (), 0, 25)

    totals = jnp.sum(count_all[:, :micro], axis=0)
    lower = (ids[None, None, :] < segments[:, 0, :, None]).astype(F32)
    starts = jnp.sum(lower * totals[:, None, :], axis=2).astype(jnp.int32)
    starts = starts.reshape(every, 1)
    attn_low, logs = attend(dp, starts, query_rot, key_all, value_all, micro, rows, nd)
    residual = inputs + jnp.dot(attn_low, w_out, preferred_element_type=F32)
    inv_two = rms_scale(residual)
    normed_two = (residual * inv_two * second_gain).astype(BF16)
    logits = jnp.dot(normed_two, w_router, preferred_element_type=F32)
    routing = routes.reshape(every, routes.shape[2])
    chosen = jnp.any(
        routing[:, :, None] == jnp.arange(EXPERTS, dtype=jnp.int32)[None, None, :], axis=1
    )
    masked = jnp.where(chosen, logits, MASKED)
    terms = jnp.where(chosen, jnp.exp(masked - jnp.max(masked, axis=1, keepdims=True)), 0.0)
    gate_probs = terms / jnp.sum(terms, axis=1, keepdims=True)
    marked = jnp.where(chosen, gate_probs, -1.0).T

    normed_all, marked_all = gather(ne, nd, (), (normed_two, marked), 1, 38)
    here = EXPERTS // ne
    probs_here = lax.dynamic_slice_in_dim(marked_all, ep * here, here, axis=1)
    probs_here = (
        probs_here.reshape(ne, here, micro, rows)
        .transpose(0, 2, 1, 3)
        .reshape(ne * micro, here, rows)
    )
    mix, grad_in, pair_dots, sums = experts(
        normed_all.reshape(ne * every, width),
        cots,
        probs_here,
        w_gate,
        w_up,
        w_down,
        micro,
        rows,
        ne,
        nd,
        6,
    )
    nb = bit_count(nd)
    sums = sums.reshape((2,) * (nb - 1) + sums.shape[1:])
    orders = [order[:-1][::-1] for order in gather_orders(nd)]
    first_kept, first_sent = zip(
        *[halves(sums, dp, nb - 1 - orders[i][0], orders[i][0], i, nb - 1) for i in range(2)]
    )
    grad_in, *first_sent = tie(grad_in, *first_sent)
    first_arrived = [swap_bit(v, orders[i][0], nd) for i, v in enumerate(first_sent)]

    pair_dots = pair_dots.reshape(here, ne, every).transpose(1, 0, 2)
    grad_back, dots_all = reduce(
        ne, nd, (), (grad_in.reshape(ne, every, width),), (pair_dots,), 2, 40
    )
    pair_dot = dots_all.reshape(EXPERTS, every).T
    grad_logits = gate_probs * (
        pair_dot - jnp.sum(gate_probs * pair_dot, axis=1, keepdims=True)
    )
    grad_w_router = jnp.einsum(
        "td,te->de", normed_two.astype(F32), grad_logits, precision=HIGHEST
    )
    grad_normed_two = (
        jnp.einsum("te,de->td", grad_logits, w_router.astype(F32), precision=HIGHEST)
        + grad_back.astype(F32)
    )
    scaled_two = grad_normed_two * second_gain
    grad_gain_two = jnp.sum(grad_normed_two * residual * inv_two, axis=0)
    grad_residual = (
        grad_output
        + inv_two * scaled_two
        - residual * inv_two**3 * jnp.mean(scaled_two * residual, axis=-1, keepdims=True)
    )
    residual_low = grad_residual.astype(BF16)
    grad_w_out = jnp.einsum("tf,td->fd", attn_low, residual_low, preferred_element_type=F32)
    grad_attn = jnp.einsum("td,fd->tf", residual_low, w_out, preferred_element_type=F32).astype(
        BF16
    )
    grad_query, grad_key_all, grad_value_all = attend_back(
        dp,
        starts,
        query_rot,
        key_all,
        value_all,
        logs,
        grad_attn,
        cosine,
        sine,
        micro,
        rows,
        nd,
    )
    mix = mix.reshape(ne, every, width)
    mix_parts = [mix[0]] + [around(mix[k], k) for k in range(1, ne)]
    grad_key, grad_value = reduce(ne, nd, (grad_key_all, grad_value_all), (), (), 3, 25)

    grads = []
    for i in range(2):
        value, bits = plus(first_kept[i], first_arrived[i]), orders[i]
        live = [b for b in range(nb - 1, 0, -1) if b != bits[0]]
        for bit in bits[1:]:
            axis = live.index(bit)
            mine = jnp.bitwise_and(lax.shift_right_logical(dp, bit), 1)
            kept = lax.dynamic_index_in_dim(value, mine, axis, keepdims=False)
            sent = lax.dynamic_index_in_dim(value, 1 - mine, axis, keepdims=False)
            grad_key, sent = tie(grad_key, sent)
            value = plus(kept, swap_bit(sent, bit, nd))
            live.remove(bit)
        grads.append(value)
    grads = jnp.concatenate(grads, axis=0).astype(F32)
    share = width // nd
    grad_w_gate, grad_w_up = grads[:, :share], grads[:, share : 2 * share]
    grad_w_down = jnp.concatenate(
        [
            grads[:, at : at + w_down.shape[1] // nd]
            for at in range(2 * share, grads.shape[1], w_down.shape[1] // nd)
        ],
        axis=2,
    )
    output = residual + sum(v.astype(F32) for v in mix_parts)
    output = output.astype(BF16).reshape(tokens.shape)
    grad_w_query, grad_w_key, grad_w_value, grad_tokens, grad_gain_one = input_grads(
        ne,
        nd,
        normed_one,
        grad_query,
        grad_key,
        grad_value,
        cosine,
        sine,
        (w_query, w_key, w_value),
        tokens_flat,
        gain_one,
        grad_residual,
    )

    small = jnp.concatenate(
        [
            grad_w_router,
            grad_gain_one.reshape(width, 1),
            grad_gain_two[:, None],
            jnp.zeros((width, 128 - EXPERTS - 2), F32),
        ],
        axis=1,
    )

    def by_owner(grad):
        share = grad.shape[0] // (ne * nd)
        return (
            grad.astype(BF16)
            .reshape(ne, nd, share, grad.shape[1])
            .transpose(1, 0, 2, 3)
            .reshape(nd, ne * share, grad.shape[1])
        )

    dense = reduce(
        ne,
        nd,
        (grad_w_query, by_owner(grad_w_out), grad_w_key, grad_w_value, by_owner(small)),
        (),
        (),
        4,
        45,
    )
    dense = reduce(ne, nd, (), [v.reshape(ne, -1, v.shape[1]) for v in dense], (), 5, 18)
    d_query, d_out, d_key, d_value, d_small = (v.astype(F32) for v in dense)
    return (
        output,
        grad_tokens.reshape(tokens.shape),
        d_small[:, EXPERTS],
        d_query,
        d_key,
        d_value,
        d_out,
        d_small[:, EXPERTS + 1],
        d_small[:, :EXPERTS],
        grad_w_gate,
        grad_w_up,
        grad_w_down,
    )


def solution(mesh):
    in_specs = (
        P(None, ("ep", "dp"), None),
        P(None, "ep", "dp"),
        P(None, ("ep", "dp"), None),
        P(),
        P(),
        P(),
        P(),
        P(),
        P(),
        P(),
        P("ep", None, None),
        P("ep", None, None),
        P("ep", None, None),
        P(None, ("ep", "dp"), None),
    )
    out_specs = (
        P(None, ("ep", "dp"), None),
        P(None, ("ep", "dp"), None),
        P(("ep", "dp")),
        P(("ep", "dp"), None),
        P(("ep", "dp"), None),
        P(("ep", "dp"), None),
        P(("ep", "dp"), None),
        P(("ep", "dp")),
        P(("ep", "dp"), None),
        P("ep", "dp", None),
        P("ep", "dp", None),
        P("ep", "dp", None),
    )
    return jax.shard_map(
        per_device, mesh=mesh, in_specs=in_specs, out_specs=out_specs, check_vma=False
    )
```

```python
import functools

import jax
import jax.numpy as jnp
from jax import lax
from jax.experimental import pallas as pl
from jax.experimental.pallas import tpu as pltpu
from jax.sharding import PartitionSpec as P

HEADS = 16
KV_HEADS = 8
HEAD_DIM = 64
EXPERTS = 32
CAP = 64
EPSILON = 1e-06
ROPE_BASE = 10000.0
MASKED = -1e30
HIGHEST = lax.Precision.HIGHEST
MESH = pl.DeviceIdType.MESH
BF16 = jnp.bfloat16
F32 = jnp.float32
VMEM = pl.BlockSpec(memory_space=pltpu.VMEM)
ANY = pl.BlockSpec(memory_space=pl.ANY)
DMA = pltpu.SemaphoreType.DMA


def bit_count(n):
    return n.bit_length() - 1


def masks(bits):
    out = [0]
    for b in bits:
        out = out + [m | (1 << b) for m in out]
    return out


def gather_orders(n):
    bits = list(range(bit_count(n)))
    return (bits[1:] + bits[:1], bits[:0:-1] + bits[:1])


def greet(ep, dp, ne, nd):
    barrier = pltpu.get_barrier_semaphore()
    for k in range(1, ne):
        pl.semaphore_signal(
            barrier, inc=1, device_id={"ep": lax.rem(ep + k, ne)}, device_id_type=MESH
        )
    for b in range(bit_count(nd)):
        pl.semaphore_signal(
            barrier, inc=1, device_id={"dp": jnp.bitwise_xor(dp, 1 << b)}, device_id_type=MESH
        )
    pl.semaphore_wait(barrier, ne - 1 + bit_count(nd))


def remote(src, dst, send, recv, where):
    return pltpu.make_async_remote_copy(
        src_ref=src, dst_ref=dst, send_sem=send, recv_sem=recv, device_id=where, device_id_type=MESH
    )


def gather_body(ne, nd, n_dp, n_ep, *refs):
    n_in = n_dp + n_ep
    ins, outs, sems = refs[:n_in], refs[n_in : 2 * n_in], refs[2 * n_in :]
    ep, dp = lax.axis_index("ep"), lax.axis_index("dp")
    own_sem, dp_send, dp_recv, ep_send, ep_recv = sems
    greet(ep, dp, ne, nd)
    own = []
    for a in range(n_in):
        me = dp if a < n_dp else ep
        copy = pltpu.make_async_copy(ins[a], outs[a].at[me], own_sem.at[a])
        copy.start()
        own.append(copy)

    def dp_copy(a, t, m):
        order = gather_orders(nd)[a % 2]
        block = jnp.bitwise_xor(dp, m)
        k = (1 << t) - 1 + masks(order[:t]).index(m)
        return remote(
            ins[a] if m == 0 else outs[a].at[block],
            outs[a].at[block],
            dp_send.at[a, k],
            dp_recv.at[a, k],
            {"dp": jnp.bitwise_xor(dp, 1 << order[t])},
        )

    def ep_copy(a, s, way):
        shard = lax.rem(ep - way * s + ne, ne)
        src = ins[n_dp + a] if s == 0 else outs[n_dp + a].at[shard]
        k = 0 if way == 1 else 1
        return remote(
            src,
            outs[n_dp + a].at[shard],
            ep_send.at[a, k, s],
            ep_recv.at[a, k, s],
            {"ep": lax.rem(ep + way + ne, ne)},
        )

    def sends(s, way):
        if way == 1:
            return (ep >= s) & (ep < ne - 1)
        return (ep + s <= ne - 1) & (ep >= 1)

    def receives(s, way):
        if way == 1:
            return ep >= 1 + s
        return ep + 1 + s <= ne - 1

    def ep_start(s):
        for a in range(n_ep):
            for way in (1, -1):

                @pl.when(sends(s, way))
                def _(a=a, way=way):
                    ep_copy(a, s, way).start()

    def ep_wait(s):
        for a in range(n_ep):
            for way in (1, -1):

                @pl.when(receives(s, way))
                def _(a=a, way=way):
                    ep_copy(a, s, way).wait_recv()

    dp_steps = bit_count(nd) if n_dp else 0
    ep_steps = ne - 1 if n_ep else 0
    for t in range(dp_steps):
        for a in range(n_dp):
            dp_copy(a, t, 0).start()
    for t in range(max(dp_steps, ep_steps) + 1):
        if 0 < t <= dp_steps:
            for a in range(n_dp):
                order = gather_orders(nd)[a % 2]
                for m in masks(order[: t - 1]):
                    dp_copy(a, t - 1, m).wait_recv()
                    for later in range(t, dp_steps):
                        dp_copy(a, later, m | (1 << order[t - 1])).start()
        if 0 < t <= ep_steps:
            ep_wait(t - 1)
        if t < ep_steps:
            ep_start(t)
    for t in range(dp_steps):
        for a in range(n_dp):
            for m in masks(gather_orders(nd)[a % 2][:t]):
                dp_copy(a, t, m).wait_send()
    for s in range(ep_steps):
        for a in range(n_ep):
            for way in (1, -1):

                @pl.when(sends(s, way))
                def _(a=a, s=s, way=way):
                    ep_copy(a, s, way).wait_send()

    for c in own:
        c.wait()


def cost(us):
    return pl.CostEstimate(flops=0, bytes_accessed=int(us * 3.0e6), transcendentals=0)


def gather(ne, nd, dp_arrays, ep_arrays, collective, us):
    arrays = list(dp_arrays) + list(ep_arrays)
    counts = [nd] * len(dp_arrays) + [ne] * len(ep_arrays)
    a, b = max(len(dp_arrays), 1), max(len(ep_arrays), 1)
    return pl.pallas_call(
        functools.partial(gather_body, ne, nd, len(dp_arrays), len(ep_arrays)),
        out_shape=[
            jax.ShapeDtypeStruct((n,) + v.shape, v.dtype) for n, v in zip(counts, arrays)
        ],
        in_specs=[ANY] * len(arrays),
        out_specs=[ANY] * len(arrays),
        scratch_shapes=[
            DMA((len(arrays),)),
            DMA((a, nd - 1)),
            DMA((a, nd - 1)),
            DMA((b, 2, ne - 1)),
            DMA((b, 2, ne - 1)),
        ],
        compiler_params=pltpu.CompilerParams(
            collective_id=collective, has_side_effects=True, vmem_limit_bytes=60 * 2**20
        ),
        cost_estimate=cost(us),
    )(*arrays)


def reduce_body(ne, nd, n_dp, n_ep, n_swap, *refs):
    n_in = n_dp + n_ep + n_swap
    ins, outs = refs[:n_in], refs[n_in : 2 * n_in]
    rest = refs[2 * n_in :]
    n_sum = n_dp + n_ep
    held = rest[:n_sum]
    landing = rest[n_sum : 2 * n_sum]
    in_sem, dp_send, dp_recv, ep_send, ep_recv, swap_send, swap_recv = rest[2 * n_sum :]
    ep, dp = lax.axis_index("ep"), lax.axis_index("dp")
    loads = []
    for a in range(n_sum):
        copy = pltpu.make_async_copy(ins[a], held[a], in_sem.at[a])
        copy.start()
        loads.append(copy)
    greet(ep, dp, ne, nd)
    swaps = []
    for a in range(n_swap):
        src, dst = ins[n_sum + a], outs[n_sum + a]
        copy = pltpu.make_async_copy(src.at[ep], dst.at[ep], in_sem.at[n_sum + a])
        copy.start()
        loads.append(copy)
        for k in range(1, ne):
            to = lax.rem(ep + k, ne)
            copy = remote(
                src.at[to], dst.at[ep], swap_send.at[a, k - 1], swap_recv.at[a, k - 1], {"ep": to}
            )
            copy.start()
            swaps.append(copy)
    for c in loads:
        c.wait()

    def add(a, block, arrived):
        held[a][block] = (held[a][block].astype(F32) + arrived.astype(F32)).astype(held[a].dtype)

    nb = bit_count(nd)

    def dp_parts(a, t):
        order = gather_orders(nd)[a % 2][::-1]
        bit, left = order[t], order[t + 1 :]
        first = sum(1 << (nb - 1 - i) for i in range(t))
        return bit, [(first + j, m) for j, m in enumerate(masks(left))]

    def dp_copies(a, t):
        bit, parts = dp_parts(a, t)
        partner = jnp.bitwise_xor(dp, 1 << bit)
        return [
            (
                m,
                k,
                remote(
                    held[a].at[jnp.bitwise_xor(partner, m)],
                    landing[a].at[k],
                    dp_send.at[a, k],
                    dp_recv.at[a, k],
                    {"dp": partner},
                ),
            )
            for k, m in parts
        ]

    def ep_copy(a, dest, way):
        k = 0 if way == 1 else 1
        return remote(
            held[n_dp + a].at[dest],
            landing[n_dp + a].at[k, dest],
            ep_send.at[a, k, dest],
            ep_recv.at[a, k, dest],
            {"ep": lax.rem(ep + way + ne, ne)},
        )

    def ep_turn(t, way):
        return ep + ne - 1 - t if way == 1 else ep + t - (ne - 1)

    def ep_has(t, way):
        return ep_turn(t, way) <= ne - 1 if way == 1 else ep_turn(t, way) >= 0

    def ep_inner(way):
        return ep >= 1 if way == 1 else ep <= ne - 2

    def ep_go(t):
        for a in range(n_ep):
            for way in (1, -1):
                dest = ep_turn(t, way)

                @pl.when(ep_has(t, way) & ep_inner(way))
                def _(a=a, way=way, dest=dest):
                    ep_copy(a, dest, way).wait_recv()
                    add(n_dp + a, dest, landing[n_dp + a][0 if way == 1 else 1, dest])

                if t < ne - 1:

                    @pl.when(ep_has(t, way))
                    def _(a=a, way=way, dest=dest):
                        ep_copy(a, dest, way).start()

    dp_steps = nb if n_dp else 0
    ep_steps = ne if n_ep else 0
    started = []
    for t in range(max(dp_steps + 1, ep_steps)):
        if t < ep_steps:
            ep_go(t)

        groups = [(a, dp_copies(a, t)) for a in range(n_dp)] if t < dp_steps else []
        for a in range(n_dp):
            if 0 < t <= dp_steps:
                for m, k, c in started[-1][a][1]:
                    c.wait_recv()
                    add(a, jnp.bitwise_xor(dp, m), landing[a][k])
            if t < dp_steps:
                for m, k, c in groups[a][1]:
                    c.start()
        started.append(groups)
    for a in range(n_dp):
        outs[a][...] = held[a][dp]
    for a in range(n_ep):
        outs[n_dp + a][...] = held[n_dp + a][ep]
    for groups in started:
        for a, group in groups:
            for m, k, c in group:
                c.wait_send()
    for t in range(ep_steps - 1):
        for a in range(n_ep):
            for way in (1, -1):
                dest = ep_turn(t, way)

                @pl.when(ep_has(t, way))
                def _(a=a, way=way, dest=dest):
                    ep_copy(a, dest, way).wait_send()

    for c in swaps:
        c.wait()


def reduce(ne, nd, dp_arrays, ep_arrays, swap_arrays, collective, us):
    sums = list(dp_arrays) + list(ep_arrays)
    landing = [(nd - 1,) + v.shape[1:] for v in dp_arrays]
    landing += [(2, ne) + v.shape[1:] for v in ep_arrays]
    a, b, c = (max(len(v), 1) for v in (dp_arrays, ep_arrays, swap_arrays))
    return pl.pallas_call(
        functools.partial(
            reduce_body, ne, nd, len(dp_arrays), len(ep_arrays), len(swap_arrays)
        ),
        out_shape=[jax.ShapeDtypeStruct(v.shape[1:], v.dtype) for v in sums]
        + [jax.ShapeDtypeStruct(v.shape, v.dtype) for v in swap_arrays],
        in_specs=[ANY] * (len(sums) + len(swap_arrays)),
        out_specs=[VMEM] * len(sums) + [ANY] * len(swap_arrays),
        scratch_shapes=[pltpu.VMEM(v.shape, v.dtype) for v in sums]
        + [pltpu.VMEM(s, v.dtype) for s, v in zip(landing, sums)]
        + [
            DMA((len(sums) + len(swap_arrays),)),
            DMA((a, nd - 1)),
            DMA((a, nd - 1)),
            DMA((b, 2, ne)),
            DMA((b, 2, ne)),
            DMA((c, ne - 1)),
            DMA((c, ne - 1)),
        ],
        compiler_params=pltpu.CompilerParams(
            collective_id=collective, has_side_effects=True, vmem_limit_bytes=48 * 2**20
        ),
        cost_estimate=cost(us),
    )(*sums, *swap_arrays)


def reduce_all_body(ne, nd, count, *refs):
    ins, outs, held = refs[:count], refs[count : 2 * count], refs[2 * count : 3 * count]
    pair_in, line_in = refs[3 * count : 4 * count], refs[4 * count : 5 * count]
    in_sem, dp_send, dp_recv, ep_send, ep_recv = refs[5 * count :]
    ep, dp = lax.axis_index("ep"), lax.axis_index("dp")
    nb = bit_count(nd)

    def load(a):
        return pltpu.make_async_copy(ins[a], held[a], in_sem.at[a])

    for a in range(count):
        load(a).start()
    greet(ep, dp, ne, nd)

    def total(x, y):
        return (x.astype(F32) + y.astype(F32)).astype(BF16)

    def pair_copies(a, t):
        order = gather_orders(nd)[a % 2][::-1]
        partner = jnp.bitwise_xor(dp, 1 << order[t])
        first = sum(1 << (nb - 1 - i) for i in range(t))
        return [
            (
                m,
                first + j,
                remote(
                    held[a].at[jnp.bitwise_xor(partner, m)],
                    pair_in[a].at[first + j],
                    dp_send.at[a, first + j],
                    dp_recv.at[a, first + j],
                    {"dp": partner},
                ),
            )
            for j, m in enumerate(masks(order[t + 1 :]))
        ]

    for t in range(nb + 1):
        for a in range(count):
            if t == 0:
                load(a).wait()
            else:
                for m, k, copy in pair_copies(a, t - 1):
                    copy.wait_recv()
                    block = jnp.bitwise_xor(dp, m)
                    held[a][block] = total(held[a][block], pair_in[a][k])
            if t < nb:
                for m, k, copy in pair_copies(a, t):
                    copy.start()

    def line_copy(a, dest, way):
        k = 0 if way == 1 else 1
        return remote(
            held[a].at[dp, dest],
            line_in[a].at[k, dest],
            ep_send.at[a, k, dest],
            ep_recv.at[a, k, dest],
            {"ep": lax.rem(ep + way + ne, ne)},
        )

    def line_turn(t, way):
        dest = ep + ne - 1 - t if way == 1 else ep + t - (ne - 1)
        has = dest <= ne - 1 if way == 1 else dest >= 0
        inner = ep >= 1 if way == 1 else ep <= ne - 2
        return dest, has, inner

    for t in range(ne):
        for a in range(count):
            for way in (1, -1):
                dest, has, inner = line_turn(t, way)

                @pl.when(has & inner)
                def _(a=a, way=way, dest=dest):
                    line_copy(a, dest, way).wait_recv()
                    held[a][dp, dest] = total(
                        held[a][dp, dest], line_in[a][0 if way == 1 else 1, dest]
                    )

                if t < ne - 1:

                    @pl.when(has)
                    def _(a=a, way=way, dest=dest):
                        line_copy(a, dest, way).start()

    for a in range(count):
        outs[a][...] = held[a][dp, ep]
        for t in range(nb):
            for m, k, copy in pair_copies(a, t):
                copy.wait_send()
        for t in range(ne - 1):
            for way in (1, -1):
                dest, has, inner = line_turn(t, way)

                @pl.when(has)
                def _(a=a, way=way, dest=dest):
                    line_copy(a, dest, way).wait_send()


def reduce_all(ne, nd, arrays, collective, us):
    n = len(arrays)
    tails = [v.shape[2:] for v in arrays]
    return pl.pallas_call(
        functools.partial(reduce_all_body, ne, nd, n),
        out_shape=[jax.ShapeDtypeStruct(s, BF16) for s in tails],
        in_specs=[ANY] * n,
        out_specs=[VMEM] * n,
        scratch_shapes=[pltpu.VMEM(v.shape, BF16) for v in arrays]
        + [pltpu.VMEM((nd - 1, ne) + s, BF16) for s in tails]
        + [pltpu.VMEM((2, ne) + s, BF16) for s in tails]
        + [
            DMA((n,)),
            DMA((n, nd - 1)),
            DMA((n, nd - 1)),
            DMA((n, 2, ne)),
            DMA((n, 2, ne)),
        ],
        compiler_params=pltpu.CompilerParams(
            collective_id=collective, has_side_effects=True, vmem_limit_bytes=48 * 2**20
        ),
        cost_estimate=cost(us),
    )(*arrays)


def dot(a, b, dims=((1,), (0,))):
    return lax.dot_general(a, b, (dims, ((), ())), preferred_element_type=F32)


def expert_body(ne, nd, micro, rows, n_prior, *refs):
    cots, prior, refs = refs[:ne], refs[ne : ne + n_prior], refs[ne + n_prior :]
    normed_ref, probs_ref, gate_ref, up_ref, down_ref = refs[:5]
    mix_ref, grad_ref, dots_ref = refs[5:8]
    kept, sent = refs[8:10], refs[10:12]
    rows_in, cots_in, picks, weights, first, second, keep, send, arrived = refs[12:21]
    load_sem, store_sem, send_sem, recv_sem, free_sem = refs[21:]
    e = pl.program_id(0)
    last = pl.num_programs(0) - 1
    ep, dp = lax.axis_index("ep"), lax.axis_index("dp")
    other = {"dp": jnp.bitwise_xor(dp, 1)}
    every = micro * rows
    blocks = ne * micro
    width = first.shape[1]
    n_exp = rows_in.shape[1]

    def exchange():
        return remote(send, arrived, send_sem, recv_sem, other)

    def loads():
        out = [pltpu.make_async_copy(normed_ref, first, load_sem.at[ne])]
        for k in range(ne):
            at = pl.multiple_of(lax.rem(ep - k + ne, ne) * every, every)
            out.append(
                pltpu.make_async_copy(cots[k], second.at[pl.ds(at, every)], load_sem.at[k])
            )
        return out

    def block_at(s):
        return pl.ds(pl.multiple_of(s * rows, rows), rows)

    def returned(t):
        k, m = t // micro, lax.rem(t, micro)
        return lax.rem(ep + k, ne) * micro + m

    def stores(t):
        s = returned(t)
        return (
            pltpu.make_async_copy(
                first.at[block_at(s)], mix_ref.at[block_at(t)], store_sem.at[0, t]
            ),
            pltpu.make_async_copy(
                second.at[block_at(s)], grad_ref.at[block_at(s)], store_sem.at[1, t]
            ),
        )

    def prior_loads(t):
        at = block_at(returned(t))
        out = []
        for k, (src, dst) in enumerate(zip(prior, (first, second))):
            out.append(
                pltpu.make_async_copy(
                    src.at[block_at(t) if k == 0 else at], dst.at[at], store_sem.at[k, t]
                )
            )
        return out

    def collect():
        exchange().wait_recv()
        pieces = keep.shape[0]
        for i, bit in enumerate(first_bits(nd)):

            def put(low, high, bit=bit):
                for j in range(pieces):
                    value = (keep[j].astype(F32) + arrived[j].astype(F32)).astype(BF16)
                    at = (j >> bit << (bit - 1)) | (j & ((1 << (bit - 1)) - 1))
                    ref = high if (j >> (bit - 1)) & 1 else low
                    ref[at, 0] = value

            here = (e - 1 < n_exp // 2) if i == 0 else (e - 1 >= n_exp // 2)
            mine = jnp.bitwise_and(lax.shift_right_logical(dp, bit), 1)

            @pl.when(here & (mine == 0))
            def _(i=i, put=put):
                put(kept[i], sent[i])

            @pl.when(here & (mine == 1))
            def _(i=i, put=put):
                put(sent[i], kept[i])

    @pl.when(e == 0)
    def _():
        for copy in loads():
            copy.start()
        barrier = pltpu.get_barrier_semaphore()
        pl.semaphore_signal(barrier, inc=1, device_id=other, device_id_type=MESH)
        pl.semaphore_wait(barrier, 1)
        before = lax.broadcasted_iota(jnp.int32, (rows, rows), 0)
        after = lax.broadcasted_iota(jnp.int32, (rows, rows), 1)
        earlier = (before < after).astype(BF16)
        slot = lax.broadcasted_iota(jnp.int32, (n_exp, CAP, rows), 1)
        for copy in loads():
            copy.wait()

        @pl.loop(0, blocks)
        def _(s):
            at = block_at(s)
            probs = probs_ref[s]
            hit = probs >= 0.0
            rank = dot(hit.astype(BF16), earlier)
            rank = jnp.where(hit, rank, -1.0).astype(jnp.int32)
            pick = jnp.broadcast_to(rank[:, None, :], (n_exp, CAP, rows)) == slot
            pick_f = pick.astype(F32)
            share = jnp.sum(pick_f * probs[:, None, :], axis=2, keepdims=True)
            weights[s] = share
            flat = pick_f.reshape(n_exp * CAP, rows).astype(BF16)
            picks[s] = flat
            rows_in[s] = dot(flat, first[at, :]).astype(BF16).reshape(n_exp, CAP, width)
            cots_in[s] = dot(flat, second[at, :]).astype(BF16).reshape(n_exp, CAP, width)

    if n_prior:

        @pl.when(e == 1)
        def _():
            @pl.loop(0, blocks)
            def _(t):
                for copy in prior_loads(t):
                    copy.start()

    @pl.when(e < last)
    def _():
        x = rows_in[:, e].reshape(blocks * CAP, width)
        c = cots_in[:, e].reshape(blocks * CAP, width)
        p = weights[:, e].reshape(blocks * CAP, 1)
        w_gate, w_up, w_down = gate_ref[0], up_ref[0], down_ref[0]
        gate_pre = dot(x, w_gate)
        up_pre = dot(x, w_up)
        sigma = jax.nn.sigmoid(gate_pre)
        silu = gate_pre * sigma
        hidden = (silu * up_pre).astype(BF16)
        out = dot(hidden, w_down) * p
        back = dot(c, w_down, ((1,), (1,)))
        wide = hidden.astype(F32)
        pair = jnp.sum(wide * back, axis=1, keepdims=True)
        back = back * p
        grad_up = (back * silu).astype(BF16)
        grad_gate = (back * up_pre * (sigma * (1.0 + gate_pre * (1.0 - sigma)))).astype(BF16)
        scaled = (wide * p).astype(BF16)
        grad_x = dot(grad_gate, w_gate, ((1,), (1,))) + dot(grad_up, w_up, ((1,), (1,)))

        flat = picks[:, pl.ds(pl.multiple_of(e * CAP, CAP), CAP), :].astype(F32)
        dots_ref[0] = jnp.sum(flat * pair.reshape(blocks, CAP, 1), axis=1)

        @pl.when(e > 0)
        def _():
            collect()
            pl.semaphore_signal(free_sem, inc=1, device_id=other, device_id_type=MESH)
            exchange().wait_send()
            pl.semaphore_wait(free_sem, 1)

        def split(value, offset):
            value = value.astype(BF16)
            piece, columns = value.shape[0] // nd, keep.shape[2]

            def put(even, odd):
                for i in range(nd):
                    ref = odd if i % 2 else even
                    for j in range(value.shape[1] // columns):
                        at = offset + j * piece
                        ref[i // 2, at : at + piece] = value[
                            i * piece : (i + 1) * piece, j * columns : (j + 1) * columns
                        ]

            @pl.when(jnp.bitwise_and(dp, 1) == 0)
            def _():
                put(keep, send)

            @pl.when(jnp.bitwise_and(dp, 1) == 1)
            def _():
                put(send, keep)

        share = width // nd
        split(dot(scaled, c, ((0,), (0,))), 2 * share)
        split(dot(x, grad_gate, ((0,), (0,))), 0)
        split(dot(x, grad_up, ((0,), (0,))), share)
        exchange().start()

        rows_in[:, e] = grad_x.astype(BF16).reshape(blocks, CAP, width)
        cots_in[:, e] = out.astype(BF16).reshape(blocks, CAP, width)

    @pl.when(e == last)
    def _():
        @pl.loop(0, blocks)
        def _(t):
            s = returned(t)
            at = block_at(s)
            flat = picks[s]
            for copy in prior_loads(t):
                copy.wait()
            for done, slots in ((first, cots_in), (second, rows_in)):
                value = dot(flat, slots[s].reshape(n_exp * CAP, width), ((0,), (0,)))
                if n_prior:
                    value = value + done[at, :].astype(F32)
                done[at, :] = value.astype(BF16)
            for copy in stores(t):
                copy.start()

        collect()
        exchange().wait_send()

        @pl.loop(0, blocks)
        def _(t):
            for copy in stores(t):
                copy.wait()


def first_bits(nd):
    return [order[-2] for order in gather_orders(nd)]


def experts(
    normed, cots, probs, prior, start, w_gate, w_up, w_down, micro, rows, ne, nd, collective
):
    n_exp, (width, inner) = probs.shape[1], w_gate.shape[1:]
    blocks = ne * micro
    half = nd // 2
    packed = 2 * width // nd + (inner // nd) * (width // inner)
    full = (blocks * rows, width)
    one = pl.Buffered(1)
    weight = lambda e: (start + jnp.minimum(e, n_exp - 1), 0, 0)
    part = (half // 2, n_exp // 2, packed, inner)
    parts = [
        pl.BlockSpec(
            (half // 2, 1, packed, inner),
            lambda e, i=i: (0, jnp.clip(e - 1 - i * (n_exp // 2), 0, n_exp // 2 - 1), 0, 0),
        )
        for i in range(2)
    ]
    return pl.pallas_call(
        functools.partial(expert_body, ne, nd, micro, rows, len(prior)),
        grid=(n_exp + 1,),
        in_specs=[ANY] * (ne + 1 + len(prior))
        + [
            pl.BlockSpec(probs.shape, lambda e: (0, 0, 0), pipeline_mode=one),
            pl.BlockSpec((1, width, inner), weight),
            pl.BlockSpec((1, width, inner), weight),
            pl.BlockSpec((1, inner, width), weight),
        ],
        out_specs=[
            ANY,
            ANY,
            pl.BlockSpec((1, blocks, rows), lambda e: (jnp.minimum(e, n_exp - 1), 0, 0)),
        ]
        + parts
        + parts,
        scratch_shapes=[
            pltpu.VMEM((blocks, n_exp, CAP, width), BF16),
            pltpu.VMEM((blocks, n_exp, CAP, width), BF16),
            pltpu.VMEM((blocks, n_exp * CAP, rows), BF16),
            pltpu.VMEM((blocks, n_exp, CAP, 1), F32),
            pltpu.VMEM(full, BF16),
            pltpu.VMEM(full, BF16),
            pltpu.VMEM((half, packed, inner), BF16),
            pltpu.VMEM((half, packed, inner), BF16),
            pltpu.VMEM((half, packed, inner), BF16),
            DMA((ne + 1,)),
            DMA((2, blocks)),
            DMA,
            DMA,
            pltpu.SemaphoreType.REGULAR,
        ],
        out_shape=[
            jax.ShapeDtypeStruct(full, BF16),
            jax.ShapeDtypeStruct(full, BF16),
            jax.ShapeDtypeStruct((n_exp, blocks, rows), F32),
        ]
        + [jax.ShapeDtypeStruct(part, BF16)] * 4,
        compiler_params=pltpu.CompilerParams(
            vmem_limit_bytes=60 * 2**20,
            dimension_semantics=("arbitrary",),
            collective_id=collective,
            has_side_effects=True,
        ),
        cost_estimate=cost(35),
    )(*cots, *prior, normed, probs, w_gate, w_up, w_down)


def rms_scale(values):
    return lax.rsqrt(jnp.mean(values * values, axis=-1, keepdims=True) + EPSILON)


def partner(x):
    lane = lax.broadcasted_iota(jnp.int32, x.shape, 1)
    half = HEAD_DIM // 2
    low = lax.rem(lane, HEAD_DIM) < half
    return jnp.where(low, pltpu.roll(x, x.shape[1] - half, 1), pltpu.roll(x, half, 1))


def turn(x, cosine, sine):
    return x * cosine + partner(x) * sine


def project_body(
    tokens_ref, gain_ref, cos_ref, sin_ref, wq_ref, wk_ref, wv_ref, n_ref, q_ref, k_ref, v_ref, *rest
):
    wq, wk, wv, sem = rest
    loads = [
        pltpu.make_async_copy(src, dst, sem.at[i])
        for i, (src, dst) in enumerate(((wk_ref, wk), (wv_ref, wv), (wq_ref, wq)))
    ]
    for copy in loads:
        copy.start()
    x = tokens_ref[...].astype(F32)
    n_ref[...] = (x * rms_scale(x) * gain_ref[...]).astype(BF16)
    normed = n_ref[...]
    cosine, sine = cos_ref[...], sin_ref[...]
    tile = 256
    for copy, (w, out, turned) in zip(
        loads, ((wk, k_ref, True), (wv, v_ref, False), (wq, q_ref, True))
    ):
        copy.wait()
        for c in range(0, w.shape[1], tile):
            y = dot(normed, w[:, c : c + tile])
            if turned:
                for i in range(0, tile, 128):
                    out[:, c + i : c + i + 128] = turn(y[:, i : i + 128], cosine, sine).astype(BF16)
            else:
                out[:, c : c + tile] = y.astype(BF16)


def project(tokens, gain, cosine, sine, w_query, w_key, w_value):
    rows, width = tokens.shape
    shapes = [width, w_query.shape[1], w_key.shape[1], w_value.shape[1]]
    return pl.pallas_call(
        project_body,
        out_shape=[jax.ShapeDtypeStruct((rows, n), BF16) for n in shapes],
        in_specs=[VMEM] * 4 + [ANY] * 3,
        out_specs=[VMEM] * 4,
        scratch_shapes=[pltpu.VMEM(w.shape, BF16) for w in (w_query, w_key, w_value)] + [DMA((3,))],
        compiler_params=pltpu.CompilerParams(vmem_limit_bytes=60 * 2**20),
        cost_estimate=cost(5),
    )(tokens, gain, cosine, sine, w_query, w_key, w_value)


def spread(x):
    lane = lax.broadcasted_iota(jnp.int32, (x.shape[0], 128), 1)
    low = lane < HEAD_DIM
    zero = jnp.zeros((), x.dtype)
    first, second = x[:, :128], x[:, 128:]
    return jnp.concatenate(
        [
            jnp.where(low, first, zero),
            jnp.where(low, pltpu.roll(first, HEAD_DIM, 1), zero),
            jnp.where(low, zero, pltpu.roll(second, HEAD_DIM, 1)),
            jnp.where(low, zero, second),
        ],
        axis=0,
    )


def gathered(x, rows):
    lane = lax.broadcasted_iota(jnp.int32, (rows, 128), 1)
    low = lane < HEAD_DIM
    h = [x[i * rows : (i + 1) * rows] for i in range(4)]
    return jnp.concatenate(
        [
            jnp.where(low, h[0], pltpu.roll(h[1], HEAD_DIM, 1)),
            jnp.where(low, pltpu.roll(h[2], HEAD_DIM, 1), h[3]),
        ],
        axis=1,
    )


def window_of(dp, span):
    return jnp.maximum(dp - (span - 1), 0)


def window_scores(dp, span, rows, starts_ref, q, k):
    keys = k.shape[0]
    scores = dot(q, k, ((1,), (1,))).reshape(4, rows, keys)
    key_pos = window_of(dp, span) * rows + lax.broadcasted_iota(jnp.int32, (rows, keys), 1)
    query_pos = dp * rows + lax.broadcasted_iota(jnp.int32, (rows, keys), 0)
    allowed = (key_pos <= query_pos) & (key_pos >= starts_ref[...])
    return jnp.where(allowed[None], scores, MASKED).reshape(4 * rows, keys)


def in_window(ref, dp, span):
    block = ref[pl.ds(window_of(dp, span), span)]
    return block.reshape(span * block.shape[1], block.shape[2])


SCALE = HEAD_DIM ** (-0.5)


def attend_body(span, dp_ref, starts_ref, q_ref, k_ref, v_ref, out_ref, log_ref):
    dp = dp_ref[0]
    rows = q_ref.shape[0]
    q = spread(q_ref[...].astype(F32) * SCALE).astype(BF16)
    scores = window_scores(dp, span, rows, starts_ref, q, in_window(k_ref, dp, span))
    top = jnp.max(scores, axis=1, keepdims=True)
    terms = jnp.exp(scores - top)
    total = jnp.sum(terms, axis=1, keepdims=True)
    log_ref[0, 0] = top + jnp.log(total)
    weights = (terms * (1.0 / total)).astype(BF16)
    out = dot(weights, in_window(v_ref, dp, span))
    out_ref[...] = gathered(out, rows).astype(BF16)


def attention_specs(micro, rows, nd):
    pairs = KV_HEADS // 2
    mine = pl.BlockSpec((rows, 4 * HEAD_DIM), lambda m, h, *_: (m, h))
    theirs = pl.BlockSpec((nd, rows, 2 * HEAD_DIM), lambda m, h, *_: (0, m, h))
    column = pl.BlockSpec((rows, 1), lambda m, h, *_: (m, 0))
    logs = pl.BlockSpec((1, 1, 4 * rows, 1), lambda m, h, *_: (m, h, 0, 0))
    log_shape = jax.ShapeDtypeStruct((micro, pairs, 4 * rows, 1), F32)
    return (micro, pairs), mine, theirs, column, logs, log_shape


def attend(dp, starts, queries, keys, values, micro, rows, nd):
    grid, mine, theirs, column, logs, log_shape = attention_specs(micro, rows, nd)
    return pl.pallas_call(
        functools.partial(attend_body, nd // 2 + 1),
        grid_spec=pltpu.PrefetchScalarGridSpec(
            num_scalar_prefetch=1,
            grid=grid,
            in_specs=[column, mine, theirs, theirs],
            out_specs=[mine, logs],
        ),
        out_shape=[jax.ShapeDtypeStruct(queries.shape, BF16), log_shape],
        compiler_params=pltpu.CompilerParams(vmem_limit_bytes=40 * 2**20),
        cost_estimate=cost(15),
    )(dp.reshape(1), starts, queries, keys, values)


def attend_back_body(
    span, dp_ref, starts_ref, q_ref, k_ref, v_ref, log_ref, g_ref, cos_ref, sin_ref, *outs
):
    dq_ref, dk_ref, dv_ref = outs
    dp = dp_ref[0]
    rows = q_ref.shape[0]
    q = spread(q_ref[...].astype(F32) * SCALE).astype(BF16)
    g = spread(g_ref[...].astype(F32)).astype(BF16)
    k, v = in_window(k_ref, dp, span), in_window(v_ref, dp, span)
    scores = window_scores(dp, span, rows, starts_ref, q, k)
    probs = jnp.exp(scores - log_ref[0, 0])
    grad_probs = dot(g, v, ((1,), (1,)))
    total = jnp.sum(probs * grad_probs, axis=1, keepdims=True)
    grad_scores = (probs * (grad_probs - total)).astype(BF16)
    dq = gathered(dot(grad_scores, k) * SCALE, rows)
    cosine, sine = cos_ref[...], -sin_ref[...]
    for i in range(0, dq.shape[1], 128):
        dq_ref[:, i : i + 128] = turn(dq[:, i : i + 128], cosine, sine).astype(BF16)
    dk_ref[...] = jnp.zeros_like(dk_ref)
    dv_ref[...] = jnp.zeros_like(dv_ref)
    here = pl.ds(window_of(dp, span), span)
    dk = dot(grad_scores, q, ((0,), (0,))).astype(BF16)
    dk_ref[here] = dk.reshape(span, rows, dk.shape[1])
    dv = dot(probs.astype(BF16), g, ((0,), (0,))).astype(BF16)
    dv_ref[here] = dv.reshape(span, rows, dv.shape[1])


def attend_back(dp, starts, queries, keys, values, logs_in, grad, cosine, sine, micro, rows, nd):
    grid, mine, theirs, column, logs, _ = attention_specs(micro, rows, nd)
    table = pl.BlockSpec((rows, 128), lambda m, h, *_: (0, 0))
    return pl.pallas_call(
        functools.partial(attend_back_body, nd // 2 + 1),
        grid_spec=pltpu.PrefetchScalarGridSpec(
            num_scalar_prefetch=1,
            grid=grid,
            in_specs=[column, mine, theirs, theirs, logs, mine, table, table],
            out_specs=[mine, theirs, theirs],
        ),
        out_shape=[
            jax.ShapeDtypeStruct(queries.shape, BF16),
            jax.ShapeDtypeStruct(keys.shape, BF16),
            jax.ShapeDtypeStruct(values.shape, BF16),
        ],
        compiler_params=pltpu.CompilerParams(vmem_limit_bytes=48 * 2**20),
        cost_estimate=cost(25),
    )(dp.reshape(1), starts, queries, keys, values, logs_in, grad, cosine, sine)


def input_body(
    ne,
    nd,
    n_ref,
    dq_ref,
    dk_ref,
    dv_ref,
    cos_ref,
    sin_ref,
    wq_ref,
    wk_ref,
    wv_ref,
    tokens_ref,
    gain_ref,
    res_ref,
    wq_out,
    wk_out,
    wv_out,
    tok_out,
    gain_out,
    dk_turned,
):
    normed = n_ref[...]
    cosine, sine = cos_ref[...], -sin_ref[...]
    for i in range(0, dk_ref.shape[1], 128):
        part = dk_ref[:, i : i + 128].astype(F32)
        dk_turned[:, i : i + 128] = turn(part, cosine, sine).astype(BF16)
    tile = 256
    for grad, out in ((dq_ref, wq_out), (dk_turned, wk_out), (dv_ref, wv_out)):
        share = out.shape[1] // ne
        for c in range(0, grad.shape[1], tile):
            y = dot(normed, grad[:, c : c + tile], ((0,), (0,))).astype(BF16)
            for e in range(ne):
                for d in range(nd):
                    r = (e * nd + d) * share
                    out[d, e * share : (e + 1) * share, c : c + tile] = y[r : r + share]
    back = (
        dot(dq_ref[...], wq_ref[...], ((1,), (1,)))
        + dot(dk_turned[...], wk_ref[...], ((1,), (1,)))
        + dot(dv_ref[...], wv_ref[...], ((1,), (1,)))
    )
    x = tokens_ref[...].astype(F32)
    r = rms_scale(x)
    scaled = back * gain_ref[...]
    gain_out[...] = jnp.sum(back * x * r, axis=0, keepdims=True)
    tok_out[...] = (
        res_ref[...] + r * scaled - x * (r * r * r) * jnp.mean(scaled * x, axis=1, keepdims=True)
    )


def input_grads(ne, nd, normed, dq, dk, dv, cosine, sine, weights, tokens, gain, grad_residual):
    rows, width = tokens.shape
    share = width // (ne * nd)
    return pl.pallas_call(
        functools.partial(input_body, ne, nd),
        out_shape=[jax.ShapeDtypeStruct((nd, ne * share, w.shape[1]), BF16) for w in weights]
        + [
            jax.ShapeDtypeStruct((rows, width), F32),
            jax.ShapeDtypeStruct((1, width), F32),
        ],
        in_specs=[VMEM] * 12,
        out_specs=[VMEM] * 5,
        scratch_shapes=[pltpu.VMEM(dk.shape, BF16)],
        compiler_params=pltpu.CompilerParams(vmem_limit_bytes=48 * 2**20),
        cost_estimate=cost(10),
    )(normed, dq, dk, dv, cosine, sine, *weights, tokens, gain, grad_residual)


def swap_bit(sent, bit, nd):
    return lax.ppermute(sent, "dp", [(i, i ^ (1 << bit)) for i in range(nd)])


def plus(a, b):
    return (a.astype(F32) + b.astype(F32)).astype(BF16)


def tie(value, *others):
    return lax.optimization_barrier((value,) + others)


def per_device(
    tokens,
    segments,
    routes,
    first_gain,
    w_query,
    w_key,
    w_value,
    w_out,
    second_gain,
    w_router,
    w_gate,
    w_up,
    w_down,
    cotangent,
):
    micro, rows, width = tokens.shape
    ne, nd = lax.axis_size("ep"), lax.axis_size("dp")
    ep, dp = lax.axis_index("ep"), lax.axis_index("dp")
    groups = HEADS // KV_HEADS
    kv_width = KV_HEADS * HEAD_DIM
    every = micro * rows
    inputs = tokens.reshape(every, width).astype(F32)
    grad_output = cotangent.reshape(every, width).astype(F32)

    query_pos = dp * rows + jnp.arange(rows, dtype=jnp.int32)
    halfway = HEAD_DIM // 2
    frequency = ROPE_BASE ** (-(jnp.arange(halfway, dtype=F32) * 2.0 / HEAD_DIM))
    angles = query_pos.astype(F32)[:, None] * frequency[None, :]
    lanes = 2 * HEAD_DIM // halfway
    sign = jnp.where(jnp.arange(2 * HEAD_DIM) % HEAD_DIM < halfway, -1.0, 1.0).astype(F32)
    cosine = jnp.tile(jnp.cos(angles), (micro, lanes))
    sine = jnp.tile(jnp.sin(angles), (micro, lanes)) * sign

    tokens_flat = tokens.reshape(every, width)
    gain_one = first_gain.reshape(1, width)
    normed_one, query_rot, key_rot, value_own = project(
        tokens_flat, gain_one, cosine, sine, w_query, w_key, w_value
    )

    ids = jnp.arange(128, dtype=jnp.int32)
    counts = jnp.sum((segments[:, 0, :, None] == ids).astype(F32), axis=1)
    counts = jnp.concatenate([counts, jnp.zeros((8 - micro, 128), F32)], axis=0)

    cot_own = cotangent.reshape(every, width)

    def around(value, k):
        return lax.ppermute(value, "ep", [(i, (i + k) % ne) for i in range(ne)])

    cots = [cot_own] + [around(cot_own, k) for k in range(1, ne)]
    key_all, value_all, count_all = gather(ne, nd, (key_rot, value_own, counts), (), 0, 25)

    totals = jnp.sum(count_all[:, :micro], axis=0)
    lower = (ids[None, None, :] < segments[:, 0, :, None]).astype(F32)
    starts = jnp.sum(lower * totals[:, None, :], axis=2).astype(jnp.int32)
    starts = starts.reshape(every, 1)
    attn_low, logs = attend(dp, starts, query_rot, key_all, value_all, micro, rows, nd)
    residual = inputs + jnp.dot(attn_low, w_out, preferred_element_type=F32)
    inv_two = rms_scale(residual)
    normed_two = (residual * inv_two * second_gain).astype(BF16)
    logits = jnp.dot(normed_two, w_router, preferred_element_type=F32)
    routing = routes.reshape(every, routes.shape[2])
    chosen = jnp.any(
        routing[:, :, None] == jnp.arange(EXPERTS, dtype=jnp.int32)[None, None, :], axis=1
    )
    masked = jnp.where(chosen, logits, MASKED)
    terms = jnp.where(chosen, jnp.exp(masked - jnp.max(masked, axis=1, keepdims=True)), 0.0)
    gate_probs = terms / jnp.sum(terms, axis=1, keepdims=True)
    marked = jnp.where(chosen, gate_probs, -1.0).T

    normed_all, marked_all = gather(ne, nd, (), (normed_two, marked), 1, 38)
    here = EXPERTS // ne
    probs_here = lax.dynamic_slice_in_dim(marked_all, ep * here, here, axis=1)
    probs_here = (
        probs_here.reshape(ne, here, micro, rows)
        .transpose(0, 2, 1, 3)
        .reshape(ne * micro, here, rows)
    )
    nb = bit_count(nd)
    orders = [order[:-1][::-1] for order in gather_orders(nd)]
    prior, dots, kept, arrived = (), [], [], []
    for h in range(2):
        count = here // 2
        *prior, dot_part, kept_a, kept_b, sent_a, sent_b = experts(
            normed_all.reshape(ne * every, width),
            cots,
            probs_here[:, h * count : (h + 1) * count],
            prior,
            h * count,
            w_gate,
            w_up,
            w_down,
            micro,
            rows,
            ne,
            nd,
            6 + h,
        )
        dots.append(dot_part)
        kept.append((kept_a, kept_b))
        arrived.append(
            [swap_bit(v, orders[i][0], nd) for i, v in enumerate((sent_a, sent_b))]
        )
    mix, grad_in = prior
    pair_dots = jnp.concatenate(dots, axis=0)

    def finish(h, i, after):
        value, bits = plus(kept[h][i], arrived[h][i]), orders[i]
        value = value.reshape((2,) * (nb - 2) + value.shape[1:])
        live = [b for b in range(nb - 1, 0, -1) if b != bits[0]]
        for n, bit in enumerate(bits[1:]):
            axis = live.index(bit)
            mine = jnp.bitwise_and(lax.shift_right_logical(dp, bit), 1)
            keeps = lax.dynamic_index_in_dim(value, mine, axis, keepdims=False)
            sends = lax.dynamic_index_in_dim(value, 1 - mine, axis, keepdims=False)
            if n == 0:
                after, sends = tie(after, sends)
            value = plus(keeps, swap_bit(sends, bit, nd))
            live.remove(bit)
        return value, after

    grads = {}
    for i in range(2):
        grads[0, i], grad_in = finish(0, i, grad_in)

    pair_dots = pair_dots.reshape(here, ne, every).transpose(1, 0, 2)
    grad_back, dots_all = reduce(
        ne, nd, (), (grad_in.reshape(ne, every, width),), (pair_dots,), 2, 40
    )
    grad_back, mix = tie(grad_back, mix)
    pair_dot = dots_all.reshape(EXPERTS, every).T
    grad_logits = gate_probs * (
        pair_dot - jnp.sum(gate_probs * pair_dot, axis=1, keepdims=True)
    )
    grad_w_router = jnp.einsum(
        "td,te->de", normed_two.astype(F32), grad_logits, precision=HIGHEST
    )
    grad_normed_two = (
        jnp.einsum("te,de->td", grad_logits, w_router.astype(F32), precision=HIGHEST)
        + grad_back.astype(F32)
    )
    scaled_two = grad_normed_two * second_gain
    grad_gain_two = jnp.sum(grad_normed_two * residual * inv_two, axis=0)
    grad_residual = (
        grad_output
        + inv_two * scaled_two
        - residual * inv_two**3 * jnp.mean(scaled_two * residual, axis=-1, keepdims=True)
    )
    residual_low = grad_residual.astype(BF16)
    grad_w_out = jnp.einsum("tf,td->fd", attn_low, residual_low, preferred_element_type=F32)
    grad_attn = jnp.einsum("td,fd->tf", residual_low, w_out, preferred_element_type=F32).astype(
        BF16
    )
    for i in range(2):
        grads[1, i], grad_attn = finish(1, i, grad_attn)
    grad_query, grad_key_all, grad_value_all = attend_back(
        dp,
        starts,
        query_rot,
        key_all,
        value_all,
        logs,
        grad_attn,
        cosine,
        sine,
        micro,
        rows,
        nd,
    )
    mix = mix.reshape(ne, every, width)
    mix_parts = [mix[0]] + [around(mix[k], k) for k in range(1, ne)]
    grad_key, grad_value = reduce(ne, nd, (grad_key_all, grad_value_all), (), (), 3, 25)

    grads = jnp.concatenate([grads[h, i] for h in range(2) for i in range(2)], axis=0).astype(F32)
    share = width // nd
    grad_w_gate, grad_w_up = grads[:, :share], grads[:, share : 2 * share]
    grad_w_down = jnp.concatenate(
        [
            grads[:, at : at + w_down.shape[1] // nd]
            for at in range(2 * share, grads.shape[1], w_down.shape[1] // nd)
        ],
        axis=2,
    )
    output = residual + sum(v.astype(F32) for v in mix_parts)
    output = output.astype(BF16).reshape(tokens.shape)
    grad_w_query, grad_w_key, grad_w_value, grad_tokens, grad_gain_one = input_grads(
        ne,
        nd,
        normed_one,
        grad_query,
        grad_key,
        grad_value,
        cosine,
        sine,
        (w_query, w_key, w_value),
        tokens_flat,
        gain_one,
        grad_residual,
    )

    small = jnp.concatenate(
        [
            grad_w_router,
            grad_gain_one.reshape(width, 1),
            grad_gain_two[:, None],
            jnp.zeros((width, 128 - EXPERTS - 2), F32),
        ],
        axis=1,
    )

    def by_owner(grad):
        share = grad.shape[0] // (ne * nd)
        return grad.astype(BF16).reshape(ne, nd, share, grad.shape[1]).transpose(1, 0, 2, 3)

    def blocks_of(grad):
        return grad.reshape(nd, ne, -1, grad.shape[2])

    dense = reduce_all(
        ne,
        nd,
        (
            blocks_of(grad_w_query),
            by_owner(grad_w_out),
            blocks_of(grad_w_key),
            blocks_of(grad_w_value),
            by_owner(small),
        ),
        4,
        60,
    )
    d_query, d_out, d_key, d_value, d_small = (v.astype(F32) for v in dense)
    return (
        output,
        grad_tokens.reshape(tokens.shape),
        d_small[:, EXPERTS],
        d_query,
        d_key,
        d_value,
        d_out,
        d_small[:, EXPERTS + 1],
        d_small[:, :EXPERTS],
        grad_w_gate,
        grad_w_up,
        grad_w_down,
    )


def solution(mesh):
    in_specs = (
        P(None, ("ep", "dp"), None),
        P(None, "ep", "dp"),
        P(None, ("ep", "dp"), None),
        P(),
        P(),
        P(),
        P(),
        P(),
        P(),
        P(),
        P("ep", None, None),
        P("ep", None, None),
        P("ep", None, None),
        P(None, ("ep", "dp"), None),
    )
    out_specs = (
        P(None, ("ep", "dp"), None),
        P(None, ("ep", "dp"), None),
        P(("ep", "dp")),
        P(("ep", "dp"), None),
        P(("ep", "dp"), None),
        P(("ep", "dp"), None),
        P(("ep", "dp"), None),
        P(("ep", "dp")),
        P(("ep", "dp"), None),
        P("ep", "dp", None),
        P("ep", "dp", None),
        P("ep", "dp", None),
    )
    return jax.shard_map(
        per_device, mesh=mesh, in_specs=in_specs, out_specs=out_specs, check_vma=False
    )
```

```python
import functools

import jax
import jax.numpy as jnp
from jax import lax
from jax.experimental import pallas as pl
from jax.experimental.pallas import tpu as pltpu
from jax.sharding import PartitionSpec as P

HEADS = 16
KV_HEADS = 8
HEAD_DIM = 64
EXPERTS = 32
CAP = 64
EPSILON = 1e-06
ROPE_BASE = 10000.0
MASKED = -1e30
HIGHEST = lax.Precision.HIGHEST
MESH = pl.DeviceIdType.MESH
BF16 = jnp.bfloat16
F32 = jnp.float32
VMEM = pl.BlockSpec(memory_space=pltpu.VMEM)
ANY = pl.BlockSpec(memory_space=pl.ANY)
DMA = pltpu.SemaphoreType.DMA


def bit_count(n):
    return n.bit_length() - 1


def masks(bits):
    out = [0]
    for b in bits:
        out = out + [m | (1 << b) for m in out]
    return out


def gather_orders(n):
    bits = list(range(bit_count(n)))
    return (bits[1:] + bits[:1], bits[:0:-1] + bits[:1])


def greet(ep, dp, ne, nd):
    barrier = pltpu.get_barrier_semaphore()
    for k in range(1, ne):
        pl.semaphore_signal(
            barrier, inc=1, device_id={"ep": lax.rem(ep + k, ne)}, device_id_type=MESH
        )
    for b in range(bit_count(nd)):
        pl.semaphore_signal(
            barrier, inc=1, device_id={"dp": jnp.bitwise_xor(dp, 1 << b)}, device_id_type=MESH
        )
    pl.semaphore_wait(barrier, ne - 1 + bit_count(nd))


def remote(src, dst, send, recv, where):
    return pltpu.make_async_remote_copy(
        src_ref=src, dst_ref=dst, send_sem=send, recv_sem=recv, device_id=where, device_id_type=MESH
    )


def gather_body(ne, nd, n_dp, n_ep, *refs):
    n_in = n_dp + n_ep
    ins, outs, sems = refs[:n_in], refs[n_in : 2 * n_in], refs[2 * n_in :]
    ep, dp = lax.axis_index("ep"), lax.axis_index("dp")
    own_sem, dp_send, dp_recv, ep_send, ep_recv = sems
    greet(ep, dp, ne, nd)
    own = []
    for a in range(n_in):
        me = dp if a < n_dp else ep
        copy = pltpu.make_async_copy(ins[a], outs[a].at[me], own_sem.at[a])
        copy.start()
        own.append(copy)

    def dp_copy(a, t, m):
        order = gather_orders(nd)[a % 2]
        block = jnp.bitwise_xor(dp, m)
        k = (1 << t) - 1 + masks(order[:t]).index(m)
        return remote(
            ins[a] if m == 0 else outs[a].at[block],
            outs[a].at[block],
            dp_send.at[a, k],
            dp_recv.at[a, k],
            {"dp": jnp.bitwise_xor(dp, 1 << order[t])},
        )

    def ep_copy(a, s, way):
        shard = lax.rem(ep - way * s + ne, ne)
        src = ins[n_dp + a] if s == 0 else outs[n_dp + a].at[shard]
        k = 0 if way == 1 else 1
        return remote(
            src,
            outs[n_dp + a].at[shard],
            ep_send.at[a, k, s],
            ep_recv.at[a, k, s],
            {"ep": lax.rem(ep + way + ne, ne)},
        )

    def sends(s, way):
        if way == 1:
            return (ep >= s) & (ep < ne - 1)
        return (ep + s <= ne - 1) & (ep >= 1)

    def receives(s, way):
        if way == 1:
            return ep >= 1 + s
        return ep + 1 + s <= ne - 1

    def ep_start(s):
        for a in range(n_ep):
            for way in (1, -1):

                @pl.when(sends(s, way))
                def _(a=a, way=way):
                    ep_copy(a, s, way).start()

    def ep_wait(s):
        for a in range(n_ep):
            for way in (1, -1):

                @pl.when(receives(s, way))
                def _(a=a, way=way):
                    ep_copy(a, s, way).wait_recv()

    dp_steps = bit_count(nd) if n_dp else 0
    ep_steps = ne - 1 if n_ep else 0
    for t in range(dp_steps):
        for a in range(n_dp):
            dp_copy(a, t, 0).start()
    for t in range(max(dp_steps, ep_steps) + 1):
        if 0 < t <= dp_steps:
            for a in range(n_dp):
                order = gather_orders(nd)[a % 2]
                for m in masks(order[: t - 1]):
                    dp_copy(a, t - 1, m).wait_recv()
                    for later in range(t, dp_steps):
                        dp_copy(a, later, m | (1 << order[t - 1])).start()
        if 0 < t <= ep_steps:
            ep_wait(t - 1)
        if t < ep_steps:
            ep_start(t)
    for t in range(dp_steps):
        for a in range(n_dp):
            for m in masks(gather_orders(nd)[a % 2][:t]):
                dp_copy(a, t, m).wait_send()
    for s in range(ep_steps):
        for a in range(n_ep):
            for way in (1, -1):

                @pl.when(sends(s, way))
                def _(a=a, s=s, way=way):
                    ep_copy(a, s, way).wait_send()

    for c in own:
        c.wait()


def cost(us):
    return pl.CostEstimate(flops=0, bytes_accessed=int(us * 3.0e6), transcendentals=0)


def gather(ne, nd, dp_arrays, ep_arrays, collective, us):
    arrays = list(dp_arrays) + list(ep_arrays)
    counts = [nd] * len(dp_arrays) + [ne] * len(ep_arrays)
    a, b = max(len(dp_arrays), 1), max(len(ep_arrays), 1)
    return pl.pallas_call(
        functools.partial(gather_body, ne, nd, len(dp_arrays), len(ep_arrays)),
        out_shape=[
            jax.ShapeDtypeStruct((n,) + v.shape, v.dtype) for n, v in zip(counts, arrays)
        ],
        in_specs=[ANY] * len(arrays),
        out_specs=[ANY] * len(arrays),
        scratch_shapes=[
            DMA((len(arrays),)),
            DMA((a, nd - 1)),
            DMA((a, nd - 1)),
            DMA((b, 2, ne - 1)),
            DMA((b, 2, ne - 1)),
        ],
        compiler_params=pltpu.CompilerParams(
            collective_id=collective, has_side_effects=True, vmem_limit_bytes=60 * 2**20
        ),
        cost_estimate=cost(us),
    )(*arrays)


def add_into(ref, arrived):
    if len(ref.shape) > 2:

        @pl.loop(0, ref.shape[0])
        def _(i):
            add_into(ref.at[i], arrived.at[i])

    else:
        ref[...] = (ref[...].astype(F32) + arrived[...].astype(F32)).astype(ref.dtype)


def reduce_body(ne, nd, pairs, n_line, n_swap, *refs):
    n_pair = len(pairs)
    n_extra = sum(extra for _, extra, _ in pairs)
    n_sum = n_pair + n_line
    sizes = (n_sum, n_extra, n_swap, n_sum, n_swap, n_sum, n_extra, n_pair)
    groups, at = [], 0
    for size in sizes:
        groups.append(refs[at : at + size])
        at += size
    ins, extra_ins, swap_ins, outs, swap_outs, held, extras, pair_in = groups
    lined = [a for a in range(n_pair) if pairs[a][2]] + list(range(n_pair, n_sum))
    line_in = dict(zip(lined, refs[at : at + len(lined)]))
    in_sem, extra_sem, out_sem, dp_send, dp_recv, ep_send, ep_recv, swap_send, swap_recv = refs[
        at + len(lined) :
    ]
    ep, dp = lax.axis_index("ep"), lax.axis_index("dp")
    extra_of = [sum(extra for _, extra, _ in pairs[:a]) for a in range(n_pair)]

    def load(a):
        return pltpu.make_async_copy(ins[a], held[a], in_sem.at[a])

    def load_extra(a):
        i = extra_of[a]
        return pltpu.make_async_copy(extra_ins[i], extras[i], extra_sem.at[i])

    for a in range(n_sum):
        load(a).start()
        if a < n_pair and pairs[a][1]:
            load_extra(a).start()
    greet(ep, dp, ne, nd)
    swaps = []
    for a in range(n_swap):
        src, dst = swap_ins[a], swap_outs[a]
        own = pltpu.make_async_copy(src.at[ep], dst.at[ep], in_sem.at[n_sum + a])
        own.start()
        swaps.append(own)
        for k in range(1, ne):
            to = lax.rem(ep + k, ne)
            copy = remote(
                src.at[to], dst.at[ep], swap_send.at[a, k - 1], swap_recv.at[a, k - 1], {"ep": to}
            )
            copy.start()
            swaps.append(copy)

    def place(order, bit):
        return sorted(order).index(bit)

    def index_of(order):
        index = 0
        for b in order:
            side = jnp.bitwise_and(lax.shift_right_logical(dp, b), 1)
            index = index + (side << place(order, b))
        return index

    def pair_copies(a, t):
        order = pairs[a][0]
        side = 1 << place(order, order[t])
        partner = jnp.bitwise_xor(index_of(order), side)
        first = sum(1 << (len(order) - 1 - i) for i in range(t))
        return [
            (
                m,
                first + j,
                remote(
                    held[a].at[jnp.bitwise_xor(partner, m)],
                    pair_in[a].at[first + j],
                    dp_send.at[a, first + j],
                    dp_recv.at[a, first + j],
                    {"dp": jnp.bitwise_xor(dp, 1 << order[t])},
                ),
            )
            for j, m in enumerate(masks([place(order, b) for b in order[t + 1 :]]))
        ]

    def pair_step(a, t):
        order = pairs[a][0]
        if t == 0:
            load(a).wait()
            if pairs[a][1]:
                load_extra(a).wait()
                add_into(held[a], extras[extra_of[a]])
        elif t <= len(order):
            for m, k, copy in pair_copies(a, t - 1):
                copy.wait_recv()
                add_into(held[a].at[jnp.bitwise_xor(index_of(order), m)], pair_in[a].at[k])
        if t < len(order):
            for m, k, copy in pair_copies(a, t):
                copy.start()

    def line_block(a, dest):
        return held[a].at[index_of(pairs[a][0]), dest] if a < n_pair else held[a].at[dest]

    def line_copy(a, dest, way):
        k = 0 if way == 1 else 1
        i = lined.index(a)
        return remote(
            line_block(a, dest),
            line_in[a].at[k, dest],
            ep_send.at[i, k, dest],
            ep_recv.at[i, k, dest],
            {"ep": lax.rem(ep + way + ne, ne)},
        )

    def line_turn(t, way):
        dest = ep + ne - 1 - t if way == 1 else ep + t - (ne - 1)
        has = dest <= ne - 1 if way == 1 else dest >= 0
        inner = ep >= 1 if way == 1 else ep <= ne - 2
        return dest, has, inner

    def line_step(a, t):
        if t == 0 and a >= n_pair:
            load(a).wait()
        for way in (1, -1):
            dest, has, inner = line_turn(t, way)

            @pl.when(has & inner)
            def _(way=way, dest=dest):
                line_copy(a, dest, way).wait_recv()
                add_into(line_block(a, dest), line_in[a].at[0 if way == 1 else 1, dest])

            if t < ne - 1:

                @pl.when(has)
                def _(way=way, dest=dest):
                    line_copy(a, dest, way).start()

    steps = max([len(order) + 1 for order, _, _ in pairs] + [ne if n_line else 0])
    for t in range(steps):
        for a in range(n_pair, n_sum):
            if t < ne:
                line_step(a, t)
        for a in range(n_pair):
            pair_step(a, t)
    for t in range(ne):
        for a in lined:
            if a < n_pair:
                line_step(a, t)

    results = []
    for a in range(n_sum):
        if a >= n_pair:
            src = held[a].at[ep]
        else:
            src = line_block(a, ep) if pairs[a][2] else held[a].at[index_of(pairs[a][0])]
        copy = pltpu.make_async_copy(src, outs[a], out_sem.at[a])
        copy.start()
        results.append(copy)
    for a in range(n_pair):
        for t in range(len(pairs[a][0])):
            for m, k, copy in pair_copies(a, t):
                copy.wait_send()
    for a in lined:
        for t in range(ne - 1):
            for way in (1, -1):
                dest, has, inner = line_turn(t, way)

                @pl.when(has)
                def _(a=a, way=way, dest=dest):
                    line_copy(a, dest, way).wait_send()

    for copy in swaps + results:
        copy.wait()


def reduce(ne, nd, pairs, lines, swaps, collective, us):
    arrays = [p[0] for p in pairs] + list(lines)
    extras = [p[2] for p in pairs if p[2] is not None]
    kinds = tuple((tuple(order), extra is not None, both) for _, order, extra, both in pairs)
    results = [v.shape[2:] if both else v.shape[1:] for v, _, _, both in pairs]
    results += [v.shape[1:] for v in lines]
    landing = [(v.shape[0] - 1,) + v.shape[1:] for v, _, _, _ in pairs]
    landing += [(2,) + v.shape[1:] for v, _, _, both in pairs if both]
    landing += [(2,) + v.shape for v in lines]
    some = lambda v: max(len(v), 1)
    line_count = max(len(lines) + sum(both for _, _, _, both in pairs), 1)
    deep = max([v.shape[0] - 1 for v, _, _, _ in pairs] + [1])
    return pl.pallas_call(
        functools.partial(reduce_body, ne, nd, kinds, len(lines), len(swaps)),
        out_shape=[jax.ShapeDtypeStruct(s, BF16) for s in results]
        + [jax.ShapeDtypeStruct(v.shape, v.dtype) for v in swaps],
        in_specs=[ANY] * (len(arrays) + len(extras) + len(swaps)),
        out_specs=[ANY] * (len(arrays) + len(swaps)),
        scratch_shapes=[pltpu.VMEM(v.shape, BF16) for v in arrays + extras]
        + [pltpu.VMEM(s, BF16) for s in landing]
        + [
            DMA((len(arrays) + len(swaps),)),
            DMA((some(extras),)),
            DMA((len(arrays),)),
            DMA((some(pairs), deep)),
            DMA((some(pairs), deep)),
            DMA((line_count, 2, ne)),
            DMA((line_count, 2, ne)),
            DMA((some(swaps), ne - 1)),
            DMA((some(swaps), ne - 1)),
        ],
        compiler_params=pltpu.CompilerParams(
            collective_id=collective, has_side_effects=True, vmem_limit_bytes=56 * 2**20
        ),
        cost_estimate=cost(us),
    )(*arrays, *extras, *swaps)


def dot(a, b, dims=((1,), (0,))):
    return lax.dot_general(a, b, (dims, ((), ())), preferred_element_type=F32)


def expert_body(ne, nd, micro, rows, *refs):
    cots, refs = refs[:ne], refs[ne:]
    normed_ref, probs_ref, gate_ref, up_ref, down_ref = refs[:5]
    mix_ref, grad_ref, dots_ref = refs[5:8]
    kept, landed = refs[8:10], refs[10:12]
    rows_in, cots_in, picks, weights, first, second, keep, send, arrived, leaving = refs[12:22]
    load_sem, store_sem, send_sem, recv_sem, free_sem, far_send, far_recv = refs[22:]
    e = pl.program_id(0)
    last = pl.num_programs(0) - 1
    ep, dp = lax.axis_index("ep"), lax.axis_index("dp")
    other = {"dp": jnp.bitwise_xor(dp, 1)}
    every = micro * rows
    blocks = ne * micro
    width = first.shape[1]
    n_exp = rows_in.shape[1]

    def exchange():
        return remote(send, arrived, send_sem, recv_sem, other)

    def loads():
        out = [pltpu.make_async_copy(normed_ref, first, load_sem.at[ne])]
        for k in range(ne):
            at = pl.multiple_of(lax.rem(ep - k + ne, ne) * every, every)
            out.append(
                pltpu.make_async_copy(cots[k], second.at[pl.ds(at, every)], load_sem.at[k])
            )
        return out

    def block_at(s):
        return pl.ds(pl.multiple_of(s * rows, rows), rows)

    def returned(t):
        k, m = t // micro, lax.rem(t, micro)
        return lax.rem(ep + k, ne) * micro + m

    def stores(t):
        s = returned(t)
        return (
            pltpu.make_async_copy(
                first.at[block_at(s)], mix_ref.at[block_at(s)], store_sem.at[0, t]
            ),
            pltpu.make_async_copy(
                second.at[block_at(s)], grad_ref.at[block_at(s)], store_sem.at[1, t]
            ),
        )

    def far(i, n):
        return remote(
            leaving.at[i],
            landed[i].at[:, n],
            far_send.at[i],
            far_recv.at[i, n],
            {"dp": jnp.bitwise_xor(dp, 1 << first_bits(nd)[i])},
        )

    def collect():
        exchange().wait_recv()
        pieces = keep.shape[0]
        n = (e - 1) // 2
        for i, bit in enumerate(first_bits(nd)):

            def put(side, i=i, bit=bit):
                for j in range(pieces):
                    value = (keep[j].astype(F32) + arrived[j].astype(F32)).astype(BF16)
                    at = (j >> bit << (bit - 1)) | (j & ((1 << (bit - 1)) - 1))
                    if (j >> (bit - 1)) & 1 == side:
                        kept[i][at, 0] = value
                    else:
                        leaving[i, at] = value

            @pl.when(lax.rem(e - 1, 2) == i)
            def _(i=i, bit=bit, put=put):
                @pl.when(n > 0)
                def _():
                    far(i, n - 1).wait_send()

                mine = jnp.bitwise_and(lax.shift_right_logical(dp, bit), 1)

                @pl.when(mine == 0)
                def _():
                    put(0)

                @pl.when(mine == 1)
                def _():
                    put(1)

                far(i, n).start()

    @pl.when(e == 0)
    def _():
        for copy in loads():
            copy.start()
        barrier = pltpu.get_barrier_semaphore()
        met = [0] + sorted(set(first_bits(nd)))
        for bit in met:
            pl.semaphore_signal(
                barrier,
                inc=1,
                device_id={"dp": jnp.bitwise_xor(dp, 1 << bit)},
                device_id_type=MESH,
            )
        pl.semaphore_wait(barrier, len(met))
        before = lax.broadcasted_iota(jnp.int32, (rows, rows), 0)
        after = lax.broadcasted_iota(jnp.int32, (rows, rows), 1)
        earlier = (before < after).astype(BF16)
        slot = lax.broadcasted_iota(jnp.int32, (n_exp, CAP, rows), 1)
        for copy in loads():
            copy.wait()

        @pl.loop(0, blocks)
        def _(s):
            at = block_at(s)
            probs = probs_ref[s]
            hit = probs >= 0.0
            rank = dot(hit.astype(BF16), earlier)
            rank = jnp.where(hit, rank, -1.0).astype(jnp.int32)
            pick = jnp.broadcast_to(rank[:, None, :], (n_exp, CAP, rows)) == slot
            pick_f = pick.astype(F32)
            share = jnp.sum(pick_f * probs[:, None, :], axis=2, keepdims=True)
            weights[s] = share
            flat = pick_f.reshape(n_exp * CAP, rows).astype(BF16)
            picks[s] = flat
            rows_in[s] = dot(flat, first[at, :]).astype(BF16).reshape(n_exp, CAP, width)
            cots_in[s] = dot(flat, second[at, :]).astype(BF16).reshape(n_exp, CAP, width)

    @pl.when(e < last)
    def _():
        x = rows_in[:, e].reshape(blocks * CAP, width)
        c = cots_in[:, e].reshape(blocks * CAP, width)
        p = weights[:, e].reshape(blocks * CAP, 1)
        w_gate, w_up, w_down = gate_ref[0], up_ref[0], down_ref[0]
        gate_pre = dot(x, w_gate)
        up_pre = dot(x, w_up)
        sigma = jax.nn.sigmoid(gate_pre)
        silu = gate_pre * sigma
        hidden = (silu * up_pre).astype(BF16)
        out = dot(hidden, w_down) * p
        back = dot(c, w_down, ((1,), (1,)))
        wide = hidden.astype(F32)
        pair = jnp.sum(wide * back, axis=1, keepdims=True)
        back = back * p
        grad_up = (back * silu).astype(BF16)
        grad_gate = (back * up_pre * (sigma * (1.0 + gate_pre * (1.0 - sigma)))).astype(BF16)
        scaled = (wide * p).astype(BF16)
        grad_x = dot(grad_gate, w_gate, ((1,), (1,))) + dot(grad_up, w_up, ((1,), (1,)))

        flat = picks[:, pl.ds(pl.multiple_of(e * CAP, CAP), CAP), :].astype(F32)
        dots_ref[0] = jnp.sum(flat * pair.reshape(blocks, CAP, 1), axis=1)

        @pl.when(e > 0)
        def _():
            collect()
            pl.semaphore_signal(free_sem, inc=1, device_id=other, device_id_type=MESH)
            exchange().wait_send()
            pl.semaphore_wait(free_sem, 1)

        def split(value, offset):
            value = value.astype(BF16)
            piece, columns = value.shape[0] // nd, keep.shape[2]

            def put(even, odd):
                for i in range(nd):
                    ref = odd if i % 2 else even
                    for j in range(value.shape[1] // columns):
                        at = offset + j * piece
                        ref[i // 2, at : at + piece] = value[
                            i * piece : (i + 1) * piece, j * columns : (j + 1) * columns
                        ]

            @pl.when(jnp.bitwise_and(dp, 1) == 0)
            def _():
                put(keep, send)

            @pl.when(jnp.bitwise_and(dp, 1) == 1)
            def _():
                put(send, keep)

        share = width // nd
        split(dot(scaled, c, ((0,), (0,))), 2 * share)
        split(dot(x, grad_gate, ((0,), (0,))), 0)
        split(dot(x, grad_up, ((0,), (0,))), share)
        exchange().start()

        rows_in[:, e] = grad_x.astype(BF16).reshape(blocks, CAP, width)
        cots_in[:, e] = out.astype(BF16).reshape(blocks, CAP, width)

    @pl.when(e == last)
    def _():
        @pl.loop(0, blocks)
        def _(t):
            s = returned(t)
            at = block_at(s)
            flat = picks[s]
            for done, slots in ((first, cots_in), (second, rows_in)):
                value = dot(flat, slots[s].reshape(n_exp * CAP, width), ((0,), (0,)))
                done[at, :] = value.astype(BF16)
            for copy in stores(t):
                copy.start()

            @pl.when(t == 1)
            def _():
                collect()
                exchange().wait_send()

        @pl.loop(0, blocks)
        def _(t):
            for copy in stores(t):
                copy.wait()

        for i in range(2):
            far(i, n_exp // 2 - 1).wait_send()

            @pl.loop(0, n_exp // 2)
            def _(n, i=i):
                far(i, n).wait_recv()


def first_bits(nd):
    return [order[-2] for order in gather_orders(nd)]


def experts(normed, cots, probs, w_gate, w_up, w_down, micro, rows, ne, nd, collective):
    n_exp, width, inner = w_gate.shape
    blocks = ne * micro
    half = nd // 2
    packed = 2 * width // nd + (inner // nd) * (width // inner)
    full = (blocks * rows, width)
    one = pl.Buffered(1)
    weight = lambda e: (jnp.minimum(e, n_exp - 1), 0, 0)
    part = (half // 2, n_exp // 2, packed, inner)
    kept = pl.BlockSpec(
        (half // 2, 1, packed, inner), lambda e: (0, jnp.maximum(e - 1, 0) // 2, 0, 0)
    )
    return pl.pallas_call(
        functools.partial(expert_body, ne, nd, micro, rows),
        grid=(n_exp + 1,),
        in_specs=[ANY] * (ne + 1)
        + [
            pl.BlockSpec(probs.shape, lambda e: (0, 0, 0), pipeline_mode=one),
            pl.BlockSpec((1, width, inner), weight),
            pl.BlockSpec((1, width, inner), weight),
            pl.BlockSpec((1, inner, width), weight),
        ],
        out_specs=[ANY, ANY, pl.BlockSpec((1, blocks, rows), weight), kept, kept, ANY, ANY],
        scratch_shapes=[
            pltpu.VMEM((blocks, n_exp, CAP, width), BF16),
            pltpu.VMEM((blocks, n_exp, CAP, width), BF16),
            pltpu.VMEM((blocks, n_exp * CAP, rows), BF16),
            pltpu.VMEM((blocks, n_exp, CAP, 1), F32),
            pltpu.VMEM(full, BF16),
            pltpu.VMEM(full, BF16),
            pltpu.VMEM((half, packed, inner), BF16),
            pltpu.VMEM((half, packed, inner), BF16),
            pltpu.VMEM((half, packed, inner), BF16),
            pltpu.VMEM((2, half // 2, packed, inner), BF16),
            DMA((ne + 1,)),
            DMA((2, blocks)),
            DMA,
            DMA,
            pltpu.SemaphoreType.REGULAR,
            DMA((2,)),
            DMA((2, n_exp // 2)),
        ],
        out_shape=[
            jax.ShapeDtypeStruct(full, BF16),
            jax.ShapeDtypeStruct(full, BF16),
            jax.ShapeDtypeStruct((n_exp, blocks, rows), F32),
        ]
        + [jax.ShapeDtypeStruct(part, BF16)] * 4,
        compiler_params=pltpu.CompilerParams(
            vmem_limit_bytes=62 * 2**20,
            dimension_semantics=("arbitrary",),
            collective_id=collective,
            has_side_effects=True,
        ),
        cost_estimate=cost(75),
    )(*cots, normed, probs, w_gate, w_up, w_down)


def rms_scale(values):
    return lax.rsqrt(jnp.mean(values * values, axis=-1, keepdims=True) + EPSILON)


def partner(x):
    lane = lax.broadcasted_iota(jnp.int32, x.shape, 1)
    half = HEAD_DIM // 2
    low = lax.rem(lane, HEAD_DIM) < half
    return jnp.where(low, pltpu.roll(x, x.shape[1] - half, 1), pltpu.roll(x, half, 1))


def turn(x, cosine, sine):
    return x * cosine + partner(x) * sine


def project_body(
    tokens_ref, gain_ref, cos_ref, sin_ref, wq_ref, wk_ref, wv_ref, n_ref, q_ref, k_ref, v_ref, *rest
):
    wq, wk, wv, sem = rest
    loads = [
        pltpu.make_async_copy(src, dst, sem.at[i])
        for i, (src, dst) in enumerate(((wk_ref, wk), (wv_ref, wv), (wq_ref, wq)))
    ]
    for copy in loads:
        copy.start()
    x = tokens_ref[...].astype(F32)
    n_ref[...] = (x * rms_scale(x) * gain_ref[...]).astype(BF16)
    normed = n_ref[...]
    cosine, sine = cos_ref[...], sin_ref[...]
    tile = 256
    for copy, (w, out, turned) in zip(
        loads, ((wk, k_ref, True), (wv, v_ref, False), (wq, q_ref, True))
    ):
        copy.wait()
        for c in range(0, w.shape[1], tile):
            y = dot(normed, w[:, c : c + tile])
            if turned:
                for i in range(0, tile, 128):
                    out[:, c + i : c + i + 128] = turn(y[:, i : i + 128], cosine, sine).astype(BF16)
            else:
                out[:, c : c + tile] = y.astype(BF16)


def project(tokens, gain, cosine, sine, w_query, w_key, w_value):
    rows, width = tokens.shape
    shapes = [width, w_query.shape[1], w_key.shape[1], w_value.shape[1]]
    return pl.pallas_call(
        project_body,
        out_shape=[jax.ShapeDtypeStruct((rows, n), BF16) for n in shapes],
        in_specs=[VMEM] * 4 + [ANY] * 3,
        out_specs=[VMEM] * 4,
        scratch_shapes=[pltpu.VMEM(w.shape, BF16) for w in (w_query, w_key, w_value)] + [DMA((3,))],
        compiler_params=pltpu.CompilerParams(vmem_limit_bytes=60 * 2**20),
        cost_estimate=cost(5),
    )(tokens, gain, cosine, sine, w_query, w_key, w_value)


def spread(x):
    lane = lax.broadcasted_iota(jnp.int32, (x.shape[0], 128), 1)
    low = lane < HEAD_DIM
    zero = jnp.zeros((), x.dtype)
    first, second = x[:, :128], x[:, 128:]
    return jnp.concatenate(
        [
            jnp.where(low, first, zero),
            jnp.where(low, pltpu.roll(first, HEAD_DIM, 1), zero),
            jnp.where(low, zero, pltpu.roll(second, HEAD_DIM, 1)),
            jnp.where(low, zero, second),
        ],
        axis=0,
    )


def gathered(x, rows):
    lane = lax.broadcasted_iota(jnp.int32, (rows, 128), 1)
    low = lane < HEAD_DIM
    h = [x[i * rows : (i + 1) * rows] for i in range(4)]
    return jnp.concatenate(
        [
            jnp.where(low, h[0], pltpu.roll(h[1], HEAD_DIM, 1)),
            jnp.where(low, pltpu.roll(h[2], HEAD_DIM, 1), h[3]),
        ],
        axis=1,
    )


def window_of(dp, span):
    return jnp.maximum(dp - (span - 1), 0)


def window_scores(dp, span, rows, starts_ref, q, k):
    keys = k.shape[0]
    scores = dot(q, k, ((1,), (1,))).reshape(4, rows, keys)
    key_pos = window_of(dp, span) * rows + lax.broadcasted_iota(jnp.int32, (rows, keys), 1)
    query_pos = dp * rows + lax.broadcasted_iota(jnp.int32, (rows, keys), 0)
    allowed = (key_pos <= query_pos) & (key_pos >= starts_ref[...])
    return jnp.where(allowed[None], scores, MASKED).reshape(4 * rows, keys)


def in_window(ref, dp, span):
    block = ref[pl.ds(window_of(dp, span), span)]
    return block.reshape(span * block.shape[1], block.shape[2])


SCALE = HEAD_DIM ** (-0.5)


def attend_body(span, dp_ref, starts_ref, q_ref, k_ref, v_ref, out_ref, log_ref):
    dp = dp_ref[0]
    rows = q_ref.shape[0]
    q = spread(q_ref[...].astype(F32) * SCALE).astype(BF16)
    scores = window_scores(dp, span, rows, starts_ref, q, in_window(k_ref, dp, span))
    top = jnp.max(scores, axis=1, keepdims=True)
    terms = jnp.exp(scores - top)
    total = jnp.sum(terms, axis=1, keepdims=True)
    log_ref[0, 0] = top + jnp.log(total)
    weights = (terms * (1.0 / total)).astype(BF16)
    out = dot(weights, in_window(v_ref, dp, span))
    out_ref[...] = gathered(out, rows).astype(BF16)


def attention_specs(micro, rows, nd):
    pairs = KV_HEADS // 2
    mine = pl.BlockSpec((rows, 4 * HEAD_DIM), lambda m, h, *_: (m, h))
    theirs = pl.BlockSpec((nd, rows, 2 * HEAD_DIM), lambda m, h, *_: (0, m, h))
    column = pl.BlockSpec((rows, 1), lambda m, h, *_: (m, 0))
    logs = pl.BlockSpec((1, 1, 4 * rows, 1), lambda m, h, *_: (m, h, 0, 0))
    log_shape = jax.ShapeDtypeStruct((micro, pairs, 4 * rows, 1), F32)
    return (micro, pairs), mine, theirs, column, logs, log_shape


def attend(dp, starts, queries, keys, values, micro, rows, nd):
    grid, mine, theirs, column, logs, log_shape = attention_specs(micro, rows, nd)
    return pl.pallas_call(
        functools.partial(attend_body, nd // 2 + 1),
        grid_spec=pltpu.PrefetchScalarGridSpec(
            num_scalar_prefetch=1,
            grid=grid,
            in_specs=[column, mine, theirs, theirs],
            out_specs=[mine, logs],
        ),
        out_shape=[jax.ShapeDtypeStruct(queries.shape, BF16), log_shape],
        compiler_params=pltpu.CompilerParams(vmem_limit_bytes=40 * 2**20),
        cost_estimate=cost(15),
    )(dp.reshape(1), starts, queries, keys, values)


def attend_back_body(
    span, dp_ref, starts_ref, q_ref, k_ref, v_ref, log_ref, g_ref, cos_ref, sin_ref, *outs
):
    dq_ref, dk_ref, dv_ref = outs
    dp = dp_ref[0]
    rows = q_ref.shape[0]
    q = spread(q_ref[...].astype(F32) * SCALE).astype(BF16)
    g = spread(g_ref[...].astype(F32)).astype(BF16)
    k, v = in_window(k_ref, dp, span), in_window(v_ref, dp, span)
    scores = window_scores(dp, span, rows, starts_ref, q, k)
    probs = jnp.exp(scores - log_ref[0, 0])
    grad_probs = dot(g, v, ((1,), (1,)))
    total = jnp.sum(probs * grad_probs, axis=1, keepdims=True)
    grad_scores = (probs * (grad_probs - total)).astype(BF16)
    dq = gathered(dot(grad_scores, k) * SCALE, rows)
    cosine, sine = cos_ref[...], -sin_ref[...]
    for i in range(0, dq.shape[1], 128):
        dq_ref[:, i : i + 128] = turn(dq[:, i : i + 128], cosine, sine).astype(BF16)
    dk_ref[...] = jnp.zeros_like(dk_ref)
    dv_ref[...] = jnp.zeros_like(dv_ref)
    here = pl.ds(window_of(dp, span), span)
    dk = dot(grad_scores, q, ((0,), (0,))).astype(BF16)
    dk_ref[here] = dk.reshape(span, rows, dk.shape[1])
    dv = dot(probs.astype(BF16), g, ((0,), (0,))).astype(BF16)
    dv_ref[here] = dv.reshape(span, rows, dv.shape[1])


def attend_back(dp, starts, queries, keys, values, logs_in, grad, cosine, sine, micro, rows, nd):
    grid, mine, theirs, column, logs, _ = attention_specs(micro, rows, nd)
    table = pl.BlockSpec((rows, 128), lambda m, h, *_: (0, 0))
    return pl.pallas_call(
        functools.partial(attend_back_body, nd // 2 + 1),
        grid_spec=pltpu.PrefetchScalarGridSpec(
            num_scalar_prefetch=1,
            grid=grid,
            in_specs=[column, mine, theirs, theirs, logs, mine, table, table],
            out_specs=[mine, theirs, theirs],
        ),
        out_shape=[
            jax.ShapeDtypeStruct(queries.shape, BF16),
            jax.ShapeDtypeStruct(keys.shape, BF16),
            jax.ShapeDtypeStruct(values.shape, BF16),
        ],
        compiler_params=pltpu.CompilerParams(vmem_limit_bytes=48 * 2**20),
        cost_estimate=cost(25),
    )(dp.reshape(1), starts, queries, keys, values, logs_in, grad, cosine, sine)


def input_body(
    ne,
    nd,
    n_ref,
    dq_ref,
    dk_ref,
    dv_ref,
    cos_ref,
    sin_ref,
    wq_ref,
    wk_ref,
    wv_ref,
    tokens_ref,
    gain_ref,
    res_ref,
    wq_out,
    wk_out,
    wv_out,
    tok_out,
    gain_out,
    dk_turned,
):
    normed = n_ref[...]
    cosine, sine = cos_ref[...], -sin_ref[...]
    for i in range(0, dk_ref.shape[1], 128):
        part = dk_ref[:, i : i + 128].astype(F32)
        dk_turned[:, i : i + 128] = turn(part, cosine, sine).astype(BF16)
    tile = 256
    for grad, out in ((dq_ref, wq_out), (dk_turned, wk_out), (dv_ref, wv_out)):
        share = out.shape[1] // ne
        for c in range(0, grad.shape[1], tile):
            y = dot(normed, grad[:, c : c + tile], ((0,), (0,))).astype(BF16)
            for e in range(ne):
                for d in range(nd):
                    r = (e * nd + d) * share
                    out[d, e * share : (e + 1) * share, c : c + tile] = y[r : r + share]
    back = (
        dot(dq_ref[...], wq_ref[...], ((1,), (1,)))
        + dot(dk_turned[...], wk_ref[...], ((1,), (1,)))
        + dot(dv_ref[...], wv_ref[...], ((1,), (1,)))
    )
    x = tokens_ref[...].astype(F32)
    r = rms_scale(x)
    scaled = back * gain_ref[...]
    gain_out[...] = jnp.sum(back * x * r, axis=0, keepdims=True)
    tok_out[...] = (
        res_ref[...] + r * scaled - x * (r * r * r) * jnp.mean(scaled * x, axis=1, keepdims=True)
    )


def input_grads(ne, nd, normed, dq, dk, dv, cosine, sine, weights, tokens, gain, grad_residual):
    rows, width = tokens.shape
    share = width // (ne * nd)
    return pl.pallas_call(
        functools.partial(input_body, ne, nd),
        out_shape=[jax.ShapeDtypeStruct((nd, ne * share, w.shape[1]), BF16) for w in weights]
        + [
            jax.ShapeDtypeStruct((rows, width), F32),
            jax.ShapeDtypeStruct((1, width), F32),
        ],
        in_specs=[VMEM] * 12,
        out_specs=[VMEM] * 5,
        scratch_shapes=[pltpu.VMEM(dk.shape, BF16)],
        compiler_params=pltpu.CompilerParams(vmem_limit_bytes=48 * 2**20),
        cost_estimate=cost(10),
    )(normed, dq, dk, dv, cosine, sine, *weights, tokens, gain, grad_residual)


def per_device(
    tokens,
    segments,
    routes,
    first_gain,
    w_query,
    w_key,
    w_value,
    w_out,
    second_gain,
    w_router,
    w_gate,
    w_up,
    w_down,
    cotangent,
):
    micro, rows, width = tokens.shape
    ne, nd = lax.axis_size("ep"), lax.axis_size("dp")
    ep, dp = lax.axis_index("ep"), lax.axis_index("dp")
    groups = HEADS // KV_HEADS
    kv_width = KV_HEADS * HEAD_DIM
    every = micro * rows
    inputs = tokens.reshape(every, width).astype(F32)
    grad_output = cotangent.reshape(every, width).astype(F32)

    query_pos = dp * rows + jnp.arange(rows, dtype=jnp.int32)
    halfway = HEAD_DIM // 2
    frequency = ROPE_BASE ** (-(jnp.arange(halfway, dtype=F32) * 2.0 / HEAD_DIM))
    angles = query_pos.astype(F32)[:, None] * frequency[None, :]
    lanes = 2 * HEAD_DIM // halfway
    sign = jnp.where(jnp.arange(2 * HEAD_DIM) % HEAD_DIM < halfway, -1.0, 1.0).astype(F32)
    cosine = jnp.tile(jnp.cos(angles), (micro, lanes))
    sine = jnp.tile(jnp.sin(angles), (micro, lanes)) * sign

    tokens_flat = tokens.reshape(every, width)
    gain_one = first_gain.reshape(1, width)
    normed_one, query_rot, key_rot, value_own = project(
        tokens_flat, gain_one, cosine, sine, w_query, w_key, w_value
    )

    ids = jnp.arange(128, dtype=jnp.int32)
    counts = jnp.sum((segments[:, 0, :, None] == ids).astype(F32), axis=1)
    counts = jnp.concatenate([counts, jnp.zeros((8 - micro, 128), F32)], axis=0)

    cot_own = cotangent.reshape(every, width)

    def around(value, k):
        return lax.ppermute(value, "ep", [(i, (i + k) % ne) for i in range(ne)])

    cots = [cot_own] + [around(cot_own, k) for k in range(1, ne)]
    key_all, value_all, count_all = gather(ne, nd, (key_rot, value_own, counts), (), 0, 25)

    totals = jnp.sum(count_all[:, :micro], axis=0)
    lower = (ids[None, None, :] < segments[:, 0, :, None]).astype(F32)
    starts = jnp.sum(lower * totals[:, None, :], axis=2).astype(jnp.int32)
    starts = starts.reshape(every, 1)
    attn_low, logs = attend(dp, starts, query_rot, key_all, value_all, micro, rows, nd)
    residual = inputs + jnp.dot(attn_low, w_out, preferred_element_type=F32)
    inv_two = rms_scale(residual)
    normed_two = (residual * inv_two * second_gain).astype(BF16)
    logits = jnp.dot(normed_two, w_router, preferred_element_type=F32)
    routing = routes.reshape(every, routes.shape[2])
    chosen = jnp.any(
        routing[:, :, None] == jnp.arange(EXPERTS, dtype=jnp.int32)[None, None, :], axis=1
    )
    masked = jnp.where(chosen, logits, MASKED)
    terms = jnp.where(chosen, jnp.exp(masked - jnp.max(masked, axis=1, keepdims=True)), 0.0)
    gate_probs = terms / jnp.sum(terms, axis=1, keepdims=True)
    marked = jnp.where(chosen, gate_probs, -1.0).T

    normed_all, marked_all = gather(ne, nd, (), (normed_two, marked), 1, 38)
    here = EXPERTS // ne
    probs_here = lax.dynamic_slice_in_dim(marked_all, ep * here, here, axis=1)
    probs_here = (
        probs_here.reshape(ne, here, micro, rows)
        .transpose(0, 2, 1, 3)
        .reshape(ne * micro, here, rows)
    )
    nb = bit_count(nd)
    orders = [order[:-1][::-1] for order in gather_orders(nd)]
    mix, grad_in, pair_dots, kept_a, kept_b, landed_a, landed_b = experts(
        normed_all.reshape(ne * every, width),
        cots,
        probs_here,
        w_gate,
        w_up,
        w_down,
        micro,
        rows,
        ne,
        nd,
        6,
    )
    pair_dots = pair_dots.reshape(here, ne, every).transpose(1, 0, 2)

    grads_a, grads_b, grad_back, dots_all = reduce(
        ne,
        nd,
        [
            (kept, order[1:], landed, False)
            for kept, landed, order in (
                (kept_a, landed_a, orders[0]),
                (kept_b, landed_b, orders[1]),
            )
        ],
        (grad_in.reshape(ne, every, width),),
        (pair_dots,),
        2,
        40,
    )
    pair_dot = dots_all.reshape(EXPERTS, every).T
    grad_logits = gate_probs * (
        pair_dot - jnp.sum(gate_probs * pair_dot, axis=1, keepdims=True)
    )
    grad_w_router = jnp.einsum(
        "td,te->de", normed_two.astype(F32), grad_logits, precision=HIGHEST
    )
    grad_normed_two = (
        jnp.einsum("te,de->td", grad_logits, w_router.astype(F32), precision=HIGHEST)
        + grad_back.astype(F32)
    )
    scaled_two = grad_normed_two * second_gain
    grad_gain_two = jnp.sum(grad_normed_two * residual * inv_two, axis=0)
    grad_residual = (
        grad_output
        + inv_two * scaled_two
        - residual * inv_two**3 * jnp.mean(scaled_two * residual, axis=-1, keepdims=True)
    )
    residual_low = grad_residual.astype(BF16)
    grad_w_out = jnp.einsum("tf,td->fd", attn_low, residual_low, preferred_element_type=F32)
    grad_attn = jnp.einsum("td,fd->tf", residual_low, w_out, preferred_element_type=F32).astype(
        BF16
    )
    grad_query, grad_key_all, grad_value_all = attend_back(
        dp,
        starts,
        query_rot,
        key_all,
        value_all,
        logs,
        grad_attn,
        cosine,
        sine,
        micro,
        rows,
        nd,
    )
    whole = [[0] + order for order in orders]
    grad_key, grad_value = reduce(
        ne,
        nd,
        [(grad_key_all, whole[0], None, False), (grad_value_all, whole[1], None, False)],
        (),
        (),
        3,
        25,
    )

    grads = jnp.stack([grads_a, grads_b], axis=1)
    grads = grads.reshape((here,) + grads.shape[2:]).astype(F32)
    share = width // nd
    grad_w_gate, grad_w_up = grads[:, :share], grads[:, share : 2 * share]
    grad_w_down = jnp.concatenate(
        [
            grads[:, at : at + w_down.shape[1] // nd]
            for at in range(2 * share, grads.shape[1], w_down.shape[1] // nd)
        ],
        axis=2,
    )
    grad_w_query, grad_w_key, grad_w_value, grad_tokens, grad_gain_one = input_grads(
        ne,
        nd,
        normed_one,
        grad_query,
        grad_key,
        grad_value,
        cosine,
        sine,
        (w_query, w_key, w_value),
        tokens_flat,
        gain_one,
        grad_residual,
    )

    small = jnp.concatenate(
        [
            grad_w_router,
            grad_gain_one.reshape(width, 1),
            grad_gain_two[:, None],
            jnp.zeros((width, 128 - EXPERTS - 2), F32),
        ],
        axis=1,
    )

    def by_owner(grad):
        share = grad.shape[0] // (ne * nd)
        return grad.astype(BF16).reshape(ne, nd, share, grad.shape[1]).transpose(1, 0, 2, 3)

    def blocks_of(grad):
        return grad.reshape(nd, ne, -1, grad.shape[2])

    dense = [
        blocks_of(grad_w_query),
        by_owner(grad_w_out),
        blocks_of(grad_w_key),
        blocks_of(grad_w_value),
        by_owner(small),
    ]
    *dense, mix_own = reduce(
        ne,
        nd,
        [(v, whole[i % 2], None, True) for i, v in enumerate(dense)],
        (mix.reshape(ne, every, width),),
        (),
        4,
        60,
    )
    d_query, d_out, d_key, d_value, d_small = (v.astype(F32) for v in dense)
    output = (residual + mix_own.astype(F32)).astype(BF16).reshape(tokens.shape)
    return (
        output,
        grad_tokens.reshape(tokens.shape),
        d_small[:, EXPERTS],
        d_query,
        d_key,
        d_value,
        d_out,
        d_small[:, EXPERTS + 1],
        d_small[:, :EXPERTS],
        grad_w_gate,
        grad_w_up,
        grad_w_down,
    )


def solution(mesh):
    in_specs = (
        P(None, ("ep", "dp"), None),
        P(None, "ep", "dp"),
        P(None, ("ep", "dp"), None),
        P(),
        P(),
        P(),
        P(),
        P(),
        P(),
        P(),
        P("ep", None, None),
        P("ep", None, None),
        P("ep", None, None),
        P(None, ("ep", "dp"), None),
    )
    out_specs = (
        P(None, ("ep", "dp"), None),
        P(None, ("ep", "dp"), None),
        P(("ep", "dp")),
        P(("ep", "dp"), None),
        P(("ep", "dp"), None),
        P(("ep", "dp"), None),
        P(("ep", "dp"), None),
        P(("ep", "dp")),
        P(("ep", "dp"), None),
        P("ep", "dp", None),
        P("ep", "dp", None),
        P("ep", "dp", None),
    )
    return jax.shard_map(
        per_device, mesh=mesh, in_specs=in_specs, out_specs=out_specs, check_vma=False
    )
```

```python
import functools

import jax
import jax.numpy as jnp
from jax import lax
from jax.experimental import pallas as pl
from jax.experimental.pallas import tpu as pltpu
from jax.sharding import PartitionSpec as P

HEADS = 16
KV_HEADS = 8
HEAD_DIM = 64
EXPERTS = 32
CAP = 64
EPSILON = 1e-06
ROPE_BASE = 10000.0
MASKED = -1e30
HIGHEST = lax.Precision.HIGHEST
MESH = pl.DeviceIdType.MESH
BF16 = jnp.bfloat16
F32 = jnp.float32
VMEM = pl.BlockSpec(memory_space=pltpu.VMEM)
ANY = pl.BlockSpec(memory_space=pl.ANY)
DMA = pltpu.SemaphoreType.DMA


def bit_count(n):
    return n.bit_length() - 1


def masks(bits):
    out = [0]
    for b in bits:
        out = out + [m | (1 << b) for m in out]
    return out


def gather_orders(n):
    bits = list(range(bit_count(n)))
    return (bits[1:] + bits[:1], bits[:0:-1] + bits[:1])


def greet(ep, dp, ne, nd):
    barrier = pltpu.get_barrier_semaphore()
    for k in range(1, ne):
        pl.semaphore_signal(
            barrier, inc=1, device_id={"ep": lax.rem(ep + k, ne)}, device_id_type=MESH
        )
    for b in range(bit_count(nd)):
        pl.semaphore_signal(
            barrier, inc=1, device_id={"dp": jnp.bitwise_xor(dp, 1 << b)}, device_id_type=MESH
        )
    pl.semaphore_wait(barrier, ne - 1 + bit_count(nd))


def remote(src, dst, send, recv, where):
    return pltpu.make_async_remote_copy(
        src_ref=src, dst_ref=dst, send_sem=send, recv_sem=recv, device_id=where, device_id_type=MESH
    )


def gather_body(ne, nd, n_dp, n_ep, *refs):
    n_in = n_dp + n_ep
    ins, outs, sems = refs[:n_in], refs[n_in : 2 * n_in], refs[2 * n_in :]
    ep, dp = lax.axis_index("ep"), lax.axis_index("dp")
    own_sem, dp_send, dp_recv, ep_send, ep_recv = sems
    greet(ep, dp, ne, nd)
    own = []
    for a in range(n_in):
        me = dp if a < n_dp else ep
        copy = pltpu.make_async_copy(ins[a], outs[a].at[me], own_sem.at[a])
        copy.start()
        own.append(copy)

    def dp_copy(a, t, m):
        order = gather_orders(nd)[a % 2]
        block = jnp.bitwise_xor(dp, m)
        k = (1 << t) - 1 + masks(order[:t]).index(m)
        return remote(
            ins[a] if m == 0 else outs[a].at[block],
            outs[a].at[block],
            dp_send.at[a, k],
            dp_recv.at[a, k],
            {"dp": jnp.bitwise_xor(dp, 1 << order[t])},
        )

    def ep_copy(a, s, way):
        shard = lax.rem(ep - way * s + ne, ne)
        src = ins[n_dp + a] if s == 0 else outs[n_dp + a].at[shard]
        k = 0 if way == 1 else 1
        return remote(
            src,
            outs[n_dp + a].at[shard],
            ep_send.at[a, k, s],
            ep_recv.at[a, k, s],
            {"ep": lax.rem(ep + way + ne, ne)},
        )

    def sends(s, way):
        if way == 1:
            return (ep >= s) & (ep < ne - 1)
        return (ep + s <= ne - 1) & (ep >= 1)

    def receives(s, way):
        if way == 1:
            return ep >= 1 + s
        return ep + 1 + s <= ne - 1

    def ep_start(s):
        for a in range(n_ep):
            for way in (1, -1):

                @pl.when(sends(s, way))
                def _(a=a, way=way):
                    ep_copy(a, s, way).start()

    def ep_wait(s):
        for a in range(n_ep):
            for way in (1, -1):

                @pl.when(receives(s, way))
                def _(a=a, way=way):
                    ep_copy(a, s, way).wait_recv()

    dp_steps = bit_count(nd) if n_dp else 0
    ep_steps = ne - 1 if n_ep else 0
    for t in range(dp_steps):
        for a in range(n_dp):
            dp_copy(a, t, 0).start()
    for t in range(max(dp_steps, ep_steps) + 1):
        if 0 < t <= dp_steps:
            for a in range(n_dp):
                order = gather_orders(nd)[a % 2]
                for m in masks(order[: t - 1]):
                    dp_copy(a, t - 1, m).wait_recv()
                    for later in range(t, dp_steps):
                        dp_copy(a, later, m | (1 << order[t - 1])).start()
        if 0 < t <= ep_steps:
            ep_wait(t - 1)
        if t < ep_steps:
            ep_start(t)
    for t in range(dp_steps):
        for a in range(n_dp):
            for m in masks(gather_orders(nd)[a % 2][:t]):
                dp_copy(a, t, m).wait_send()
    for s in range(ep_steps):
        for a in range(n_ep):
            for way in (1, -1):

                @pl.when(sends(s, way))
                def _(a=a, s=s, way=way):
                    ep_copy(a, s, way).wait_send()

    for c in own:
        c.wait()


def cost(us):
    return pl.CostEstimate(flops=0, bytes_accessed=int(us * 3.0e6), transcendentals=0)


def gather(ne, nd, dp_arrays, ep_arrays, collective, us):
    arrays = list(dp_arrays) + list(ep_arrays)
    counts = [nd] * len(dp_arrays) + [ne] * len(ep_arrays)
    a, b = max(len(dp_arrays), 1), max(len(ep_arrays), 1)
    return pl.pallas_call(
        functools.partial(gather_body, ne, nd, len(dp_arrays), len(ep_arrays)),
        out_shape=[
            jax.ShapeDtypeStruct((n,) + v.shape, v.dtype) for n, v in zip(counts, arrays)
        ],
        in_specs=[ANY] * len(arrays),
        out_specs=[ANY] * len(arrays),
        scratch_shapes=[
            DMA((len(arrays),)),
            DMA((a, nd - 1)),
            DMA((a, nd - 1)),
            DMA((b, 2, ne - 1)),
            DMA((b, 2, ne - 1)),
        ],
        compiler_params=pltpu.CompilerParams(
            collective_id=collective, has_side_effects=True, vmem_limit_bytes=60 * 2**20
        ),
        cost_estimate=cost(us),
    )(*arrays)


def add_into(ref, arrived):
    if len(ref.shape) > 2:

        @pl.loop(0, ref.shape[0])
        def _(i):
            add_into(ref.at[i], arrived.at[i])

    else:
        ref[...] = (ref[...].astype(F32) + arrived[...].astype(F32)).astype(ref.dtype)


class PairSum:
    def __init__(self, dp, order, sources, held, extra, landing, load_sem, send_sem, recv_sem):
        self.dp, self.order, self.held, self.landing = dp, order, held, landing
        self.send_sem, self.recv_sem = send_sem, recv_sem
        self.extra = extra
        self.loads = [
            pltpu.make_async_copy(src, dst, load_sem.at[i])
            for i, (src, dst) in enumerate(zip(sources, (held, extra)))
        ]
        self.index = 0
        for b in order:
            side = jnp.bitwise_and(lax.shift_right_logical(dp, b), 1)
            self.index = self.index + (side << self.place(b))

    def place(self, bit):
        return sorted(self.order).index(bit)

    def copies(self, t):
        order = self.order
        partner = jnp.bitwise_xor(self.index, 1 << self.place(order[t]))
        first = sum(1 << (len(order) - 1 - i) for i in range(t))
        return [
            (
                m,
                first + j,
                remote(
                    self.held.at[jnp.bitwise_xor(partner, m)],
                    self.landing.at[first + j],
                    self.send_sem.at[first + j],
                    self.recv_sem.at[first + j],
                    {"dp": jnp.bitwise_xor(self.dp, 1 << order[t])},
                ),
            )
            for j, m in enumerate(masks([self.place(b) for b in order[t + 1 :]]))
        ]

    def load(self):
        for copy in self.loads:
            copy.start()

    def step(self, t):
        if t == 0:
            for copy in self.loads:
                copy.wait()
            if len(self.loads) > 1:
                add_into(self.held, self.extra)
        elif t <= len(self.order):
            for m, k, copy in self.copies(t - 1):
                copy.wait_recv()
                add_into(self.held.at[jnp.bitwise_xor(self.index, m)], self.landing.at[k])
        if t < len(self.order):
            for m, k, copy in self.copies(t):
                copy.start()

    def own(self):
        return self.held.at[self.index]

    def wait_sends(self):
        for t in range(len(self.order)):
            for m, k, copy in self.copies(t):
                copy.wait_send()


class LineSum:
    def __init__(self, ep, ne, blocks, landing, send_sem, recv_sem):
        self.ep, self.ne, self.blocks, self.landing = ep, ne, blocks, landing
        self.send_sem, self.recv_sem = send_sem, recv_sem

    def copy(self, dest, way):
        k = 0 if way == 1 else 1
        return remote(
            self.blocks.at[dest],
            self.landing.at[k, dest],
            self.send_sem.at[k, dest],
            self.recv_sem.at[k, dest],
            {"ep": lax.rem(self.ep + way + self.ne, self.ne)},
        )

    def turn(self, t, way):
        ep, ne = self.ep, self.ne
        dest = ep + ne - 1 - t if way == 1 else ep + t - (ne - 1)
        has = dest <= ne - 1 if way == 1 else dest >= 0
        inner = ep >= 1 if way == 1 else ep <= ne - 2
        return dest, has, inner

    def step(self, t):
        for way in (1, -1):
            dest, has, inner = self.turn(t, way)

            @pl.when(has & inner)
            def _(way=way, dest=dest):
                self.copy(dest, way).wait_recv()
                add_into(self.blocks.at[dest], self.landing.at[0 if way == 1 else 1, dest])

            if t < self.ne - 1:

                @pl.when(has)
                def _(way=way, dest=dest):
                    self.copy(dest, way).start()

    def own(self):
        return self.blocks.at[self.ep]

    def wait_sends(self):
        for t in range(self.ne - 1):
            for way in (1, -1):
                dest, has, inner = self.turn(t, way)

                @pl.when(has)
                def _(way=way, dest=dest):
                    self.copy(dest, way).wait_send()


def shape_at(array, where):
    return tuple(len(range(*w.indices(n))) for w, n in zip(where, array.shape)) + array.shape[len(where) :]


def reduce_body(ne, nd, pairs, n_line, n_swap, *refs):
    refs = list(refs)

    def take(n):
        return [refs.pop(0) for _ in range(n)]

    n_pair = len(pairs)
    n_extra = sum(p[2] for p in pairs)
    n_both = sum(p[3] for p in pairs)
    n_sum = n_pair + n_line
    ins, extra_ins, swap_ins = take(n_sum), take(n_extra), take(n_swap)
    outs, swap_outs = take(n_sum), take(n_swap)
    held, extras, pair_in = take(n_sum), take(n_extra), take(n_pair)
    both_in, line_in = take(n_both), take(n_line)
    load_sem, out_sem, dp_send, dp_recv, ep_send, ep_recv, swap_send, swap_recv = refs
    ep, dp = lax.axis_index("ep"), lax.axis_index("dp")
    sums, then = [], []
    for a, (order, where, has_extra, both) in enumerate(pairs):
        sources = [ins[a].at[where] if where else ins[a]]
        extra = extras.pop(0) if has_extra else None
        if has_extra:
            source = extra_ins.pop(0)
            sources.append(source.at[where] if where else source)
        sums.append(
            PairSum(
                dp,
                order,
                sources,
                held[a],
                extra,
                pair_in[a],
                load_sem.at[a],
                dp_send.at[a],
                dp_recv.at[a],
            )
        )
        if both:
            i = len(then)
            then.append(
                LineSum(ep, ne, sums[a].own(), both_in[i], ep_send.at[i], ep_recv.at[i])
            )
    lines, line_loads = [], []
    for i in range(n_line):
        a = n_pair + i
        line_loads.append(pltpu.make_async_copy(ins[a], held[a], load_sem.at[a, 0]))
        lines.append(
            LineSum(
                ep, ne, held[a], line_in[i], ep_send.at[n_both + i], ep_recv.at[n_both + i]
            )
        )
    for copy in line_loads:
        copy.start()
    for each in sums:
        each.load()
    greet(ep, dp, ne, nd)
    swaps = []
    for a in range(n_swap):
        src, dst = swap_ins[a], swap_outs[a]
        own = pltpu.make_async_copy(src.at[ep], dst.at[ep], load_sem.at[n_sum + a, 0])
        own.start()
        swaps.append(own)
        for k in range(1, ne):
            to = lax.rem(ep + k, ne)
            copy = remote(
                src.at[to], dst.at[ep], swap_send.at[a, k - 1], swap_recv.at[a, k - 1], {"ep": to}
            )
            copy.start()
            swaps.append(copy)
    for copy in line_loads:
        copy.wait()
    steps = max([len(p[0]) + 1 for p in pairs] + [ne if n_line else 0])
    for t in range(steps):
        if t < ne:
            for each in lines:
                each.step(t)
        for each in sums:
            each.step(t)
    for t in range(ne):
        for each in then:
            each.step(t)
    results, after = [], iter(then)
    for a in range(n_sum):
        if a >= n_pair:
            src = lines[a - n_pair].own()
        else:
            src = next(after).own() if pairs[a][3] else sums[a].own()
        copy = pltpu.make_async_copy(src, outs[a], out_sem.at[a])
        copy.start()
        results.append(copy)
    for each in sums + then + lines:
        each.wait_sends()
    for copy in swaps + results:
        copy.wait()


def reduce(ne, nd, pairs, lines, swaps, collective, us):
    arrays = [p[0] for p in pairs] + list(lines)
    extras = [p[3] for p in pairs if p[3] is not None]
    kinds = tuple((tuple(p[1]), p[2], p[3] is not None, p[4]) for p in pairs)
    shapes = [shape_at(p[0], p[2]) if p[2] else p[0].shape for p in pairs]
    boths = [s for s, p in zip(shapes, pairs) if p[4]]
    results = [s[2:] if p[4] else s[1:] for s, p in zip(shapes, pairs)]
    results += [v.shape[1:] for v in lines]
    scratch = shapes + [v.shape for v in lines]
    scratch += [s for s, p in zip(shapes, pairs) if p[3] is not None]
    scratch += [(s[0] - 1,) + s[1:] for s in shapes]
    scratch += [(2,) + s[1:] for s in boths] + [(2,) + v.shape for v in lines]
    some = lambda n: max(n, 1)
    line_count = some(len(lines) + len(boths))
    deep = max([s[0] - 1 for s in shapes] + [1])
    return pl.pallas_call(
        functools.partial(reduce_body, ne, nd, kinds, len(lines), len(swaps)),
        out_shape=[jax.ShapeDtypeStruct(s, BF16) for s in results]
        + [jax.ShapeDtypeStruct(v.shape, v.dtype) for v in swaps],
        in_specs=[ANY] * (len(arrays) + len(extras) + len(swaps)),
        out_specs=[ANY] * (len(arrays) + len(swaps)),
        scratch_shapes=[pltpu.VMEM(s, BF16) for s in scratch]
        + [
            DMA((len(arrays) + len(swaps), 2)),
            DMA((len(arrays),)),
            DMA((some(len(pairs)), deep)),
            DMA((some(len(pairs)), deep)),
            DMA((line_count, 2, ne)),
            DMA((line_count, 2, ne)),
            DMA((some(len(swaps)), ne - 1)),
            DMA((some(len(swaps)), ne - 1)),
        ],
        compiler_params=pltpu.CompilerParams(
            collective_id=collective, has_side_effects=True, vmem_limit_bytes=60 * 2**20
        ),
        cost_estimate=cost(us),
    )(*arrays, *extras, *swaps)


def dot(a, b, dims=((1,), (0,))):
    return lax.dot_general(a, b, (dims, ((), ())), preferred_element_type=F32)


def expert_body(ne, nd, micro, rows, *refs):
    cots, refs = refs[:ne], refs[ne:]
    normed_ref, probs_ref, gate_ref, up_ref, down_ref = refs[:5]
    mix_ref, grad_ref, dots_ref = refs[5:8]
    kept, landed, whole = refs[8:10], refs[10:12], refs[12:14]
    rows_in, cots_in, picks, first, second, keep, send, arrived, leaving = refs[14:23]
    load_sem, store_sem, send_sem, recv_sem, free_sem, far_send, far_recv = refs[23:]
    e = pl.program_id(0)
    last = pl.num_programs(0) - 1
    ep, dp = lax.axis_index("ep"), lax.axis_index("dp")
    other = {"dp": jnp.bitwise_xor(dp, 1)}
    every = micro * rows
    blocks = ne * micro
    width = first.shape[1]
    n_exp = rows_in.shape[1]

    def exchange():
        return remote(send, arrived, send_sem, recv_sem, other)

    def loads():
        out = [pltpu.make_async_copy(normed_ref, first, load_sem.at[ne])]
        for k in range(ne):
            at = pl.multiple_of(lax.rem(ep - k + ne, ne) * every, every)
            out.append(
                pltpu.make_async_copy(cots[k], second.at[pl.ds(at, every)], load_sem.at[k])
            )
        return out

    def block_at(s):
        return pl.ds(pl.multiple_of(s * rows, rows), rows)

    def returned(t):
        k, m = t // micro, lax.rem(t, micro)
        return lax.rem(ep + k, ne) * micro + m

    def stores(t):
        s = returned(t)
        return (
            pltpu.make_async_copy(
                first.at[block_at(s)], mix_ref.at[block_at(s)], store_sem.at[0, t]
            ),
            pltpu.make_async_copy(
                second.at[block_at(s)], grad_ref.at[block_at(s)], store_sem.at[1, t]
            ),
        )

    def far(i, n):
        return remote(
            leaving.at[i],
            landed[i].at[:, n],
            far_send.at[i],
            far_recv.at[i, n],
            {"dp": jnp.bitwise_xor(dp, 1 << first_bits(nd)[i])},
        )

    def last_copy():
        return pltpu.make_async_copy(keep, whole[1], load_sem.at[0])

    def collect():
        exchange().wait_recv()
        pieces = keep.shape[0]
        n = (e - 1) // 2
        for i, bit in enumerate(first_bits(nd)):

            def put(side, i=i, bit=bit):
                for j in range(pieces):
                    value = (keep[j].astype(F32) + arrived[j].astype(F32)).astype(BF16)
                    at = (j >> bit << (bit - 1)) | (j & ((1 << (bit - 1)) - 1))
                    if (j >> (bit - 1)) & 1 == side:
                        kept[i][at, 0] = value
                    else:
                        leaving[i, at] = value

            @pl.when((lax.rem(e - 1, 2) == i) & (n < n_exp // 2 - 1))
            def _(i=i, bit=bit, put=put):
                @pl.when(n > 0)
                def _():
                    far(i, n - 1).wait_send()

                mine = jnp.bitwise_and(lax.shift_right_logical(dp, bit), 1)

                @pl.when(mine == 0)
                def _():
                    put(0)

                @pl.when(mine == 1)
                def _():
                    put(1)

                far(i, n).start()

            @pl.when((lax.rem(e - 1, 2) == i) & (n == n_exp // 2 - 1))
            def _(i=i):
                add_into(keep, arrived)
                if i == 0:
                    whole[0][...] = keep[...]
                else:
                    last_copy().start()

    @pl.when(e == 0)
    def _():
        for copy in loads():
            copy.start()
        barrier = pltpu.get_barrier_semaphore()
        met = [0] + sorted(set(first_bits(nd)))
        for bit in met:
            pl.semaphore_signal(
                barrier,
                inc=1,
                device_id={"dp": jnp.bitwise_xor(dp, 1 << bit)},
                device_id_type=MESH,
            )
        pl.semaphore_wait(barrier, len(met))
        before = lax.broadcasted_iota(jnp.int32, (rows, rows), 0)
        after = lax.broadcasted_iota(jnp.int32, (rows, rows), 1)
        earlier = (before < after).astype(BF16)
        slot = lax.broadcasted_iota(jnp.int32, (n_exp, CAP, rows), 1)
        for copy in loads():
            copy.wait()

        @pl.loop(0, blocks)
        def _(s):
            at = block_at(s)
            probs = probs_ref[s]
            hit = probs >= 0.0
            rank = dot(hit.astype(BF16), earlier)
            rank = jnp.where(hit, rank, -1.0).astype(jnp.int32)
            pick = jnp.broadcast_to(rank[:, None, :], (n_exp, CAP, rows)) == slot
            pick_f = pick.astype(F32)
            flat = pick_f.reshape(n_exp * CAP, rows).astype(BF16)
            picks[s] = flat
            rows_in[s] = dot(flat, first[at, :]).astype(BF16).reshape(n_exp, CAP, width)
            cots_in[s] = dot(flat, second[at, :]).astype(BF16).reshape(n_exp, CAP, width)

    @pl.when(e < last)
    def _():
        x = rows_in[:, e].reshape(blocks * CAP, width)
        c = cots_in[:, e].reshape(blocks * CAP, width)
        flat = picks[:, pl.ds(pl.multiple_of(e * CAP, CAP), CAP), :].astype(F32)
        p = jnp.sum(flat * probs_ref[:, pl.ds(e, 1), :], axis=2, keepdims=True)
        p = p.reshape(blocks * CAP, 1)
        w_gate, w_up, w_down = gate_ref[0], up_ref[0], down_ref[0]
        gate_pre = dot(x, w_gate)
        up_pre = dot(x, w_up)
        sigma = jax.nn.sigmoid(gate_pre)
        silu = gate_pre * sigma
        hidden = (silu * up_pre).astype(BF16)
        out = dot(hidden, w_down) * p
        back = dot(c, w_down, ((1,), (1,)))
        wide = hidden.astype(F32)
        pair = jnp.sum(wide * back, axis=1, keepdims=True)
        back = back * p
        grad_up = (back * silu).astype(BF16)
        grad_gate = (back * up_pre * (sigma * (1.0 + gate_pre * (1.0 - sigma)))).astype(BF16)
        scaled = (wide * p).astype(BF16)
        grad_x = dot(grad_gate, w_gate, ((1,), (1,))) + dot(grad_up, w_up, ((1,), (1,)))

        dots_ref[0] = jnp.sum(flat * pair.reshape(blocks, CAP, 1), axis=1)

        @pl.when(e > 0)
        def _():
            collect()
            pl.semaphore_signal(free_sem, inc=1, device_id=other, device_id_type=MESH)
            exchange().wait_send()
            pl.semaphore_wait(free_sem, 1)

        def split(value, offset):
            value = value.astype(BF16)
            piece, columns = value.shape[0] // nd, keep.shape[2]

            def put(even, odd):
                for i in range(nd):
                    ref = odd if i % 2 else even
                    for j in range(value.shape[1] // columns):
                        at = offset + j * piece
                        ref[i // 2, at : at + piece] = value[
                            i * piece : (i + 1) * piece, j * columns : (j + 1) * columns
                        ]

            @pl.when(jnp.bitwise_and(dp, 1) == 0)
            def _():
                put(keep, send)

            @pl.when(jnp.bitwise_and(dp, 1) == 1)
            def _():
                put(send, keep)

        share = width // nd
        split(dot(scaled, c, ((0,), (0,))), 2 * share)
        split(dot(x, grad_gate, ((0,), (0,))), 0)
        split(dot(x, grad_up, ((0,), (0,))), share)
        exchange().start()

        rows_in[:, e] = grad_x.astype(BF16).reshape(blocks, CAP, width)
        cots_in[:, e] = out.astype(BF16).reshape(blocks, CAP, width)

    @pl.when(e == last)
    def _():
        @pl.loop(0, blocks)
        def _(t):
            s = returned(t)
            at = block_at(s)
            flat = picks[s]
            for done, slots in ((first, cots_in), (second, rows_in)):
                value = dot(flat, slots[s].reshape(n_exp * CAP, width), ((0,), (0,)))
                done[at, :] = value.astype(BF16)
            for copy in stores(t):
                copy.start()

            @pl.when(t == 1)
            def _():
                collect()
                exchange().wait_send()

        @pl.loop(0, blocks)
        def _(t):
            for copy in stores(t):
                copy.wait()

        last_copy().wait()
        for i in range(2):
            far(i, n_exp // 2 - 2).wait_send()

            @pl.loop(0, n_exp // 2 - 1)
            def _(n, i=i):
                far(i, n).wait_recv()


def first_bits(nd):
    return [order[-2] for order in gather_orders(nd)]


def experts(normed, cots, probs, w_gate, w_up, w_down, micro, rows, ne, nd, collective):
    n_exp, width, inner = w_gate.shape
    blocks = ne * micro
    half = nd // 2
    packed = 2 * width // nd + (inner // nd) * (width // inner)
    full = (blocks * rows, width)
    one = pl.Buffered(1)
    weight = lambda e: (jnp.minimum(e, n_exp - 1), 0, 0)
    early = n_exp // 2 - 1
    part = (half // 2, early, packed, inner)
    kept = pl.BlockSpec(
        (half // 2, 1, packed, inner),
        lambda e: (0, jnp.minimum(jnp.maximum(e - 1, 0) // 2, early - 1), 0, 0),
    )
    last = (half, packed, inner)
    return pl.pallas_call(
        functools.partial(expert_body, ne, nd, micro, rows),
        grid=(n_exp + 1,),
        in_specs=[ANY] * (ne + 1)
        + [
            pl.BlockSpec(probs.shape, lambda e: (0, 0, 0), pipeline_mode=one),
            pl.BlockSpec((1, width, inner), weight),
            pl.BlockSpec((1, width, inner), weight),
            pl.BlockSpec((1, inner, width), weight),
        ],
        out_specs=[ANY, ANY, pl.BlockSpec((1, blocks, rows), weight), kept, kept, ANY, ANY]
        + [pl.BlockSpec(last, lambda e: (0, 0, 0), pipeline_mode=one), ANY],
        scratch_shapes=[
            pltpu.VMEM((blocks, n_exp, CAP, width), BF16),
            pltpu.VMEM((blocks, n_exp, CAP, width), BF16),
            pltpu.VMEM((blocks, n_exp * CAP, rows), BF16),
            pltpu.VMEM(full, BF16),
            pltpu.VMEM(full, BF16),
            pltpu.VMEM((half, packed, inner), BF16),
            pltpu.VMEM((half, packed, inner), BF16),
            pltpu.VMEM((half, packed, inner), BF16),
            pltpu.VMEM((2, half // 2, packed, inner), BF16),
            DMA((ne + 1,)),
            DMA((2, blocks)),
            DMA,
            DMA,
            pltpu.SemaphoreType.REGULAR,
            DMA((2,)),
            DMA((2, early)),
        ],
        out_shape=[
            jax.ShapeDtypeStruct(full, BF16),
            jax.ShapeDtypeStruct(full, BF16),
            jax.ShapeDtypeStruct((n_exp, blocks, rows), F32),
        ]
        + [jax.ShapeDtypeStruct(part, BF16)] * 4
        + [jax.ShapeDtypeStruct(last, BF16)] * 2,
        compiler_params=pltpu.CompilerParams(
            vmem_limit_bytes=62 * 2**20,
            dimension_semantics=("arbitrary",),
            collective_id=collective,
            has_side_effects=True,
        ),
        cost_estimate=cost(75),
    )(*cots, normed, probs, w_gate, w_up, w_down)


def rms_scale(values):
    return lax.rsqrt(jnp.mean(values * values, axis=-1, keepdims=True) + EPSILON)


def partner(x):
    lane = lax.broadcasted_iota(jnp.int32, x.shape, 1)
    half = HEAD_DIM // 2
    low = lax.rem(lane, HEAD_DIM) < half
    return jnp.where(low, pltpu.roll(x, x.shape[1] - half, 1), pltpu.roll(x, half, 1))


def turn(x, cosine, sine):
    return x * cosine + partner(x) * sine


def project_body(
    tokens_ref, gain_ref, cos_ref, sin_ref, wq_ref, wk_ref, wv_ref, n_ref, q_ref, k_ref, v_ref, *rest
):
    wq, wk, wv, sem = rest
    loads = [
        pltpu.make_async_copy(src, dst, sem.at[i])
        for i, (src, dst) in enumerate(((wk_ref, wk), (wv_ref, wv), (wq_ref, wq)))
    ]
    for copy in loads:
        copy.start()
    x = tokens_ref[...].astype(F32)
    n_ref[...] = (x * rms_scale(x) * gain_ref[...]).astype(BF16)
    normed = n_ref[...]
    cosine, sine = cos_ref[...], sin_ref[...]
    tile = 256
    for copy, (w, out, turned) in zip(
        loads, ((wk, k_ref, True), (wv, v_ref, False), (wq, q_ref, True))
    ):
        copy.wait()
        for c in range(0, w.shape[1], tile):
            y = dot(normed, w[:, c : c + tile])
            if turned:
                for i in range(0, tile, 128):
                    out[:, c + i : c + i + 128] = turn(y[:, i : i + 128], cosine, sine).astype(BF16)
            else:
                out[:, c : c + tile] = y.astype(BF16)


def project(tokens, gain, cosine, sine, w_query, w_key, w_value):
    rows, width = tokens.shape
    shapes = [width, w_query.shape[1], w_key.shape[1], w_value.shape[1]]
    return pl.pallas_call(
        project_body,
        out_shape=[jax.ShapeDtypeStruct((rows, n), BF16) for n in shapes],
        in_specs=[VMEM] * 4 + [ANY] * 3,
        out_specs=[VMEM] * 4,
        scratch_shapes=[pltpu.VMEM(w.shape, BF16) for w in (w_query, w_key, w_value)] + [DMA((3,))],
        compiler_params=pltpu.CompilerParams(vmem_limit_bytes=60 * 2**20),
        cost_estimate=cost(5),
    )(tokens, gain, cosine, sine, w_query, w_key, w_value)


def spread(x):
    lane = lax.broadcasted_iota(jnp.int32, (x.shape[0], 128), 1)
    low = lane < HEAD_DIM
    zero = jnp.zeros((), x.dtype)
    first, second = x[:, :128], x[:, 128:]
    return jnp.concatenate(
        [
            jnp.where(low, first, zero),
            jnp.where(low, pltpu.roll(first, HEAD_DIM, 1), zero),
            jnp.where(low, zero, pltpu.roll(second, HEAD_DIM, 1)),
            jnp.where(low, zero, second),
        ],
        axis=0,
    )


def gathered(x, rows):
    lane = lax.broadcasted_iota(jnp.int32, (rows, 128), 1)
    low = lane < HEAD_DIM
    h = [x[i * rows : (i + 1) * rows] for i in range(4)]
    return jnp.concatenate(
        [
            jnp.where(low, h[0], pltpu.roll(h[1], HEAD_DIM, 1)),
            jnp.where(low, pltpu.roll(h[2], HEAD_DIM, 1), h[3]),
        ],
        axis=1,
    )


def window_of(dp, span):
    return jnp.maximum(dp - (span - 1), 0)


def window_scores(dp, span, rows, starts_ref, q, k):
    keys = k.shape[0]
    scores = dot(q, k, ((1,), (1,))).reshape(4, rows, keys)
    key_pos = window_of(dp, span) * rows + lax.broadcasted_iota(jnp.int32, (rows, keys), 1)
    query_pos = dp * rows + lax.broadcasted_iota(jnp.int32, (rows, keys), 0)
    allowed = (key_pos <= query_pos) & (key_pos >= starts_ref[...])
    return jnp.where(allowed[None], scores, MASKED).reshape(4 * rows, keys)


def in_window(ref, dp, span):
    block = ref[pl.ds(window_of(dp, span), span)]
    return block.reshape(span * block.shape[1], block.shape[2])


SCALE = HEAD_DIM ** (-0.5)


def attend_body(span, dp_ref, starts_ref, q_ref, k_ref, v_ref, out_ref, log_ref):
    dp = dp_ref[0]
    rows = q_ref.shape[0]
    q = spread(q_ref[...].astype(F32) * SCALE).astype(BF16)
    scores = window_scores(dp, span, rows, starts_ref, q, in_window(k_ref, dp, span))
    top = jnp.max(scores, axis=1, keepdims=True)
    terms = jnp.exp(scores - top)
    total = jnp.sum(terms, axis=1, keepdims=True)
    log_ref[0, 0] = top + jnp.log(total)
    weights = (terms * (1.0 / total)).astype(BF16)
    out = dot(weights, in_window(v_ref, dp, span))
    out_ref[...] = gathered(out, rows).astype(BF16)


def attention_specs(micro, rows, nd):
    pairs = KV_HEADS // 2
    mine = pl.BlockSpec((rows, 4 * HEAD_DIM), lambda m, h, *_: (m, h))
    theirs = pl.BlockSpec((nd, rows, 2 * HEAD_DIM), lambda m, h, *_: (0, m, h))
    column = pl.BlockSpec((rows, 1), lambda m, h, *_: (m, 0))
    logs = pl.BlockSpec((1, 1, 4 * rows, 1), lambda m, h, *_: (m, h, 0, 0))
    log_shape = jax.ShapeDtypeStruct((micro, pairs, 4 * rows, 1), F32)
    return (micro, pairs), mine, theirs, column, logs, log_shape


def attend(dp, starts, queries, keys, values, micro, rows, nd):
    grid, mine, theirs, column, logs, log_shape = attention_specs(micro, rows, nd)
    return pl.pallas_call(
        functools.partial(attend_body, nd // 2 + 1),
        grid_spec=pltpu.PrefetchScalarGridSpec(
            num_scalar_prefetch=1,
            grid=grid,
            in_specs=[column, mine, theirs, theirs],
            out_specs=[mine, logs],
        ),
        out_shape=[jax.ShapeDtypeStruct(queries.shape, BF16), log_shape],
        compiler_params=pltpu.CompilerParams(vmem_limit_bytes=60 * 2**20),
        cost_estimate=cost(15),
    )(dp.reshape(1), starts, queries, keys, values)


def attend_back_body(span, nd, orders, *refs):
    starts_ref, q_ref, k_ref, v_ref, log_ref, g_ref, cos_ref, sin_ref = refs[:8]
    n = len(orders)
    sources, extras = refs[8 : 8 + n], refs[8 + n : 8 + 2 * n]
    dq_ref, dk_ref, dv_ref = refs[8 + 2 * n : 11 + 2 * n]
    outs, rest = refs[11 + 2 * n : 11 + 3 * n], refs[11 + 3 * n :]
    dp = lax.axis_index("dp")
    step = pl.program_id(0) * pl.num_programs(1) + pl.program_id(1)
    final = pl.num_programs(0) * pl.num_programs(1) - 1
    if n:
        held, more, landing, (load_sem, out_sem, send_sem, recv_sem) = (
            rest[:n],
            rest[n : 2 * n],
            rest[2 * n : 3 * n],
            rest[3 * n :],
        )
        sums = [
            PairSum(
                dp,
                orders[a],
                (sources[a].at[:, 1:], extras[a].at[:, 1:]),
                held[a],
                more[a],
                landing[a],
                load_sem.at[a],
                send_sem.at[a],
                recv_sem.at[a],
            )
            for a in range(n)
        ]

        @pl.when(step == 0)
        def _():
            for each in sums:
                each.load()
            barrier = pltpu.get_barrier_semaphore()
            met = sorted(set(b for order in orders for b in order))
            for bit in met:
                pl.semaphore_signal(
                    barrier,
                    inc=1,
                    device_id={"dp": jnp.bitwise_xor(dp, 1 << bit)},
                    device_id_type=MESH,
                )
            pl.semaphore_wait(barrier, len(met))
            for each in sums:
                each.step(0)

    rows = q_ref.shape[0]
    q = spread(q_ref[...].astype(F32) * SCALE).astype(BF16)
    g = spread(g_ref[...].astype(F32)).astype(BF16)
    k, v = in_window(k_ref, dp, span), in_window(v_ref, dp, span)
    scores = window_scores(dp, span, rows, starts_ref, q, k)
    probs = jnp.exp(scores - log_ref[0, 0])
    grad_probs = dot(g, v, ((1,), (1,)))
    total = jnp.sum(probs * grad_probs, axis=1, keepdims=True)
    grad_scores = (probs * (grad_probs - total)).astype(BF16)
    dq = gathered(dot(grad_scores, k) * SCALE, rows)
    cosine, sine = cos_ref[...], -sin_ref[...]
    for i in range(0, dq.shape[1], 128):
        dq_ref[:, i : i + 128] = turn(dq[:, i : i + 128], cosine, sine).astype(BF16)
    dk_ref[...] = jnp.zeros_like(dk_ref)
    dv_ref[...] = jnp.zeros_like(dv_ref)
    here = pl.ds(window_of(dp, span), span)
    dk = dot(grad_scores, q, ((0,), (0,))).astype(BF16)
    dk_ref[here] = dk.reshape(span, rows, dk.shape[1])
    dv = dot(probs.astype(BF16), g, ((0,), (0,))).astype(BF16)
    dv_ref[here] = dv.reshape(span, rows, dv.shape[1])

    if n:

        @pl.when(step == final)
        def _():
            copies = []
            for t in range(1, max(len(order) for order in orders) + 1):
                for each in sums:
                    each.step(t)
            for a, each in enumerate(sums):
                copies.append(pltpu.make_async_copy(each.own(), outs[a], out_sem.at[a]))
                copies[a].start()
            for each in sums:
                each.wait_sends()
            for copy in copies:
                copy.wait()


def attend_back(
    starts, queries, keys, values, logs_in, grad, cosine, sine, sums, micro, rows, nd, collective
):
    grid, mine, theirs, column, logs, _ = attention_specs(micro, rows, nd)
    table = pl.BlockSpec((rows, 128), lambda m, h, *_: (0, 0))
    n = len(sums)
    shapes = [(v.shape[0], v.shape[1] - 1) + v.shape[2:] for v, _, _ in sums]
    deep = max([s[0] - 1 for s in shapes] + [1])
    scratch = [pltpu.VMEM(s, BF16) for s in shapes] * 2
    scratch += [pltpu.VMEM((s[0] - 1,) + s[1:], BF16) for s in shapes]
    scratch += [DMA((n, 2)), DMA((n,)), DMA((n, deep)), DMA((n, deep))] if n else []
    remote_params = dict(collective_id=collective, has_side_effects=True) if n else {}
    return pl.pallas_call(
        functools.partial(
            attend_back_body, nd // 2 + 1, nd, tuple(tuple(order) for _, order, _ in sums)
        ),
        grid=grid,
        in_specs=[column, mine, theirs, theirs, logs, mine, table, table] + [ANY] * (2 * n),
        out_specs=[mine, theirs, theirs] + [ANY] * n,
        out_shape=[
            jax.ShapeDtypeStruct(queries.shape, BF16),
            jax.ShapeDtypeStruct(keys.shape, BF16),
            jax.ShapeDtypeStruct(values.shape, BF16),
        ]
        + [jax.ShapeDtypeStruct(s[1:], BF16) for s in shapes],
        scratch_shapes=scratch,
        compiler_params=pltpu.CompilerParams(vmem_limit_bytes=60 * 2**20, **remote_params),
        cost_estimate=cost(25),
    )(
        starts,
        queries,
        keys,
        values,
        logs_in,
        grad,
        cosine,
        sine,
        *[v for v, _, _ in sums],
        *[extra for _, _, extra in sums],
    )


def input_body(
    ne,
    nd,
    n_ref,
    dq_ref,
    dk_ref,
    dv_ref,
    cos_ref,
    sin_ref,
    wq_ref,
    wk_ref,
    wv_ref,
    tokens_ref,
    gain_ref,
    res_ref,
    wq_out,
    wk_out,
    wv_out,
    tok_out,
    gain_out,
    dk_turned,
):
    normed = n_ref[...]
    cosine, sine = cos_ref[...], -sin_ref[...]
    for i in range(0, dk_ref.shape[1], 128):
        part = dk_ref[:, i : i + 128].astype(F32)
        dk_turned[:, i : i + 128] = turn(part, cosine, sine).astype(BF16)
    tile = 256
    for grad, out in ((dq_ref, wq_out), (dk_turned, wk_out), (dv_ref, wv_out)):
        share = out.shape[1] // ne
        for c in range(0, grad.shape[1], tile):
            y = dot(normed, grad[:, c : c + tile], ((0,), (0,))).astype(BF16)
            for e in range(ne):
                for d in range(nd):
                    r = (e * nd + d) * share
                    out[d, e * share : (e + 1) * share, c : c + tile] = y[r : r + share]
    back = (
        dot(dq_ref[...], wq_ref[...], ((1,), (1,)))
        + dot(dk_turned[...], wk_ref[...], ((1,), (1,)))
        + dot(dv_ref[...], wv_ref[...], ((1,), (1,)))
    )
    x = tokens_ref[...].astype(F32)
    r = rms_scale(x)
    scaled = back * gain_ref[...]
    gain_out[...] = jnp.sum(back * x * r, axis=0, keepdims=True)
    tok_out[...] = (
        res_ref[...] + r * scaled - x * (r * r * r) * jnp.mean(scaled * x, axis=1, keepdims=True)
    )


def input_grads(ne, nd, normed, dq, dk, dv, cosine, sine, weights, tokens, gain, grad_residual):
    rows, width = tokens.shape
    share = width // (ne * nd)
    return pl.pallas_call(
        functools.partial(input_body, ne, nd),
        out_shape=[jax.ShapeDtypeStruct((nd, ne * share, w.shape[1]), BF16) for w in weights]
        + [
            jax.ShapeDtypeStruct((rows, width), F32),
            jax.ShapeDtypeStruct((1, width), F32),
        ],
        in_specs=[VMEM] * 12,
        out_specs=[VMEM] * 5,
        scratch_shapes=[pltpu.VMEM(dk.shape, BF16)],
        compiler_params=pltpu.CompilerParams(vmem_limit_bytes=60 * 2**20),
        cost_estimate=cost(10),
    )(normed, dq, dk, dv, cosine, sine, *weights, tokens, gain, grad_residual)


def per_device(
    tokens,
    segments,
    routes,
    first_gain,
    w_query,
    w_key,
    w_value,
    w_out,
    second_gain,
    w_router,
    w_gate,
    w_up,
    w_down,
    cotangent,
):
    micro, rows, width = tokens.shape
    ne, nd = lax.axis_size("ep"), lax.axis_size("dp")
    ep, dp = lax.axis_index("ep"), lax.axis_index("dp")
    groups = HEADS // KV_HEADS
    kv_width = KV_HEADS * HEAD_DIM
    every = micro * rows
    inputs = tokens.reshape(every, width).astype(F32)
    grad_output = cotangent.reshape(every, width).astype(F32)

    query_pos = dp * rows + jnp.arange(rows, dtype=jnp.int32)
    halfway = HEAD_DIM // 2
    frequency = ROPE_BASE ** (-(jnp.arange(halfway, dtype=F32) * 2.0 / HEAD_DIM))
    angles = query_pos.astype(F32)[:, None] * frequency[None, :]
    lanes = 2 * HEAD_DIM // halfway
    sign = jnp.where(jnp.arange(2 * HEAD_DIM) % HEAD_DIM < halfway, -1.0, 1.0).astype(F32)
    cosine = jnp.tile(jnp.cos(angles), (micro, lanes))
    sine = jnp.tile(jnp.sin(angles), (micro, lanes)) * sign

    tokens_flat = tokens.reshape(every, width)
    gain_one = first_gain.reshape(1, width)
    normed_one, query_rot, key_rot, value_own = project(
        tokens_flat, gain_one, cosine, sine, w_query, w_key, w_value
    )

    ids = jnp.arange(128, dtype=jnp.int32)
    counts = jnp.sum((segments[:, 0, :, None] == ids).astype(F32), axis=1)
    counts = jnp.concatenate([counts, jnp.zeros((8 - micro, 128), F32)], axis=0)

    cot_own = cotangent.reshape(every, width)

    def around(value, k):
        return lax.ppermute(value, "ep", [(i, (i + k) % ne) for i in range(ne)])

    cots = [cot_own] + [around(cot_own, k) for k in range(1, ne)]
    key_all, value_all, count_all = gather(ne, nd, (key_rot, value_own, counts), (), 0, 25)

    totals = jnp.sum(count_all[:, :micro], axis=0)
    lower = (ids[None, None, :] < segments[:, 0, :, None]).astype(F32)
    starts = jnp.sum(lower * totals[:, None, :], axis=2).astype(jnp.int32)
    starts = starts.reshape(every, 1)
    attn_low, logs = attend(dp, starts, query_rot, key_all, value_all, micro, rows, nd)
    residual = inputs + jnp.dot(attn_low, w_out, preferred_element_type=F32)
    inv_two = rms_scale(residual)
    normed_two = (residual * inv_two * second_gain).astype(BF16)
    logits = jnp.dot(normed_two, w_router, preferred_element_type=F32)
    routing = routes.reshape(every, routes.shape[2])
    chosen = jnp.any(
        routing[:, :, None] == jnp.arange(EXPERTS, dtype=jnp.int32)[None, None, :], axis=1
    )
    masked = jnp.where(chosen, logits, MASKED)
    terms = jnp.where(chosen, jnp.exp(masked - jnp.max(masked, axis=1, keepdims=True)), 0.0)
    gate_probs = terms / jnp.sum(terms, axis=1, keepdims=True)
    marked = jnp.where(chosen, gate_probs, -1.0).T

    normed_all, marked_all = gather(ne, nd, (), (normed_two, marked), 1, 38)
    here = EXPERTS // ne
    probs_here = lax.dynamic_slice_in_dim(marked_all, ep * here, here, axis=1)
    probs_here = (
        probs_here.reshape(ne, here, micro, rows)
        .transpose(0, 2, 1, 3)
        .reshape(ne * micro, here, rows)
    )
    nb = bit_count(nd)
    orders = [order[:-1][::-1] for order in gather_orders(nd)]
    mix, grad_in, pair_dots, *grads = experts(
        normed_all.reshape(ne * every, width),
        cots,
        probs_here,
        w_gate,
        w_up,
        w_down,
        micro,
        rows,
        ne,
        nd,
        6,
    )
    kept, landed, last = grads[:2], grads[2:4], grads[4:]
    pair_dots = pair_dots.reshape(here, ne, every).transpose(1, 0, 2)
    head = (slice(None), slice(0, 1))
    *grads, grad_back, dots_all = reduce(
        ne,
        nd,
        [(last[i], orders[i], None, None, False) for i in range(2)]
        + [(kept[i], orders[i][1:], head, landed[i], False) for i in range(2)],
        (grad_in.reshape(ne, every, width),),
        (pair_dots,),
        2,
        40,
    )
    grads_last, grads_head = grads[:2], grads[2:]
    pair_dot = dots_all.reshape(EXPERTS, every).T
    grad_logits = gate_probs * (
        pair_dot - jnp.sum(gate_probs * pair_dot, axis=1, keepdims=True)
    )
    grad_w_router = jnp.einsum(
        "td,te->de", normed_two.astype(F32), grad_logits, precision=HIGHEST
    )
    grad_normed_two = (
        jnp.einsum("te,de->td", grad_logits, w_router.astype(F32), precision=HIGHEST)
        + grad_back.astype(F32)
    )
    scaled_two = grad_normed_two * second_gain
    grad_gain_two = jnp.sum(grad_normed_two * residual * inv_two, axis=0)
    grad_residual = (
        grad_output
        + inv_two * scaled_two
        - residual * inv_two**3 * jnp.mean(scaled_two * residual, axis=-1, keepdims=True)
    )
    residual_low = grad_residual.astype(BF16)
    grad_w_out = jnp.einsum("tf,td->fd", attn_low, residual_low, preferred_element_type=F32)
    grad_attn = jnp.einsum("td,fd->tf", residual_low, w_out, preferred_element_type=F32).astype(
        BF16
    )
    more = kept[0].shape[1] > 1
    grad_query, grad_key_all, grad_value_all, *grads_more = attend_back(
        starts,
        query_rot,
        key_all,
        value_all,
        logs,
        grad_attn,
        cosine,
        sine,
        [(kept[i], orders[i][1:], landed[i]) for i in range(2)] if more else [],
        micro,
        rows,
        nd,
        5,
    )

    def by_owner(grad):
        share = grad.shape[0] // (ne * nd)
        return grad.astype(BF16).reshape(ne, nd, share, grad.shape[1]).transpose(1, 0, 2, 3)

    full = [[0] + order for order in orders]
    grad_w_out = by_owner(grad_w_out)
    columns = [(slice(None),) * 3 + (slice(i * kv_width, (i + 1) * kv_width),) for i in range(2)]
    grad_key, grad_value, *d_out = reduce(
        ne,
        nd,
        [
            (grad_key_all, full[0], None, None, False),
            (grad_value_all, full[1], None, None, False),
            (grad_w_out, full[0], columns[0], None, True),
            (grad_w_out, full[1], columns[1], None, True),
        ],
        (),
        (),
        3,
        35,
    )
    d_out = jnp.concatenate(d_out, axis=1).astype(F32)

    per_path = [
        jnp.concatenate(
            [grads_head[i]] + ([grads_more[i]] if more else []) + [grads_last[i][None]], axis=0
        )
        for i in range(2)
    ]
    grads = jnp.stack(per_path, axis=1)
    grads = grads.reshape((here,) + grads.shape[2:]).astype(F32)
    share = width // nd
    grad_w_gate, grad_w_up = grads[:, :share], grads[:, share : 2 * share]
    grad_w_down = jnp.concatenate(
        [
            grads[:, at : at + w_down.shape[1] // nd]
            for at in range(2 * share, grads.shape[1], w_down.shape[1] // nd)
        ],
        axis=2,
    )
    grad_w_query, grad_w_key, grad_w_value, grad_tokens, grad_gain_one = input_grads(
        ne,
        nd,
        normed_one,
        grad_query,
        grad_key,
        grad_value,
        cosine,
        sine,
        (w_query, w_key, w_value),
        tokens_flat,
        gain_one,
        grad_residual,
    )

    small = jnp.concatenate(
        [
            grad_w_router,
            grad_gain_one.reshape(width, 1),
            grad_gain_two[:, None],
            jnp.zeros((width, 128 - EXPERTS - 2), F32),
        ],
        axis=1,
    )

    def blocks_of(grad):
        return grad.reshape(nd, ne, -1, grad.shape[2])

    *dense, mix_own = reduce(
        ne,
        nd,
        [
            (blocks_of(grad_w_query), full[0], None, None, True),
            (blocks_of(grad_w_key), full[1], None, None, True),
            (blocks_of(grad_w_value), full[1], None, None, True),
            (by_owner(small), full[0], None, None, True),
        ],
        (mix.reshape(ne, every, width),),
        (),
        4,
        50,
    )
    d_query, d_key, d_value, d_small = (v.astype(F32) for v in dense)
    output = (residual + mix_own.astype(F32)).astype(BF16).reshape(tokens.shape)
    return (
        output,
        grad_tokens.reshape(tokens.shape),
        d_small[:, EXPERTS],
        d_query,
        d_key,
        d_value,
        d_out,
        d_small[:, EXPERTS + 1],
        d_small[:, :EXPERTS],
        grad_w_gate,
        grad_w_up,
        grad_w_down,
    )


def solution(mesh):
    in_specs = (
        P(None, ("ep", "dp"), None),
        P(None, "ep", "dp"),
        P(None, ("ep", "dp"), None),
        P(),
        P(),
        P(),
        P(),
        P(),
        P(),
        P(),
        P("ep", None, None),
        P("ep", None, None),
        P("ep", None, None),
        P(None, ("ep", "dp"), None),
    )
    out_specs = (
        P(None, ("ep", "dp"), None),
        P(None, ("ep", "dp"), None),
        P(("ep", "dp")),
        P(("ep", "dp"), None),
        P(("ep", "dp"), None),
        P(("ep", "dp"), None),
        P(("ep", "dp"), None),
        P(("ep", "dp")),
        P(("ep", "dp"), None),
        P("ep", "dp", None),
        P("ep", "dp", None),
        P("ep", "dp", None),
    )
    return jax.shard_map(
        per_device, mesh=mesh, in_specs=in_specs, out_specs=out_specs, check_vma=False
    )
```

```python
import functools

import jax
import jax.numpy as jnp
from jax import lax
from jax.experimental import pallas as pl
from jax.experimental.pallas import tpu as pltpu
from jax.sharding import PartitionSpec as P

HEADS = 16
KV_HEADS = 8
HEAD_DIM = 64
EXPERTS = 32
CAP = 64
EPSILON = 1e-06
ROPE_BASE = 10000.0
MASKED = -1e30
HIGHEST = lax.Precision.HIGHEST
MESH = pl.DeviceIdType.MESH
BF16 = jnp.bfloat16
F32 = jnp.float32
VMEM = pl.BlockSpec(memory_space=pltpu.VMEM)
ANY = pl.BlockSpec(memory_space=pl.ANY)
DMA = pltpu.SemaphoreType.DMA


def bit_count(n):
    return n.bit_length() - 1


def masks(bits):
    out = [0]
    for b in bits:
        out = out + [m | (1 << b) for m in out]
    return out


def gather_orders(n):
    bits = list(range(bit_count(n)))
    return (bits[1:] + bits[:1], bits[:0:-1] + bits[:1])


def greet(ep, dp, ne, nd):
    barrier = pltpu.get_barrier_semaphore()
    for k in range(1, ne):
        pl.semaphore_signal(
            barrier, inc=1, device_id={"ep": lax.rem(ep + k, ne)}, device_id_type=MESH
        )
    for b in range(bit_count(nd)):
        pl.semaphore_signal(
            barrier, inc=1, device_id={"dp": jnp.bitwise_xor(dp, 1 << b)}, device_id_type=MESH
        )
    pl.semaphore_wait(barrier, ne - 1 + bit_count(nd))


def remote(src, dst, send, recv, where):
    return pltpu.make_async_remote_copy(
        src_ref=src, dst_ref=dst, send_sem=send, recv_sem=recv, device_id=where, device_id_type=MESH
    )


def gather_body(ne, nd, n_dp, n_ep, *refs):
    n_in = n_dp + n_ep
    ins, outs, sems = refs[:n_in], refs[n_in : 2 * n_in], refs[2 * n_in :]
    ep, dp = lax.axis_index("ep"), lax.axis_index("dp")
    own_sem, dp_send, dp_recv, ep_send, ep_recv = sems
    greet(ep, dp, ne, nd)
    own = []
    for a in range(n_in):
        me = dp if a < n_dp else ep
        copy = pltpu.make_async_copy(ins[a], outs[a].at[me], own_sem.at[a])
        copy.start()
        own.append(copy)

    def dp_copy(a, t, m):
        order = gather_orders(nd)[a % 2]
        block = jnp.bitwise_xor(dp, m)
        k = (1 << t) - 1 + masks(order[:t]).index(m)
        return remote(
            ins[a] if m == 0 else outs[a].at[block],
            outs[a].at[block],
            dp_send.at[a, k],
            dp_recv.at[a, k],
            {"dp": jnp.bitwise_xor(dp, 1 << order[t])},
        )

    def ep_copy(a, s, way):
        shard = lax.rem(ep - way * s + ne, ne)
        src = ins[n_dp + a] if s == 0 else outs[n_dp + a].at[shard]
        k = 0 if way == 1 else 1
        return remote(
            src,
            outs[n_dp + a].at[shard],
            ep_send.at[a, k, s],
            ep_recv.at[a, k, s],
            {"ep": lax.rem(ep + way + ne, ne)},
        )

    def sends(s, way):
        if way == 1:
            return (ep >= s) & (ep < ne - 1)
        return (ep + s <= ne - 1) & (ep >= 1)

    def receives(s, way):
        if way == 1:
            return ep >= 1 + s
        return ep + 1 + s <= ne - 1

    def ep_start(s):
        for a in range(n_ep):
            for way in (1, -1):

                @pl.when(sends(s, way))
                def _(a=a, way=way):
                    ep_copy(a, s, way).start()

    def ep_wait(s):
        for a in range(n_ep):
            for way in (1, -1):

                @pl.when(receives(s, way))
                def _(a=a, way=way):
                    ep_copy(a, s, way).wait_recv()

    dp_steps = bit_count(nd) if n_dp else 0
    ep_steps = ne - 1 if n_ep else 0
    for t in range(dp_steps):
        for a in range(n_dp):
            dp_copy(a, t, 0).start()
    for t in range(max(dp_steps, ep_steps) + 1):
        if 0 < t <= dp_steps:
            for a in range(n_dp):
                order = gather_orders(nd)[a % 2]
                for m in masks(order[: t - 1]):
                    dp_copy(a, t - 1, m).wait_recv()
                    for later in range(t, dp_steps):
                        dp_copy(a, later, m | (1 << order[t - 1])).start()
        if 0 < t <= ep_steps:
            ep_wait(t - 1)
        if t < ep_steps:
            ep_start(t)
    for t in range(dp_steps):
        for a in range(n_dp):
            for m in masks(gather_orders(nd)[a % 2][:t]):
                dp_copy(a, t, m).wait_send()
    for s in range(ep_steps):
        for a in range(n_ep):
            for way in (1, -1):

                @pl.when(sends(s, way))
                def _(a=a, s=s, way=way):
                    ep_copy(a, s, way).wait_send()

    for c in own:
        c.wait()


def cost(us):
    return pl.CostEstimate(flops=0, bytes_accessed=int(us * 3.0e6), transcendentals=0)


def gather(ne, nd, dp_arrays, ep_arrays, collective, us):
    arrays = list(dp_arrays) + list(ep_arrays)
    counts = [nd] * len(dp_arrays) + [ne] * len(ep_arrays)
    a, b = max(len(dp_arrays), 1), max(len(ep_arrays), 1)
    return pl.pallas_call(
        functools.partial(gather_body, ne, nd, len(dp_arrays), len(ep_arrays)),
        out_shape=[
            jax.ShapeDtypeStruct((n,) + v.shape, v.dtype) for n, v in zip(counts, arrays)
        ],
        in_specs=[ANY] * len(arrays),
        out_specs=[ANY] * len(arrays),
        scratch_shapes=[
            DMA((len(arrays),)),
            DMA((a, nd - 1)),
            DMA((a, nd - 1)),
            DMA((b, 2, ne - 1)),
            DMA((b, 2, ne - 1)),
        ],
        compiler_params=pltpu.CompilerParams(
            collective_id=collective, has_side_effects=True, vmem_limit_bytes=60 * 2**20
        ),
        cost_estimate=cost(us),
    )(*arrays)


def add_into(ref, arrived):
    if len(ref.shape) > 2:

        @pl.loop(0, ref.shape[0])
        def _(i):
            add_into(ref.at[i], arrived.at[i])

    else:
        ref[...] = (ref[...].astype(F32) + arrived[...].astype(F32)).astype(ref.dtype)


class PairSum:
    def __init__(self, dp, order, loads, held, extra, landing, send_sem, recv_sem):
        self.dp, self.order, self.held, self.landing = dp, order, held, landing
        self.send_sem, self.recv_sem = send_sem, recv_sem
        self.extra, self.loads = extra, loads
        self.index = 0
        for b in order:
            side = jnp.bitwise_and(lax.shift_right_logical(dp, b), 1)
            self.index = self.index + (side << self.place(b))

    def place(self, bit):
        return sorted(self.order).index(bit)

    def copies(self, t):
        order = self.order
        partner = jnp.bitwise_xor(self.index, 1 << self.place(order[t]))
        first = sum(1 << (len(order) - 1 - i) for i in range(t))
        return [
            (
                m,
                first + j,
                remote(
                    self.held.at[jnp.bitwise_xor(partner, m)],
                    self.landing.at[first + j],
                    self.send_sem.at[first + j],
                    self.recv_sem.at[first + j],
                    {"dp": jnp.bitwise_xor(self.dp, 1 << order[t])},
                ),
            )
            for j, m in enumerate(masks([self.place(b) for b in order[t + 1 :]]))
        ]

    def load(self):
        for copy in self.loads:
            copy.start()

    def step(self, t):
        if t == 0:
            for copy in self.loads:
                copy.wait()
            if self.extra is not None:
                add_into(self.held, self.extra)
        elif t <= len(self.order):
            for m, k, copy in self.copies(t - 1):
                copy.wait_recv()
                add_into(self.held.at[jnp.bitwise_xor(self.index, m)], self.landing.at[k])
        if t < len(self.order):
            for m, k, copy in self.copies(t):
                copy.start()

    def own(self):
        return self.held.at[self.index]

    def wait_sends(self):
        for t in range(len(self.order)):
            for m, k, copy in self.copies(t):
                copy.wait_send()


class LineSum:
    def __init__(self, ep, ne, blocks, landing, send_sem, recv_sem):
        self.ep, self.ne, self.blocks, self.landing = ep, ne, blocks, landing
        self.send_sem, self.recv_sem = send_sem, recv_sem

    def copy(self, dest, way):
        k = 0 if way == 1 else 1
        return remote(
            self.blocks.at[dest],
            self.landing.at[k, dest],
            self.send_sem.at[k, dest],
            self.recv_sem.at[k, dest],
            {"ep": lax.rem(self.ep + way + self.ne, self.ne)},
        )

    def turn(self, t, way):
        ep, ne = self.ep, self.ne
        dest = ep + ne - 1 - t if way == 1 else ep + t - (ne - 1)
        has = dest <= ne - 1 if way == 1 else dest >= 0
        inner = ep >= 1 if way == 1 else ep <= ne - 2
        return dest, has, inner

    def step(self, t):
        for way in (1, -1):
            dest, has, inner = self.turn(t, way)

            @pl.when(has & inner)
            def _(way=way, dest=dest):
                self.copy(dest, way).wait_recv()
                add_into(self.blocks.at[dest], self.landing.at[0 if way == 1 else 1, dest])

            if t < self.ne - 1:

                @pl.when(has)
                def _(way=way, dest=dest):
                    self.copy(dest, way).start()

    def own(self):
        return self.blocks.at[self.ep]

    def wait_sends(self):
        for t in range(self.ne - 1):
            for way in (1, -1):
                dest, has, inner = self.turn(t, way)

                @pl.when(has)
                def _(way=way, dest=dest):
                    self.copy(dest, way).wait_send()


def shape_at(array, where):
    return tuple(len(range(*w.indices(n))) for w, n in zip(where, array.shape)) + array.shape[len(where) :]


def reduce_body(ne, nd, pairs, line_parts, n_swap, *refs):
    refs = list(refs)

    def take(n):
        return [refs.pop(0) for _ in range(n)]

    n_pair, n_line = len(pairs), len(line_parts)
    n_extra = sum(p[2] for p in pairs)
    n_both = sum(p[3] for p in pairs)
    n_sum = n_pair + n_line
    ins, extra_ins, swap_ins = take(n_sum), take(n_extra), take(n_swap)
    outs, swap_outs = take(n_sum), take(n_swap)
    held, extras, pair_in = take(n_sum), take(n_extra), take(n_pair)
    both_in, line_in = take(n_both), take(n_line)
    load_sem, out_sem, dp_send, dp_recv, ep_send, ep_recv, swap_send, swap_recv = refs
    ep, dp = lax.axis_index("ep"), lax.axis_index("dp")
    sums, then = [], []
    for a, (order, where, has_extra, both) in enumerate(pairs):
        targets = [(ins[a], held[a])]
        extra = extras.pop(0) if has_extra else None
        if has_extra:
            targets.append((extra_ins.pop(0), extra))
        loads = [
            pltpu.make_async_copy(src.at[where] if where else src, dst, load_sem.at[a, i])
            for i, (src, dst) in enumerate(targets)
        ]
        sums.append(
            PairSum(dp, order, loads, held[a], extra, pair_in[a], dp_send.at[a], dp_recv.at[a])
        )
        if both:
            i = len(then)
            then.append(
                LineSum(ep, ne, sums[a].own(), both_in[i], ep_send.at[i], ep_recv.at[i])
            )
    lines, line_loads = [], []
    for i in range(n_line):
        a = n_pair + i
        src = ins[a].at[line_parts[i]] if line_parts[i] else ins[a]
        line_loads.append(pltpu.make_async_copy(src, held[a], load_sem.at[a, 0]))
        lines.append(
            LineSum(
                ep, ne, held[a], line_in[i], ep_send.at[n_both + i], ep_recv.at[n_both + i]
            )
        )
    for copy in line_loads:
        copy.start()
    for each in sums:
        each.load()
    greet(ep, dp, ne, nd)
    swaps = []
    for a in range(n_swap):
        src, dst = swap_ins[a], swap_outs[a]
        own = pltpu.make_async_copy(src.at[ep], dst.at[ep], load_sem.at[n_sum + a, 0])
        own.start()
        swaps.append(own)
        for k in range(1, ne):
            to = lax.rem(ep + k, ne)
            copy = remote(
                src.at[to], dst.at[ep], swap_send.at[a, k - 1], swap_recv.at[a, k - 1], {"ep": to}
            )
            copy.start()
            swaps.append(copy)
    for copy in line_loads:
        copy.wait()
    steps = max([len(p[0]) + 1 for p in pairs] + [ne if n_line else 0])
    for t in range(steps):
        if t < ne:
            for each in lines:
                each.step(t)
        for each in sums:
            each.step(t)
    for t in range(ne):
        for each in then:
            each.step(t)
    results, after = [], iter(then)
    for a in range(n_sum):
        if a >= n_pair:
            src = lines[a - n_pair].own()
        else:
            src = next(after).own() if pairs[a][3] else sums[a].own()
        copy = pltpu.make_async_copy(src, outs[a], out_sem.at[a])
        copy.start()
        results.append(copy)
    for each in sums + then + lines:
        each.wait_sends()
    for copy in swaps + results:
        copy.wait()


def reduce(ne, nd, pairs, lines, swaps, collective, us):
    line_parts = tuple(where for _, where in lines)
    line_shapes = [shape_at(v, where) if where else v.shape for v, where in lines]
    lines = [v for v, _ in lines]
    arrays = [p[0] for p in pairs] + list(lines)
    extras = [p[3] for p in pairs if p[3] is not None]
    kinds = tuple((tuple(p[1]), p[2], p[3] is not None, p[4]) for p in pairs)
    shapes = [shape_at(p[0], p[2]) if p[2] else p[0].shape for p in pairs]
    boths = [s for s, p in zip(shapes, pairs) if p[4]]
    results = [s[2:] if p[4] else s[1:] for s, p in zip(shapes, pairs)]
    results += [s[1:] for s in line_shapes]
    scratch = shapes + line_shapes
    scratch += [s for s, p in zip(shapes, pairs) if p[3] is not None]
    scratch += [(s[0] - 1,) + s[1:] for s in shapes]
    scratch += [(2,) + s[1:] for s in boths] + [(2,) + s for s in line_shapes]
    some = lambda n: max(n, 1)
    line_count = some(len(lines) + len(boths))
    deep = max([s[0] - 1 for s in shapes] + [1])
    return pl.pallas_call(
        functools.partial(reduce_body, ne, nd, kinds, line_parts, len(swaps)),
        out_shape=[jax.ShapeDtypeStruct(s, BF16) for s in results]
        + [jax.ShapeDtypeStruct(v.shape, v.dtype) for v in swaps],
        in_specs=[ANY] * (len(arrays) + len(extras) + len(swaps)),
        out_specs=[ANY] * (len(arrays) + len(swaps)),
        scratch_shapes=[pltpu.VMEM(s, BF16) for s in scratch]
        + [
            DMA((len(arrays) + len(swaps), 2)),
            DMA((len(arrays),)),
            DMA((some(len(pairs)), deep)),
            DMA((some(len(pairs)), deep)),
            DMA((line_count, 2, ne)),
            DMA((line_count, 2, ne)),
            DMA((some(len(swaps)), ne - 1)),
            DMA((some(len(swaps)), ne - 1)),
        ],
        compiler_params=pltpu.CompilerParams(
            collective_id=collective, has_side_effects=True, vmem_limit_bytes=60 * 2**20
        ),
        cost_estimate=cost(us),
    )(*arrays, *extras, *swaps)


def dot(a, b, dims=((1,), (0,))):
    return lax.dot_general(a, b, (dims, ((), ())), preferred_element_type=F32)


def expert_body(ne, nd, micro, rows, *refs):
    cots, refs = refs[:ne], refs[ne:]
    normed_ref, probs_ref, gate_ref, up_ref, down_ref = refs[:5]
    mix_ref, grad_ref, dots_ref = refs[5:8]
    kept, landed, whole = refs[8:10], refs[10:12], refs[12:14]
    rows_in, cots_in, picks, first, second, keep, send, arrived, leaving = refs[14:23]
    load_sem, store_sem, send_sem, recv_sem, free_sem, far_send, far_recv = refs[23:]
    e = pl.program_id(0)
    last = pl.num_programs(0) - 1
    ep, dp = lax.axis_index("ep"), lax.axis_index("dp")
    other = {"dp": jnp.bitwise_xor(dp, 1)}
    every = micro * rows
    blocks = ne * micro
    width = first.shape[1]
    n_exp = rows_in.shape[1]

    def exchange():
        return remote(send, arrived, send_sem, recv_sem, other)

    def loads():
        out = [pltpu.make_async_copy(normed_ref, first, load_sem.at[ne])]
        for k in range(ne):
            at = pl.multiple_of(lax.rem(ep - k + ne, ne) * every, every)
            out.append(
                pltpu.make_async_copy(cots[k], second.at[pl.ds(at, every)], load_sem.at[k])
            )
        return out

    def block_at(s):
        return pl.ds(pl.multiple_of(s * rows, rows), rows)

    def returned(t):
        k, m = t // micro, lax.rem(t, micro)
        return lax.rem(ep + k, ne) * micro + m

    def stores(t):
        s = returned(t)
        return (
            pltpu.make_async_copy(
                first.at[block_at(s)], mix_ref.at[block_at(s)], store_sem.at[0, t]
            ),
            pltpu.make_async_copy(
                second.at[block_at(s)], grad_ref.at[block_at(s)], store_sem.at[1, t]
            ),
        )

    def far(i, n):
        return remote(
            leaving.at[i],
            landed[i].at[:, n],
            far_send.at[i],
            far_recv.at[i, n],
            {"dp": jnp.bitwise_xor(dp, 1 << first_bits(nd)[i])},
        )

    def last_copy():
        return pltpu.make_async_copy(keep, whole[1], load_sem.at[0])

    def collect():
        exchange().wait_recv()
        pieces = keep.shape[0]
        n = (e - 1) // 2
        for i, bit in enumerate(first_bits(nd)):

            def put(side, i=i, bit=bit):
                for j in range(pieces):
                    value = (keep[j].astype(F32) + arrived[j].astype(F32)).astype(BF16)
                    at = (j >> bit << (bit - 1)) | (j & ((1 << (bit - 1)) - 1))
                    if (j >> (bit - 1)) & 1 == side:
                        kept[i][at, 0] = value
                    else:
                        leaving[i, at] = value

            @pl.when((lax.rem(e - 1, 2) == i) & (n < n_exp // 2 - 1))
            def _(i=i, bit=bit, put=put):
                @pl.when(n > 0)
                def _():
                    far(i, n - 1).wait_send()

                mine = jnp.bitwise_and(lax.shift_right_logical(dp, bit), 1)

                @pl.when(mine == 0)
                def _():
                    put(0)

                @pl.when(mine == 1)
                def _():
                    put(1)

                far(i, n).start()

            @pl.when((lax.rem(e - 1, 2) == i) & (n == n_exp // 2 - 1))
            def _(i=i):
                add_into(keep, arrived)
                if i == 0:
                    whole[0][...] = keep[...]
                else:
                    last_copy().start()

    @pl.when(e == 0)
    def _():
        for copy in loads():
            copy.start()
        barrier = pltpu.get_barrier_semaphore()
        met = [0] + sorted(set(first_bits(nd)))
        for bit in met:
            pl.semaphore_signal(
                barrier,
                inc=1,
                device_id={"dp": jnp.bitwise_xor(dp, 1 << bit)},
                device_id_type=MESH,
            )
        pl.semaphore_wait(barrier, len(met))
        before = lax.broadcasted_iota(jnp.int32, (rows, rows), 0)
        after = lax.broadcasted_iota(jnp.int32, (rows, rows), 1)
        earlier = (before < after).astype(BF16)
        slot = lax.broadcasted_iota(jnp.int32, (n_exp, CAP, rows), 1)
        for copy in loads():
            copy.wait()

        @pl.loop(0, blocks)
        def _(s):
            at = block_at(s)
            probs = probs_ref[s]
            hit = probs >= 0.0
            rank = dot(hit.astype(BF16), earlier)
            rank = jnp.where(hit, rank, -1.0).astype(jnp.int32)
            pick = jnp.broadcast_to(rank[:, None, :], (n_exp, CAP, rows)) == slot
            pick_f = pick.astype(F32)
            flat = pick_f.reshape(n_exp * CAP, rows).astype(BF16)
            picks[s] = flat
            rows_in[s] = dot(flat, first[at, :]).astype(BF16).reshape(n_exp, CAP, width)
            cots_in[s] = dot(flat, second[at, :]).astype(BF16).reshape(n_exp, CAP, width)

    @pl.when(e < last)
    def _():
        x = rows_in[:, e].reshape(blocks * CAP, width)
        c = cots_in[:, e].reshape(blocks * CAP, width)
        flat = picks[:, pl.ds(pl.multiple_of(e * CAP, CAP), CAP), :].astype(F32)
        p = jnp.sum(flat * probs_ref[:, pl.ds(e, 1), :], axis=2, keepdims=True)
        p = p.reshape(blocks * CAP, 1)
        w_gate, w_up, w_down = gate_ref[0], up_ref[0], down_ref[0]
        gate_pre = dot(x, w_gate)
        up_pre = dot(x, w_up)
        sigma = jax.nn.sigmoid(gate_pre)
        silu = gate_pre * sigma
        hidden = (silu * up_pre).astype(BF16)
        out = dot(hidden, w_down) * p
        back = dot(c, w_down, ((1,), (1,)))
        wide = hidden.astype(F32)
        pair = jnp.sum(wide * back, axis=1, keepdims=True)
        back = back * p
        grad_up = (back * silu).astype(BF16)
        grad_gate = (back * up_pre * (sigma * (1.0 + gate_pre * (1.0 - sigma)))).astype(BF16)
        scaled = (wide * p).astype(BF16)
        grad_x = dot(grad_gate, w_gate, ((1,), (1,))) + dot(grad_up, w_up, ((1,), (1,)))

        dots_ref[0] = jnp.sum(flat * pair.reshape(blocks, CAP, 1), axis=1)

        @pl.when(e > 0)
        def _():
            collect()
            pl.semaphore_signal(free_sem, inc=1, device_id=other, device_id_type=MESH)
            exchange().wait_send()
            pl.semaphore_wait(free_sem, 1)

        def split(value, offset):
            value = value.astype(BF16)
            piece, columns = value.shape[0] // nd, keep.shape[2]

            def put(even, odd):
                for i in range(nd):
                    ref = odd if i % 2 else even
                    for j in range(value.shape[1] // columns):
                        at = offset + j * piece
                        ref[i // 2, at : at + piece] = value[
                            i * piece : (i + 1) * piece, j * columns : (j + 1) * columns
                        ]

            @pl.when(jnp.bitwise_and(dp, 1) == 0)
            def _():
                put(keep, send)

            @pl.when(jnp.bitwise_and(dp, 1) == 1)
            def _():
                put(send, keep)

        share = width // nd
        split(dot(scaled, c, ((0,), (0,))), 2 * share)
        split(dot(x, grad_gate, ((0,), (0,))), 0)
        split(dot(x, grad_up, ((0,), (0,))), share)
        exchange().start()

        rows_in[:, e] = grad_x.astype(BF16).reshape(blocks, CAP, width)
        cots_in[:, e] = out.astype(BF16).reshape(blocks, CAP, width)

    @pl.when(e == last)
    def _():
        @pl.loop(0, blocks)
        def _(t):
            s = returned(t)
            at = block_at(s)
            flat = picks[s]
            for done, slots in ((first, cots_in), (second, rows_in)):
                value = dot(flat, slots[s].reshape(n_exp * CAP, width), ((0,), (0,)))
                done[at, :] = value.astype(BF16)
            for copy in stores(t):
                copy.start()

            @pl.when(t == 1)
            def _():
                collect()
                exchange().wait_send()

        @pl.loop(0, blocks)
        def _(t):
            for copy in stores(t):
                copy.wait()

        last_copy().wait()
        for i in range(2):
            far(i, n_exp // 2 - 2).wait_send()

            @pl.loop(0, n_exp // 2 - 1)
            def _(n, i=i):
                far(i, n).wait_recv()


def first_bits(nd):
    return [order[-2] for order in gather_orders(nd)]


def experts(normed, cots, probs, w_gate, w_up, w_down, micro, rows, ne, nd, collective):
    n_exp, width, inner = w_gate.shape
    blocks = ne * micro
    half = nd // 2
    packed = 2 * width // nd + (inner // nd) * (width // inner)
    full = (blocks * rows, width)
    one = pl.Buffered(1)
    weight = lambda e: (jnp.minimum(e, n_exp - 1), 0, 0)
    early = n_exp // 2 - 1
    part = (half // 2, early, packed, inner)
    kept = pl.BlockSpec(
        (half // 2, 1, packed, inner),
        lambda e: (0, jnp.minimum(jnp.maximum(e - 1, 0) // 2, early - 1), 0, 0),
    )
    last = (half, packed, inner)
    return pl.pallas_call(
        functools.partial(expert_body, ne, nd, micro, rows),
        grid=(n_exp + 1,),
        in_specs=[ANY] * (ne + 1)
        + [
            pl.BlockSpec(probs.shape, lambda e: (0, 0, 0), pipeline_mode=one),
            pl.BlockSpec((1, width, inner), weight),
            pl.BlockSpec((1, width, inner), weight),
            pl.BlockSpec((1, inner, width), weight),
        ],
        out_specs=[ANY, ANY, pl.BlockSpec((1, blocks, rows), weight), kept, kept, ANY, ANY]
        + [pl.BlockSpec(last, lambda e: (0, 0, 0), pipeline_mode=one), ANY],
        scratch_shapes=[
            pltpu.VMEM((blocks, n_exp, CAP, width), BF16),
            pltpu.VMEM((blocks, n_exp, CAP, width), BF16),
            pltpu.VMEM((blocks, n_exp * CAP, rows), BF16),
            pltpu.VMEM(full, BF16),
            pltpu.VMEM(full, BF16),
            pltpu.VMEM((half, packed, inner), BF16),
            pltpu.VMEM((half, packed, inner), BF16),
            pltpu.VMEM((half, packed, inner), BF16),
            pltpu.VMEM((2, half // 2, packed, inner), BF16),
            DMA((ne + 1,)),
            DMA((2, blocks)),
            DMA,
            DMA,
            pltpu.SemaphoreType.REGULAR,
            DMA((2,)),
            DMA((2, early)),
        ],
        out_shape=[
            jax.ShapeDtypeStruct(full, BF16),
            jax.ShapeDtypeStruct(full, BF16),
            jax.ShapeDtypeStruct((n_exp, blocks, rows), F32),
        ]
        + [jax.ShapeDtypeStruct(part, BF16)] * 4
        + [jax.ShapeDtypeStruct(last, BF16)] * 2,
        compiler_params=pltpu.CompilerParams(
            vmem_limit_bytes=62 * 2**20,
            dimension_semantics=("arbitrary",),
            collective_id=collective,
            has_side_effects=True,
        ),
        cost_estimate=cost(75),
    )(*cots, normed, probs, w_gate, w_up, w_down)


def rms_scale(values):
    return lax.rsqrt(jnp.mean(values * values, axis=-1, keepdims=True) + EPSILON)


def partner(x):
    lane = lax.broadcasted_iota(jnp.int32, x.shape, 1)
    half = HEAD_DIM // 2
    low = lax.rem(lane, HEAD_DIM) < half
    return jnp.where(low, pltpu.roll(x, x.shape[1] - half, 1), pltpu.roll(x, half, 1))


def turn(x, cosine, sine):
    return x * cosine + partner(x) * sine


def project_body(
    tokens_ref, gain_ref, cos_ref, sin_ref, wq_ref, wk_ref, wv_ref, n_ref, q_ref, k_ref, v_ref, *rest
):
    wq, wk, wv, sem = rest
    loads = [
        pltpu.make_async_copy(src, dst, sem.at[i])
        for i, (src, dst) in enumerate(((wk_ref, wk), (wv_ref, wv), (wq_ref, wq)))
    ]
    for copy in loads:
        copy.start()
    x = tokens_ref[...].astype(F32)
    n_ref[...] = (x * rms_scale(x) * gain_ref[...]).astype(BF16)
    normed = n_ref[...]
    cosine, sine = cos_ref[...], sin_ref[...]
    tile = 256
    for copy, (w, out, turned) in zip(
        loads, ((wk, k_ref, True), (wv, v_ref, False), (wq, q_ref, True))
    ):
        copy.wait()
        for c in range(0, w.shape[1], tile):
            y = dot(normed, w[:, c : c + tile])
            if turned:
                for i in range(0, tile, 128):
                    out[:, c + i : c + i + 128] = turn(y[:, i : i + 128], cosine, sine).astype(BF16)
            else:
                out[:, c : c + tile] = y.astype(BF16)


def project(tokens, gain, cosine, sine, w_query, w_key, w_value):
    rows, width = tokens.shape
    shapes = [width, w_query.shape[1], w_key.shape[1], w_value.shape[1]]
    return pl.pallas_call(
        project_body,
        out_shape=[jax.ShapeDtypeStruct((rows, n), BF16) for n in shapes],
        in_specs=[VMEM] * 4 + [ANY] * 3,
        out_specs=[VMEM] * 4,
        scratch_shapes=[pltpu.VMEM(w.shape, BF16) for w in (w_query, w_key, w_value)] + [DMA((3,))],
        compiler_params=pltpu.CompilerParams(vmem_limit_bytes=60 * 2**20),
        cost_estimate=cost(5),
    )(tokens, gain, cosine, sine, w_query, w_key, w_value)


def spread(x):
    lane = lax.broadcasted_iota(jnp.int32, (x.shape[0], 128), 1)
    low = lane < HEAD_DIM
    zero = jnp.zeros((), x.dtype)
    first, second = x[:, :128], x[:, 128:]
    return jnp.concatenate(
        [
            jnp.where(low, first, zero),
            jnp.where(low, pltpu.roll(first, HEAD_DIM, 1), zero),
            jnp.where(low, zero, pltpu.roll(second, HEAD_DIM, 1)),
            jnp.where(low, zero, second),
        ],
        axis=0,
    )


def gathered(x, rows):
    lane = lax.broadcasted_iota(jnp.int32, (rows, 128), 1)
    low = lane < HEAD_DIM
    h = [x[i * rows : (i + 1) * rows] for i in range(4)]
    return jnp.concatenate(
        [
            jnp.where(low, h[0], pltpu.roll(h[1], HEAD_DIM, 1)),
            jnp.where(low, pltpu.roll(h[2], HEAD_DIM, 1), h[3]),
        ],
        axis=1,
    )


def window_of(dp, span):
    return jnp.maximum(dp - (span - 1), 0)


def window_scores(dp, span, rows, starts_ref, q, k):
    keys = k.shape[0]
    scores = dot(q, k, ((1,), (1,))).reshape(4, rows, keys)
    key_pos = window_of(dp, span) * rows + lax.broadcasted_iota(jnp.int32, (rows, keys), 1)
    query_pos = dp * rows + lax.broadcasted_iota(jnp.int32, (rows, keys), 0)
    allowed = (key_pos <= query_pos) & (key_pos >= starts_ref[...])
    return jnp.where(allowed[None], scores, MASKED).reshape(4 * rows, keys)


def in_window(ref, dp, span):
    block = ref[pl.ds(window_of(dp, span), span)]
    return block.reshape(span * block.shape[1], block.shape[2])


SCALE = HEAD_DIM ** (-0.5)


def attend_body(span, dp_ref, starts_ref, q_ref, k_ref, v_ref, out_ref, log_ref):
    dp = dp_ref[0]
    rows = q_ref.shape[0]
    q = spread(q_ref[...].astype(F32) * SCALE).astype(BF16)
    scores = window_scores(dp, span, rows, starts_ref, q, in_window(k_ref, dp, span))
    top = jnp.max(scores, axis=1, keepdims=True)
    terms = jnp.exp(scores - top)
    total = jnp.sum(terms, axis=1, keepdims=True)
    log_ref[0, 0] = top + jnp.log(total)
    weights = (terms * (1.0 / total)).astype(BF16)
    out = dot(weights, in_window(v_ref, dp, span))
    out_ref[...] = gathered(out, rows).astype(BF16)


def attention_specs(micro, rows, nd):
    pairs = KV_HEADS // 2
    mine = pl.BlockSpec((rows, 4 * HEAD_DIM), lambda m, h, *_: (m, h))
    theirs = pl.BlockSpec((nd, rows, 2 * HEAD_DIM), lambda m, h, *_: (0, m, h))
    column = pl.BlockSpec((rows, 1), lambda m, h, *_: (m, 0))
    logs = pl.BlockSpec((1, 1, 4 * rows, 1), lambda m, h, *_: (m, h, 0, 0))
    log_shape = jax.ShapeDtypeStruct((micro, pairs, 4 * rows, 1), F32)
    return (micro, pairs), mine, theirs, column, logs, log_shape


def attend(dp, starts, queries, keys, values, micro, rows, nd):
    grid, mine, theirs, column, logs, log_shape = attention_specs(micro, rows, nd)
    return pl.pallas_call(
        functools.partial(attend_body, nd // 2 + 1),
        grid_spec=pltpu.PrefetchScalarGridSpec(
            num_scalar_prefetch=1,
            grid=grid,
            in_specs=[column, mine, theirs, theirs],
            out_specs=[mine, logs],
        ),
        out_shape=[jax.ShapeDtypeStruct(queries.shape, BF16), log_shape],
        compiler_params=pltpu.CompilerParams(vmem_limit_bytes=60 * 2**20),
        cost_estimate=cost(15),
    )(dp.reshape(1), starts, queries, keys, values)


def attend_back_body(span, ne, nd, orders, *refs):
    refs = list(refs)

    def take(n):
        return [refs.pop(0) for _ in range(n)]

    starts_ref, q_ref, k_ref, v_ref, log_ref, g_ref, cos_ref, sin_ref = take(8)
    n = len(orders)
    sources, extras, (mix_ref,) = take(n), take(n), take(1)
    dq_ref, dk_ref, dv_ref = take(3)
    outs, (mix_out,) = take(n), take(1)
    held, more, landing, (mix_held, mix_in) = take(n), take(n), take(n), take(2)
    load_sem, out_sem, send_sem, recv_sem, mix_sem, line_send, line_recv = refs
    ep, dp = lax.axis_index("ep"), lax.axis_index("dp")
    step = pl.program_id(0) * pl.num_programs(1) + pl.program_id(1)
    final = pl.num_programs(0) * pl.num_programs(1) - 1
    sums = []
    for a in range(n):
        part = pl.ds(1, sources[a].shape[1] - 1)
        loads = [
            pltpu.make_async_copy(src.at[:, part], dst, load_sem.at[a, i])
            for i, (src, dst) in enumerate(((sources[a], held[a]), (extras[a], more[a])))
        ]
        sums.append(
            PairSum(
                dp, orders[a], loads, held[a], more[a], landing[a], send_sem.at[a], recv_sem.at[a]
            )
        )
    line = LineSum(ep, ne, mix_held, mix_in, line_send, line_recv)
    mix_load = pltpu.make_async_copy(
        mix_ref.at[:, pl.ds(0, mix_held.shape[1])], mix_held, mix_sem.at[0]
    )

    @pl.when(step == 0)
    def _():
        mix_load.start()
        for each in sums:
            each.load()
        greet(ep, dp, ne, nd)
        mix_load.wait()
        line.step(0)
        for each in sums:
            each.step(0)

    @pl.when(step == final // 2 + 1)
    def _():
        line.step(1)

    rows = q_ref.shape[0]
    q = spread(q_ref[...].astype(F32) * SCALE).astype(BF16)
    g = spread(g_ref[...].astype(F32)).astype(BF16)
    k, v = in_window(k_ref, dp, span), in_window(v_ref, dp, span)
    scores = window_scores(dp, span, rows, starts_ref, q, k)
    probs = jnp.exp(scores - log_ref[0, 0])
    grad_probs = dot(g, v, ((1,), (1,)))
    total = jnp.sum(probs * grad_probs, axis=1, keepdims=True)
    grad_scores = (probs * (grad_probs - total)).astype(BF16)
    dq = gathered(dot(grad_scores, k) * SCALE, rows)
    cosine, sine = cos_ref[...], -sin_ref[...]
    for i in range(0, dq.shape[1], 128):
        dq_ref[:, i : i + 128] = turn(dq[:, i : i + 128], cosine, sine).astype(BF16)
    dk_ref[...] = jnp.zeros_like(dk_ref)
    dv_ref[...] = jnp.zeros_like(dv_ref)
    here = pl.ds(window_of(dp, span), span)
    dk = dot(grad_scores, q, ((0,), (0,))).astype(BF16)
    dk_ref[here] = dk.reshape(span, rows, dk.shape[1])
    dv = dot(probs.astype(BF16), g, ((0,), (0,))).astype(BF16)
    dv_ref[here] = dv.reshape(span, rows, dv.shape[1])

    @pl.when(step == final)
    def _():
        for t in range(2, ne):
            line.step(t)
        for t in range(1, max([len(order) for order in orders] + [0]) + 1):
            for each in sums:
                each.step(t)
        copies = [pltpu.make_async_copy(line.own(), mix_out, mix_sem.at[1])]
        for a, each in enumerate(sums):
            copies.append(pltpu.make_async_copy(each.own(), outs[a], out_sem.at[a]))
        for copy in copies:
            copy.start()
        for each in sums + [line]:
            each.wait_sends()
        for copy in copies:
            copy.wait()


def attend_back(
    starts, queries, keys, values, logs_in, grad, cosine, sine, sums, mix, micro, rows, collective
):
    nd, ne = keys.shape[0], mix.shape[0]
    grid, mine, theirs, column, logs, _ = attention_specs(micro, rows, nd)
    table = pl.BlockSpec((rows, 128), lambda m, h, *_: (0, 0))
    n = len(sums)
    shapes = [(v.shape[0], v.shape[1] - 1) + v.shape[2:] for v, _, _ in sums]
    deep = max([s[0] - 1 for s in shapes] + [1])
    some = max(n, 1)
    line = (ne, rows, mix.shape[2])
    return pl.pallas_call(
        functools.partial(
            attend_back_body, nd // 2 + 1, ne, nd, tuple(tuple(order) for _, order, _ in sums)
        ),
        grid=grid,
        in_specs=[column, mine, theirs, theirs, logs, mine, table, table] + [ANY] * (2 * n + 1),
        out_specs=[mine, theirs, theirs] + [ANY] * (n + 1),
        out_shape=[
            jax.ShapeDtypeStruct(queries.shape, BF16),
            jax.ShapeDtypeStruct(keys.shape, BF16),
            jax.ShapeDtypeStruct(values.shape, BF16),
        ]
        + [jax.ShapeDtypeStruct(s[1:], BF16) for s in shapes]
        + [jax.ShapeDtypeStruct(line[1:], BF16)],
        scratch_shapes=[pltpu.VMEM(s, BF16) for s in shapes] * 2
        + [pltpu.VMEM((s[0] - 1,) + s[1:], BF16) for s in shapes]
        + [pltpu.VMEM(line, BF16), pltpu.VMEM((2,) + line, BF16)]
        + [
            DMA((some, 2)),
            DMA((some,)),
            DMA((some, deep)),
            DMA((some, deep)),
            DMA((2,)),
            DMA((2, ne)),
            DMA((2, ne)),
        ],
        compiler_params=pltpu.CompilerParams(
            vmem_limit_bytes=60 * 2**20, collective_id=collective, has_side_effects=True
        ),
        cost_estimate=cost(25),
    )(
        starts,
        queries,
        keys,
        values,
        logs_in,
        grad,
        cosine,
        sine,
        *[v for v, _, _ in sums],
        *[extra for _, _, extra in sums],
        mix,
    )


def finish_body(ne, nd, orders, n_out, *refs):
    refs = list(refs)

    def take(n):
        return [refs.pop(0) for _ in range(n)]

    n_ref, dq_ref, dk_ref, dv_ref, cos_ref, sin_ref, tokens_ref, gain_ref = take(8)
    res_ref, wq_ref, wk_ref, wv_ref, wo_ref, small_ref = take(6)
    (tok_out,) = take(1)
    count = 2 * n_out + 3
    outs, held, pair_in, line_in = take(count), take(count), take(count), take(count)
    dk_turned, wq, wk, wv, res = take(5)
    load_sem, own_sem, out_sem, dp_send, dp_recv, ep_send, ep_recv = refs
    ep, dp = lax.axis_index("ep"), lax.axis_index("dp")
    columns = held[0].shape[3]
    own = [
        pltpu.make_async_copy(src, dst, own_sem.at[i])
        for i, (src, dst) in enumerate(
            ((wq_ref, wq), (wk_ref, wk), (wv_ref, wv), (res_ref, res))
        )
    ]
    sums = []
    for a in range(count):
        loads = []
        if a < n_out or a == count - 1:
            src = wo_ref if a < n_out else small_ref
            at = pl.ds(a * columns if a < n_out else 0, held[a].shape[3])
            loads = [
                pltpu.make_async_copy(src.at[e, :, :, at], held[a].at[:, e], load_sem.at[a, e])
                for e in range(ne)
            ]
        sums.append(
            PairSum(
                dp, orders[a % 2], loads, held[a], None, pair_in[a], dp_send.at[a], dp_recv.at[a]
            )
        )
    lines = [
        LineSum(ep, ne, sums[a].own(), line_in[a], ep_send.at[a], ep_recv.at[a])
        for a in range(count)
    ]
    early, made, small = sums[:n_out], sums[n_out:-1], sums[-1]
    for each in early + [small]:
        each.load()
    for copy in own:
        copy.start()
    greet(ep, dp, ne, nd)
    for each in early:
        each.step(0)

    normed = n_ref[...]
    cosine, sine = cos_ref[...], -sin_ref[...]
    for i in range(0, dk_ref.shape[1], 128):
        part = dk_ref[:, i : i + 128].astype(F32)
        dk_turned[:, i : i + 128] = turn(part, cosine, sine).astype(BF16)
    tile = 256

    def product(grad, first, each):
        share = each.held.shape[2]
        for c in range(0, each.held.shape[3], tile):
            y = dot(normed, grad[:, first + c : first + c + tile], ((0,), (0,))).astype(BF16)
            for e in range(ne):
                for d in range(nd):
                    r = (e * nd + d) * share
                    each.held[d, e, :, c : c + tile] = y[r : r + share]
        each.step(0)

    turns = bit_count(nd)
    for i, each in enumerate(made):
        if i < n_out:
            product(dq_ref, i * columns, each)
        else:
            product((dk_turned, dv_ref)[i - n_out], 0, each)
        if i == 1:
            for first in early:
                first.step(1)
    for copy in own:
        copy.wait()
    back = (
        dot(dq_ref[...], wq[...], ((1,), (1,)))
        + dot(dk_turned[...], wk[...], ((1,), (1,)))
        + dot(dv_ref[...], wv[...], ((1,), (1,)))
    )
    for each in made:
        each.step(1)
    for each in early:
        each.step(2)
    x = tokens_ref[...].astype(F32)
    r = rms_scale(x)
    scaled = back * gain_ref[...]
    tok_out[...] = (
        res[...] + r * scaled - x * (r * r * r) * jnp.mean(scaled * x, axis=1, keepdims=True)
    )
    term = back * x * r
    high = term.astype(BF16)
    low = (term - high.astype(F32)).astype(BF16)
    ones = jnp.ones((x.shape[0], 128), BF16)
    column = dot(high, ones, ((0,), (0,))) + dot(low, ones, ((0,), (0,)))
    lane = lax.broadcasted_iota(jnp.int32, column.shape, 1)
    column = jnp.where(lane == EXPERTS, column, 0.0)
    for copy in small.loads:
        copy.wait()
    share = held[-1].shape[2]
    for e in range(ne):
        for d in range(nd):
            i = (e * nd + d) * share
            held[-1][d, e] = (held[-1][d, e].astype(F32) + column[i : i + share]).astype(BF16)
    small.loads = []
    small.step(0)
    small.step(1)
    for t in range(2, turns + 1):
        for each in early:
            if t > 2:
                each.step(t)
        for each in made + [small]:
            each.step(t)
    order = list(range(count))
    for t in range(ne):
        for a in order:
            lines[a].step(t)
    copies = []
    for a in order:
        copies.append(pltpu.make_async_copy(lines[a].own(), outs[a], out_sem.at[a]))
        copies[-1].start()
    for each in sums + lines:
        each.wait_sends()
    for copy in copies:
        copy.wait()


def finish(
    ne, nd, orders, normed, grads, cosine, sine, tokens, gain, grad_residual, weights, w_out, small
):
    rows, width = tokens.shape
    share = width // (ne * nd)
    columns = weights[1].shape[1]
    n_out = width // columns
    count = 2 * n_out + 3
    wide = [columns] * (count - 1) + [128]
    split = lambda v: v.reshape(ne, nd, share, v.shape[1])
    return pl.pallas_call(
        functools.partial(finish_body, ne, nd, tuple(map(tuple, orders)), n_out),
        out_shape=[jax.ShapeDtypeStruct((rows, width), F32)]
        + [jax.ShapeDtypeStruct((share, c), BF16) for c in wide],
        in_specs=[VMEM] * 8 + [ANY] * 6,
        out_specs=[VMEM] + [ANY] * count,
        scratch_shapes=[pltpu.VMEM((nd, ne, share, c), BF16) for c in wide]
        + [pltpu.VMEM((nd - 1, ne, share, c), BF16) for c in wide]
        + [pltpu.VMEM((2, ne, share, c), BF16) for c in wide]
        + [pltpu.VMEM(grads[1].shape, BF16)]
        + [pltpu.VMEM(w.shape, BF16) for w in weights]
        + [pltpu.VMEM((rows, width), F32)]
        + [
            DMA((count, ne)),
            DMA((4,)),
            DMA((count,)),
            DMA((count, nd - 1)),
            DMA((count, nd - 1)),
            DMA((count, 2, ne)),
            DMA((count, 2, ne)),
        ],
        compiler_params=pltpu.CompilerParams(
            vmem_limit_bytes=60 * 2**20, collective_id=4, has_side_effects=True
        ),
        cost_estimate=cost(45),
    )(
        normed,
        *grads,
        cosine,
        sine,
        tokens,
        gain,
        grad_residual,
        *weights,
        split(w_out),
        split(small),
    )


def per_device(
    tokens,
    segments,
    routes,
    first_gain,
    w_query,
    w_key,
    w_value,
    w_out,
    second_gain,
    w_router,
    w_gate,
    w_up,
    w_down,
    cotangent,
):
    micro, rows, width = tokens.shape
    ne, nd = lax.axis_size("ep"), lax.axis_size("dp")
    ep, dp = lax.axis_index("ep"), lax.axis_index("dp")
    groups = HEADS // KV_HEADS
    kv_width = KV_HEADS * HEAD_DIM
    every = micro * rows
    inputs = tokens.reshape(every, width).astype(F32)
    grad_output = cotangent.reshape(every, width).astype(F32)

    query_pos = dp * rows + jnp.arange(rows, dtype=jnp.int32)
    halfway = HEAD_DIM // 2
    frequency = ROPE_BASE ** (-(jnp.arange(halfway, dtype=F32) * 2.0 / HEAD_DIM))
    angles = query_pos.astype(F32)[:, None] * frequency[None, :]
    lanes = 2 * HEAD_DIM // halfway
    sign = jnp.where(jnp.arange(2 * HEAD_DIM) % HEAD_DIM < halfway, -1.0, 1.0).astype(F32)
    cosine = jnp.tile(jnp.cos(angles), (micro, lanes))
    sine = jnp.tile(jnp.sin(angles), (micro, lanes)) * sign

    tokens_flat = tokens.reshape(every, width)
    gain_one = first_gain.reshape(1, width)
    normed_one, query_rot, key_rot, value_own = project(
        tokens_flat, gain_one, cosine, sine, w_query, w_key, w_value
    )

    ids = jnp.arange(128, dtype=jnp.int32)
    counts = jnp.sum((segments[:, 0, :, None] == ids).astype(F32), axis=1)
    counts = jnp.concatenate([counts, jnp.zeros((8 - micro, 128), F32)], axis=0)

    cot_own = cotangent.reshape(every, width)

    def around(value, k):
        return lax.ppermute(value, "ep", [(i, (i + k) % ne) for i in range(ne)])

    cots = [cot_own] + [around(cot_own, k) for k in range(1, ne)]
    key_all, value_all, count_all = gather(ne, nd, (key_rot, value_own, counts), (), 0, 25)

    totals = jnp.sum(count_all[:, :micro], axis=0)
    lower = (ids[None, None, :] < segments[:, 0, :, None]).astype(F32)
    starts = jnp.sum(lower * totals[:, None, :], axis=2).astype(jnp.int32)
    starts = starts.reshape(every, 1)
    attn_low, logs = attend(dp, starts, query_rot, key_all, value_all, micro, rows, nd)
    residual = inputs + jnp.dot(attn_low, w_out, preferred_element_type=F32)
    inv_two = rms_scale(residual)
    normed_two = (residual * inv_two * second_gain).astype(BF16)
    logits = jnp.dot(normed_two, w_router, preferred_element_type=F32)
    routing = routes.reshape(every, routes.shape[2])
    chosen = jnp.any(
        routing[:, :, None] == jnp.arange(EXPERTS, dtype=jnp.int32)[None, None, :], axis=1
    )
    masked = jnp.where(chosen, logits, MASKED)
    terms = jnp.where(chosen, jnp.exp(masked - jnp.max(masked, axis=1, keepdims=True)), 0.0)
    gate_probs = terms / jnp.sum(terms, axis=1, keepdims=True)
    marked = jnp.where(chosen, gate_probs, -1.0).T

    normed_all, marked_all = gather(ne, nd, (), (normed_two, marked), 1, 38)
    here = EXPERTS // ne
    probs_here = lax.dynamic_slice_in_dim(marked_all, ep * here, here, axis=1)
    probs_here = (
        probs_here.reshape(ne, here, micro, rows)
        .transpose(0, 2, 1, 3)
        .reshape(ne * micro, here, rows)
    )
    nb = bit_count(nd)
    orders = [order[:-1][::-1] for order in gather_orders(nd)]
    mix, grad_in, pair_dots, *grads = experts(
        normed_all.reshape(ne * every, width),
        cots,
        probs_here,
        w_gate,
        w_up,
        w_down,
        micro,
        rows,
        ne,
        nd,
        6,
    )
    kept, landed, last = grads[:2], grads[2:4], grads[4:]
    pair_dots = pair_dots.reshape(here, ne, every).transpose(1, 0, 2)
    head = (slice(None), slice(0, 1))
    *grads, grad_back, dots_all = reduce(
        ne,
        nd,
        [(last[i], orders[i], None, None, False) for i in range(2)]
        + [(kept[i], orders[i][1:], head, landed[i], False) for i in range(2)],
        ((grad_in.reshape(ne, every, width), None),),
        (pair_dots,),
        2,
        40,
    )
    grads_last, grads_head = grads[:2], grads[2:]
    pair_dot = dots_all.reshape(EXPERTS, every).T
    grad_logits = gate_probs * (
        pair_dot - jnp.sum(gate_probs * pair_dot, axis=1, keepdims=True)
    )
    grad_w_router = jnp.einsum(
        "td,te->de", normed_two.astype(F32), grad_logits, precision=HIGHEST
    )
    grad_normed_two = (
        jnp.einsum("te,de->td", grad_logits, w_router.astype(F32), precision=HIGHEST)
        + grad_back.astype(F32)
    )
    scaled_two = grad_normed_two * second_gain
    grad_gain_two = jnp.sum(grad_normed_two * residual * inv_two, axis=0)
    grad_residual = (
        grad_output
        + inv_two * scaled_two
        - residual * inv_two**3 * jnp.mean(scaled_two * residual, axis=-1, keepdims=True)
    )
    residual_low = grad_residual.astype(BF16)
    grad_w_out = jnp.einsum("tf,td->fd", attn_low, residual_low, preferred_element_type=F32)
    grad_attn = jnp.einsum("td,fd->tf", residual_low, w_out, preferred_element_type=F32).astype(
        BF16
    )
    more = kept[0].shape[1] > 1
    mix = mix.reshape(ne, every, width)
    grad_query, grad_key_all, grad_value_all, *grads_more, mix_first = attend_back(
        starts,
        query_rot,
        key_all,
        value_all,
        logs,
        grad_attn,
        cosine,
        sine,
        [(kept[i], orders[i][1:], landed[i]) for i in range(2)] if more else [],
        mix,
        micro,
        rows,
        5,
    )
    full = [[0] + order for order in orders]
    grad_key, grad_value, mix_rest = reduce(
        ne,
        nd,
        [
            (grad_key_all, full[0], None, None, False),
            (grad_value_all, full[1], None, None, False),
        ],
        ((mix, (slice(None), slice(rows, every))),),
        (),
        3,
        30,
    )
    mix_own = jnp.concatenate([mix_first, mix_rest], axis=0)

    per_path = [
        jnp.concatenate(
            [grads_head[i]] + ([grads_more[i]] if more else []) + [grads_last[i][None]], axis=0
        )
        for i in range(2)
    ]
    grads = jnp.stack(per_path, axis=1)
    grads = grads.reshape((here,) + grads.shape[2:]).astype(F32)
    share = width // nd
    grad_w_gate, grad_w_up = grads[:, :share], grads[:, share : 2 * share]
    grad_w_down = jnp.concatenate(
        [
            grads[:, at : at + w_down.shape[1] // nd]
            for at in range(2 * share, grads.shape[1], w_down.shape[1] // nd)
        ],
        axis=2,
    )
    small = jnp.concatenate(
        [
            grad_w_router,
            jnp.zeros((width, 1), F32),
            grad_gain_two[:, None],
            jnp.zeros((width, 128 - EXPERTS - 2), F32),
        ],
        axis=1,
    ).astype(BF16)
    grad_tokens, *dense = finish(
        ne,
        nd,
        full,
        normed_one,
        (grad_query, grad_key, grad_value),
        cosine,
        sine,
        tokens_flat,
        gain_one,
        grad_residual,
        (w_query, w_key, w_value),
        grad_w_out.astype(BF16),
        small,
    )
    n_out = width // kv_width
    d_out = jnp.concatenate(dense[:n_out], axis=1).astype(F32)
    d_query = jnp.concatenate(dense[n_out : 2 * n_out], axis=1).astype(F32)
    d_key, d_value, d_small = (v.astype(F32) for v in dense[2 * n_out :])
    output = (residual + mix_own.astype(F32)).astype(BF16).reshape(tokens.shape)
    return (
        output,
        grad_tokens.reshape(tokens.shape),
        d_small[:, EXPERTS],
        d_query,
        d_key,
        d_value,
        d_out,
        d_small[:, EXPERTS + 1],
        d_small[:, :EXPERTS],
        grad_w_gate,
        grad_w_up,
        grad_w_down,
    )


def solution(mesh):
    in_specs = (
        P(None, ("ep", "dp"), None),
        P(None, "ep", "dp"),
        P(None, ("ep", "dp"), None),
        P(),
        P(),
        P(),
        P(),
        P(),
        P(),
        P(),
        P("ep", None, None),
        P("ep", None, None),
        P("ep", None, None),
        P(None, ("ep", "dp"), None),
    )
    out_specs = (
        P(None, ("ep", "dp"), None),
        P(None, ("ep", "dp"), None),
        P(("ep", "dp")),
        P(("ep", "dp"), None),
        P(("ep", "dp"), None),
        P(("ep", "dp"), None),
        P(("ep", "dp"), None),
        P(("ep", "dp")),
        P(("ep", "dp"), None),
        P("ep", "dp", None),
        P("ep", "dp", None),
        P("ep", "dp", None),
    )
    return jax.shard_map(
        per_device, mesh=mesh, in_specs=in_specs, out_specs=out_specs, check_vma=False
    )
```

```python
import functools

import jax
import jax.numpy as jnp
from jax import lax
from jax.experimental import pallas as pl
from jax.experimental.pallas import tpu as pltpu
from jax.sharding import PartitionSpec as P

HEADS = 16
KV_HEADS = 8
HEAD_DIM = 64
EXPERTS = 32
CAP = 64
EPSILON = 1e-06
ROPE_BASE = 10000.0
MASKED = -1e30
HIGHEST = lax.Precision.HIGHEST
MESH = pl.DeviceIdType.MESH
BF16 = jnp.bfloat16
F32 = jnp.float32
VMEM = pl.BlockSpec(memory_space=pltpu.VMEM)
ANY = pl.BlockSpec(memory_space=pl.ANY)
DMA = pltpu.SemaphoreType.DMA


def bit_count(n):
    return n.bit_length() - 1


def masks(bits):
    out = [0]
    for b in bits:
        out = out + [m | (1 << b) for m in out]
    return out


def gather_orders(n):
    bits = list(range(bit_count(n)))
    return (bits[1:] + bits[:1], bits[:0:-1] + bits[:1])


def greet(ep, dp, ne, nd):
    barrier = pltpu.get_barrier_semaphore()
    for k in range(1, ne):
        pl.semaphore_signal(
            barrier, inc=1, device_id={"ep": lax.rem(ep + k, ne)}, device_id_type=MESH
        )
    for b in range(bit_count(nd)):
        pl.semaphore_signal(
            barrier, inc=1, device_id={"dp": jnp.bitwise_xor(dp, 1 << b)}, device_id_type=MESH
        )
    pl.semaphore_wait(barrier, ne - 1 + bit_count(nd))


def remote(src, dst, send, recv, where):
    return pltpu.make_async_remote_copy(
        src_ref=src, dst_ref=dst, send_sem=send, recv_sem=recv, device_id=where, device_id_type=MESH
    )


def gather_body(ne, nd, n_dp, n_ep, *refs):
    n_in = n_dp + n_ep
    ins, outs, sems = refs[:n_in], refs[n_in : 2 * n_in], refs[2 * n_in :]
    ep, dp = lax.axis_index("ep"), lax.axis_index("dp")
    own_sem, dp_send, dp_recv, ep_send, ep_recv = sems
    greet(ep, dp, ne, nd)
    own = []
    for a in range(n_in):
        me = dp if a < n_dp else ep
        copy = pltpu.make_async_copy(ins[a], outs[a].at[me], own_sem.at[a])
        copy.start()
        own.append(copy)

    def dp_copy(a, t, m):
        order = gather_orders(nd)[a % 2]
        block = jnp.bitwise_xor(dp, m)
        k = (1 << t) - 1 + masks(order[:t]).index(m)
        return remote(
            ins[a] if m == 0 else outs[a].at[block],
            outs[a].at[block],
            dp_send.at[a, k],
            dp_recv.at[a, k],
            {"dp": jnp.bitwise_xor(dp, 1 << order[t])},
        )

    def ep_copy(a, s, way):
        shard = lax.rem(ep - way * s + ne, ne)
        src = ins[n_dp + a] if s == 0 else outs[n_dp + a].at[shard]
        k = 0 if way == 1 else 1
        return remote(
            src,
            outs[n_dp + a].at[shard],
            ep_send.at[a, k, s],
            ep_recv.at[a, k, s],
            {"ep": lax.rem(ep + way + ne, ne)},
        )

    def sends(s, way):
        if way == 1:
            return (ep >= s) & (ep < ne - 1)
        return (ep + s <= ne - 1) & (ep >= 1)

    def receives(s, way):
        if way == 1:
            return ep >= 1 + s
        return ep + 1 + s <= ne - 1

    def ep_start(s):
        for a in range(n_ep):
            for way in (1, -1):

                @pl.when(sends(s, way))
                def _(a=a, way=way):
                    ep_copy(a, s, way).start()

    def ep_wait(s):
        for a in range(n_ep):
            for way in (1, -1):

                @pl.when(receives(s, way))
                def _(a=a, way=way):
                    ep_copy(a, s, way).wait_recv()

    dp_steps = bit_count(nd) if n_dp else 0
    ep_steps = ne - 1 if n_ep else 0
    for t in range(dp_steps):
        for a in range(n_dp):
            dp_copy(a, t, 0).start()
    for t in range(max(dp_steps, ep_steps) + 1):
        if 0 < t <= dp_steps:
            for a in range(n_dp):
                order = gather_orders(nd)[a % 2]
                for m in masks(order[: t - 1]):
                    dp_copy(a, t - 1, m).wait_recv()
                    for later in range(t, dp_steps):
                        dp_copy(a, later, m | (1 << order[t - 1])).start()
        if 0 < t <= ep_steps:
            ep_wait(t - 1)
        if t < ep_steps:
            ep_start(t)
    for t in range(dp_steps):
        for a in range(n_dp):
            for m in masks(gather_orders(nd)[a % 2][:t]):
                dp_copy(a, t, m).wait_send()
    for s in range(ep_steps):
        for a in range(n_ep):
            for way in (1, -1):

                @pl.when(sends(s, way))
                def _(a=a, s=s, way=way):
                    ep_copy(a, s, way).wait_send()

    for c in own:
        c.wait()


def cost(us):
    return pl.CostEstimate(flops=0, bytes_accessed=int(us * 3.0e6), transcendentals=0)


def gather(ne, nd, dp_arrays, ep_arrays, collective, us):
    arrays = list(dp_arrays) + list(ep_arrays)
    counts = [nd] * len(dp_arrays) + [ne] * len(ep_arrays)
    a, b = max(len(dp_arrays), 1), max(len(ep_arrays), 1)
    return pl.pallas_call(
        functools.partial(gather_body, ne, nd, len(dp_arrays), len(ep_arrays)),
        out_shape=[
            jax.ShapeDtypeStruct((n,) + v.shape, v.dtype) for n, v in zip(counts, arrays)
        ],
        in_specs=[ANY] * len(arrays),
        out_specs=[ANY] * len(arrays),
        scratch_shapes=[
            DMA((len(arrays),)),
            DMA((a, nd - 1)),
            DMA((a, nd - 1)),
            DMA((b, 2, ne - 1)),
            DMA((b, 2, ne - 1)),
        ],
        compiler_params=pltpu.CompilerParams(
            collective_id=collective, has_side_effects=True, vmem_limit_bytes=60 * 2**20
        ),
        cost_estimate=cost(us),
    )(*arrays)


def add_into(ref, arrived):
    if len(ref.shape) > 2:

        @pl.loop(0, ref.shape[0])
        def _(i):
            add_into(ref.at[i], arrived.at[i])

    else:
        ref[...] = (ref[...].astype(F32) + arrived[...].astype(F32)).astype(ref.dtype)


class PairSum:
    def __init__(self, dp, order, loads, held, extra, landing, send_sem, recv_sem):
        self.dp, self.order, self.held, self.landing = dp, order, held, landing
        self.send_sem, self.recv_sem = send_sem, recv_sem
        self.extra, self.loads = extra, loads
        self.index = 0
        for b in order:
            side = jnp.bitwise_and(lax.shift_right_logical(dp, b), 1)
            self.index = self.index + (side << self.place(b))

    def place(self, bit):
        return sorted(self.order).index(bit)

    def copies(self, t):
        order = self.order
        partner = jnp.bitwise_xor(self.index, 1 << self.place(order[t]))
        first = sum(1 << (len(order) - 1 - i) for i in range(t))
        return [
            (
                m,
                first + j,
                remote(
                    self.held.at[jnp.bitwise_xor(partner, m)],
                    self.landing.at[first + j],
                    self.send_sem.at[first + j],
                    self.recv_sem.at[first + j],
                    {"dp": jnp.bitwise_xor(self.dp, 1 << order[t])},
                ),
            )
            for j, m in enumerate(masks([self.place(b) for b in order[t + 1 :]]))
        ]

    def load(self):
        for copy in self.loads:
            copy.start()

    def step(self, t):
        if t == 0:
            for copy in self.loads:
                copy.wait()
            if self.extra is not None:
                add_into(self.held, self.extra)
        elif t <= len(self.order):
            for m, k, copy in self.copies(t - 1):
                copy.wait_recv()
                add_into(self.held.at[jnp.bitwise_xor(self.index, m)], self.landing.at[k])
        if t < len(self.order):
            for m, k, copy in self.copies(t):
                copy.start()

    def own(self):
        return self.held.at[self.index]

    def wait_sends(self):
        for t in range(len(self.order)):
            for m, k, copy in self.copies(t):
                copy.wait_send()


class LineSum:
    def __init__(self, ep, ne, blocks, landing, send_sem, recv_sem):
        self.ep, self.ne, self.blocks, self.landing = ep, ne, blocks, landing
        self.send_sem, self.recv_sem = send_sem, recv_sem

    def copy(self, dest, way):
        k = 0 if way == 1 else 1
        return remote(
            self.blocks.at[dest],
            self.landing.at[k, dest],
            self.send_sem.at[k, dest],
            self.recv_sem.at[k, dest],
            {"ep": lax.rem(self.ep + way + self.ne, self.ne)},
        )

    def turn(self, t, way):
        ep, ne = self.ep, self.ne
        dest = ep + ne - 1 - t if way == 1 else ep + t - (ne - 1)
        has = dest <= ne - 1 if way == 1 else dest >= 0
        inner = ep >= 1 if way == 1 else ep <= ne - 2
        return dest, has, inner

    def step(self, t):
        for way in (1, -1):
            dest, has, inner = self.turn(t, way)

            @pl.when(has & inner)
            def _(way=way, dest=dest):
                self.copy(dest, way).wait_recv()
                add_into(self.blocks.at[dest], self.landing.at[0 if way == 1 else 1, dest])

            if t < self.ne - 1:

                @pl.when(has)
                def _(way=way, dest=dest):
                    self.copy(dest, way).start()

    def own(self):
        return self.blocks.at[self.ep]

    def wait_sends(self):
        for t in range(self.ne - 1):
            for way in (1, -1):
                dest, has, inner = self.turn(t, way)

                @pl.when(has)
                def _(way=way, dest=dest):
                    self.copy(dest, way).wait_send()


def shape_at(array, where):
    return tuple(len(range(*w.indices(n))) for w, n in zip(where, array.shape)) + array.shape[len(where) :]


def reduce_body(ne, nd, pairs, line_parts, n_swap, *refs):
    refs = list(refs)

    def take(n):
        return [refs.pop(0) for _ in range(n)]

    n_pair, n_line = len(pairs), len(line_parts)
    n_extra = sum(p[2] for p in pairs)
    n_both = sum(p[3] for p in pairs)
    n_sum = n_pair + n_line
    ins, extra_ins, swap_ins = take(n_sum), take(n_extra), take(n_swap)
    outs, swap_outs = take(n_sum), take(n_swap)
    held, extras, pair_in = take(n_sum), take(n_extra), take(n_pair)
    both_in, line_in = take(n_both), take(n_line)
    load_sem, out_sem, dp_send, dp_recv, ep_send, ep_recv, swap_send, swap_recv = refs
    ep, dp = lax.axis_index("ep"), lax.axis_index("dp")
    sums, then = [], []
    for a, (order, where, has_extra, both) in enumerate(pairs):
        targets = [(ins[a], held[a])]
        extra = extras.pop(0) if has_extra else None
        if has_extra:
            targets.append((extra_ins.pop(0), extra))
        loads = [
            pltpu.make_async_copy(src.at[where] if where else src, dst, load_sem.at[a, i])
            for i, (src, dst) in enumerate(targets)
        ]
        sums.append(
            PairSum(dp, order, loads, held[a], extra, pair_in[a], dp_send.at[a], dp_recv.at[a])
        )
        if both:
            i = len(then)
            then.append(
                LineSum(ep, ne, sums[a].own(), both_in[i], ep_send.at[i], ep_recv.at[i])
            )
    lines, line_loads = [], []
    for i in range(n_line):
        a = n_pair + i
        src = ins[a].at[line_parts[i]] if line_parts[i] else ins[a]
        line_loads.append(pltpu.make_async_copy(src, held[a], load_sem.at[a, 0]))
        lines.append(
            LineSum(
                ep, ne, held[a], line_in[i], ep_send.at[n_both + i], ep_recv.at[n_both + i]
            )
        )
    for copy in line_loads:
        copy.start()
    for each in sums:
        each.load()
    greet(ep, dp, ne, nd)
    swaps = []
    for a in range(n_swap):
        src, dst = swap_ins[a], swap_outs[a]
        own = pltpu.make_async_copy(src.at[ep], dst.at[ep], load_sem.at[n_sum + a, 0])
        own.start()
        swaps.append(own)
        for k in range(1, ne):
            to = lax.rem(ep + k, ne)
            copy = remote(
                src.at[to], dst.at[ep], swap_send.at[a, k - 1], swap_recv.at[a, k - 1], {"ep": to}
            )
            copy.start()
            swaps.append(copy)
    for copy in line_loads:
        copy.wait()
    steps = max([len(p[0]) + 1 for p in pairs] + [ne if n_line else 0])
    for t in range(steps):
        if t < ne:
            for each in lines:
                each.step(t)
        for each in sums:
            each.step(t)
    for t in range(ne):
        for each in then:
            each.step(t)
    results, after = [], iter(then)
    for a in range(n_sum):
        if a >= n_pair:
            src = lines[a - n_pair].own()
        else:
            src = next(after).own() if pairs[a][3] else sums[a].own()
        copy = pltpu.make_async_copy(src, outs[a], out_sem.at[a])
        copy.start()
        results.append(copy)
    for each in sums + then + lines:
        each.wait_sends()
    for copy in swaps + results:
        copy.wait()


def reduce(ne, nd, pairs, lines, swaps, collective, us):
    line_parts = tuple(where for _, where in lines)
    line_shapes = [shape_at(v, where) if where else v.shape for v, where in lines]
    lines = [v for v, _ in lines]
    arrays = [p[0] for p in pairs] + list(lines)
    extras = [p[3] for p in pairs if p[3] is not None]
    kinds = tuple((tuple(p[1]), p[2], p[3] is not None, p[4]) for p in pairs)
    shapes = [shape_at(p[0], p[2]) if p[2] else p[0].shape for p in pairs]
    boths = [s for s, p in zip(shapes, pairs) if p[4]]
    results = [s[2:] if p[4] else s[1:] for s, p in zip(shapes, pairs)]
    results += [s[1:] for s in line_shapes]
    scratch = shapes + line_shapes
    scratch += [s for s, p in zip(shapes, pairs) if p[3] is not None]
    scratch += [(s[0] - 1,) + s[1:] for s in shapes]
    scratch += [(2,) + s[1:] for s in boths] + [(2,) + s for s in line_shapes]
    some = lambda n: max(n, 1)
    line_count = some(len(lines) + len(boths))
    deep = max([s[0] - 1 for s in shapes] + [1])
    return pl.pallas_call(
        functools.partial(reduce_body, ne, nd, kinds, line_parts, len(swaps)),
        out_shape=[jax.ShapeDtypeStruct(s, BF16) for s in results]
        + [jax.ShapeDtypeStruct(v.shape, v.dtype) for v in swaps],
        in_specs=[ANY] * (len(arrays) + len(extras) + len(swaps)),
        out_specs=[ANY] * (len(arrays) + len(swaps)),
        scratch_shapes=[pltpu.VMEM(s, BF16) for s in scratch]
        + [
            DMA((len(arrays) + len(swaps), 2)),
            DMA((len(arrays),)),
            DMA((some(len(pairs)), deep)),
            DMA((some(len(pairs)), deep)),
            DMA((line_count, 2, ne)),
            DMA((line_count, 2, ne)),
            DMA((some(len(swaps)), ne - 1)),
            DMA((some(len(swaps)), ne - 1)),
        ],
        compiler_params=pltpu.CompilerParams(
            collective_id=collective, has_side_effects=True, vmem_limit_bytes=60 * 2**20
        ),
        cost_estimate=cost(us),
    )(*arrays, *extras, *swaps)


def dot(a, b, dims=((1,), (0,))):
    return lax.dot_general(a, b, (dims, ((), ())), preferred_element_type=F32)


def expert_body(ne, nd, micro, rows, *refs):
    cots, refs = refs[:ne], refs[ne:]
    normed_ref, probs_ref, gate_ref, up_ref, down_ref = refs[:5]
    mix_ref, grad_ref, dots_ref = refs[5:8]
    kept, landed, whole = refs[8:10], refs[10:12], refs[12:14]
    rows_in, cots_in, picks, first, second, keep, send, arrived, leaving = refs[14:23]
    load_sem, store_sem, send_sem, recv_sem, free_sem, far_send, far_recv = refs[23:]
    e = pl.program_id(0)
    last = pl.num_programs(0) - 1
    ep, dp = lax.axis_index("ep"), lax.axis_index("dp")
    other = {"dp": jnp.bitwise_xor(dp, 1)}
    every = micro * rows
    blocks = ne * micro
    width = first.shape[1]
    n_exp = rows_in.shape[1]

    def exchange():
        return remote(send, arrived, send_sem, recv_sem, other)

    def loads():
        out = [pltpu.make_async_copy(normed_ref, first, load_sem.at[ne])]
        for k in range(ne):
            at = pl.multiple_of(lax.rem(ep - k + ne, ne) * every, every)
            out.append(
                pltpu.make_async_copy(cots[k], second.at[pl.ds(at, every)], load_sem.at[k])
            )
        return out

    def block_at(s):
        return pl.ds(pl.multiple_of(s * rows, rows), rows)

    def returned(t):
        k, m = t // micro, lax.rem(t, micro)
        return lax.rem(ep + k, ne) * micro + m

    def stores(t):
        s = returned(t)
        return (
            pltpu.make_async_copy(
                first.at[block_at(s)], mix_ref.at[block_at(s)], store_sem.at[0, t]
            ),
            pltpu.make_async_copy(
                second.at[block_at(s)], grad_ref.at[block_at(s)], store_sem.at[1, t]
            ),
        )

    def far(i, n):
        return remote(
            leaving.at[i],
            landed[i].at[:, n],
            far_send.at[i],
            far_recv.at[i, n],
            {"dp": jnp.bitwise_xor(dp, 1 << first_bits(nd)[i])},
        )

    def last_copy():
        return pltpu.make_async_copy(keep, whole[1], load_sem.at[0])

    def collect():
        exchange().wait_recv()
        pieces = keep.shape[0]
        n = (e - 1) // 2
        for i, bit in enumerate(first_bits(nd)):

            def put(side, i=i, bit=bit):
                for j in range(pieces):
                    value = (keep[j].astype(F32) + arrived[j].astype(F32)).astype(BF16)
                    at = (j >> bit << (bit - 1)) | (j & ((1 << (bit - 1)) - 1))
                    if (j >> (bit - 1)) & 1 == side:
                        kept[i][at, 0] = value
                    else:
                        leaving[i, at] = value

            @pl.when((lax.rem(e - 1, 2) == i) & (n < n_exp // 2 - 1))
            def _(i=i, bit=bit, put=put):
                @pl.when(n > 0)
                def _():
                    far(i, n - 1).wait_send()

                mine = jnp.bitwise_and(lax.shift_right_logical(dp, bit), 1)

                @pl.when(mine == 0)
                def _():
                    put(0)

                @pl.when(mine == 1)
                def _():
                    put(1)

                far(i, n).start()

            @pl.when((lax.rem(e - 1, 2) == i) & (n == n_exp // 2 - 1))
            def _(i=i):
                add_into(keep, arrived)
                if i == 0:
                    whole[0][...] = keep[...]
                else:
                    last_copy().start()

    @pl.when(e == 0)
    def _():
        for copy in loads():
            copy.start()
        barrier = pltpu.get_barrier_semaphore()
        met = [0] + sorted(set(first_bits(nd)))
        for bit in met:
            pl.semaphore_signal(
                barrier,
                inc=1,
                device_id={"dp": jnp.bitwise_xor(dp, 1 << bit)},
                device_id_type=MESH,
            )
        pl.semaphore_wait(barrier, len(met))
        before = lax.broadcasted_iota(jnp.int32, (rows, rows), 0)
        after = lax.broadcasted_iota(jnp.int32, (rows, rows), 1)
        earlier = (before < after).astype(BF16)
        slot = lax.broadcasted_iota(jnp.int32, (n_exp, CAP, rows), 1)
        for copy in loads():
            copy.wait()

        @pl.loop(0, blocks)
        def _(s):
            at = block_at(s)
            probs = probs_ref[s]
            hit = probs >= 0.0
            rank = dot(hit.astype(BF16), earlier)
            rank = jnp.where(hit, rank, -1.0).astype(jnp.int32)
            pick = jnp.broadcast_to(rank[:, None, :], (n_exp, CAP, rows)) == slot
            pick_f = pick.astype(F32)
            flat = pick_f.reshape(n_exp * CAP, rows).astype(BF16)
            picks[s] = flat
            rows_in[s] = dot(flat, first[at, :]).astype(BF16).reshape(n_exp, CAP, width)
            cots_in[s] = dot(flat, second[at, :]).astype(BF16).reshape(n_exp, CAP, width)

    @pl.when(e < last)
    def _():
        x = rows_in[:, e].reshape(blocks * CAP, width)
        c = cots_in[:, e].reshape(blocks * CAP, width)
        flat = picks[:, pl.ds(pl.multiple_of(e * CAP, CAP), CAP), :].astype(F32)
        p = jnp.sum(flat * probs_ref[:, pl.ds(e, 1), :], axis=2, keepdims=True)
        p = p.reshape(blocks * CAP, 1)
        w_gate, w_up, w_down = gate_ref[0], up_ref[0], down_ref[0]
        gate_pre = dot(x, w_gate)
        up_pre = dot(x, w_up)
        sigma = jax.nn.sigmoid(gate_pre)
        silu = gate_pre * sigma
        hidden = (silu * up_pre).astype(BF16)
        out = dot(hidden, w_down) * p
        back = dot(c, w_down, ((1,), (1,)))
        wide = hidden.astype(F32)
        pair = jnp.sum(wide * back, axis=1, keepdims=True)
        back = back * p
        grad_up = (back * silu).astype(BF16)
        grad_gate = (back * up_pre * (sigma * (1.0 + gate_pre * (1.0 - sigma)))).astype(BF16)
        scaled = (wide * p).astype(BF16)
        grad_x = dot(grad_gate, w_gate, ((1,), (1,))) + dot(grad_up, w_up, ((1,), (1,)))

        dots_ref[0] = jnp.sum(flat * pair.reshape(blocks, CAP, 1), axis=1)

        @pl.when(e > 0)
        def _():
            collect()
            pl.semaphore_signal(free_sem, inc=1, device_id=other, device_id_type=MESH)
            exchange().wait_send()
            pl.semaphore_wait(free_sem, 1)

        def split(value, offset):
            value = value.astype(BF16)
            piece, columns = value.shape[0] // nd, keep.shape[2]

            def put(even, odd):
                for i in range(nd):
                    ref = odd if i % 2 else even
                    for j in range(value.shape[1] // columns):
                        at = offset + j * piece
                        ref[i // 2, at : at + piece] = value[
                            i * piece : (i + 1) * piece, j * columns : (j + 1) * columns
                        ]

            @pl.when(jnp.bitwise_and(dp, 1) == 0)
            def _():
                put(keep, send)

            @pl.when(jnp.bitwise_and(dp, 1) == 1)
            def _():
                put(send, keep)

        share = width // nd
        split(dot(scaled, c, ((0,), (0,))), 2 * share)
        split(dot(x, grad_gate, ((0,), (0,))), 0)
        split(dot(x, grad_up, ((0,), (0,))), share)
        exchange().start()

        rows_in[:, e] = grad_x.astype(BF16).reshape(blocks, CAP, width)
        cots_in[:, e] = out.astype(BF16).reshape(blocks, CAP, width)

    @pl.when(e == last)
    def _():
        @pl.loop(0, blocks)
        def _(t):
            s = returned(t)
            at = block_at(s)
            flat = picks[s]
            for done, slots in ((first, cots_in), (second, rows_in)):
                value = dot(flat, slots[s].reshape(n_exp * CAP, width), ((0,), (0,)))
                done[at, :] = value.astype(BF16)
            for copy in stores(t):
                copy.start()

            @pl.when(t == 1)
            def _():
                collect()
                exchange().wait_send()

        @pl.loop(0, blocks)
        def _(t):
            for copy in stores(t):
                copy.wait()

        last_copy().wait()
        for i in range(2):
            far(i, n_exp // 2 - 2).wait_send()

            @pl.loop(0, n_exp // 2 - 1)
            def _(n, i=i):
                far(i, n).wait_recv()


def first_bits(nd):
    return [order[-2] for order in gather_orders(nd)]


def experts(normed, cots, probs, w_gate, w_up, w_down, micro, rows, ne, nd, collective):
    n_exp, width, inner = w_gate.shape
    blocks = ne * micro
    half = nd // 2
    packed = 2 * width // nd + (inner // nd) * (width // inner)
    full = (blocks * rows, width)
    one = pl.Buffered(1)
    weight = lambda e: (jnp.minimum(e, n_exp - 1), 0, 0)
    early = n_exp // 2 - 1
    part = (half // 2, early, packed, inner)
    kept = pl.BlockSpec(
        (half // 2, 1, packed, inner),
        lambda e: (0, jnp.minimum(jnp.maximum(e - 1, 0) // 2, early - 1), 0, 0),
    )
    last = (half, packed, inner)
    return pl.pallas_call(
        functools.partial(expert_body, ne, nd, micro, rows),
        grid=(n_exp + 1,),
        in_specs=[ANY] * (ne + 1)
        + [
            pl.BlockSpec(probs.shape, lambda e: (0, 0, 0), pipeline_mode=one),
            pl.BlockSpec((1, width, inner), weight),
            pl.BlockSpec((1, width, inner), weight),
            pl.BlockSpec((1, inner, width), weight),
        ],
        out_specs=[ANY, ANY, pl.BlockSpec((1, blocks, rows), weight), kept, kept, ANY, ANY]
        + [pl.BlockSpec(last, lambda e: (0, 0, 0), pipeline_mode=one), ANY],
        scratch_shapes=[
            pltpu.VMEM((blocks, n_exp, CAP, width), BF16),
            pltpu.VMEM((blocks, n_exp, CAP, width), BF16),
            pltpu.VMEM((blocks, n_exp * CAP, rows), BF16),
            pltpu.VMEM(full, BF16),
            pltpu.VMEM(full, BF16),
            pltpu.VMEM((half, packed, inner), BF16),
            pltpu.VMEM((half, packed, inner), BF16),
            pltpu.VMEM((half, packed, inner), BF16),
            pltpu.VMEM((2, half // 2, packed, inner), BF16),
            DMA((ne + 1,)),
            DMA((2, blocks)),
            DMA,
            DMA,
            pltpu.SemaphoreType.REGULAR,
            DMA((2,)),
            DMA((2, early)),
        ],
        out_shape=[
            jax.ShapeDtypeStruct(full, BF16),
            jax.ShapeDtypeStruct(full, BF16),
            jax.ShapeDtypeStruct((n_exp, blocks, rows), F32),
        ]
        + [jax.ShapeDtypeStruct(part, BF16)] * 4
        + [jax.ShapeDtypeStruct(last, BF16)] * 2,
        compiler_params=pltpu.CompilerParams(
            vmem_limit_bytes=62 * 2**20,
            dimension_semantics=("arbitrary",),
            collective_id=collective,
            has_side_effects=True,
        ),
        cost_estimate=cost(75),
    )(*cots, normed, probs, w_gate, w_up, w_down)


def rms_scale(values):
    return lax.rsqrt(jnp.mean(values * values, axis=-1, keepdims=True) + EPSILON)


def partner(x):
    lane = lax.broadcasted_iota(jnp.int32, x.shape, 1)
    half = HEAD_DIM // 2
    low = lax.rem(lane, HEAD_DIM) < half
    return jnp.where(low, pltpu.roll(x, x.shape[1] - half, 1), pltpu.roll(x, half, 1))


def turn(x, cosine, sine):
    return x * cosine + partner(x) * sine


def project_body(
    tokens_ref, gain_ref, cos_ref, sin_ref, wq_ref, wk_ref, wv_ref, n_ref, q_ref, k_ref, v_ref, *rest
):
    wq, wk, wv, sem = rest
    loads = [
        pltpu.make_async_copy(src, dst, sem.at[i])
        for i, (src, dst) in enumerate(((wk_ref, wk), (wv_ref, wv), (wq_ref, wq)))
    ]
    for copy in loads:
        copy.start()
    x = tokens_ref[...].astype(F32)
    n_ref[...] = (x * rms_scale(x) * gain_ref[...]).astype(BF16)
    normed = n_ref[...]
    cosine, sine = cos_ref[...], sin_ref[...]
    tile = 256
    for copy, (w, out, turned) in zip(
        loads, ((wk, k_ref, True), (wv, v_ref, False), (wq, q_ref, True))
    ):
        copy.wait()
        for c in range(0, w.shape[1], tile):
            y = dot(normed, w[:, c : c + tile])
            if turned:
                for i in range(0, tile, 128):
                    out[:, c + i : c + i + 128] = turn(y[:, i : i + 128], cosine, sine).astype(BF16)
            else:
                out[:, c : c + tile] = y.astype(BF16)


def project(tokens, gain, cosine, sine, w_query, w_key, w_value):
    rows, width = tokens.shape
    shapes = [width, w_query.shape[1], w_key.shape[1], w_value.shape[1]]
    return pl.pallas_call(
        project_body,
        out_shape=[jax.ShapeDtypeStruct((rows, n), BF16) for n in shapes],
        in_specs=[VMEM] * 4 + [ANY] * 3,
        out_specs=[VMEM] * 4,
        scratch_shapes=[pltpu.VMEM(w.shape, BF16) for w in (w_query, w_key, w_value)] + [DMA((3,))],
        compiler_params=pltpu.CompilerParams(vmem_limit_bytes=60 * 2**20),
        cost_estimate=cost(5),
    )(tokens, gain, cosine, sine, w_query, w_key, w_value)


def spread(x):
    lane = lax.broadcasted_iota(jnp.int32, (x.shape[0], 128), 1)
    low = lane < HEAD_DIM
    zero = jnp.zeros((), x.dtype)
    first, second = x[:, :128], x[:, 128:]
    return jnp.concatenate(
        [
            jnp.where(low, first, zero),
            jnp.where(low, pltpu.roll(first, HEAD_DIM, 1), zero),
            jnp.where(low, zero, pltpu.roll(second, HEAD_DIM, 1)),
            jnp.where(low, zero, second),
        ],
        axis=0,
    )


def gathered(x, rows):
    lane = lax.broadcasted_iota(jnp.int32, (rows, 128), 1)
    low = lane < HEAD_DIM
    h = [x[i * rows : (i + 1) * rows] for i in range(4)]
    return jnp.concatenate(
        [
            jnp.where(low, h[0], pltpu.roll(h[1], HEAD_DIM, 1)),
            jnp.where(low, pltpu.roll(h[2], HEAD_DIM, 1), h[3]),
        ],
        axis=1,
    )


def window_of(dp, span):
    return jnp.maximum(dp - (span - 1), 0)


def window_scores(dp, span, rows, starts_ref, q, k):
    keys = k.shape[0]
    scores = dot(q, k, ((1,), (1,))).reshape(4, rows, keys)
    key_pos = window_of(dp, span) * rows + lax.broadcasted_iota(jnp.int32, (rows, keys), 1)
    query_pos = dp * rows + lax.broadcasted_iota(jnp.int32, (rows, keys), 0)
    allowed = (key_pos <= query_pos) & (key_pos >= starts_ref[...])
    return jnp.where(allowed[None], scores, MASKED).reshape(4 * rows, keys)


def in_window(ref, dp, span):
    block = ref[pl.ds(window_of(dp, span), span)]
    return block.reshape(span * block.shape[1], block.shape[2])


SCALE = HEAD_DIM ** (-0.5)


def attend_body(span, dp_ref, starts_ref, q_ref, k_ref, v_ref, out_ref, log_ref):
    dp = dp_ref[0]
    rows = q_ref.shape[0]
    q = spread(q_ref[...].astype(F32) * SCALE).astype(BF16)
    scores = window_scores(dp, span, rows, starts_ref, q, in_window(k_ref, dp, span))
    top = jnp.max(scores, axis=1, keepdims=True)
    terms = jnp.exp(scores - top)
    total = jnp.sum(terms, axis=1, keepdims=True)
    log_ref[0, 0] = top + jnp.log(total)
    weights = (terms * (1.0 / total)).astype(BF16)
    out = dot(weights, in_window(v_ref, dp, span))
    out_ref[...] = gathered(out, rows).astype(BF16)


def attention_specs(micro, rows, nd):
    pairs = KV_HEADS // 2
    mine = pl.BlockSpec((rows, 4 * HEAD_DIM), lambda m, h, *_: (m, h))
    theirs = pl.BlockSpec((nd, rows, 2 * HEAD_DIM), lambda m, h, *_: (0, m, h))
    column = pl.BlockSpec((rows, 1), lambda m, h, *_: (m, 0))
    logs = pl.BlockSpec((1, 1, 4 * rows, 1), lambda m, h, *_: (m, h, 0, 0))
    log_shape = jax.ShapeDtypeStruct((micro, pairs, 4 * rows, 1), F32)
    return (micro, pairs), mine, theirs, column, logs, log_shape


def attend(dp, starts, queries, keys, values, micro, rows, nd):
    grid, mine, theirs, column, logs, log_shape = attention_specs(micro, rows, nd)
    return pl.pallas_call(
        functools.partial(attend_body, nd // 2 + 1),
        grid_spec=pltpu.PrefetchScalarGridSpec(
            num_scalar_prefetch=1,
            grid=grid,
            in_specs=[column, mine, theirs, theirs],
            out_specs=[mine, logs],
        ),
        out_shape=[jax.ShapeDtypeStruct(queries.shape, BF16), log_shape],
        compiler_params=pltpu.CompilerParams(vmem_limit_bytes=60 * 2**20),
        cost_estimate=cost(15),
    )(dp.reshape(1), starts, queries, keys, values)


def attend_back_body(span, ne, nd, orders, *refs):
    refs = list(refs)

    def take(n):
        return [refs.pop(0) for _ in range(n)]

    starts_ref, q_ref, k_ref, v_ref, log_ref, g_ref, cos_ref, sin_ref = take(8)
    n = len(orders)
    sources, extras = take(n), take(n)
    dq_ref, dk_ref, dv_ref = take(3)
    outs = take(n)
    held, more, landing = take(n), take(n), take(n)
    load_sem, out_sem, send_sem, recv_sem = refs
    ep, dp = lax.axis_index("ep"), lax.axis_index("dp")
    step = pl.program_id(0) * pl.num_programs(1) + pl.program_id(1)
    final = pl.num_programs(0) * pl.num_programs(1) - 1
    sums = []
    for a in range(n):
        part = pl.ds(1, sources[a].shape[1] - 1)
        loads = [
            pltpu.make_async_copy(src.at[:, part], dst, load_sem.at[a, i])
            for i, (src, dst) in enumerate(((sources[a], held[a]), (extras[a], more[a])))
        ]
        sums.append(
            PairSum(
                dp, orders[a], loads, held[a], more[a], landing[a], send_sem.at[a], recv_sem.at[a]
            )
        )
    @pl.when(step == 0)
    def _():
        for each in sums:
            each.load()
        greet(ep, dp, ne, nd)
        for each in sums:
            each.step(0)

    rows = q_ref.shape[0]
    q = spread(q_ref[...].astype(F32) * SCALE).astype(BF16)
    g = spread(g_ref[...].astype(F32)).astype(BF16)
    k, v = in_window(k_ref, dp, span), in_window(v_ref, dp, span)
    scores = window_scores(dp, span, rows, starts_ref, q, k)
    probs = jnp.exp(scores - log_ref[0, 0])
    grad_probs = dot(g, v, ((1,), (1,)))
    total = jnp.sum(probs * grad_probs, axis=1, keepdims=True)
    grad_scores = (probs * (grad_probs - total)).astype(BF16)
    dq = gathered(dot(grad_scores, k) * SCALE, rows)
    cosine, sine = cos_ref[...], -sin_ref[...]
    for i in range(0, dq.shape[1], 128):
        dq_ref[:, i : i + 128] = turn(dq[:, i : i + 128], cosine, sine).astype(BF16)
    dk_ref[...] = jnp.zeros_like(dk_ref)
    dv_ref[...] = jnp.zeros_like(dv_ref)
    here = pl.ds(window_of(dp, span), span)
    dk = dot(grad_scores, q, ((0,), (0,))).astype(BF16)
    dk_ref[here] = dk.reshape(span, rows, dk.shape[1])
    dv = dot(probs.astype(BF16), g, ((0,), (0,))).astype(BF16)
    dv_ref[here] = dv.reshape(span, rows, dv.shape[1])

    @pl.when(step == final)
    def _():
        for t in range(1, max([len(order) for order in orders] + [0]) + 1):
            for each in sums:
                each.step(t)
        copies = [
            pltpu.make_async_copy(each.own(), outs[a], out_sem.at[a]) for a, each in enumerate(sums)
        ]
        for copy in copies:
            copy.start()
        for each in sums:
            each.wait_sends()
        for copy in copies:
            copy.wait()


def attend_back(
    starts, queries, keys, values, logs_in, grad, cosine, sine, sums, micro, rows, ne, collective
):
    nd = keys.shape[0]
    grid, mine, theirs, column, logs, _ = attention_specs(micro, rows, nd)
    table = pl.BlockSpec((rows, 128), lambda m, h, *_: (0, 0))
    n = len(sums)
    shapes = [(v.shape[0], v.shape[1] - 1) + v.shape[2:] for v, _, _ in sums]
    deep = max([s[0] - 1 for s in shapes] + [1])
    some = max(n, 1)
    return pl.pallas_call(
        functools.partial(
            attend_back_body, nd // 2 + 1, ne, nd, tuple(tuple(order) for _, order, _ in sums)
        ),
        grid=grid,
        in_specs=[column, mine, theirs, theirs, logs, mine, table, table] + [ANY] * (2 * n),
        out_specs=[mine, theirs, theirs] + [ANY] * n,
        out_shape=[
            jax.ShapeDtypeStruct(queries.shape, BF16),
            jax.ShapeDtypeStruct(keys.shape, BF16),
            jax.ShapeDtypeStruct(values.shape, BF16),
        ]
        + [jax.ShapeDtypeStruct(s[1:], BF16) for s in shapes],
        scratch_shapes=[pltpu.VMEM(s, BF16) for s in shapes] * 2
        + [pltpu.VMEM((s[0] - 1,) + s[1:], BF16) for s in shapes]
        + [DMA((some, 2)), DMA((some,)), DMA((some, deep)), DMA((some, deep))],
        compiler_params=pltpu.CompilerParams(
            vmem_limit_bytes=60 * 2**20, collective_id=collective, has_side_effects=True
        ),
        cost_estimate=cost(25),
    )(
        starts,
        queries,
        keys,
        values,
        logs_in,
        grad,
        cosine,
        sine,
        *[v for v, _, _ in sums],
        *[extra for _, _, extra in sums],
    )


def finish_body(ne, nd, orders, n_out, *refs):
    refs = list(refs)

    def take(n):
        return [refs.pop(0) for _ in range(n)]

    n_ref, dq_ref, dk_ref, dv_ref, cos_ref, sin_ref, tokens_ref, gain_ref = take(8)
    res_ref, wq_ref, wk_ref, wv_ref, wo_ref, small_ref, mix_ref = take(7)
    (tok_out,) = take(1)
    count = 2 * n_out + 3
    outs, (mix_out,) = take(count), take(1)
    held, pair_in, line_in = take(count), take(count), take(count)
    dk_turned, wq, wk, wv, res, mix_held, mix_in = take(7)
    load_sem, own_sem, out_sem, dp_send, dp_recv, ep_send, ep_recv = refs
    ep, dp = lax.axis_index("ep"), lax.axis_index("dp")
    columns = held[0].shape[3]
    own = [
        pltpu.make_async_copy(src, dst, own_sem.at[i])
        for i, (src, dst) in enumerate(
            ((wq_ref, wq), (wk_ref, wk), (wv_ref, wv), (res_ref, res))
        )
    ]
    sums = []
    for a in range(count):
        loads = []
        if a < n_out or a == count - 1:
            src = wo_ref if a < n_out else small_ref
            at = pl.ds(a * columns if a < n_out else 0, held[a].shape[3])
            loads = [
                pltpu.make_async_copy(src.at[e, :, :, at], held[a].at[:, e], load_sem.at[a, e])
                for e in range(ne)
            ]
        sums.append(
            PairSum(
                dp, orders[a % 2], loads, held[a], None, pair_in[a], dp_send.at[a], dp_recv.at[a]
            )
        )
    lines = [
        LineSum(ep, ne, sums[a].own(), line_in[a], ep_send.at[a], ep_recv.at[a])
        for a in range(count)
    ]
    early, made, small = sums[:n_out], sums[n_out:-1], sums[-1]
    queries, others = made[:n_out], made[n_out:]
    mix = LineSum(ep, ne, mix_held, mix_in, ep_send.at[count], ep_recv.at[count])
    mix_load = pltpu.make_async_copy(
        mix_ref.at[:, pl.ds(mix_ref.shape[1] - mix_held.shape[1], mix_held.shape[1])],
        mix_held,
        own_sem.at[4],
    )
    for each in early:
        each.load()
    mix_load.start()
    for copy in own:
        copy.start()
    small.load()
    greet(ep, dp, ne, nd)
    turns = bit_count(nd)

    def steps(group, t):
        for each in group:
            if t <= turns:
                each.step(t)

    def line_steps(group, t):
        for each in group:
            if t < ne:
                lines[sums.index(each)].step(t)

    steps(early, 0)
    mix_load.wait()
    mix.step(0)

    normed = n_ref[...]
    cosine, sine = cos_ref[...], -sin_ref[...]
    for i in range(0, dk_ref.shape[1], 128):
        part = dk_ref[:, i : i + 128].astype(F32)
        dk_turned[:, i : i + 128] = turn(part, cosine, sine).astype(BF16)
    tile = 256

    def product(grad, first, each):
        share = each.held.shape[2]
        for c in range(0, each.held.shape[3], tile):
            y = dot(normed, grad[:, first + c : first + c + tile], ((0,), (0,))).astype(BF16)
            for e in range(ne):
                for d in range(nd):
                    r = (e * nd + d) * share
                    each.held[d, e, :, c : c + tile] = y[r : r + share]
        each.step(0)

    for i, each in enumerate(made):
        if i < n_out:
            product(dq_ref, i * columns, each)
        else:
            product((dk_turned, dv_ref)[i - n_out], 0, each)
        if i == 0:
            steps(early, 1)
        else:
            made[i - 1].step(1)
    for copy in own:
        copy.wait()
    back = dot(dq_ref[...], wq[...], ((1,), (1,)))
    steps(made[-1:], 1)
    mix.step(1)
    back = back + dot(dk_turned[...], wk[...], ((1,), (1,)))
    back = back + dot(dv_ref[...], wv[...], ((1,), (1,)))
    steps(early, 2)
    x = tokens_ref[...].astype(F32)
    r = rms_scale(x)
    scaled = back * gain_ref[...]
    tok_out[...] = (
        res[...] + r * scaled - x * (r * r * r) * jnp.mean(scaled * x, axis=1, keepdims=True)
    )
    term = back * x * r
    high = term.astype(BF16)
    low = (term - high.astype(F32)).astype(BF16)
    ones = jnp.ones((x.shape[0], 128), BF16)
    column = dot(high, ones, ((0,), (0,))) + dot(low, ones, ((0,), (0,)))
    lane = lax.broadcasted_iota(jnp.int32, column.shape, 1)
    column = jnp.where(lane == EXPERTS, column, 0.0)
    for copy in small.loads:
        copy.wait()
    share = held[-1].shape[2]
    for e in range(ne):
        for d in range(nd):
            i = (e * nd + d) * share
            held[-1][d, e] = (held[-1][d, e].astype(F32) + column[i : i + share]).astype(BF16)
    small.loads = []
    steps([small], 0)
    steps(queries, 2)
    steps([small], 1)
    mix.step(2)
    for t in range(3, turns + 1):
        steps(early, t)
    line_steps(early, 0)
    steps(others, 2)
    for t in range(3, turns + 1):
        steps(queries, t)
    for t in range(3, ne):
        mix.step(t)
    line_steps(early, 1)
    line_steps(queries, 0)
    steps([small], 2)
    for t in range(3, turns + 1):
        steps(others, t)
        steps([small], t)
    tail = others + [small]
    for t in range(ne):
        line_steps(early, t + 2)
        line_steps(queries, t + 1)
        line_steps(tail, t)
    order = list(range(count))
    copies = []
    for a in order:
        copies.append(pltpu.make_async_copy(lines[a].own(), outs[a], out_sem.at[a]))
        copies[-1].start()
    copies.append(pltpu.make_async_copy(mix.own(), mix_out, out_sem.at[count]))
    copies[-1].start()
    for each in sums + lines + [mix]:
        each.wait_sends()
    for copy in copies:
        copy.wait()


def finish(
    ne,
    nd,
    orders,
    normed,
    grads,
    cosine,
    sine,
    tokens,
    gain,
    grad_residual,
    weights,
    w_out,
    small,
    mix,
    mix_rows,
):
    rows, width = tokens.shape
    line = (ne, mix_rows, width)
    share = width // (ne * nd)
    columns = weights[1].shape[1]
    n_out = width // columns
    count = 2 * n_out + 3
    wide = [columns] * (count - 1) + [128]
    split = lambda v: v.reshape(ne, nd, share, v.shape[1])
    return pl.pallas_call(
        functools.partial(finish_body, ne, nd, tuple(map(tuple, orders)), n_out),
        out_shape=[jax.ShapeDtypeStruct((rows, width), F32)]
        + [jax.ShapeDtypeStruct((share, c), BF16) for c in wide]
        + [jax.ShapeDtypeStruct(line[1:], BF16)],
        in_specs=[VMEM] * 8 + [ANY] * 7,
        out_specs=[VMEM] + [ANY] * (count + 1),
        scratch_shapes=[pltpu.VMEM((nd, ne, share, c), BF16) for c in wide]
        + [pltpu.VMEM((nd - 1, ne, share, c), BF16) for c in wide]
        + [pltpu.VMEM((2, ne, share, c), BF16) for c in wide]
        + [pltpu.VMEM(grads[1].shape, BF16)]
        + [pltpu.VMEM(w.shape, BF16) for w in weights]
        + [pltpu.VMEM((rows, width), F32)]
        + [pltpu.VMEM(line, BF16), pltpu.VMEM((2,) + line, BF16)]
        + [
            DMA((count, ne)),
            DMA((5,)),
            DMA((count + 1,)),
            DMA((count, nd - 1)),
            DMA((count, nd - 1)),
            DMA((count + 1, 2, ne)),
            DMA((count + 1, 2, ne)),
        ],
        compiler_params=pltpu.CompilerParams(
            vmem_limit_bytes=60 * 2**20, collective_id=4, has_side_effects=True
        ),
        cost_estimate=cost(45),
    )(
        normed,
        *grads,
        cosine,
        sine,
        tokens,
        gain,
        grad_residual,
        *weights,
        split(w_out),
        split(small),
        mix,
    )


def results_body(share, n_out, per_path, *refs):
    refs = list(refs)

    def take(n):
        return [refs.pop(0) for _ in range(n)]

    residual_ref, mix_first, mix_rest = take(3)
    paths = [take(per_path) for _ in range(2)]
    dense = take(2 * n_out + 3)
    out_ref, d_out, d_query, d_key, d_value, router, gain_one, gain_two = take(8)
    gate, up, down = refs
    e = pl.program_id(0)

    @pl.when(e == 0)
    def _():
        rows = mix_first.shape[0]
        for i, mix in enumerate((mix_first, mix_rest)):
            at = slice(i * rows, i * rows + mix.shape[0])
            out_ref[at, :] = (residual_ref[at, :] + mix[...].astype(F32)).astype(BF16)
        width = dense[0].shape[1]
        for i in range(n_out):
            d_out[:, i * width : (i + 1) * width] = dense[i][...].astype(F32)
            d_query[:, i * width : (i + 1) * width] = dense[n_out + i][...].astype(F32)
        d_key[...] = dense[2 * n_out][...].astype(F32)
        d_value[...] = dense[2 * n_out + 1][...].astype(F32)
        small = dense[-1][...].astype(F32)
        router[...] = small[:, :EXPERTS]
        turned = small.T
        gain_one[...] = turned[EXPERTS : EXPERTS + 1]
        gain_two[...] = turned[EXPERTS + 1 : EXPERTS + 2]

    k = 0
    for n in range(per_path):
        for m in range(paths[0][n].shape[0]):
            for i in range(2):

                @pl.when(e == k)
                def _(src=paths[i][n], m=m):
                    gate[0] = src[m, :share].astype(F32)
                    up[0] = src[m, share : 2 * share].astype(F32)
                    piece, columns = down.shape[1], src.shape[2]
                    for j in range(down.shape[2] // columns):
                        at = 2 * share + j * piece
                        down[0, :, j * columns : (j + 1) * columns] = src[
                            m, at : at + piece
                        ].astype(F32)

                k += 1


def results(residual, mix, grads, dense, n_out, share, w_gate, w_down, nd, rows_share):
    rows, width = residual.shape
    n_exp, _, inner = w_gate.shape
    piece = w_down.shape[1] // nd
    ins = [residual, *mix, *grads[0], *grads[1], *dense]
    kv = dense[-2].shape[1]
    same = lambda v: pl.BlockSpec(v, lambda e: (0,) * len(v))
    outs = [
        ((rows, width), BF16),
        ((rows_share, width), F32),
        ((rows_share, width), F32),
        ((rows_share, kv), F32),
        ((rows_share, kv), F32),
        ((rows_share, EXPERTS), F32),
        ((1, rows_share), F32),
        ((1, rows_share), F32),
    ]
    experts_out = [((n_exp, share, inner), F32)] * 2 + [((n_exp, piece, width), F32)]
    return pl.pallas_call(
        functools.partial(results_body, share, n_out, len(grads[0])),
        grid=(n_exp,),
        out_shape=[jax.ShapeDtypeStruct(*v) for v in outs + experts_out],
        in_specs=[same(v.shape) for v in ins],
        out_specs=[same(v[0]) for v in outs]
        + [pl.BlockSpec((1,) + v[0][1:], lambda e: (e, 0, 0)) for v in experts_out],
        compiler_params=pltpu.CompilerParams(vmem_limit_bytes=60 * 2**20),
        cost_estimate=cost(6),
    )(*ins)


def per_device(
    tokens,
    segments,
    routes,
    first_gain,
    w_query,
    w_key,
    w_value,
    w_out,
    second_gain,
    w_router,
    w_gate,
    w_up,
    w_down,
    cotangent,
):
    micro, rows, width = tokens.shape
    ne, nd = lax.axis_size("ep"), lax.axis_size("dp")
    ep, dp = lax.axis_index("ep"), lax.axis_index("dp")
    groups = HEADS // KV_HEADS
    kv_width = KV_HEADS * HEAD_DIM
    every = micro * rows
    inputs = tokens.reshape(every, width).astype(F32)
    grad_output = cotangent.reshape(every, width).astype(F32)

    query_pos = dp * rows + jnp.arange(rows, dtype=jnp.int32)
    halfway = HEAD_DIM // 2
    frequency = ROPE_BASE ** (-(jnp.arange(halfway, dtype=F32) * 2.0 / HEAD_DIM))
    angles = query_pos.astype(F32)[:, None] * frequency[None, :]
    lanes = 2 * HEAD_DIM // halfway
    sign = jnp.where(jnp.arange(2 * HEAD_DIM) % HEAD_DIM < halfway, -1.0, 1.0).astype(F32)
    cosine = jnp.tile(jnp.cos(angles), (micro, lanes))
    sine = jnp.tile(jnp.sin(angles), (micro, lanes)) * sign

    tokens_flat = tokens.reshape(every, width)
    gain_one = first_gain.reshape(1, width)
    normed_one, query_rot, key_rot, value_own = project(
        tokens_flat, gain_one, cosine, sine, w_query, w_key, w_value
    )

    ids = jnp.arange(128, dtype=jnp.int32)
    counts = jnp.sum((segments[:, 0, :, None] == ids).astype(F32), axis=1)
    counts = jnp.concatenate([counts, jnp.zeros((8 - micro, 128), F32)], axis=0)

    cot_own = cotangent.reshape(every, width)

    def around(value, k):
        return lax.ppermute(value, "ep", [(i, (i + k) % ne) for i in range(ne)])

    cots = [cot_own] + [around(cot_own, k) for k in range(1, ne)]
    key_all, value_all, count_all = gather(ne, nd, (key_rot, value_own, counts), (), 0, 25)

    totals = jnp.sum(count_all[:, :micro], axis=0)
    lower = (ids[None, None, :] < segments[:, 0, :, None]).astype(F32)
    starts = jnp.sum(lower * totals[:, None, :], axis=2).astype(jnp.int32)
    starts = starts.reshape(every, 1)
    attn_low, logs = attend(dp, starts, query_rot, key_all, value_all, micro, rows, nd)
    residual = inputs + jnp.dot(attn_low, w_out, preferred_element_type=F32)
    inv_two = rms_scale(residual)
    normed_two = (residual * inv_two * second_gain).astype(BF16)
    logits = jnp.dot(normed_two, w_router, preferred_element_type=F32)
    routing = routes.reshape(every, routes.shape[2])
    chosen = jnp.any(
        routing[:, :, None] == jnp.arange(EXPERTS, dtype=jnp.int32)[None, None, :], axis=1
    )
    masked = jnp.where(chosen, logits, MASKED)
    terms = jnp.where(chosen, jnp.exp(masked - jnp.max(masked, axis=1, keepdims=True)), 0.0)
    gate_probs = terms / jnp.sum(terms, axis=1, keepdims=True)
    marked = jnp.where(chosen, gate_probs, -1.0).T

    normed_all, marked_all = gather(ne, nd, (), (normed_two, marked), 1, 38)
    here = EXPERTS // ne
    probs_here = lax.dynamic_slice_in_dim(marked_all, ep * here, here, axis=1)
    probs_here = (
        probs_here.reshape(ne, here, micro, rows)
        .transpose(0, 2, 1, 3)
        .reshape(ne * micro, here, rows)
    )
    nb = bit_count(nd)
    orders = [order[:-1][::-1] for order in gather_orders(nd)]
    mix, grad_in, pair_dots, *grads = experts(
        normed_all.reshape(ne * every, width),
        cots,
        probs_here,
        w_gate,
        w_up,
        w_down,
        micro,
        rows,
        ne,
        nd,
        6,
    )
    kept, landed, last = grads[:2], grads[2:4], grads[4:]
    pair_dots = pair_dots.reshape(here, ne, every).transpose(1, 0, 2)
    head = (slice(None), slice(0, 1))
    *grads, grad_back, dots_all = reduce(
        ne,
        nd,
        [(last[i], orders[i], None, None, False) for i in range(2)]
        + [(kept[i], orders[i][1:], head, landed[i], False) for i in range(2)],
        ((grad_in.reshape(ne, every, width), None),),
        (pair_dots,),
        2,
        40,
    )
    grads_last, grads_head = grads[:2], grads[2:]
    pair_dot = dots_all.reshape(EXPERTS, every).T
    grad_logits = gate_probs * (
        pair_dot - jnp.sum(gate_probs * pair_dot, axis=1, keepdims=True)
    )
    grad_w_router = jnp.einsum(
        "td,te->de", normed_two.astype(F32), grad_logits, precision=HIGHEST
    )
    grad_normed_two = (
        jnp.einsum("te,de->td", grad_logits, w_router.astype(F32), precision=HIGHEST)
        + grad_back.astype(F32)
    )
    scaled_two = grad_normed_two * second_gain
    grad_gain_two = jnp.sum(grad_normed_two * residual * inv_two, axis=0)
    grad_residual = (
        grad_output
        + inv_two * scaled_two
        - residual * inv_two**3 * jnp.mean(scaled_two * residual, axis=-1, keepdims=True)
    )
    residual_low = grad_residual.astype(BF16)
    grad_w_out = jnp.einsum("tf,td->fd", attn_low, residual_low, preferred_element_type=F32)
    grad_attn = jnp.einsum("td,fd->tf", residual_low, w_out, preferred_element_type=F32).astype(
        BF16
    )
    more = kept[0].shape[1] > 1
    mix = mix.reshape(ne, every, width)
    grad_query, grad_key_all, grad_value_all, *grads_more = attend_back(
        starts,
        query_rot,
        key_all,
        value_all,
        logs,
        grad_attn,
        cosine,
        sine,
        [(kept[i], orders[i][1:], landed[i]) for i in range(2)] if more else [],
        micro,
        rows,
        ne,
        5,
    )
    full = [[0] + order for order in orders]
    grad_key, grad_value, mix_first = reduce(
        ne,
        nd,
        [
            (grad_key_all, full[0], None, None, False),
            (grad_value_all, full[1], None, None, False),
        ],
        ((mix, (slice(None), slice(0, rows))),),
        (),
        3,
        30,
    )
    small = jnp.concatenate(
        [
            grad_w_router,
            jnp.zeros((width, 1), F32),
            grad_gain_two[:, None],
            jnp.zeros((width, 128 - EXPERTS - 2), F32),
        ],
        axis=1,
    ).astype(BF16)
    grad_tokens, *dense, mix_rest = finish(
        ne,
        nd,
        full,
        normed_one,
        (grad_query, grad_key, grad_value),
        cosine,
        sine,
        tokens_flat,
        gain_one,
        grad_residual,
        (w_query, w_key, w_value),
        grad_w_out.astype(BF16),
        small,
        mix,
        every - rows,
    )
    (
        output,
        d_out,
        d_query,
        d_key,
        d_value,
        d_router,
        d_gain_one,
        d_gain_two,
        d_gate,
        d_up,
        d_down,
    ) = results(
        residual,
        (mix_first, mix_rest),
        [
            [grads_head[i]] + ([grads_more[i]] if more else []) + [grads_last[i][None]]
            for i in range(2)
        ],
        dense,
        width // kv_width,
        width // nd,
        w_gate,
        w_down,
        nd,
        width // (ne * nd),
    )
    return (
        output.reshape(tokens.shape),
        grad_tokens.reshape(tokens.shape),
        d_gain_one.reshape(-1),
        d_query,
        d_key,
        d_value,
        d_out,
        d_gain_two.reshape(-1),
        d_router,
        d_gate,
        d_up,
        d_down,
    )


def solution(mesh):
    in_specs = (
        P(None, ("ep", "dp"), None),
        P(None, "ep", "dp"),
        P(None, ("ep", "dp"), None),
        P(),
        P(),
        P(),
        P(),
        P(),
        P(),
        P(),
        P("ep", None, None),
        P("ep", None, None),
        P("ep", None, None),
        P(None, ("ep", "dp"), None),
    )
    out_specs = (
        P(None, ("ep", "dp"), None),
        P(None, ("ep", "dp"), None),
        P(("ep", "dp")),
        P(("ep", "dp"), None),
        P(("ep", "dp"), None),
        P(("ep", "dp"), None),
        P(("ep", "dp"), None),
        P(("ep", "dp")),
        P(("ep", "dp"), None),
        P("ep", "dp", None),
        P("ep", "dp", None),
        P("ep", "dp", None),
    )
    return jax.shard_map(
        per_device, mesh=mesh, in_specs=in_specs, out_specs=out_specs, check_vma=False
    )
```

```python
import functools

import jax
import jax.numpy as jnp
import numpy as np
from jax import lax
from jax.experimental import pallas as pl
from jax.experimental.pallas import tpu as pltpu
from jax.sharding import PartitionSpec as P

HEADS = 16
KV_HEADS = 8
HEAD_DIM = 64
EXPERTS = 32
CAP = 64
EPSILON = 1e-06
ROPE_BASE = 10000.0
MASKED = -1e30
HIGHEST = lax.Precision.HIGHEST
MESH = pl.DeviceIdType.MESH
BF16 = jnp.bfloat16
F32 = jnp.float32
VMEM = pl.BlockSpec(memory_space=pltpu.VMEM)
ANY = pl.BlockSpec(memory_space=pl.ANY)
DMA = pltpu.SemaphoreType.DMA


def bit_count(n):
    return n.bit_length() - 1


def masks(bits):
    out = [0]
    for b in bits:
        out = out + [m | (1 << b) for m in out]
    return out


def gather_orders(n):
    bits = list(range(bit_count(n)))
    return (bits[1:] + bits[:1], bits[:0:-1] + bits[:1])


def greet(ep, dp, ne, nd):
    barrier = pltpu.get_barrier_semaphore()
    for k in range(1, ne):
        pl.semaphore_signal(
            barrier, inc=1, device_id={"ep": lax.rem(ep + k, ne)}, device_id_type=MESH
        )
    for b in range(bit_count(nd)):
        pl.semaphore_signal(
            barrier, inc=1, device_id={"dp": jnp.bitwise_xor(dp, 1 << b)}, device_id_type=MESH
        )
    pl.semaphore_wait(barrier, ne - 1 + bit_count(nd))


def remote(src, dst, send, recv, where):
    return pltpu.make_async_remote_copy(
        src_ref=src, dst_ref=dst, send_sem=send, recv_sem=recv, device_id=where, device_id_type=MESH
    )


def gather_body(ne, nd, n_dp, n_ep, *refs):
    n_in = n_dp + n_ep
    ins, outs, sems = refs[:n_in], refs[n_in : 2 * n_in], refs[2 * n_in :]
    ep, dp = lax.axis_index("ep"), lax.axis_index("dp")
    own_sem, dp_send, dp_recv, ep_send, ep_recv = sems
    greet(ep, dp, ne, nd)
    own = []
    for a in range(n_in):
        me = dp if a < n_dp else ep
        copy = pltpu.make_async_copy(ins[a], outs[a].at[me], own_sem.at[a])
        copy.start()
        own.append(copy)

    def dp_copy(a, t, m):
        order = gather_orders(nd)[a % 2]
        block = jnp.bitwise_xor(dp, m)
        k = (1 << t) - 1 + masks(order[:t]).index(m)
        return remote(
            ins[a] if m == 0 else outs[a].at[block],
            outs[a].at[block],
            dp_send.at[a, k],
            dp_recv.at[a, k],
            {"dp": jnp.bitwise_xor(dp, 1 << order[t])},
        )

    def ep_copy(a, s, way):
        shard = lax.rem(ep - way * s + ne, ne)
        src = ins[n_dp + a] if s == 0 else outs[n_dp + a].at[shard]
        k = 0 if way == 1 else 1
        return remote(
            src,
            outs[n_dp + a].at[shard],
            ep_send.at[a, k, s],
            ep_recv.at[a, k, s],
            {"ep": lax.rem(ep + way + ne, ne)},
        )

    def sends(s, way):
        if way == 1:
            return (ep >= s) & (ep < ne - 1)
        return (ep + s <= ne - 1) & (ep >= 1)

    def receives(s, way):
        if way == 1:
            return ep >= 1 + s
        return ep + 1 + s <= ne - 1

    def ep_start(s):
        for a in range(n_ep):
            for way in (1, -1):

                @pl.when(sends(s, way))
                def _(a=a, way=way):
                    ep_copy(a, s, way).start()

    def ep_wait(s):
        for a in range(n_ep):
            for way in (1, -1):

                @pl.when(receives(s, way))
                def _(a=a, way=way):
                    ep_copy(a, s, way).wait_recv()

    dp_steps = bit_count(nd) if n_dp else 0
    ep_steps = ne - 1 if n_ep else 0
    for t in range(dp_steps):
        for a in range(n_dp):
            dp_copy(a, t, 0).start()
    for t in range(max(dp_steps, ep_steps) + 1):
        if 0 < t <= dp_steps:
            for a in range(n_dp):
                order = gather_orders(nd)[a % 2]
                for m in masks(order[: t - 1]):
                    dp_copy(a, t - 1, m).wait_recv()
                    for later in range(t, dp_steps):
                        dp_copy(a, later, m | (1 << order[t - 1])).start()
        if 0 < t <= ep_steps:
            ep_wait(t - 1)
        if t < ep_steps:
            ep_start(t)
    for t in range(dp_steps):
        for a in range(n_dp):
            for m in masks(gather_orders(nd)[a % 2][:t]):
                dp_copy(a, t, m).wait_send()
    for s in range(ep_steps):
        for a in range(n_ep):
            for way in (1, -1):

                @pl.when(sends(s, way))
                def _(a=a, s=s, way=way):
                    ep_copy(a, s, way).wait_send()

    for c in own:
        c.wait()


def cost(us):
    return pl.CostEstimate(flops=0, bytes_accessed=int(us * 3.0e6), transcendentals=0)


def gather(ne, nd, dp_arrays, ep_arrays, collective, us):
    arrays = list(dp_arrays) + list(ep_arrays)
    counts = [nd] * len(dp_arrays) + [ne] * len(ep_arrays)
    a, b = max(len(dp_arrays), 1), max(len(ep_arrays), 1)
    return pl.pallas_call(
        functools.partial(gather_body, ne, nd, len(dp_arrays), len(ep_arrays)),
        out_shape=[
            jax.ShapeDtypeStruct((n,) + v.shape, v.dtype) for n, v in zip(counts, arrays)
        ],
        in_specs=[ANY] * len(arrays),
        out_specs=[ANY] * len(arrays),
        scratch_shapes=[
            DMA((len(arrays),)),
            DMA((a, nd - 1)),
            DMA((a, nd - 1)),
            DMA((b, 2, ne - 1)),
            DMA((b, 2, ne - 1)),
        ],
        compiler_params=pltpu.CompilerParams(
            collective_id=collective, has_side_effects=True, vmem_limit_bytes=60 * 2**20
        ),
        cost_estimate=cost(us),
    )(*arrays)


def add_into(ref, arrived):
    if len(ref.shape) > 2:

        @pl.loop(0, ref.shape[0])
        def _(i):
            add_into(ref.at[i], arrived.at[i])

    else:
        ref[...] = (ref[...].astype(F32) + arrived[...].astype(F32)).astype(ref.dtype)


class PairSum:
    def __init__(self, dp, order, loads, held, extra, landing, send_sem, recv_sem):
        self.dp, self.order, self.held, self.landing = dp, order, held, landing
        self.send_sem, self.recv_sem = send_sem, recv_sem
        self.extra, self.loads = extra, loads
        self.index = 0
        for b in order:
            side = jnp.bitwise_and(lax.shift_right_logical(dp, b), 1)
            self.index = self.index + (side << self.place(b))

    def place(self, bit):
        return sorted(self.order).index(bit)

    def copies(self, t):
        order = self.order
        partner = jnp.bitwise_xor(self.index, 1 << self.place(order[t]))
        first = sum(1 << (len(order) - 1 - i) for i in range(t))
        return [
            (
                m,
                first + j,
                remote(
                    self.held.at[jnp.bitwise_xor(partner, m)],
                    self.landing.at[first + j],
                    self.send_sem.at[first + j],
                    self.recv_sem.at[first + j],
                    {"dp": jnp.bitwise_xor(self.dp, 1 << order[t])},
                ),
            )
            for j, m in enumerate(masks([self.place(b) for b in order[t + 1 :]]))
        ]

    def load(self):
        for copy in self.loads:
            copy.start()

    def step(self, t):
        if t == 0:
            for copy in self.loads:
                copy.wait()
            if self.extra is not None:
                add_into(self.held, self.extra)
        elif t <= len(self.order):
            for m, k, copy in self.copies(t - 1):
                copy.wait_recv()
                add_into(self.held.at[jnp.bitwise_xor(self.index, m)], self.landing.at[k])
        if t < len(self.order):
            for m, k, copy in self.copies(t):
                copy.start()

    def own(self):
        return self.held.at[self.index]

    def wait_sends(self):
        for t in range(len(self.order)):
            for m, k, copy in self.copies(t):
                copy.wait_send()


class LineSum:
    def __init__(self, ep, ne, blocks, landing, send_sem, recv_sem):
        self.ep, self.ne, self.blocks, self.landing = ep, ne, blocks, landing
        self.send_sem, self.recv_sem = send_sem, recv_sem

    def copy(self, dest, way):
        k = 0 if way == 1 else 1
        return remote(
            self.blocks.at[dest],
            self.landing.at[k, dest],
            self.send_sem.at[k, dest],
            self.recv_sem.at[k, dest],
            {"ep": lax.rem(self.ep + way + self.ne, self.ne)},
        )

    def turn(self, t, way):
        ep, ne = self.ep, self.ne
        dest = ep + ne - 1 - t if way == 1 else ep + t - (ne - 1)
        has = dest <= ne - 1 if way == 1 else dest >= 0
        inner = ep >= 1 if way == 1 else ep <= ne - 2
        return dest, has, inner

    def step(self, t):
        for way in (1, -1):
            dest, has, inner = self.turn(t, way)

            @pl.when(has & inner)
            def _(way=way, dest=dest):
                self.copy(dest, way).wait_recv()
                add_into(self.blocks.at[dest], self.landing.at[0 if way == 1 else 1, dest])

            if t < self.ne - 1:

                @pl.when(has)
                def _(way=way, dest=dest):
                    self.copy(dest, way).start()

    def own(self):
        return self.blocks.at[self.ep]

    def wait_sends(self):
        for t in range(self.ne - 1):
            for way in (1, -1):
                dest, has, inner = self.turn(t, way)

                @pl.when(has)
                def _(way=way, dest=dest):
                    self.copy(dest, way).wait_send()


def shape_at(array, where):
    return tuple(len(range(*w.indices(n))) for w, n in zip(where, array.shape)) + array.shape[len(where) :]


def reduce_body(ne, nd, pairs, line_parts, n_swap, *refs):
    refs = list(refs)

    def take(n):
        return [refs.pop(0) for _ in range(n)]

    n_pair, n_line = len(pairs), len(line_parts)
    n_extra = sum(p[2] for p in pairs)
    n_both = sum(p[3] for p in pairs)
    n_sum = n_pair + n_line
    ins, extra_ins, swap_ins = take(n_sum), take(n_extra), take(n_swap)
    outs, swap_outs = take(n_sum), take(n_swap)
    held, extras, pair_in = take(n_sum), take(n_extra), take(n_pair)
    both_in, line_in = take(n_both), take(n_line)
    load_sem, out_sem, dp_send, dp_recv, ep_send, ep_recv, swap_send, swap_recv = refs
    ep, dp = lax.axis_index("ep"), lax.axis_index("dp")
    sums, then = [], []
    for a, (order, where, has_extra, both) in enumerate(pairs):
        targets = [(ins[a], held[a])]
        extra = extras.pop(0) if has_extra else None
        if has_extra:
            targets.append((extra_ins.pop(0), extra))
        loads = [
            pltpu.make_async_copy(src.at[where] if where else src, dst, load_sem.at[a, i])
            for i, (src, dst) in enumerate(targets)
        ]
        sums.append(
            PairSum(dp, order, loads, held[a], extra, pair_in[a], dp_send.at[a], dp_recv.at[a])
        )
        if both:
            i = len(then)
            then.append(
                LineSum(ep, ne, sums[a].own(), both_in[i], ep_send.at[i], ep_recv.at[i])
            )
    lines, line_loads = [], []
    for i in range(n_line):
        a = n_pair + i
        src = ins[a].at[line_parts[i]] if line_parts[i] else ins[a]
        line_loads.append(pltpu.make_async_copy(src, held[a], load_sem.at[a, 0]))
        lines.append(
            LineSum(
                ep, ne, held[a], line_in[i], ep_send.at[n_both + i], ep_recv.at[n_both + i]
            )
        )
    for copy in line_loads:
        copy.start()
    for each in sums:
        each.load()
    greet(ep, dp, ne, nd)
    swaps = []
    for a in range(n_swap):
        src, dst = swap_ins[a], swap_outs[a]
        own = pltpu.make_async_copy(src.at[ep], dst.at[ep], load_sem.at[n_sum + a, 0])
        own.start()
        swaps.append(own)
        for k in range(1, ne):
            to = lax.rem(ep + k, ne)
            copy = remote(
                src.at[to], dst.at[ep], swap_send.at[a, k - 1], swap_recv.at[a, k - 1], {"ep": to}
            )
            copy.start()
            swaps.append(copy)
    for copy in line_loads:
        copy.wait()
    steps = max([len(p[0]) + 1 for p in pairs] + [ne if n_line else 0])
    for t in range(steps):
        if t < ne:
            for each in lines:
                each.step(t)
        for each in sums:
            each.step(t)
    for t in range(ne):
        for each in then:
            each.step(t)
    results, after = [], iter(then)
    for a in range(n_sum):
        if a >= n_pair:
            src = lines[a - n_pair].own()
        else:
            src = next(after).own() if pairs[a][3] else sums[a].own()
        copy = pltpu.make_async_copy(src, outs[a], out_sem.at[a])
        copy.start()
        results.append(copy)
    for each in sums + then + lines:
        each.wait_sends()
    for copy in swaps + results:
        copy.wait()


def reduce(ne, nd, pairs, lines, swaps, collective, us):
    line_parts = tuple(where for _, where in lines)
    line_shapes = [shape_at(v, where) if where else v.shape for v, where in lines]
    lines = [v for v, _ in lines]
    arrays = [p[0] for p in pairs] + list(lines)
    extras = [p[3] for p in pairs if p[3] is not None]
    kinds = tuple((tuple(p[1]), p[2], p[3] is not None, p[4]) for p in pairs)
    shapes = [shape_at(p[0], p[2]) if p[2] else p[0].shape for p in pairs]
    boths = [s for s, p in zip(shapes, pairs) if p[4]]
    results = [s[2:] if p[4] else s[1:] for s, p in zip(shapes, pairs)]
    results += [s[1:] for s in line_shapes]
    scratch = shapes + line_shapes
    scratch += [s for s, p in zip(shapes, pairs) if p[3] is not None]
    scratch += [(s[0] - 1,) + s[1:] for s in shapes]
    scratch += [(2,) + s[1:] for s in boths] + [(2,) + s for s in line_shapes]
    some = lambda n: max(n, 1)
    line_count = some(len(lines) + len(boths))
    deep = max([s[0] - 1 for s in shapes] + [1])
    return pl.pallas_call(
        functools.partial(reduce_body, ne, nd, kinds, line_parts, len(swaps)),
        out_shape=[jax.ShapeDtypeStruct(s, BF16) for s in results]
        + [jax.ShapeDtypeStruct(v.shape, v.dtype) for v in swaps],
        in_specs=[ANY] * (len(arrays) + len(extras) + len(swaps)),
        out_specs=[ANY] * (len(arrays) + len(swaps)),
        scratch_shapes=[pltpu.VMEM(s, BF16) for s in scratch]
        + [
            DMA((len(arrays) + len(swaps), 2)),
            DMA((len(arrays),)),
            DMA((some(len(pairs)), deep)),
            DMA((some(len(pairs)), deep)),
            DMA((line_count, 2, ne)),
            DMA((line_count, 2, ne)),
            DMA((some(len(swaps)), ne - 1)),
            DMA((some(len(swaps)), ne - 1)),
        ],
        compiler_params=pltpu.CompilerParams(
            collective_id=collective, has_side_effects=True, vmem_limit_bytes=60 * 2**20
        ),
        cost_estimate=cost(us),
    )(*arrays, *extras, *swaps)


def dot(a, b, dims=((1,), (0,))):
    return lax.dot_general(a, b, (dims, ((), ())), preferred_element_type=F32)


def expert_body(ne, nd, micro, rows, *refs):
    cots, refs = refs[:ne], refs[ne:]
    normed_ref, probs_ref, gate_ref, up_ref, down_ref = refs[:5]
    mix_ref, grad_ref, dots_ref = refs[5:8]
    kept, landed, whole = refs[8:10], refs[10:12], refs[12:14]
    rows_in, cots_in, picks, first, second, sides, arrived, leaving = refs[14:22]
    load_sem, store_sem, send_sem, recv_sem, free_sem, far_send, far_recv = refs[22:]
    e = pl.program_id(0)
    last = pl.num_programs(0) - 1
    ep, dp = lax.axis_index("ep"), lax.axis_index("dp")
    other = {"dp": jnp.bitwise_xor(dp, 1)}
    every = micro * rows
    blocks = ne * micro
    width = first.shape[1]
    n_exp = rows_in.shape[1]

    core = jnp.bitwise_and(dp, 1)
    keep, send = sides.at[core], sides.at[1 - core]

    def exchange():
        return remote(send, arrived, send_sem, recv_sem, other)

    def loads():
        out = [pltpu.make_async_copy(normed_ref, first, load_sem.at[ne])]
        for k in range(ne):
            at = pl.multiple_of(lax.rem(ep - k + ne, ne) * every, every)
            out.append(
                pltpu.make_async_copy(cots[k], second.at[pl.ds(at, every)], load_sem.at[k])
            )
        return out

    def block_at(s):
        return pl.ds(pl.multiple_of(s * rows, rows), rows)

    def returned(t):
        k, m = t // micro, lax.rem(t, micro)
        return lax.rem(ep + k, ne) * micro + m

    def stores(t):
        s = returned(t)
        return (
            pltpu.make_async_copy(
                first.at[block_at(s)], mix_ref.at[block_at(s)], store_sem.at[0, t]
            ),
            pltpu.make_async_copy(
                second.at[block_at(s)], grad_ref.at[block_at(s)], store_sem.at[1, t]
            ),
        )

    def far(i, n):
        return remote(
            leaving.at[i, lax.rem(n, leaving.shape[1])],
            landed[i].at[:, n],
            far_send.at[i, lax.rem(n, leaving.shape[1])],
            far_recv.at[i, n],
            {"dp": jnp.bitwise_xor(dp, 1 << first_bits(nd)[i])},
        )

    def last_copy():
        return pltpu.make_async_copy(keep, whole[1], load_sem.at[0])

    def collect():
        exchange().wait_recv()
        pieces = sides.shape[1]
        n = (e - 1) // 2
        for i, bit in enumerate(first_bits(nd)):
            mine = jnp.bitwise_and(lax.shift_right_logical(dp, bit), 1)

            def piece(at, side, bit=bit):
                low = (1 << (bit - 1)) - 1
                j = ((at & ~low) << 1 | (at & low)) + (side << (bit - 1))
                return (keep[j].astype(F32) + arrived[j].astype(F32)).astype(BF16)

            @pl.when((lax.rem(e - 1, 2) == i) & (n < n_exp // 2 - 1))
            def _(i=i, mine=mine, piece=piece):
                slots = leaving.shape[1]

                @pl.when(n >= slots)
                def _():
                    far(i, n - slots).wait_send()

                for at in range(pieces // 2):
                    leaving[i, lax.rem(n, slots), at] = piece(at, 1 - mine)
                far(i, n).start()
                for at in range(pieces // 2):
                    kept[i][at, 0] = piece(at, mine)

            @pl.when((lax.rem(e - 1, 2) == i) & (n == n_exp // 2 - 1))
            def _(i=i):
                add_into(keep, arrived)
                if i == 0:
                    whole[0][...] = keep[...]
                else:
                    last_copy().start()

    @pl.when(e == 0)
    def _():
        for copy in loads():
            copy.start()
        barrier = pltpu.get_barrier_semaphore()
        met = [0] + sorted(set(first_bits(nd)))
        for bit in met:
            pl.semaphore_signal(
                barrier,
                inc=1,
                device_id={"dp": jnp.bitwise_xor(dp, 1 << bit)},
                device_id_type=MESH,
            )
        pl.semaphore_wait(barrier, len(met))
        before = lax.broadcasted_iota(jnp.int32, (rows, rows), 0)
        after = lax.broadcasted_iota(jnp.int32, (rows, rows), 1)
        earlier = (before < after).astype(BF16)
        slot = lax.broadcasted_iota(jnp.int32, (n_exp, CAP, rows), 1)
        for copy in loads():
            copy.wait()

        @pl.loop(0, blocks)
        def _(s):
            at = block_at(s)
            probs = probs_ref[s]
            hit = probs >= 0.0
            rank = dot(hit.astype(BF16), earlier)
            rank = jnp.where(hit, rank, -1.0).astype(jnp.int32)
            pick = jnp.broadcast_to(rank[:, None, :], (n_exp, CAP, rows)) == slot
            pick_f = pick.astype(F32)
            flat = pick_f.reshape(n_exp * CAP, rows).astype(BF16)
            picks[s] = flat
            rows_in[s] = dot(flat, first[at, :]).astype(BF16).reshape(n_exp, CAP, width)
            cots_in[s] = dot(flat, second[at, :]).astype(BF16).reshape(n_exp, CAP, width)

    @pl.when(e < last)
    def _():
        x = rows_in[:, e].reshape(blocks * CAP, width)
        c = cots_in[:, e].reshape(blocks * CAP, width)
        flat = picks[:, pl.ds(pl.multiple_of(e * CAP, CAP), CAP), :].astype(F32)
        p = jnp.sum(flat * probs_ref[:, pl.ds(e, 1), :], axis=2, keepdims=True)
        p = p.reshape(blocks * CAP, 1)
        w_gate, w_up, w_down = gate_ref[0], up_ref[0], down_ref[0]
        gate_pre = dot(x, w_gate)
        up_pre = dot(x, w_up)
        sigma = jax.nn.sigmoid(gate_pre)
        silu = gate_pre * sigma
        hidden = (silu * up_pre).astype(BF16)
        out = dot(hidden, w_down) * p
        back = dot(c, w_down, ((1,), (1,)))
        wide = hidden.astype(F32)
        pair = jnp.sum(wide * back, axis=1, keepdims=True)
        back = back * p
        grad_up = (back * silu).astype(BF16)
        grad_gate = (back * up_pre * (sigma * (1.0 + gate_pre * (1.0 - sigma)))).astype(BF16)
        scaled = (wide * p).astype(BF16)
        grad_x = dot(grad_gate, w_gate, ((1,), (1,))) + dot(grad_up, w_up, ((1,), (1,)))

        dots_ref[0] = jnp.sum(flat * pair.reshape(blocks, CAP, 1), axis=1)

        @pl.when(e > 0)
        def _():
            collect()
            pl.semaphore_signal(free_sem, inc=1, device_id=other, device_id_type=MESH)
            exchange().wait_send()
            pl.semaphore_wait(free_sem, 1)

        def split(value, offset):
            value = value.astype(BF16)
            piece, columns = value.shape[0] // nd, sides.shape[3]

            for i in range(nd):
                for j in range(value.shape[1] // columns):
                    at = offset + j * piece
                    sides[i % 2, i // 2, at : at + piece] = value[
                        i * piece : (i + 1) * piece, j * columns : (j + 1) * columns
                    ]

        share = width // nd
        split(dot(scaled, c, ((0,), (0,))), 2 * share)
        split(dot(x, grad_gate, ((0,), (0,))), 0)
        split(dot(x, grad_up, ((0,), (0,))), share)
        exchange().start()

        rows_in[:, e] = grad_x.astype(BF16).reshape(blocks, CAP, width)
        cots_in[:, e] = out.astype(BF16).reshape(blocks, CAP, width)

    @pl.when(e == last)
    def _():
        @pl.loop(0, blocks)
        def _(t):
            s = returned(t)
            at = block_at(s)
            flat = picks[s]
            for done, slots in ((first, cots_in), (second, rows_in)):
                value = dot(flat, slots[s].reshape(n_exp * CAP, width), ((0,), (0,)))
                done[at, :] = value.astype(BF16)
            for copy in stores(t):
                copy.start()

            @pl.when(t == 1)
            def _():
                collect()
                exchange().wait_send()

        @pl.loop(0, blocks)
        def _(t):
            for copy in stores(t):
                copy.wait()

        last_copy().wait()
        for i in range(2):
            for n in range(max(n_exp // 2 - 1 - leaving.shape[1], 0), n_exp // 2 - 1):
                far(i, n).wait_send()

            @pl.loop(0, n_exp // 2 - 1)
            def _(n, i=i):
                far(i, n).wait_recv()


def first_bits(nd):
    return [order[-2] for order in gather_orders(nd)]


def experts(normed, cots, probs, w_gate, w_up, w_down, micro, rows, ne, nd, collective):
    n_exp, width, inner = w_gate.shape
    blocks = ne * micro
    half = nd // 2
    packed = 2 * width // nd + (inner // nd) * (width // inner)
    full = (blocks * rows, width)
    one = pl.Buffered(1)
    weight = lambda e: (jnp.minimum(e, n_exp - 1), 0, 0)
    early = n_exp // 2 - 1
    part = (half // 2, early, packed, inner)
    kept = pl.BlockSpec(
        (half // 2, 1, packed, inner),
        lambda e: (0, jnp.minimum(jnp.maximum(e - 1, 0) // 2, early - 1), 0, 0),
    )
    last = (half, packed, inner)
    return pl.pallas_call(
        functools.partial(expert_body, ne, nd, micro, rows),
        grid=(n_exp + 1,),
        in_specs=[ANY] * (ne + 1)
        + [
            pl.BlockSpec(probs.shape, lambda e: (0, 0, 0), pipeline_mode=one),
            pl.BlockSpec((1, width, inner), weight),
            pl.BlockSpec((1, width, inner), weight),
            pl.BlockSpec((1, inner, width), weight),
        ],
        out_specs=[ANY, ANY, pl.BlockSpec((1, blocks, rows), weight), kept, kept, ANY, ANY]
        + [pl.BlockSpec(last, lambda e: (0, 0, 0), pipeline_mode=one), ANY],
        scratch_shapes=[
            pltpu.VMEM((blocks, n_exp, CAP, width), BF16),
            pltpu.VMEM((blocks, n_exp, CAP, width), BF16),
            pltpu.VMEM((blocks, n_exp * CAP, rows), BF16),
            pltpu.VMEM(full, BF16),
            pltpu.VMEM(full, BF16),
            pltpu.VMEM((2, half, packed, inner), BF16),
            pltpu.VMEM((half, packed, inner), BF16),
            pltpu.VMEM((2, min(early, 2), half // 2, packed, inner), BF16),
            DMA((ne + 1,)),
            DMA((2, blocks)),
            DMA,
            DMA,
            pltpu.SemaphoreType.REGULAR,
            DMA((2, 2)),
            DMA((2, early)),
        ],
        out_shape=[
            jax.ShapeDtypeStruct(full, BF16),
            jax.ShapeDtypeStruct(full, BF16),
            jax.ShapeDtypeStruct((n_exp, blocks, rows), F32),
        ]
        + [jax.ShapeDtypeStruct(part, BF16)] * 4
        + [jax.ShapeDtypeStruct(last, BF16)] * 2,
        compiler_params=pltpu.CompilerParams(
            vmem_limit_bytes=62 * 2**20,
            dimension_semantics=("arbitrary",),
            collective_id=collective,
            has_side_effects=True,
        ),
        cost_estimate=cost(75),
    )(*cots, normed, probs, w_gate, w_up, w_down)


def rms_scale(values):
    return lax.rsqrt(jnp.mean(values * values, axis=-1, keepdims=True) + EPSILON)


def partner(x):
    lane = lax.broadcasted_iota(jnp.int32, x.shape, 1)
    half = HEAD_DIM // 2
    low = lax.rem(lane, HEAD_DIM) < half
    return jnp.where(low, pltpu.roll(x, x.shape[1] - half, 1), pltpu.roll(x, half, 1))


def turn(x, cosine, sine):
    return x * cosine + partner(x) * sine


def repeated(table, rows):
    return jnp.concatenate([table] * (rows // table.shape[0]), axis=0)


def project_body(
    tokens_ref, gain_ref, tables_ref, wq_ref, wk_ref, wv_ref, n_ref, q_ref, k_ref, v_ref, *rest
):
    wq, wk, wv, sem = rest
    loads = [
        pltpu.make_async_copy(src, dst, sem.at[i])
        for i, (src, dst) in enumerate(((wk_ref, wk), (wv_ref, wv), (wq_ref, wq)))
    ]
    for copy in loads:
        copy.start()
    x = tokens_ref[...].astype(F32)
    n_ref[...] = (x * rms_scale(x) * gain_ref[...]).astype(BF16)
    normed = n_ref[...]
    cosine, sine = (repeated(tables_ref[i], x.shape[0]) for i in range(2))
    tile = 256
    for copy, (w, out, turned) in zip(
        loads, ((wk, k_ref, True), (wv, v_ref, False), (wq, q_ref, True))
    ):
        copy.wait()
        for c in range(0, w.shape[1], tile):
            y = dot(normed, w[:, c : c + tile])
            if turned:
                for i in range(0, tile, 128):
                    out[:, c + i : c + i + 128] = turn(y[:, i : i + 128], cosine, sine).astype(BF16)
            else:
                out[:, c : c + tile] = y.astype(BF16)


def project(tokens, gain, tables, w_query, w_key, w_value):
    rows, width = tokens.shape
    shapes = [width, w_query.shape[1], w_key.shape[1], w_value.shape[1]]
    return pl.pallas_call(
        project_body,
        out_shape=[jax.ShapeDtypeStruct((rows, n), BF16) for n in shapes],
        in_specs=[VMEM] * 3 + [ANY] * 3,
        out_specs=[VMEM] * 4,
        scratch_shapes=[pltpu.VMEM(w.shape, BF16) for w in (w_query, w_key, w_value)] + [DMA((3,))],
        compiler_params=pltpu.CompilerParams(vmem_limit_bytes=60 * 2**20),
        cost_estimate=cost(5),
    )(tokens, gain, tables, w_query, w_key, w_value)


def spread(x):
    lane = lax.broadcasted_iota(jnp.int32, (x.shape[0], 128), 1)
    low = lane < HEAD_DIM
    zero = jnp.zeros((), x.dtype)
    first, second = x[:, :128], x[:, 128:]
    return jnp.concatenate(
        [
            jnp.where(low, first, zero),
            jnp.where(low, pltpu.roll(first, HEAD_DIM, 1), zero),
            jnp.where(low, zero, pltpu.roll(second, HEAD_DIM, 1)),
            jnp.where(low, zero, second),
        ],
        axis=0,
    )


def gathered(x, rows):
    lane = lax.broadcasted_iota(jnp.int32, (rows, 128), 1)
    low = lane < HEAD_DIM
    h = [x[i * rows : (i + 1) * rows] for i in range(4)]
    return jnp.concatenate(
        [
            jnp.where(low, h[0], pltpu.roll(h[1], HEAD_DIM, 1)),
            jnp.where(low, pltpu.roll(h[2], HEAD_DIM, 1), h[3]),
        ],
        axis=1,
    )


def window_of(dp, span):
    return jnp.maximum(dp - (span - 1), 0)


def window_scores(dp, span, rows, starts_ref, q, k):
    keys = k.shape[0]
    scores = dot(q, k, ((1,), (1,))).reshape(4, rows, keys)
    key_pos = window_of(dp, span) * rows + lax.broadcasted_iota(jnp.int32, (rows, keys), 1)
    query_pos = dp * rows + lax.broadcasted_iota(jnp.int32, (rows, keys), 0)
    allowed = (key_pos <= query_pos) & (key_pos >= starts_ref[...])
    return jnp.where(allowed[None], scores, MASKED).reshape(4 * rows, keys)


def in_window(ref, dp, span):
    block = ref[pl.ds(window_of(dp, span), span)]
    return block.reshape(span * block.shape[1], block.shape[2])


SCALE = HEAD_DIM ** (-0.5)


class LineGather:
    def __init__(self, ep, ne, own, whole, send_sem, recv_sem):
        self.ep, self.ne, self.own, self.whole = ep, ne, own, whole
        self.send_sem, self.recv_sem = send_sem, recv_sem

    def copy(self, m, s, way):
        shard = lax.rem(self.ep - way * s + self.ne, self.ne)
        k = 0 if way == 1 else 1
        return remote(
            self.own.at[m] if s == 0 else self.whole.at[shard, m],
            self.whole.at[shard, m],
            self.send_sem.at[m, k, s],
            self.recv_sem.at[m, k, s],
            {"ep": lax.rem(self.ep + way + self.ne, self.ne)},
        )

    def sends(self, s, way):
        ep, ne = self.ep, self.ne
        return (ep >= s) & (ep < ne - 1) if way == 1 else (ep + s <= ne - 1) & (ep >= 1)

    def receives(self, s, way):
        return self.ep >= 1 + s if way == 1 else self.ep + 1 + s <= self.ne - 1

    def step(self, m, s):
        for way in (1, -1):
            if s > 0:

                @pl.when(self.receives(s - 1, way))
                def _(way=way):
                    self.copy(m, s - 1, way).wait_recv()

            if s < self.ne - 1:

                @pl.when(self.sends(s, way))
                def _(way=way):
                    self.copy(m, s, way).start()

    def wait_sends(self, m):
        for s in range(self.ne - 1):
            for way in (1, -1):

                @pl.when(self.sends(s, way))
                def _(s=s, way=way):
                    self.copy(m, s, way).wait_send()


def attend_body(span, ne, nd, micro, *refs):
    starts_ref, q_ref, k_ref, v_ref, tokens_ref, wo_ref, gain_ref, router_ref, hit_ref = refs[:9]
    out_ref, log_ref, res_ref, normed_ref, probs_ref, normed_all, marked_all = refs[9:16]
    attn, normed_own, marked_own, own_sem, send_sem, recv_sem = refs[16:]
    ep, dp = lax.axis_index("ep"), lax.axis_index("dp")
    m, h = pl.program_id(0), pl.program_id(1)
    final = pl.num_programs(1) - 1
    rows = q_ref.shape[0]
    lines = [
        LineGather(ep, ne, own, whole, send_sem.at[i], recv_sem.at[i])
        for i, (own, whole) in enumerate(((normed_own, normed_all), (marked_own, marked_all)))
    ]

    def hop(batch, s):
        for line in lines:
            line.step(batch, s)

    @pl.when((m == 0) & (h == 0))
    def _():
        greet(ep, dp, ne, nd)

    q = spread(q_ref[...].astype(F32) * SCALE).astype(BF16)
    scores = window_scores(dp, span, rows, starts_ref, q, in_window(k_ref, dp, span))
    top = jnp.max(scores, axis=1, keepdims=True)
    terms = jnp.exp(scores - top)
    total = jnp.sum(terms, axis=1, keepdims=True)
    log_ref[0, 0] = top + jnp.log(total)
    weights = (terms * (1.0 / total)).astype(BF16)
    out = gathered(dot(weights, in_window(v_ref, dp, span)), rows).astype(BF16)
    out_ref[...] = out
    attn[:, pl.ds(pl.multiple_of(h * out.shape[1], out.shape[1]), out.shape[1])] = out

    def own_copies(batch):
        return [
            pltpu.make_async_copy(line.own.at[batch], line.whole.at[ep, batch], own_sem.at[i, batch])
            for i, line in enumerate(lines)
        ]

    for batch in range(micro):

        @pl.when((m == batch) & (h == final))
        def _(batch=batch):
            for earlier in range(batch):
                hop(earlier, batch - earlier)
            residual = tokens_ref[...].astype(F32) + dot(attn[...], wo_ref[...])
            res_ref[...] = residual
            normed = (residual * rms_scale(residual) * gain_ref[...]).astype(BF16)
            normed_ref[...] = normed
            normed_own[batch] = normed
            hit = hit_ref[...] > 0.0
            logits = jnp.where(hit, dot(router_ref[...], normed, ((1,), (1,))), MASKED)
            terms = jnp.exp(logits - jnp.max(logits, axis=0, keepdims=True))
            terms = jnp.where(hit, terms, 0.0)
            probs = terms / jnp.sum(terms, axis=0, keepdims=True)
            probs_ref[...] = probs
            marked_own[batch] = jnp.where(hit, probs, -1.0)
            hop(batch, 0)
            for copy in own_copies(batch):
                copy.start()
            if batch == micro - 1:
                for t in range(1, ne + micro - 1):
                    for each in range(micro):
                        s = t + micro - 1 - each
                        if s < ne:
                            hop(each, s)
                for each in range(micro):
                    for line in lines:
                        line.wait_sends(each)
                    for copy in own_copies(each):
                        copy.wait()


def attention_specs(micro, rows, nd):
    pairs = KV_HEADS // 2
    mine = pl.BlockSpec((rows, 4 * HEAD_DIM), lambda m, h, *_: (m, h))
    theirs = pl.BlockSpec((nd, rows, 2 * HEAD_DIM), lambda m, h, *_: (0, m, h))
    column = pl.BlockSpec((rows, 1), lambda m, h, *_: (m, 0))
    logs = pl.BlockSpec((1, 1, 4 * rows, 1), lambda m, h, *_: (m, h, 0, 0))
    log_shape = jax.ShapeDtypeStruct((micro, pairs, 4 * rows, 1), F32)
    return (micro, pairs), mine, theirs, column, logs, log_shape


def attend(
    starts, queries, keys, values, tokens, w_out, gain, router, hit, micro, rows, ne, collective
):
    nd, width = keys.shape[0], tokens.shape[1]
    grid, mine, theirs, column, logs, log_shape = attention_specs(micro, rows, nd)
    one = pl.Buffered(1)
    whole = lambda v: pl.BlockSpec(v.shape, lambda m, h: (0, 0), pipeline_mode=one)
    wide = pl.BlockSpec((rows, width), lambda m, h: (m, 0))
    chosen = pl.BlockSpec((hit.shape[0], rows), lambda m, h: (0, m))
    every = micro * rows
    return pl.pallas_call(
        functools.partial(attend_body, nd // 2 + 1, ne, nd, micro),
        grid=grid,
        in_specs=[column, mine, theirs, theirs, wide, whole(w_out), whole(gain), whole(router)]
        + [chosen],
        out_specs=[mine, logs, wide, wide, chosen, ANY, ANY],
        out_shape=[
            jax.ShapeDtypeStruct(queries.shape, BF16),
            log_shape,
            jax.ShapeDtypeStruct((every, width), F32),
            jax.ShapeDtypeStruct((every, width), BF16),
            jax.ShapeDtypeStruct(hit.shape, F32),
            jax.ShapeDtypeStruct((ne, micro, rows, width), BF16),
            jax.ShapeDtypeStruct((ne, micro, hit.shape[0], rows), F32),
        ],
        scratch_shapes=[
            pltpu.VMEM((rows, width), BF16),
            pltpu.VMEM((micro, rows, width), BF16),
            pltpu.VMEM((micro, hit.shape[0], rows), F32),
            DMA((2, micro)),
            DMA((2, micro, 2, ne - 1)),
            DMA((2, micro, 2, ne - 1)),
        ],
        compiler_params=pltpu.CompilerParams(
            vmem_limit_bytes=60 * 2**20, collective_id=collective, has_side_effects=True
        ),
        cost_estimate=cost(50),
    )(starts, queries, keys, values, tokens, w_out, gain, router, hit)


def attend_back_body(span, ne, nd, orders, *refs):
    refs = list(refs)

    def take(n):
        return [refs.pop(0) for _ in range(n)]

    starts_ref, q_ref, k_ref, v_ref, log_ref, g_ref, tables_ref = take(7)
    n = len(orders)
    sources, extras = take(n), take(n)
    dq_ref, dk_ref, dv_ref = take(3)
    outs = take(n)
    held, more, landing = take(n), take(n), take(n)
    load_sem, out_sem, send_sem, recv_sem = refs
    ep, dp = lax.axis_index("ep"), lax.axis_index("dp")
    step = pl.program_id(0) * pl.num_programs(1) + pl.program_id(1)
    final = pl.num_programs(0) * pl.num_programs(1) - 1
    sums = []
    for a in range(n):
        part = pl.ds(1, sources[a].shape[1] - 1)
        loads = [
            pltpu.make_async_copy(src.at[:, part], dst, load_sem.at[a, i])
            for i, (src, dst) in enumerate(((sources[a], held[a]), (extras[a], more[a])))
        ]
        sums.append(
            PairSum(
                dp, orders[a], loads, held[a], more[a], landing[a], send_sem.at[a], recv_sem.at[a]
            )
        )
    @pl.when(step == 0)
    def _():
        for each in sums:
            each.load()
        greet(ep, dp, ne, nd)
        for each in sums:
            each.step(0)

    rows = q_ref.shape[0]
    q = spread(q_ref[...].astype(F32) * SCALE).astype(BF16)
    g = spread(g_ref[...].astype(F32)).astype(BF16)
    k, v = in_window(k_ref, dp, span), in_window(v_ref, dp, span)
    scores = window_scores(dp, span, rows, starts_ref, q, k)
    probs = jnp.exp(scores - log_ref[0, 0])
    grad_probs = dot(g, v, ((1,), (1,)))
    total = jnp.sum(probs * grad_probs, axis=1, keepdims=True)
    grad_scores = (probs * (grad_probs - total)).astype(BF16)
    dq = gathered(dot(grad_scores, k) * SCALE, rows)
    cosine, sine = tables_ref[0], -tables_ref[1]
    for i in range(0, dq.shape[1], 128):
        dq_ref[:, i : i + 128] = turn(dq[:, i : i + 128], cosine, sine).astype(BF16)
    dk_ref[...] = jnp.zeros_like(dk_ref)
    dv_ref[...] = jnp.zeros_like(dv_ref)
    here = pl.ds(window_of(dp, span), span)
    dk = dot(grad_scores, q, ((0,), (0,))).astype(BF16)
    dk_ref[here] = dk.reshape(span, rows, dk.shape[1])
    dv = dot(probs.astype(BF16), g, ((0,), (0,))).astype(BF16)
    dv_ref[here] = dv.reshape(span, rows, dv.shape[1])

    @pl.when(step == final)
    def _():
        for t in range(1, max([len(order) for order in orders] + [0]) + 1):
            for each in sums:
                each.step(t)
        copies = [
            pltpu.make_async_copy(each.own(), outs[a], out_sem.at[a]) for a, each in enumerate(sums)
        ]
        for copy in copies:
            copy.start()
        for each in sums:
            each.wait_sends()
        for copy in copies:
            copy.wait()


def attend_back(
    starts, queries, keys, values, logs_in, grad, tables, sums, micro, rows, ne, collective
):
    nd = keys.shape[0]
    grid, mine, theirs, column, logs, _ = attention_specs(micro, rows, nd)
    table = pl.BlockSpec(tables.shape, lambda m, h: (0, 0, 0))
    n = len(sums)
    shapes = [(v.shape[0], v.shape[1] - 1) + v.shape[2:] for v, _, _ in sums]
    deep = max([s[0] - 1 for s in shapes] + [1])
    some = max(n, 1)
    return pl.pallas_call(
        functools.partial(
            attend_back_body, nd // 2 + 1, ne, nd, tuple(tuple(order) for _, order, _ in sums)
        ),
        grid=grid,
        in_specs=[column, mine, theirs, theirs, logs, mine, table] + [ANY] * (2 * n),
        out_specs=[mine, theirs, theirs] + [ANY] * n,
        out_shape=[
            jax.ShapeDtypeStruct(queries.shape, BF16),
            jax.ShapeDtypeStruct(keys.shape, BF16),
            jax.ShapeDtypeStruct(values.shape, BF16),
        ]
        + [jax.ShapeDtypeStruct(s[1:], BF16) for s in shapes],
        scratch_shapes=[pltpu.VMEM(s, BF16) for s in shapes] * 2
        + [pltpu.VMEM((s[0] - 1,) + s[1:], BF16) for s in shapes]
        + [DMA((some, 2)), DMA((some,)), DMA((some, deep)), DMA((some, deep))],
        compiler_params=pltpu.CompilerParams(
            vmem_limit_bytes=60 * 2**20, collective_id=collective, has_side_effects=True
        ),
        cost_estimate=cost(25),
    )(
        starts,
        queries,
        keys,
        values,
        logs_in,
        grad,
        tables,
        *[v for v, _, _ in sums],
        *[extra for _, _, extra in sums],
    )


def finish_body(ne, nd, orders, n_out, *refs):
    refs = list(refs)

    def take(n):
        return [refs.pop(0) for _ in range(n)]

    n_ref, dq_ref, dk_ref, dv_ref, tables_ref, tokens_ref, gain_ref = take(7)
    res_ref, wq_ref, wk_ref, wv_ref, wo_ref, small_ref, mix_ref = take(7)
    (tok_out,) = take(1)
    count = 2 * n_out + 3
    outs, (mix_out,) = take(count), take(1)
    held, pair_in, line_in = take(count), take(count), take(count)
    dk_turned, wq, wk, wv, res, mix_held, mix_in = take(7)
    load_sem, own_sem, out_sem, dp_send, dp_recv, ep_send, ep_recv = refs
    ep, dp = lax.axis_index("ep"), lax.axis_index("dp")
    columns = held[0].shape[3]
    own = [
        pltpu.make_async_copy(src, dst, own_sem.at[i])
        for i, (src, dst) in enumerate(
            ((wq_ref, wq), (wk_ref, wk), (wv_ref, wv), (res_ref, res))
        )
    ]
    sums = []
    for a in range(count):
        loads = []
        if a < n_out or a == count - 1:
            src = wo_ref if a < n_out else small_ref
            at = pl.ds(a * columns if a < n_out else 0, held[a].shape[3])
            loads = [
                pltpu.make_async_copy(src.at[e, :, :, at], held[a].at[:, e], load_sem.at[a, e])
                for e in range(ne)
            ]
        sums.append(
            PairSum(
                dp, orders[a % 2], loads, held[a], None, pair_in[a], dp_send.at[a], dp_recv.at[a]
            )
        )
    lines = [
        LineSum(ep, ne, sums[a].own(), line_in[a], ep_send.at[a], ep_recv.at[a])
        for a in range(count)
    ]
    early, made, small = sums[:n_out], sums[n_out:-1], sums[-1]
    queries, others = made[:n_out], made[n_out:]
    mix = LineSum(ep, ne, mix_held, mix_in, ep_send.at[count], ep_recv.at[count])
    mix_load = pltpu.make_async_copy(
        mix_ref.at[:, pl.ds(mix_ref.shape[1] - mix_held.shape[1], mix_held.shape[1])],
        mix_held,
        own_sem.at[4],
    )
    for each in early:
        each.load()
    mix_load.start()
    for copy in own:
        copy.start()
    small.load()
    greet(ep, dp, ne, nd)
    turns = bit_count(nd)

    def steps(group, t):
        for each in group:
            if t <= turns:
                each.step(t)

    def line_steps(group, t):
        for each in group:
            if t < ne:
                lines[sums.index(each)].step(t)

    steps(early, 0)
    mix_load.wait()
    mix.step(0)

    normed = n_ref[...]
    cosine, sine = (repeated(tables_ref[i], normed.shape[0]) for i in range(2))
    sine = -sine
    for i in range(0, dk_ref.shape[1], 128):
        part = dk_ref[:, i : i + 128].astype(F32)
        dk_turned[:, i : i + 128] = turn(part, cosine, sine).astype(BF16)
    tile = 256

    def product(grad, first, each):
        share = each.held.shape[2]
        for c in range(0, each.held.shape[3], tile):
            y = dot(normed, grad[:, first + c : first + c + tile], ((0,), (0,))).astype(BF16)
            for e in range(ne):
                for d in range(nd):
                    r = (e * nd + d) * share
                    each.held[d, e, :, c : c + tile] = y[r : r + share]
        each.step(0)

    for i, each in enumerate(made):
        if i < n_out:
            product(dq_ref, i * columns, each)
        else:
            product((dk_turned, dv_ref)[i - n_out], 0, each)
        if i == 0:
            steps(early, 1)
        else:
            made[i - 1].step(1)
    for copy in own:
        copy.wait()
    back = dot(dq_ref[...], wq[...], ((1,), (1,)))
    steps(made[-1:], 1)
    mix.step(1)
    back = back + dot(dk_turned[...], wk[...], ((1,), (1,)))
    back = back + dot(dv_ref[...], wv[...], ((1,), (1,)))
    steps(early, 2)
    x = tokens_ref[...].astype(F32)
    r = rms_scale(x)
    scaled = back * gain_ref[...]
    tok_out[...] = (
        res[...] + r * scaled - x * (r * r * r) * jnp.mean(scaled * x, axis=1, keepdims=True)
    )
    term = back * x * r
    high = term.astype(BF16)
    low = (term - high.astype(F32)).astype(BF16)
    ones = jnp.ones((x.shape[0], 128), BF16)
    column = dot(high, ones, ((0,), (0,))) + dot(low, ones, ((0,), (0,)))
    lane = lax.broadcasted_iota(jnp.int32, column.shape, 1)
    column = jnp.where(lane == EXPERTS, column, 0.0)
    for copy in small.loads:
        copy.wait()
    share = held[-1].shape[2]
    for e in range(ne):
        for d in range(nd):
            i = (e * nd + d) * share
            held[-1][d, e] = (held[-1][d, e].astype(F32) + column[i : i + share]).astype(BF16)
    small.loads = []
    steps([small], 0)
    steps(queries, 2)
    steps([small], 1)
    mix.step(2)
    for t in range(3, turns + 1):
        steps(early, t)
    line_steps(early, 0)
    steps(others, 2)
    for t in range(3, turns + 1):
        steps(queries, t)
    for t in range(3, ne):
        mix.step(t)
    line_steps(early, 1)
    line_steps(queries, 0)
    steps([small], 2)
    for t in range(3, turns + 1):
        steps(others, t)
        steps([small], t)
    tail = others + [small]
    for t in range(ne):
        line_steps(early, t + 2)
        line_steps(queries, t + 1)
        line_steps(tail, t)
    order = list(range(count))
    copies = []
    for a in order:
        copies.append(pltpu.make_async_copy(lines[a].own(), outs[a], out_sem.at[a]))
        copies[-1].start()
    copies.append(pltpu.make_async_copy(mix.own(), mix_out, out_sem.at[count]))
    copies[-1].start()
    for each in sums + lines + [mix]:
        each.wait_sends()
    for copy in copies:
        copy.wait()


def finish(
    ne,
    nd,
    orders,
    normed,
    grads,
    tables,
    tokens,
    gain,
    grad_residual,
    weights,
    w_out,
    small,
    mix,
    mix_rows,
):
    rows, width = tokens.shape
    line = (ne, mix_rows, width)
    share = width // (ne * nd)
    columns = weights[1].shape[1]
    n_out = width // columns
    count = 2 * n_out + 3
    wide = [columns] * (count - 1) + [128]
    split = lambda v: v.reshape(ne, nd, share, v.shape[1])
    return pl.pallas_call(
        functools.partial(finish_body, ne, nd, tuple(map(tuple, orders)), n_out),
        out_shape=[jax.ShapeDtypeStruct((rows, width), F32)]
        + [jax.ShapeDtypeStruct((share, c), BF16) for c in wide]
        + [jax.ShapeDtypeStruct(line[1:], BF16)],
        in_specs=[VMEM] * 7 + [ANY] * 7,
        out_specs=[VMEM] + [ANY] * (count + 1),
        scratch_shapes=[pltpu.VMEM((nd, ne, share, c), BF16) for c in wide]
        + [pltpu.VMEM((nd - 1, ne, share, c), BF16) for c in wide]
        + [pltpu.VMEM((2, ne, share, c), BF16) for c in wide]
        + [pltpu.VMEM(grads[1].shape, BF16)]
        + [pltpu.VMEM(w.shape, BF16) for w in weights]
        + [pltpu.VMEM((rows, width), F32)]
        + [pltpu.VMEM(line, BF16), pltpu.VMEM((2,) + line, BF16)]
        + [
            DMA((count, ne)),
            DMA((5,)),
            DMA((count + 1,)),
            DMA((count, nd - 1)),
            DMA((count, nd - 1)),
            DMA((count + 1, 2, ne)),
            DMA((count + 1, 2, ne)),
        ],
        compiler_params=pltpu.CompilerParams(
            vmem_limit_bytes=60 * 2**20, collective_id=4, has_side_effects=True
        ),
        cost_estimate=cost(45),
    )(
        normed,
        *grads,
        tables,
        tokens,
        gain,
        grad_residual,
        *weights,
        split(w_out),
        split(small),
        mix,
    )


def results_body(share, n_out, per_path, *refs):
    refs = list(refs)

    def take(n):
        return [refs.pop(0) for _ in range(n)]

    residual_ref, mix_first, mix_rest = take(3)
    paths = [take(per_path) for _ in range(2)]
    dense = take(2 * n_out + 3)
    out_ref, d_out, d_query, d_key, d_value, router, gain_one, gain_two = take(8)
    gate, up, down = refs
    e = pl.program_id(0)

    @pl.when(e == 0)
    def _():
        rows = mix_first.shape[0]
        for i, mix in enumerate((mix_first, mix_rest)):
            at = slice(i * rows, i * rows + mix.shape[0])
            out_ref[at, :] = (residual_ref[at, :] + mix[...].astype(F32)).astype(BF16)
        width = dense[0].shape[1]
        for i in range(n_out):
            d_out[:, i * width : (i + 1) * width] = dense[i][...].astype(F32)
            d_query[:, i * width : (i + 1) * width] = dense[n_out + i][...].astype(F32)
        d_key[...] = dense[2 * n_out][...].astype(F32)
        d_value[...] = dense[2 * n_out + 1][...].astype(F32)
        small = dense[-1][...].astype(F32)
        router[...] = small[:, :EXPERTS]
        turned = small.T
        gain_one[...] = turned[EXPERTS : EXPERTS + 1]
        gain_two[...] = turned[EXPERTS + 1 : EXPERTS + 2]

    k = 0
    for n in range(per_path):
        for m in range(paths[0][n].shape[0]):
            for i in range(2):

                @pl.when(e == k)
                def _(src=paths[i][n], m=m):
                    gate[0] = src[m, :share].astype(F32)
                    up[0] = src[m, share : 2 * share].astype(F32)
                    piece, columns = down.shape[1], src.shape[2]
                    for j in range(down.shape[2] // columns):
                        at = 2 * share + j * piece
                        down[0, :, j * columns : (j + 1) * columns] = src[
                            m, at : at + piece
                        ].astype(F32)

                k += 1


def results(residual, mix, grads, dense, n_out, share, w_gate, w_down, nd, rows_share):
    rows, width = residual.shape
    n_exp, _, inner = w_gate.shape
    piece = w_down.shape[1] // nd
    ins = [residual, *mix, *grads[0], *grads[1], *dense]
    kv = dense[-2].shape[1]
    same = lambda v: pl.BlockSpec(v, lambda e: (0,) * len(v))
    outs = [
        ((rows, width), BF16),
        ((rows_share, width), F32),
        ((rows_share, width), F32),
        ((rows_share, kv), F32),
        ((rows_share, kv), F32),
        ((rows_share, EXPERTS), F32),
        ((1, rows_share), F32),
        ((1, rows_share), F32),
    ]
    experts_out = [((n_exp, share, inner), F32)] * 2 + [((n_exp, piece, width), F32)]
    return pl.pallas_call(
        functools.partial(results_body, share, n_out, len(grads[0])),
        grid=(n_exp,),
        out_shape=[jax.ShapeDtypeStruct(*v) for v in outs + experts_out],
        in_specs=[same(v.shape) for v in ins],
        out_specs=[same(v[0]) for v in outs]
        + [pl.BlockSpec((1,) + v[0][1:], lambda e: (e, 0, 0)) for v in experts_out],
        compiler_params=pltpu.CompilerParams(vmem_limit_bytes=60 * 2**20),
        cost_estimate=cost(6),
    )(*ins)


def per_device(
    tokens,
    segments,
    routes,
    first_gain,
    w_query,
    w_key,
    w_value,
    w_out,
    second_gain,
    w_router,
    w_gate,
    w_up,
    w_down,
    cotangent,
):
    micro, rows, width = tokens.shape
    ne, nd = lax.axis_size("ep"), lax.axis_size("dp")
    ep, dp = lax.axis_index("ep"), lax.axis_index("dp")
    groups = HEADS // KV_HEADS
    kv_width = KV_HEADS * HEAD_DIM
    every = micro * rows
    inputs = tokens.reshape(every, width).astype(F32)
    grad_output = cotangent.reshape(every, width).astype(F32)

    halfway = HEAD_DIM // 2
    frequency = ROPE_BASE ** (-(np.arange(halfway) * 2.0 / HEAD_DIM))
    angles = np.arange(nd * rows)[:, None] * frequency[None, :]
    lanes = 2 * HEAD_DIM // halfway
    sign = np.where(np.arange(2 * HEAD_DIM) % HEAD_DIM < halfway, -1.0, 1.0)
    tables = np.stack([np.tile(np.cos(angles), lanes), np.tile(np.sin(angles), lanes) * sign])
    tables = lax.dynamic_slice_in_dim(jnp.asarray(tables, F32), dp * rows, rows, axis=1)

    tokens_flat = tokens.reshape(every, width)
    gain_one = first_gain.reshape(1, width)
    normed_one, query_rot, key_rot, value_own = project(
        tokens_flat, gain_one, tables, w_query, w_key, w_value
    )

    ids = jnp.arange(128, dtype=jnp.int32)
    counts = jnp.sum((segments[:, 0, :, None] == ids).astype(F32), axis=1)
    counts = jnp.concatenate([counts, jnp.zeros((8 - micro, 128), F32)], axis=0)

    cot_own = cotangent.reshape(every, width)

    def around(value, k):
        return lax.ppermute(value, "ep", [(i, (i + k) % ne) for i in range(ne)])

    cots = [cot_own] + [around(cot_own, k) for k in range(1, ne)]
    key_all, value_all, count_all = gather(ne, nd, (key_rot, value_own, counts), (), 0, 25)

    totals = jnp.sum(count_all[:, :micro], axis=0)
    lower = (ids[None, None, :] < segments[:, 0, :, None]).astype(F32)
    starts = jnp.sum(lower * totals[:, None, :], axis=2).astype(jnp.int32)
    starts = starts.reshape(every, 1)
    routing = routes.reshape(every, routes.shape[2])
    hit = jnp.any(
        jnp.arange(EXPERTS, dtype=jnp.int32)[:, None, None] == routing[None], axis=2
    ).astype(F32)
    attn_low, logs, residual, normed_two, gate_probs, normed_all, marked_all = attend(
        starts,
        query_rot,
        key_all,
        value_all,
        tokens_flat,
        w_out,
        second_gain.reshape(1, width),
        w_router.T,
        hit,
        micro,
        rows,
        ne,
        1,
    )
    inv_two = rms_scale(residual)
    here = EXPERTS // ne
    probs_here = lax.dynamic_slice_in_dim(marked_all, ep * here, here, axis=2)
    probs_here = probs_here.reshape(ne * micro, here, rows)
    nb = bit_count(nd)
    orders = [order[:-1][::-1] for order in gather_orders(nd)]
    mix, grad_in, pair_dots, *grads = experts(
        normed_all.reshape(ne * every, width),
        cots,
        probs_here,
        w_gate,
        w_up,
        w_down,
        micro,
        rows,
        ne,
        nd,
        6,
    )
    kept, landed, last = grads[:2], grads[2:4], grads[4:]
    pair_dots = pair_dots.reshape(here, ne, every).transpose(1, 0, 2)
    head = (slice(None), slice(0, 1))
    *grads, grad_back, dots_all = reduce(
        ne,
        nd,
        [(last[i], orders[i], None, None, False) for i in range(2)]
        + [(kept[i], orders[i][1:], head, landed[i], False) for i in range(2)],
        ((grad_in.reshape(ne, every, width), None),),
        (pair_dots,),
        2,
        40,
    )
    grads_last, grads_head = grads[:2], grads[2:]
    pair_dot = dots_all.reshape(EXPERTS, every)
    grad_logits = gate_probs * (
        pair_dot - jnp.sum(gate_probs * pair_dot, axis=0, keepdims=True)
    )
    grad_w_router = jnp.einsum(
        "td,et->de", normed_two.astype(F32), grad_logits, precision=HIGHEST
    )
    grad_normed_two = (
        jnp.einsum("et,de->td", grad_logits, w_router.astype(F32), precision=HIGHEST)
        + grad_back.astype(F32)
    )
    scaled_two = grad_normed_two * second_gain
    grad_gain_two = jnp.sum(grad_normed_two * residual * inv_two, axis=0)
    grad_residual = (
        grad_output
        + inv_two * scaled_two
        - residual * inv_two**3 * jnp.mean(scaled_two * residual, axis=-1, keepdims=True)
    )
    residual_low = grad_residual.astype(BF16)
    grad_w_out = jnp.einsum("tf,td->fd", attn_low, residual_low, preferred_element_type=F32)
    grad_attn = jnp.einsum("td,fd->tf", residual_low, w_out, preferred_element_type=F32).astype(
        BF16
    )
    more = kept[0].shape[1] > 1
    mix = mix.reshape(ne, every, width)
    grad_query, grad_key_all, grad_value_all, *grads_more = attend_back(
        starts,
        query_rot,
        key_all,
        value_all,
        logs,
        grad_attn,
        tables,
        [(kept[i], orders[i][1:], landed[i]) for i in range(2)] if more else [],
        micro,
        rows,
        ne,
        5,
    )
    full = [[0] + order for order in orders]
    grad_key, grad_value, mix_first = reduce(
        ne,
        nd,
        [
            (grad_key_all, full[0], None, None, False),
            (grad_value_all, full[1], None, None, False),
        ],
        ((mix, (slice(None), slice(0, rows))),),
        (),
        3,
        30,
    )
    small = jnp.concatenate(
        [
            grad_w_router,
            jnp.zeros((width, 1), F32),
            grad_gain_two[:, None],
            jnp.zeros((width, 128 - EXPERTS - 2), F32),
        ],
        axis=1,
    ).astype(BF16)
    grad_tokens, *dense, mix_rest = finish(
        ne,
        nd,
        full,
        normed_one,
        (grad_query, grad_key, grad_value),
        tables,
        tokens_flat,
        gain_one,
        grad_residual,
        (w_query, w_key, w_value),
        grad_w_out.astype(BF16),
        small,
        mix,
        every - rows,
    )
    (
        output,
        d_out,
        d_query,
        d_key,
        d_value,
        d_router,
        d_gain_one,
        d_gain_two,
        d_gate,
        d_up,
        d_down,
    ) = results(
        residual,
        (mix_first, mix_rest),
        [
            [grads_head[i]] + ([grads_more[i]] if more else []) + [grads_last[i][None]]
            for i in range(2)
        ],
        dense,
        width // kv_width,
        width // nd,
        w_gate,
        w_down,
        nd,
        width // (ne * nd),
    )
    return (
        output.reshape(tokens.shape),
        grad_tokens.reshape(tokens.shape),
        d_gain_one.reshape(-1),
        d_query,
        d_key,
        d_value,
        d_out,
        d_gain_two.reshape(-1),
        d_router,
        d_gate,
        d_up,
        d_down,
    )


def solution(mesh):
    in_specs = (
        P(None, ("ep", "dp"), None),
        P(None, "ep", "dp"),
        P(None, ("ep", "dp"), None),
        P(),
        P(),
        P(),
        P(),
        P(),
        P(),
        P(),
        P("ep", None, None),
        P("ep", None, None),
        P("ep", None, None),
        P(None, ("ep", "dp"), None),
    )
    out_specs = (
        P(None, ("ep", "dp"), None),
        P(None, ("ep", "dp"), None),
        P(("ep", "dp")),
        P(("ep", "dp"), None),
        P(("ep", "dp"), None),
        P(("ep", "dp"), None),
        P(("ep", "dp"), None),
        P(("ep", "dp")),
        P(("ep", "dp"), None),
        P("ep", "dp", None),
        P("ep", "dp", None),
        P("ep", "dp", None),
    )
    return jax.shard_map(
        per_device, mesh=mesh, in_specs=in_specs, out_specs=out_specs, check_vma=False
    )
```

```python
import functools

import jax
import jax.numpy as jnp
import numpy as np
from jax import lax
from jax.experimental import pallas as pl
from jax.experimental.pallas import tpu as pltpu
from jax.sharding import PartitionSpec as P

HEADS = 16
KV_HEADS = 8
HEAD_DIM = 64
EXPERTS = 32
CAP = 64
EPSILON = 1e-06
ROPE_BASE = 10000.0
MASKED = -1e30
HIGHEST = lax.Precision.HIGHEST
MESH = pl.DeviceIdType.MESH
BF16 = jnp.bfloat16
F32 = jnp.float32
VMEM = pl.BlockSpec(memory_space=pltpu.VMEM)
ANY = pl.BlockSpec(memory_space=pl.ANY)
DMA = pltpu.SemaphoreType.DMA


def bit_count(n):
    return n.bit_length() - 1


def masks(bits):
    out = [0]
    for b in bits:
        out = out + [m | (1 << b) for m in out]
    return out


def gather_orders(n):
    bits = list(range(bit_count(n)))
    return (bits[1:] + bits[:1], bits[:0:-1] + bits[:1])


def greet(ep, dp, ne, nd):
    barrier = pltpu.get_barrier_semaphore()
    for k in range(1, ne):
        pl.semaphore_signal(
            barrier, inc=1, device_id={"ep": lax.rem(ep + k, ne)}, device_id_type=MESH
        )
    for b in range(bit_count(nd)):
        pl.semaphore_signal(
            barrier, inc=1, device_id={"dp": jnp.bitwise_xor(dp, 1 << b)}, device_id_type=MESH
        )
    pl.semaphore_wait(barrier, ne - 1 + bit_count(nd))


def remote(src, dst, send, recv, where):
    return pltpu.make_async_remote_copy(
        src_ref=src, dst_ref=dst, send_sem=send, recv_sem=recv, device_id=where, device_id_type=MESH
    )


def gather_body(ne, nd, n_dp, n_ep, *refs):
    n_in = n_dp + n_ep
    ins, outs, sems = refs[:n_in], refs[n_in : 2 * n_in], refs[2 * n_in :]
    ep, dp = lax.axis_index("ep"), lax.axis_index("dp")
    own_sem, dp_send, dp_recv, ep_send, ep_recv = sems
    greet(ep, dp, ne, nd)
    own = []
    for a in range(n_in):
        me = dp if a < n_dp else ep
        copy = pltpu.make_async_copy(ins[a], outs[a].at[me], own_sem.at[a])
        copy.start()
        own.append(copy)

    def dp_copy(a, t, m):
        order = gather_orders(nd)[a % 2]
        block = jnp.bitwise_xor(dp, m)
        k = (1 << t) - 1 + masks(order[:t]).index(m)
        return remote(
            ins[a] if m == 0 else outs[a].at[block],
            outs[a].at[block],
            dp_send.at[a, k],
            dp_recv.at[a, k],
            {"dp": jnp.bitwise_xor(dp, 1 << order[t])},
        )

    def ep_copy(a, s, way):
        shard = lax.rem(ep - way * s + ne, ne)
        src = ins[n_dp + a] if s == 0 else outs[n_dp + a].at[shard]
        k = 0 if way == 1 else 1
        return remote(
            src,
            outs[n_dp + a].at[shard],
            ep_send.at[a, k, s],
            ep_recv.at[a, k, s],
            {"ep": lax.rem(ep + way + ne, ne)},
        )

    def sends(s, way):
        if way == 1:
            return (ep >= s) & (ep < ne - 1)
        return (ep + s <= ne - 1) & (ep >= 1)

    def receives(s, way):
        if way == 1:
            return ep >= 1 + s
        return ep + 1 + s <= ne - 1

    def ep_start(s):
        for a in range(n_ep):
            for way in (1, -1):

                @pl.when(sends(s, way))
                def _(a=a, way=way):
                    ep_copy(a, s, way).start()

    def ep_wait(s):
        for a in range(n_ep):
            for way in (1, -1):

                @pl.when(receives(s, way))
                def _(a=a, way=way):
                    ep_copy(a, s, way).wait_recv()

    dp_steps = bit_count(nd) if n_dp else 0
    ep_steps = ne - 1 if n_ep else 0
    for t in range(dp_steps):
        for a in range(n_dp):
            dp_copy(a, t, 0).start()
    for t in range(max(dp_steps, ep_steps) + 1):
        if 0 < t <= dp_steps:
            for a in range(n_dp):
                order = gather_orders(nd)[a % 2]
                for m in masks(order[: t - 1]):
                    dp_copy(a, t - 1, m).wait_recv()
                    for later in range(t, dp_steps):
                        dp_copy(a, later, m | (1 << order[t - 1])).start()
        if 0 < t <= ep_steps:
            ep_wait(t - 1)
        if t < ep_steps:
            ep_start(t)
    for t in range(dp_steps):
        for a in range(n_dp):
            for m in masks(gather_orders(nd)[a % 2][:t]):
                dp_copy(a, t, m).wait_send()
    for s in range(ep_steps):
        for a in range(n_ep):
            for way in (1, -1):

                @pl.when(sends(s, way))
                def _(a=a, s=s, way=way):
                    ep_copy(a, s, way).wait_send()

    for c in own:
        c.wait()


def cost(us):
    return pl.CostEstimate(flops=0, bytes_accessed=int(us * 3.0e6), transcendentals=0)


def gather(ne, nd, dp_arrays, ep_arrays, collective, us):
    arrays = list(dp_arrays) + list(ep_arrays)
    counts = [nd] * len(dp_arrays) + [ne] * len(ep_arrays)
    a, b = max(len(dp_arrays), 1), max(len(ep_arrays), 1)
    return pl.pallas_call(
        functools.partial(gather_body, ne, nd, len(dp_arrays), len(ep_arrays)),
        out_shape=[
            jax.ShapeDtypeStruct((n,) + v.shape, v.dtype) for n, v in zip(counts, arrays)
        ],
        in_specs=[ANY] * len(arrays),
        out_specs=[ANY] * len(arrays),
        scratch_shapes=[
            DMA((len(arrays),)),
            DMA((a, nd - 1)),
            DMA((a, nd - 1)),
            DMA((b, 2, ne - 1)),
            DMA((b, 2, ne - 1)),
        ],
        compiler_params=pltpu.CompilerParams(
            collective_id=collective, has_side_effects=True, vmem_limit_bytes=60 * 2**20
        ),
        cost_estimate=cost(us),
    )(*arrays)


def add_into(ref, arrived):
    if len(ref.shape) > 2:

        @pl.loop(0, ref.shape[0])
        def _(i):
            add_into(ref.at[i], arrived.at[i])

    else:
        ref[...] = (ref[...].astype(F32) + arrived[...].astype(F32)).astype(ref.dtype)


class PairSum:
    def __init__(self, dp, order, loads, held, extra, landing, send_sem, recv_sem):
        self.dp, self.order, self.held, self.landing = dp, order, held, landing
        self.send_sem, self.recv_sem = send_sem, recv_sem
        self.extra, self.loads = extra, loads
        self.index = 0
        for b in order:
            side = jnp.bitwise_and(lax.shift_right_logical(dp, b), 1)
            self.index = self.index + (side << self.place(b))

    def place(self, bit):
        return sorted(self.order).index(bit)

    def copies(self, t):
        order = self.order
        partner = jnp.bitwise_xor(self.index, 1 << self.place(order[t]))
        first = sum(1 << (len(order) - 1 - i) for i in range(t))
        return [
            (
                m,
                first + j,
                remote(
                    self.held.at[jnp.bitwise_xor(partner, m)],
                    self.landing.at[first + j],
                    self.send_sem.at[first + j],
                    self.recv_sem.at[first + j],
                    {"dp": jnp.bitwise_xor(self.dp, 1 << order[t])},
                ),
            )
            for j, m in enumerate(masks([self.place(b) for b in order[t + 1 :]]))
        ]

    def load(self):
        for copy in self.loads:
            copy.start()

    def step(self, t):
        if t == 0:
            for copy in self.loads:
                copy.wait()
            if self.extra is not None:
                add_into(self.held, self.extra)
        elif t <= len(self.order):
            for m, k, copy in self.copies(t - 1):
                copy.wait_recv()
                add_into(self.held.at[jnp.bitwise_xor(self.index, m)], self.landing.at[k])
        if t < len(self.order):
            for m, k, copy in self.copies(t):
                copy.start()

    def own(self):
        return self.held.at[self.index]

    def wait_sends(self):
        for t in range(len(self.order)):
            for m, k, copy in self.copies(t):
                copy.wait_send()


class LineSum:
    def __init__(self, ep, ne, blocks, landing, send_sem, recv_sem):
        self.ep, self.ne, self.blocks, self.landing = ep, ne, blocks, landing
        self.send_sem, self.recv_sem = send_sem, recv_sem

    def copy(self, dest, way):
        k = 0 if way == 1 else 1
        return remote(
            self.blocks.at[dest],
            self.landing.at[k, dest],
            self.send_sem.at[k, dest],
            self.recv_sem.at[k, dest],
            {"ep": lax.rem(self.ep + way + self.ne, self.ne)},
        )

    def turn(self, t, way):
        ep, ne = self.ep, self.ne
        dest = ep + ne - 1 - t if way == 1 else ep + t - (ne - 1)
        has = dest <= ne - 1 if way == 1 else dest >= 0
        inner = ep >= 1 if way == 1 else ep <= ne - 2
        return dest, has, inner

    def step(self, t):
        for way in (1, -1):
            dest, has, inner = self.turn(t, way)

            @pl.when(has & inner)
            def _(way=way, dest=dest):
                self.copy(dest, way).wait_recv()
                add_into(self.blocks.at[dest], self.landing.at[0 if way == 1 else 1, dest])

            if t < self.ne - 1:

                @pl.when(has)
                def _(way=way, dest=dest):
                    self.copy(dest, way).start()

    def own(self):
        return self.blocks.at[self.ep]

    def wait_sends(self):
        for t in range(self.ne - 1):
            for way in (1, -1):
                dest, has, inner = self.turn(t, way)

                @pl.when(has)
                def _(way=way, dest=dest):
                    self.copy(dest, way).wait_send()


def shape_at(array, where):
    return tuple(len(range(*w.indices(n))) for w, n in zip(where, array.shape)) + array.shape[len(where) :]


def reduce_body(ne, nd, pairs, line_parts, n_swap, *refs):
    refs = list(refs)

    def take(n):
        return [refs.pop(0) for _ in range(n)]

    n_pair, n_line = len(pairs), len(line_parts)
    n_extra = sum(p[2] for p in pairs)
    n_both = sum(p[3] for p in pairs)
    n_sum = n_pair + n_line
    ins, extra_ins, swap_ins = take(n_sum), take(n_extra), take(n_swap)
    outs, swap_outs = take(n_sum), take(n_swap)
    held, extras, pair_in = take(n_sum), take(n_extra), take(n_pair)
    both_in, line_in = take(n_both), take(n_line)
    load_sem, out_sem, dp_send, dp_recv, ep_send, ep_recv, swap_send, swap_recv = refs
    ep, dp = lax.axis_index("ep"), lax.axis_index("dp")
    sums, then = [], []
    for a, (order, where, has_extra, both) in enumerate(pairs):
        targets = [(ins[a], held[a])]
        extra = extras.pop(0) if has_extra else None
        if has_extra:
            targets.append((extra_ins.pop(0), extra))
        loads = [
            pltpu.make_async_copy(src.at[where] if where else src, dst, load_sem.at[a, i])
            for i, (src, dst) in enumerate(targets)
        ]
        sums.append(
            PairSum(dp, order, loads, held[a], extra, pair_in[a], dp_send.at[a], dp_recv.at[a])
        )
        if both:
            i = len(then)
            then.append(
                LineSum(ep, ne, sums[a].own(), both_in[i], ep_send.at[i], ep_recv.at[i])
            )
    lines, line_loads = [], []
    for i in range(n_line):
        a = n_pair + i
        src = ins[a].at[line_parts[i]] if line_parts[i] else ins[a]
        line_loads.append(pltpu.make_async_copy(src, held[a], load_sem.at[a, 0]))
        lines.append(
            LineSum(
                ep, ne, held[a], line_in[i], ep_send.at[n_both + i], ep_recv.at[n_both + i]
            )
        )
    for copy in line_loads:
        copy.start()
    for each in sums:
        each.load()
    greet(ep, dp, ne, nd)
    swaps = []
    for a in range(n_swap):
        src, dst = swap_ins[a], swap_outs[a]
        own = pltpu.make_async_copy(src.at[ep], dst.at[ep], load_sem.at[n_sum + a, 0])
        own.start()
        swaps.append(own)
        for k in range(1, ne):
            to = lax.rem(ep + k, ne)
            copy = remote(
                src.at[to], dst.at[ep], swap_send.at[a, k - 1], swap_recv.at[a, k - 1], {"ep": to}
            )
            copy.start()
            swaps.append(copy)
    for copy in line_loads:
        copy.wait()
    steps = max([len(p[0]) + 1 for p in pairs] + [ne if n_line else 0])
    for t in range(steps):
        if t < ne:
            for each in lines:
                each.step(t)
        for each in sums:
            each.step(t)
    for t in range(ne):
        for each in then:
            each.step(t)
    results, after = [], iter(then)
    for a in range(n_sum):
        if a >= n_pair:
            src = lines[a - n_pair].own()
        else:
            src = next(after).own() if pairs[a][3] else sums[a].own()
        copy = pltpu.make_async_copy(src, outs[a], out_sem.at[a])
        copy.start()
        results.append(copy)
    for each in sums + then + lines:
        each.wait_sends()
    for copy in swaps + results:
        copy.wait()


def reduce(ne, nd, pairs, lines, swaps, collective, us):
    line_parts = tuple(where for _, where in lines)
    line_shapes = [shape_at(v, where) if where else v.shape for v, where in lines]
    lines = [v for v, _ in lines]
    arrays = [p[0] for p in pairs] + list(lines)
    extras = [p[3] for p in pairs if p[3] is not None]
    kinds = tuple((tuple(p[1]), p[2], p[3] is not None, p[4]) for p in pairs)
    shapes = [shape_at(p[0], p[2]) if p[2] else p[0].shape for p in pairs]
    boths = [s for s, p in zip(shapes, pairs) if p[4]]
    results = [s[2:] if p[4] else s[1:] for s, p in zip(shapes, pairs)]
    results += [s[1:] for s in line_shapes]
    scratch = shapes + line_shapes
    scratch += [s for s, p in zip(shapes, pairs) if p[3] is not None]
    scratch += [(s[0] - 1,) + s[1:] for s in shapes]
    scratch += [(2,) + s[1:] for s in boths] + [(2,) + s for s in line_shapes]
    some = lambda n: max(n, 1)
    line_count = some(len(lines) + len(boths))
    deep = max([s[0] - 1 for s in shapes] + [1])
    return pl.pallas_call(
        functools.partial(reduce_body, ne, nd, kinds, line_parts, len(swaps)),
        out_shape=[jax.ShapeDtypeStruct(s, BF16) for s in results]
        + [jax.ShapeDtypeStruct(v.shape, v.dtype) for v in swaps],
        in_specs=[ANY] * (len(arrays) + len(extras) + len(swaps)),
        out_specs=[ANY] * (len(arrays) + len(swaps)),
        scratch_shapes=[pltpu.VMEM(s, BF16) for s in scratch]
        + [
            DMA((len(arrays) + len(swaps), 2)),
            DMA((len(arrays),)),
            DMA((some(len(pairs)), deep)),
            DMA((some(len(pairs)), deep)),
            DMA((line_count, 2, ne)),
            DMA((line_count, 2, ne)),
            DMA((some(len(swaps)), ne - 1)),
            DMA((some(len(swaps)), ne - 1)),
        ],
        compiler_params=pltpu.CompilerParams(
            collective_id=collective, has_side_effects=True, vmem_limit_bytes=60 * 2**20
        ),
        cost_estimate=cost(us),
    )(*arrays, *extras, *swaps)


def dot(a, b, dims=((1,), (0,))):
    return lax.dot_general(a, b, (dims, ((), ())), preferred_element_type=F32)


def expert_body(ne, nd, micro, rows, *refs):
    cots, refs = refs[:ne], refs[ne:]
    normed_ref, probs_ref, gate_ref, up_ref, down_ref = refs[:5]
    mix_ref, grad_ref, dots_ref = refs[5:8]
    kept, landed, whole = refs[8:10], refs[10:12], refs[12:14]
    rows_in, cots_in, picks, first, second, chances, sides, arrived, leaving = refs[14:23]
    load_sem, store_sem, send_sem, recv_sem, free_sem, far_send, far_recv = refs[23:]
    e = pl.program_id(0)
    last = pl.num_programs(0) - 1
    ep, dp = lax.axis_index("ep"), lax.axis_index("dp")
    other = {"dp": jnp.bitwise_xor(dp, 1)}
    every = micro * rows
    blocks = ne * micro
    width = first.shape[1]
    n_exp = rows_in.shape[1]

    core = jnp.bitwise_and(dp, 1)
    keep, send = sides.at[core], sides.at[1 - core]

    def exchange():
        return remote(send, arrived, send_sem, recv_sem, other)

    def loads():
        out = [
            pltpu.make_async_copy(normed_ref, first, load_sem.at[ne]),
            pltpu.make_async_copy(
                probs_ref.at[:, pl.ds(pl.multiple_of(ep * n_exp, n_exp), n_exp)],
                chances,
                load_sem.at[ne + 1],
            ),
        ]
        for k in range(ne):
            at = pl.multiple_of(lax.rem(ep - k + ne, ne) * every, every)
            out.append(
                pltpu.make_async_copy(cots[k], second.at[pl.ds(at, every)], load_sem.at[k])
            )
        return out

    def block_at(s):
        return pl.ds(pl.multiple_of(s * rows, rows), rows)

    def returned(t):
        k, m = t // micro, lax.rem(t, micro)
        return lax.rem(ep + k, ne) * micro + m

    def stores(t):
        s = returned(t)
        return (
            pltpu.make_async_copy(
                first.at[block_at(s)], mix_ref.at[block_at(s)], store_sem.at[0, t]
            ),
            pltpu.make_async_copy(
                second.at[block_at(s)], grad_ref.at[block_at(s)], store_sem.at[1, t]
            ),
        )

    def far(i, n):
        return remote(
            leaving.at[i, lax.rem(n, leaving.shape[1])],
            landed[i].at[:, n],
            far_send.at[i, lax.rem(n, leaving.shape[1])],
            far_recv.at[i, n],
            {"dp": jnp.bitwise_xor(dp, 1 << first_bits(nd)[i])},
        )

    def last_copy(k):
        return pltpu.make_async_copy(keep, whole[k], load_sem.at[k])

    def collect():
        exchange().wait_recv()
        pieces, height, slots = sides.shape[1], leaving.shape[3], leaving.shape[1]
        n = e - 1
        early = n_exp - 2

        @pl.when(n < early)
        def _():
            @pl.when(n >= slots)
            def _():
                for i in range(2):
                    far(i, n - slots).wait_send()

            def piece(i, at, other_side):
                bit = first_bits(nd)[i]
                mine = jnp.bitwise_and(lax.shift_right_logical(dp, bit), 1)
                side = 1 - mine if other_side else mine
                low = (1 << (bit - 1)) - 1
                j = ((at & ~low) << 1 | (at & low)) + (side << (bit - 1))
                part = slice(i * height, (i + 1) * height)
                return (keep[j, part].astype(F32) + arrived[j, part].astype(F32)).astype(BF16)

            for i in range(2):
                for at in range(pieces // 2):
                    leaving[i, lax.rem(n, slots), at] = piece(i, at, True)
                far(i, n).start()
            for i in range(2):
                for at in range(pieces // 2):
                    kept[i][at, 0] = piece(i, at, False)

        for k in range(2):

            @pl.when(n == early + k)
            def _(k=k):
                add_into(keep, arrived)
                last_copy(k).start()

    @pl.when(e == 0)
    def _():
        for copy in loads():
            copy.start()
        barrier = pltpu.get_barrier_semaphore()
        met = [0] + sorted(set(first_bits(nd)))
        for bit in met:
            pl.semaphore_signal(
                barrier,
                inc=1,
                device_id={"dp": jnp.bitwise_xor(dp, 1 << bit)},
                device_id_type=MESH,
            )
        pl.semaphore_wait(barrier, len(met))
        before = lax.broadcasted_iota(jnp.int32, (rows, rows), 0)
        after = lax.broadcasted_iota(jnp.int32, (rows, rows), 1)
        earlier = (before < after).astype(BF16)
        slot = lax.broadcasted_iota(jnp.int32, (n_exp, CAP, rows), 1)
        for copy in loads():
            copy.wait()

        @pl.loop(0, blocks)
        def _(s):
            at = block_at(s)
            probs = chances[s]
            hit = probs >= 0.0
            rank = dot(hit.astype(BF16), earlier)
            rank = jnp.where(hit, rank, -1.0).astype(jnp.int32)
            pick = jnp.broadcast_to(rank[:, None, :], (n_exp, CAP, rows)) == slot
            pick_f = pick.astype(F32)
            flat = pick_f.reshape(n_exp * CAP, rows).astype(BF16)
            picks[s] = flat
            rows_in[s] = dot(flat, first[at, :]).astype(BF16).reshape(n_exp, CAP, width)
            cots_in[s] = dot(flat, second[at, :]).astype(BF16).reshape(n_exp, CAP, width)

    @pl.when(e < last)
    def _():
        x = rows_in[:, e].reshape(blocks * CAP, width)
        c = cots_in[:, e].reshape(blocks * CAP, width)
        flat = picks[:, pl.ds(pl.multiple_of(e * CAP, CAP), CAP), :].astype(F32)
        p = jnp.sum(flat * chances[:, pl.ds(e, 1), :], axis=2, keepdims=True)
        p = p.reshape(blocks * CAP, 1)
        w_gate, w_up, w_down = gate_ref[0], up_ref[0], down_ref[0]
        gate_pre = dot(x, w_gate)
        up_pre = dot(x, w_up)
        back = dot(c, w_down, ((1,), (1,)))

        @pl.when(e > 0)
        def _():
            collect()
            pl.semaphore_signal(free_sem, inc=1, device_id=other, device_id_type=MESH)

        sigma = jax.nn.sigmoid(gate_pre)
        silu = gate_pre * sigma
        hidden = (silu * up_pre).astype(BF16)
        out = dot(hidden, w_down) * p
        wide = hidden.astype(F32)
        pair = jnp.sum(wide * back, axis=1, keepdims=True)
        back = back * p
        grad_up = (back * silu).astype(BF16)
        grad_gate = (back * up_pre * (sigma * (1.0 + gate_pre * (1.0 - sigma)))).astype(BF16)
        scaled = (wide * p).astype(BF16)
        grad_x = dot(grad_gate, w_gate, ((1,), (1,))) + dot(grad_up, w_up, ((1,), (1,)))
        pair = jnp.sum(flat * pair.reshape(blocks, CAP, 1), axis=1)
        dots_ref[:, 0] = pair.reshape(ne, micro, rows)

        @pl.when(e > 0)
        def _():
            exchange().wait_send()
            pl.semaphore_wait(free_sem, 1)

        @pl.when(e == n_exp - 1)
        def _():
            last_copy(0).wait()

        def split(value, offset):
            value = value.astype(BF16)
            piece, columns = value.shape[0] // nd, sides.shape[3]

            for i in range(nd):
                for j in range(value.shape[1] // columns):
                    at = offset + j * piece
                    sides[i % 2, i // 2, at : at + piece] = value[
                        i * piece : (i + 1) * piece, j * columns : (j + 1) * columns
                    ]

        share = width // nd
        split(dot(scaled, c, ((0,), (0,))), 2 * share)
        split(dot(x, grad_gate, ((0,), (0,))), 0)
        split(dot(x, grad_up, ((0,), (0,))), share)
        exchange().start()

        rows_in[:, e] = grad_x.astype(BF16).reshape(blocks, CAP, width)
        cots_in[:, e] = out.astype(BF16).reshape(blocks, CAP, width)

    @pl.when(e == last)
    def _():
        @pl.loop(0, blocks)
        def _(t):
            s = returned(t)
            at = block_at(s)
            flat = picks[s]
            for done, slots in ((first, cots_in), (second, rows_in)):
                value = dot(flat, slots[s].reshape(n_exp * CAP, width), ((0,), (0,)))
                done[at, :] = value.astype(BF16)
            for copy in stores(t):
                copy.start()

            @pl.when(t == 1)
            def _():
                collect()
                exchange().wait_send()

        @pl.loop(0, blocks)
        def _(t):
            for copy in stores(t):
                copy.wait()

        last_copy(1).wait()
        early, slots = n_exp - 2, leaving.shape[1]
        for i in range(2):
            for n in range(max(early - slots, 0), early):
                far(i, n).wait_send()

            @pl.loop(0, early)
            def _(n, i=i):
                far(i, n).wait_recv()


def first_bits(nd):
    return [order[-2] for order in gather_orders(nd)]


def experts(normed, cots, probs, w_gate, w_up, w_down, micro, rows, ne, nd, collective):
    n_exp, width, inner = w_gate.shape
    blocks = ne * micro
    half = nd // 2
    packed = 2 * width // nd + (inner // nd) * (width // inner)
    full = (blocks * rows, width)
    weight = lambda e: (jnp.minimum(e, n_exp - 1), 0, 0)
    early = n_exp - 2
    part = (half // 2, early, packed // 2, inner)
    kept = pl.BlockSpec(
        (half // 2, 1, packed // 2, inner), lambda e: (0, jnp.clip(e - 1, 0, early - 1), 0, 0)
    )
    last = (half, packed, inner)
    return pl.pallas_call(
        functools.partial(expert_body, ne, nd, micro, rows),
        grid=(n_exp + 1,),
        in_specs=[ANY] * (ne + 2)
        + [
            pl.BlockSpec((1, width, inner), weight),
            pl.BlockSpec((1, width, inner), weight),
            pl.BlockSpec((1, inner, width), weight),
        ],
        out_specs=[
            ANY,
            ANY,
            pl.BlockSpec((ne, 1, micro, rows), lambda e: (0, jnp.minimum(e, n_exp - 1), 0, 0)),
            kept,
            kept,
            ANY,
            ANY,
            ANY,
            ANY,
        ],
        scratch_shapes=[
            pltpu.VMEM((blocks, n_exp, CAP, width), BF16),
            pltpu.VMEM((blocks, n_exp, CAP, width), BF16),
            pltpu.VMEM((blocks, n_exp * CAP, rows), BF16),
            pltpu.VMEM(full, BF16),
            pltpu.VMEM(full, BF16),
            pltpu.VMEM((blocks, n_exp, rows), F32),
            pltpu.VMEM((2, half, packed, inner), BF16),
            pltpu.VMEM((half, packed, inner), BF16),
            pltpu.VMEM((2, 2 if early > 2 else 1, half // 2, packed // 2, inner), BF16),
            DMA((ne + 2,)),
            DMA((2, blocks)),
            DMA,
            DMA,
            pltpu.SemaphoreType.REGULAR,
            DMA((2, 2)),
            DMA((2, early)),
        ],
        out_shape=[
            jax.ShapeDtypeStruct(full, BF16),
            jax.ShapeDtypeStruct(full, BF16),
            jax.ShapeDtypeStruct((ne, n_exp, micro, rows), F32),
        ]
        + [jax.ShapeDtypeStruct(part, BF16)] * 4
        + [jax.ShapeDtypeStruct(last, BF16)] * 2,
        compiler_params=pltpu.CompilerParams(
            vmem_limit_bytes=63 * 2**20,
            dimension_semantics=("arbitrary",),
            collective_id=collective,
            has_side_effects=True,
        ),
        cost_estimate=cost(75),
    )(*cots, normed, probs, w_gate, w_up, w_down)


def rms_scale(values):
    return lax.rsqrt(jnp.mean(values * values, axis=-1, keepdims=True) + EPSILON)


def partner(x):
    lane = lax.broadcasted_iota(jnp.int32, x.shape, 1)
    half = HEAD_DIM // 2
    low = lax.rem(lane, HEAD_DIM) < half
    return jnp.where(low, pltpu.roll(x, x.shape[1] - half, 1), pltpu.roll(x, half, 1))


def turn(x, cosine, sine):
    return x * cosine + partner(x) * sine


def repeated(table, rows):
    return jnp.concatenate([table] * (rows // table.shape[0]), axis=0)


def project_body(
    tokens_ref, gain_ref, tables_ref, wq_ref, wk_ref, wv_ref, n_ref, q_ref, k_ref, v_ref, *rest
):
    wq, wk, wv, sem = rest
    loads = [
        pltpu.make_async_copy(src, dst, sem.at[i])
        for i, (src, dst) in enumerate(((wk_ref, wk), (wv_ref, wv), (wq_ref, wq)))
    ]
    for copy in loads:
        copy.start()
    x = tokens_ref[...].astype(F32)
    n_ref[...] = (x * rms_scale(x) * gain_ref[...]).astype(BF16)
    normed = n_ref[...]
    cosine, sine = (repeated(tables_ref[i], x.shape[0]) for i in range(2))
    tile = 256
    for copy, (w, out, turned) in zip(
        loads, ((wk, k_ref, True), (wv, v_ref, False), (wq, q_ref, True))
    ):
        copy.wait()
        for c in range(0, w.shape[1], tile):
            y = dot(normed, w[:, c : c + tile])
            if turned:
                for i in range(0, tile, 128):
                    out[:, c + i : c + i + 128] = turn(y[:, i : i + 128], cosine, sine).astype(BF16)
            else:
                out[:, c : c + tile] = y.astype(BF16)


def project(tokens, gain, tables, w_query, w_key, w_value):
    rows, width = tokens.shape
    shapes = [width, w_query.shape[1], w_key.shape[1], w_value.shape[1]]
    return pl.pallas_call(
        project_body,
        out_shape=[jax.ShapeDtypeStruct((rows, n), BF16) for n in shapes],
        in_specs=[VMEM] * 3 + [ANY] * 3,
        out_specs=[VMEM] * 4,
        scratch_shapes=[pltpu.VMEM(w.shape, BF16) for w in (w_query, w_key, w_value)] + [DMA((3,))],
        compiler_params=pltpu.CompilerParams(vmem_limit_bytes=60 * 2**20),
        cost_estimate=cost(5),
    )(tokens, gain, tables, w_query, w_key, w_value)


def spread(x):
    lane = lax.broadcasted_iota(jnp.int32, (x.shape[0], 128), 1)
    low = lane < HEAD_DIM
    zero = jnp.zeros((), x.dtype)
    first, second = x[:, :128], x[:, 128:]
    return jnp.concatenate(
        [
            jnp.where(low, first, zero),
            jnp.where(low, pltpu.roll(first, HEAD_DIM, 1), zero),
            jnp.where(low, zero, pltpu.roll(second, HEAD_DIM, 1)),
            jnp.where(low, zero, second),
        ],
        axis=0,
    )


def gathered(x, rows):
    lane = lax.broadcasted_iota(jnp.int32, (rows, 128), 1)
    low = lane < HEAD_DIM
    h = [x[i * rows : (i + 1) * rows] for i in range(4)]
    return jnp.concatenate(
        [
            jnp.where(low, h[0], pltpu.roll(h[1], HEAD_DIM, 1)),
            jnp.where(low, pltpu.roll(h[2], HEAD_DIM, 1), h[3]),
        ],
        axis=1,
    )


def window_of(dp, span):
    return jnp.maximum(dp - (span - 1), 0)


def window_scores(dp, span, rows, starts_ref, q, k):
    keys = k.shape[0]
    scores = dot(q, k, ((1,), (1,))).reshape(4, rows, keys)
    key_pos = window_of(dp, span) * rows + lax.broadcasted_iota(jnp.int32, (rows, keys), 1)
    query_pos = dp * rows + lax.broadcasted_iota(jnp.int32, (rows, keys), 0)
    allowed = (key_pos <= query_pos) & (key_pos >= starts_ref[...])
    return jnp.where(allowed[None], scores, MASKED).reshape(4 * rows, keys)


def in_window(ref, dp, span):
    block = ref[pl.ds(window_of(dp, span), span)]
    return block.reshape(span * block.shape[1], block.shape[2])


SCALE = HEAD_DIM ** (-0.5)


class LineGather:
    def __init__(self, ep, ne, own, whole, send_sem, recv_sem):
        self.ep, self.ne, self.own, self.whole = ep, ne, own, whole
        self.send_sem, self.recv_sem = send_sem, recv_sem

    def copy(self, m, s, way):
        shard = lax.rem(self.ep - way * s + self.ne, self.ne)
        k = 0 if way == 1 else 1
        return remote(
            self.own.at[m] if s == 0 else self.whole.at[shard, m],
            self.whole.at[shard, m],
            self.send_sem.at[m, k, s],
            self.recv_sem.at[m, k, s],
            {"ep": lax.rem(self.ep + way + self.ne, self.ne)},
        )

    def sends(self, s, way):
        ep, ne = self.ep, self.ne
        return (ep >= s) & (ep < ne - 1) if way == 1 else (ep + s <= ne - 1) & (ep >= 1)

    def receives(self, s, way):
        return self.ep >= 1 + s if way == 1 else self.ep + 1 + s <= self.ne - 1

    def step(self, m, s):
        for way in (1, -1):
            if s > 0:

                @pl.when(self.receives(s - 1, way))
                def _(way=way):
                    self.copy(m, s - 1, way).wait_recv()

            if s < self.ne - 1:

                @pl.when(self.sends(s, way))
                def _(way=way):
                    self.copy(m, s, way).start()

    def wait_sends(self, m):
        for s in range(self.ne - 1):
            for way in (1, -1):

                @pl.when(self.sends(s, way))
                def _(s=s, way=way):
                    self.copy(m, s, way).wait_send()


def attend_body(span, ne, nd, micro, *refs):
    starts_ref, q_ref, k_ref, v_ref, tokens_ref, wo_ref, gain_ref, router_ref, hit_ref = refs[:9]
    out_ref, log_ref, res_ref, normed_ref, probs_ref, normed_all, marked_all = refs[9:16]
    attn, normed_own, marked_own, own_sem, send_sem, recv_sem = refs[16:]
    ep, dp = lax.axis_index("ep"), lax.axis_index("dp")
    m, h = pl.program_id(0), pl.program_id(1)
    final = pl.num_programs(1) - 1
    rows = q_ref.shape[0]
    lines = [
        LineGather(ep, ne, own, whole, send_sem.at[i], recv_sem.at[i])
        for i, (own, whole) in enumerate(((normed_own, normed_all), (marked_own, marked_all)))
    ]

    def hop(batch, s):
        for line in lines:
            line.step(batch, s)

    @pl.when((m == 0) & (h == 0))
    def _():
        greet(ep, dp, ne, nd)

    q = spread(q_ref[...].astype(F32) * SCALE).astype(BF16)
    scores = window_scores(dp, span, rows, starts_ref, q, in_window(k_ref, dp, span))
    top = jnp.max(scores, axis=1, keepdims=True)
    terms = jnp.exp(scores - top)
    total = jnp.sum(terms, axis=1, keepdims=True)
    log_ref[0, 0] = top + jnp.log(total)
    weights = (terms * (1.0 / total)).astype(BF16)
    out = gathered(dot(weights, in_window(v_ref, dp, span)), rows).astype(BF16)
    out_ref[...] = out
    attn[:, pl.ds(pl.multiple_of(h * out.shape[1], out.shape[1]), out.shape[1])] = out

    def own_copies(batch):
        return [
            pltpu.make_async_copy(line.own.at[batch], line.whole.at[ep, batch], own_sem.at[i, batch])
            for i, line in enumerate(lines)
        ]

    for batch in range(micro):

        @pl.when((m == batch) & (h == final))
        def _(batch=batch):
            for earlier in range(batch):
                hop(earlier, batch - earlier)
            residual = tokens_ref[...].astype(F32) + dot(attn[...], wo_ref[...])
            res_ref[...] = residual
            normed = (residual * rms_scale(residual) * gain_ref[...]).astype(BF16)
            normed_ref[...] = normed
            normed_own[batch] = normed
            hit = hit_ref[...] > 0.0
            logits = jnp.where(hit, dot(router_ref[...], normed, ((1,), (1,))), MASKED)
            terms = jnp.exp(logits - jnp.max(logits, axis=0, keepdims=True))
            terms = jnp.where(hit, terms, 0.0)
            probs = terms / jnp.sum(terms, axis=0, keepdims=True)
            probs_ref[...] = probs
            marked_own[batch] = jnp.where(hit, probs, -1.0)
            hop(batch, 0)
            for copy in own_copies(batch):
                copy.start()
            if batch == micro - 1:
                for t in range(1, ne + micro - 1):
                    for each in range(micro):
                        s = t + micro - 1 - each
                        if s < ne:
                            hop(each, s)
                for each in range(micro):
                    for line in lines:
                        line.wait_sends(each)
                    for copy in own_copies(each):
                        copy.wait()


def attention_specs(micro, rows, nd):
    pairs = KV_HEADS // 2
    mine = pl.BlockSpec((rows, 4 * HEAD_DIM), lambda m, h, *_: (m, h))
    theirs = pl.BlockSpec((nd, rows, 2 * HEAD_DIM), lambda m, h, *_: (0, m, h))
    column = pl.BlockSpec((rows, 1), lambda m, h, *_: (m, 0))
    logs = pl.BlockSpec((1, 1, 4 * rows, 1), lambda m, h, *_: (m, h, 0, 0))
    log_shape = jax.ShapeDtypeStruct((micro, pairs, 4 * rows, 1), F32)
    return (micro, pairs), mine, theirs, column, logs, log_shape


def attend(
    starts, queries, keys, values, tokens, w_out, gain, router, hit, micro, rows, ne, collective
):
    nd, width = keys.shape[0], tokens.shape[1]
    grid, mine, theirs, column, logs, log_shape = attention_specs(micro, rows, nd)
    one = pl.Buffered(1)
    whole = lambda v: pl.BlockSpec(v.shape, lambda m, h: (0, 0), pipeline_mode=one)
    wide = pl.BlockSpec((rows, width), lambda m, h: (m, 0))
    chosen = pl.BlockSpec((hit.shape[0], rows), lambda m, h: (0, m))
    every = micro * rows
    return pl.pallas_call(
        functools.partial(attend_body, nd // 2 + 1, ne, nd, micro),
        grid=grid,
        in_specs=[column, mine, theirs, theirs, wide, whole(w_out), whole(gain), whole(router)]
        + [chosen],
        out_specs=[mine, logs, wide, wide, chosen, ANY, ANY],
        out_shape=[
            jax.ShapeDtypeStruct(queries.shape, BF16),
            log_shape,
            jax.ShapeDtypeStruct((every, width), F32),
            jax.ShapeDtypeStruct((every, width), BF16),
            jax.ShapeDtypeStruct(hit.shape, F32),
            jax.ShapeDtypeStruct((ne, micro, rows, width), BF16),
            jax.ShapeDtypeStruct((ne, micro, hit.shape[0], rows), F32),
        ],
        scratch_shapes=[
            pltpu.VMEM((rows, width), BF16),
            pltpu.VMEM((micro, rows, width), BF16),
            pltpu.VMEM((micro, hit.shape[0], rows), F32),
            DMA((2, micro)),
            DMA((2, micro, 2, ne - 1)),
            DMA((2, micro, 2, ne - 1)),
        ],
        compiler_params=pltpu.CompilerParams(
            vmem_limit_bytes=60 * 2**20, collective_id=collective, has_side_effects=True
        ),
        cost_estimate=cost(50),
    )(starts, queries, keys, values, tokens, w_out, gain, router, hit)


def attend_back_body(span, ne, nd, micro, skip, orders, *refs):
    refs = list(refs)

    def take(n):
        return [refs.pop(0) for _ in range(n)]

    starts_ref, q_ref, k_ref, v_ref, log_ref, tables_ref = take(6)
    cot_ref, dots_ref, probs_ref, grad_ref, residual_ref, gain_ref, normed_ref, attn_ref = take(8)
    wo_ref, router_ref = take(2)
    n = len(orders)
    sources, extras = take(n), take(n)
    dq_ref, dk_ref, dv_ref, res_out, wo_out, router_out, gain_out = take(7)
    outs = take(n)
    (grads,) = take(1)
    held, more, landing = take(n), take(n), take(n)
    load_sem, out_sem, send_sem, recv_sem = refs
    ep, dp = lax.axis_index("ep"), lax.axis_index("dp")
    step = pl.program_id(0) * pl.num_programs(1) + pl.program_id(1)
    final = pl.num_programs(0) * pl.num_programs(1) - 1
    sums = []
    for a in range(n):
        part = pl.ds(skip, sources[a].shape[1] - skip)
        loads = [
            pltpu.make_async_copy(src.at[:, part], dst, load_sem.at[a, i])
            for i, (src, dst) in enumerate(((sources[a], held[a]), (extras[a], more[a])))
        ]
        sums.append(
            PairSum(
                dp, orders[a], loads, held[a], more[a], landing[a], send_sem.at[a], recv_sem.at[a]
            )
        )
    @pl.when(step == 0)
    def _():
        for each in sums:
            each.load()
        greet(ep, dp, ne, nd)
        for each in sums:
            each.step(0)
        rows = q_ref.shape[0]
        pairs = [dots_ref[:, :, m, :].reshape(-1, rows) for m in range(micro)]
        pair = jnp.concatenate(pairs, axis=1)
        probs = probs_ref[...]
        grad_logits = probs * (pair - jnp.sum(probs * pair, axis=0, keepdims=True))
        high = grad_logits.astype(BF16)
        low = (grad_logits - high.astype(F32)).astype(BF16)
        normed = normed_ref[...]
        router_out[...] = dot(high, normed) + dot(low, normed)
        router = router_ref[...]
        grad_normed = (
            grad_ref[...].astype(F32)
            + dot(high, router, ((0,), (0,)))
            + dot(low, router, ((0,), (0,)))
        )
        residual = residual_ref[...]
        r = rms_scale(residual)
        gain_out[...] = jnp.sum(grad_normed * residual * r, axis=0, keepdims=True)
        scaled = grad_normed * gain_ref[...]
        mean = jnp.mean(scaled * residual, axis=1, keepdims=True)
        grad_residual = cot_ref[...].astype(F32) + r * scaled - residual * (r * r * r) * mean
        res_out[...] = grad_residual
        low_res = grad_residual.astype(BF16)
        tile = 256
        for c in range(0, wo_out.shape[1], tile):
            wo_out[:, c : c + tile] = dot(
                attn_ref[...], low_res[:, c : c + tile], ((0,), (0,))
            ).astype(BF16)
        for c in range(0, wo_ref.shape[0], tile):
            grads[c // tile] = dot(low_res, wo_ref[c : c + tile, :], ((1,), (1,))).astype(BF16)

    rows = q_ref.shape[0]
    q = spread(q_ref[...].astype(F32) * SCALE).astype(BF16)
    mine = pl.ds(pl.multiple_of(pl.program_id(0) * rows, rows), rows)
    g = spread(grads[pl.program_id(1), mine, :].astype(F32)).astype(BF16)
    k, v = in_window(k_ref, dp, span), in_window(v_ref, dp, span)
    scores = window_scores(dp, span, rows, starts_ref, q, k)
    probs = jnp.exp(scores - log_ref[0, 0])
    grad_probs = dot(g, v, ((1,), (1,)))
    total = jnp.sum(probs * grad_probs, axis=1, keepdims=True)
    grad_scores = (probs * (grad_probs - total)).astype(BF16)
    dq = gathered(dot(grad_scores, k) * SCALE, rows)
    cosine, sine = tables_ref[0], -tables_ref[1]
    for i in range(0, dq.shape[1], 128):
        dq_ref[:, i : i + 128] = turn(dq[:, i : i + 128], cosine, sine).astype(BF16)
    dk_ref[...] = jnp.zeros_like(dk_ref)
    dv_ref[...] = jnp.zeros_like(dv_ref)
    here = pl.ds(window_of(dp, span), span)
    dk = dot(grad_scores, q, ((0,), (0,))).astype(BF16)
    dk_ref[here] = dk.reshape(span, rows, dk.shape[1])
    dv = dot(probs.astype(BF16), g, ((0,), (0,))).astype(BF16)
    dv_ref[here] = dv.reshape(span, rows, dv.shape[1])

    @pl.when(step == final)
    def _():
        for t in range(1, max([len(order) for order in orders] + [0]) + 1):
            for each in sums:
                each.step(t)
        copies = [
            pltpu.make_async_copy(each.own(), outs[a], out_sem.at[a]) for a, each in enumerate(sums)
        ]
        for copy in copies:
            copy.start()
        for each in sums:
            each.wait_sends()
        for copy in copies:
            copy.wait()


def attend_back(
    starts,
    queries,
    keys,
    values,
    logs_in,
    tables,
    cot,
    dots,
    probs,
    grad_normed,
    residual,
    gain,
    normed,
    attn,
    w_out,
    router,
    sums,
    skip,
    collective,
):
    nd, ne, micro, rows = keys.shape[0], dots.shape[0], dots.shape[2], dots.shape[3]
    every, width = residual.shape
    grid, mine, theirs, column, logs, _ = attention_specs(micro, rows, nd)
    one = pl.Buffered(1)
    whole = lambda v: pl.BlockSpec(v.shape, lambda m, h: (0,) * len(v.shape), pipeline_mode=one)
    n = len(sums)
    shapes = [(v.shape[0], v.shape[1] - skip) + v.shape[2:] for v, _, _ in sums]
    deep = max([s[0] - 1 for s in shapes] + [1])
    some = max(n, 1)
    before = [cot, dots, probs, grad_normed, residual, gain, normed, attn, w_out, router]
    after = [
        jax.ShapeDtypeStruct((every, width), F32),
        jax.ShapeDtypeStruct(w_out.shape, BF16),
        jax.ShapeDtypeStruct(router.shape, F32),
        jax.ShapeDtypeStruct((1, width), F32),
    ]
    tile = 4 * HEAD_DIM
    return pl.pallas_call(
        functools.partial(
            attend_back_body,
            nd // 2 + 1,
            ne,
            nd,
            micro,
            skip,
            tuple(tuple(order) for _, order, _ in sums),
        ),
        grid=grid,
        in_specs=[column, mine, theirs, theirs, logs, whole(tables)]
        + [whole(v) for v in before]
        + [ANY] * (2 * n),
        out_specs=[mine, theirs, theirs] + [whole(v) for v in after] + [ANY] * n,
        out_shape=[
            jax.ShapeDtypeStruct(queries.shape, BF16),
            jax.ShapeDtypeStruct(keys.shape, BF16),
            jax.ShapeDtypeStruct(values.shape, BF16),
        ]
        + after
        + [jax.ShapeDtypeStruct(s[1:], BF16) for s in shapes],
        scratch_shapes=[pltpu.VMEM((w_out.shape[0] // tile, every, tile), BF16)]
        + [pltpu.VMEM(s, BF16) for s in shapes] * 2
        + [pltpu.VMEM((s[0] - 1,) + s[1:], BF16) for s in shapes]
        + [DMA((some, 2)), DMA((some,)), DMA((some, deep)), DMA((some, deep))],
        compiler_params=pltpu.CompilerParams(
            vmem_limit_bytes=60 * 2**20, collective_id=collective, has_side_effects=True
        ),
        cost_estimate=cost(28),
    )(
        starts,
        queries,
        keys,
        values,
        logs_in,
        tables,
        *before,
        *[v for v, _, _ in sums],
        *[extra for _, _, extra in sums],
    )


def finish_body(ne, nd, orders, n_out, *refs):
    refs = list(refs)

    def take(n):
        return [refs.pop(0) for _ in range(n)]

    n_ref, dq_ref, dk_ref, dv_ref, tables_ref, tokens_ref, gain_ref, router_ref, gain_two = take(9)
    res_ref, wq_ref, wk_ref, wv_ref, wo_ref, mix_ref = take(6)
    (tok_out,) = take(1)
    count = 2 * n_out + 3
    outs, (mix_out,) = take(count), take(1)
    held, pair_in, line_in = take(count), take(count), take(count)
    dk_turned, wq, wk, wv, res, mix_held, mix_in = take(7)
    load_sem, own_sem, out_sem, dp_send, dp_recv, ep_send, ep_recv = refs
    ep, dp = lax.axis_index("ep"), lax.axis_index("dp")
    columns = held[0].shape[3]
    own = [
        pltpu.make_async_copy(src, dst, own_sem.at[i])
        for i, (src, dst) in enumerate(
            ((wq_ref, wq), (wk_ref, wk), (wv_ref, wv), (res_ref, res))
        )
    ]
    sums = []
    for a in range(count):
        loads = []
        if a < n_out:
            at = pl.ds(a * columns, columns)
            loads = [
                pltpu.make_async_copy(wo_ref.at[e, :, :, at], held[a].at[:, e], load_sem.at[a, e])
                for e in range(ne)
            ]
        sums.append(
            PairSum(
                dp, orders[a % 2], loads, held[a], None, pair_in[a], dp_send.at[a], dp_recv.at[a]
            )
        )
    lines = [
        LineSum(ep, ne, sums[a].own(), line_in[a], ep_send.at[a], ep_recv.at[a])
        for a in range(count)
    ]
    early, made, small = sums[:n_out], sums[n_out:-1], sums[-1]
    queries, others = made[:n_out], made[n_out:]
    mix = LineSum(ep, ne, mix_held, mix_in, ep_send.at[count], ep_recv.at[count])
    mix_load = pltpu.make_async_copy(
        mix_ref.at[:, pl.ds(mix_ref.shape[1] - mix_held.shape[1], mix_held.shape[1])],
        mix_held,
        own_sem.at[4],
    )
    for each in early:
        each.load()
    mix_load.start()
    for copy in own:
        copy.start()
    greet(ep, dp, ne, nd)
    turns = bit_count(nd)

    def steps(group, t):
        for each in group:
            if t <= turns:
                each.step(t)

    def line_steps(group, t):
        for each in group:
            if t < ne:
                lines[sums.index(each)].step(t)

    steps(early, 0)
    mix_load.wait()
    mix.step(0)

    normed = n_ref[...]
    cosine, sine = (repeated(tables_ref[i], normed.shape[0]) for i in range(2))
    sine = -sine
    for i in range(0, dk_ref.shape[1], 128):
        part = dk_ref[:, i : i + 128].astype(F32)
        dk_turned[:, i : i + 128] = turn(part, cosine, sine).astype(BF16)
    tile = 256

    def product(grad, first, each):
        share = each.held.shape[2]
        for c in range(0, each.held.shape[3], tile):
            y = dot(normed, grad[:, first + c : first + c + tile], ((0,), (0,))).astype(BF16)
            for e in range(ne):
                for d in range(nd):
                    r = (e * nd + d) * share
                    each.held[d, e, :, c : c + tile] = y[r : r + share]
        each.step(0)

    for i, each in enumerate(made):
        if i < n_out:
            product(dq_ref, i * columns, each)
        else:
            product((dk_turned, dv_ref)[i - n_out], 0, each)
        if i == 0:
            steps(early, 1)
        else:
            made[i - 1].step(1)
    for copy in own:
        copy.wait()
    back = dot(dq_ref[...], wq[...], ((1,), (1,)))
    steps(made[-1:], 1)
    mix.step(1)
    back = back + dot(dk_turned[...], wk[...], ((1,), (1,)))
    back = back + dot(dv_ref[...], wv[...], ((1,), (1,)))
    steps(early, 2)
    x = tokens_ref[...].astype(F32)
    r = rms_scale(x)
    scaled = back * gain_ref[...]
    tok_out[...] = (
        res[...] + r * scaled - x * (r * r * r) * jnp.mean(scaled * x, axis=1, keepdims=True)
    )
    one_row = jnp.sum(back * x * r, axis=0, keepdims=True)
    blank = jnp.zeros((held[-1].shape[3] - EXPERTS - 2, x.shape[1]), F32)
    column = jnp.concatenate([router_ref[...], one_row, gain_two[...], blank], axis=0).T
    share = held[-1].shape[2]
    for e in range(ne):
        for d in range(nd):
            i = (e * nd + d) * share
            held[-1][d, e] = column[i : i + share].astype(BF16)
    steps([small], 0)
    steps(queries, 2)
    steps([small], 1)
    mix.step(2)
    for t in range(3, turns + 1):
        steps(early, t)
    line_steps(early, 0)
    steps(others, 2)
    for t in range(3, turns + 1):
        steps(queries, t)
    for t in range(3, ne):
        mix.step(t)
    line_steps(early, 1)
    line_steps(queries, 0)
    steps([small], 2)
    for t in range(3, turns + 1):
        steps(others, t)
        steps([small], t)
    tail = others + [small]
    for t in range(ne):
        line_steps(early, t + 2)
        line_steps(queries, t + 1)
        line_steps(tail, t)
    order = list(range(count))
    copies = []
    for a in order:
        copies.append(pltpu.make_async_copy(lines[a].own(), outs[a], out_sem.at[a]))
        copies[-1].start()
    copies.append(pltpu.make_async_copy(mix.own(), mix_out, out_sem.at[count]))
    copies[-1].start()
    for each in sums + lines + [mix]:
        each.wait_sends()
    for copy in copies:
        copy.wait()


def finish(
    ne,
    nd,
    orders,
    normed,
    grads,
    tables,
    tokens,
    gain,
    grad_residual,
    weights,
    w_out,
    router_grad,
    gain_two_grad,
    mix,
    mix_rows,
):
    rows, width = tokens.shape
    line = (ne, mix_rows, width)
    share = width // (ne * nd)
    columns = weights[1].shape[1]
    n_out = width // columns
    count = 2 * n_out + 3
    wide = [columns] * (count - 1) + [128]
    split = lambda v: v.reshape(ne, nd, share, v.shape[1])
    return pl.pallas_call(
        functools.partial(finish_body, ne, nd, tuple(map(tuple, orders)), n_out),
        out_shape=[jax.ShapeDtypeStruct((rows, width), F32)]
        + [jax.ShapeDtypeStruct((share, c), BF16) for c in wide]
        + [jax.ShapeDtypeStruct(line[1:], BF16)],
        in_specs=[VMEM] * 9 + [ANY] * 6,
        out_specs=[VMEM] + [ANY] * (count + 1),
        scratch_shapes=[pltpu.VMEM((nd, ne, share, c), BF16) for c in wide]
        + [pltpu.VMEM((nd - 1, ne, share, c), BF16) for c in wide]
        + [pltpu.VMEM((2, ne, share, c), BF16) for c in wide]
        + [pltpu.VMEM(grads[1].shape, BF16)]
        + [pltpu.VMEM(w.shape, BF16) for w in weights]
        + [pltpu.VMEM((rows, width), F32)]
        + [pltpu.VMEM(line, BF16), pltpu.VMEM((2,) + line, BF16)]
        + [
            DMA((count, ne)),
            DMA((5,)),
            DMA((count + 1,)),
            DMA((count, nd - 1)),
            DMA((count, nd - 1)),
            DMA((count + 1, 2, ne)),
            DMA((count + 1, 2, ne)),
        ],
        compiler_params=pltpu.CompilerParams(
            vmem_limit_bytes=60 * 2**20, collective_id=4, has_side_effects=True
        ),
        cost_estimate=cost(45),
    )(
        normed,
        *grads,
        tables,
        tokens,
        gain,
        router_grad,
        gain_two_grad,
        grad_residual,
        *weights,
        split(w_out),
        mix,
    )


def results_body(share, n_out, groups, *refs):
    refs = list(refs)

    def take(n):
        return [refs.pop(0) for _ in range(n)]

    residual_ref, mix_first, mix_rest = take(3)
    halves = [take(groups) for _ in range(2)]
    dense = take(2 * n_out + 3)
    out_ref, d_out, d_query, d_key, d_value, router, gain_one, gain_two = take(8)
    gate, up, down = refs
    e = pl.program_id(0)

    @pl.when(e == 0)
    def _():
        rows = mix_first.shape[0]
        for i, mix in enumerate((mix_first, mix_rest)):
            at = slice(i * rows, i * rows + mix.shape[0])
            out_ref[at, :] = (residual_ref[at, :] + mix[...].astype(F32)).astype(BF16)
        width = dense[0].shape[1]
        for i in range(n_out):
            d_out[:, i * width : (i + 1) * width] = dense[i][...].astype(F32)
            d_query[:, i * width : (i + 1) * width] = dense[n_out + i][...].astype(F32)
        d_key[...] = dense[2 * n_out][...].astype(F32)
        d_value[...] = dense[2 * n_out + 1][...].astype(F32)
        small = dense[-1][...].astype(F32)
        router[...] = small[:, :EXPERTS]
        turned = small.T
        gain_one[...] = turned[EXPERTS : EXPERTS + 1]
        gain_two[...] = turned[EXPERTS + 1 : EXPERTS + 2]

    k = 0
    for first, second in zip(*halves):
        for m in range(first.shape[0]):

            @pl.when(e == k)
            def _(first=first, second=second, m=m):
                over = first.shape[1] - share
                gate[0] = first[m, :share].astype(F32)
                up[0, :over] = first[m, share:].astype(F32)
                up[0, over:] = second[m, : share - over].astype(F32)
                piece, columns = down.shape[1], second.shape[2]
                for j in range(down.shape[2] // columns):
                    at = share - over + j * piece
                    down[0, :, j * columns : (j + 1) * columns] = second[
                        m, at : at + piece
                    ].astype(F32)

            k += 1


def results(residual, mix, grads, dense, n_out, share, w_gate, w_down, nd, rows_share):
    rows, width = residual.shape
    n_exp, _, inner = w_gate.shape
    piece = w_down.shape[1] // nd
    ins = [residual, *mix, *grads[0], *grads[1], *dense]
    kv = dense[-2].shape[1]
    same = lambda v: pl.BlockSpec(v, lambda e: (0,) * len(v))
    outs = [
        ((rows, width), BF16),
        ((rows_share, width), F32),
        ((rows_share, width), F32),
        ((rows_share, kv), F32),
        ((rows_share, kv), F32),
        ((rows_share, EXPERTS), F32),
        ((1, rows_share), F32),
        ((1, rows_share), F32),
    ]
    experts_out = [((n_exp, share, inner), F32)] * 2 + [((n_exp, piece, width), F32)]
    return pl.pallas_call(
        functools.partial(results_body, share, n_out, len(grads[0])),
        grid=(n_exp,),
        out_shape=[jax.ShapeDtypeStruct(*v) for v in outs + experts_out],
        in_specs=[same(v.shape) for v in ins],
        out_specs=[same(v[0]) for v in outs]
        + [pl.BlockSpec((1,) + v[0][1:], lambda e: (e, 0, 0)) for v in experts_out],
        compiler_params=pltpu.CompilerParams(vmem_limit_bytes=60 * 2**20),
        cost_estimate=cost(6),
    )(*ins)


def per_device(
    tokens,
    segments,
    routes,
    first_gain,
    w_query,
    w_key,
    w_value,
    w_out,
    second_gain,
    w_router,
    w_gate,
    w_up,
    w_down,
    cotangent,
):
    micro, rows, width = tokens.shape
    ne, nd = lax.axis_size("ep"), lax.axis_size("dp")
    dp = lax.axis_index("dp")
    kv_width = KV_HEADS * HEAD_DIM
    every = micro * rows

    halfway = HEAD_DIM // 2
    frequency = ROPE_BASE ** (-(np.arange(halfway) * 2.0 / HEAD_DIM))
    angles = np.arange(nd * rows)[:, None] * frequency[None, :]
    lanes = 2 * HEAD_DIM // halfway
    sign = np.where(np.arange(2 * HEAD_DIM) % HEAD_DIM < halfway, -1.0, 1.0)
    tables = np.stack([np.tile(np.cos(angles), lanes), np.tile(np.sin(angles), lanes) * sign])
    tables = lax.dynamic_slice_in_dim(jnp.asarray(tables, F32), dp * rows, rows, axis=1)

    tokens_flat = tokens.reshape(every, width)
    gain_one = first_gain.reshape(1, width)
    normed_one, query_rot, key_rot, value_own = project(
        tokens_flat, gain_one, tables, w_query, w_key, w_value
    )

    ids = jnp.arange(128, dtype=jnp.int32)
    counts = jnp.sum((segments[:, 0, :, None] == ids).astype(F32), axis=1)
    counts = jnp.concatenate([counts, jnp.zeros((8 - micro, 128), F32)], axis=0)

    cot_own = cotangent.reshape(every, width)

    def around(value, k):
        return lax.ppermute(value, "ep", [(i, (i + k) % ne) for i in range(ne)])

    cots = [cot_own] + [around(cot_own, k) for k in range(1, ne)]
    key_all, value_all, count_all = gather(ne, nd, (key_rot, value_own, counts), (), 0, 25)

    totals = jnp.sum(count_all[:, :micro], axis=0)
    lower = (ids[None, None, :] < segments[:, 0, :, None]).astype(F32)
    starts = jnp.sum(lower * totals[:, None, :], axis=2).astype(jnp.int32)
    starts = starts.reshape(every, 1)
    routing = routes.reshape(every, routes.shape[2])
    hit = jnp.any(
        jnp.arange(EXPERTS, dtype=jnp.int32)[:, None, None] == routing[None], axis=2
    ).astype(F32)
    router = w_router.T
    attn_low, logs, residual, normed_two, gate_probs, normed_all, marked_all = attend(
        starts,
        query_rot,
        key_all,
        value_all,
        tokens_flat,
        w_out,
        second_gain.reshape(1, width),
        router,
        hit,
        micro,
        rows,
        ne,
        1,
    )
    orders = [order[:-1][::-1] for order in gather_orders(nd)]
    mix, grad_in, pair_dots, *grads = experts(
        normed_all.reshape(ne * every, width),
        cots,
        marked_all.reshape(ne * micro, EXPERTS, rows),
        w_gate,
        w_up,
        w_down,
        micro,
        rows,
        ne,
        nd,
        6,
    )
    kept, landed, last = grads[:2], grads[2:4], grads[4:]
    height = kept[0].shape[2]
    halves = [(slice(None), slice(i * height, (i + 1) * height)) for i in range(2)]
    skip = min(2, kept[0].shape[1])
    more = kept[0].shape[1] > skip
    head = (slice(None), slice(0, skip))
    *grads, grad_back, dots_all = reduce(
        ne,
        nd,
        [(last[k], orders[i], halves[i], None, False) for k in range(2) for i in range(2)]
        + [(kept[i], orders[i][1:], head, landed[i], False) for i in range(2)],
        ((grad_in.reshape(ne, every, width), None),),
        (pair_dots,),
        2,
        40,
    )
    grads_last, grads_head = grads[:4], grads[4:]
    mix = mix.reshape(ne, every, width)
    (
        grad_query,
        grad_key_all,
        grad_value_all,
        grad_residual,
        grad_w_out,
        grad_router,
        grad_gain_two,
        *grads_more,
    ) = attend_back(
        starts,
        query_rot,
        key_all,
        value_all,
        logs,
        tables,
        cot_own,
        dots_all,
        gate_probs,
        grad_back,
        residual,
        second_gain.reshape(1, width),
        normed_two,
        attn_low,
        w_out,
        router,
        [(kept[i], orders[i][1:], landed[i]) for i in range(2)] if more else [],
        skip,
        5,
    )
    full = [[0] + order for order in orders]
    grad_key, grad_value, mix_first = reduce(
        ne,
        nd,
        [
            (grad_key_all, full[0], None, None, False),
            (grad_value_all, full[1], None, None, False),
        ],
        ((mix, (slice(None), slice(0, rows))),),
        (),
        3,
        30,
    )
    grad_tokens, *dense, mix_rest = finish(
        ne,
        nd,
        full,
        normed_one,
        (grad_query, grad_key, grad_value),
        tables,
        tokens_flat,
        gain_one,
        grad_residual,
        (w_query, w_key, w_value),
        grad_w_out,
        grad_router,
        grad_gain_two,
        mix,
        every - rows,
    )
    (
        output,
        d_out,
        d_query,
        d_key,
        d_value,
        d_router,
        d_gain_one,
        d_gain_two,
        d_gate,
        d_up,
        d_down,
    ) = results(
        residual,
        (mix_first, mix_rest),
        [
            [grads_head[i]]
            + ([grads_more[i]] if more else [])
            + [grads_last[i][None], grads_last[2 + i][None]]
            for i in range(2)
        ],
        dense,
        width // kv_width,
        width // nd,
        w_gate,
        w_down,
        nd,
        width // (ne * nd),
    )
    return (
        output.reshape(tokens.shape),
        grad_tokens.reshape(tokens.shape),
        d_gain_one.reshape(-1),
        d_query,
        d_key,
        d_value,
        d_out,
        d_gain_two.reshape(-1),
        d_router,
        d_gate,
        d_up,
        d_down,
    )


def solution(mesh):
    in_specs = (
        P(None, ("ep", "dp"), None),
        P(None, "ep", "dp"),
        P(None, ("ep", "dp"), None),
        P(),
        P(),
        P(),
        P(),
        P(),
        P(),
        P(),
        P("ep", None, None),
        P("ep", None, None),
        P("ep", None, None),
        P(None, ("ep", "dp"), None),
    )
    out_specs = (
        P(None, ("ep", "dp"), None),
        P(None, ("ep", "dp"), None),
        P(("ep", "dp")),
        P(("ep", "dp"), None),
        P(("ep", "dp"), None),
        P(("ep", "dp"), None),
        P(("ep", "dp"), None),
        P(("ep", "dp")),
        P(("ep", "dp"), None),
        P("ep", "dp", None),
        P("ep", "dp", None),
        P("ep", "dp", None),
    )
    return jax.shard_map(
        per_device, mesh=mesh, in_specs=in_specs, out_specs=out_specs, check_vma=False
    )
```

```python
import functools

import jax
import jax.numpy as jnp
import numpy as np
from jax import lax
from jax.experimental import pallas as pl
from jax.experimental.pallas import tpu as pltpu
from jax.sharding import PartitionSpec as P

HEADS = 16
KV_HEADS = 8
HEAD_DIM = 64
EXPERTS = 32
CAP = 64
EPSILON = 1e-06
ROPE_BASE = 10000.0
MASKED = -1e30
HIGHEST = lax.Precision.HIGHEST
MESH = pl.DeviceIdType.MESH
BF16 = jnp.bfloat16
F32 = jnp.float32
VMEM = pl.BlockSpec(memory_space=pltpu.VMEM)
ANY = pl.BlockSpec(memory_space=pl.ANY)
DMA = pltpu.SemaphoreType.DMA


def bit_count(n):
    return n.bit_length() - 1


def masks(bits):
    out = [0]
    for b in bits:
        out = out + [m | (1 << b) for m in out]
    return out


def gather_orders(n):
    bits = list(range(bit_count(n)))
    return (bits[1:] + bits[:1], bits[:0:-1] + bits[:1])


def greet(ep, dp, ne, nd):
    barrier = pltpu.get_barrier_semaphore()
    for k in range(1, ne):
        pl.semaphore_signal(
            barrier, inc=1, device_id={"ep": lax.rem(ep + k, ne)}, device_id_type=MESH
        )
    for b in range(bit_count(nd)):
        pl.semaphore_signal(
            barrier, inc=1, device_id={"dp": jnp.bitwise_xor(dp, 1 << b)}, device_id_type=MESH
        )
    pl.semaphore_wait(barrier, ne - 1 + bit_count(nd))


def remote(src, dst, send, recv, where):
    return pltpu.make_async_remote_copy(
        src_ref=src, dst_ref=dst, send_sem=send, recv_sem=recv, device_id=where, device_id_type=MESH
    )


def gather_body(ne, nd, n_dp, n_ep, *refs):
    n_in = n_dp + n_ep
    ins, outs, sems = refs[:n_in], refs[n_in : 2 * n_in], refs[2 * n_in :]
    ep, dp = lax.axis_index("ep"), lax.axis_index("dp")
    own_sem, dp_send, dp_recv, ep_send, ep_recv = sems
    greet(ep, dp, ne, nd)
    own = []
    for a in range(n_in):
        me = dp if a < n_dp else ep
        copy = pltpu.make_async_copy(ins[a], outs[a].at[me], own_sem.at[a])
        copy.start()
        own.append(copy)

    def dp_copy(a, t, m):
        order = gather_orders(nd)[a % 2]
        block = jnp.bitwise_xor(dp, m)
        k = (1 << t) - 1 + masks(order[:t]).index(m)
        return remote(
            ins[a] if m == 0 else outs[a].at[block],
            outs[a].at[block],
            dp_send.at[a, k],
            dp_recv.at[a, k],
            {"dp": jnp.bitwise_xor(dp, 1 << order[t])},
        )

    def ep_copy(a, s, way):
        shard = lax.rem(ep - way * s + ne, ne)
        src = ins[n_dp + a] if s == 0 else outs[n_dp + a].at[shard]
        k = 0 if way == 1 else 1
        return remote(
            src,
            outs[n_dp + a].at[shard],
            ep_send.at[a, k, s],
            ep_recv.at[a, k, s],
            {"ep": lax.rem(ep + way + ne, ne)},
        )

    def sends(s, way):
        if way == 1:
            return (ep >= s) & (ep < ne - 1)
        return (ep + s <= ne - 1) & (ep >= 1)

    def receives(s, way):
        if way == 1:
            return ep >= 1 + s
        return ep + 1 + s <= ne - 1

    def ep_start(s):
        for a in range(n_ep):
            for way in (1, -1):

                @pl.when(sends(s, way))
                def _(a=a, way=way):
                    ep_copy(a, s, way).start()

    def ep_wait(s):
        for a in range(n_ep):
            for way in (1, -1):

                @pl.when(receives(s, way))
                def _(a=a, way=way):
                    ep_copy(a, s, way).wait_recv()

    dp_steps = bit_count(nd) if n_dp else 0
    ep_steps = ne - 1 if n_ep else 0
    for t in range(dp_steps):
        for a in range(n_dp):
            dp_copy(a, t, 0).start()
    for t in range(max(dp_steps, ep_steps) + 1):
        if 0 < t <= dp_steps:
            for a in range(n_dp):
                order = gather_orders(nd)[a % 2]
                for m in masks(order[: t - 1]):
                    dp_copy(a, t - 1, m).wait_recv()
                    for later in range(t, dp_steps):
                        dp_copy(a, later, m | (1 << order[t - 1])).start()
        if 0 < t <= ep_steps:
            ep_wait(t - 1)
        if t < ep_steps:
            ep_start(t)
    for t in range(dp_steps):
        for a in range(n_dp):
            for m in masks(gather_orders(nd)[a % 2][:t]):
                dp_copy(a, t, m).wait_send()
    for s in range(ep_steps):
        for a in range(n_ep):
            for way in (1, -1):

                @pl.when(sends(s, way))
                def _(a=a, s=s, way=way):
                    ep_copy(a, s, way).wait_send()

    for c in own:
        c.wait()


def cost(us):
    return pl.CostEstimate(flops=0, bytes_accessed=int(us * 3.0e6), transcendentals=0)


def gather(ne, nd, dp_arrays, ep_arrays, collective, us):
    arrays = list(dp_arrays) + list(ep_arrays)
    counts = [nd] * len(dp_arrays) + [ne] * len(ep_arrays)
    a, b = max(len(dp_arrays), 1), max(len(ep_arrays), 1)
    return pl.pallas_call(
        functools.partial(gather_body, ne, nd, len(dp_arrays), len(ep_arrays)),
        out_shape=[
            jax.ShapeDtypeStruct((n,) + v.shape, v.dtype) for n, v in zip(counts, arrays)
        ],
        in_specs=[ANY] * len(arrays),
        out_specs=[ANY] * len(arrays),
        scratch_shapes=[
            DMA((len(arrays),)),
            DMA((a, nd - 1)),
            DMA((a, nd - 1)),
            DMA((b, 2, ne - 1)),
            DMA((b, 2, ne - 1)),
        ],
        compiler_params=pltpu.CompilerParams(
            collective_id=collective, has_side_effects=True, vmem_limit_bytes=60 * 2**20
        ),
        cost_estimate=cost(us),
    )(*arrays)


def add_into(ref, arrived):
    if len(ref.shape) > 2:

        @pl.loop(0, ref.shape[0])
        def _(i):
            add_into(ref.at[i], arrived.at[i])

    else:
        ref[...] = (ref[...].astype(F32) + arrived[...].astype(F32)).astype(ref.dtype)


class PairSum:
    def __init__(self, dp, order, loads, held, extra, landing, send_sem, recv_sem):
        self.dp, self.order, self.held, self.landing = dp, order, held, landing
        self.send_sem, self.recv_sem = send_sem, recv_sem
        self.extra, self.loads = extra, loads
        self.index = 0
        for b in order:
            side = jnp.bitwise_and(lax.shift_right_logical(dp, b), 1)
            self.index = self.index + (side << self.place(b))

    def place(self, bit):
        return sorted(self.order).index(bit)

    def copies(self, t):
        order = self.order
        partner = jnp.bitwise_xor(self.index, 1 << self.place(order[t]))
        first = sum(1 << (len(order) - 1 - i) for i in range(t))
        return [
            (
                m,
                first + j,
                remote(
                    self.held.at[jnp.bitwise_xor(partner, m)],
                    self.landing.at[first + j],
                    self.send_sem.at[first + j],
                    self.recv_sem.at[first + j],
                    {"dp": jnp.bitwise_xor(self.dp, 1 << order[t])},
                ),
            )
            for j, m in enumerate(masks([self.place(b) for b in order[t + 1 :]]))
        ]

    def load(self):
        for copy in self.loads:
            copy.start()

    def step(self, t):
        if t == 0:
            for copy in self.loads:
                copy.wait()
            if self.extra is not None:
                add_into(self.held, self.extra)
        elif t <= len(self.order):
            for m, k, copy in self.copies(t - 1):
                copy.wait_recv()
                add_into(self.held.at[jnp.bitwise_xor(self.index, m)], self.landing.at[k])
        if t < len(self.order):
            for m, k, copy in self.copies(t):
                copy.start()

    def own(self):
        return self.held.at[self.index]

    def wait_sends(self):
        for t in range(len(self.order)):
            for m, k, copy in self.copies(t):
                copy.wait_send()


class LineSum:
    def __init__(self, ep, ne, blocks, landing, send_sem, recv_sem):
        self.ep, self.ne, self.blocks, self.landing = ep, ne, blocks, landing
        self.send_sem, self.recv_sem = send_sem, recv_sem

    def copy(self, dest, way):
        k = 0 if way == 1 else 1
        return remote(
            self.blocks.at[dest],
            self.landing.at[k, dest],
            self.send_sem.at[k, dest],
            self.recv_sem.at[k, dest],
            {"ep": lax.rem(self.ep + way + self.ne, self.ne)},
        )

    def turn(self, t, way):
        ep, ne = self.ep, self.ne
        dest = ep + ne - 1 - t if way == 1 else ep + t - (ne - 1)
        has = dest <= ne - 1 if way == 1 else dest >= 0
        inner = ep >= 1 if way == 1 else ep <= ne - 2
        return dest, has, inner

    def step(self, t):
        for way in (1, -1):
            dest, has, inner = self.turn(t, way)

            @pl.when(has & inner)
            def _(way=way, dest=dest):
                self.copy(dest, way).wait_recv()
                add_into(self.blocks.at[dest], self.landing.at[0 if way == 1 else 1, dest])

            if t < self.ne - 1:

                @pl.when(has)
                def _(way=way, dest=dest):
                    self.copy(dest, way).start()

    def own(self):
        return self.blocks.at[self.ep]

    def wait_sends(self):
        for t in range(self.ne - 1):
            for way in (1, -1):
                dest, has, inner = self.turn(t, way)

                @pl.when(has)
                def _(way=way, dest=dest):
                    self.copy(dest, way).wait_send()


def shape_at(array, where):
    return tuple(len(range(*w.indices(n))) for w, n in zip(where, array.shape)) + array.shape[len(where) :]


def reduce_body(ne, nd, pairs, line_parts, n_swap, *refs):
    refs = list(refs)

    def take(n):
        return [refs.pop(0) for _ in range(n)]

    n_pair, n_line = len(pairs), len(line_parts)
    n_extra = sum(p[2] for p in pairs)
    n_both = sum(p[3] for p in pairs)
    n_sum = n_pair + n_line
    ins, extra_ins, swap_ins = take(n_sum), take(n_extra), take(n_swap)
    outs, swap_outs = take(n_sum), take(n_swap)
    held, extras, pair_in = take(n_sum), take(n_extra), take(n_pair)
    both_in, line_in = take(n_both), take(n_line)
    load_sem, out_sem, dp_send, dp_recv, ep_send, ep_recv, swap_send, swap_recv = refs
    ep, dp = lax.axis_index("ep"), lax.axis_index("dp")
    sums, then = [], []
    for a, (order, where, has_extra, both) in enumerate(pairs):
        targets = [(ins[a], held[a])]
        extra = extras.pop(0) if has_extra else None
        if has_extra:
            targets.append((extra_ins.pop(0), extra))
        loads = [
            pltpu.make_async_copy(src.at[where] if where else src, dst, load_sem.at[a, i])
            for i, (src, dst) in enumerate(targets)
        ]
        sums.append(
            PairSum(dp, order, loads, held[a], extra, pair_in[a], dp_send.at[a], dp_recv.at[a])
        )
        if both:
            i = len(then)
            then.append(
                LineSum(ep, ne, sums[a].own(), both_in[i], ep_send.at[i], ep_recv.at[i])
            )
    lines, line_loads = [], []
    for i in range(n_line):
        a = n_pair + i
        src = ins[a].at[line_parts[i]] if line_parts[i] else ins[a]
        line_loads.append(pltpu.make_async_copy(src, held[a], load_sem.at[a, 0]))
        lines.append(
            LineSum(
                ep, ne, held[a], line_in[i], ep_send.at[n_both + i], ep_recv.at[n_both + i]
            )
        )
    for copy in line_loads:
        copy.start()
    for each in sums:
        each.load()
    greet(ep, dp, ne, nd)
    swaps = []
    for a in range(n_swap):
        src, dst = swap_ins[a], swap_outs[a]
        own = pltpu.make_async_copy(src.at[ep], dst.at[ep], load_sem.at[n_sum + a, 0])
        own.start()
        swaps.append(own)
        for k in range(1, ne):
            to = lax.rem(ep + k, ne)
            copy = remote(
                src.at[to], dst.at[ep], swap_send.at[a, k - 1], swap_recv.at[a, k - 1], {"ep": to}
            )
            copy.start()
            swaps.append(copy)
    for copy in line_loads:
        copy.wait()
    steps = max([len(p[0]) + 1 for p in pairs] + [ne if n_line else 0])
    for t in range(steps):
        if t < ne:
            for each in lines:
                each.step(t)
        for each in sums:
            each.step(t)
    for t in range(ne):
        for each in then:
            each.step(t)
    results, after = [], iter(then)
    for a in range(n_sum):
        if a >= n_pair:
            src = lines[a - n_pair].own()
        else:
            src = next(after).own() if pairs[a][3] else sums[a].own()
        copy = pltpu.make_async_copy(src, outs[a], out_sem.at[a])
        copy.start()
        results.append(copy)
    for each in sums + then + lines:
        each.wait_sends()
    for copy in swaps + results:
        copy.wait()


def reduce(ne, nd, pairs, lines, swaps, collective, us):
    line_parts = tuple(where for _, where in lines)
    line_shapes = [shape_at(v, where) if where else v.shape for v, where in lines]
    lines = [v for v, _ in lines]
    arrays = [p[0] for p in pairs] + list(lines)
    extras = [p[3] for p in pairs if p[3] is not None]
    kinds = tuple((tuple(p[1]), p[2], p[3] is not None, p[4]) for p in pairs)
    shapes = [shape_at(p[0], p[2]) if p[2] else p[0].shape for p in pairs]
    boths = [s for s, p in zip(shapes, pairs) if p[4]]
    results = [s[2:] if p[4] else s[1:] for s, p in zip(shapes, pairs)]
    results += [s[1:] for s in line_shapes]
    scratch = shapes + line_shapes
    scratch += [s for s, p in zip(shapes, pairs) if p[3] is not None]
    scratch += [(s[0] - 1,) + s[1:] for s in shapes]
    scratch += [(2,) + s[1:] for s in boths] + [(2,) + s for s in line_shapes]
    some = lambda n: max(n, 1)
    line_count = some(len(lines) + len(boths))
    deep = max([s[0] - 1 for s in shapes] + [1])
    return pl.pallas_call(
        functools.partial(reduce_body, ne, nd, kinds, line_parts, len(swaps)),
        out_shape=[jax.ShapeDtypeStruct(s, BF16) for s in results]
        + [jax.ShapeDtypeStruct(v.shape, v.dtype) for v in swaps],
        in_specs=[ANY] * (len(arrays) + len(extras) + len(swaps)),
        out_specs=[ANY] * (len(arrays) + len(swaps)),
        scratch_shapes=[pltpu.VMEM(s, BF16) for s in scratch]
        + [
            DMA((len(arrays) + len(swaps), 2)),
            DMA((len(arrays),)),
            DMA((some(len(pairs)), deep)),
            DMA((some(len(pairs)), deep)),
            DMA((line_count, 2, ne)),
            DMA((line_count, 2, ne)),
            DMA((some(len(swaps)), ne - 1)),
            DMA((some(len(swaps)), ne - 1)),
        ],
        compiler_params=pltpu.CompilerParams(
            collective_id=collective, has_side_effects=True, vmem_limit_bytes=60 * 2**20
        ),
        cost_estimate=cost(us),
    )(*arrays, *extras, *swaps)


def dot(a, b, dims=((1,), (0,))):
    return lax.dot_general(a, b, (dims, ((), ())), preferred_element_type=F32)


def expert_body(ne, nd, micro, rows, *refs):
    cots, refs = refs[:ne], refs[ne:]
    normed_ref, probs_ref, gate_ref, up_ref, down_ref = refs[:5]
    mix_ref, grad_ref, dots_ref = refs[5:8]
    kept, landed, whole = refs[8:10], refs[10:12], refs[12:14]
    rows_in, cots_in, picks, first, second, chances, sides, arrived, leaving = refs[14:23]
    load_sem, store_sem, send_sem, recv_sem, free_sem, far_send, far_recv = refs[23:]
    e = pl.program_id(0)
    last = pl.num_programs(0) - 1
    ep, dp = lax.axis_index("ep"), lax.axis_index("dp")
    other = {"dp": jnp.bitwise_xor(dp, 1)}
    every = micro * rows
    blocks = ne * micro
    width = first.shape[1]
    n_exp = rows_in.shape[1]

    core = jnp.bitwise_and(dp, 1)
    keep, send = sides.at[core], sides.at[1 - core]

    def exchange():
        return remote(send, arrived, send_sem, recv_sem, other)

    def loads():
        out = [
            pltpu.make_async_copy(normed_ref, first, load_sem.at[ne]),
            pltpu.make_async_copy(
                probs_ref.at[:, pl.ds(pl.multiple_of(ep * n_exp, n_exp), n_exp)],
                chances,
                load_sem.at[ne + 1],
            ),
        ]
        for k in range(ne):
            at = pl.multiple_of(lax.rem(ep - k + ne, ne) * every, every)
            out.append(
                pltpu.make_async_copy(cots[k], second.at[pl.ds(at, every)], load_sem.at[k])
            )
        return out

    def block_at(s):
        return pl.ds(pl.multiple_of(s * rows, rows), rows)

    def returned(t):
        k, m = t // micro, lax.rem(t, micro)
        return lax.rem(ep + k, ne) * micro + m

    def stores(t):
        s = returned(t)
        return (
            pltpu.make_async_copy(
                first.at[block_at(s)], mix_ref.at[block_at(s)], store_sem.at[0, t]
            ),
            pltpu.make_async_copy(
                second.at[block_at(s)], grad_ref.at[block_at(s)], store_sem.at[1, t]
            ),
        )

    def far(i, n):
        return remote(
            leaving.at[i, lax.rem(n, leaving.shape[1])],
            landed[i].at[:, n],
            far_send.at[i, lax.rem(n, leaving.shape[1])],
            far_recv.at[i, n],
            {"dp": jnp.bitwise_xor(dp, 1 << first_bits(nd)[i])},
        )

    def last_copy(k):
        return pltpu.make_async_copy(keep, whole[k], load_sem.at[k])

    def collect():
        exchange().wait_recv()
        pieces, height, slots = sides.shape[1], leaving.shape[3], leaving.shape[1]
        n = e - 1
        early = n_exp - 2

        @pl.when(n < early)
        def _():
            @pl.when(n >= slots)
            def _():
                for i in range(2):
                    far(i, n - slots).wait_send()

            def piece(i, at, other_side):
                bit = first_bits(nd)[i]
                mine = jnp.bitwise_and(lax.shift_right_logical(dp, bit), 1)
                side = 1 - mine if other_side else mine
                low = (1 << (bit - 1)) - 1
                j = ((at & ~low) << 1 | (at & low)) + (side << (bit - 1))
                part = slice(i * height, (i + 1) * height)
                return (keep[j, part].astype(F32) + arrived[j, part].astype(F32)).astype(BF16)

            for i in range(2):
                for at in range(pieces // 2):
                    leaving[i, lax.rem(n, slots), at] = piece(i, at, True)
                far(i, n).start()
            for i in range(2):
                for at in range(pieces // 2):
                    kept[i][at, 0] = piece(i, at, False)

        for k in range(2):

            @pl.when(n == early + k)
            def _(k=k):
                add_into(keep, arrived)
                last_copy(k).start()

    @pl.when(e == 0)
    def _():
        for copy in loads():
            copy.start()
        barrier = pltpu.get_barrier_semaphore()
        met = [0] + sorted(set(first_bits(nd)))
        for bit in met:
            pl.semaphore_signal(
                barrier,
                inc=1,
                device_id={"dp": jnp.bitwise_xor(dp, 1 << bit)},
                device_id_type=MESH,
            )
        pl.semaphore_wait(barrier, len(met))
        before = lax.broadcasted_iota(jnp.int32, (rows, rows), 0)
        after = lax.broadcasted_iota(jnp.int32, (rows, rows), 1)
        earlier = (before < after).astype(BF16)
        slot = lax.broadcasted_iota(jnp.int32, (n_exp, CAP, rows), 1)
        for copy in loads():
            copy.wait()

        @pl.loop(0, blocks)
        def _(s):
            at = block_at(s)
            probs = chances[s]
            hit = probs >= 0.0
            rank = dot(hit.astype(BF16), earlier)
            rank = jnp.where(hit, rank, -1.0).astype(jnp.int32)
            pick = jnp.broadcast_to(rank[:, None, :], (n_exp, CAP, rows)) == slot
            pick_f = pick.astype(F32)
            flat = pick_f.reshape(n_exp * CAP, rows).astype(BF16)
            picks[s] = flat
            rows_in[s] = dot(flat, first[at, :]).astype(BF16).reshape(n_exp, CAP, width)
            cots_in[s] = dot(flat, second[at, :]).astype(BF16).reshape(n_exp, CAP, width)

    @pl.when(e < last)
    def _():
        x = rows_in[:, e].reshape(blocks * CAP, width)
        c = cots_in[:, e].reshape(blocks * CAP, width)
        flat = picks[:, pl.ds(pl.multiple_of(e * CAP, CAP), CAP), :].astype(F32)
        p = jnp.sum(flat * chances[:, pl.ds(e, 1), :], axis=2, keepdims=True)
        p = p.reshape(blocks * CAP, 1)
        w_gate, w_up, w_down = gate_ref[0], up_ref[0], down_ref[0]
        gate_pre = dot(x, w_gate)
        up_pre = dot(x, w_up)
        back = dot(c, w_down, ((1,), (1,)))

        @pl.when(e > 0)
        def _():
            collect()
            pl.semaphore_signal(free_sem, inc=1, device_id=other, device_id_type=MESH)

        sigma = jax.nn.sigmoid(gate_pre)
        silu = gate_pre * sigma
        hidden = (silu * up_pre).astype(BF16)
        out = dot(hidden, w_down) * p
        wide = hidden.astype(F32)
        pair = jnp.sum(wide * back, axis=1, keepdims=True)
        back = back * p
        grad_up = (back * silu).astype(BF16)
        grad_gate = (back * up_pre * (sigma * (1.0 + gate_pre * (1.0 - sigma)))).astype(BF16)
        scaled = (wide * p).astype(BF16)
        grad_x = dot(grad_gate, w_gate, ((1,), (1,))) + dot(grad_up, w_up, ((1,), (1,)))
        pair = jnp.sum(flat * pair.reshape(blocks, CAP, 1), axis=1)
        dots_ref[:, 0] = pair.reshape(ne, micro, rows)

        @pl.when(e > 0)
        def _():
            exchange().wait_send()
            pl.semaphore_wait(free_sem, 1)

        @pl.when(e == n_exp - 1)
        def _():
            last_copy(0).wait()

        def split(value, offset):
            value = value.astype(BF16)
            piece, columns = value.shape[0] // nd, sides.shape[3]

            for i in range(nd):
                for j in range(value.shape[1] // columns):
                    at = offset + j * piece
                    sides[i % 2, i // 2, at : at + piece] = value[
                        i * piece : (i + 1) * piece, j * columns : (j + 1) * columns
                    ]

        share = width // nd
        split(dot(scaled, c, ((0,), (0,))), 2 * share)
        split(dot(x, grad_gate, ((0,), (0,))), 0)
        split(dot(x, grad_up, ((0,), (0,))), share)
        exchange().start()

        rows_in[:, e] = grad_x.astype(BF16).reshape(blocks, CAP, width)
        cots_in[:, e] = out.astype(BF16).reshape(blocks, CAP, width)

    @pl.when(e == last)
    def _():
        @pl.loop(0, blocks)
        def _(t):
            s = returned(t)
            at = block_at(s)
            flat = picks[s]
            for done, slots in ((first, cots_in), (second, rows_in)):
                value = dot(flat, slots[s].reshape(n_exp * CAP, width), ((0,), (0,)))
                done[at, :] = value.astype(BF16)
            for copy in stores(t):
                copy.start()

            @pl.when(t == 1)
            def _():
                collect()
                exchange().wait_send()

        @pl.loop(0, blocks)
        def _(t):
            for copy in stores(t):
                copy.wait()

        last_copy(1).wait()
        early, slots = n_exp - 2, leaving.shape[1]
        for i in range(2):
            for n in range(max(early - slots, 0), early):
                far(i, n).wait_send()

            @pl.loop(0, early)
            def _(n, i=i):
                far(i, n).wait_recv()


def first_bits(nd):
    return [order[-2] for order in gather_orders(nd)]


def experts(normed, cots, probs, w_gate, w_up, w_down, micro, rows, ne, nd, collective):
    n_exp, width, inner = w_gate.shape
    blocks = ne * micro
    half = nd // 2
    packed = 2 * width // nd + (inner // nd) * (width // inner)
    full = (blocks * rows, width)
    weight = lambda e: (jnp.minimum(e, n_exp - 1), 0, 0)
    early = n_exp - 2
    part = (half // 2, early, packed // 2, inner)
    kept = pl.BlockSpec(
        (half // 2, 1, packed // 2, inner), lambda e: (0, jnp.clip(e - 1, 0, early - 1), 0, 0)
    )
    last = (half, packed, inner)
    return pl.pallas_call(
        functools.partial(expert_body, ne, nd, micro, rows),
        grid=(n_exp + 1,),
        in_specs=[ANY] * (ne + 2)
        + [
            pl.BlockSpec((1, width, inner), weight),
            pl.BlockSpec((1, width, inner), weight),
            pl.BlockSpec((1, inner, width), weight),
        ],
        out_specs=[
            ANY,
            ANY,
            pl.BlockSpec((ne, 1, micro, rows), lambda e: (0, jnp.minimum(e, n_exp - 1), 0, 0)),
            kept,
            kept,
            ANY,
            ANY,
            ANY,
            ANY,
        ],
        scratch_shapes=[
            pltpu.VMEM((blocks, n_exp, CAP, width), BF16),
            pltpu.VMEM((blocks, n_exp, CAP, width), BF16),
            pltpu.VMEM((blocks, n_exp * CAP, rows), BF16),
            pltpu.VMEM(full, BF16),
            pltpu.VMEM(full, BF16),
            pltpu.VMEM((blocks, n_exp, rows), F32),
            pltpu.VMEM((2, half, packed, inner), BF16),
            pltpu.VMEM((half, packed, inner), BF16),
            pltpu.VMEM((2, 2 if early > 2 else 1, half // 2, packed // 2, inner), BF16),
            DMA((ne + 2,)),
            DMA((2, blocks)),
            DMA,
            DMA,
            pltpu.SemaphoreType.REGULAR,
            DMA((2, 2)),
            DMA((2, early)),
        ],
        out_shape=[
            jax.ShapeDtypeStruct(full, BF16),
            jax.ShapeDtypeStruct(full, BF16),
            jax.ShapeDtypeStruct((ne, n_exp, micro, rows), F32),
        ]
        + [jax.ShapeDtypeStruct(part, BF16)] * 4
        + [jax.ShapeDtypeStruct(last, BF16)] * 2,
        compiler_params=pltpu.CompilerParams(
            vmem_limit_bytes=63 * 2**20,
            dimension_semantics=("arbitrary",),
            collective_id=collective,
            has_side_effects=True,
        ),
        cost_estimate=cost(75),
    )(*cots, normed, probs, w_gate, w_up, w_down)


def rms_scale(values):
    return lax.rsqrt(jnp.mean(values * values, axis=-1, keepdims=True) + EPSILON)


def partner(x):
    lane = lax.broadcasted_iota(jnp.int32, x.shape, 1)
    half = HEAD_DIM // 2
    low = lax.rem(lane, HEAD_DIM) < half
    return jnp.where(low, pltpu.roll(x, x.shape[1] - half, 1), pltpu.roll(x, half, 1))


def turn(x, cosine, sine):
    return x * cosine + partner(x) * sine


def repeated(table, rows):
    return jnp.concatenate([table] * (rows // table.shape[0]), axis=0)


def project_body(
    tokens_ref, gain_ref, tables_ref, wq_ref, wk_ref, wv_ref, n_ref, q_ref, k_ref, v_ref, *rest
):
    wq, wk, wv, sem = rest
    loads = [
        pltpu.make_async_copy(src, dst, sem.at[i])
        for i, (src, dst) in enumerate(((wk_ref, wk), (wv_ref, wv), (wq_ref, wq)))
    ]
    for copy in loads:
        copy.start()
    x = tokens_ref[...].astype(F32)
    n_ref[...] = (x * rms_scale(x) * gain_ref[...]).astype(BF16)
    normed = n_ref[...]
    cosine, sine = (repeated(tables_ref[i], x.shape[0]) for i in range(2))
    tile = 256
    for copy, (w, out, turned) in zip(
        loads, ((wk, k_ref, True), (wv, v_ref, False), (wq, q_ref, True))
    ):
        copy.wait()
        for c in range(0, w.shape[1], tile):
            y = dot(normed, w[:, c : c + tile])
            if turned:
                for i in range(0, tile, 128):
                    out[:, c + i : c + i + 128] = turn(y[:, i : i + 128], cosine, sine).astype(BF16)
            else:
                out[:, c : c + tile] = y.astype(BF16)


def project(tokens, gain, tables, w_query, w_key, w_value):
    rows, width = tokens.shape
    shapes = [width, w_query.shape[1], w_key.shape[1], w_value.shape[1]]
    return pl.pallas_call(
        project_body,
        out_shape=[jax.ShapeDtypeStruct((rows, n), BF16) for n in shapes],
        in_specs=[VMEM] * 3 + [ANY] * 3,
        out_specs=[VMEM] * 4,
        scratch_shapes=[pltpu.VMEM(w.shape, BF16) for w in (w_query, w_key, w_value)] + [DMA((3,))],
        compiler_params=pltpu.CompilerParams(vmem_limit_bytes=60 * 2**20),
        cost_estimate=cost(5),
    )(tokens, gain, tables, w_query, w_key, w_value)


def spread(x):
    lane = lax.broadcasted_iota(jnp.int32, (x.shape[0], 128), 1)
    low = lane < HEAD_DIM
    zero = jnp.zeros((), x.dtype)
    first, second = x[:, :128], x[:, 128:]
    return jnp.concatenate(
        [
            jnp.where(low, first, zero),
            jnp.where(low, pltpu.roll(first, HEAD_DIM, 1), zero),
            jnp.where(low, zero, pltpu.roll(second, HEAD_DIM, 1)),
            jnp.where(low, zero, second),
        ],
        axis=0,
    )


def gathered(x, rows):
    lane = lax.broadcasted_iota(jnp.int32, (rows, 128), 1)
    low = lane < HEAD_DIM
    h = [x[i * rows : (i + 1) * rows] for i in range(4)]
    return jnp.concatenate(
        [
            jnp.where(low, h[0], pltpu.roll(h[1], HEAD_DIM, 1)),
            jnp.where(low, pltpu.roll(h[2], HEAD_DIM, 1), h[3]),
        ],
        axis=1,
    )


def window_of(dp, span):
    return jnp.maximum(dp - (span - 1), 0)


def window_scores(dp, span, rows, starts_ref, q, k):
    keys = k.shape[0]
    scores = dot(q, k, ((1,), (1,))).reshape(4, rows, keys)
    key_pos = window_of(dp, span) * rows + lax.broadcasted_iota(jnp.int32, (rows, keys), 1)
    query_pos = dp * rows + lax.broadcasted_iota(jnp.int32, (rows, keys), 0)
    allowed = (key_pos <= query_pos) & (key_pos >= starts_ref[...])
    return jnp.where(allowed[None], scores, MASKED).reshape(4 * rows, keys)


def in_window(ref, dp, span):
    block = ref[pl.ds(window_of(dp, span), span)]
    return block.reshape(span * block.shape[1], block.shape[2])


SCALE = HEAD_DIM ** (-0.5)


class LineGather:
    def __init__(self, ep, ne, own, whole, send_sem, recv_sem):
        self.ep, self.ne, self.own, self.whole = ep, ne, own, whole
        self.send_sem, self.recv_sem = send_sem, recv_sem

    def copy(self, m, s, way):
        shard = lax.rem(self.ep - way * s + self.ne, self.ne)
        k = 0 if way == 1 else 1
        return remote(
            self.own.at[m] if s == 0 else self.whole.at[shard, m],
            self.whole.at[shard, m],
            self.send_sem.at[m, k, s],
            self.recv_sem.at[m, k, s],
            {"ep": lax.rem(self.ep + way + self.ne, self.ne)},
        )

    def sends(self, s, way):
        ep, ne = self.ep, self.ne
        return (ep >= s) & (ep < ne - 1) if way == 1 else (ep + s <= ne - 1) & (ep >= 1)

    def receives(self, s, way):
        return self.ep >= 1 + s if way == 1 else self.ep + 1 + s <= self.ne - 1

    def step(self, m, s):
        for way in (1, -1):
            if s > 0:

                @pl.when(self.receives(s - 1, way))
                def _(way=way):
                    self.copy(m, s - 1, way).wait_recv()

            if s < self.ne - 1:

                @pl.when(self.sends(s, way))
                def _(way=way):
                    self.copy(m, s, way).start()

    def wait_sends(self, m):
        for s in range(self.ne - 1):
            for way in (1, -1):

                @pl.when(self.sends(s, way))
                def _(s=s, way=way):
                    self.copy(m, s, way).wait_send()


def attend_body(span, ne, nd, micro, *refs):
    starts_ref, q_ref, k_ref, v_ref, tokens_ref, wo_ref, gain_ref, router_ref, hit_ref = refs[:9]
    out_ref, log_ref, res_ref, normed_ref, probs_ref, normed_all, marked_all = refs[9:16]
    attn, normed_own, marked_own, own_sem, send_sem, recv_sem = refs[16:]
    ep, dp = lax.axis_index("ep"), lax.axis_index("dp")
    m, h = pl.program_id(0), pl.program_id(1)
    final = pl.num_programs(1) - 1
    rows = q_ref.shape[0]
    lines = [
        LineGather(ep, ne, own, whole, send_sem.at[i], recv_sem.at[i])
        for i, (own, whole) in enumerate(((normed_own, normed_all), (marked_own, marked_all)))
    ]

    def hop(batch, s):
        for line in lines:
            line.step(batch, s)

    @pl.when((m == 0) & (h == 0))
    def _():
        greet(ep, dp, ne, nd)

    q = spread(q_ref[...].astype(F32) * SCALE).astype(BF16)
    scores = window_scores(dp, span, rows, starts_ref, q, in_window(k_ref, dp, span))
    top = jnp.max(scores, axis=1, keepdims=True)
    terms = jnp.exp(scores - top)
    total = jnp.sum(terms, axis=1, keepdims=True)
    log_ref[0, 0] = top + jnp.log(total)
    weights = (terms * (1.0 / total)).astype(BF16)
    out = gathered(dot(weights, in_window(v_ref, dp, span)), rows).astype(BF16)
    out_ref[...] = out
    attn[:, pl.ds(pl.multiple_of(h * out.shape[1], out.shape[1]), out.shape[1])] = out

    def own_copies(batch):
        return [
            pltpu.make_async_copy(line.own.at[batch], line.whole.at[ep, batch], own_sem.at[i, batch])
            for i, line in enumerate(lines)
        ]

    for batch in range(micro):

        @pl.when((m == batch) & (h == final))
        def _(batch=batch):
            for earlier in range(batch):
                hop(earlier, batch - earlier)
            residual = tokens_ref[...].astype(F32) + dot(attn[...], wo_ref[...])
            res_ref[...] = residual
            normed = (residual * rms_scale(residual) * gain_ref[...]).astype(BF16)
            normed_ref[...] = normed
            normed_own[batch] = normed
            hit = hit_ref[...] > 0.0
            logits = jnp.where(hit, dot(router_ref[...], normed, ((1,), (1,))), MASKED)
            terms = jnp.exp(logits - jnp.max(logits, axis=0, keepdims=True))
            terms = jnp.where(hit, terms, 0.0)
            probs = terms / jnp.sum(terms, axis=0, keepdims=True)
            probs_ref[...] = probs
            marked_own[batch] = jnp.where(hit, probs, -1.0)
            hop(batch, 0)
            for copy in own_copies(batch):
                copy.start()
            if batch == micro - 1:
                for t in range(1, ne + micro - 1):
                    for each in range(micro):
                        s = t + micro - 1 - each
                        if s < ne:
                            hop(each, s)
                for each in range(micro):
                    for line in lines:
                        line.wait_sends(each)
                    for copy in own_copies(each):
                        copy.wait()


def attention_specs(micro, rows, nd):
    pairs = KV_HEADS // 2
    mine = pl.BlockSpec((rows, 4 * HEAD_DIM), lambda m, h, *_: (m, h))
    theirs = pl.BlockSpec((nd, rows, 2 * HEAD_DIM), lambda m, h, *_: (0, m, h))
    column = pl.BlockSpec((rows, 1), lambda m, h, *_: (m, 0))
    logs = pl.BlockSpec((1, 1, 4 * rows, 1), lambda m, h, *_: (m, h, 0, 0))
    log_shape = jax.ShapeDtypeStruct((micro, pairs, 4 * rows, 1), F32)
    return (micro, pairs), mine, theirs, column, logs, log_shape


def attend(
    starts, queries, keys, values, tokens, w_out, gain, router, hit, micro, rows, ne, collective
):
    nd, width = keys.shape[0], tokens.shape[1]
    grid, mine, theirs, column, logs, log_shape = attention_specs(micro, rows, nd)
    one = pl.Buffered(1)
    whole = lambda v: pl.BlockSpec(v.shape, lambda m, h: (0, 0), pipeline_mode=one)
    wide = pl.BlockSpec((rows, width), lambda m, h: (m, 0))
    chosen = pl.BlockSpec((hit.shape[0], rows), lambda m, h: (0, m))
    every = micro * rows
    return pl.pallas_call(
        functools.partial(attend_body, nd // 2 + 1, ne, nd, micro),
        grid=grid,
        in_specs=[column, mine, theirs, theirs, wide, whole(w_out), whole(gain), whole(router)]
        + [chosen],
        out_specs=[mine, logs, wide, wide, chosen, ANY, ANY],
        out_shape=[
            jax.ShapeDtypeStruct(queries.shape, BF16),
            log_shape,
            jax.ShapeDtypeStruct((every, width), F32),
            jax.ShapeDtypeStruct((every, width), BF16),
            jax.ShapeDtypeStruct(hit.shape, F32),
            jax.ShapeDtypeStruct((ne, micro, rows, width), BF16),
            jax.ShapeDtypeStruct((ne, micro, hit.shape[0], rows), F32),
        ],
        scratch_shapes=[
            pltpu.VMEM((rows, width), BF16),
            pltpu.VMEM((micro, rows, width), BF16),
            pltpu.VMEM((micro, hit.shape[0], rows), F32),
            DMA((2, micro)),
            DMA((2, micro, 2, ne - 1)),
            DMA((2, micro, 2, ne - 1)),
        ],
        compiler_params=pltpu.CompilerParams(
            vmem_limit_bytes=60 * 2**20, collective_id=collective, has_side_effects=True
        ),
        cost_estimate=cost(50),
    )(starts, queries, keys, values, tokens, w_out, gain, router, hit)


def attend_back_body(span, ne, nd, micro, skip, full, orders, *refs):
    refs = list(refs)

    def take(n):
        return [refs.pop(0) for _ in range(n)]

    starts_ref, q_ref, k_ref, v_ref, log_ref, tables_ref = take(6)
    cot_ref, dots_ref, probs_ref, grad_ref, residual_ref, gain_ref, normed_ref, attn_ref = take(8)
    wo_ref, router_ref, mix_ref = take(3)
    n = len(orders)
    sources, extras = take(n), take(n)
    dq_ref, res_out, wo_out, router_out, gain_out, dk_out, dv_out, mix_out = take(8)
    outs = take(n)
    grads, mix_held, mix_in = take(3)
    kv_held, kv_in = take(2), take(2)
    held, more, landing = take(n), take(n), take(n)
    load_sem, out_sem, send_sem, recv_sem, kv_send, kv_recv, kv_out, mix_sem, line_send, line_recv = refs
    ep, dp = lax.axis_index("ep"), lax.axis_index("dp")
    step = pl.program_id(0) * pl.num_programs(1) + pl.program_id(1)
    final = pl.num_programs(0) * pl.num_programs(1) - 1
    sums = []
    for a in range(n):
        part = pl.ds(skip, sources[a].shape[1] - skip)
        loads = [
            pltpu.make_async_copy(src.at[:, part], dst, load_sem.at[a, i])
            for i, (src, dst) in enumerate(((sources[a], held[a]), (extras[a], more[a])))
        ]
        sums.append(
            PairSum(
                dp, orders[a], loads, held[a], more[a], landing[a], send_sem.at[a], recv_sem.at[a]
            )
        )
    batch_sums = [
        [
            PairSum(
                dp,
                full[i],
                [],
                kv_held[i].at[m],
                None,
                kv_in[i].at[m],
                kv_send.at[i, m],
                kv_recv.at[i, m],
            )
            for i in range(2)
        ]
        for m in range(micro)
    ]
    lines = [
        LineSum(ep, ne, mix_held.at[m], mix_in.at[m], line_send.at[m], line_recv.at[m])
        for m in range(micro)
    ]
    count = q_ref.shape[0]
    line_loads = [
        pltpu.make_async_copy(
            mix_ref.at[:, pl.ds(m * count, count)], mix_held.at[m], mix_sem.at[0, m]
        )
        for m in range(micro)
    ]
    turns = bit_count(nd)

    def batch_step(m, t):
        if t <= turns:
            for each in batch_sums[m]:
                each.step(t)

    def line_step(m, t):
        if t < ne:
            lines[m].step(t)

    @pl.when(step == 0)
    def _():
        for copy in line_loads:
            copy.start()
        for each in sums:
            each.load()
        greet(ep, dp, ne, nd)
        for m in range(micro):
            line_loads[m].wait()
            line_step(m, 0)
        for each in sums:
            each.step(0)
        for i in range(2):
            kv_held[i][...] = jnp.zeros_like(kv_held[i])
        rows = q_ref.shape[0]
        pairs = [dots_ref[:, :, m, :].reshape(-1, rows) for m in range(micro)]
        pair = jnp.concatenate(pairs, axis=1)
        probs = probs_ref[...]
        grad_logits = probs * (pair - jnp.sum(probs * pair, axis=0, keepdims=True))
        high = grad_logits.astype(BF16)
        low = (grad_logits - high.astype(F32)).astype(BF16)
        normed = normed_ref[...]
        router_out[...] = dot(high, normed) + dot(low, normed)
        router = router_ref[...]
        grad_normed = (
            grad_ref[...].astype(F32)
            + dot(high, router, ((0,), (0,)))
            + dot(low, router, ((0,), (0,)))
        )
        residual = residual_ref[...]
        r = rms_scale(residual)
        gain_out[...] = jnp.sum(grad_normed * residual * r, axis=0, keepdims=True)
        scaled = grad_normed * gain_ref[...]
        mean = jnp.mean(scaled * residual, axis=1, keepdims=True)
        grad_residual = cot_ref[...].astype(F32) + r * scaled - residual * (r * r * r) * mean
        res_out[...] = grad_residual
        low_res = grad_residual.astype(BF16)
        tile = 256
        for c in range(0, wo_out.shape[1], tile):
            wo_out[:, c : c + tile] = dot(
                attn_ref[...], low_res[:, c : c + tile], ((0,), (0,))
            ).astype(BF16)
        for c in range(0, wo_ref.shape[0], tile):
            grads[c // tile] = dot(low_res, wo_ref[c : c + tile, :], ((1,), (1,))).astype(BF16)

    rows = q_ref.shape[0]
    q = spread(q_ref[...].astype(F32) * SCALE).astype(BF16)
    mine = pl.ds(pl.multiple_of(pl.program_id(0) * rows, rows), rows)
    g = spread(grads[pl.program_id(1), mine, :].astype(F32)).astype(BF16)
    k, v = in_window(k_ref, dp, span), in_window(v_ref, dp, span)
    scores = window_scores(dp, span, rows, starts_ref, q, k)
    probs = jnp.exp(scores - log_ref[0, 0])
    grad_probs = dot(g, v, ((1,), (1,)))
    total = jnp.sum(probs * grad_probs, axis=1, keepdims=True)
    grad_scores = (probs * (grad_probs - total)).astype(BF16)
    dq = gathered(dot(grad_scores, k) * SCALE, rows)
    cosine, sine = tables_ref[0], -tables_ref[1]
    for i in range(0, dq.shape[1], 128):
        dq_ref[:, i : i + 128] = turn(dq[:, i : i + 128], cosine, sine).astype(BF16)
    here = pl.ds(window_of(dp, span), span)
    head = pl.program_id(1)
    at = pl.ds(pl.multiple_of(head * 2 * HEAD_DIM, 2 * HEAD_DIM), 2 * HEAD_DIM)
    batch = pl.program_id(0)
    dk = dot(grad_scores, q, ((0,), (0,))).astype(BF16)
    kv_held[0][batch, here, :, at] = dk.reshape(span, rows, dk.shape[1])
    dv = dot(probs.astype(BF16), g, ((0,), (0,))).astype(BF16)
    kv_held[1][batch, here, :, at] = dv.reshape(span, rows, dv.shape[1])

    heads = pl.num_programs(1)
    for m in range(micro):

        @pl.when((batch == m) & (head == heads - 1))
        def _(m=m):
            batch_step(m, 0)

        if m > 0:

            @pl.when((batch == m) & (head == 0))
            def _(m=m):
                batch_step(m - 1, 1)

    @pl.when(step == final // 4 + 1)
    def _():
        line_step(0, 1)

    @pl.when(step == final // 2 + 2)
    def _():
        line_step(1, 1)

    @pl.when(step == final)
    def _():
        copies = []

        def leave(copy):
            copy.start()
            copies.append(copy)

        line_step(0, 2)
        last = micro - 1
        batch_step(last - 1, 2)
        for t in range(1, max([len(order) for order in orders] + [0]) + 1):
            for each in sums:
                each.step(t)
        for a, each in enumerate(sums):
            leave(pltpu.make_async_copy(each.own(), outs[a], out_sem.at[a]))
        batch_step(last, 1)
        line_step(1, 2)
        for t in range(3, turns + 1):
            batch_step(last - 1, t)
        batch_step(last, 2)
        for t in range(3, ne):
            line_step(0, t)
            line_step(1, t)
        for t in range(3, turns + 1):
            batch_step(last, t)
        for m in range(micro):
            own = pl.ds(m * rows, rows)
            for i, out in enumerate((dk_out, dv_out)):
                leave(pltpu.make_async_copy(batch_sums[m][i].own(), out.at[own], kv_out.at[i, m]))
            leave(pltpu.make_async_copy(lines[m].own(), mix_out.at[own], mix_sem.at[1, m]))
        for each in sums + lines + sum(batch_sums, []):
            each.wait_sends()
        for copy in copies:
            copy.wait()


def attend_back(
    starts,
    queries,
    keys,
    values,
    logs_in,
    tables,
    cot,
    dots,
    probs,
    grad_normed,
    residual,
    gain,
    normed,
    attn,
    w_out,
    router,
    mix,
    sums,
    full,
    skip,
    collective,
):
    nd, ne, micro, rows = keys.shape[0], dots.shape[0], dots.shape[2], dots.shape[3]
    every, width = residual.shape
    grid, mine, theirs, column, logs, _ = attention_specs(micro, rows, nd)
    one = pl.Buffered(1)
    whole = lambda v: pl.BlockSpec(v.shape, lambda m, h: (0,) * len(v.shape), pipeline_mode=one)
    n = len(sums)
    shapes = [(v.shape[0], v.shape[1] - skip) + v.shape[2:] for v, _, _ in sums]
    deep = max([s[0] - 1 for s in shapes] + [1])
    some = max(n, 1)
    before = [cot, dots, probs, grad_normed, residual, gain, normed, attn, w_out, router]
    after = [
        jax.ShapeDtypeStruct((every, width), F32),
        jax.ShapeDtypeStruct(w_out.shape, BF16),
        jax.ShapeDtypeStruct(router.shape, F32),
        jax.ShapeDtypeStruct((1, width), F32),
    ]
    tile = 4 * HEAD_DIM
    return pl.pallas_call(
        functools.partial(
            attend_back_body,
            nd // 2 + 1,
            ne,
            nd,
            micro,
            skip,
            tuple(map(tuple, full)),
            tuple(tuple(order) for _, order, _ in sums),
        ),
        grid=grid,
        in_specs=[column, mine, theirs, theirs, logs, whole(tables)]
        + [whole(v) for v in before]
        + [ANY] * (2 * n + 1),
        out_specs=[mine] + [whole(v) for v in after] + [ANY] * (n + 3),
        out_shape=[jax.ShapeDtypeStruct(queries.shape, BF16)]
        + after
        + [jax.ShapeDtypeStruct((every, keys.shape[2]), BF16)] * 2
        + [jax.ShapeDtypeStruct((every, width), BF16)]
        + [jax.ShapeDtypeStruct(s[1:], BF16) for s in shapes],
        scratch_shapes=[
            pltpu.VMEM((w_out.shape[0] // tile, every, tile), BF16),
            pltpu.VMEM((micro, ne, rows, width), BF16),
            pltpu.VMEM((micro, 2, ne, rows, width), BF16),
        ]
        + [pltpu.VMEM((micro, nd, rows, keys.shape[2]), BF16)] * 2
        + [pltpu.VMEM((micro, nd - 1, rows, keys.shape[2]), BF16)] * 2
        + [pltpu.VMEM(s, BF16) for s in shapes] * 2
        + [pltpu.VMEM((s[0] - 1,) + s[1:], BF16) for s in shapes]
        + [
            DMA((some, 2)),
            DMA((some,)),
            DMA((some, deep)),
            DMA((some, deep)),
            DMA((2, micro, nd - 1)),
            DMA((2, micro, nd - 1)),
            DMA((2, micro)),
            DMA((2, micro)),
            DMA((micro, 2, ne)),
            DMA((micro, 2, ne)),
        ],
        compiler_params=pltpu.CompilerParams(
            vmem_limit_bytes=63 * 2**20, collective_id=collective, has_side_effects=True
        ),
        cost_estimate=cost(40),
    )(
        starts,
        queries,
        keys,
        values,
        logs_in,
        tables,
        *before,
        mix,
        *[v for v, _, _ in sums],
        *[extra for _, _, extra in sums],
    )


def finish_body(ne, nd, orders, n_out, *refs):
    refs = list(refs)

    def take(n):
        return [refs.pop(0) for _ in range(n)]

    n_ref, dq_ref, dk_ref, dv_ref, tables_ref, tokens_ref, gain_ref, router_ref, gain_two = take(9)
    res_ref, wq_ref, wk_ref, wv_ref, wo_ref = take(5)
    (tok_out,) = take(1)
    count = 2 * n_out + 3
    outs, held, pair_in, line_in = take(count), take(count), take(count), take(count)
    dk_turned, wq, wk, wv, res = take(5)
    load_sem, own_sem, out_sem, dp_send, dp_recv, ep_send, ep_recv = refs
    ep, dp = lax.axis_index("ep"), lax.axis_index("dp")
    columns = held[0].shape[3]
    own = [
        pltpu.make_async_copy(src, dst, own_sem.at[i])
        for i, (src, dst) in enumerate(
            ((wq_ref, wq), (wk_ref, wk), (wv_ref, wv), (res_ref, res))
        )
    ]
    sums = []
    for a in range(count):
        loads = []
        if a < n_out:
            at = pl.ds(a * columns, columns)
            loads = [
                pltpu.make_async_copy(wo_ref.at[e, :, :, at], held[a].at[:, e], load_sem.at[a, e])
                for e in range(ne)
            ]
        sums.append(
            PairSum(
                dp, orders[a % 2], loads, held[a], None, pair_in[a], dp_send.at[a], dp_recv.at[a]
            )
        )
    lines = [
        LineSum(ep, ne, sums[a].own(), line_in[a], ep_send.at[a], ep_recv.at[a])
        for a in range(count)
    ]
    early, made, small = sums[:n_out], sums[n_out:-1], sums[-1]
    queries, others = made[:n_out], made[n_out:]
    for each in early:
        each.load()
    for copy in own:
        copy.start()
    greet(ep, dp, ne, nd)
    turns = bit_count(nd)

    def steps(group, t):
        for each in group:
            if t <= turns:
                each.step(t)

    def line_steps(group, t):
        for each in group:
            if t < ne:
                lines[sums.index(each)].step(t)

    steps(early, 0)

    normed = n_ref[...]
    cosine, sine = (repeated(tables_ref[i], normed.shape[0]) for i in range(2))
    sine = -sine
    for i in range(0, dk_ref.shape[1], 128):
        part = dk_ref[:, i : i + 128].astype(F32)
        dk_turned[:, i : i + 128] = turn(part, cosine, sine).astype(BF16)
    tile = 256

    def product(grad, first, each):
        share = each.held.shape[2]
        for c in range(0, each.held.shape[3], tile):
            y = dot(normed, grad[:, first + c : first + c + tile], ((0,), (0,))).astype(BF16)
            for e in range(ne):
                for d in range(nd):
                    r = (e * nd + d) * share
                    each.held[d, e, :, c : c + tile] = y[r : r + share]
        each.step(0)

    for i, each in enumerate(made):
        if i < n_out:
            product(dq_ref, i * columns, each)
        else:
            product((dk_turned, dv_ref)[i - n_out], 0, each)
        if i == 0:
            steps(early, 1)
        else:
            made[i - 1].step(1)
    for copy in own:
        copy.wait()
    back = dot(dq_ref[...], wq[...], ((1,), (1,)))
    steps(made[-1:], 1)
    back = back + dot(dk_turned[...], wk[...], ((1,), (1,)))
    back = back + dot(dv_ref[...], wv[...], ((1,), (1,)))
    steps(early, 2)
    x = tokens_ref[...].astype(F32)
    r = rms_scale(x)
    scaled = back * gain_ref[...]
    tok_out[...] = (
        res[...] + r * scaled - x * (r * r * r) * jnp.mean(scaled * x, axis=1, keepdims=True)
    )
    one_row = jnp.sum(back * x * r, axis=0, keepdims=True)
    blank = jnp.zeros((held[-1].shape[3] - EXPERTS - 2, x.shape[1]), F32)
    column = jnp.concatenate([router_ref[...], one_row, gain_two[...], blank], axis=0).T
    share = held[-1].shape[2]
    for e in range(ne):
        for d in range(nd):
            i = (e * nd + d) * share
            held[-1][d, e] = column[i : i + share].astype(BF16)
    steps([small], 0)
    steps(queries, 2)
    steps([small], 1)
    for t in range(3, turns + 1):
        steps(early, t)
    line_steps(early, 0)
    steps(others, 2)
    for t in range(3, turns + 1):
        steps(queries, t)
    line_steps(early, 1)
    line_steps(queries, 0)
    steps([small], 2)
    for t in range(3, turns + 1):
        steps(others, t)
        steps([small], t)
    tail = others + [small]
    for t in range(ne):
        line_steps(early, t + 2)
        line_steps(queries, t + 1)
        line_steps(tail, t)
    order = list(range(count))
    copies = []
    for a in order:
        copies.append(pltpu.make_async_copy(lines[a].own(), outs[a], out_sem.at[a]))
        copies[-1].start()
    for each in sums + lines:
        each.wait_sends()
    for copy in copies:
        copy.wait()


def finish(
    ne,
    nd,
    orders,
    normed,
    grads,
    tables,
    tokens,
    gain,
    grad_residual,
    weights,
    w_out,
    router_grad,
    gain_two_grad,
):
    rows, width = tokens.shape
    share = width // (ne * nd)
    columns = weights[1].shape[1]
    n_out = width // columns
    count = 2 * n_out + 3
    wide = [columns] * (count - 1) + [128]
    split = lambda v: v.reshape(ne, nd, share, v.shape[1])
    return pl.pallas_call(
        functools.partial(finish_body, ne, nd, tuple(map(tuple, orders)), n_out),
        out_shape=[jax.ShapeDtypeStruct((rows, width), F32)]
        + [jax.ShapeDtypeStruct((share, c), BF16) for c in wide],
        in_specs=[VMEM] * 9 + [ANY] * 5,
        out_specs=[VMEM] + [ANY] * count,
        scratch_shapes=[pltpu.VMEM((nd, ne, share, c), BF16) for c in wide]
        + [pltpu.VMEM((nd - 1, ne, share, c), BF16) for c in wide]
        + [pltpu.VMEM((2, ne, share, c), BF16) for c in wide]
        + [pltpu.VMEM(grads[1].shape, BF16)]
        + [pltpu.VMEM(w.shape, BF16) for w in weights]
        + [pltpu.VMEM((rows, width), F32)]
        + [
            DMA((count, ne)),
            DMA((4,)),
            DMA((count,)),
            DMA((count, nd - 1)),
            DMA((count, nd - 1)),
            DMA((count, 2, ne)),
            DMA((count, 2, ne)),
        ],
        compiler_params=pltpu.CompilerParams(
            vmem_limit_bytes=60 * 2**20, collective_id=4, has_side_effects=True
        ),
        cost_estimate=cost(45),
    )(
        normed,
        *grads,
        tables,
        tokens,
        gain,
        router_grad,
        gain_two_grad,
        grad_residual,
        *weights,
        split(w_out),
    )


def results_body(share, n_out, groups, *refs):
    refs = list(refs)

    def take(n):
        return [refs.pop(0) for _ in range(n)]

    residual_ref, mix_ref = take(2)
    halves = [take(groups) for _ in range(2)]
    dense = take(2 * n_out + 3)
    out_ref, d_out, d_query, d_key, d_value, router, gain_one, gain_two = take(8)
    gate, up, down = refs
    e = pl.program_id(0)

    @pl.when(e == 0)
    def _():
        out_ref[...] = (residual_ref[...] + mix_ref[...].astype(F32)).astype(BF16)
        width = dense[0].shape[1]
        for i in range(n_out):
            d_out[:, i * width : (i + 1) * width] = dense[i][...].astype(F32)
            d_query[:, i * width : (i + 1) * width] = dense[n_out + i][...].astype(F32)
        d_key[...] = dense[2 * n_out][...].astype(F32)
        d_value[...] = dense[2 * n_out + 1][...].astype(F32)
        small = dense[-1][...].astype(F32)
        router[...] = small[:, :EXPERTS]
        turned = small.T
        gain_one[...] = turned[EXPERTS : EXPERTS + 1]
        gain_two[...] = turned[EXPERTS + 1 : EXPERTS + 2]

    k = 0
    for first, second in zip(*halves):
        for m in range(first.shape[0]):

            @pl.when(e == k)
            def _(first=first, second=second, m=m):
                over = first.shape[1] - share
                gate[0] = first[m, :share].astype(F32)
                up[0, :over] = first[m, share:].astype(F32)
                up[0, over:] = second[m, : share - over].astype(F32)
                piece, columns = down.shape[1], second.shape[2]
                for j in range(down.shape[2] // columns):
                    at = share - over + j * piece
                    down[0, :, j * columns : (j + 1) * columns] = second[
                        m, at : at + piece
                    ].astype(F32)

            k += 1


def results(residual, mix, grads, dense, n_out, share, w_gate, w_down, nd, rows_share):
    rows, width = residual.shape
    n_exp, _, inner = w_gate.shape
    piece = w_down.shape[1] // nd
    ins = [residual, *mix, *grads[0], *grads[1], *dense]
    kv = dense[-2].shape[1]
    same = lambda v: pl.BlockSpec(v, lambda e: (0,) * len(v))
    outs = [
        ((rows, width), BF16),
        ((rows_share, width), F32),
        ((rows_share, width), F32),
        ((rows_share, kv), F32),
        ((rows_share, kv), F32),
        ((rows_share, EXPERTS), F32),
        ((1, rows_share), F32),
        ((1, rows_share), F32),
    ]
    experts_out = [((n_exp, share, inner), F32)] * 2 + [((n_exp, piece, width), F32)]
    return pl.pallas_call(
        functools.partial(results_body, share, n_out, len(grads[0])),
        grid=(n_exp,),
        out_shape=[jax.ShapeDtypeStruct(*v) for v in outs + experts_out],
        in_specs=[same(v.shape) for v in ins],
        out_specs=[same(v[0]) for v in outs]
        + [pl.BlockSpec((1,) + v[0][1:], lambda e: (e, 0, 0)) for v in experts_out],
        compiler_params=pltpu.CompilerParams(vmem_limit_bytes=60 * 2**20),
        cost_estimate=cost(6),
    )(*ins)


def per_device(
    tokens,
    segments,
    routes,
    first_gain,
    w_query,
    w_key,
    w_value,
    w_out,
    second_gain,
    w_router,
    w_gate,
    w_up,
    w_down,
    cotangent,
):
    micro, rows, width = tokens.shape
    ne, nd = lax.axis_size("ep"), lax.axis_size("dp")
    dp = lax.axis_index("dp")
    kv_width = KV_HEADS * HEAD_DIM
    every = micro * rows

    halfway = HEAD_DIM // 2
    frequency = ROPE_BASE ** (-(np.arange(halfway) * 2.0 / HEAD_DIM))
    angles = np.arange(nd * rows)[:, None] * frequency[None, :]
    lanes = 2 * HEAD_DIM // halfway
    sign = np.where(np.arange(2 * HEAD_DIM) % HEAD_DIM < halfway, -1.0, 1.0)
    tables = np.stack([np.tile(np.cos(angles), lanes), np.tile(np.sin(angles), lanes) * sign])
    tables = lax.dynamic_slice_in_dim(jnp.asarray(tables, F32), dp * rows, rows, axis=1)

    tokens_flat = tokens.reshape(every, width)
    gain_one = first_gain.reshape(1, width)
    normed_one, query_rot, key_rot, value_own = project(
        tokens_flat, gain_one, tables, w_query, w_key, w_value
    )

    ids = jnp.arange(128, dtype=jnp.int32)
    counts = jnp.sum((segments[:, 0, :, None] == ids).astype(F32), axis=1)
    counts = jnp.concatenate([counts, jnp.zeros((8 - micro, 128), F32)], axis=0)

    cot_own = cotangent.reshape(every, width)

    def around(value, k):
        return lax.ppermute(value, "ep", [(i, (i + k) % ne) for i in range(ne)])

    cots = [cot_own] + [around(cot_own, k) for k in range(1, ne)]
    key_all, value_all, count_all = gather(ne, nd, (key_rot, value_own, counts), (), 0, 25)

    totals = jnp.sum(count_all[:, :micro], axis=0)
    lower = (ids[None, None, :] < segments[:, 0, :, None]).astype(F32)
    starts = jnp.sum(lower * totals[:, None, :], axis=2).astype(jnp.int32)
    starts = starts.reshape(every, 1)
    routing = routes.reshape(every, routes.shape[2])
    hit = jnp.any(
        jnp.arange(EXPERTS, dtype=jnp.int32)[:, None, None] == routing[None], axis=2
    ).astype(F32)
    router = w_router.T
    attn_low, logs, residual, normed_two, gate_probs, normed_all, marked_all = attend(
        starts,
        query_rot,
        key_all,
        value_all,
        tokens_flat,
        w_out,
        second_gain.reshape(1, width),
        router,
        hit,
        micro,
        rows,
        ne,
        1,
    )
    orders = [order[:-1][::-1] for order in gather_orders(nd)]
    mix, grad_in, pair_dots, *grads = experts(
        normed_all.reshape(ne * every, width),
        cots,
        marked_all.reshape(ne * micro, EXPERTS, rows),
        w_gate,
        w_up,
        w_down,
        micro,
        rows,
        ne,
        nd,
        6,
    )
    kept, landed, last = grads[:2], grads[2:4], grads[4:]
    height = kept[0].shape[2]
    halves = [(slice(None), slice(i * height, (i + 1) * height)) for i in range(2)]
    skip = min(2, kept[0].shape[1])
    more = kept[0].shape[1] > skip
    head = (slice(None), slice(0, skip))
    *grads, grad_back, dots_all = reduce(
        ne,
        nd,
        [(last[k], orders[i], halves[i], None, False) for k in range(2) for i in range(2)]
        + [(kept[i], orders[i][1:], head, landed[i], False) for i in range(2)],
        ((grad_in.reshape(ne, every, width), None),),
        (pair_dots,),
        2,
        40,
    )
    grads_last, grads_head = grads[:4], grads[4:]
    mix = mix.reshape(ne, every, width)
    full = [[0] + order for order in orders]
    (
        grad_query,
        grad_residual,
        grad_w_out,
        grad_router,
        grad_gain_two,
        grad_key,
        grad_value,
        mix_own,
        *grads_more,
    ) = attend_back(
        starts,
        query_rot,
        key_all,
        value_all,
        logs,
        tables,
        cot_own,
        dots_all,
        gate_probs,
        grad_back,
        residual,
        second_gain.reshape(1, width),
        normed_two,
        attn_low,
        w_out,
        router,
        mix,
        [(kept[i], orders[i][1:], landed[i]) for i in range(2)] if more else [],
        full,
        skip,
        5,
    )
    grad_tokens, *dense = finish(
        ne,
        nd,
        full,
        normed_one,
        (grad_query, grad_key, grad_value),
        tables,
        tokens_flat,
        gain_one,
        grad_residual,
        (w_query, w_key, w_value),
        grad_w_out,
        grad_router,
        grad_gain_two,
    )
    (
        output,
        d_out,
        d_query,
        d_key,
        d_value,
        d_router,
        d_gain_one,
        d_gain_two,
        d_gate,
        d_up,
        d_down,
    ) = results(
        residual,
        (mix_own,),
        [
            [grads_head[i]]
            + ([grads_more[i]] if more else [])
            + [grads_last[i][None], grads_last[2 + i][None]]
            for i in range(2)
        ],
        dense,
        width // kv_width,
        width // nd,
        w_gate,
        w_down,
        nd,
        width // (ne * nd),
    )
    return (
        output.reshape(tokens.shape),
        grad_tokens.reshape(tokens.shape),
        d_gain_one.reshape(-1),
        d_query,
        d_key,
        d_value,
        d_out,
        d_gain_two.reshape(-1),
        d_router,
        d_gate,
        d_up,
        d_down,
    )


def solution(mesh):
    in_specs = (
        P(None, ("ep", "dp"), None),
        P(None, "ep", "dp"),
        P(None, ("ep", "dp"), None),
        P(),
        P(),
        P(),
        P(),
        P(),
        P(),
        P(),
        P("ep", None, None),
        P("ep", None, None),
        P("ep", None, None),
        P(None, ("ep", "dp"), None),
    )
    out_specs = (
        P(None, ("ep", "dp"), None),
        P(None, ("ep", "dp"), None),
        P(("ep", "dp")),
        P(("ep", "dp"), None),
        P(("ep", "dp"), None),
        P(("ep", "dp"), None),
        P(("ep", "dp"), None),
        P(("ep", "dp")),
        P(("ep", "dp"), None),
        P("ep", "dp", None),
        P("ep", "dp", None),
        P("ep", "dp", None),
    )
    return jax.shard_map(
        per_device, mesh=mesh, in_specs=in_specs, out_specs=out_specs, check_vma=False
    )
```

```python
import functools

import jax
import jax.numpy as jnp
import numpy as np
from jax import lax
from jax.experimental import pallas as pl
from jax.experimental.pallas import tpu as pltpu
from jax.sharding import PartitionSpec as P

HEADS = 16
KV_HEADS = 8
HEAD_DIM = 64
EXPERTS = 32
CAP = 64
SEGMENT_IDS = 4
EPSILON = 1e-06
ROPE_BASE = 10000.0
MASKED = -1e30
HIGHEST = lax.Precision.HIGHEST
MESH = pl.DeviceIdType.MESH
BF16 = jnp.bfloat16
F32 = jnp.float32
VMEM = pl.BlockSpec(memory_space=pltpu.VMEM)
ANY = pl.BlockSpec(memory_space=pl.ANY)
DMA = pltpu.SemaphoreType.DMA


def bit_count(n):
    return n.bit_length() - 1


def masks(bits):
    out = [0]
    for b in bits:
        out = out + [m | (1 << b) for m in out]
    return out


def gather_orders(n):
    bits = list(range(bit_count(n)))
    return (bits[1:] + bits[:1], bits[:0:-1] + bits[:1])


def greet(ep, dp, ne, nd):
    barrier = pltpu.get_barrier_semaphore()
    for k in range(1, ne):
        pl.semaphore_signal(
            barrier, inc=1, device_id={"ep": lax.rem(ep + k, ne)}, device_id_type=MESH
        )
    for b in range(bit_count(nd)):
        pl.semaphore_signal(
            barrier, inc=1, device_id={"dp": jnp.bitwise_xor(dp, 1 << b)}, device_id_type=MESH
        )
    pl.semaphore_wait(barrier, ne - 1 + bit_count(nd))


def remote(src, dst, send, recv, where):
    return pltpu.make_async_remote_copy(
        src_ref=src, dst_ref=dst, send_sem=send, recv_sem=recv, device_id=where, device_id_type=MESH
    )


class PairGather:
    def __init__(self, dp, nd, order, own, whole, send_sem, recv_sem):
        self.dp, self.order, self.own, self.whole = dp, order, own, whole
        self.send_sem, self.recv_sem = send_sem, recv_sem

    def copy(self, t, m):
        block = jnp.bitwise_xor(self.dp, m)
        k = (1 << t) - 1 + masks(self.order[:t]).index(m)
        return remote(
            self.own if m == 0 else self.whole.at[block],
            self.whole.at[block],
            self.send_sem.at[k],
            self.recv_sem.at[k],
            {"dp": jnp.bitwise_xor(self.dp, 1 << self.order[t])},
        )

    def start(self):
        for t in range(len(self.order)):
            self.copy(t, 0).start()

    def step(self, t):
        for m in masks(self.order[:t]):
            self.copy(t, m).wait_recv()
            for later in range(t + 1, len(self.order)):
                self.copy(later, m | (1 << self.order[t])).start()

    def wait_sends(self):
        for t in range(len(self.order)):
            for m in masks(self.order[:t]):
                self.copy(t, m).wait_send()


def cost(us):
    return pl.CostEstimate(flops=0, bytes_accessed=int(us * 3.0e6), transcendentals=0)


def add_into(ref, arrived):
    if len(ref.shape) > 2:

        @pl.loop(0, ref.shape[0])
        def _(i):
            add_into(ref.at[i], arrived.at[i])

    else:
        ref[...] = (ref[...].astype(F32) + arrived[...].astype(F32)).astype(ref.dtype)


class PairSum:
    def __init__(self, dp, order, loads, held, extra, landing, send_sem, recv_sem):
        self.dp, self.order, self.held, self.landing = dp, order, held, landing
        self.send_sem, self.recv_sem = send_sem, recv_sem
        self.extra, self.loads = extra, loads
        self.index = 0
        for b in order:
            side = jnp.bitwise_and(lax.shift_right_logical(dp, b), 1)
            self.index = self.index + (side << self.place(b))

    def place(self, bit):
        return sorted(self.order).index(bit)

    def copies(self, t):
        order = self.order
        partner = jnp.bitwise_xor(self.index, 1 << self.place(order[t]))
        first = sum(1 << (len(order) - 1 - i) for i in range(t))
        return [
            (
                m,
                first + j,
                remote(
                    self.held.at[jnp.bitwise_xor(partner, m)],
                    self.landing.at[first + j],
                    self.send_sem.at[first + j],
                    self.recv_sem.at[first + j],
                    {"dp": jnp.bitwise_xor(self.dp, 1 << order[t])},
                ),
            )
            for j, m in enumerate(masks([self.place(b) for b in order[t + 1 :]]))
        ]

    def load(self):
        for copy in self.loads:
            copy.start()

    def step(self, t):
        if t == 0:
            for copy in self.loads:
                copy.wait()
            if self.extra is not None:
                add_into(self.held, self.extra)
        elif t <= len(self.order):
            for m, k, copy in self.copies(t - 1):
                copy.wait_recv()
                add_into(self.held.at[jnp.bitwise_xor(self.index, m)], self.landing.at[k])
        if t < len(self.order):
            for m, k, copy in self.copies(t):
                copy.start()

    def own(self):
        return self.held.at[self.index]

    def wait_sends(self):
        for t in range(len(self.order)):
            for m, k, copy in self.copies(t):
                copy.wait_send()


class LineSum:
    def __init__(self, ep, ne, blocks, landing, send_sem, recv_sem):
        self.ep, self.ne, self.blocks, self.landing = ep, ne, blocks, landing
        self.send_sem, self.recv_sem = send_sem, recv_sem

    def copy(self, dest, way):
        k = 0 if way == 1 else 1
        return remote(
            self.blocks.at[dest],
            self.landing.at[k, dest],
            self.send_sem.at[k, dest],
            self.recv_sem.at[k, dest],
            {"ep": lax.rem(self.ep + way + self.ne, self.ne)},
        )

    def turn(self, t, way):
        ep, ne = self.ep, self.ne
        dest = ep + ne - 1 - t if way == 1 else ep + t - (ne - 1)
        has = dest <= ne - 1 if way == 1 else dest >= 0
        inner = ep >= 1 if way == 1 else ep <= ne - 2
        return dest, has, inner

    def step(self, t):
        for way in (1, -1):
            dest, has, inner = self.turn(t, way)

            @pl.when(has & inner)
            def _(way=way, dest=dest):
                self.copy(dest, way).wait_recv()
                add_into(self.blocks.at[dest], self.landing.at[0 if way == 1 else 1, dest])

            if t < self.ne - 1:

                @pl.when(has)
                def _(way=way, dest=dest):
                    self.copy(dest, way).start()

    def own(self):
        return self.blocks.at[self.ep]

    def wait_sends(self):
        for t in range(self.ne - 1):
            for way in (1, -1):
                dest, has, inner = self.turn(t, way)

                @pl.when(has)
                def _(way=way, dest=dest):
                    self.copy(dest, way).wait_send()


class SpreadSum:
    def __init__(self, ep, ne, blocks, landing, send_sem, recv_sem):
        self.ep, self.blocks, self.landing = ep, blocks, landing
        self.copies = []
        for k in range(1, ne):
            to = lax.rem(ep + k, ne)
            self.copies.append(
                remote(
                    blocks.at[to],
                    landing.at[k - 1],
                    send_sem.at[k - 1],
                    recv_sem.at[k - 1],
                    {"ep": to},
                )
            )

    def step(self, t):
        if t == 0:
            for copy in self.copies:
                copy.start()
        elif t == 1:
            total = self.blocks[self.ep].astype(F32)
            for k, copy in enumerate(self.copies):
                copy.wait_recv()
                total = total + self.landing[k].astype(F32)
            self.blocks[self.ep] = total.astype(BF16)

    def own(self):
        return self.blocks.at[self.ep]

    def wait_sends(self):
        for copy in self.copies:
            copy.wait_send()


def shape_at(array, where):
    return tuple(len(range(*w.indices(n))) for w, n in zip(where, array.shape)) + array.shape[len(where) :]


def reduce_body(ne, nd, pairs, line_parts, n_swap, *refs):
    refs = list(refs)

    def take(n):
        return [refs.pop(0) for _ in range(n)]

    n_pair, n_line = len(pairs), len(line_parts)
    n_extra = sum(p[2] for p in pairs)
    n_both = sum(p[3] for p in pairs)
    n_sum = n_pair + n_line
    ins, extra_ins, swap_ins = take(n_sum), take(n_extra), take(n_swap)
    outs, swap_outs = take(n_sum), take(n_swap)
    held, extras, pair_in = take(n_sum), take(n_extra), take(n_pair)
    both_in, line_in = take(n_both), take(n_line)
    load_sem, out_sem, dp_send, dp_recv, ep_send, ep_recv, swap_send, swap_recv = refs
    ep, dp = lax.axis_index("ep"), lax.axis_index("dp")
    sums, then = [], []
    for a, (order, where, has_extra, both) in enumerate(pairs):
        targets = [(ins[a], held[a])]
        extra = extras.pop(0) if has_extra else None
        if has_extra:
            targets.append((extra_ins.pop(0), extra))
        loads = [
            pltpu.make_async_copy(src.at[where] if where else src, dst, load_sem.at[a, i])
            for i, (src, dst) in enumerate(targets)
        ]
        sums.append(
            PairSum(dp, order, loads, held[a], extra, pair_in[a], dp_send.at[a], dp_recv.at[a])
        )
        if both:
            i = len(then)
            then.append(
                LineSum(ep, ne, sums[a].own(), both_in[i], ep_send.at[i], ep_recv.at[i])
            )
    lines, line_loads = [], []
    for i in range(n_line):
        a = n_pair + i
        src = ins[a].at[line_parts[i]] if line_parts[i] else ins[a]
        line_loads.append(pltpu.make_async_copy(src, held[a], load_sem.at[a, 0]))
        lines.append(
            LineSum(
                ep, ne, held[a], line_in[i], ep_send.at[n_both + i], ep_recv.at[n_both + i]
            )
        )
    for copy in line_loads:
        copy.start()
    for each in sums:
        each.load()
    greet(ep, dp, ne, nd)
    swaps = []
    for a in range(n_swap):
        src, dst = swap_ins[a], swap_outs[a]
        own = pltpu.make_async_copy(src.at[ep], dst.at[ep], load_sem.at[n_sum + a, 0])
        own.start()
        swaps.append(own)
        for k in range(1, ne):
            to = lax.rem(ep + k, ne)
            copy = remote(
                src.at[to], dst.at[ep], swap_send.at[a, k - 1], swap_recv.at[a, k - 1], {"ep": to}
            )
            copy.start()
            swaps.append(copy)
    for copy in line_loads:
        copy.wait()
    steps = max([len(p[0]) + 1 for p in pairs] + [ne if n_line else 0])
    for t in range(steps):
        if t < ne:
            for each in lines:
                each.step(t)
        for each in sums:
            each.step(t)
    for t in range(ne):
        for each in then:
            each.step(t)
    results, after = [], iter(then)
    for a in range(n_sum):
        if a >= n_pair:
            src = lines[a - n_pair].own()
        else:
            src = next(after).own() if pairs[a][3] else sums[a].own()
        copy = pltpu.make_async_copy(src, outs[a], out_sem.at[a])
        copy.start()
        results.append(copy)
    for each in sums + then + lines:
        each.wait_sends()
    for copy in swaps + results:
        copy.wait()


def reduce(ne, nd, pairs, lines, swaps, collective, us):
    line_parts = tuple(where for _, where in lines)
    line_shapes = [shape_at(v, where) if where else v.shape for v, where in lines]
    lines = [v for v, _ in lines]
    arrays = [p[0] for p in pairs] + list(lines)
    extras = [p[3] for p in pairs if p[3] is not None]
    kinds = tuple((tuple(p[1]), p[2], p[3] is not None, p[4]) for p in pairs)
    shapes = [shape_at(p[0], p[2]) if p[2] else p[0].shape for p in pairs]
    boths = [s for s, p in zip(shapes, pairs) if p[4]]
    results = [s[2:] if p[4] else s[1:] for s, p in zip(shapes, pairs)]
    results += [s[1:] for s in line_shapes]
    scratch = shapes + line_shapes
    scratch += [s for s, p in zip(shapes, pairs) if p[3] is not None]
    scratch += [(s[0] - 1,) + s[1:] for s in shapes]
    scratch += [(2,) + s[1:] for s in boths] + [(2,) + s for s in line_shapes]
    some = lambda n: max(n, 1)
    line_count = some(len(lines) + len(boths))
    deep = max([s[0] - 1 for s in shapes] + [1])
    return pl.pallas_call(
        functools.partial(reduce_body, ne, nd, kinds, line_parts, len(swaps)),
        out_shape=[jax.ShapeDtypeStruct(s, BF16) for s in results]
        + [jax.ShapeDtypeStruct(v.shape, v.dtype) for v in swaps],
        in_specs=[ANY] * (len(arrays) + len(extras) + len(swaps)),
        out_specs=[ANY] * (len(arrays) + len(swaps)),
        scratch_shapes=[pltpu.VMEM(s, BF16) for s in scratch]
        + [
            DMA((len(arrays) + len(swaps), 2)),
            DMA((len(arrays),)),
            DMA((some(len(pairs)), deep)),
            DMA((some(len(pairs)), deep)),
            DMA((line_count, 2, ne)),
            DMA((line_count, 2, ne)),
            DMA((some(len(swaps)), ne - 1)),
            DMA((some(len(swaps)), ne - 1)),
        ],
        compiler_params=pltpu.CompilerParams(
            collective_id=collective, has_side_effects=True, vmem_limit_bytes=60 * 2**20
        ),
        cost_estimate=cost(us),
    )(*arrays, *extras, *swaps)


def dot(a, b, dims=((1,), (0,))):
    return lax.dot_general(a, b, (dims, ((), ())), preferred_element_type=F32)


def expert_body(ne, nd, micro, rows, *refs):
    cots, refs = refs[:ne], refs[ne:]
    normed_ref, probs_ref, gate_ref, up_ref, down_ref = refs[:5]
    mix_ref, grad_ref, dots_ref = refs[5:8]
    kept, landed, whole = refs[8:10], refs[10:12], refs[12:14]
    rows_in, cots_in, picks, first, second, chances, sides, arrived, leaving = refs[14:23]
    load_sem, store_sem, send_sem, recv_sem, free_sem, far_send, far_recv = refs[23:]
    e = pl.program_id(0)
    last = pl.num_programs(0) - 1
    ep, dp = lax.axis_index("ep"), lax.axis_index("dp")
    other = {"dp": jnp.bitwise_xor(dp, 1)}
    every = micro * rows
    blocks = ne * micro
    width = first.shape[1]
    n_exp = rows_in.shape[1]

    core = jnp.bitwise_and(dp, 1)
    keep, send = sides.at[core], sides.at[1 - core]

    def exchange():
        return remote(send, arrived, send_sem, recv_sem, other)

    def loads():
        out = [
            pltpu.make_async_copy(normed_ref, first, load_sem.at[ne]),
            pltpu.make_async_copy(
                probs_ref.at[:, pl.ds(pl.multiple_of(ep * n_exp, n_exp), n_exp)],
                chances,
                load_sem.at[ne + 1],
            ),
        ]
        for k in range(ne):
            at = pl.multiple_of(lax.rem(ep - k + ne, ne) * every, every)
            out.append(
                pltpu.make_async_copy(cots[k], second.at[pl.ds(at, every)], load_sem.at[k])
            )
        return out

    def block_at(s):
        return pl.ds(pl.multiple_of(s * rows, rows), rows)

    def returned(t):
        k, m = t // micro, lax.rem(t, micro)
        return lax.rem(ep + k, ne) * micro + m

    def stores(t):
        s = returned(t)
        return (
            pltpu.make_async_copy(
                first.at[block_at(s)], mix_ref.at[block_at(s)], store_sem.at[0, t]
            ),
            pltpu.make_async_copy(
                second.at[block_at(s)], grad_ref.at[block_at(s)], store_sem.at[1, t]
            ),
        )

    def far(i, n):
        return remote(
            leaving.at[i, lax.rem(n, leaving.shape[1])],
            landed[i].at[:, n],
            far_send.at[i, lax.rem(n, leaving.shape[1])],
            far_recv.at[i, n],
            {"dp": jnp.bitwise_xor(dp, 1 << first_bits(nd)[i])},
        )

    def last_copy(k):
        return pltpu.make_async_copy(keep, whole[k], load_sem.at[k])

    def collect():
        exchange().wait_recv()
        pieces, height, slots = sides.shape[1], leaving.shape[3], leaving.shape[1]
        n = e - 1
        early = n_exp - 2

        @pl.when(n < early)
        def _():
            @pl.when(n >= slots)
            def _():
                for i in range(2):
                    far(i, n - slots).wait_send()

            def piece(i, at, other_side):
                bit = first_bits(nd)[i]
                mine = jnp.bitwise_and(lax.shift_right_logical(dp, bit), 1)
                side = 1 - mine if other_side else mine
                low = (1 << (bit - 1)) - 1
                j = ((at & ~low) << 1 | (at & low)) + (side << (bit - 1))
                part = slice(i * height, (i + 1) * height)
                return (keep[j, part].astype(F32) + arrived[j, part].astype(F32)).astype(BF16)

            for i in range(2):
                for at in range(pieces // 2):
                    leaving[i, lax.rem(n, slots), at] = piece(i, at, True)
                far(i, n).start()
            for i in range(2):
                for at in range(pieces // 2):
                    kept[i][at, 0] = piece(i, at, False)

        for k in range(2):

            @pl.when(n == early + k)
            def _(k=k):
                add_into(keep, arrived)
                last_copy(k).start()

    @pl.when(e == 0)
    def _():
        for copy in loads():
            copy.start()
        barrier = pltpu.get_barrier_semaphore()
        met = [0] + sorted(set(first_bits(nd)))
        for bit in met:
            pl.semaphore_signal(
                barrier,
                inc=1,
                device_id={"dp": jnp.bitwise_xor(dp, 1 << bit)},
                device_id_type=MESH,
            )
        pl.semaphore_wait(barrier, len(met))
        before = lax.broadcasted_iota(jnp.int32, (rows, rows), 0)
        after = lax.broadcasted_iota(jnp.int32, (rows, rows), 1)
        earlier = (before < after).astype(BF16)
        slot = lax.broadcasted_iota(jnp.int32, (n_exp, CAP, rows), 1)
        for copy in loads():
            copy.wait()

        @pl.loop(0, blocks)
        def _(s):
            at = block_at(s)
            probs = chances[s]
            hit = probs >= 0.0
            rank = dot(hit.astype(BF16), earlier)
            rank = jnp.where(hit, rank, -1.0).astype(jnp.int32)
            pick = jnp.broadcast_to(rank[:, None, :], (n_exp, CAP, rows)) == slot
            pick_f = pick.astype(F32)
            flat = pick_f.reshape(n_exp * CAP, rows).astype(BF16)
            picks[s] = flat
            rows_in[s] = dot(flat, first[at, :]).astype(BF16).reshape(n_exp, CAP, width)
            cots_in[s] = dot(flat, second[at, :]).astype(BF16).reshape(n_exp, CAP, width)

    @pl.when(e < last)
    def _():
        x = rows_in[:, e].reshape(blocks * CAP, width)
        c = cots_in[:, e].reshape(blocks * CAP, width)
        flat = picks[:, pl.ds(pl.multiple_of(e * CAP, CAP), CAP), :].astype(F32)
        p = jnp.sum(flat * chances[:, pl.ds(e, 1), :], axis=2, keepdims=True)
        p = p.reshape(blocks * CAP, 1)
        w_gate, w_up, w_down = gate_ref[0], up_ref[0], down_ref[0]
        gate_pre = dot(x, w_gate)
        up_pre = dot(x, w_up)
        back = dot(c, w_down, ((1,), (1,)))

        @pl.when(e > 0)
        def _():
            collect()
            pl.semaphore_signal(free_sem, inc=1, device_id=other, device_id_type=MESH)

        sigma = jax.nn.sigmoid(gate_pre)
        silu = gate_pre * sigma
        hidden = (silu * up_pre).astype(BF16)
        out = dot(hidden, w_down) * p
        wide = hidden.astype(F32)
        pair = jnp.sum(wide * back, axis=1, keepdims=True)
        back = back * p
        grad_up = (back * silu).astype(BF16)
        grad_gate = (back * up_pre * (sigma * (1.0 + gate_pre * (1.0 - sigma)))).astype(BF16)
        scaled = (wide * p).astype(BF16)
        grad_x = dot(grad_gate, w_gate, ((1,), (1,))) + dot(grad_up, w_up, ((1,), (1,)))
        pair = jnp.sum(flat * pair.reshape(blocks, CAP, 1), axis=1)
        dots_ref[:, 0] = pair.reshape(ne, micro, rows)

        @pl.when(e > 0)
        def _():
            exchange().wait_send()
            pl.semaphore_wait(free_sem, 1)

        @pl.when(e == n_exp - 1)
        def _():
            last_copy(0).wait()

        def split(value, offset):
            value = value.astype(BF16)
            piece, columns = value.shape[0] // nd, sides.shape[3]

            for i in range(nd):
                for j in range(value.shape[1] // columns):
                    at = offset + j * piece
                    sides[i % 2, i // 2, at : at + piece] = value[
                        i * piece : (i + 1) * piece, j * columns : (j + 1) * columns
                    ]

        share = width // nd
        split(dot(scaled, c, ((0,), (0,))), 2 * share)
        split(dot(x, grad_gate, ((0,), (0,))), 0)
        split(dot(x, grad_up, ((0,), (0,))), share)
        exchange().start()

        rows_in[:, e] = grad_x.astype(BF16).reshape(blocks, CAP, width)
        cots_in[:, e] = out.astype(BF16).reshape(blocks, CAP, width)

    @pl.when(e == last)
    def _():
        @pl.loop(0, blocks)
        def _(t):
            s = returned(t)
            at = block_at(s)
            flat = picks[s]
            for done, slots in ((first, cots_in), (second, rows_in)):
                value = dot(flat, slots[s].reshape(n_exp * CAP, width), ((0,), (0,)))
                done[at, :] = value.astype(BF16)
            for copy in stores(t):
                copy.start()

            @pl.when(t == 1)
            def _():
                collect()
                exchange().wait_send()

        @pl.loop(0, blocks)
        def _(t):
            for copy in stores(t):
                copy.wait()

        last_copy(1).wait()
        early, slots = n_exp - 2, leaving.shape[1]
        for i in range(2):
            for n in range(max(early - slots, 0), early):
                far(i, n).wait_send()

            @pl.loop(0, early)
            def _(n, i=i):
                far(i, n).wait_recv()


def first_bits(nd):
    return [order[-2] for order in gather_orders(nd)]


def experts(normed, cots, probs, w_gate, w_up, w_down, micro, rows, ne, nd, collective):
    n_exp, width, inner = w_gate.shape
    blocks = ne * micro
    half = nd // 2
    packed = 2 * width // nd + (inner // nd) * (width // inner)
    full = (blocks * rows, width)
    weight = lambda e: (jnp.minimum(e, n_exp - 1), 0, 0)
    early = n_exp - 2
    part = (half // 2, early, packed // 2, inner)
    kept = pl.BlockSpec(
        (half // 2, 1, packed // 2, inner), lambda e: (0, jnp.clip(e - 1, 0, early - 1), 0, 0)
    )
    last = (half, packed, inner)
    return pl.pallas_call(
        functools.partial(expert_body, ne, nd, micro, rows),
        grid=(n_exp + 1,),
        in_specs=[ANY] * (ne + 2)
        + [
            pl.BlockSpec((1, width, inner), weight),
            pl.BlockSpec((1, width, inner), weight),
            pl.BlockSpec((1, inner, width), weight),
        ],
        out_specs=[
            ANY,
            ANY,
            pl.BlockSpec((ne, 1, micro, rows), lambda e: (0, jnp.minimum(e, n_exp - 1), 0, 0)),
            kept,
            kept,
            ANY,
            ANY,
            ANY,
            ANY,
        ],
        scratch_shapes=[
            pltpu.VMEM((blocks, n_exp, CAP, width), BF16),
            pltpu.VMEM((blocks, n_exp, CAP, width), BF16),
            pltpu.VMEM((blocks, n_exp * CAP, rows), BF16),
            pltpu.VMEM(full, BF16),
            pltpu.VMEM(full, BF16),
            pltpu.VMEM((blocks, n_exp, rows), F32),
            pltpu.VMEM((2, half, packed, inner), BF16),
            pltpu.VMEM((half, packed, inner), BF16),
            pltpu.VMEM((2, 2 if early > 2 else 1, half // 2, packed // 2, inner), BF16),
            DMA((ne + 2,)),
            DMA((2, blocks)),
            DMA,
            DMA,
            pltpu.SemaphoreType.REGULAR,
            DMA((2, 2)),
            DMA((2, early)),
        ],
        out_shape=[
            jax.ShapeDtypeStruct(full, BF16),
            jax.ShapeDtypeStruct(full, BF16),
            jax.ShapeDtypeStruct((ne, n_exp, micro, rows), F32),
        ]
        + [jax.ShapeDtypeStruct(part, BF16)] * 4
        + [jax.ShapeDtypeStruct(last, BF16)] * 2,
        compiler_params=pltpu.CompilerParams(
            vmem_limit_bytes=63 * 2**20,
            dimension_semantics=("arbitrary",),
            collective_id=collective,
            has_side_effects=True,
        ),
        cost_estimate=cost(75),
    )(*cots, normed, probs, w_gate, w_up, w_down)


def rms_scale(values):
    return lax.rsqrt(jnp.mean(values * values, axis=-1, keepdims=True) + EPSILON)


def partner(x):
    lane = lax.broadcasted_iota(jnp.int32, x.shape, 1)
    half = HEAD_DIM // 2
    low = lax.rem(lane, HEAD_DIM) < half
    return jnp.where(low, pltpu.roll(x, x.shape[1] - half, 1), pltpu.roll(x, half, 1))


def turn(x, cosine, sine):
    return x * cosine + partner(x) * sine


def repeated(table, rows):
    return jnp.concatenate([table] * (rows // table.shape[0]), axis=0)


def project_body(ne, nd, *refs):
    tokens_ref, gain_ref, segments_ref, tables_all, wq_ref, wk_ref, wv_ref = refs[:7]
    n_ref, q_ref, tables_ref, starts_ref, key_all, value_all = refs[7:13]
    wq, wk, wv, key_own, value_own, count_own, count_all = refs[13:20]
    sem, own_sem, send_sem, recv_sem = refs[20:]
    ep, dp = lax.axis_index("ep"), lax.axis_index("dp")
    micro, rows = segments_ref.shape
    loads = [
        pltpu.make_async_copy(src, dst, sem.at[i])
        for i, (src, dst) in enumerate(
            (
                (tables_all.at[:, pl.ds(pl.multiple_of(dp * rows, rows), rows)], tables_ref),
                (wk_ref, wk),
                (wv_ref, wv),
                (wq_ref, wq),
            )
        )
    ]
    for copy in loads:
        copy.start()
    arrays = ((count_own, count_all), (key_own, key_all), (value_own, value_all))
    gathers = [
        PairGather(
            dp, nd, gather_orders(nd)[i // 2], own, whole, send_sem.at[i], recv_sem.at[i]
        )
        for i, (own, whole) in enumerate(arrays)
    ]
    own_copies = [
        pltpu.make_async_copy(own, whole.at[dp], own_sem.at[i])
        for i, (own, whole) in enumerate(arrays)
    ]

    def leave(i):
        gathers[i].start()
        own_copies[i].start()

    segments = segments_ref[...]
    lane = lax.broadcasted_iota(jnp.int32, (micro, count_own.shape[1]), 1)
    counts = jnp.zeros(lane.shape, F32)
    for i in range(SEGMENT_IDS):
        held = jnp.sum((segments == i).astype(F32), axis=1, keepdims=True)
        counts = counts + jnp.where(lane == i, held, 0.0)
    count_own[...] = jnp.zeros_like(count_own)
    count_own[:micro] = counts
    greet(ep, dp, ne, nd)
    leave(0)

    x = tokens_ref[...].astype(F32)
    n_ref[...] = (x * rms_scale(x) * gain_ref[...]).astype(BF16)
    normed = n_ref[...]
    loads[0].wait()
    cosine, sine = (repeated(tables_ref[i], x.shape[0]) for i in range(2))
    tile = 256
    steps = (
        (wk, key_own, True, 1),
        (wv, value_own, False, 2),
        (wq, q_ref, True, None),
    )
    for copy, (w, out, turned, array) in zip(loads[1:], steps):
        copy.wait()
        for c in range(0, w.shape[1], tile):
            y = dot(normed, w[:, c : c + tile])
            if turned:
                for i in range(0, tile, 128):
                    out[:, c + i : c + i + 128] = turn(y[:, i : i + 128], cosine, sine).astype(BF16)
            else:
                out[:, c : c + tile] = y.astype(BF16)
        if array is not None:
            leave(array)
    for t in range(bit_count(nd)):
        for each in gathers:
            each.step(t)
    for copy in own_copies:
        copy.wait()
    totals = jnp.sum(count_all[...], axis=0)
    padded = jnp.concatenate([segments, jnp.zeros((8 - micro, rows), jnp.int32)], axis=0)
    column = padded.astype(F32).T
    ids = lax.broadcasted_iota(jnp.int32, (rows, totals.shape[1]), 1).astype(F32)
    for m in range(micro):
        lower = jnp.where(ids < column[:, m : m + 1], totals[m : m + 1], 0.0)
        starts_ref[m * rows : (m + 1) * rows] = jnp.sum(lower, axis=1, keepdims=True).astype(
            jnp.int32
        )
    for each in gathers:
        each.wait_sends()


def project(tokens, gain, segments, tables, w_query, w_key, w_value, ne, nd, collective):
    rows, width = tokens.shape
    micro, count = segments.shape
    keys = jax.ShapeDtypeStruct((nd, rows, w_key.shape[1]), BF16)
    return pl.pallas_call(
        functools.partial(project_body, ne, nd),
        out_shape=[
            jax.ShapeDtypeStruct((rows, width), BF16),
            jax.ShapeDtypeStruct((rows, w_query.shape[1]), BF16),
            jax.ShapeDtypeStruct((2, count, tables.shape[2]), F32),
            jax.ShapeDtypeStruct((rows, 1), jnp.int32),
            keys,
            keys,
        ],
        in_specs=[VMEM] * 3 + [ANY] * 4,
        out_specs=[VMEM] * 4 + [ANY] * 2,
        scratch_shapes=[pltpu.VMEM(w.shape, BF16) for w in (w_query, w_key, w_value)]
        + [pltpu.VMEM(keys.shape[1:], BF16)] * 2
        + [pltpu.VMEM((8, 128), F32), pltpu.VMEM((nd, 8, 128), F32)]
        + [DMA((4,)), DMA((3,)), DMA((3, nd - 1)), DMA((3, nd - 1))],
        compiler_params=pltpu.CompilerParams(
            vmem_limit_bytes=60 * 2**20, collective_id=collective, has_side_effects=True
        ),
        cost_estimate=cost(26),
    )(tokens, gain, segments, tables, w_query, w_key, w_value)


def spread(x):
    lane = lax.broadcasted_iota(jnp.int32, (x.shape[0], 128), 1)
    low = lane < HEAD_DIM
    zero = jnp.zeros((), x.dtype)
    first, second = x[:, :128], x[:, 128:]
    return jnp.concatenate(
        [
            jnp.where(low, first, zero),
            jnp.where(low, pltpu.roll(first, HEAD_DIM, 1), zero),
            jnp.where(low, zero, pltpu.roll(second, HEAD_DIM, 1)),
            jnp.where(low, zero, second),
        ],
        axis=0,
    )


def gathered(x, rows):
    lane = lax.broadcasted_iota(jnp.int32, (rows, 128), 1)
    low = lane < HEAD_DIM
    h = [x[i * rows : (i + 1) * rows] for i in range(4)]
    return jnp.concatenate(
        [
            jnp.where(low, h[0], pltpu.roll(h[1], HEAD_DIM, 1)),
            jnp.where(low, pltpu.roll(h[2], HEAD_DIM, 1), h[3]),
        ],
        axis=1,
    )


def window_of(dp, span):
    return jnp.maximum(dp - (span - 1), 0)


def window_scores(dp, span, rows, starts_ref, q, k):
    keys = k.shape[0]
    scores = dot(q, k, ((1,), (1,))).reshape(4, rows, keys)
    key_pos = window_of(dp, span) * rows + lax.broadcasted_iota(jnp.int32, (rows, keys), 1)
    query_pos = dp * rows + lax.broadcasted_iota(jnp.int32, (rows, keys), 0)
    allowed = (key_pos <= query_pos) & (key_pos >= starts_ref[...])
    return jnp.where(allowed[None], scores, MASKED).reshape(4 * rows, keys)


def in_window(ref, dp, span):
    block = ref[pl.ds(window_of(dp, span), span)]
    return block.reshape(span * block.shape[1], block.shape[2])


SCALE = HEAD_DIM ** (-0.5)


class LineGather:
    def __init__(self, ep, ne, own, whole, send_sem, recv_sem):
        self.ep, self.ne, self.own, self.whole = ep, ne, own, whole
        self.send_sem, self.recv_sem = send_sem, recv_sem

    def copy(self, m, s, way):
        shard = lax.rem(self.ep - way * s + self.ne, self.ne)
        k = 0 if way == 1 else 1
        return remote(
            self.own.at[m] if s == 0 else self.whole.at[shard, m],
            self.whole.at[shard, m],
            self.send_sem.at[m, k, s],
            self.recv_sem.at[m, k, s],
            {"ep": lax.rem(self.ep + way + self.ne, self.ne)},
        )

    def sends(self, s, way):
        ep, ne = self.ep, self.ne
        return (ep >= s) & (ep < ne - 1) if way == 1 else (ep + s <= ne - 1) & (ep >= 1)

    def receives(self, s, way):
        return self.ep >= 1 + s if way == 1 else self.ep + 1 + s <= self.ne - 1

    def step(self, m, s):
        for way in (1, -1):
            if s > 0:

                @pl.when(self.receives(s - 1, way))
                def _(way=way):
                    self.copy(m, s - 1, way).wait_recv()

            if s < self.ne - 1:

                @pl.when(self.sends(s, way))
                def _(way=way):
                    self.copy(m, s, way).start()

    def wait_sends(self, m):
        for s in range(self.ne - 1):
            for way in (1, -1):

                @pl.when(self.sends(s, way))
                def _(s=s, way=way):
                    self.copy(m, s, way).wait_send()


def attend_body(span, ne, nd, micro, *refs):
    starts_ref, q_ref, k_ref, v_ref, tokens_ref, wo_ref, gain_ref, router_ref, hit_ref = refs[:9]
    out_ref, log_ref, res_ref, normed_ref, probs_ref, normed_all, marked_all = refs[9:16]
    attn, normed_own, marked_own, own_sem, send_sem, recv_sem = refs[16:]
    ep, dp = lax.axis_index("ep"), lax.axis_index("dp")
    m, h = pl.program_id(0), pl.program_id(1)
    final = pl.num_programs(1) - 1
    rows = q_ref.shape[0]
    lines = [
        LineGather(ep, ne, own, whole, send_sem.at[i], recv_sem.at[i])
        for i, (own, whole) in enumerate(((normed_own, normed_all), (marked_own, marked_all)))
    ]

    def hop(batch, s):
        for line in lines:
            line.step(batch, s)

    @pl.when((m == 0) & (h == 0))
    def _():
        greet(ep, dp, ne, nd)

    q = spread(q_ref[...].astype(F32) * SCALE).astype(BF16)
    scores = window_scores(dp, span, rows, starts_ref, q, in_window(k_ref, dp, span))
    top = jnp.max(scores, axis=1, keepdims=True)
    terms = jnp.exp(scores - top)
    total = jnp.sum(terms, axis=1, keepdims=True)
    log_ref[0, 0] = top + jnp.log(total)
    weights = (terms * (1.0 / total)).astype(BF16)
    out = gathered(dot(weights, in_window(v_ref, dp, span)), rows).astype(BF16)
    out_ref[...] = out
    attn[:, pl.ds(pl.multiple_of(h * out.shape[1], out.shape[1]), out.shape[1])] = out

    def own_copies(batch):
        return [
            pltpu.make_async_copy(line.own.at[batch], line.whole.at[ep, batch], own_sem.at[i, batch])
            for i, line in enumerate(lines)
        ]

    for batch in range(micro):

        @pl.when((m == batch) & (h == final))
        def _(batch=batch):
            for earlier in range(batch):
                hop(earlier, batch - earlier)
            residual = tokens_ref[...].astype(F32) + dot(attn[...], wo_ref[...])
            res_ref[...] = residual
            normed = (residual * rms_scale(residual) * gain_ref[...]).astype(BF16)
            normed_ref[...] = normed
            normed_own[batch] = normed
            hit = hit_ref[...] > 0.0
            logits = jnp.where(hit, dot(router_ref[...], normed, ((1,), (1,))), MASKED)
            terms = jnp.exp(logits - jnp.max(logits, axis=0, keepdims=True))
            terms = jnp.where(hit, terms, 0.0)
            probs = terms / jnp.sum(terms, axis=0, keepdims=True)
            probs_ref[...] = probs
            marked_own[batch] = jnp.where(hit, probs, -1.0)
            hop(batch, 0)
            for copy in own_copies(batch):
                copy.start()
            if batch == micro - 1:
                for t in range(1, ne + micro - 1):
                    for each in range(micro):
                        s = t + micro - 1 - each
                        if s < ne:
                            hop(each, s)
                for each in range(micro):
                    for line in lines:
                        line.wait_sends(each)
                    for copy in own_copies(each):
                        copy.wait()


def attention_specs(micro, rows, nd):
    pairs = KV_HEADS // 2
    mine = pl.BlockSpec((rows, 4 * HEAD_DIM), lambda m, h, *_: (m, h))
    theirs = pl.BlockSpec((nd, rows, 2 * HEAD_DIM), lambda m, h, *_: (0, m, h))
    column = pl.BlockSpec((rows, 1), lambda m, h, *_: (m, 0))
    logs = pl.BlockSpec((1, 1, 4 * rows, 1), lambda m, h, *_: (m, h, 0, 0))
    log_shape = jax.ShapeDtypeStruct((micro, pairs, 4 * rows, 1), F32)
    return (micro, pairs), mine, theirs, column, logs, log_shape


def attend(
    starts, queries, keys, values, tokens, w_out, gain, router, hit, micro, rows, ne, collective
):
    nd, width = keys.shape[0], tokens.shape[1]
    grid, mine, theirs, column, logs, log_shape = attention_specs(micro, rows, nd)
    one = pl.Buffered(1)
    whole = lambda v: pl.BlockSpec(v.shape, lambda m, h: (0, 0), pipeline_mode=one)
    wide = pl.BlockSpec((rows, width), lambda m, h: (m, 0))
    chosen = pl.BlockSpec((hit.shape[0], rows), lambda m, h: (0, m))
    every = micro * rows
    return pl.pallas_call(
        functools.partial(attend_body, nd // 2 + 1, ne, nd, micro),
        grid=grid,
        in_specs=[column, mine, theirs, theirs, wide, whole(w_out), whole(gain), whole(router)]
        + [chosen],
        out_specs=[mine, logs, wide, wide, chosen, ANY, ANY],
        out_shape=[
            jax.ShapeDtypeStruct(queries.shape, BF16),
            log_shape,
            jax.ShapeDtypeStruct((every, width), F32),
            jax.ShapeDtypeStruct((every, width), BF16),
            jax.ShapeDtypeStruct(hit.shape, F32),
            jax.ShapeDtypeStruct((ne, micro, rows, width), BF16),
            jax.ShapeDtypeStruct((ne, micro, hit.shape[0], rows), F32),
        ],
        scratch_shapes=[
            pltpu.VMEM((rows, width), BF16),
            pltpu.VMEM((micro, rows, width), BF16),
            pltpu.VMEM((micro, hit.shape[0], rows), F32),
            DMA((2, micro)),
            DMA((2, micro, 2, ne - 1)),
            DMA((2, micro, 2, ne - 1)),
        ],
        compiler_params=pltpu.CompilerParams(
            vmem_limit_bytes=60 * 2**20, collective_id=collective, has_side_effects=True
        ),
        cost_estimate=cost(50),
    )(starts, queries, keys, values, tokens, w_out, gain, router, hit)


def attend_back_body(span, ne, nd, micro, skip, full, orders, *refs):
    refs = list(refs)

    def take(n):
        return [refs.pop(0) for _ in range(n)]

    starts_ref, q_ref, k_ref, v_ref, log_ref, tables_ref = take(6)
    cot_ref, dots_ref, probs_ref, grad_ref, residual_ref, gain_ref, normed_ref, attn_ref = take(8)
    wo_ref, router_ref, mix_ref = take(3)
    n = len(orders)
    sources, extras = take(n), take(n)
    dq_ref, res_out, wo_out, router_out, gain_out, dk_out, dv_out, mix_out = take(8)
    outs = take(n)
    grads, mix_held, mix_in = take(3)
    kv_held, kv_in = take(2), take(2)
    held, more, landing = take(n), take(n), take(n)
    load_sem, out_sem, send_sem, recv_sem, kv_send, kv_recv, kv_out, mix_sem, line_send, line_recv = refs
    ep, dp = lax.axis_index("ep"), lax.axis_index("dp")
    step = pl.program_id(0) * pl.num_programs(1) + pl.program_id(1)
    final = pl.num_programs(0) * pl.num_programs(1) - 1
    sums = []
    for a in range(n):
        part = pl.ds(skip, sources[a].shape[1] - skip)
        loads = [
            pltpu.make_async_copy(src.at[:, part], dst, load_sem.at[a, i])
            for i, (src, dst) in enumerate(((sources[a], held[a]), (extras[a], more[a])))
        ]
        sums.append(
            PairSum(
                dp, orders[a], loads, held[a], more[a], landing[a], send_sem.at[a], recv_sem.at[a]
            )
        )
    batch_sums = [
        [
            PairSum(
                dp,
                full[i],
                [],
                kv_held[i].at[m],
                None,
                kv_in[i].at[m],
                kv_send.at[i, m],
                kv_recv.at[i, m],
            )
            for i in range(2)
        ]
        for m in range(micro)
    ]
    lines = [
        LineSum(ep, ne, mix_held.at[m], mix_in.at[m], line_send.at[m], line_recv.at[m])
        for m in range(micro)
    ]
    count = q_ref.shape[0]
    line_loads = [
        pltpu.make_async_copy(
            mix_ref.at[:, pl.ds(m * count, count)], mix_held.at[m], mix_sem.at[0, m]
        )
        for m in range(micro)
    ]
    turns = bit_count(nd)

    def batch_step(m, t):
        if t <= turns:
            for each in batch_sums[m]:
                each.step(t)

    def line_step(m, t):
        if t < ne:
            lines[m].step(t)

    @pl.when(step == 0)
    def _():
        for copy in line_loads:
            copy.start()
        for each in sums:
            each.load()
        greet(ep, dp, ne, nd)
        for m in range(micro):
            line_loads[m].wait()
            line_step(m, 0)
        for each in sums:
            each.step(0)
        for i in range(2):
            kv_held[i][...] = jnp.zeros_like(kv_held[i])
        rows = q_ref.shape[0]
        pairs = [dots_ref[:, :, m, :].reshape(-1, rows) for m in range(micro)]
        pair = jnp.concatenate(pairs, axis=1)
        probs = probs_ref[...]
        grad_logits = probs * (pair - jnp.sum(probs * pair, axis=0, keepdims=True))
        high = grad_logits.astype(BF16)
        low = (grad_logits - high.astype(F32)).astype(BF16)
        normed = normed_ref[...]
        router_out[...] = dot(high, normed) + dot(low, normed)
        router = router_ref[...]
        grad_normed = (
            grad_ref[...].astype(F32)
            + dot(high, router, ((0,), (0,)))
            + dot(low, router, ((0,), (0,)))
        )
        residual = residual_ref[...]
        r = rms_scale(residual)
        gain_out[...] = jnp.sum(grad_normed * residual * r, axis=0, keepdims=True)
        scaled = grad_normed * gain_ref[...]
        mean = jnp.mean(scaled * residual, axis=1, keepdims=True)
        grad_residual = cot_ref[...].astype(F32) + r * scaled - residual * (r * r * r) * mean
        res_out[...] = grad_residual
        low_res = grad_residual.astype(BF16)
        tile = 256
        for c in range(0, wo_out.shape[1], tile):
            wo_out[:, c : c + tile] = dot(
                attn_ref[...], low_res[:, c : c + tile], ((0,), (0,))
            ).astype(BF16)
        for c in range(0, wo_ref.shape[0], tile):
            grads[c // tile] = dot(low_res, wo_ref[c : c + tile, :], ((1,), (1,))).astype(BF16)

    rows = q_ref.shape[0]
    q = spread(q_ref[...].astype(F32) * SCALE).astype(BF16)
    mine = pl.ds(pl.multiple_of(pl.program_id(0) * rows, rows), rows)
    g = spread(grads[pl.program_id(1), mine, :].astype(F32)).astype(BF16)
    k, v = in_window(k_ref, dp, span), in_window(v_ref, dp, span)
    scores = window_scores(dp, span, rows, starts_ref, q, k)
    probs = jnp.exp(scores - log_ref[0, 0])
    grad_probs = dot(g, v, ((1,), (1,)))
    total = jnp.sum(probs * grad_probs, axis=1, keepdims=True)
    grad_scores = (probs * (grad_probs - total)).astype(BF16)
    dq = gathered(dot(grad_scores, k) * SCALE, rows)
    cosine, sine = tables_ref[0], -tables_ref[1]
    for i in range(0, dq.shape[1], 128):
        dq_ref[:, i : i + 128] = turn(dq[:, i : i + 128], cosine, sine).astype(BF16)
    here = pl.ds(window_of(dp, span), span)
    head = pl.program_id(1)
    at = pl.ds(pl.multiple_of(head * 2 * HEAD_DIM, 2 * HEAD_DIM), 2 * HEAD_DIM)
    batch = pl.program_id(0)
    dk = dot(grad_scores, q, ((0,), (0,))).astype(BF16)
    kv_held[0][batch, here, :, at] = dk.reshape(span, rows, dk.shape[1])
    dv = dot(probs.astype(BF16), g, ((0,), (0,))).astype(BF16)
    kv_held[1][batch, here, :, at] = dv.reshape(span, rows, dv.shape[1])

    heads = pl.num_programs(1)
    for m in range(micro):

        @pl.when((batch == m) & (head == heads - 1))
        def _(m=m):
            batch_step(m, 0)

        if m > 0:

            @pl.when((batch == m) & (head == 0))
            def _(m=m):
                batch_step(m - 1, 1)

    @pl.when(step == final // 4 + 1)
    def _():
        line_step(0, 1)

    @pl.when(step == final // 2 + 2)
    def _():
        line_step(1, 1)

    @pl.when(step == final)
    def _():
        copies = []

        def leave(copy):
            copy.start()
            copies.append(copy)

        line_step(0, 2)
        last = micro - 1
        batch_step(last - 1, 2)
        for t in range(1, max([len(order) for order in orders] + [0]) + 1):
            for each in sums:
                each.step(t)
        for a, each in enumerate(sums):
            leave(pltpu.make_async_copy(each.own(), outs[a], out_sem.at[a]))
        batch_step(last, 1)
        line_step(1, 2)
        for t in range(3, turns + 1):
            batch_step(last - 1, t)
        batch_step(last, 2)
        for t in range(3, ne):
            line_step(0, t)
            line_step(1, t)
        for t in range(3, turns + 1):
            batch_step(last, t)
        for m in range(micro):
            own = pl.ds(m * rows, rows)
            for i, out in enumerate((dk_out, dv_out)):
                leave(pltpu.make_async_copy(batch_sums[m][i].own(), out.at[own], kv_out.at[i, m]))
            leave(pltpu.make_async_copy(lines[m].own(), mix_out.at[own], mix_sem.at[1, m]))
        for each in sums + lines + sum(batch_sums, []):
            each.wait_sends()
        for copy in copies:
            copy.wait()


def attend_back(
    starts,
    queries,
    keys,
    values,
    logs_in,
    tables,
    cot,
    dots,
    probs,
    grad_normed,
    residual,
    gain,
    normed,
    attn,
    w_out,
    router,
    mix,
    sums,
    full,
    skip,
    collective,
):
    nd, ne, micro, rows = keys.shape[0], dots.shape[0], dots.shape[2], dots.shape[3]
    every, width = residual.shape
    grid, mine, theirs, column, logs, _ = attention_specs(micro, rows, nd)
    one = pl.Buffered(1)
    whole = lambda v: pl.BlockSpec(v.shape, lambda m, h: (0,) * len(v.shape), pipeline_mode=one)
    n = len(sums)
    shapes = [(v.shape[0], v.shape[1] - skip) + v.shape[2:] for v, _, _ in sums]
    deep = max([s[0] - 1 for s in shapes] + [1])
    some = max(n, 1)
    before = [cot, dots, probs, grad_normed, residual, gain, normed, attn, w_out, router]
    after = [
        jax.ShapeDtypeStruct((every, width), F32),
        jax.ShapeDtypeStruct(w_out.shape, BF16),
        jax.ShapeDtypeStruct(router.shape, F32),
        jax.ShapeDtypeStruct((1, width), F32),
    ]
    tile = 4 * HEAD_DIM
    return pl.pallas_call(
        functools.partial(
            attend_back_body,
            nd // 2 + 1,
            ne,
            nd,
            micro,
            skip,
            tuple(map(tuple, full)),
            tuple(tuple(order) for _, order, _ in sums),
        ),
        grid=grid,
        in_specs=[column, mine, theirs, theirs, logs, whole(tables)]
        + [whole(v) for v in before]
        + [ANY] * (2 * n + 1),
        out_specs=[mine] + [whole(v) for v in after] + [ANY] * (n + 3),
        out_shape=[jax.ShapeDtypeStruct(queries.shape, BF16)]
        + after
        + [jax.ShapeDtypeStruct((every, keys.shape[2]), BF16)] * 2
        + [jax.ShapeDtypeStruct((every, width), BF16)]
        + [jax.ShapeDtypeStruct(s[1:], BF16) for s in shapes],
        scratch_shapes=[
            pltpu.VMEM((w_out.shape[0] // tile, every, tile), BF16),
            pltpu.VMEM((micro, ne, rows, width), BF16),
            pltpu.VMEM((micro, 2, ne, rows, width), BF16),
        ]
        + [pltpu.VMEM((micro, nd, rows, keys.shape[2]), BF16)] * 2
        + [pltpu.VMEM((micro, nd - 1, rows, keys.shape[2]), BF16)] * 2
        + [pltpu.VMEM(s, BF16) for s in shapes] * 2
        + [pltpu.VMEM((s[0] - 1,) + s[1:], BF16) for s in shapes]
        + [
            DMA((some, 2)),
            DMA((some,)),
            DMA((some, deep)),
            DMA((some, deep)),
            DMA((2, micro, nd - 1)),
            DMA((2, micro, nd - 1)),
            DMA((2, micro)),
            DMA((2, micro)),
            DMA((micro, 2, ne)),
            DMA((micro, 2, ne)),
        ],
        compiler_params=pltpu.CompilerParams(
            vmem_limit_bytes=63 * 2**20, collective_id=collective, has_side_effects=True
        ),
        cost_estimate=cost(40),
    )(
        starts,
        queries,
        keys,
        values,
        logs_in,
        tables,
        *before,
        mix,
        *[v for v, _, _ in sums],
        *[extra for _, _, extra in sums],
    )


def finish_body(ne, nd, orders, n_out, *refs):
    refs = list(refs)

    def take(n):
        return [refs.pop(0) for _ in range(n)]

    n_ref, dq_ref, dk_ref, dv_ref, tables_ref, tokens_ref, gain_ref, router_ref, gain_two = take(9)
    res_ref, wq_ref, wk_ref, wv_ref, wo_ref = take(5)
    (tok_out,) = take(1)
    count = 2 * n_out + 3
    outs, held, pair_in, line_in = take(count), take(count), take(count), take(count)
    dk_turned, wq, wk, wv, res = take(5)
    load_sem, own_sem, out_sem, dp_send, dp_recv, ep_send, ep_recv = refs
    ep, dp = lax.axis_index("ep"), lax.axis_index("dp")
    columns = held[0].shape[3]
    own = [
        pltpu.make_async_copy(src, dst, own_sem.at[i])
        for i, (src, dst) in enumerate(
            ((wq_ref, wq), (wk_ref, wk), (wv_ref, wv), (res_ref, res))
        )
    ]
    sums = []
    for a in range(count):
        loads = []
        if a < n_out:
            at = pl.ds(a * columns, columns)
            loads = [
                pltpu.make_async_copy(wo_ref.at[e, :, :, at], held[a].at[:, e], load_sem.at[a, e])
                for e in range(ne)
            ]
        sums.append(
            PairSum(
                dp, orders[a % 2], loads, held[a], None, pair_in[a], dp_send.at[a], dp_recv.at[a]
            )
        )
    spreads = [
        SpreadSum(ep, ne, sums[a].own(), line_in[a], ep_send.at[a], ep_recv.at[a])
        for a in range(count)
    ]
    early, made, small = sums[:n_out], sums[n_out:-1], sums[-1]
    queries, others = made[:n_out], made[n_out:]
    for each in early:
        each.load()
    for copy in own:
        copy.start()
    greet(ep, dp, ne, nd)
    turns = bit_count(nd)

    def steps(group, t):
        for each in group:
            if t <= turns:
                each.step(t)

    def spread_steps(group, t):
        for each in group:
            spreads[sums.index(each)].step(t)

    steps(early, 0)

    normed = n_ref[...]
    cosine, sine = (repeated(tables_ref[i], normed.shape[0]) for i in range(2))
    sine = -sine
    for i in range(0, dk_ref.shape[1], 128):
        part = dk_ref[:, i : i + 128].astype(F32)
        dk_turned[:, i : i + 128] = turn(part, cosine, sine).astype(BF16)
    tile = 256

    def product(grad, first, each):
        share = each.held.shape[2]
        for c in range(0, each.held.shape[3], tile):
            y = dot(normed, grad[:, first + c : first + c + tile], ((0,), (0,))).astype(BF16)
            for e in range(ne):
                for d in range(nd):
                    r = (e * nd + d) * share
                    each.held[d, e, :, c : c + tile] = y[r : r + share]
        each.step(0)

    for i, each in enumerate(made):
        if i < n_out:
            product(dq_ref, i * columns, each)
        else:
            product((dk_turned, dv_ref)[i - n_out], 0, each)
        if i == 0:
            steps(early, 1)
        else:
            made[i - 1].step(1)
    for copy in own:
        copy.wait()
    back = dot(dq_ref[...], wq[...], ((1,), (1,)))
    steps(made[-1:], 1)
    back = back + dot(dk_turned[...], wk[...], ((1,), (1,)))
    back = back + dot(dv_ref[...], wv[...], ((1,), (1,)))
    steps(early, 2)
    x = tokens_ref[...].astype(F32)
    r = rms_scale(x)
    scaled = back * gain_ref[...]
    tok_out[...] = (
        res[...] + r * scaled - x * (r * r * r) * jnp.mean(scaled * x, axis=1, keepdims=True)
    )
    one_row = jnp.sum(back * x * r, axis=0, keepdims=True)
    blank = jnp.zeros((held[-1].shape[3] - EXPERTS - 2, x.shape[1]), F32)
    column = jnp.concatenate([router_ref[...], one_row, gain_two[...], blank], axis=0).T
    share = held[-1].shape[2]
    for e in range(ne):
        for d in range(nd):
            i = (e * nd + d) * share
            held[-1][d, e] = column[i : i + share].astype(BF16)
    steps([small], 0)
    steps(queries, 2)
    steps([small], 1)
    for t in range(3, turns + 1):
        steps(early, t)
    spread_steps(early, 0)
    steps(others, 2)
    for t in range(3, turns + 1):
        steps(queries, t)
    spread_steps(queries, 0)
    steps([small], 2)
    for t in range(3, turns + 1):
        steps(others, t)
        steps([small], t)
    spread_steps(others + [small], 0)
    spread_steps(early, 1)
    spread_steps(queries, 1)
    spread_steps(others + [small], 1)
    copies = []
    for a in range(count):
        copies.append(pltpu.make_async_copy(spreads[a].own(), outs[a], out_sem.at[a]))
        copies[-1].start()
    for each in sums + spreads:
        each.wait_sends()
    for copy in copies:
        copy.wait()


def finish(
    ne,
    nd,
    orders,
    normed,
    grads,
    tables,
    tokens,
    gain,
    grad_residual,
    weights,
    w_out,
    router_grad,
    gain_two_grad,
):
    rows, width = tokens.shape
    share = width // (ne * nd)
    columns = weights[1].shape[1]
    n_out = width // columns
    count = 2 * n_out + 3
    wide = [columns] * (count - 1) + [128]
    split = lambda v: v.reshape(ne, nd, share, v.shape[1])
    return pl.pallas_call(
        functools.partial(finish_body, ne, nd, tuple(map(tuple, orders)), n_out),
        out_shape=[jax.ShapeDtypeStruct((rows, width), F32)]
        + [jax.ShapeDtypeStruct((share, c), BF16) for c in wide],
        in_specs=[VMEM] * 9 + [ANY] * 5,
        out_specs=[VMEM] + [ANY] * count,
        scratch_shapes=[pltpu.VMEM((nd, ne, share, c), BF16) for c in wide]
        + [pltpu.VMEM((nd - 1, ne, share, c), BF16) for c in wide]
        + [pltpu.VMEM((ne - 1, share, c), BF16) for c in wide]
        + [pltpu.VMEM(grads[1].shape, BF16)]
        + [pltpu.VMEM(w.shape, BF16) for w in weights]
        + [pltpu.VMEM((rows, width), F32)]
        + [
            DMA((count, ne)),
            DMA((4,)),
            DMA((count,)),
            DMA((count, nd - 1)),
            DMA((count, nd - 1)),
            DMA((count, ne - 1)),
            DMA((count, ne - 1)),
        ],
        compiler_params=pltpu.CompilerParams(
            vmem_limit_bytes=60 * 2**20, collective_id=4, has_side_effects=True
        ),
        cost_estimate=cost(45),
    )(
        normed,
        *grads,
        tables,
        tokens,
        gain,
        router_grad,
        gain_two_grad,
        grad_residual,
        *weights,
        split(w_out),
    )


def results_body(share, n_out, groups, *refs):
    refs = list(refs)

    def take(n):
        return [refs.pop(0) for _ in range(n)]

    residual_ref, mix_ref = take(2)
    halves = [take(groups) for _ in range(2)]
    dense = take(2 * n_out + 3)
    out_ref, d_out, d_query, d_key, d_value, router, gain_one, gain_two = take(8)
    gate, up, down = refs
    e = pl.program_id(0)

    @pl.when(e == 0)
    def _():
        out_ref[...] = (residual_ref[...] + mix_ref[...].astype(F32)).astype(BF16)
        width = dense[0].shape[1]
        for i in range(n_out):
            d_out[:, i * width : (i + 1) * width] = dense[i][...].astype(F32)
            d_query[:, i * width : (i + 1) * width] = dense[n_out + i][...].astype(F32)
        d_key[...] = dense[2 * n_out][...].astype(F32)
        d_value[...] = dense[2 * n_out + 1][...].astype(F32)
        small = dense[-1][...].astype(F32)
        router[...] = small[:, :EXPERTS]
        turned = small.T
        gain_one[...] = turned[EXPERTS : EXPERTS + 1]
        gain_two[...] = turned[EXPERTS + 1 : EXPERTS + 2]

    k = 0
    for first, second in zip(*halves):
        for m in range(first.shape[0]):

            @pl.when(e == k)
            def _(first=first, second=second, m=m):
                over = first.shape[1] - share
                gate[0] = first[m, :share].astype(F32)
                up[0, :over] = first[m, share:].astype(F32)
                up[0, over:] = second[m, : share - over].astype(F32)
                piece, columns = down.shape[1], second.shape[2]
                for j in range(down.shape[2] // columns):
                    at = share - over + j * piece
                    down[0, :, j * columns : (j + 1) * columns] = second[
                        m, at : at + piece
                    ].astype(F32)

            k += 1


def results(residual, mix, grads, dense, n_out, share, w_gate, w_down, nd, rows_share):
    rows, width = residual.shape
    n_exp, _, inner = w_gate.shape
    piece = w_down.shape[1] // nd
    ins = [residual, *mix, *grads[0], *grads[1], *dense]
    kv = dense[-2].shape[1]
    same = lambda v: pl.BlockSpec(v, lambda e: (0,) * len(v))
    outs = [
        ((rows, width), BF16),
        ((rows_share, width), F32),
        ((rows_share, width), F32),
        ((rows_share, kv), F32),
        ((rows_share, kv), F32),
        ((rows_share, EXPERTS), F32),
        ((1, rows_share), F32),
        ((1, rows_share), F32),
    ]
    experts_out = [((n_exp, share, inner), F32)] * 2 + [((n_exp, piece, width), F32)]
    return pl.pallas_call(
        functools.partial(results_body, share, n_out, len(grads[0])),
        grid=(n_exp,),
        out_shape=[jax.ShapeDtypeStruct(*v) for v in outs + experts_out],
        in_specs=[same(v.shape) for v in ins],
        out_specs=[same(v[0]) for v in outs]
        + [pl.BlockSpec((1,) + v[0][1:], lambda e: (e, 0, 0)) for v in experts_out],
        compiler_params=pltpu.CompilerParams(vmem_limit_bytes=60 * 2**20),
        cost_estimate=cost(6),
    )(*ins)


def per_device(
    tokens,
    segments,
    routes,
    first_gain,
    w_query,
    w_key,
    w_value,
    w_out,
    second_gain,
    w_router,
    w_gate,
    w_up,
    w_down,
    cotangent,
):
    micro, rows, width = tokens.shape
    ne, nd = lax.axis_size("ep"), lax.axis_size("dp")
    kv_width = KV_HEADS * HEAD_DIM
    every = micro * rows

    halfway = HEAD_DIM // 2
    frequency = ROPE_BASE ** (-(np.arange(halfway) * 2.0 / HEAD_DIM))
    angles = np.arange(nd * rows)[:, None] * frequency[None, :]
    lanes = 2 * HEAD_DIM // halfway
    sign = np.where(np.arange(2 * HEAD_DIM) % HEAD_DIM < halfway, -1.0, 1.0)
    tables = np.stack([np.tile(np.cos(angles), lanes), np.tile(np.sin(angles), lanes) * sign])
    tokens_flat = tokens.reshape(every, width)
    gain_one = first_gain.reshape(1, width)
    normed_one, query_rot, tables, starts, key_all, value_all = project(
        tokens_flat,
        gain_one,
        segments.reshape(micro, rows),
        jnp.asarray(tables, F32),
        w_query,
        w_key,
        w_value,
        ne,
        nd,
        0,
    )
    cot_own = cotangent.reshape(every, width)

    def around(value, k):
        return lax.ppermute(value, "ep", [(i, (i + k) % ne) for i in range(ne)])

    cots = [cot_own] + [around(cot_own, k) for k in range(1, ne)]
    routing = routes.reshape(every, routes.shape[2])
    hit = jnp.any(
        jnp.arange(EXPERTS, dtype=jnp.int32)[:, None, None] == routing[None], axis=2
    ).astype(F32)
    router = w_router.T
    attn_low, logs, residual, normed_two, gate_probs, normed_all, marked_all = attend(
        starts,
        query_rot,
        key_all,
        value_all,
        tokens_flat,
        w_out,
        second_gain.reshape(1, width),
        router,
        hit,
        micro,
        rows,
        ne,
        1,
    )
    orders = [order[:-1][::-1] for order in gather_orders(nd)]
    mix, grad_in, pair_dots, *grads = experts(
        normed_all.reshape(ne * every, width),
        cots,
        marked_all.reshape(ne * micro, EXPERTS, rows),
        w_gate,
        w_up,
        w_down,
        micro,
        rows,
        ne,
        nd,
        6,
    )
    kept, landed, last = grads[:2], grads[2:4], grads[4:]
    height = kept[0].shape[2]
    halves = [(slice(None), slice(i * height, (i + 1) * height)) for i in range(2)]
    skip = min(2, kept[0].shape[1])
    more = kept[0].shape[1] > skip
    head = (slice(None), slice(0, skip))
    *grads, grad_back, dots_all = reduce(
        ne,
        nd,
        [(last[k], orders[i], halves[i], None, False) for k in range(2) for i in range(2)]
        + [(kept[i], orders[i][1:], head, landed[i], False) for i in range(2)],
        ((grad_in.reshape(ne, every, width), None),),
        (pair_dots,),
        2,
        40,
    )
    grads_last, grads_head = grads[:4], grads[4:]
    mix = mix.reshape(ne, every, width)
    full = [[0] + order for order in orders]
    (
        grad_query,
        grad_residual,
        grad_w_out,
        grad_router,
        grad_gain_two,
        grad_key,
        grad_value,
        mix_own,
        *grads_more,
    ) = attend_back(
        starts,
        query_rot,
        key_all,
        value_all,
        logs,
        tables,
        cot_own,
        dots_all,
        gate_probs,
        grad_back,
        residual,
        second_gain.reshape(1, width),
        normed_two,
        attn_low,
        w_out,
        router,
        mix,
        [(kept[i], orders[i][1:], landed[i]) for i in range(2)] if more else [],
        full,
        skip,
        5,
    )
    grad_tokens, *dense = finish(
        ne,
        nd,
        full,
        normed_one,
        (grad_query, grad_key, grad_value),
        tables,
        tokens_flat,
        gain_one,
        grad_residual,
        (w_query, w_key, w_value),
        grad_w_out,
        grad_router,
        grad_gain_two,
    )
    (
        output,
        d_out,
        d_query,
        d_key,
        d_value,
        d_router,
        d_gain_one,
        d_gain_two,
        d_gate,
        d_up,
        d_down,
    ) = results(
        residual,
        (mix_own,),
        [
            [grads_head[i]]
            + ([grads_more[i]] if more else [])
            + [grads_last[i][None], grads_last[2 + i][None]]
            for i in range(2)
        ],
        dense,
        width // kv_width,
        width // nd,
        w_gate,
        w_down,
        nd,
        width // (ne * nd),
    )
    return (
        output.reshape(tokens.shape),
        grad_tokens.reshape(tokens.shape),
        d_gain_one.reshape(-1),
        d_query,
        d_key,
        d_value,
        d_out,
        d_gain_two.reshape(-1),
        d_router,
        d_gate,
        d_up,
        d_down,
    )


def solution(mesh):
    in_specs = (
        P(None, ("ep", "dp"), None),
        P(None, "ep", "dp"),
        P(None, ("ep", "dp"), None),
        P(),
        P(),
        P(),
        P(),
        P(),
        P(),
        P(),
        P("ep", None, None),
        P("ep", None, None),
        P("ep", None, None),
        P(None, ("ep", "dp"), None),
    )
    out_specs = (
        P(None, ("ep", "dp"), None),
        P(None, ("ep", "dp"), None),
        P(("ep", "dp")),
        P(("ep", "dp"), None),
        P(("ep", "dp"), None),
        P(("ep", "dp"), None),
        P(("ep", "dp"), None),
        P(("ep", "dp")),
        P(("ep", "dp"), None),
        P("ep", "dp", None),
        P("ep", "dp", None),
        P("ep", "dp", None),
    )
    return jax.shard_map(
        per_device, mesh=mesh, in_specs=in_specs, out_specs=out_specs, check_vma=False
    )
```

```python
import functools

import jax
import jax.numpy as jnp
import numpy as np
from jax import lax
from jax.experimental import pallas as pl
from jax.experimental.pallas import tpu as pltpu
from jax.sharding import PartitionSpec as P

HEADS = 16
KV_HEADS = 8
HEAD_DIM = 64
EXPERTS = 32
CAP = 64
SEGMENT_IDS = 4
EPSILON = 1e-06
ROPE_BASE = 10000.0
MASKED = -1e30
HIGHEST = lax.Precision.HIGHEST
MESH = pl.DeviceIdType.MESH
BF16 = jnp.bfloat16
F32 = jnp.float32
VMEM = pl.BlockSpec(memory_space=pltpu.VMEM)
ANY = pl.BlockSpec(memory_space=pl.ANY)
DMA = pltpu.SemaphoreType.DMA


def bit_count(n):
    return n.bit_length() - 1


def masks(bits):
    out = [0]
    for b in bits:
        out = out + [m | (1 << b) for m in out]
    return out


def gather_orders(n):
    bits = list(range(bit_count(n)))
    return (bits[1:] + bits[:1], bits[:0:-1] + bits[:1])


def greet(ep, dp, ne, nd):
    barrier = pltpu.get_barrier_semaphore()
    for k in range(1, ne):
        pl.semaphore_signal(
            barrier, inc=1, device_id={"ep": lax.rem(ep + k, ne)}, device_id_type=MESH
        )
    for b in range(bit_count(nd)):
        pl.semaphore_signal(
            barrier, inc=1, device_id={"dp": jnp.bitwise_xor(dp, 1 << b)}, device_id_type=MESH
        )
    pl.semaphore_wait(barrier, ne - 1 + bit_count(nd))


def remote(src, dst, send, recv, where):
    return pltpu.make_async_remote_copy(
        src_ref=src, dst_ref=dst, send_sem=send, recv_sem=recv, device_id=where, device_id_type=MESH
    )


class PairGather:
    def __init__(self, dp, nd, order, own, whole, send_sem, recv_sem):
        self.dp, self.order, self.own, self.whole = dp, order, own, whole
        self.send_sem, self.recv_sem = send_sem, recv_sem

    def copy(self, t, m):
        block = jnp.bitwise_xor(self.dp, m)
        k = (1 << t) - 1 + masks(self.order[:t]).index(m)
        return remote(
            self.own if m == 0 else self.whole.at[block],
            self.whole.at[block],
            self.send_sem.at[k],
            self.recv_sem.at[k],
            {"dp": jnp.bitwise_xor(self.dp, 1 << self.order[t])},
        )

    def start(self):
        for t in range(len(self.order)):
            self.copy(t, 0).start()

    def step(self, t):
        for m in masks(self.order[:t]):
            self.copy(t, m).wait_recv()
            for later in range(t + 1, len(self.order)):
                self.copy(later, m | (1 << self.order[t])).start()

    def wait_sends(self):
        for t in range(len(self.order)):
            for m in masks(self.order[:t]):
                self.copy(t, m).wait_send()


def cost(us):
    return pl.CostEstimate(flops=0, bytes_accessed=int(us * 3.0e6), transcendentals=0)


def add_into(ref, arrived):
    if len(ref.shape) > 2:

        @pl.loop(0, ref.shape[0])
        def _(i):
            add_into(ref.at[i], arrived.at[i])

    else:
        ref[...] = (ref[...].astype(F32) + arrived[...].astype(F32)).astype(ref.dtype)


class PairSum:
    def __init__(self, dp, order, loads, held, extra, landing, send_sem, recv_sem, major=False):
        self.dp, self.order, self.held, self.landing = dp, order, held, landing
        self.send_sem, self.recv_sem = send_sem, recv_sem
        self.extra, self.loads, self.major = extra, loads, major
        self.index = 0
        for b in order:
            side = jnp.bitwise_and(lax.shift_right_logical(dp, b), 1)
            self.index = self.index + (side << self.place(b))

    def place(self, bit):
        if self.major:
            return len(self.order) - 1 - self.order.index(bit)
        return sorted(self.order).index(bit)

    def copies(self, t):
        order = self.order
        if self.major:
            count = 1 << (len(order) - 1 - t)
            first = sum(1 << (len(order) - 1 - i) for i in range(t))
            mine = self.index - lax.rem(self.index, count)
            copy = remote(
                self.held.at[pl.ds(jnp.bitwise_xor(mine, count), count)],
                self.landing.at[pl.ds(first, count)],
                self.send_sem.at[t],
                self.recv_sem.at[t],
                {"dp": jnp.bitwise_xor(self.dp, 1 << order[t])},
            )
            return [(pl.ds(mine, count), pl.ds(first, count), copy)]
        partner = jnp.bitwise_xor(self.index, 1 << self.place(order[t]))
        first = sum(1 << (len(order) - 1 - i) for i in range(t))
        return [
            (
                m,
                first + j,
                remote(
                    self.held.at[jnp.bitwise_xor(partner, m)],
                    self.landing.at[first + j],
                    self.send_sem.at[first + j],
                    self.recv_sem.at[first + j],
                    {"dp": jnp.bitwise_xor(self.dp, 1 << order[t])},
                ),
            )
            for j, m in enumerate(masks([self.place(b) for b in order[t + 1 :]]))
        ]

    def load(self):
        for copy in self.loads:
            copy.start()

    def step(self, t):
        if t == 0:
            for copy in self.loads:
                copy.wait()
            if self.extra is not None:
                add_into(self.held, self.extra)
        elif t <= len(self.order):
            for m, k, copy in self.copies(t - 1):
                copy.wait_recv()
                mine = m if self.major else jnp.bitwise_xor(self.index, m)
                add_into(self.held.at[mine], self.landing.at[k])
        if t < len(self.order):
            for m, k, copy in self.copies(t):
                copy.start()

    def own(self):
        return self.held.at[self.index]

    def wait_sends(self):
        for t in range(len(self.order)):
            for m, k, copy in self.copies(t):
                copy.wait_send()


def slot_of(order, d):
    return sum(((d >> b) & 1) << (len(order) - 1 - i) for i, b in enumerate(order))


class LineSum:
    def __init__(self, ep, ne, blocks, landing, send_sem, recv_sem):
        self.ep, self.ne, self.blocks, self.landing = ep, ne, blocks, landing
        self.send_sem, self.recv_sem = send_sem, recv_sem

    def copy(self, dest, way):
        k = 0 if way == 1 else 1
        return remote(
            self.blocks.at[dest],
            self.landing.at[k, dest],
            self.send_sem.at[k, dest],
            self.recv_sem.at[k, dest],
            {"ep": lax.rem(self.ep + way + self.ne, self.ne)},
        )

    def turn(self, t, way):
        ep, ne = self.ep, self.ne
        dest = ep + ne - 1 - t if way == 1 else ep + t - (ne - 1)
        has = dest <= ne - 1 if way == 1 else dest >= 0
        inner = ep >= 1 if way == 1 else ep <= ne - 2
        return dest, has, inner

    def step(self, t):
        for way in (1, -1):
            dest, has, inner = self.turn(t, way)

            @pl.when(has & inner)
            def _(way=way, dest=dest):
                self.copy(dest, way).wait_recv()
                add_into(self.blocks.at[dest], self.landing.at[0 if way == 1 else 1, dest])

            if t < self.ne - 1:

                @pl.when(has)
                def _(way=way, dest=dest):
                    self.copy(dest, way).start()

    def own(self):
        return self.blocks.at[self.ep]

    def wait_sends(self):
        for t in range(self.ne - 1):
            for way in (1, -1):
                dest, has, inner = self.turn(t, way)

                @pl.when(has)
                def _(way=way, dest=dest):
                    self.copy(dest, way).wait_send()


class SpreadSum:
    def __init__(self, ep, ne, blocks, landing, send_sem, recv_sem):
        self.ep, self.blocks, self.landing = ep, blocks, landing
        self.copies = []
        for k in range(1, ne):
            to = lax.rem(ep + k, ne)
            self.copies.append(
                remote(
                    blocks.at[to],
                    landing.at[k - 1],
                    send_sem.at[k - 1],
                    recv_sem.at[k - 1],
                    {"ep": to},
                )
            )

    def step(self, t):
        if t == 0:
            for copy in self.copies:
                copy.start()
        elif t == 1:
            total = self.blocks[self.ep].astype(F32)
            for k, copy in enumerate(self.copies):
                copy.wait_recv()
                total = total + self.landing[k].astype(F32)
            self.blocks[self.ep] = total.astype(BF16)

    def own(self):
        return self.blocks.at[self.ep]

    def wait_sends(self):
        for copy in self.copies:
            copy.wait_send()


def shape_at(array, where):
    return tuple(len(range(*w.indices(n))) for w, n in zip(where, array.shape)) + array.shape[len(where) :]


def reduce_body(ne, nd, pairs, line_parts, n_swap, *refs):
    refs = list(refs)

    def take(n):
        return [refs.pop(0) for _ in range(n)]

    n_pair, n_line = len(pairs), len(line_parts)
    n_extra = sum(p[2] for p in pairs)
    n_both = sum(p[3] for p in pairs)
    n_sum = n_pair + n_line
    ins, extra_ins, swap_ins = take(n_sum), take(n_extra), take(n_swap)
    outs, swap_outs = take(n_sum), take(n_swap)
    held, extras, pair_in = take(n_sum), take(n_extra), take(n_pair)
    both_in, line_in = take(n_both), take(n_line)
    load_sem, out_sem, dp_send, dp_recv, ep_send, ep_recv, swap_send, swap_recv = refs
    ep, dp = lax.axis_index("ep"), lax.axis_index("dp")
    sums, then = [], []
    for a, (order, where, has_extra, both) in enumerate(pairs):
        targets = [(ins[a], held[a])]
        extra = extras.pop(0) if has_extra else None
        if has_extra:
            targets.append((extra_ins.pop(0), extra))
        loads = [
            pltpu.make_async_copy(src.at[where] if where else src, dst, load_sem.at[a, i])
            for i, (src, dst) in enumerate(targets)
        ]
        sums.append(
            PairSum(dp, order, loads, held[a], extra, pair_in[a], dp_send.at[a], dp_recv.at[a])
        )
        if both:
            i = len(then)
            then.append(
                LineSum(ep, ne, sums[a].own(), both_in[i], ep_send.at[i], ep_recv.at[i])
            )
    lines, line_loads = [], []
    for i in range(n_line):
        a = n_pair + i
        src = ins[a].at[line_parts[i]] if line_parts[i] else ins[a]
        line_loads.append(pltpu.make_async_copy(src, held[a], load_sem.at[a, 0]))
        lines.append(
            LineSum(
                ep, ne, held[a], line_in[i], ep_send.at[n_both + i], ep_recv.at[n_both + i]
            )
        )
    for copy in line_loads:
        copy.start()
    for each in sums:
        each.load()
    greet(ep, dp, ne, nd)
    swaps = []
    for a in range(n_swap):
        src, dst = swap_ins[a], swap_outs[a]
        own = pltpu.make_async_copy(src.at[ep], dst.at[ep], load_sem.at[n_sum + a, 0])
        own.start()
        swaps.append(own)
        for k in range(1, ne):
            to = lax.rem(ep + k, ne)
            copy = remote(
                src.at[to], dst.at[ep], swap_send.at[a, k - 1], swap_recv.at[a, k - 1], {"ep": to}
            )
            copy.start()
            swaps.append(copy)
    for copy in line_loads:
        copy.wait()
    steps = max([len(p[0]) + 1 for p in pairs] + [ne if n_line else 0])
    for t in range(steps):
        if t < ne:
            for each in lines:
                each.step(t)
        for each in sums:
            each.step(t)
    for t in range(ne):
        for each in then:
            each.step(t)
    results, after = [], iter(then)
    for a in range(n_sum):
        if a >= n_pair:
            src = lines[a - n_pair].own()
        else:
            src = next(after).own() if pairs[a][3] else sums[a].own()
        copy = pltpu.make_async_copy(src, outs[a], out_sem.at[a])
        copy.start()
        results.append(copy)
    for each in sums + then + lines:
        each.wait_sends()
    for copy in swaps + results:
        copy.wait()


def reduce(ne, nd, pairs, lines, swaps, collective, us):
    line_parts = tuple(where for _, where in lines)
    line_shapes = [shape_at(v, where) if where else v.shape for v, where in lines]
    lines = [v for v, _ in lines]
    arrays = [p[0] for p in pairs] + list(lines)
    extras = [p[3] for p in pairs if p[3] is not None]
    kinds = tuple((tuple(p[1]), p[2], p[3] is not None, p[4]) for p in pairs)
    shapes = [shape_at(p[0], p[2]) if p[2] else p[0].shape for p in pairs]
    boths = [s for s, p in zip(shapes, pairs) if p[4]]
    results = [s[2:] if p[4] else s[1:] for s, p in zip(shapes, pairs)]
    results += [s[1:] for s in line_shapes]
    scratch = shapes + line_shapes
    scratch += [s for s, p in zip(shapes, pairs) if p[3] is not None]
    scratch += [(s[0] - 1,) + s[1:] for s in shapes]
    scratch += [(2,) + s[1:] for s in boths] + [(2,) + s for s in line_shapes]
    some = lambda n: max(n, 1)
    line_count = some(len(lines) + len(boths))
    deep = max([s[0] - 1 for s in shapes] + [1])
    return pl.pallas_call(
        functools.partial(reduce_body, ne, nd, kinds, line_parts, len(swaps)),
        out_shape=[jax.ShapeDtypeStruct(s, BF16) for s in results]
        + [jax.ShapeDtypeStruct(v.shape, v.dtype) for v in swaps],
        in_specs=[ANY] * (len(arrays) + len(extras) + len(swaps)),
        out_specs=[ANY] * (len(arrays) + len(swaps)),
        scratch_shapes=[pltpu.VMEM(s, BF16) for s in scratch]
        + [
            DMA((len(arrays) + len(swaps), 2)),
            DMA((len(arrays),)),
            DMA((some(len(pairs)), deep)),
            DMA((some(len(pairs)), deep)),
            DMA((line_count, 2, ne)),
            DMA((line_count, 2, ne)),
            DMA((some(len(swaps)), ne - 1)),
            DMA((some(len(swaps)), ne - 1)),
        ],
        compiler_params=pltpu.CompilerParams(
            collective_id=collective, has_side_effects=True, vmem_limit_bytes=60 * 2**20
        ),
        cost_estimate=cost(us),
    )(*arrays, *extras, *swaps)


def dot(a, b, dims=((1,), (0,))):
    return lax.dot_general(a, b, (dims, ((), ())), preferred_element_type=F32)


def expert_body(ne, nd, micro, rows, *refs):
    cot_first, cots, refs = refs[0], refs[1 : ne + 1], refs[ne + 1 :]
    normed_ref, probs_ref, gate_ref, up_ref, down_ref = refs[:5]
    mix_ref, grad_ref, dots_ref = refs[5:8]
    kept, landed, whole = refs[8:10], refs[10:12], refs[12:14]
    rows_in, cots_in, picks, first, second, chances, sides, arrived, leaving = refs[14:23]
    load_sem, store_sem, send_sem, recv_sem, free_sem, far_send, far_recv = refs[23:]
    e = pl.program_id(0)
    last = pl.num_programs(0) - 1
    ep, dp = lax.axis_index("ep"), lax.axis_index("dp")
    other = {"dp": jnp.bitwise_xor(dp, 1)}
    every = micro * rows
    blocks = ne * micro
    width = first.shape[1]
    n_exp = rows_in.shape[1]

    core = jnp.bitwise_and(dp, 1)
    keep, send = sides.at[core], sides.at[1 - core]

    def exchange():
        return remote(send, arrived, send_sem, recv_sem, other)

    def loads():
        out = [
            pltpu.make_async_copy(normed_ref, first, load_sem.at[ne]),
            pltpu.make_async_copy(
                probs_ref.at[:, pl.ds(pl.multiple_of(ep * n_exp, n_exp), n_exp)],
                chances,
                load_sem.at[ne + 1],
            ),
        ]
        held = every - rows
        for k in range(ne):
            at = pl.multiple_of(lax.rem(ep - k + ne, ne) * every + rows, rows)
            out.append(
                pltpu.make_async_copy(cots[k], second.at[pl.ds(at, held)], load_sem.at[k])
            )
            out.append(
                pltpu.make_async_copy(
                    cot_first.at[k], second.at[pl.ds(k * every, rows)], load_sem.at[ne + 2 + k]
                )
            )
        return out

    def block_at(s):
        return pl.ds(pl.multiple_of(s * rows, rows), rows)

    def returned(t):
        k, m = t // micro, lax.rem(t, micro)
        return lax.rem(ep + k, ne) * micro + m

    def stores(t):
        s = returned(t)
        return (
            pltpu.make_async_copy(
                first.at[block_at(s)], mix_ref.at[block_at(s)], store_sem.at[0, t]
            ),
            pltpu.make_async_copy(
                second.at[block_at(s)], grad_ref.at[block_at(s)], store_sem.at[1, t]
            ),
        )

    def far(i, n):
        return remote(
            leaving.at[i, lax.rem(n, leaving.shape[1])],
            landed[i].at[:, n],
            far_send.at[i, lax.rem(n, leaving.shape[1])],
            far_recv.at[i, n],
            {"dp": jnp.bitwise_xor(dp, 1 << first_bits(nd)[i])},
        )

    def last_copy(k):
        return pltpu.make_async_copy(keep, whole[k], load_sem.at[k])

    def collect():
        exchange().wait_recv()
        pieces, height, slots = sides.shape[1], leaving.shape[3], leaving.shape[1]
        n = e - 1
        early = n_exp - 2

        @pl.when(n < early)
        def _():
            @pl.when(n >= slots)
            def _():
                for i in range(2):
                    far(i, n - slots).wait_send()

            def piece(i, at, other_side):
                bit = first_bits(nd)[i]
                mine = jnp.bitwise_and(lax.shift_right_logical(dp, bit), 1)
                side = 1 - mine if other_side else mine
                low = (1 << (bit - 1)) - 1
                j = ((at & ~low) << 1 | (at & low)) + (side << (bit - 1))
                part = slice(i * height, (i + 1) * height)
                return (keep[j, part].astype(F32) + arrived[j, part].astype(F32)).astype(BF16)

            for i in range(2):
                for at in range(pieces // 2):
                    leaving[i, lax.rem(n, slots), at] = piece(i, at, True)
                far(i, n).start()
            for i in range(2):
                for at in range(pieces // 2):
                    kept[i][at, 0] = piece(i, at, False)

        for k in range(2):

            @pl.when(n == early + k)
            def _(k=k):
                add_into(keep, arrived)
                last_copy(k).start()

    @pl.when(e == 0)
    def _():
        for copy in loads():
            copy.start()
        barrier = pltpu.get_barrier_semaphore()
        met = [0] + sorted(set(first_bits(nd)))
        for bit in met:
            pl.semaphore_signal(
                barrier,
                inc=1,
                device_id={"dp": jnp.bitwise_xor(dp, 1 << bit)},
                device_id_type=MESH,
            )
        pl.semaphore_wait(barrier, len(met))
        before = lax.broadcasted_iota(jnp.int32, (rows, rows), 0)
        after = lax.broadcasted_iota(jnp.int32, (rows, rows), 1)
        earlier = (before < after).astype(BF16)
        slot = lax.broadcasted_iota(jnp.int32, (n_exp, CAP, rows), 1)
        for copy in loads():
            copy.wait()

        @pl.loop(0, blocks)
        def _(s):
            at = block_at(s)
            probs = chances[s]
            hit = probs >= 0.0
            rank = dot(hit.astype(BF16), earlier)
            rank = jnp.where(hit, rank, -1.0).astype(jnp.int32)
            pick = jnp.broadcast_to(rank[:, None, :], (n_exp, CAP, rows)) == slot
            pick_f = pick.astype(F32)
            flat = pick_f.reshape(n_exp * CAP, rows).astype(BF16)
            picks[s] = flat
            rows_in[s] = dot(flat, first[at, :]).astype(BF16).reshape(n_exp, CAP, width)
            cots_in[s] = dot(flat, second[at, :]).astype(BF16).reshape(n_exp, CAP, width)

    @pl.when(e < last)
    def _():
        x = rows_in[:, e].reshape(blocks * CAP, width)
        c = cots_in[:, e].reshape(blocks * CAP, width)
        flat = picks[:, pl.ds(pl.multiple_of(e * CAP, CAP), CAP), :].astype(F32)
        p = jnp.sum(flat * chances[:, pl.ds(e, 1), :], axis=2, keepdims=True)
        p = p.reshape(blocks * CAP, 1)
        w_gate, w_up, w_down = gate_ref[0], up_ref[0], down_ref[0]
        gate_pre = dot(x, w_gate)
        up_pre = dot(x, w_up)
        back = dot(c, w_down, ((1,), (1,)))

        @pl.when(e > 0)
        def _():
            collect()
            pl.semaphore_signal(free_sem, inc=1, device_id=other, device_id_type=MESH)

        sigma = jax.nn.sigmoid(gate_pre)
        silu = gate_pre * sigma
        hidden = (silu * up_pre).astype(BF16)
        out = dot(hidden, w_down) * p
        wide = hidden.astype(F32)
        pair = jnp.sum(wide * back, axis=1, keepdims=True)
        back = back * p
        grad_up = (back * silu).astype(BF16)
        grad_gate = (back * up_pre * (sigma * (1.0 + gate_pre * (1.0 - sigma)))).astype(BF16)
        scaled = (wide * p).astype(BF16)
        grad_x = dot(grad_gate, w_gate, ((1,), (1,))) + dot(grad_up, w_up, ((1,), (1,)))
        pair = jnp.sum(flat * pair.reshape(blocks, CAP, 1), axis=1)
        dots_ref[:, 0] = pair.reshape(ne, micro, rows)

        @pl.when(e > 0)
        def _():
            exchange().wait_send()
            pl.semaphore_wait(free_sem, 1)

        @pl.when(e == n_exp - 1)
        def _():
            last_copy(0).wait()

        def split(value, offset):
            value = value.astype(BF16)
            piece, columns = value.shape[0] // nd, sides.shape[3]

            for i in range(nd):
                for j in range(value.shape[1] // columns):
                    at = offset + j * piece
                    sides[i % 2, i // 2, at : at + piece] = value[
                        i * piece : (i + 1) * piece, j * columns : (j + 1) * columns
                    ]

        share = width // nd
        split(dot(scaled, c, ((0,), (0,))), 2 * share)
        split(dot(x, grad_gate, ((0,), (0,))), 0)
        split(dot(x, grad_up, ((0,), (0,))), share)
        exchange().start()

        rows_in[:, e] = grad_x.astype(BF16).reshape(blocks, CAP, width)
        cots_in[:, e] = out.astype(BF16).reshape(blocks, CAP, width)

    @pl.when(e == last)
    def _():
        @pl.loop(0, blocks)
        def _(t):
            s = returned(t)
            at = block_at(s)
            flat = picks[s]
            for done, slots in ((first, cots_in), (second, rows_in)):
                value = dot(flat, slots[s].reshape(n_exp * CAP, width), ((0,), (0,)))
                done[at, :] = value.astype(BF16)
            for copy in stores(t):
                copy.start()

            @pl.when(t == 1)
            def _():
                collect()
                exchange().wait_send()

        @pl.loop(0, blocks)
        def _(t):
            for copy in stores(t):
                copy.wait()

        last_copy(1).wait()
        early, slots = n_exp - 2, leaving.shape[1]
        for i in range(2):
            for n in range(max(early - slots, 0), early):
                far(i, n).wait_send()

            @pl.loop(0, early)
            def _(n, i=i):
                far(i, n).wait_recv()


def first_bits(nd):
    return [order[-2] for order in gather_orders(nd)]


def experts(normed, cots, probs, w_gate, w_up, w_down, micro, rows, ne, nd, collective):
    n_exp, width, inner = w_gate.shape
    blocks = ne * micro
    half = nd // 2
    packed = 2 * width // nd + (inner // nd) * (width // inner)
    full = (blocks * rows, width)
    weight = lambda e: (jnp.minimum(e, n_exp - 1), 0, 0)
    early = n_exp - 2
    part = (half // 2, early, packed // 2, inner)
    kept = pl.BlockSpec(
        (half // 2, 1, packed // 2, inner), lambda e: (0, jnp.clip(e - 1, 0, early - 1), 0, 0)
    )
    last = (half, packed, inner)
    return pl.pallas_call(
        functools.partial(expert_body, ne, nd, micro, rows),
        grid=(n_exp + 1,),
        in_specs=[ANY] * (ne + 3)
        + [
            pl.BlockSpec((1, width, inner), weight),
            pl.BlockSpec((1, width, inner), weight),
            pl.BlockSpec((1, inner, width), weight),
        ],
        out_specs=[
            ANY,
            ANY,
            pl.BlockSpec((ne, 1, micro, rows), lambda e: (0, jnp.minimum(e, n_exp - 1), 0, 0)),
            kept,
            kept,
            ANY,
            ANY,
            ANY,
            ANY,
        ],
        scratch_shapes=[
            pltpu.VMEM((blocks, n_exp, CAP, width), BF16),
            pltpu.VMEM((blocks, n_exp, CAP, width), BF16),
            pltpu.VMEM((blocks, n_exp * CAP, rows), BF16),
            pltpu.VMEM(full, BF16),
            pltpu.VMEM(full, BF16),
            pltpu.VMEM((blocks, n_exp, rows), F32),
            pltpu.VMEM((2, half, packed, inner), BF16),
            pltpu.VMEM((half, packed, inner), BF16),
            pltpu.VMEM((2, 2 if early > 2 else 1, half // 2, packed // 2, inner), BF16),
            DMA((2 * ne + 2,)),
            DMA((2, blocks)),
            DMA,
            DMA,
            pltpu.SemaphoreType.REGULAR,
            DMA((2, 2)),
            DMA((2, early)),
        ],
        out_shape=[
            jax.ShapeDtypeStruct(full, BF16),
            jax.ShapeDtypeStruct(full, BF16),
            jax.ShapeDtypeStruct((ne, n_exp, micro, rows), F32),
        ]
        + [jax.ShapeDtypeStruct(part, BF16)] * 4
        + [jax.ShapeDtypeStruct(last, BF16)] * 2,
        compiler_params=pltpu.CompilerParams(
            vmem_limit_bytes=63 * 2**20,
            dimension_semantics=("arbitrary",),
            collective_id=collective,
            has_side_effects=True,
        ),
        cost_estimate=cost(75),
    )(*cots, normed, probs, w_gate, w_up, w_down)


def rms_scale(values):
    return lax.rsqrt(jnp.mean(values * values, axis=-1, keepdims=True) + EPSILON)


def partner(x):
    lane = lax.broadcasted_iota(jnp.int32, x.shape, 1)
    half = HEAD_DIM // 2
    low = lax.rem(lane, HEAD_DIM) < half
    return jnp.where(low, pltpu.roll(x, x.shape[1] - half, 1), pltpu.roll(x, half, 1))


def turn(x, cosine, sine):
    return x * cosine + partner(x) * sine


def repeated(table, rows):
    return jnp.concatenate([table] * (rows // table.shape[0]), axis=0)


def project_body(ne, nd, *refs):
    tokens_ref, gain_ref, segments_ref, tables_all, wq_ref, wk_ref, wv_ref, cot_ref = refs[:8]
    n_ref, q_ref, tables_ref, starts_ref, key_all, value_all, cot_all = refs[8:15]
    wq, wk, wv, key_own, value_own, count_own, count_all = refs[15:22]
    sem, own_sem, send_sem, recv_sem, line_send, line_recv = refs[22:]
    ep, dp = lax.axis_index("ep"), lax.axis_index("dp")
    micro, rows = segments_ref.shape
    loads = [
        pltpu.make_async_copy(src, dst, sem.at[i])
        for i, (src, dst) in enumerate(
            (
                (tables_all.at[:, pl.ds(pl.multiple_of(dp * rows, rows), rows)], tables_ref),
                (wk_ref, wk),
                (wv_ref, wv),
                (wq_ref, wq),
            )
        )
    ]
    for copy in loads:
        copy.start()
    arrays = ((count_own, count_all), (key_own, key_all), (value_own, value_all))
    gathers = [
        PairGather(
            dp, nd, gather_orders(nd)[i // 2], own, whole, send_sem.at[i], recv_sem.at[i]
        )
        for i, (own, whole) in enumerate(arrays)
    ]
    own_copies = [
        pltpu.make_async_copy(own, whole.at[dp], own_sem.at[i])
        for i, (own, whole) in enumerate(arrays)
    ]

    line = LineGather(ep, ne, cot_ref, cot_all, line_send, line_recv)
    own_copies.append(pltpu.make_async_copy(cot_ref.at[0], cot_all.at[ep, 0], own_sem.at[3]))

    def leave(i):
        gathers[i].start()
        own_copies[i].start()

    segments = segments_ref[...]
    lane = lax.broadcasted_iota(jnp.int32, (micro, count_own.shape[1]), 1)
    counts = jnp.zeros(lane.shape, F32)
    for i in range(SEGMENT_IDS):
        held = jnp.sum((segments == i).astype(F32), axis=1, keepdims=True)
        counts = counts + jnp.where(lane == i, held, 0.0)
    count_own[...] = jnp.zeros_like(count_own)
    count_own[:micro] = counts
    greet(ep, dp, ne, nd)
    leave(0)
    line.step(0, 0)
    own_copies[3].start()

    x = tokens_ref[...].astype(F32)
    rounded = (x * rms_scale(x) * gain_ref[...]).astype(BF16)
    normed = rounded
    loads[0].wait()
    cosine, sine = (repeated(tables_ref[i], x.shape[0]) for i in range(2))
    tile = 256
    steps = (
        (wk, key_own, True, 1),
        (wv, value_own, False, 2),
        (wq, q_ref, True, None),
    )
    for copy, (w, out, turned, array) in zip(loads[1:], steps):
        copy.wait()
        for c in range(0, w.shape[1], tile):
            y = dot(normed, w[:, c : c + tile])
            if turned:
                for i in range(0, tile, 128):
                    out[:, c + i : c + i + 128] = turn(y[:, i : i + 128], cosine, sine).astype(BF16)
            else:
                out[:, c : c + tile] = y.astype(BF16)
        if array is not None:
            leave(array)
    n_ref[...] = rounded.astype(F32).T.astype(BF16)
    hops = iter(range(1, ne))
    for t in range(bit_count(nd)):
        for each in gathers:
            each.step(t)
        for s in hops:
            line.step(0, s)
            break
    for s in hops:
        line.step(0, s)
    for copy in own_copies:
        copy.wait()
    totals = jnp.sum(count_all[...], axis=0)
    padded = jnp.concatenate([segments, jnp.zeros((8 - micro, rows), jnp.int32)], axis=0)
    column = padded.astype(F32).T
    ids = lax.broadcasted_iota(jnp.int32, (rows, totals.shape[1]), 1).astype(F32)
    for m in range(micro):
        lower = jnp.where(ids < column[:, m : m + 1], totals[m : m + 1], 0.0)
        starts_ref[m * rows : (m + 1) * rows] = jnp.sum(lower, axis=1, keepdims=True).astype(
            jnp.int32
        )
    for each in gathers:
        each.wait_sends()
    line.wait_sends(0)


def project(tokens, gain, segments, tables, w_query, w_key, w_value, cot, ne, nd, collective):
    rows, width = tokens.shape
    micro, count = segments.shape
    keys = jax.ShapeDtypeStruct((nd, rows, w_key.shape[1]), BF16)
    return pl.pallas_call(
        functools.partial(project_body, ne, nd),
        out_shape=[
            jax.ShapeDtypeStruct((width, rows), BF16),
            jax.ShapeDtypeStruct((rows, w_query.shape[1]), BF16),
            jax.ShapeDtypeStruct((2, count, tables.shape[2]), F32),
            jax.ShapeDtypeStruct((rows, 1), jnp.int32),
            keys,
            keys,
            jax.ShapeDtypeStruct((ne, 1) + cot.shape[1:], BF16),
        ],
        in_specs=[VMEM] * 3 + [ANY] * 5,
        out_specs=[VMEM] * 4 + [ANY] * 3,
        scratch_shapes=[pltpu.VMEM(w.shape, BF16) for w in (w_query, w_key, w_value)]
        + [pltpu.VMEM(keys.shape[1:], BF16)] * 2
        + [pltpu.VMEM((8, 128), F32), pltpu.VMEM((nd, 8, 128), F32)]
        + [DMA((4,)), DMA((4,)), DMA((3, nd - 1)), DMA((3, nd - 1))]
        + [DMA((1, 2, ne - 1)), DMA((1, 2, ne - 1))],
        compiler_params=pltpu.CompilerParams(
            vmem_limit_bytes=60 * 2**20, collective_id=collective, has_side_effects=True
        ),
        cost_estimate=cost(26),
    )(tokens, gain, segments, tables, w_query, w_key, w_value, cot)


def spread(x):
    lane = lax.broadcasted_iota(jnp.int32, (x.shape[0], 128), 1)
    low = lane < HEAD_DIM
    zero = jnp.zeros((), x.dtype)
    first, second = x[:, :128], x[:, 128:]
    return jnp.concatenate(
        [
            jnp.where(low, first, zero),
            jnp.where(low, pltpu.roll(first, HEAD_DIM, 1), zero),
            jnp.where(low, zero, pltpu.roll(second, HEAD_DIM, 1)),
            jnp.where(low, zero, second),
        ],
        axis=0,
    )


def gathered(x, rows):
    lane = lax.broadcasted_iota(jnp.int32, (rows, 128), 1)
    low = lane < HEAD_DIM
    h = [x[i * rows : (i + 1) * rows] for i in range(4)]
    return jnp.concatenate(
        [
            jnp.where(low, h[0], pltpu.roll(h[1], HEAD_DIM, 1)),
            jnp.where(low, pltpu.roll(h[2], HEAD_DIM, 1), h[3]),
        ],
        axis=1,
    )


def window_of(dp, span):
    return jnp.maximum(dp - (span - 1), 0)


def window_scores(dp, span, rows, starts_ref, q, k):
    keys = k.shape[0]
    scores = dot(q, k, ((1,), (1,))).reshape(4, rows, keys)
    key_pos = window_of(dp, span) * rows + lax.broadcasted_iota(jnp.int32, (rows, keys), 1)
    query_pos = dp * rows + lax.broadcasted_iota(jnp.int32, (rows, keys), 0)
    allowed = (key_pos <= query_pos) & (key_pos >= starts_ref[...])
    return jnp.where(allowed[None], scores, MASKED).reshape(4 * rows, keys)


def in_window(ref, dp, span):
    block = ref[pl.ds(window_of(dp, span), span)]
    return block.reshape(span * block.shape[1], block.shape[2])


SCALE = HEAD_DIM ** (-0.5)


class LineGather:
    def __init__(self, ep, ne, own, whole, send_sem, recv_sem):
        self.ep, self.ne, self.own, self.whole = ep, ne, own, whole
        self.send_sem, self.recv_sem = send_sem, recv_sem

    def copy(self, m, s, way):
        shard = lax.rem(self.ep - way * s + self.ne, self.ne)
        k = 0 if way == 1 else 1
        return remote(
            self.own.at[m] if s == 0 else self.whole.at[shard, m],
            self.whole.at[shard, m],
            self.send_sem.at[m, k, s],
            self.recv_sem.at[m, k, s],
            {"ep": lax.rem(self.ep + way + self.ne, self.ne)},
        )

    def sends(self, s, way):
        ep, ne = self.ep, self.ne
        return (ep >= s) & (ep < ne - 1) if way == 1 else (ep + s <= ne - 1) & (ep >= 1)

    def receives(self, s, way):
        return self.ep >= 1 + s if way == 1 else self.ep + 1 + s <= self.ne - 1

    def step(self, m, s):
        for way in (1, -1):
            if s > 0:

                @pl.when(self.receives(s - 1, way))
                def _(way=way):
                    self.copy(m, s - 1, way).wait_recv()

            if s < self.ne - 1:

                @pl.when(self.sends(s, way))
                def _(way=way):
                    self.copy(m, s, way).start()

    def wait_sends(self, m):
        for s in range(self.ne - 1):
            for way in (1, -1):

                @pl.when(self.sends(s, way))
                def _(s=s, way=way):
                    self.copy(m, s, way).wait_send()


def attend_body(span, ne, nd, micro, *refs):
    starts_ref, q_ref, k_ref, v_ref, tokens_ref, wo_ref, gain_ref, router_ref, hit_ref = refs[:9]
    out_ref, log_ref, res_ref, normed_ref, probs_ref, normed_all, marked_all = refs[9:16]
    attn, normed_own, marked_own, own_sem, send_sem, recv_sem = refs[16:]
    ep, dp = lax.axis_index("ep"), lax.axis_index("dp")
    m, h = pl.program_id(0), pl.program_id(1)
    final = pl.num_programs(1) - 1
    rows = q_ref.shape[0]
    lines = [
        LineGather(ep, ne, own, whole, send_sem.at[i], recv_sem.at[i])
        for i, (own, whole) in enumerate(((normed_own, normed_all), (marked_own, marked_all)))
    ]

    def hop(batch, s):
        for line in lines:
            line.step(batch, s)

    @pl.when((m == 0) & (h == 0))
    def _():
        greet(ep, dp, ne, nd)

    q = spread(q_ref[...].astype(F32) * SCALE).astype(BF16)
    scores = window_scores(dp, span, rows, starts_ref, q, in_window(k_ref, dp, span))
    top = jnp.max(scores, axis=1, keepdims=True)
    terms = jnp.exp(scores - top)
    total = jnp.sum(terms, axis=1, keepdims=True)
    log_ref[0, 0] = top + jnp.log(total)
    weights = (terms * (1.0 / total)).astype(BF16)
    out = gathered(dot(weights, in_window(v_ref, dp, span)), rows).astype(BF16)
    out_ref[...] = out
    attn[:, pl.ds(pl.multiple_of(h * out.shape[1], out.shape[1]), out.shape[1])] = out

    def own_copies(batch):
        return [
            pltpu.make_async_copy(line.own.at[batch], line.whole.at[ep, batch], own_sem.at[i, batch])
            for i, line in enumerate(lines)
        ]

    for batch in range(micro):

        @pl.when((m == batch) & (h == final))
        def _(batch=batch):
            for earlier in range(batch):
                hop(earlier, batch - earlier)
            residual = tokens_ref[...].astype(F32) + dot(attn[...], wo_ref[...])
            res_ref[...] = residual
            normed = (residual * rms_scale(residual) * gain_ref[...]).astype(BF16)
            normed_ref[...] = normed
            normed_own[batch] = normed
            hit = hit_ref[...] > 0.0
            logits = jnp.where(hit, dot(router_ref[...], normed, ((1,), (1,))), MASKED)
            terms = jnp.exp(logits - jnp.max(logits, axis=0, keepdims=True))
            terms = jnp.where(hit, terms, 0.0)
            probs = terms / jnp.sum(terms, axis=0, keepdims=True)
            probs_ref[...] = probs
            marked_own[batch] = jnp.where(hit, probs, -1.0)
            hop(batch, 0)
            for copy in own_copies(batch):
                copy.start()
            if batch == micro - 1:
                for t in range(1, ne + micro - 1):
                    for each in range(micro):
                        s = t + micro - 1 - each
                        if s < ne:
                            hop(each, s)
                for each in range(micro):
                    for line in lines:
                        line.wait_sends(each)
                    for copy in own_copies(each):
                        copy.wait()


def attention_specs(micro, rows, nd):
    pairs = KV_HEADS // 2
    mine = pl.BlockSpec((rows, 4 * HEAD_DIM), lambda m, h, *_: (m, h))
    theirs = pl.BlockSpec((nd, rows, 2 * HEAD_DIM), lambda m, h, *_: (0, m, h))
    column = pl.BlockSpec((rows, 1), lambda m, h, *_: (m, 0))
    logs = pl.BlockSpec((1, 1, 4 * rows, 1), lambda m, h, *_: (m, h, 0, 0))
    log_shape = jax.ShapeDtypeStruct((micro, pairs, 4 * rows, 1), F32)
    return (micro, pairs), mine, theirs, column, logs, log_shape


def attend(
    starts, queries, keys, values, tokens, w_out, gain, router, hit, micro, rows, ne, collective
):
    nd, width = keys.shape[0], tokens.shape[1]
    grid, mine, theirs, column, logs, log_shape = attention_specs(micro, rows, nd)
    one = pl.Buffered(1)
    whole = lambda v: pl.BlockSpec(v.shape, lambda m, h: (0, 0), pipeline_mode=one)
    wide = pl.BlockSpec((rows, width), lambda m, h: (m, 0))
    chosen = pl.BlockSpec((hit.shape[0], rows), lambda m, h: (0, m))
    every = micro * rows
    return pl.pallas_call(
        functools.partial(attend_body, nd // 2 + 1, ne, nd, micro),
        grid=grid,
        in_specs=[column, mine, theirs, theirs, wide, whole(w_out), whole(gain), whole(router)]
        + [chosen],
        out_specs=[mine, logs, wide, wide, chosen, ANY, ANY],
        out_shape=[
            jax.ShapeDtypeStruct(queries.shape, BF16),
            log_shape,
            jax.ShapeDtypeStruct((every, width), F32),
            jax.ShapeDtypeStruct((every, width), BF16),
            jax.ShapeDtypeStruct(hit.shape, F32),
            jax.ShapeDtypeStruct((ne, micro, rows, width), BF16),
            jax.ShapeDtypeStruct((ne, micro, hit.shape[0], rows), F32),
        ],
        scratch_shapes=[
            pltpu.VMEM((rows, width), BF16),
            pltpu.VMEM((micro, rows, width), BF16),
            pltpu.VMEM((micro, hit.shape[0], rows), F32),
            DMA((2, micro)),
            DMA((2, micro, 2, ne - 1)),
            DMA((2, micro, 2, ne - 1)),
        ],
        compiler_params=pltpu.CompilerParams(
            vmem_limit_bytes=60 * 2**20, collective_id=collective, has_side_effects=True
        ),
        cost_estimate=cost(50),
    )(starts, queries, keys, values, tokens, w_out, gain, router, hit)


def attend_back_body(span, ne, nd, micro, skip, full, orders, *refs):
    refs = list(refs)

    def take(n):
        return [refs.pop(0) for _ in range(n)]

    starts_ref, q_ref, k_ref, v_ref, log_ref, tables_ref = take(6)
    cot_ref, dots_ref, probs_ref, grad_ref, residual_ref, gain_ref, normed_ref, attn_ref = take(8)
    wo_ref, router_ref, mix_ref = take(3)
    n = len(orders)
    sources, extras = take(n), take(n)
    dq_ref, res_out, wo_out, router_out, gain_out, dk_out, dv_out, mix_out = take(8)
    outs = take(n)
    grads, mix_held, mix_in = take(3)
    kv_held, kv_in = take(2), take(2)
    held, more, landing = take(n), take(n), take(n)
    load_sem, out_sem, send_sem, recv_sem, kv_send, kv_recv, kv_out, mix_sem, line_send, line_recv = refs
    ep, dp = lax.axis_index("ep"), lax.axis_index("dp")
    step = pl.program_id(0) * pl.num_programs(1) + pl.program_id(1)
    final = pl.num_programs(0) * pl.num_programs(1) - 1
    sums = []
    for a in range(n):
        part = pl.ds(skip, sources[a].shape[1] - skip)
        loads = [
            pltpu.make_async_copy(src.at[:, part], dst, load_sem.at[a, i])
            for i, (src, dst) in enumerate(((sources[a], held[a]), (extras[a], more[a])))
        ]
        sums.append(
            PairSum(
                dp, orders[a], loads, held[a], more[a], landing[a], send_sem.at[a], recv_sem.at[a]
            )
        )
    batch_sums = [
        [
            PairSum(
                dp,
                full[i],
                [],
                kv_held[i].at[m],
                None,
                kv_in[i].at[m],
                kv_send.at[i, m],
                kv_recv.at[i, m],
            )
            for i in range(2)
        ]
        for m in range(micro)
    ]
    lines = [
        LineSum(ep, ne, mix_held.at[m], mix_in.at[m], line_send.at[m], line_recv.at[m])
        for m in range(micro)
    ]
    count = q_ref.shape[0]
    line_loads = [
        pltpu.make_async_copy(
            mix_ref.at[:, pl.ds(m * count, count)], mix_held.at[m], mix_sem.at[0, m]
        )
        for m in range(micro)
    ]
    turns = bit_count(nd)

    def batch_step(m, t):
        if t <= turns:
            for each in batch_sums[m]:
                each.step(t)

    def line_step(m, t):
        if t < ne:
            lines[m].step(t)

    @pl.when(step == 0)
    def _():
        for copy in line_loads:
            copy.start()
        for each in sums:
            each.load()
        greet(ep, dp, ne, nd)
        for m in range(micro):
            line_loads[m].wait()
            line_step(m, 0)
        for each in sums:
            each.step(0)
        for i in range(2):
            kv_held[i][...] = jnp.zeros_like(kv_held[i])
        rows = q_ref.shape[0]
        pairs = [dots_ref[:, :, m, :].reshape(-1, rows) for m in range(micro)]
        pair = jnp.concatenate(pairs, axis=1)
        probs = probs_ref[...]
        grad_logits = probs * (pair - jnp.sum(probs * pair, axis=0, keepdims=True))
        high = grad_logits.astype(BF16)
        low = (grad_logits - high.astype(F32)).astype(BF16)
        normed = normed_ref[...]
        router_out[...] = dot(high, normed) + dot(low, normed)
        router = router_ref[...]
        grad_normed = (
            grad_ref[...].astype(F32)
            + dot(high, router, ((0,), (0,)))
            + dot(low, router, ((0,), (0,)))
        )
        residual = residual_ref[...]
        r = rms_scale(residual)
        gain_out[...] = jnp.sum(grad_normed * residual * r, axis=0, keepdims=True)
        scaled = grad_normed * gain_ref[...]
        mean = jnp.mean(scaled * residual, axis=1, keepdims=True)
        grad_residual = cot_ref[...].astype(F32) + r * scaled - residual * (r * r * r) * mean
        res_out[...] = grad_residual
        low_res = grad_residual.astype(BF16)
        tile = 256
        for c in range(0, wo_ref.shape[1], tile):
            y = dot(attn_ref[...], low_res[:, c : c + tile], ((0,), (0,))).astype(BF16)
            a, at = c // wo_out.shape[4], c % wo_out.shape[4]
            share = wo_out.shape[3]
            for e in range(ne):
                for d in range(nd):
                    i = (e * nd + d) * share
                    slot = slot_of(full[a % 2], d)
                    wo_out[a, slot, e, :, at : at + tile] = y[i : i + share]
        for c in range(0, wo_ref.shape[0], tile):
            grads[c // tile] = dot(low_res, wo_ref[c : c + tile, :], ((1,), (1,))).astype(BF16)

    rows = q_ref.shape[0]
    q = spread(q_ref[...].astype(F32) * SCALE).astype(BF16)
    mine = pl.ds(pl.multiple_of(pl.program_id(0) * rows, rows), rows)
    g = spread(grads[pl.program_id(1), mine, :].astype(F32)).astype(BF16)
    k, v = in_window(k_ref, dp, span), in_window(v_ref, dp, span)
    scores = window_scores(dp, span, rows, starts_ref, q, k)
    probs = jnp.exp(scores - log_ref[0, 0])
    grad_probs = dot(g, v, ((1,), (1,)))
    total = jnp.sum(probs * grad_probs, axis=1, keepdims=True)
    grad_scores = (probs * (grad_probs - total)).astype(BF16)
    dq = gathered(dot(grad_scores, k) * SCALE, rows)
    cosine, sine = tables_ref[0], -tables_ref[1]
    for i in range(0, dq.shape[1], 128):
        dq_ref[:, i : i + 128] = turn(dq[:, i : i + 128], cosine, sine).astype(BF16)
    here = pl.ds(window_of(dp, span), span)
    head = pl.program_id(1)
    at = pl.ds(pl.multiple_of(head * 2 * HEAD_DIM, 2 * HEAD_DIM), 2 * HEAD_DIM)
    batch = pl.program_id(0)
    dk = dot(grad_scores, q, ((0,), (0,))).astype(BF16)
    kv_held[0][batch, here, :, at] = dk.reshape(span, rows, dk.shape[1])
    dv = dot(probs.astype(BF16), g, ((0,), (0,))).astype(BF16)
    kv_held[1][batch, here, :, at] = dv.reshape(span, rows, dv.shape[1])

    heads = pl.num_programs(1)
    for m in range(micro):

        @pl.when((batch == m) & (head == heads - 1))
        def _(m=m):
            batch_step(m, 0)

        if m > 0:

            @pl.when((batch == m) & (head == 0))
            def _(m=m):
                batch_step(m - 1, 1)

    @pl.when(step == final // 4 + 1)
    def _():
        line_step(0, 1)

    @pl.when(step == final // 2 + 2)
    def _():
        line_step(1, 1)

    @pl.when(step == final)
    def _():
        copies = []

        def leave(copy):
            copy.start()
            copies.append(copy)

        line_step(0, 2)
        last = micro - 1
        batch_step(last - 1, 2)
        for t in range(1, max([len(order) for order in orders] + [0]) + 1):
            for each in sums:
                each.step(t)
        for a, each in enumerate(sums):
            leave(pltpu.make_async_copy(each.own(), outs[a], out_sem.at[a]))
        batch_step(last, 1)
        line_step(1, 2)
        for t in range(3, turns + 1):
            batch_step(last - 1, t)
        batch_step(last, 2)
        for t in range(3, ne):
            line_step(0, t)
            line_step(1, t)
        for t in range(3, turns + 1):
            batch_step(last, t)
        for m in range(micro):
            own = pl.ds(m * rows, rows)
            for i, out in enumerate((dk_out, dv_out)):
                leave(pltpu.make_async_copy(batch_sums[m][i].own(), out.at[own], kv_out.at[i, m]))
            leave(pltpu.make_async_copy(lines[m].own(), mix_out.at[own], mix_sem.at[1, m]))
        for each in sums + lines + sum(batch_sums, []):
            each.wait_sends()
        for copy in copies:
            copy.wait()


def attend_back(
    starts,
    queries,
    keys,
    values,
    logs_in,
    tables,
    cot,
    dots,
    probs,
    grad_normed,
    residual,
    gain,
    normed,
    attn,
    w_out,
    router,
    mix,
    sums,
    full,
    skip,
    collective,
):
    nd, ne, micro, rows = keys.shape[0], dots.shape[0], dots.shape[2], dots.shape[3]
    every, width = residual.shape
    grid, mine, theirs, column, logs, _ = attention_specs(micro, rows, nd)
    one = pl.Buffered(1)
    whole = lambda v: pl.BlockSpec(v.shape, lambda m, h: (0,) * len(v.shape), pipeline_mode=one)
    n = len(sums)
    shapes = [(v.shape[0], v.shape[1] - skip) + v.shape[2:] for v, _, _ in sums]
    deep = max([s[0] - 1 for s in shapes] + [1])
    some = max(n, 1)
    kv_width = keys.shape[2]
    wo_shape = (width // kv_width, nd, ne, w_out.shape[0] // (ne * nd), kv_width)
    before = [cot, dots, probs, grad_normed, residual, gain, normed, attn, w_out, router]
    after = [
        jax.ShapeDtypeStruct((every, width), F32),
        jax.ShapeDtypeStruct(wo_shape, BF16),
        jax.ShapeDtypeStruct(router.shape, F32),
        jax.ShapeDtypeStruct((1, width), F32),
    ]
    tile = 4 * HEAD_DIM
    return pl.pallas_call(
        functools.partial(
            attend_back_body,
            nd // 2 + 1,
            ne,
            nd,
            micro,
            skip,
            tuple(map(tuple, full)),
            tuple(tuple(order) for _, order, _ in sums),
        ),
        grid=grid,
        in_specs=[column, mine, theirs, theirs, logs, whole(tables)]
        + [whole(v) for v in before]
        + [ANY] * (2 * n + 1),
        out_specs=[mine] + [whole(v) for v in after] + [ANY] * (n + 3),
        out_shape=[jax.ShapeDtypeStruct(queries.shape, BF16)]
        + after
        + [jax.ShapeDtypeStruct((every, keys.shape[2]), BF16)] * 2
        + [jax.ShapeDtypeStruct((every, width), BF16)]
        + [jax.ShapeDtypeStruct(s[1:], BF16) for s in shapes],
        scratch_shapes=[
            pltpu.VMEM((w_out.shape[0] // tile, every, tile), BF16),
            pltpu.VMEM((micro, ne, rows, width), BF16),
            pltpu.VMEM((micro, 2, ne, rows, width), BF16),
        ]
        + [pltpu.VMEM((micro, nd, rows, keys.shape[2]), BF16)] * 2
        + [pltpu.VMEM((micro, nd - 1, rows, keys.shape[2]), BF16)] * 2
        + [pltpu.VMEM(s, BF16) for s in shapes] * 2
        + [pltpu.VMEM((s[0] - 1,) + s[1:], BF16) for s in shapes]
        + [
            DMA((some, 2)),
            DMA((some,)),
            DMA((some, deep)),
            DMA((some, deep)),
            DMA((2, micro, nd - 1)),
            DMA((2, micro, nd - 1)),
            DMA((2, micro)),
            DMA((2, micro)),
            DMA((micro, 2, ne)),
            DMA((micro, 2, ne)),
        ],
        compiler_params=pltpu.CompilerParams(
            vmem_limit_bytes=63 * 2**20, collective_id=collective, has_side_effects=True
        ),
        cost_estimate=cost(40),
    )(
        starts,
        queries,
        keys,
        values,
        logs_in,
        tables,
        *before,
        mix,
        *[v for v, _, _ in sums],
        *[extra for _, _, extra in sums],
    )


def finish_body(ne, nd, orders, n_out, *refs):
    refs = list(refs)

    def take(n):
        return [refs.pop(0) for _ in range(n)]

    n_ref, dq_ref, dk_ref, dv_ref, tables_ref, tokens_ref, gain_ref, router_ref, gain_two = take(9)
    res_ref, wq_ref, wk_ref, wv_ref, wo_ref = take(5)
    (tok_out,) = take(1)
    count = 2 * n_out + 3
    outs, held, pair_in, line_in = take(count), take(count), take(count), take(count)
    dk_turned, wq, wk, wv, res = take(5)
    load_sem, own_sem, out_sem, dp_send, dp_recv, ep_send, ep_recv = refs
    ep, dp = lax.axis_index("ep"), lax.axis_index("dp")
    columns = held[0].shape[3]
    own = [
        pltpu.make_async_copy(src, dst, own_sem.at[i])
        for i, (src, dst) in enumerate(
            ((wq_ref, wq), (wk_ref, wk), (wv_ref, wv), (res_ref, res))
        )
    ]
    sums = []
    for a in range(count):
        loads = []
        if a < n_out:
            loads = [pltpu.make_async_copy(wo_ref.at[a], held[a], load_sem.at[a])]
        sums.append(
            PairSum(
                dp,
                orders[a % 2],
                loads,
                held[a],
                None,
                pair_in[a],
                dp_send.at[a],
                dp_recv.at[a],
                major=True,
            )
        )
    spreads = [
        SpreadSum(ep, ne, sums[a].own(), line_in[a], ep_send.at[a], ep_recv.at[a])
        for a in range(count)
    ]
    early, made, small = sums[:n_out], sums[n_out:-1], sums[-1]
    queries, others = made[:n_out], made[n_out:]
    for each in early:
        each.load()
    for copy in own:
        copy.start()
    greet(ep, dp, ne, nd)
    turns = bit_count(nd)

    def steps(group, t):
        for each in group:
            if t <= turns:
                each.step(t)

    def spread_steps(group, t):
        for each in group:
            spreads[sums.index(each)].step(t)

    steps(early, 0)

    normed = n_ref[...]
    cosine, sine = (repeated(tables_ref[i], normed.shape[1]) for i in range(2))
    sine = -sine
    for i in range(0, dk_ref.shape[1], 128):
        part = dk_ref[:, i : i + 128].astype(F32)
        dk_turned[:, i : i + 128] = turn(part, cosine, sine).astype(BF16)
    tile = 256

    def product(grad, first, each):
        share = each.held.shape[2]
        for c in range(0, each.held.shape[3], tile):
            y = dot(normed, grad[:, first + c : first + c + tile]).astype(BF16)
            for e in range(ne):
                for d in range(nd):
                    r = (e * nd + d) * share
                    each.held[slot_of(each.order, d), e, :, c : c + tile] = y[r : r + share]
        each.step(0)

    for i, each in enumerate(made):
        if i < n_out:
            product(dq_ref, i * columns, each)
        else:
            product((dk_turned, dv_ref)[i - n_out], 0, each)
        if i == 0:
            steps(early, 1)
        if i == 2:
            steps(queries, 1)
    for copy in own:
        copy.wait()
    back = dot(dq_ref[...], wq[...], ((1,), (1,)))
    steps(early, 2)
    steps(others, 1)
    back = back + dot(dk_turned[...], wk[...], ((1,), (1,)))
    back = back + dot(dv_ref[...], wv[...], ((1,), (1,)))
    x = tokens_ref[...].astype(F32)
    r = rms_scale(x)
    scaled = back * gain_ref[...]
    tok_out[...] = (
        res[...] + r * scaled - x * (r * r * r) * jnp.mean(scaled * x, axis=1, keepdims=True)
    )
    for t in range(3, turns + 1):
        steps(early, t)
    spread_steps(early, 0)
    one_row = jnp.sum(back * x * r, axis=0, keepdims=True)
    blank = jnp.zeros((held[-1].shape[3] - EXPERTS - 2, x.shape[1]), F32)
    column = jnp.concatenate([router_ref[...], one_row, gain_two[...], blank], axis=0).T
    share = held[-1].shape[2]
    for e in range(ne):
        for d in range(nd):
            i = (e * nd + d) * share
            held[-1][slot_of(small.order, d), e] = column[i : i + share].astype(BF16)
    steps([small], 0)
    steps(queries, 2)
    steps([small], 1)
    for t in range(3, turns + 1):
        steps(queries, t)
    spread_steps(queries, 0)
    steps(others + [small], 2)
    for t in range(3, turns + 1):
        steps(others + [small], t)
    spread_steps(others + [small], 0)
    spread_steps(early, 1)
    spread_steps(queries, 1)
    spread_steps(others + [small], 1)
    copies = []
    for a in range(count):
        copies.append(pltpu.make_async_copy(spreads[a].own(), outs[a], out_sem.at[a]))
        copies[-1].start()
    for each in sums + spreads:
        each.wait_sends()
    for copy in copies:
        copy.wait()


def finish(
    ne,
    nd,
    orders,
    normed,
    grads,
    tables,
    tokens,
    gain,
    grad_residual,
    weights,
    w_out,
    router_grad,
    gain_two_grad,
):
    rows, width = tokens.shape
    share = width // (ne * nd)
    columns = weights[1].shape[1]
    n_out = width // columns
    count = 2 * n_out + 3
    wide = [columns] * (count - 1) + [128]
    return pl.pallas_call(
        functools.partial(finish_body, ne, nd, tuple(map(tuple, orders)), n_out),
        out_shape=[jax.ShapeDtypeStruct((rows, width), F32)]
        + [jax.ShapeDtypeStruct((share, c), BF16) for c in wide],
        in_specs=[VMEM] * 9 + [ANY] * 5,
        out_specs=[VMEM] + [ANY] * count,
        scratch_shapes=[pltpu.VMEM((nd, ne, share, c), BF16) for c in wide]
        + [pltpu.VMEM((nd - 1, ne, share, c), BF16) for c in wide]
        + [pltpu.VMEM((ne - 1, share, c), BF16) for c in wide]
        + [pltpu.VMEM(grads[1].shape, BF16)]
        + [pltpu.VMEM(w.shape, BF16) for w in weights]
        + [pltpu.VMEM((rows, width), F32)]
        + [
            DMA((count,)),
            DMA((4,)),
            DMA((count,)),
            DMA((count, bit_count(nd))),
            DMA((count, bit_count(nd))),
            DMA((count, ne - 1)),
            DMA((count, ne - 1)),
        ],
        compiler_params=pltpu.CompilerParams(
            vmem_limit_bytes=60 * 2**20, collective_id=4, has_side_effects=True
        ),
        cost_estimate=cost(45),
    )(
        normed,
        *grads,
        tables,
        tokens,
        gain,
        router_grad,
        gain_two_grad,
        grad_residual,
        *weights,
        w_out,
    )


def results_body(share, n_out, groups, *refs):
    refs = list(refs)

    def take(n):
        return [refs.pop(0) for _ in range(n)]

    residual_ref, mix_ref = take(2)
    halves = [take(groups) for _ in range(2)]
    dense = take(2 * n_out + 3)
    out_ref, d_out, d_query, d_key, d_value, router, gain_one, gain_two = take(8)
    gate, up, down = refs
    e = pl.program_id(0)

    @pl.when(e == 0)
    def _():
        out_ref[...] = (residual_ref[...] + mix_ref[...].astype(F32)).astype(BF16)
        width = dense[0].shape[1]
        for i in range(n_out):
            d_out[:, i * width : (i + 1) * width] = dense[i][...].astype(F32)
            d_query[:, i * width : (i + 1) * width] = dense[n_out + i][...].astype(F32)
        d_key[...] = dense[2 * n_out][...].astype(F32)
        d_value[...] = dense[2 * n_out + 1][...].astype(F32)
        small = dense[-1][...].astype(F32)
        router[...] = small[:, :EXPERTS]
        turned = small.T
        gain_one[...] = turned[EXPERTS : EXPERTS + 1]
        gain_two[...] = turned[EXPERTS + 1 : EXPERTS + 2]

    k = 0
    for first, second in zip(*halves):
        for m in range(first.shape[0]):

            @pl.when(e == k)
            def _(first=first, second=second, m=m):
                over = first.shape[1] - share
                gate[0] = first[m, :share].astype(F32)
                up[0, :over] = first[m, share:].astype(F32)
                up[0, over:] = second[m, : share - over].astype(F32)
                piece, columns = down.shape[1], second.shape[2]
                for j in range(down.shape[2] // columns):
                    at = share - over + j * piece
                    down[0, :, j * columns : (j + 1) * columns] = second[
                        m, at : at + piece
                    ].astype(F32)

            k += 1


def results(residual, mix, grads, dense, n_out, share, w_gate, w_down, nd, rows_share):
    rows, width = residual.shape
    n_exp, _, inner = w_gate.shape
    piece = w_down.shape[1] // nd
    ins = [residual, *mix, *grads[0], *grads[1], *dense]
    kv = dense[-2].shape[1]
    same = lambda v: pl.BlockSpec(v, lambda e: (0,) * len(v))
    outs = [
        ((rows, width), BF16),
        ((rows_share, width), F32),
        ((rows_share, width), F32),
        ((rows_share, kv), F32),
        ((rows_share, kv), F32),
        ((rows_share, EXPERTS), F32),
        ((1, rows_share), F32),
        ((1, rows_share), F32),
    ]
    experts_out = [((n_exp, share, inner), F32)] * 2 + [((n_exp, piece, width), F32)]
    return pl.pallas_call(
        functools.partial(results_body, share, n_out, len(grads[0])),
        grid=(n_exp,),
        out_shape=[jax.ShapeDtypeStruct(*v) for v in outs + experts_out],
        in_specs=[same(v.shape) for v in ins],
        out_specs=[same(v[0]) for v in outs]
        + [pl.BlockSpec((1,) + v[0][1:], lambda e: (e, 0, 0)) for v in experts_out],
        compiler_params=pltpu.CompilerParams(vmem_limit_bytes=60 * 2**20),
        cost_estimate=cost(6),
    )(*ins)


def per_device(
    tokens,
    segments,
    routes,
    first_gain,
    w_query,
    w_key,
    w_value,
    w_out,
    second_gain,
    w_router,
    w_gate,
    w_up,
    w_down,
    cotangent,
):
    micro, rows, width = tokens.shape
    ne, nd = lax.axis_size("ep"), lax.axis_size("dp")
    kv_width = KV_HEADS * HEAD_DIM
    every = micro * rows

    halfway = HEAD_DIM // 2
    frequency = ROPE_BASE ** (-(np.arange(halfway) * 2.0 / HEAD_DIM))
    angles = np.arange(nd * rows)[:, None] * frequency[None, :]
    lanes = 2 * HEAD_DIM // halfway
    sign = np.where(np.arange(2 * HEAD_DIM) % HEAD_DIM < halfway, -1.0, 1.0)
    tables = np.stack([np.tile(np.cos(angles), lanes), np.tile(np.sin(angles), lanes) * sign])
    tokens_flat = tokens.reshape(every, width)
    gain_one = first_gain.reshape(1, width)
    normed_one, query_rot, tables, starts, key_all, value_all, cot_first = project(
        tokens_flat,
        gain_one,
        segments.reshape(micro, rows),
        jnp.asarray(tables, F32),
        w_query,
        w_key,
        w_value,
        cotangent,
        ne,
        nd,
        0,
    )
    cot_own = cotangent.reshape(every, width)

    def around(value, k):
        return lax.ppermute(value, "ep", [(i, (i + k) % ne) for i in range(ne)])

    rest = cot_own[rows:]
    cots = [cot_first.reshape(ne, rows, width), rest] + [around(rest, k) for k in range(1, ne)]
    routing = routes.reshape(every, routes.shape[2])
    hit = jnp.any(
        jnp.arange(EXPERTS, dtype=jnp.int32)[:, None, None] == routing[None], axis=2
    ).astype(F32)
    router = w_router.T
    attn_low, logs, residual, normed_two, gate_probs, normed_all, marked_all = attend(
        starts,
        query_rot,
        key_all,
        value_all,
        tokens_flat,
        w_out,
        second_gain.reshape(1, width),
        router,
        hit,
        micro,
        rows,
        ne,
        1,
    )
    orders = [order[:-1][::-1] for order in gather_orders(nd)]
    mix, grad_in, pair_dots, *grads = experts(
        normed_all.reshape(ne * every, width),
        cots,
        marked_all.reshape(ne * micro, EXPERTS, rows),
        w_gate,
        w_up,
        w_down,
        micro,
        rows,
        ne,
        nd,
        6,
    )
    kept, landed, last = grads[:2], grads[2:4], grads[4:]
    height = kept[0].shape[2]
    halves = [(slice(None), slice(i * height, (i + 1) * height)) for i in range(2)]
    skip = min(2, kept[0].shape[1])
    more = kept[0].shape[1] > skip
    head = (slice(None), slice(0, skip))
    *grads, grad_back, dots_all = reduce(
        ne,
        nd,
        [(last[k], orders[i], halves[i], None, False) for k in range(2) for i in range(2)]
        + [(kept[i], orders[i][1:], head, landed[i], False) for i in range(2)],
        ((grad_in.reshape(ne, every, width), None),),
        (pair_dots,),
        2,
        40,
    )
    grads_last, grads_head = grads[:4], grads[4:]
    mix = mix.reshape(ne, every, width)
    full = [[0] + order for order in orders]
    (
        grad_query,
        grad_residual,
        grad_w_out,
        grad_router,
        grad_gain_two,
        grad_key,
        grad_value,
        mix_own,
        *grads_more,
    ) = attend_back(
        starts,
        query_rot,
        key_all,
        value_all,
        logs,
        tables,
        cot_own,
        dots_all,
        gate_probs,
        grad_back,
        residual,
        second_gain.reshape(1, width),
        normed_two,
        attn_low,
        w_out,
        router,
        mix,
        [(kept[i], orders[i][1:], landed[i]) for i in range(2)] if more else [],
        full,
        skip,
        5,
    )
    grad_tokens, *dense = finish(
        ne,
        nd,
        full,
        normed_one,
        (grad_query, grad_key, grad_value),
        tables,
        tokens_flat,
        gain_one,
        grad_residual,
        (w_query, w_key, w_value),
        grad_w_out,
        grad_router,
        grad_gain_two,
    )
    (
        output,
        d_out,
        d_query,
        d_key,
        d_value,
        d_router,
        d_gain_one,
        d_gain_two,
        d_gate,
        d_up,
        d_down,
    ) = results(
        residual,
        (mix_own,),
        [
            [grads_head[i]]
            + ([grads_more[i]] if more else [])
            + [grads_last[i][None], grads_last[2 + i][None]]
            for i in range(2)
        ],
        dense,
        width // kv_width,
        width // nd,
        w_gate,
        w_down,
        nd,
        width // (ne * nd),
    )
    return (
        output.reshape(tokens.shape),
        grad_tokens.reshape(tokens.shape),
        d_gain_one.reshape(-1),
        d_query,
        d_key,
        d_value,
        d_out,
        d_gain_two.reshape(-1),
        d_router,
        d_gate,
        d_up,
        d_down,
    )


def solution(mesh):
    in_specs = (
        P(None, ("ep", "dp"), None),
        P(None, "ep", "dp"),
        P(None, ("ep", "dp"), None),
        P(),
        P(),
        P(),
        P(),
        P(),
        P(),
        P(),
        P("ep", None, None),
        P("ep", None, None),
        P("ep", None, None),
        P(None, ("ep", "dp"), None),
    )
    out_specs = (
        P(None, ("ep", "dp"), None),
        P(None, ("ep", "dp"), None),
        P(("ep", "dp")),
        P(("ep", "dp"), None),
        P(("ep", "dp"), None),
        P(("ep", "dp"), None),
        P(("ep", "dp"), None),
        P(("ep", "dp")),
        P(("ep", "dp"), None),
        P("ep", "dp", None),
        P("ep", "dp", None),
        P("ep", "dp", None),
    )
    return jax.shard_map(
        per_device, mesh=mesh, in_specs=in_specs, out_specs=out_specs, check_vma=False
    )
```

```python
import functools

import jax
import jax.numpy as jnp
import numpy as np
from jax import lax
from jax.experimental import pallas as pl
from jax.experimental.pallas import tpu as pltpu
from jax.sharding import PartitionSpec as P

HEADS = 16
KV_HEADS = 8
HEAD_DIM = 64
EXPERTS = 32
CAP = 64
SEGMENT_IDS = 4
EPSILON = 1e-06
ROPE_BASE = 10000.0
MASKED = -1e30
HIGHEST = lax.Precision.HIGHEST
MESH = pl.DeviceIdType.MESH
BF16 = jnp.bfloat16
F32 = jnp.float32
VMEM = pl.BlockSpec(memory_space=pltpu.VMEM)
ANY = pl.BlockSpec(memory_space=pl.ANY)
DMA = pltpu.SemaphoreType.DMA


def bit_count(n):
    return n.bit_length() - 1


def masks(bits):
    out = [0]
    for b in bits:
        out = out + [m | (1 << b) for m in out]
    return out


def gather_orders(n):
    bits = list(range(bit_count(n)))
    return (bits[1:] + bits[:1], bits[:0:-1] + bits[:1])


def greet(ep, dp, ne, nd):
    barrier = pltpu.get_barrier_semaphore()
    for k in range(1, ne):
        pl.semaphore_signal(
            barrier, inc=1, device_id={"ep": lax.rem(ep + k, ne)}, device_id_type=MESH
        )
    for b in range(bit_count(nd)):
        pl.semaphore_signal(
            barrier, inc=1, device_id={"dp": jnp.bitwise_xor(dp, 1 << b)}, device_id_type=MESH
        )
    pl.semaphore_wait(barrier, ne - 1 + bit_count(nd))


def remote(src, dst, send, recv, where):
    return pltpu.make_async_remote_copy(
        src_ref=src, dst_ref=dst, send_sem=send, recv_sem=recv, device_id=where, device_id_type=MESH
    )


class PairGather:
    def __init__(self, dp, nd, order, own, whole, send_sem, recv_sem):
        self.dp, self.order, self.own, self.whole = dp, order, own, whole
        self.send_sem, self.recv_sem = send_sem, recv_sem

    def copy(self, t, m):
        block = jnp.bitwise_xor(self.dp, m)
        k = (1 << t) - 1 + masks(self.order[:t]).index(m)
        return remote(
            self.own if m == 0 else self.whole.at[block],
            self.whole.at[block],
            self.send_sem.at[k],
            self.recv_sem.at[k],
            {"dp": jnp.bitwise_xor(self.dp, 1 << self.order[t])},
        )

    def start(self):
        for t in range(len(self.order)):
            self.copy(t, 0).start()

    def step(self, t, first=0, last=None):
        for m in masks(self.order[:t])[first:last]:
            self.copy(t, m).wait_recv()
            for later in range(t + 1, len(self.order)):
                self.copy(later, m | (1 << self.order[t])).start()

    def wait_sends(self):
        for t in range(len(self.order)):
            for m in masks(self.order[:t]):
                self.copy(t, m).wait_send()


def cost(us):
    return pl.CostEstimate(flops=0, bytes_accessed=int(us * 3.0e6), transcendentals=0)


def add_into(ref, arrived):
    if len(ref.shape) > 2:

        @pl.loop(0, ref.shape[0])
        def _(i):
            add_into(ref.at[i], arrived.at[i])

    else:
        ref[...] = (ref[...].astype(F32) + arrived[...].astype(F32)).astype(ref.dtype)


class PairSum:
    def __init__(self, dp, order, loads, held, extra, landing, send_sem, recv_sem, major=False):
        self.dp, self.order, self.held, self.landing = dp, order, held, landing
        self.send_sem, self.recv_sem = send_sem, recv_sem
        self.extra, self.loads, self.major = extra, loads, major
        self.index = 0
        for b in order:
            side = jnp.bitwise_and(lax.shift_right_logical(dp, b), 1)
            self.index = self.index + (side << self.place(b))

    def place(self, bit):
        if self.major:
            return len(self.order) - 1 - self.order.index(bit)
        return sorted(self.order).index(bit)

    def copies(self, t):
        order = self.order
        if self.major:
            count = 1 << (len(order) - 1 - t)
            first = sum(1 << (len(order) - 1 - i) for i in range(t))
            mine = self.index - lax.rem(self.index, count)
            copy = remote(
                self.held.at[pl.ds(jnp.bitwise_xor(mine, count), count)],
                self.landing.at[pl.ds(first, count)],
                self.send_sem.at[t],
                self.recv_sem.at[t],
                {"dp": jnp.bitwise_xor(self.dp, 1 << order[t])},
            )
            return [(pl.ds(mine, count), pl.ds(first, count), copy)]
        partner = jnp.bitwise_xor(self.index, 1 << self.place(order[t]))
        first = sum(1 << (len(order) - 1 - i) for i in range(t))
        return [
            (
                m,
                first + j,
                remote(
                    self.held.at[jnp.bitwise_xor(partner, m)],
                    self.landing.at[first + j],
                    self.send_sem.at[first + j],
                    self.recv_sem.at[first + j],
                    {"dp": jnp.bitwise_xor(self.dp, 1 << order[t])},
                ),
            )
            for j, m in enumerate(masks([self.place(b) for b in order[t + 1 :]]))
        ]

    def load(self):
        for copy in self.loads:
            copy.start()

    def step(self, t):
        if t == 0:
            for copy in self.loads:
                copy.wait()
            if self.extra is not None:
                add_into(self.held, self.extra)
        elif t <= len(self.order):
            for m, k, copy in self.copies(t - 1):
                copy.wait_recv()
                mine = m if self.major else jnp.bitwise_xor(self.index, m)
                add_into(self.held.at[mine], self.landing.at[k])
        if t < len(self.order):
            for m, k, copy in self.copies(t):
                copy.start()

    def own(self):
        return self.held.at[self.index]

    def wait_sends(self):
        for t in range(len(self.order)):
            for m, k, copy in self.copies(t):
                copy.wait_send()


def slot_of(order, d):
    return sum(((d >> b) & 1) << (len(order) - 1 - i) for i, b in enumerate(order))


class LineSum:
    def __init__(self, ep, ne, blocks, landing, send_sem, recv_sem):
        self.ep, self.ne, self.blocks, self.landing = ep, ne, blocks, landing
        self.send_sem, self.recv_sem = send_sem, recv_sem

    def copy(self, dest, way):
        k = 0 if way == 1 else 1
        return remote(
            self.blocks.at[dest],
            self.landing.at[k, dest],
            self.send_sem.at[k, dest],
            self.recv_sem.at[k, dest],
            {"ep": lax.rem(self.ep + way + self.ne, self.ne)},
        )

    def turn(self, t, way):
        ep, ne = self.ep, self.ne
        dest = ep + ne - 1 - t if way == 1 else ep + t - (ne - 1)
        has = dest <= ne - 1 if way == 1 else dest >= 0
        inner = ep >= 1 if way == 1 else ep <= ne - 2
        return dest, has, inner

    def step(self, t):
        for way in (1, -1):
            dest, has, inner = self.turn(t, way)

            @pl.when(has & inner)
            def _(way=way, dest=dest):
                self.copy(dest, way).wait_recv()
                add_into(self.blocks.at[dest], self.landing.at[0 if way == 1 else 1, dest])

            if t < self.ne - 1:

                @pl.when(has)
                def _(way=way, dest=dest):
                    self.copy(dest, way).start()

    def own(self):
        return self.blocks.at[self.ep]

    def wait_sends(self):
        for t in range(self.ne - 1):
            for way in (1, -1):
                dest, has, inner = self.turn(t, way)

                @pl.when(has)
                def _(way=way, dest=dest):
                    self.copy(dest, way).wait_send()


class SpreadSum:
    def __init__(self, ep, ne, blocks, landing, send_sem, recv_sem):
        self.ep, self.blocks, self.landing = ep, blocks, landing
        self.copies = []
        for k in range(1, ne):
            to = lax.rem(ep + k, ne)
            self.copies.append(
                remote(
                    blocks.at[to],
                    landing.at[k - 1],
                    send_sem.at[k - 1],
                    recv_sem.at[k - 1],
                    {"ep": to},
                )
            )

    def step(self, t):
        if t == 0:
            for copy in self.copies:
                copy.start()
        elif t == 1:
            total = self.blocks[self.ep].astype(F32)
            for k, copy in enumerate(self.copies):
                copy.wait_recv()
                total = total + self.landing[k].astype(F32)
            self.blocks[self.ep] = total.astype(BF16)

    def own(self):
        return self.blocks.at[self.ep]

    def wait_sends(self):
        for copy in self.copies:
            copy.wait_send()


def shape_at(array, where):
    return tuple(len(range(*w.indices(n))) for w, n in zip(where, array.shape)) + array.shape[len(where) :]


def reduce_body(ne, nd, pairs, line_parts, n_swap, *refs):
    refs = list(refs)

    def take(n):
        return [refs.pop(0) for _ in range(n)]

    n_pair, n_line = len(pairs), len(line_parts)
    n_extra = sum(p[2] for p in pairs)
    n_both = sum(p[3] for p in pairs)
    n_sum = n_pair + n_line
    ins, extra_ins, swap_ins = take(n_sum), take(n_extra), take(n_swap)
    outs, swap_outs = take(n_sum), take(n_swap)
    held, extras, pair_in = take(n_sum), take(n_extra), take(n_pair)
    both_in, line_in = take(n_both), take(n_line)
    load_sem, out_sem, dp_send, dp_recv, ep_send, ep_recv, swap_send, swap_recv = refs
    ep, dp = lax.axis_index("ep"), lax.axis_index("dp")
    sums, then = [], []
    for a, (order, where, has_extra, both) in enumerate(pairs):
        targets = [(ins[a], held[a])]
        extra = extras.pop(0) if has_extra else None
        if has_extra:
            targets.append((extra_ins.pop(0), extra))
        loads = [
            pltpu.make_async_copy(src.at[where] if where else src, dst, load_sem.at[a, i])
            for i, (src, dst) in enumerate(targets)
        ]
        sums.append(
            PairSum(dp, order, loads, held[a], extra, pair_in[a], dp_send.at[a], dp_recv.at[a])
        )
        if both:
            i = len(then)
            then.append(
                LineSum(ep, ne, sums[a].own(), both_in[i], ep_send.at[i], ep_recv.at[i])
            )
    lines, line_loads = [], []
    for i in range(n_line):
        a = n_pair + i
        src = ins[a].at[line_parts[i]] if line_parts[i] else ins[a]
        line_loads.append(pltpu.make_async_copy(src, held[a], load_sem.at[a, 0]))
        lines.append(
            LineSum(
                ep, ne, held[a], line_in[i], ep_send.at[n_both + i], ep_recv.at[n_both + i]
            )
        )
    for copy in line_loads:
        copy.start()
    for each in sums:
        each.load()
    greet(ep, dp, ne, nd)
    swaps = []
    for a in range(n_swap):
        src, dst = swap_ins[a], swap_outs[a]
        own = pltpu.make_async_copy(src.at[ep], dst.at[ep], load_sem.at[n_sum + a, 0])
        own.start()
        swaps.append(own)
        for k in range(1, ne):
            to = lax.rem(ep + k, ne)
            copy = remote(
                src.at[to], dst.at[ep], swap_send.at[a, k - 1], swap_recv.at[a, k - 1], {"ep": to}
            )
            copy.start()
            swaps.append(copy)
    for copy in line_loads:
        copy.wait()
    steps = max([len(p[0]) + 1 for p in pairs] + [ne if n_line else 0])
    for t in range(steps):
        if t < ne:
            for each in lines:
                each.step(t)
        for each in sums:
            each.step(t)
    for t in range(ne):
        for each in then:
            each.step(t)
    results, after = [], iter(then)
    for a in range(n_sum):
        if a >= n_pair:
            src = lines[a - n_pair].own()
        else:
            src = next(after).own() if pairs[a][3] else sums[a].own()
        copy = pltpu.make_async_copy(src, outs[a], out_sem.at[a])
        copy.start()
        results.append(copy)
    for each in sums + then + lines:
        each.wait_sends()
    for copy in swaps + results:
        copy.wait()


def reduce(ne, nd, pairs, lines, swaps, collective, us):
    line_parts = tuple(where for _, where in lines)
    line_shapes = [shape_at(v, where) if where else v.shape for v, where in lines]
    lines = [v for v, _ in lines]
    arrays = [p[0] for p in pairs] + list(lines)
    extras = [p[3] for p in pairs if p[3] is not None]
    kinds = tuple((tuple(p[1]), p[2], p[3] is not None, p[4]) for p in pairs)
    shapes = [shape_at(p[0], p[2]) if p[2] else p[0].shape for p in pairs]
    boths = [s for s, p in zip(shapes, pairs) if p[4]]
    results = [s[2:] if p[4] else s[1:] for s, p in zip(shapes, pairs)]
    results += [s[1:] for s in line_shapes]
    scratch = shapes + line_shapes
    scratch += [s for s, p in zip(shapes, pairs) if p[3] is not None]
    scratch += [(s[0] - 1,) + s[1:] for s in shapes]
    scratch += [(2,) + s[1:] for s in boths] + [(2,) + s for s in line_shapes]
    some = lambda n: max(n, 1)
    line_count = some(len(lines) + len(boths))
    deep = max([s[0] - 1 for s in shapes] + [1])
    return pl.pallas_call(
        functools.partial(reduce_body, ne, nd, kinds, line_parts, len(swaps)),
        out_shape=[jax.ShapeDtypeStruct(s, BF16) for s in results]
        + [jax.ShapeDtypeStruct(v.shape, v.dtype) for v in swaps],
        in_specs=[ANY] * (len(arrays) + len(extras) + len(swaps)),
        out_specs=[ANY] * (len(arrays) + len(swaps)),
        scratch_shapes=[pltpu.VMEM(s, BF16) for s in scratch]
        + [
            DMA((len(arrays) + len(swaps), 2)),
            DMA((len(arrays),)),
            DMA((some(len(pairs)), deep)),
            DMA((some(len(pairs)), deep)),
            DMA((line_count, 2, ne)),
            DMA((line_count, 2, ne)),
            DMA((some(len(swaps)), ne - 1)),
            DMA((some(len(swaps)), ne - 1)),
        ],
        compiler_params=pltpu.CompilerParams(
            collective_id=collective, has_side_effects=True, vmem_limit_bytes=60 * 2**20
        ),
        cost_estimate=cost(us),
    )(*arrays, *extras, *swaps)


def dot(a, b, dims=((1,), (0,))):
    return lax.dot_general(a, b, (dims, ((), ())), preferred_element_type=F32)


def expert_body(ne, nd, micro, rows, *refs):
    cots, refs = refs[:2], refs[2:]
    normed_ref, probs_ref, gate_ref, up_ref, down_ref = refs[:5]
    mix_ref, grad_ref, dots_ref = refs[5:8]
    kept, landed, whole = refs[8:10], refs[10:12], refs[12:14]
    rows_in, cots_in, picks, first, second, chances, sides, arrived, leaving = refs[14:23]
    load_sem, store_sem, send_sem, recv_sem, free_sem, far_send, far_recv = refs[23:]
    e = pl.program_id(0)
    last = pl.num_programs(0) - 1
    ep, dp = lax.axis_index("ep"), lax.axis_index("dp")
    other = {"dp": jnp.bitwise_xor(dp, 1)}
    every = micro * rows
    blocks = ne * micro
    width = first.shape[1]
    n_exp = rows_in.shape[1]

    core = jnp.bitwise_and(dp, 1)
    keep, send = sides.at[core], sides.at[1 - core]

    def exchange():
        return remote(send, arrived, send_sem, recv_sem, other)

    def loads():
        out = [
            pltpu.make_async_copy(normed_ref, first, load_sem.at[ne]),
            pltpu.make_async_copy(
                probs_ref.at[:, pl.ds(pl.multiple_of(ep * n_exp, n_exp), n_exp)],
                chances,
                load_sem.at[ne + 1],
            ),
        ]
        for k in range(ne):
            at = k * every
            for i, part in enumerate(cots):
                out.append(
                    pltpu.make_async_copy(
                        part.at[k],
                        second.at[pl.ds(at, part.shape[1])],
                        load_sem.at[k if i == 0 else ne + 2 + k],
                    )
                )
                at += part.shape[1]
        return out

    def block_at(s):
        return pl.ds(pl.multiple_of(s * rows, rows), rows)

    def returned(t):
        k, m = t // micro, lax.rem(t, micro)
        return lax.rem(ep + k, ne) * micro + m

    def stores(t):
        s = returned(t)
        return (
            pltpu.make_async_copy(
                first.at[block_at(s)], mix_ref.at[block_at(s)], store_sem.at[0, t]
            ),
            pltpu.make_async_copy(
                second.at[block_at(s)], grad_ref.at[block_at(s)], store_sem.at[1, t]
            ),
        )

    def far(i, n):
        return remote(
            leaving.at[i, lax.rem(n, leaving.shape[1])],
            landed[i].at[:, n],
            far_send.at[i, lax.rem(n, leaving.shape[1])],
            far_recv.at[i, n],
            {"dp": jnp.bitwise_xor(dp, 1 << first_bits(nd)[i])},
        )

    def last_copy(k):
        return pltpu.make_async_copy(keep, whole[k], load_sem.at[k])

    def collect():
        exchange().wait_recv()
        pieces, height, slots = sides.shape[1], leaving.shape[3], leaving.shape[1]
        n = e - 1
        early = n_exp - 2

        @pl.when(n < early)
        def _():
            @pl.when(n >= slots)
            def _():
                for i in range(2):
                    far(i, n - slots).wait_send()

            def piece(i, at, other_side):
                bit = first_bits(nd)[i]
                mine = jnp.bitwise_and(lax.shift_right_logical(dp, bit), 1)
                side = 1 - mine if other_side else mine
                low = (1 << (bit - 1)) - 1
                j = ((at & ~low) << 1 | (at & low)) + (side << (bit - 1))
                part = slice(i * height, (i + 1) * height)
                return (keep[j, part].astype(F32) + arrived[j, part].astype(F32)).astype(BF16)

            for i in range(2):
                for at in range(pieces // 2):
                    leaving[i, lax.rem(n, slots), at] = piece(i, at, True)
                far(i, n).start()
            for i in range(2):
                for at in range(pieces // 2):
                    kept[i][at, 0] = piece(i, at, False)

        for k in range(2):

            @pl.when(n == early + k)
            def _(k=k):
                add_into(keep, arrived)
                last_copy(k).start()

    @pl.when(e == 0)
    def _():
        for copy in loads():
            copy.start()
        barrier = pltpu.get_barrier_semaphore()
        met = [0] + sorted(set(first_bits(nd)))
        for bit in met:
            pl.semaphore_signal(
                barrier,
                inc=1,
                device_id={"dp": jnp.bitwise_xor(dp, 1 << bit)},
                device_id_type=MESH,
            )
        pl.semaphore_wait(barrier, len(met))
        before = lax.broadcasted_iota(jnp.int32, (rows, rows), 0)
        after = lax.broadcasted_iota(jnp.int32, (rows, rows), 1)
        earlier = (before < after).astype(BF16)
        slot = lax.broadcasted_iota(jnp.int32, (n_exp, CAP, rows), 1)
        for copy in loads():
            copy.wait()

        @pl.loop(0, blocks)
        def _(s):
            at = block_at(s)
            probs = chances[s]
            hit = probs >= 0.0
            rank = dot(hit.astype(BF16), earlier)
            rank = jnp.where(hit, rank, -1.0).astype(jnp.int32)
            pick = jnp.broadcast_to(rank[:, None, :], (n_exp, CAP, rows)) == slot
            pick_f = pick.astype(F32)
            flat = pick_f.reshape(n_exp * CAP, rows).astype(BF16)
            picks[s] = flat
            rows_in[s] = dot(flat, first[at, :]).astype(BF16).reshape(n_exp, CAP, width)
            cots_in[s] = dot(flat, second[at, :]).astype(BF16).reshape(n_exp, CAP, width)

    @pl.when(e < last)
    def _():
        x = rows_in[:, e].reshape(blocks * CAP, width)
        c = cots_in[:, e].reshape(blocks * CAP, width)
        flat = picks[:, pl.ds(pl.multiple_of(e * CAP, CAP), CAP), :].astype(F32)
        p = jnp.sum(flat * chances[:, pl.ds(e, 1), :], axis=2, keepdims=True)
        p = p.reshape(blocks * CAP, 1)
        w_gate, w_up, w_down = gate_ref[0], up_ref[0], down_ref[0]
        gate_pre = dot(x, w_gate)
        up_pre = dot(x, w_up)
        back = dot(c, w_down, ((1,), (1,)))

        @pl.when(e > 0)
        def _():
            collect()
            pl.semaphore_signal(free_sem, inc=1, device_id=other, device_id_type=MESH)

        sigma = jax.nn.sigmoid(gate_pre)
        silu = gate_pre * sigma
        hidden = (silu * up_pre).astype(BF16)
        out = dot(hidden, w_down) * p
        wide = hidden.astype(F32)
        pair = jnp.sum(wide * back, axis=1, keepdims=True)
        back = back * p
        grad_up = (back * silu).astype(BF16)
        grad_gate = (back * up_pre * (sigma * (1.0 + gate_pre * (1.0 - sigma)))).astype(BF16)
        scaled = (wide * p).astype(BF16)
        grad_x = dot(grad_gate, w_gate, ((1,), (1,))) + dot(grad_up, w_up, ((1,), (1,)))
        pair = jnp.sum(flat * pair.reshape(blocks, CAP, 1), axis=1)
        dots_ref[:, 0] = pair.reshape(ne, micro, rows)

        @pl.when(e > 0)
        def _():
            exchange().wait_send()
            pl.semaphore_wait(free_sem, 1)

        @pl.when(e == n_exp - 1)
        def _():
            last_copy(0).wait()

        def split(value, offset):
            value = value.astype(BF16)
            piece, columns = value.shape[0] // nd, sides.shape[3]

            for i in range(nd):
                for j in range(value.shape[1] // columns):
                    at = offset + j * piece
                    sides[i % 2, i // 2, at : at + piece] = value[
                        i * piece : (i + 1) * piece, j * columns : (j + 1) * columns
                    ]

        share = width // nd
        split(dot(scaled, c, ((0,), (0,))), 2 * share)
        split(dot(x, grad_gate, ((0,), (0,))), 0)
        split(dot(x, grad_up, ((0,), (0,))), share)
        exchange().start()

        rows_in[:, e] = grad_x.astype(BF16).reshape(blocks, CAP, width)
        cots_in[:, e] = out.astype(BF16).reshape(blocks, CAP, width)

    @pl.when(e == last)
    def _():
        @pl.loop(0, blocks)
        def _(t):
            s = returned(t)
            at = block_at(s)
            flat = picks[s]
            for done, slots in ((first, cots_in), (second, rows_in)):
                value = dot(flat, slots[s].reshape(n_exp * CAP, width), ((0,), (0,)))
                done[at, :] = value.astype(BF16)
            for copy in stores(t):
                copy.start()

            @pl.when(t == 1)
            def _():
                collect()
                exchange().wait_send()

        @pl.loop(0, blocks)
        def _(t):
            for copy in stores(t):
                copy.wait()

        last_copy(1).wait()
        early, slots = n_exp - 2, leaving.shape[1]
        for i in range(2):
            for n in range(max(early - slots, 0), early):
                far(i, n).wait_send()

            @pl.loop(0, early)
            def _(n, i=i):
                far(i, n).wait_recv()


def first_bits(nd):
    return [order[-2] for order in gather_orders(nd)]


def experts(normed, cots, probs, w_gate, w_up, w_down, micro, rows, ne, nd, collective):
    n_exp, width, inner = w_gate.shape
    blocks = ne * micro
    half = nd // 2
    packed = 2 * width // nd + (inner // nd) * (width // inner)
    full = (blocks * rows, width)
    weight = lambda e: (jnp.minimum(e, n_exp - 1), 0, 0)
    early = n_exp - 2
    part = (half // 2, early, packed // 2, inner)
    kept = pl.BlockSpec(
        (half // 2, 1, packed // 2, inner), lambda e: (0, jnp.clip(e - 1, 0, early - 1), 0, 0)
    )
    last = (half, packed, inner)
    return pl.pallas_call(
        functools.partial(expert_body, ne, nd, micro, rows),
        grid=(n_exp + 1,),
        in_specs=[ANY] * 4
        + [
            pl.BlockSpec((1, width, inner), weight),
            pl.BlockSpec((1, width, inner), weight),
            pl.BlockSpec((1, inner, width), weight),
        ],
        out_specs=[
            ANY,
            ANY,
            pl.BlockSpec((ne, 1, micro, rows), lambda e: (0, jnp.minimum(e, n_exp - 1), 0, 0)),
            kept,
            kept,
            ANY,
            ANY,
            ANY,
            ANY,
        ],
        scratch_shapes=[
            pltpu.VMEM((blocks, n_exp, CAP, width), BF16),
            pltpu.VMEM((blocks, n_exp, CAP, width), BF16),
            pltpu.VMEM((blocks, n_exp * CAP, rows), BF16),
            pltpu.VMEM(full, BF16),
            pltpu.VMEM(full, BF16),
            pltpu.VMEM((blocks, n_exp, rows), F32),
            pltpu.VMEM((2, half, packed, inner), BF16),
            pltpu.VMEM((half, packed, inner), BF16),
            pltpu.VMEM((2, 2 if early > 2 else 1, half // 2, packed // 2, inner), BF16),
            DMA((2 * ne + 2,)),
            DMA((2, blocks)),
            DMA,
            DMA,
            pltpu.SemaphoreType.REGULAR,
            DMA((2, 2)),
            DMA((2, early)),
        ],
        out_shape=[
            jax.ShapeDtypeStruct(full, BF16),
            jax.ShapeDtypeStruct(full, BF16),
            jax.ShapeDtypeStruct((ne, n_exp, micro, rows), F32),
        ]
        + [jax.ShapeDtypeStruct(part, BF16)] * 4
        + [jax.ShapeDtypeStruct(last, BF16)] * 2,
        compiler_params=pltpu.CompilerParams(
            vmem_limit_bytes=63 * 2**20,
            dimension_semantics=("arbitrary",),
            collective_id=collective,
            has_side_effects=True,
        ),
        cost_estimate=cost(75),
    )(*cots, normed, probs, w_gate, w_up, w_down)


def rms_scale(values):
    return lax.rsqrt(jnp.mean(values * values, axis=-1, keepdims=True) + EPSILON)


def partner(x):
    lane = lax.broadcasted_iota(jnp.int32, x.shape, 1)
    half = HEAD_DIM // 2
    low = lax.rem(lane, HEAD_DIM) < half
    return jnp.where(low, pltpu.roll(x, x.shape[1] - half, 1), pltpu.roll(x, half, 1))


def turn(x, cosine, sine):
    return x * cosine + partner(x) * sine


def repeated(table, rows):
    return jnp.concatenate([table] * (rows // table.shape[0]), axis=0)


def project_body(ne, nd, *refs):
    tokens_ref, gain_ref, segments_ref, tables_all, wq_ref, wk_ref, wv_ref, cot_ref = refs[:8]
    n_ref, q_ref, tables_ref, starts_ref, key_all, value_all, cot_all = refs[8:15]
    wq, wk, wv, key_own, value_own, count_own, count_all = refs[15:22]
    sem, own_sem, send_sem, recv_sem, line_send, line_recv = refs[22:]
    ep, dp = lax.axis_index("ep"), lax.axis_index("dp")
    micro, rows = segments_ref.shape
    loads = [
        pltpu.make_async_copy(src, dst, sem.at[i])
        for i, (src, dst) in enumerate(
            (
                (tables_all.at[:, pl.ds(pl.multiple_of(dp * rows, rows), rows)], tables_ref),
                (wk_ref, wk),
                (wv_ref, wv),
                (wq_ref, wq),
            )
        )
    ]
    for copy in loads:
        copy.start()
    arrays = ((count_own, count_all), (key_own, key_all), (value_own, value_all))
    gathers = [
        PairGather(
            dp, nd, gather_orders(nd)[i // 2], own, whole, send_sem.at[i], recv_sem.at[i]
        )
        for i, (own, whole) in enumerate(arrays)
    ]
    own_copies = [
        pltpu.make_async_copy(own, whole.at[dp], own_sem.at[i])
        for i, (own, whole) in enumerate(arrays)
    ]

    cot_own = cot_ref.at[:, pl.ds(0, cot_all.shape[2])]
    line = LineGather(ep, ne, cot_own, cot_all, line_send, line_recv)
    own_copies.append(pltpu.make_async_copy(cot_own.at[0], cot_all.at[ep, 0], own_sem.at[3]))

    def leave(i):
        gathers[i].start()
        own_copies[i].start()

    segments = segments_ref[...]
    lane = lax.broadcasted_iota(jnp.int32, (micro, count_own.shape[1]), 1)
    counts = jnp.zeros(lane.shape, F32)
    for i in range(SEGMENT_IDS):
        held = jnp.sum((segments == i).astype(F32), axis=1, keepdims=True)
        counts = counts + jnp.where(lane == i, held, 0.0)
    count_own[...] = jnp.zeros_like(count_own)
    count_own[:micro] = counts
    greet(ep, dp, ne, nd)
    leave(0)
    line.step(0, 0)
    own_copies[3].start()

    x = tokens_ref[...].astype(F32)
    rounded = (x * rms_scale(x) * gain_ref[...]).astype(BF16)
    normed = rounded
    loads[0].wait()
    cosine, sine = (repeated(tables_ref[i], x.shape[0]) for i in range(2))
    tile = 256
    steps = (
        (wk, key_own, True, 1),
        (wv, value_own, False, 2),
        (wq, q_ref, True, None),
    )
    for copy, (w, out, turned, array) in zip(loads[1:], steps):
        copy.wait()
        for c in range(0, w.shape[1], tile):
            y = dot(normed, w[:, c : c + tile])
            if turned:
                for i in range(0, tile, 128):
                    out[:, c + i : c + i + 128] = turn(y[:, i : i + 128], cosine, sine).astype(BF16)
            else:
                out[:, c : c + tile] = y.astype(BF16)
        if array is not None:
            leave(array)
    n_ref[...] = rounded.astype(F32).T.astype(BF16)
    hops = iter(range(1, ne))
    for t in range(bit_count(nd)):
        for each in gathers:
            each.step(t, 0, 1)
        for s in hops:
            line.step(0, s)
            break
        for each in gathers:
            each.step(t, 1)
    for s in hops:
        line.step(0, s)
    for copy in own_copies:
        copy.wait()
    totals = jnp.sum(count_all[...], axis=0)
    padded = jnp.concatenate([segments, jnp.zeros((8 - micro, rows), jnp.int32)], axis=0)
    column = padded.astype(F32).T
    ids = lax.broadcasted_iota(jnp.int32, (rows, totals.shape[1]), 1).astype(F32)
    for m in range(micro):
        lower = jnp.where(ids < column[:, m : m + 1], totals[m : m + 1], 0.0)
        starts_ref[m * rows : (m + 1) * rows] = jnp.sum(lower, axis=1, keepdims=True).astype(
            jnp.int32
        )
    for each in gathers:
        each.wait_sends()
    line.wait_sends(0)


def project(
    tokens, gain, segments, tables, w_query, w_key, w_value, cot, early, ne, nd, collective
):
    rows, width = tokens.shape
    micro, count = segments.shape
    keys = jax.ShapeDtypeStruct((nd, rows, w_key.shape[1]), BF16)
    return pl.pallas_call(
        functools.partial(project_body, ne, nd),
        out_shape=[
            jax.ShapeDtypeStruct((width, rows), BF16),
            jax.ShapeDtypeStruct((rows, w_query.shape[1]), BF16),
            jax.ShapeDtypeStruct((2, count, tables.shape[2]), F32),
            jax.ShapeDtypeStruct((rows, 1), jnp.int32),
            keys,
            keys,
            jax.ShapeDtypeStruct((ne, 1, early, width), BF16),
        ],
        in_specs=[VMEM] * 3 + [ANY] * 5,
        out_specs=[VMEM] * 4 + [ANY] * 3,
        scratch_shapes=[pltpu.VMEM(w.shape, BF16) for w in (w_query, w_key, w_value)]
        + [pltpu.VMEM(keys.shape[1:], BF16)] * 2
        + [pltpu.VMEM((8, 128), F32), pltpu.VMEM((nd, 8, 128), F32)]
        + [DMA((4,)), DMA((4,)), DMA((3, nd - 1)), DMA((3, nd - 1))]
        + [DMA((1, 2, ne - 1)), DMA((1, 2, ne - 1))],
        compiler_params=pltpu.CompilerParams(
            vmem_limit_bytes=60 * 2**20, collective_id=collective, has_side_effects=True
        ),
        cost_estimate=cost(26),
    )(tokens, gain, segments, tables, w_query, w_key, w_value, cot)


def spread(x):
    lane = lax.broadcasted_iota(jnp.int32, (x.shape[0], 128), 1)
    low = lane < HEAD_DIM
    zero = jnp.zeros((), x.dtype)
    first, second = x[:, :128], x[:, 128:]
    return jnp.concatenate(
        [
            jnp.where(low, first, zero),
            jnp.where(low, pltpu.roll(first, HEAD_DIM, 1), zero),
            jnp.where(low, zero, pltpu.roll(second, HEAD_DIM, 1)),
            jnp.where(low, zero, second),
        ],
        axis=0,
    )


def gathered(x, rows):
    lane = lax.broadcasted_iota(jnp.int32, (rows, 128), 1)
    low = lane < HEAD_DIM
    h = [x[i * rows : (i + 1) * rows] for i in range(4)]
    return jnp.concatenate(
        [
            jnp.where(low, h[0], pltpu.roll(h[1], HEAD_DIM, 1)),
            jnp.where(low, pltpu.roll(h[2], HEAD_DIM, 1), h[3]),
        ],
        axis=1,
    )


def window_of(dp, span):
    return jnp.maximum(dp - (span - 1), 0)


def window_scores(dp, span, rows, starts_ref, q, k):
    keys = k.shape[0]
    scores = dot(q, k, ((1,), (1,))).reshape(4, rows, keys)
    key_pos = window_of(dp, span) * rows + lax.broadcasted_iota(jnp.int32, (rows, keys), 1)
    query_pos = dp * rows + lax.broadcasted_iota(jnp.int32, (rows, keys), 0)
    allowed = (key_pos <= query_pos) & (key_pos >= starts_ref[...])
    return jnp.where(allowed[None], scores, MASKED).reshape(4 * rows, keys)


def in_window(ref, dp, span):
    block = ref[pl.ds(window_of(dp, span), span)]
    return block.reshape(span * block.shape[1], block.shape[2])


SCALE = HEAD_DIM ** (-0.5)


class LineGather:
    def __init__(self, ep, ne, own, whole, send_sem, recv_sem):
        self.ep, self.ne, self.own, self.whole = ep, ne, own, whole
        self.send_sem, self.recv_sem = send_sem, recv_sem

    def copy(self, m, s, way):
        shard = lax.rem(self.ep - way * s + self.ne, self.ne)
        k = 0 if way == 1 else 1
        return remote(
            self.own.at[m] if s == 0 else self.whole.at[shard, m],
            self.whole.at[shard, m],
            self.send_sem.at[m, k, s],
            self.recv_sem.at[m, k, s],
            {"ep": lax.rem(self.ep + way + self.ne, self.ne)},
        )

    def sends(self, s, way):
        ep, ne = self.ep, self.ne
        return (ep >= s) & (ep < ne - 1) if way == 1 else (ep + s <= ne - 1) & (ep >= 1)

    def receives(self, s, way):
        return self.ep >= 1 + s if way == 1 else self.ep + 1 + s <= self.ne - 1

    def step(self, m, s):
        for way in (1, -1):
            if s > 0:

                @pl.when(self.receives(s - 1, way))
                def _(way=way):
                    self.copy(m, s - 1, way).wait_recv()

            if s < self.ne - 1:

                @pl.when(self.sends(s, way))
                def _(way=way):
                    self.copy(m, s, way).start()

    def wait_sends(self, m):
        for s in range(self.ne - 1):
            for way in (1, -1):

                @pl.when(self.sends(s, way))
                def _(s=s, way=way):
                    self.copy(m, s, way).wait_send()


def attend_body(span, ne, nd, micro, *refs):
    starts_ref, q_ref, k_ref, v_ref, tokens_ref, wo_ref, gain_ref, router_ref, hit_ref = refs[:9]
    cot_ref = refs[9]
    out_ref, log_ref, res_ref, normed_ref, probs_ref, normed_all, marked_all, cot_all = refs[10:18]
    attn, normed_own, marked_own, own_sem, send_sem, recv_sem, cot_sem, cot_send, cot_recv = refs[18:]
    ep, dp = lax.axis_index("ep"), lax.axis_index("dp")
    m, h = pl.program_id(0), pl.program_id(1)
    final = pl.num_programs(1) - 1
    final_step = micro * (KV_HEADS // 2) - 1
    rows = q_ref.shape[0]
    lines = [
        LineGather(ep, ne, own, whole, send_sem.at[i], recv_sem.at[i])
        for i, (own, whole) in enumerate(((normed_own, normed_all), (marked_own, marked_all)))
    ]

    def hop(batch, s):
        for line in lines:
            line.step(batch, s)

    count = cot_all.shape[2]
    cot_own = cot_ref.at[:, pl.ds(cot_ref.shape[1] - count, count)]
    cot_line = LineGather(ep, ne, cot_own, cot_all, cot_send, cot_recv)
    cot_copy = pltpu.make_async_copy(cot_own.at[0], cot_all.at[ep, 0], cot_sem)

    @pl.when((m == 0) & (h == 0))
    def _():
        greet(ep, dp, ne, nd)
        cot_line.step(0, 0)
        cot_copy.start()

    for s in range(1, ne):
        at = min(1 + 2 * s, final_step)

        @pl.when(m * pl.num_programs(1) + h == at)
        def _(s=s):
            cot_line.step(0, s)

    q = spread(q_ref[...].astype(F32) * SCALE).astype(BF16)
    scores = window_scores(dp, span, rows, starts_ref, q, in_window(k_ref, dp, span))
    top = jnp.max(scores, axis=1, keepdims=True)
    terms = jnp.exp(scores - top)
    total = jnp.sum(terms, axis=1, keepdims=True)
    log_ref[0, 0] = top + jnp.log(total)
    weights = (terms * (1.0 / total)).astype(BF16)
    out = gathered(dot(weights, in_window(v_ref, dp, span)), rows).astype(BF16)
    out_ref[...] = out
    attn[:, pl.ds(pl.multiple_of(h * out.shape[1], out.shape[1]), out.shape[1])] = out

    def own_copies(batch):
        return [
            pltpu.make_async_copy(line.own.at[batch], line.whole.at[ep, batch], own_sem.at[i, batch])
            for i, line in enumerate(lines)
        ]

    for batch in range(micro):

        @pl.when((m == batch) & (h == final))
        def _(batch=batch):
            for earlier in range(batch):
                hop(earlier, batch - earlier)
            residual = tokens_ref[...].astype(F32) + dot(attn[...], wo_ref[...])
            res_ref[...] = residual
            normed = (residual * rms_scale(residual) * gain_ref[...]).astype(BF16)
            normed_ref[...] = normed
            normed_own[batch] = normed
            hit = hit_ref[...] > 0.0
            logits = jnp.where(hit, dot(router_ref[...], normed, ((1,), (1,))), MASKED)
            terms = jnp.exp(logits - jnp.max(logits, axis=0, keepdims=True))
            terms = jnp.where(hit, terms, 0.0)
            probs = terms / jnp.sum(terms, axis=0, keepdims=True)
            probs_ref[...] = probs
            marked_own[batch] = jnp.where(hit, probs, -1.0)
            hop(batch, 0)
            for copy in own_copies(batch):
                copy.start()
            if batch == micro - 1:
                for t in range(1, ne + micro - 1):
                    for each in range(micro):
                        s = t + micro - 1 - each
                        if s < ne:
                            hop(each, s)
                for each in range(micro):
                    for line in lines:
                        line.wait_sends(each)
                    for copy in own_copies(each):
                        copy.wait()
                cot_line.wait_sends(0)
                cot_copy.wait()


def attention_specs(micro, rows, nd):
    pairs = KV_HEADS // 2
    mine = pl.BlockSpec((rows, 4 * HEAD_DIM), lambda m, h, *_: (m, h))
    theirs = pl.BlockSpec((nd, rows, 2 * HEAD_DIM), lambda m, h, *_: (0, m, h))
    column = pl.BlockSpec((rows, 1), lambda m, h, *_: (m, 0))
    logs = pl.BlockSpec((1, 1, 4 * rows, 1), lambda m, h, *_: (m, h, 0, 0))
    log_shape = jax.ShapeDtypeStruct((micro, pairs, 4 * rows, 1), F32)
    return (micro, pairs), mine, theirs, column, logs, log_shape


def attend(
    starts, queries, keys, values, tokens, w_out, gain, router, hit, cot, late, micro, rows, ne, collective
):
    nd, width = keys.shape[0], tokens.shape[1]
    grid, mine, theirs, column, logs, log_shape = attention_specs(micro, rows, nd)
    one = pl.Buffered(1)
    whole = lambda v: pl.BlockSpec(v.shape, lambda m, h: (0, 0), pipeline_mode=one)
    wide = pl.BlockSpec((rows, width), lambda m, h: (m, 0))
    chosen = pl.BlockSpec((hit.shape[0], rows), lambda m, h: (0, m))
    every = micro * rows
    return pl.pallas_call(
        functools.partial(attend_body, nd // 2 + 1, ne, nd, micro),
        grid=grid,
        in_specs=[column, mine, theirs, theirs, wide, whole(w_out), whole(gain), whole(router)]
        + [chosen, ANY],
        out_specs=[mine, logs, wide, wide, chosen, ANY, ANY, ANY],
        out_shape=[
            jax.ShapeDtypeStruct(queries.shape, BF16),
            log_shape,
            jax.ShapeDtypeStruct((every, width), F32),
            jax.ShapeDtypeStruct((every, width), BF16),
            jax.ShapeDtypeStruct(hit.shape, F32),
            jax.ShapeDtypeStruct((ne, micro, rows, width), BF16),
            jax.ShapeDtypeStruct((ne, micro, hit.shape[0], rows), F32),
            jax.ShapeDtypeStruct((ne, 1, late, width), BF16),
        ],
        scratch_shapes=[
            pltpu.VMEM((rows, width), BF16),
            pltpu.VMEM((micro, rows, width), BF16),
            pltpu.VMEM((micro, hit.shape[0], rows), F32),
            DMA((2, micro)),
            DMA((2, micro, 2, ne - 1)),
            DMA((2, micro, 2, ne - 1)),
            DMA,
            DMA((1, 2, ne - 1)),
            DMA((1, 2, ne - 1)),
        ],
        compiler_params=pltpu.CompilerParams(
            vmem_limit_bytes=60 * 2**20, collective_id=collective, has_side_effects=True
        ),
        cost_estimate=cost(50),
    )(starts, queries, keys, values, tokens, w_out, gain, router, hit, cot)


def attend_back_body(span, ne, nd, micro, skip, full, orders, *refs):
    refs = list(refs)

    def take(n):
        return [refs.pop(0) for _ in range(n)]

    starts_ref, q_ref, k_ref, v_ref, log_ref, tables_ref = take(6)
    cot_ref, dots_ref, probs_ref, grad_ref, residual_ref, gain_ref, normed_ref, attn_ref = take(8)
    wo_ref, router_ref, mix_ref = take(3)
    n = len(orders)
    sources, extras = take(n), take(n)
    dq_ref, res_out, wo_out, router_out, gain_out, dk_out, dv_out, mix_out = take(8)
    outs = take(n)
    grads, mix_held, mix_in = take(3)
    kv_held, kv_in = take(2), take(2)
    held, more, landing = take(n), take(n), take(n)
    load_sem, out_sem, send_sem, recv_sem, kv_send, kv_recv, kv_out, mix_sem, line_send, line_recv = refs
    ep, dp = lax.axis_index("ep"), lax.axis_index("dp")
    step = pl.program_id(0) * pl.num_programs(1) + pl.program_id(1)
    final = pl.num_programs(0) * pl.num_programs(1) - 1
    sums = []
    for a in range(n):
        part = pl.ds(skip, sources[a].shape[1] - skip)
        loads = [
            pltpu.make_async_copy(src.at[:, part], dst, load_sem.at[a, i])
            for i, (src, dst) in enumerate(((sources[a], held[a]), (extras[a], more[a])))
        ]
        sums.append(
            PairSum(
                dp, orders[a], loads, held[a], more[a], landing[a], send_sem.at[a], recv_sem.at[a]
            )
        )
    batch_sums = [
        [
            PairSum(
                dp,
                full[i],
                [],
                kv_held[i].at[m],
                None,
                kv_in[i].at[m],
                kv_send.at[i, m],
                kv_recv.at[i, m],
            )
            for i in range(2)
        ]
        for m in range(micro)
    ]
    lines = [
        LineSum(ep, ne, mix_held.at[m], mix_in.at[m], line_send.at[m], line_recv.at[m])
        for m in range(micro)
    ]
    count = q_ref.shape[0]
    line_loads = [
        pltpu.make_async_copy(
            mix_ref.at[:, pl.ds(m * count, count)], mix_held.at[m], mix_sem.at[0, m]
        )
        for m in range(micro)
    ]
    turns = bit_count(nd)

    def batch_step(m, t):
        if t <= turns:
            for each in batch_sums[m]:
                each.step(t)

    def line_step(m, t):
        if t < ne:
            lines[m].step(t)

    @pl.when(step == 0)
    def _():
        for copy in line_loads:
            copy.start()
        for each in sums:
            each.load()
        greet(ep, dp, ne, nd)
        for m in range(micro):
            line_loads[m].wait()
            line_step(m, 0)
        for each in sums:
            each.step(0)
        for i in range(2):
            kv_held[i][...] = jnp.zeros_like(kv_held[i])
        rows = q_ref.shape[0]
        pairs = [dots_ref[:, :, m, :].reshape(-1, rows) for m in range(micro)]
        pair = jnp.concatenate(pairs, axis=1)
        probs = probs_ref[...]
        grad_logits = probs * (pair - jnp.sum(probs * pair, axis=0, keepdims=True))
        high = grad_logits.astype(BF16)
        low = (grad_logits - high.astype(F32)).astype(BF16)
        normed = normed_ref[...]
        router_out[...] = dot(high, normed) + dot(low, normed)
        router = router_ref[...]
        grad_normed = (
            grad_ref[...].astype(F32)
            + dot(high, router, ((0,), (0,)))
            + dot(low, router, ((0,), (0,)))
        )
        residual = residual_ref[...]
        r = rms_scale(residual)
        gain_out[...] = jnp.sum(grad_normed * residual * r, axis=0, keepdims=True)
        scaled = grad_normed * gain_ref[...]
        mean = jnp.mean(scaled * residual, axis=1, keepdims=True)
        grad_residual = cot_ref[...].astype(F32) + r * scaled - residual * (r * r * r) * mean
        res_out[...] = grad_residual
        low_res = grad_residual.astype(BF16)
        tile = 256
        for c in range(0, wo_ref.shape[1], tile):
            y = dot(attn_ref[...], low_res[:, c : c + tile], ((0,), (0,))).astype(BF16)
            a, at = c // wo_out.shape[4], c % wo_out.shape[4]
            share = wo_out.shape[3]
            for e in range(ne):
                for d in range(nd):
                    i = (e * nd + d) * share
                    slot = slot_of(full[a % 2], d)
                    wo_out[a, slot, e, :, at : at + tile] = y[i : i + share]
        for c in range(0, wo_ref.shape[0], tile):
            grads[c // tile] = dot(low_res, wo_ref[c : c + tile, :], ((1,), (1,))).astype(BF16)

    rows = q_ref.shape[0]
    q = spread(q_ref[...].astype(F32) * SCALE).astype(BF16)
    mine = pl.ds(pl.multiple_of(pl.program_id(0) * rows, rows), rows)
    g = spread(grads[pl.program_id(1), mine, :].astype(F32)).astype(BF16)
    k, v = in_window(k_ref, dp, span), in_window(v_ref, dp, span)
    scores = window_scores(dp, span, rows, starts_ref, q, k)
    probs = jnp.exp(scores - log_ref[0, 0])
    grad_probs = dot(g, v, ((1,), (1,)))
    total = jnp.sum(probs * grad_probs, axis=1, keepdims=True)
    grad_scores = (probs * (grad_probs - total)).astype(BF16)
    dq = gathered(dot(grad_scores, k) * SCALE, rows)
    cosine, sine = tables_ref[0], -tables_ref[1]
    for i in range(0, dq.shape[1], 128):
        dq_ref[:, i : i + 128] = turn(dq[:, i : i + 128], cosine, sine).astype(BF16)
    here = pl.ds(window_of(dp, span), span)
    head = pl.program_id(1)
    at = pl.ds(pl.multiple_of(head * 2 * HEAD_DIM, 2 * HEAD_DIM), 2 * HEAD_DIM)
    batch = pl.program_id(0)
    dk = dot(grad_scores, q, ((0,), (0,))).astype(BF16)
    kv_held[0][batch, here, :, at] = dk.reshape(span, rows, dk.shape[1])
    dv = dot(probs.astype(BF16), g, ((0,), (0,))).astype(BF16)
    kv_held[1][batch, here, :, at] = dv.reshape(span, rows, dv.shape[1])

    heads = pl.num_programs(1)
    for m in range(micro):

        @pl.when((batch == m) & (head == heads - 1))
        def _(m=m):
            batch_step(m, 0)

        if m > 0:

            @pl.when((batch == m) & (head == 0))
            def _(m=m):
                batch_step(m - 1, 1)

    @pl.when(step == final // 4 + 1)
    def _():
        line_step(0, 1)

    @pl.when(step == final // 2 + 2)
    def _():
        line_step(1, 1)

    @pl.when(step == final)
    def _():
        copies = []

        def leave(copy):
            copy.start()
            copies.append(copy)

        line_step(0, 2)
        last = micro - 1
        batch_step(last - 1, 2)
        for t in range(1, max([len(order) for order in orders] + [0]) + 1):
            for each in sums:
                each.step(t)
        for a, each in enumerate(sums):
            leave(pltpu.make_async_copy(each.own(), outs[a], out_sem.at[a]))
        batch_step(last, 1)
        line_step(1, 2)
        for t in range(3, turns + 1):
            batch_step(last - 1, t)
        batch_step(last, 2)
        for t in range(3, ne):
            line_step(0, t)
            line_step(1, t)
        for t in range(3, turns + 1):
            batch_step(last, t)
        for m in range(micro):
            own = pl.ds(m * rows, rows)
            for i, out in enumerate((dk_out, dv_out)):
                leave(pltpu.make_async_copy(batch_sums[m][i].own(), out.at[own], kv_out.at[i, m]))
            leave(pltpu.make_async_copy(lines[m].own(), mix_out.at[own], mix_sem.at[1, m]))
        for each in sums + lines + sum(batch_sums, []):
            each.wait_sends()
        for copy in copies:
            copy.wait()


def attend_back(
    starts,
    queries,
    keys,
    values,
    logs_in,
    tables,
    cot,
    dots,
    probs,
    grad_normed,
    residual,
    gain,
    normed,
    attn,
    w_out,
    router,
    mix,
    sums,
    full,
    skip,
    collective,
):
    nd, ne, micro, rows = keys.shape[0], dots.shape[0], dots.shape[2], dots.shape[3]
    every, width = residual.shape
    grid, mine, theirs, column, logs, _ = attention_specs(micro, rows, nd)
    one = pl.Buffered(1)
    whole = lambda v: pl.BlockSpec(v.shape, lambda m, h: (0,) * len(v.shape), pipeline_mode=one)
    n = len(sums)
    shapes = [(v.shape[0], v.shape[1] - skip) + v.shape[2:] for v, _, _ in sums]
    deep = max([s[0] - 1 for s in shapes] + [1])
    some = max(n, 1)
    kv_width = keys.shape[2]
    wo_shape = (width // kv_width, nd, ne, w_out.shape[0] // (ne * nd), kv_width)
    before = [cot, dots, probs, grad_normed, residual, gain, normed, attn, w_out, router]
    after = [
        jax.ShapeDtypeStruct((every, width), F32),
        jax.ShapeDtypeStruct(wo_shape, BF16),
        jax.ShapeDtypeStruct(router.shape, F32),
        jax.ShapeDtypeStruct((1, width), F32),
    ]
    tile = 4 * HEAD_DIM
    return pl.pallas_call(
        functools.partial(
            attend_back_body,
            nd // 2 + 1,
            ne,
            nd,
            micro,
            skip,
            tuple(map(tuple, full)),
            tuple(tuple(order) for _, order, _ in sums),
        ),
        grid=grid,
        in_specs=[column, mine, theirs, theirs, logs, whole(tables)]
        + [whole(v) for v in before]
        + [ANY] * (2 * n + 1),
        out_specs=[mine] + [whole(v) for v in after] + [ANY] * (n + 3),
        out_shape=[jax.ShapeDtypeStruct(queries.shape, BF16)]
        + after
        + [jax.ShapeDtypeStruct((every, keys.shape[2]), BF16)] * 2
        + [jax.ShapeDtypeStruct((every, width), BF16)]
        + [jax.ShapeDtypeStruct(s[1:], BF16) for s in shapes],
        scratch_shapes=[
            pltpu.VMEM((w_out.shape[0] // tile, every, tile), BF16),
            pltpu.VMEM((micro, ne, rows, width), BF16),
            pltpu.VMEM((micro, 2, ne, rows, width), BF16),
        ]
        + [pltpu.VMEM((micro, nd, rows, keys.shape[2]), BF16)] * 2
        + [pltpu.VMEM((micro, nd - 1, rows, keys.shape[2]), BF16)] * 2
        + [pltpu.VMEM(s, BF16) for s in shapes] * 2
        + [pltpu.VMEM((s[0] - 1,) + s[1:], BF16) for s in shapes]
        + [
            DMA((some, 2)),
            DMA((some,)),
            DMA((some, deep)),
            DMA((some, deep)),
            DMA((2, micro, nd - 1)),
            DMA((2, micro, nd - 1)),
            DMA((2, micro)),
            DMA((2, micro)),
            DMA((micro, 2, ne)),
            DMA((micro, 2, ne)),
        ],
        compiler_params=pltpu.CompilerParams(
            vmem_limit_bytes=63 * 2**20, collective_id=collective, has_side_effects=True
        ),
        cost_estimate=cost(40),
    )(
        starts,
        queries,
        keys,
        values,
        logs_in,
        tables,
        *before,
        mix,
        *[v for v, _, _ in sums],
        *[extra for _, _, extra in sums],
    )


def finish_body(ne, nd, orders, n_out, *refs):
    refs = list(refs)

    def take(n):
        return [refs.pop(0) for _ in range(n)]

    n_ref, dq_ref, dk_ref, dv_ref, tables_ref, tokens_ref, gain_ref, router_ref, gain_two = take(9)
    res_ref, wq_ref, wk_ref, wv_ref, wo_ref = take(5)
    (tok_out,) = take(1)
    count = 2 * n_out + 3
    outs, held, pair_in, line_in = take(count), take(count), take(count), take(count)
    dk_turned, wq, wk, wv, res = take(5)
    load_sem, own_sem, out_sem, dp_send, dp_recv, ep_send, ep_recv = refs
    ep, dp = lax.axis_index("ep"), lax.axis_index("dp")
    columns = held[0].shape[3]
    own = [
        pltpu.make_async_copy(src, dst, own_sem.at[i])
        for i, (src, dst) in enumerate(
            ((wq_ref, wq), (wk_ref, wk), (wv_ref, wv), (res_ref, res))
        )
    ]
    sums = []
    for a in range(count):
        loads = []
        if a < n_out:
            loads = [pltpu.make_async_copy(wo_ref.at[a], held[a], load_sem.at[a])]
        sums.append(
            PairSum(
                dp,
                orders[a % 2],
                loads,
                held[a],
                None,
                pair_in[a],
                dp_send.at[a],
                dp_recv.at[a],
                major=True,
            )
        )
    spreads = [
        SpreadSum(ep, ne, sums[a].own(), line_in[a], ep_send.at[a], ep_recv.at[a])
        for a in range(count)
    ]
    early, made, small = sums[:n_out], sums[n_out:-1], sums[-1]
    queries, others = made[:n_out], made[n_out:]
    for each in early:
        each.load()
    for copy in own:
        copy.start()
    greet(ep, dp, ne, nd)
    turns = bit_count(nd)

    def steps(group, t):
        for each in group:
            if t <= turns:
                each.step(t)

    def spread_steps(group, t):
        for each in group:
            spreads[sums.index(each)].step(t)

    steps(early, 0)

    normed = n_ref[...]
    cosine, sine = (repeated(tables_ref[i], normed.shape[1]) for i in range(2))
    sine = -sine
    for i in range(0, dk_ref.shape[1], 128):
        part = dk_ref[:, i : i + 128].astype(F32)
        dk_turned[:, i : i + 128] = turn(part, cosine, sine).astype(BF16)
    tile = 256

    def product(grad, first, each):
        share = each.held.shape[2]
        for c in range(0, each.held.shape[3], tile):
            y = dot(normed, grad[:, first + c : first + c + tile]).astype(BF16)
            for e in range(ne):
                for d in range(nd):
                    r = (e * nd + d) * share
                    each.held[slot_of(each.order, d), e, :, c : c + tile] = y[r : r + share]
        each.step(0)

    for i, each in enumerate(made):
        if i < n_out:
            product(dq_ref, i * columns, each)
        else:
            product((dk_turned, dv_ref)[i - n_out], 0, each)
        if i == 0:
            steps(early, 1)
        if i == 2:
            steps(queries, 1)
    for copy in own:
        copy.wait()
    back = dot(dq_ref[...], wq[...], ((1,), (1,)))
    steps(early, 2)
    steps(others, 1)
    back = back + dot(dk_turned[...], wk[...], ((1,), (1,)))
    back = back + dot(dv_ref[...], wv[...], ((1,), (1,)))
    x = tokens_ref[...].astype(F32)
    r = rms_scale(x)
    scaled = back * gain_ref[...]
    tok_out[...] = (
        res[...] + r * scaled - x * (r * r * r) * jnp.mean(scaled * x, axis=1, keepdims=True)
    )
    for t in range(3, turns + 1):
        steps(early, t)
    spread_steps(early, 0)
    one_row = jnp.sum(back * x * r, axis=0, keepdims=True)
    blank = jnp.zeros((held[-1].shape[3] - EXPERTS - 2, x.shape[1]), F32)
    column = jnp.concatenate([router_ref[...], one_row, gain_two[...], blank], axis=0).T
    share = held[-1].shape[2]
    for e in range(ne):
        for d in range(nd):
            i = (e * nd + d) * share
            held[-1][slot_of(small.order, d), e] = column[i : i + share].astype(BF16)
    steps([small], 0)
    steps(queries, 2)
    steps([small], 1)
    for t in range(3, turns + 1):
        steps(queries, t)
    spread_steps(queries, 0)
    steps(others + [small], 2)
    for t in range(3, turns + 1):
        steps(others + [small], t)
    spread_steps(others + [small], 0)
    spread_steps(early, 1)
    spread_steps(queries, 1)
    spread_steps(others + [small], 1)
    copies = []
    for a in range(count):
        copies.append(pltpu.make_async_copy(spreads[a].own(), outs[a], out_sem.at[a]))
        copies[-1].start()
    for each in sums + spreads:
        each.wait_sends()
    for copy in copies:
        copy.wait()


def finish(
    ne,
    nd,
    orders,
    normed,
    grads,
    tables,
    tokens,
    gain,
    grad_residual,
    weights,
    w_out,
    router_grad,
    gain_two_grad,
):
    rows, width = tokens.shape
    share = width // (ne * nd)
    columns = weights[1].shape[1]
    n_out = width // columns
    count = 2 * n_out + 3
    wide = [columns] * (count - 1) + [128]
    return pl.pallas_call(
        functools.partial(finish_body, ne, nd, tuple(map(tuple, orders)), n_out),
        out_shape=[jax.ShapeDtypeStruct((rows, width), F32)]
        + [jax.ShapeDtypeStruct((share, c), BF16) for c in wide],
        in_specs=[VMEM] * 9 + [ANY] * 5,
        out_specs=[VMEM] + [ANY] * count,
        scratch_shapes=[pltpu.VMEM((nd, ne, share, c), BF16) for c in wide]
        + [pltpu.VMEM((nd - 1, ne, share, c), BF16) for c in wide]
        + [pltpu.VMEM((ne - 1, share, c), BF16) for c in wide]
        + [pltpu.VMEM(grads[1].shape, BF16)]
        + [pltpu.VMEM(w.shape, BF16) for w in weights]
        + [pltpu.VMEM((rows, width), F32)]
        + [
            DMA((count,)),
            DMA((4,)),
            DMA((count,)),
            DMA((count, bit_count(nd))),
            DMA((count, bit_count(nd))),
            DMA((count, ne - 1)),
            DMA((count, ne - 1)),
        ],
        compiler_params=pltpu.CompilerParams(
            vmem_limit_bytes=60 * 2**20, collective_id=4, has_side_effects=True
        ),
        cost_estimate=cost(45),
    )(
        normed,
        *grads,
        tables,
        tokens,
        gain,
        router_grad,
        gain_two_grad,
        grad_residual,
        *weights,
        w_out,
    )


def results_body(share, n_out, groups, *refs):
    refs = list(refs)

    def take(n):
        return [refs.pop(0) for _ in range(n)]

    residual_ref, mix_ref = take(2)
    halves = [take(groups) for _ in range(2)]
    dense = take(2 * n_out + 3)
    out_ref, d_out, d_query, d_key, d_value, router, gain_one, gain_two = take(8)
    gate, up, down = refs
    e = pl.program_id(0)

    @pl.when(e == 0)
    def _():
        out_ref[...] = (residual_ref[...] + mix_ref[...].astype(F32)).astype(BF16)
        width = dense[0].shape[1]
        for i in range(n_out):
            d_out[:, i * width : (i + 1) * width] = dense[i][...].astype(F32)
            d_query[:, i * width : (i + 1) * width] = dense[n_out + i][...].astype(F32)
        d_key[...] = dense[2 * n_out][...].astype(F32)
        d_value[...] = dense[2 * n_out + 1][...].astype(F32)
        small = dense[-1][...].astype(F32)
        router[...] = small[:, :EXPERTS]
        turned = small.T
        gain_one[...] = turned[EXPERTS : EXPERTS + 1]
        gain_two[...] = turned[EXPERTS + 1 : EXPERTS + 2]

    k = 0
    for first, second in zip(*halves):
        for m in range(first.shape[0]):

            @pl.when(e == k)
            def _(first=first, second=second, m=m):
                over = first.shape[1] - share
                gate[0] = first[m, :share].astype(F32)
                up[0, :over] = first[m, share:].astype(F32)
                up[0, over:] = second[m, : share - over].astype(F32)
                piece, columns = down.shape[1], second.shape[2]
                for j in range(down.shape[2] // columns):
                    at = share - over + j * piece
                    down[0, :, j * columns : (j + 1) * columns] = second[
                        m, at : at + piece
                    ].astype(F32)

            k += 1


def results(residual, mix, grads, dense, n_out, share, w_gate, w_down, nd, rows_share):
    rows, width = residual.shape
    n_exp, _, inner = w_gate.shape
    piece = w_down.shape[1] // nd
    ins = [residual, *mix, *grads[0], *grads[1], *dense]
    kv = dense[-2].shape[1]
    same = lambda v: pl.BlockSpec(v, lambda e: (0,) * len(v))
    outs = [
        ((rows, width), BF16),
        ((rows_share, width), F32),
        ((rows_share, width), F32),
        ((rows_share, kv), F32),
        ((rows_share, kv), F32),
        ((rows_share, EXPERTS), F32),
        ((1, rows_share), F32),
        ((1, rows_share), F32),
    ]
    experts_out = [((n_exp, share, inner), F32)] * 2 + [((n_exp, piece, width), F32)]
    return pl.pallas_call(
        functools.partial(results_body, share, n_out, len(grads[0])),
        grid=(n_exp,),
        out_shape=[jax.ShapeDtypeStruct(*v) for v in outs + experts_out],
        in_specs=[same(v.shape) for v in ins],
        out_specs=[same(v[0]) for v in outs]
        + [pl.BlockSpec((1,) + v[0][1:], lambda e: (e, 0, 0)) for v in experts_out],
        compiler_params=pltpu.CompilerParams(vmem_limit_bytes=60 * 2**20),
        cost_estimate=cost(6),
    )(*ins)


def per_device(
    tokens,
    segments,
    routes,
    first_gain,
    w_query,
    w_key,
    w_value,
    w_out,
    second_gain,
    w_router,
    w_gate,
    w_up,
    w_down,
    cotangent,
):
    micro, rows, width = tokens.shape
    ne, nd = lax.axis_size("ep"), lax.axis_size("dp")
    kv_width = KV_HEADS * HEAD_DIM
    every = micro * rows

    halfway = HEAD_DIM // 2
    frequency = ROPE_BASE ** (-(np.arange(halfway) * 2.0 / HEAD_DIM))
    angles = np.arange(nd * rows)[:, None] * frequency[None, :]
    lanes = 2 * HEAD_DIM // halfway
    sign = np.where(np.arange(2 * HEAD_DIM) % HEAD_DIM < halfway, -1.0, 1.0)
    tables = np.stack([np.tile(np.cos(angles), lanes), np.tile(np.sin(angles), lanes) * sign])
    tokens_flat = tokens.reshape(every, width)
    gain_one = first_gain.reshape(1, width)
    cot_own = cotangent.reshape(every, width)
    late = rows // 2
    normed_one, query_rot, tables, starts, key_all, value_all, cot_first = project(
        tokens_flat,
        gain_one,
        segments.reshape(micro, rows),
        jnp.asarray(tables, F32),
        w_query,
        w_key,
        w_value,
        cot_own[None],
        every - late,
        ne,
        nd,
        0,
    )
    routing = routes.reshape(every, routes.shape[2])
    hit = jnp.any(
        jnp.arange(EXPERTS, dtype=jnp.int32)[:, None, None] == routing[None], axis=2
    ).astype(F32)
    router = w_router.T
    attn_low, logs, residual, normed_two, gate_probs, normed_all, marked_all, cot_last = attend(
        starts,
        query_rot,
        key_all,
        value_all,
        tokens_flat,
        w_out,
        second_gain.reshape(1, width),
        router,
        hit,
        cot_own[None],
        late,
        micro,
        rows,
        ne,
        1,
    )
    orders = [order[:-1][::-1] for order in gather_orders(nd)]
    mix, grad_in, pair_dots, *grads = experts(
        normed_all.reshape(ne * every, width),
        [cot.reshape(ne, -1, width) for cot in (cot_first, cot_last)],
        marked_all.reshape(ne * micro, EXPERTS, rows),
        w_gate,
        w_up,
        w_down,
        micro,
        rows,
        ne,
        nd,
        6,
    )
    kept, landed, last = grads[:2], grads[2:4], grads[4:]
    height = kept[0].shape[2]
    halves = [(slice(None), slice(i * height, (i + 1) * height)) for i in range(2)]
    skip = min(2, kept[0].shape[1])
    more = kept[0].shape[1] > skip
    head = (slice(None), slice(0, skip))
    *grads, grad_back, dots_all = reduce(
        ne,
        nd,
        [(last[k], orders[i], halves[i], None, False) for k in range(2) for i in range(2)]
        + [(kept[i], orders[i][1:], head, landed[i], False) for i in range(2)],
        ((grad_in.reshape(ne, every, width), None),),
        (pair_dots,),
        2,
        40,
    )
    grads_last, grads_head = grads[:4], grads[4:]
    mix = mix.reshape(ne, every, width)
    full = [[0] + order for order in orders]
    (
        grad_query,
        grad_residual,
        grad_w_out,
        grad_router,
        grad_gain_two,
        grad_key,
        grad_value,
        mix_own,
        *grads_more,
    ) = attend_back(
        starts,
        query_rot,
        key_all,
        value_all,
        logs,
        tables,
        cot_own,
        dots_all,
        gate_probs,
        grad_back,
        residual,
        second_gain.reshape(1, width),
        normed_two,
        attn_low,
        w_out,
        router,
        mix,
        [(kept[i], orders[i][1:], landed[i]) for i in range(2)] if more else [],
        full,
        skip,
        5,
    )
    grad_tokens, *dense = finish(
        ne,
        nd,
        full,
        normed_one,
        (grad_query, grad_key, grad_value),
        tables,
        tokens_flat,
        gain_one,
        grad_residual,
        (w_query, w_key, w_value),
        grad_w_out,
        grad_router,
        grad_gain_two,
    )
    (
        output,
        d_out,
        d_query,
        d_key,
        d_value,
        d_router,
        d_gain_one,
        d_gain_two,
        d_gate,
        d_up,
        d_down,
    ) = results(
        residual,
        (mix_own,),
        [
            [grads_head[i]]
            + ([grads_more[i]] if more else [])
            + [grads_last[i][None], grads_last[2 + i][None]]
            for i in range(2)
        ],
        dense,
        width // kv_width,
        width // nd,
        w_gate,
        w_down,
        nd,
        width // (ne * nd),
    )
    return (
        output.reshape(tokens.shape),
        grad_tokens.reshape(tokens.shape),
        d_gain_one.reshape(-1),
        d_query,
        d_key,
        d_value,
        d_out,
        d_gain_two.reshape(-1),
        d_router,
        d_gate,
        d_up,
        d_down,
    )


def solution(mesh):
    in_specs = (
        P(None, ("ep", "dp"), None),
        P(None, "ep", "dp"),
        P(None, ("ep", "dp"), None),
        P(),
        P(),
        P(),
        P(),
        P(),
        P(),
        P(),
        P("ep", None, None),
        P("ep", None, None),
        P("ep", None, None),
        P(None, ("ep", "dp"), None),
    )
    out_specs = (
        P(None, ("ep", "dp"), None),
        P(None, ("ep", "dp"), None),
        P(("ep", "dp")),
        P(("ep", "dp"), None),
        P(("ep", "dp"), None),
        P(("ep", "dp"), None),
        P(("ep", "dp"), None),
        P(("ep", "dp")),
        P(("ep", "dp"), None),
        P("ep", "dp", None),
        P("ep", "dp", None),
        P("ep", "dp", None),
    )
    return jax.shard_map(
        per_device, mesh=mesh, in_specs=in_specs, out_specs=out_specs, check_vma=False
    )
```

```python
import functools

import jax
import jax.numpy as jnp
import numpy as np
from jax import lax
from jax.experimental import pallas as pl
from jax.experimental.pallas import tpu as pltpu
from jax.sharding import PartitionSpec as P

HEADS = 16
KV_HEADS = 8
HEAD_DIM = 64
EXPERTS = 32
CAP = 64
SEGMENT_IDS = 4
EPSILON = 1e-06
ROPE_BASE = 10000.0
MASKED = -1e30
HIGHEST = lax.Precision.HIGHEST
MESH = pl.DeviceIdType.MESH
BF16 = jnp.bfloat16
F32 = jnp.float32
VMEM = pl.BlockSpec(memory_space=pltpu.VMEM)
ANY = pl.BlockSpec(memory_space=pl.ANY)
DMA = pltpu.SemaphoreType.DMA


def bit_count(n):
    return n.bit_length() - 1


def masks(bits):
    out = [0]
    for b in bits:
        out = out + [m | (1 << b) for m in out]
    return out


def gather_orders(n):
    bits = list(range(bit_count(n)))
    return (bits[1:] + bits[:1], bits[:0:-1] + bits[:1])


def greet(ep, dp, ne, nd):
    barrier = pltpu.get_barrier_semaphore()
    for k in range(1, ne):
        pl.semaphore_signal(
            barrier, inc=1, device_id={"ep": lax.rem(ep + k, ne)}, device_id_type=MESH
        )
    for b in range(bit_count(nd)):
        pl.semaphore_signal(
            barrier, inc=1, device_id={"dp": jnp.bitwise_xor(dp, 1 << b)}, device_id_type=MESH
        )
    pl.semaphore_wait(barrier, ne - 1 + bit_count(nd))


def remote(src, dst, send, recv, where):
    return pltpu.make_async_remote_copy(
        src_ref=src, dst_ref=dst, send_sem=send, recv_sem=recv, device_id=where, device_id_type=MESH
    )


class PairGather:
    def __init__(self, dp, nd, order, own, whole, send_sem, recv_sem):
        self.dp, self.order, self.own, self.whole = dp, order, own, whole
        self.send_sem, self.recv_sem = send_sem, recv_sem

    def copy(self, t, m):
        block = jnp.bitwise_xor(self.dp, m)
        k = (1 << t) - 1 + masks(self.order[:t]).index(m)
        return remote(
            self.own if m == 0 else self.whole.at[block],
            self.whole.at[block],
            self.send_sem.at[k],
            self.recv_sem.at[k],
            {"dp": jnp.bitwise_xor(self.dp, 1 << self.order[t])},
        )

    def start(self):
        for t in range(len(self.order)):
            self.copy(t, 0).start()

    def step(self, t, first=0, last=None):
        for m in masks(self.order[:t])[first:last]:
            self.copy(t, m).wait_recv()
            for later in range(t + 1, len(self.order)):
                self.copy(later, m | (1 << self.order[t])).start()

    def wait_sends(self):
        for t in range(len(self.order)):
            for m in masks(self.order[:t]):
                self.copy(t, m).wait_send()


def cost(us):
    return pl.CostEstimate(flops=0, bytes_accessed=int(us * 3.0e6), transcendentals=0)


def add_into(ref, arrived):
    if len(ref.shape) > 2:

        @pl.loop(0, ref.shape[0])
        def _(i):
            add_into(ref.at[i], arrived.at[i])

    else:
        ref[...] = (ref[...].astype(F32) + arrived[...].astype(F32)).astype(ref.dtype)


class PairSum:
    def __init__(self, dp, order, loads, held, extra, landing, send_sem, recv_sem, major=False):
        self.dp, self.order, self.held, self.landing = dp, order, held, landing
        self.send_sem, self.recv_sem = send_sem, recv_sem
        self.extra, self.loads, self.major = extra, loads, major
        self.index = 0
        for b in order:
            side = jnp.bitwise_and(lax.shift_right_logical(dp, b), 1)
            self.index = self.index + (side << self.place(b))

    def place(self, bit):
        if self.major:
            return len(self.order) - 1 - self.order.index(bit)
        return sorted(self.order).index(bit)

    def copies(self, t):
        order = self.order
        if self.major:
            count = 1 << (len(order) - 1 - t)
            first = sum(1 << (len(order) - 1 - i) for i in range(t))
            mine = self.index - lax.rem(self.index, count)
            copy = remote(
                self.held.at[pl.ds(jnp.bitwise_xor(mine, count), count)],
                self.landing.at[pl.ds(first, count)],
                self.send_sem.at[t],
                self.recv_sem.at[t],
                {"dp": jnp.bitwise_xor(self.dp, 1 << order[t])},
            )
            return [(pl.ds(mine, count), pl.ds(first, count), copy)]
        partner = jnp.bitwise_xor(self.index, 1 << self.place(order[t]))
        first = sum(1 << (len(order) - 1 - i) for i in range(t))
        return [
            (
                m,
                first + j,
                remote(
                    self.held.at[jnp.bitwise_xor(partner, m)],
                    self.landing.at[first + j],
                    self.send_sem.at[first + j],
                    self.recv_sem.at[first + j],
                    {"dp": jnp.bitwise_xor(self.dp, 1 << order[t])},
                ),
            )
            for j, m in enumerate(masks([self.place(b) for b in order[t + 1 :]]))
        ]

    def load(self):
        for copy in self.loads:
            copy.start()

    def step(self, t):
        if t == 0:
            for copy in self.loads:
                copy.wait()
            if self.extra is not None:
                add_into(self.held, self.extra)
        elif t <= len(self.order):
            for m, k, copy in self.copies(t - 1):
                copy.wait_recv()
                mine = m if self.major else jnp.bitwise_xor(self.index, m)
                add_into(self.held.at[mine], self.landing.at[k])
        if t < len(self.order):
            for m, k, copy in self.copies(t):
                copy.start()

    def own(self):
        return self.held.at[self.index]

    def wait_sends(self):
        for t in range(len(self.order)):
            for m, k, copy in self.copies(t):
                copy.wait_send()


def slot_of(order, d):
    return sum(((d >> b) & 1) << (len(order) - 1 - i) for i, b in enumerate(order))


class LineSum:
    def __init__(self, ep, ne, blocks, landing, send_sem, recv_sem):
        self.ep, self.ne, self.blocks, self.landing = ep, ne, blocks, landing
        self.send_sem, self.recv_sem = send_sem, recv_sem

    def copy(self, dest, way):
        k = 0 if way == 1 else 1
        return remote(
            self.blocks.at[dest],
            self.landing.at[k, dest],
            self.send_sem.at[k, dest],
            self.recv_sem.at[k, dest],
            {"ep": lax.rem(self.ep + way + self.ne, self.ne)},
        )

    def turn(self, t, way):
        ep, ne = self.ep, self.ne
        dest = ep + ne - 1 - t if way == 1 else ep + t - (ne - 1)
        has = dest <= ne - 1 if way == 1 else dest >= 0
        inner = ep >= 1 if way == 1 else ep <= ne - 2
        return dest, has, inner

    def step(self, t):
        for way in (1, -1):
            dest, has, inner = self.turn(t, way)

            @pl.when(has & inner)
            def _(way=way, dest=dest):
                self.copy(dest, way).wait_recv()
                add_into(self.blocks.at[dest], self.landing.at[0 if way == 1 else 1, dest])

            if t < self.ne - 1:

                @pl.when(has)
                def _(way=way, dest=dest):
                    self.copy(dest, way).start()

    def own(self):
        return self.blocks.at[self.ep]

    def wait_sends(self):
        for t in range(self.ne - 1):
            for way in (1, -1):
                dest, has, inner = self.turn(t, way)

                @pl.when(has)
                def _(way=way, dest=dest):
                    self.copy(dest, way).wait_send()


class SpreadSum:
    def __init__(self, ep, ne, blocks, landing, send_sem, recv_sem):
        self.ep, self.blocks, self.landing = ep, blocks, landing
        self.copies = []
        for k in range(1, ne):
            to = lax.rem(ep + k, ne)
            self.copies.append(
                remote(
                    blocks.at[to],
                    landing.at[k - 1],
                    send_sem.at[k - 1],
                    recv_sem.at[k - 1],
                    {"ep": to},
                )
            )

    def step(self, t):
        if t == 0:
            for copy in self.copies:
                copy.start()
        elif t == 1:
            total = self.blocks[self.ep].astype(F32)
            for k, copy in enumerate(self.copies):
                copy.wait_recv()
                total = total + self.landing[k].astype(F32)
            self.blocks[self.ep] = total.astype(BF16)

    def own(self):
        return self.blocks.at[self.ep]

    def wait_sends(self):
        for copy in self.copies:
            copy.wait_send()


def shape_at(array, where):
    return tuple(len(range(*w.indices(n))) for w, n in zip(where, array.shape)) + array.shape[len(where) :]


def reduce_body(ne, nd, pairs, line_parts, n_swap, *refs):
    refs = list(refs)

    def take(n):
        return [refs.pop(0) for _ in range(n)]

    n_pair, n_line = len(pairs), len(line_parts)
    n_extra = sum(p[2] for p in pairs)
    n_both = sum(p[3] for p in pairs)
    n_sum = n_pair + n_line
    ins, extra_ins, swap_ins = take(n_sum), take(n_extra), take(n_swap)
    outs, swap_outs = take(n_sum), take(n_swap)
    held, extras, pair_in = take(n_sum), take(n_extra), take(n_pair)
    both_in, line_in = take(n_both), take(n_line)
    load_sem, out_sem, dp_send, dp_recv, ep_send, ep_recv, swap_send, swap_recv = refs
    ep, dp = lax.axis_index("ep"), lax.axis_index("dp")
    sums, then = [], []
    for a, (order, where, has_extra, both) in enumerate(pairs):
        targets = [(ins[a], held[a])]
        extra = extras.pop(0) if has_extra else None
        if has_extra:
            targets.append((extra_ins.pop(0), extra))
        loads = [
            pltpu.make_async_copy(src.at[where] if where else src, dst, load_sem.at[a, i])
            for i, (src, dst) in enumerate(targets)
        ]
        sums.append(
            PairSum(dp, order, loads, held[a], extra, pair_in[a], dp_send.at[a], dp_recv.at[a])
        )
        if both:
            i = len(then)
            then.append(
                LineSum(ep, ne, sums[a].own(), both_in[i], ep_send.at[i], ep_recv.at[i])
            )
    lines, line_loads = [], []
    for i in range(n_line):
        a = n_pair + i
        src = ins[a].at[line_parts[i]] if line_parts[i] else ins[a]
        line_loads.append(pltpu.make_async_copy(src, held[a], load_sem.at[a, 0]))
        lines.append(
            LineSum(
                ep, ne, held[a], line_in[i], ep_send.at[n_both + i], ep_recv.at[n_both + i]
            )
        )
    for copy in line_loads:
        copy.start()
    for each in sums:
        each.load()
    greet(ep, dp, ne, nd)
    swaps = []
    for a in range(n_swap):
        src, dst = swap_ins[a], swap_outs[a]
        own = pltpu.make_async_copy(src.at[ep], dst.at[ep], load_sem.at[n_sum + a, 0])
        own.start()
        swaps.append(own)
        for k in range(1, ne):
            to = lax.rem(ep + k, ne)
            copy = remote(
                src.at[to], dst.at[ep], swap_send.at[a, k - 1], swap_recv.at[a, k - 1], {"ep": to}
            )
            copy.start()
            swaps.append(copy)
    for copy in line_loads:
        copy.wait()
    steps = max([len(p[0]) + 1 for p in pairs] + [ne if n_line else 0])
    for t in range(steps):
        if t < ne:
            for each in lines:
                each.step(t)
        for each in sums:
            each.step(t)
    for t in range(ne):
        for each in then:
            each.step(t)
    results, after = [], iter(then)
    for a in range(n_sum):
        if a >= n_pair:
            src = lines[a - n_pair].own()
        else:
            src = next(after).own() if pairs[a][3] else sums[a].own()
        copy = pltpu.make_async_copy(src, outs[a], out_sem.at[a])
        copy.start()
        results.append(copy)
    for each in sums + then + lines:
        each.wait_sends()
    for copy in swaps + results:
        copy.wait()


def reduce(ne, nd, pairs, lines, swaps, collective, us):
    line_parts = tuple(where for _, where in lines)
    line_shapes = [shape_at(v, where) if where else v.shape for v, where in lines]
    lines = [v for v, _ in lines]
    arrays = [p[0] for p in pairs] + list(lines)
    extras = [p[3] for p in pairs if p[3] is not None]
    kinds = tuple((tuple(p[1]), p[2], p[3] is not None, p[4]) for p in pairs)
    shapes = [shape_at(p[0], p[2]) if p[2] else p[0].shape for p in pairs]
    boths = [s for s, p in zip(shapes, pairs) if p[4]]
    results = [s[2:] if p[4] else s[1:] for s, p in zip(shapes, pairs)]
    results += [s[1:] for s in line_shapes]
    scratch = shapes + line_shapes
    scratch += [s for s, p in zip(shapes, pairs) if p[3] is not None]
    scratch += [(s[0] - 1,) + s[1:] for s in shapes]
    scratch += [(2,) + s[1:] for s in boths] + [(2,) + s for s in line_shapes]
    some = lambda n: max(n, 1)
    line_count = some(len(lines) + len(boths))
    deep = max([s[0] - 1 for s in shapes] + [1])
    return pl.pallas_call(
        functools.partial(reduce_body, ne, nd, kinds, line_parts, len(swaps)),
        out_shape=[jax.ShapeDtypeStruct(s, BF16) for s in results]
        + [jax.ShapeDtypeStruct(v.shape, v.dtype) for v in swaps],
        in_specs=[ANY] * (len(arrays) + len(extras) + len(swaps)),
        out_specs=[ANY] * (len(arrays) + len(swaps)),
        scratch_shapes=[pltpu.VMEM(s, BF16) for s in scratch]
        + [
            DMA((len(arrays) + len(swaps), 2)),
            DMA((len(arrays),)),
            DMA((some(len(pairs)), deep)),
            DMA((some(len(pairs)), deep)),
            DMA((line_count, 2, ne)),
            DMA((line_count, 2, ne)),
            DMA((some(len(swaps)), ne - 1)),
            DMA((some(len(swaps)), ne - 1)),
        ],
        compiler_params=pltpu.CompilerParams(
            collective_id=collective, has_side_effects=True, vmem_limit_bytes=60 * 2**20
        ),
        cost_estimate=cost(us),
    )(*arrays, *extras, *swaps)


def dot(a, b, dims=((1,), (0,))):
    return lax.dot_general(a, b, (dims, ((), ())), preferred_element_type=F32)


def expert_body(ne, nd, micro, rows, *refs):
    cots, refs = refs[:2], refs[2:]
    normed_ref, probs_ref, gate_ref, up_ref, down_ref = refs[:5]
    mix_ref, grad_ref, dots_ref = refs[5:8]
    kept, landed, whole = refs[8:10], refs[10:12], refs[12:14]
    rows_in, cots_in, picks, first, second, chances, sides, arrived, leaving = refs[14:23]
    load_sem, store_sem, send_sem, recv_sem, free_sem, far_send, far_recv = refs[23:]
    e = pl.program_id(0)
    last = pl.num_programs(0) - 1
    ep, dp = lax.axis_index("ep"), lax.axis_index("dp")
    other = {"dp": jnp.bitwise_xor(dp, 1)}
    every = micro * rows
    blocks = ne * micro
    width = first.shape[1]
    n_exp = rows_in.shape[1]

    core = jnp.bitwise_and(dp, 1)
    keep, send = sides.at[core], sides.at[1 - core]

    def exchange():
        return remote(send, arrived, send_sem, recv_sem, other)

    def loads():
        out = [
            pltpu.make_async_copy(normed_ref, first, load_sem.at[ne]),
            pltpu.make_async_copy(
                probs_ref.at[:, pl.ds(pl.multiple_of(ep * n_exp, n_exp), n_exp)],
                chances,
                load_sem.at[ne + 1],
            ),
        ]
        for k in range(ne):
            at = k * every
            for i, part in enumerate(cots):
                out.append(
                    pltpu.make_async_copy(
                        part.at[k],
                        second.at[pl.ds(at, part.shape[1])],
                        load_sem.at[k if i == 0 else ne + 2 + k],
                    )
                )
                at += part.shape[1]
        return out

    def block_at(s):
        return pl.ds(pl.multiple_of(s * rows, rows), rows)

    def returned(t):
        k, m = t // micro, lax.rem(t, micro)
        return lax.rem(ep + k, ne) * micro + m

    def stores(t):
        s = returned(t)
        return (
            pltpu.make_async_copy(
                first.at[block_at(s)], mix_ref.at[block_at(s)], store_sem.at[0, t]
            ),
            pltpu.make_async_copy(
                second.at[block_at(s)], grad_ref.at[block_at(s)], store_sem.at[1, t]
            ),
        )

    def far(i, n):
        return remote(
            leaving.at[i, lax.rem(n, leaving.shape[1])],
            landed[i].at[:, n],
            far_send.at[i, lax.rem(n, leaving.shape[1])],
            far_recv.at[i, n],
            {"dp": jnp.bitwise_xor(dp, 1 << first_bits(nd)[i])},
        )

    def last_copy(k):
        return pltpu.make_async_copy(keep, whole[k], load_sem.at[k])

    def collect():
        exchange().wait_recv()
        pieces, height, slots = sides.shape[1], leaving.shape[3], leaving.shape[1]
        n = e - 1
        early = n_exp - 2

        @pl.when(n < early)
        def _():
            @pl.when(n >= slots)
            def _():
                for i in range(2):
                    far(i, n - slots).wait_send()

            def piece(i, at, other_side):
                bit = first_bits(nd)[i]
                mine = jnp.bitwise_and(lax.shift_right_logical(dp, bit), 1)
                side = 1 - mine if other_side else mine
                low = (1 << (bit - 1)) - 1
                j = ((at & ~low) << 1 | (at & low)) + (side << (bit - 1))
                part = slice(i * height, (i + 1) * height)
                return (keep[j, part].astype(F32) + arrived[j, part].astype(F32)).astype(BF16)

            for i in range(2):
                for at in range(pieces // 2):
                    leaving[i, lax.rem(n, slots), at] = piece(i, at, True)
                far(i, n).start()
            for i in range(2):
                for at in range(pieces // 2):
                    kept[i][at, 0] = piece(i, at, False)

        for k in range(2):

            @pl.when(n == early + k)
            def _(k=k):
                add_into(keep, arrived)
                last_copy(k).start()

    @pl.when(e == 0)
    def _():
        for copy in loads():
            copy.start()
        barrier = pltpu.get_barrier_semaphore()
        met = [0] + sorted(set(first_bits(nd)))
        for bit in met:
            pl.semaphore_signal(
                barrier,
                inc=1,
                device_id={"dp": jnp.bitwise_xor(dp, 1 << bit)},
                device_id_type=MESH,
            )
        pl.semaphore_wait(barrier, len(met))
        before = lax.broadcasted_iota(jnp.int32, (rows, rows), 0)
        after = lax.broadcasted_iota(jnp.int32, (rows, rows), 1)
        earlier = (before < after).astype(BF16)
        slot = lax.broadcasted_iota(jnp.int32, (n_exp, CAP, rows), 1)
        for copy in loads():
            copy.wait()

        @pl.loop(0, blocks)
        def _(s):
            at = block_at(s)
            probs = chances[s]
            hit = probs >= 0.0
            rank = dot(hit.astype(BF16), earlier)
            rank = jnp.where(hit, rank, -1.0).astype(jnp.int32)
            pick = jnp.broadcast_to(rank[:, None, :], (n_exp, CAP, rows)) == slot
            pick_f = pick.astype(F32)
            flat = pick_f.reshape(n_exp * CAP, rows).astype(BF16)
            picks[s] = flat
            rows_in[s] = dot(flat, first[at, :]).astype(BF16).reshape(n_exp, CAP, width)
            cots_in[s] = dot(flat, second[at, :]).astype(BF16).reshape(n_exp, CAP, width)

    @pl.when(e < last)
    def _():
        x = rows_in[:, e].reshape(blocks * CAP, width)
        c = cots_in[:, e].reshape(blocks * CAP, width)
        flat = picks[:, pl.ds(pl.multiple_of(e * CAP, CAP), CAP), :].astype(F32)
        p = jnp.sum(flat * chances[:, pl.ds(e, 1), :], axis=2, keepdims=True)
        p = p.reshape(blocks * CAP, 1)
        w_gate, w_up, w_down = gate_ref[0], up_ref[0], down_ref[0]
        gate_pre = dot(x, w_gate)
        up_pre = dot(x, w_up)
        back = dot(c, w_down, ((1,), (1,)))

        @pl.when(e > 0)
        def _():
            collect()
            pl.semaphore_signal(free_sem, inc=1, device_id=other, device_id_type=MESH)

        sigma = jax.nn.sigmoid(gate_pre)
        silu = gate_pre * sigma
        hidden = (silu * up_pre).astype(BF16)
        out = dot(hidden, w_down) * p
        wide = hidden.astype(F32)
        pair = jnp.sum(wide * back, axis=1, keepdims=True)
        back = back * p
        grad_up = (back * silu).astype(BF16)
        grad_gate = (back * up_pre * (sigma * (1.0 + gate_pre * (1.0 - sigma)))).astype(BF16)
        scaled = (wide * p).astype(BF16)
        pair = jnp.sum(flat * pair.reshape(blocks, CAP, 1), axis=1)
        dots_ref[:, 0] = pair.reshape(ne, micro, rows)

        @pl.when(e > 0)
        def _():
            exchange().wait_send()
            pl.semaphore_wait(free_sem, 1)

        @pl.when(e == n_exp - 1)
        def _():
            last_copy(0).wait()

        def split(value, offset):
            value = value.astype(BF16)
            piece, columns = value.shape[0] // nd, sides.shape[3]

            for i in range(nd):
                for j in range(value.shape[1] // columns):
                    at = offset + j * piece
                    sides[i % 2, i // 2, at : at + piece] = value[
                        i * piece : (i + 1) * piece, j * columns : (j + 1) * columns
                    ]

        share = width // nd
        split(dot(scaled, c, ((0,), (0,))), 2 * share)
        split(dot(x, grad_gate, ((0,), (0,))), 0)
        split(dot(x, grad_up, ((0,), (0,))), share)
        exchange().start()

        grad_x = dot(grad_gate, w_gate, ((1,), (1,))) + dot(grad_up, w_up, ((1,), (1,)))
        rows_in[:, e] = grad_x.astype(BF16).reshape(blocks, CAP, width)
        cots_in[:, e] = out.astype(BF16).reshape(blocks, CAP, width)

    @pl.when(e == last)
    def _():
        @pl.loop(0, blocks)
        def _(t):
            s = returned(t)
            at = block_at(s)
            flat = picks[s]
            for done, slots in ((first, cots_in), (second, rows_in)):
                value = dot(flat, slots[s].reshape(n_exp * CAP, width), ((0,), (0,)))
                done[at, :] = value.astype(BF16)
            for copy in stores(t):
                copy.start()

            @pl.when(t == 1)
            def _():
                collect()
                exchange().wait_send()

        @pl.loop(0, blocks)
        def _(t):
            for copy in stores(t):
                copy.wait()

        last_copy(1).wait()
        early, slots = n_exp - 2, leaving.shape[1]
        for i in range(2):
            for n in range(max(early - slots, 0), early):
                far(i, n).wait_send()

            @pl.loop(0, early)
            def _(n, i=i):
                far(i, n).wait_recv()


def first_bits(nd):
    return [order[-2] for order in gather_orders(nd)]


def experts(normed, cots, probs, w_gate, w_up, w_down, micro, rows, ne, nd, collective):
    n_exp, width, inner = w_gate.shape
    blocks = ne * micro
    half = nd // 2
    packed = 2 * width // nd + (inner // nd) * (width // inner)
    full = (blocks * rows, width)
    weight = lambda e: (jnp.minimum(e, n_exp - 1), 0, 0)
    early = n_exp - 2
    part = (half // 2, early, packed // 2, inner)
    kept = pl.BlockSpec(
        (half // 2, 1, packed // 2, inner), lambda e: (0, jnp.clip(e - 1, 0, early - 1), 0, 0)
    )
    last = (half, packed, inner)
    return pl.pallas_call(
        functools.partial(expert_body, ne, nd, micro, rows),
        grid=(n_exp + 1,),
        in_specs=[ANY] * 4
        + [
            pl.BlockSpec((1, width, inner), weight),
            pl.BlockSpec((1, width, inner), weight),
            pl.BlockSpec((1, inner, width), weight),
        ],
        out_specs=[
            ANY,
            ANY,
            pl.BlockSpec((ne, 1, micro, rows), lambda e: (0, jnp.minimum(e, n_exp - 1), 0, 0)),
            kept,
            kept,
            ANY,
            ANY,
            ANY,
            ANY,
        ],
        scratch_shapes=[
            pltpu.VMEM((blocks, n_exp, CAP, width), BF16),
            pltpu.VMEM((blocks, n_exp, CAP, width), BF16),
            pltpu.VMEM((blocks, n_exp * CAP, rows), BF16),
            pltpu.VMEM(full, BF16),
            pltpu.VMEM(full, BF16),
            pltpu.VMEM((blocks, n_exp, rows), F32),
            pltpu.VMEM((2, half, packed, inner), BF16),
            pltpu.VMEM((half, packed, inner), BF16),
            pltpu.VMEM((2, 2 if early > 2 else 1, half // 2, packed // 2, inner), BF16),
            DMA((2 * ne + 2,)),
            DMA((2, blocks)),
            DMA,
            DMA,
            pltpu.SemaphoreType.REGULAR,
            DMA((2, 2)),
            DMA((2, early)),
        ],
        out_shape=[
            jax.ShapeDtypeStruct(full, BF16),
            jax.ShapeDtypeStruct(full, BF16),
            jax.ShapeDtypeStruct((ne, n_exp, micro, rows), F32),
        ]
        + [jax.ShapeDtypeStruct(part, BF16)] * 4
        + [jax.ShapeDtypeStruct(last, BF16)] * 2,
        compiler_params=pltpu.CompilerParams(
            vmem_limit_bytes=63 * 2**20,
            dimension_semantics=("arbitrary",),
            collective_id=collective,
            has_side_effects=True,
        ),
        cost_estimate=cost(75),
    )(*cots, normed, probs, w_gate, w_up, w_down)


def rms_scale(values):
    return lax.rsqrt(jnp.mean(values * values, axis=-1, keepdims=True) + EPSILON)


def partner(x):
    lane = lax.broadcasted_iota(jnp.int32, x.shape, 1)
    half = HEAD_DIM // 2
    low = lax.rem(lane, HEAD_DIM) < half
    return jnp.where(low, pltpu.roll(x, x.shape[1] - half, 1), pltpu.roll(x, half, 1))


def turn(x, cosine, sine):
    return x * cosine + partner(x) * sine


def repeated(table, rows):
    return jnp.concatenate([table] * (rows // table.shape[0]), axis=0)


def project_body(ne, nd, *refs):
    tokens_ref, gain_ref, segments_ref, tables_all, wq_ref, wk_ref, wv_ref, cot_ref = refs[:8]
    n_ref, q_ref, tables_ref, starts_ref, key_all, value_all, cot_all = refs[8:15]
    wq, wk, wv, key_own, value_own, count_own, count_all = refs[15:22]
    sem, own_sem, send_sem, recv_sem, line_send, line_recv = refs[22:]
    ep, dp = lax.axis_index("ep"), lax.axis_index("dp")
    micro, rows = segments_ref.shape
    loads = [
        pltpu.make_async_copy(src, dst, sem.at[i])
        for i, (src, dst) in enumerate(
            (
                (tables_all.at[:, pl.ds(pl.multiple_of(dp * rows, rows), rows)], tables_ref),
                (wk_ref, wk),
                (wv_ref, wv),
                (wq_ref, wq),
            )
        )
    ]
    for copy in loads:
        copy.start()
    arrays = ((count_own, count_all), (key_own, key_all), (value_own, value_all))
    gathers = [
        PairGather(
            dp, nd, gather_orders(nd)[i // 2], own, whole, send_sem.at[i], recv_sem.at[i]
        )
        for i, (own, whole) in enumerate(arrays)
    ]
    own_copies = [
        pltpu.make_async_copy(own, whole.at[dp], own_sem.at[i])
        for i, (own, whole) in enumerate(arrays)
    ]

    cot_own = cot_ref.at[:, pl.ds(0, cot_all.shape[2])]
    line = LineGather(ep, ne, cot_own, cot_all, line_send, line_recv)
    own_copies.append(pltpu.make_async_copy(cot_own.at[0], cot_all.at[ep, 0], own_sem.at[3]))

    def leave(i):
        gathers[i].start()
        own_copies[i].start()

    segments = segments_ref[...]
    lane = lax.broadcasted_iota(jnp.int32, (micro, count_own.shape[1]), 1)
    counts = jnp.zeros(lane.shape, F32)
    for i in range(SEGMENT_IDS):
        held = jnp.sum((segments == i).astype(F32), axis=1, keepdims=True)
        counts = counts + jnp.where(lane == i, held, 0.0)
    count_own[...] = jnp.zeros_like(count_own)
    count_own[:micro] = counts
    greet(ep, dp, ne, nd)
    leave(0)
    line.step(0, 0)
    own_copies[3].start()

    x = tokens_ref[...].astype(F32)
    rounded = (x * rms_scale(x) * gain_ref[...]).astype(BF16)
    normed = rounded
    loads[0].wait()
    cosine, sine = (repeated(tables_ref[i], x.shape[0]) for i in range(2))
    tile = 256
    steps = (
        (wk, key_own, True, 1),
        (wv, value_own, False, 2),
        (wq, q_ref, True, None),
    )
    for copy, (w, out, turned, array) in zip(loads[1:], steps):
        copy.wait()
        for c in range(0, w.shape[1], tile):
            y = dot(normed, w[:, c : c + tile])
            if turned:
                for i in range(0, tile, 128):
                    out[:, c + i : c + i + 128] = turn(y[:, i : i + 128], cosine, sine).astype(BF16)
            else:
                out[:, c : c + tile] = y.astype(BF16)
        if array is not None:
            leave(array)
    n_ref[...] = rounded.astype(F32).T.astype(BF16)
    hops = iter(range(1, ne))
    for t in range(bit_count(nd)):
        for each in gathers:
            each.step(t, 0, 1)
        for s in hops:
            line.step(0, s)
            break
        for each in gathers:
            each.step(t, 1)
    for s in hops:
        line.step(0, s)
    for copy in own_copies:
        copy.wait()
    totals = jnp.sum(count_all[...], axis=0)
    padded = jnp.concatenate([segments, jnp.zeros((8 - micro, rows), jnp.int32)], axis=0)
    column = padded.astype(F32).T
    ids = lax.broadcasted_iota(jnp.int32, (rows, totals.shape[1]), 1).astype(F32)
    for m in range(micro):
        lower = jnp.where(ids < column[:, m : m + 1], totals[m : m + 1], 0.0)
        starts_ref[m * rows : (m + 1) * rows] = jnp.sum(lower, axis=1, keepdims=True).astype(
            jnp.int32
        )
    for each in gathers:
        each.wait_sends()
    line.wait_sends(0)


def project(
    tokens, gain, segments, tables, w_query, w_key, w_value, cot, early, ne, nd, collective
):
    rows, width = tokens.shape
    micro, count = segments.shape
    keys = jax.ShapeDtypeStruct((nd, rows, w_key.shape[1]), BF16)
    return pl.pallas_call(
        functools.partial(project_body, ne, nd),
        out_shape=[
            jax.ShapeDtypeStruct((width, rows), BF16),
            jax.ShapeDtypeStruct((rows, w_query.shape[1]), BF16),
            jax.ShapeDtypeStruct((2, count, tables.shape[2]), F32),
            jax.ShapeDtypeStruct((rows, 1), jnp.int32),
            keys,
            keys,
            jax.ShapeDtypeStruct((ne, 1, early, width), BF16),
        ],
        in_specs=[VMEM] * 3 + [ANY] * 5,
        out_specs=[VMEM] * 4 + [ANY] * 3,
        scratch_shapes=[pltpu.VMEM(w.shape, BF16) for w in (w_query, w_key, w_value)]
        + [pltpu.VMEM(keys.shape[1:], BF16)] * 2
        + [pltpu.VMEM((8, 128), F32), pltpu.VMEM((nd, 8, 128), F32)]
        + [DMA((4,)), DMA((4,)), DMA((3, nd - 1)), DMA((3, nd - 1))]
        + [DMA((1, 2, ne - 1)), DMA((1, 2, ne - 1))],
        compiler_params=pltpu.CompilerParams(
            vmem_limit_bytes=60 * 2**20, collective_id=collective, has_side_effects=True
        ),
        cost_estimate=cost(26),
    )(tokens, gain, segments, tables, w_query, w_key, w_value, cot)


def spread(x):
    lane = lax.broadcasted_iota(jnp.int32, (x.shape[0], 128), 1)
    low = lane < HEAD_DIM
    zero = jnp.zeros((), x.dtype)
    first, second = x[:, :128], x[:, 128:]
    return jnp.concatenate(
        [
            jnp.where(low, first, zero),
            jnp.where(low, pltpu.roll(first, HEAD_DIM, 1), zero),
            jnp.where(low, zero, pltpu.roll(second, HEAD_DIM, 1)),
            jnp.where(low, zero, second),
        ],
        axis=0,
    )


def gathered(x, rows):
    lane = lax.broadcasted_iota(jnp.int32, (rows, 128), 1)
    low = lane < HEAD_DIM
    h = [x[i * rows : (i + 1) * rows] for i in range(4)]
    return jnp.concatenate(
        [
            jnp.where(low, h[0], pltpu.roll(h[1], HEAD_DIM, 1)),
            jnp.where(low, pltpu.roll(h[2], HEAD_DIM, 1), h[3]),
        ],
        axis=1,
    )


def window_of(dp, span):
    return jnp.maximum(dp - (span - 1), 0)


def window_scores(dp, span, rows, starts_ref, q, k):
    keys = k.shape[0]
    scores = dot(q, k, ((1,), (1,))).reshape(4, rows, keys)
    key_pos = window_of(dp, span) * rows + lax.broadcasted_iota(jnp.int32, (rows, keys), 1)
    query_pos = dp * rows + lax.broadcasted_iota(jnp.int32, (rows, keys), 0)
    allowed = (key_pos <= query_pos) & (key_pos >= starts_ref[...])
    return jnp.where(allowed[None], scores, MASKED).reshape(4 * rows, keys)


def in_window(ref, dp, span):
    block = ref[pl.ds(window_of(dp, span), span)]
    return block.reshape(span * block.shape[1], block.shape[2])


SCALE = HEAD_DIM ** (-0.5)


class LineGather:
    def __init__(self, ep, ne, own, whole, send_sem, recv_sem):
        self.ep, self.ne, self.own, self.whole = ep, ne, own, whole
        self.send_sem, self.recv_sem = send_sem, recv_sem

    def copy(self, m, s, way):
        shard = lax.rem(self.ep - way * s + self.ne, self.ne)
        k = 0 if way == 1 else 1
        return remote(
            self.own.at[m] if s == 0 else self.whole.at[shard, m],
            self.whole.at[shard, m],
            self.send_sem.at[m, k, s],
            self.recv_sem.at[m, k, s],
            {"ep": lax.rem(self.ep + way + self.ne, self.ne)},
        )

    def sends(self, s, way):
        ep, ne = self.ep, self.ne
        return (ep >= s) & (ep < ne - 1) if way == 1 else (ep + s <= ne - 1) & (ep >= 1)

    def receives(self, s, way):
        return self.ep >= 1 + s if way == 1 else self.ep + 1 + s <= self.ne - 1

    def step(self, m, s):
        for way in (1, -1):
            if s > 0:

                @pl.when(self.receives(s - 1, way))
                def _(way=way):
                    self.copy(m, s - 1, way).wait_recv()

            if s < self.ne - 1:

                @pl.when(self.sends(s, way))
                def _(way=way):
                    self.copy(m, s, way).start()

    def wait_sends(self, m):
        for s in range(self.ne - 1):
            for way in (1, -1):

                @pl.when(self.sends(s, way))
                def _(s=s, way=way):
                    self.copy(m, s, way).wait_send()


def attend_body(span, ne, nd, micro, *refs):
    starts_ref, q_ref, k_ref, v_ref, tokens_ref, wo_ref, gain_ref, router_ref, hit_ref = refs[:9]
    cot_ref = refs[9]
    out_ref, log_ref, res_ref, normed_ref, probs_ref, normed_all, marked_all, cot_all = refs[10:18]
    attn, normed_own, marked_own, own_sem, send_sem, recv_sem, cot_sem, cot_send, cot_recv = refs[18:]
    ep, dp = lax.axis_index("ep"), lax.axis_index("dp")
    m, h = pl.program_id(0), pl.program_id(1)
    final = pl.num_programs(1) - 1
    final_step = micro * (KV_HEADS // 2) - 1
    rows = q_ref.shape[0]
    lines = [
        LineGather(ep, ne, own, whole, send_sem.at[i], recv_sem.at[i])
        for i, (own, whole) in enumerate(((normed_own, normed_all), (marked_own, marked_all)))
    ]

    def hop(batch, s):
        for line in lines:
            line.step(batch, s)

    count = cot_all.shape[2]
    cot_own = cot_ref.at[:, pl.ds(cot_ref.shape[1] - count, count)]
    cot_line = LineGather(ep, ne, cot_own, cot_all, cot_send, cot_recv)
    cot_copy = pltpu.make_async_copy(cot_own.at[0], cot_all.at[ep, 0], cot_sem)

    @pl.when((m == 0) & (h == 0))
    def _():
        greet(ep, dp, ne, nd)
        cot_line.step(0, 0)
        cot_copy.start()

    for s in range(1, ne):
        at = min(1 + 2 * s, final_step)

        @pl.when(m * pl.num_programs(1) + h == at)
        def _(s=s):
            cot_line.step(0, s)

    q = spread(q_ref[...].astype(F32) * SCALE).astype(BF16)
    scores = window_scores(dp, span, rows, starts_ref, q, in_window(k_ref, dp, span))
    top = jnp.max(scores, axis=1, keepdims=True)
    terms = jnp.exp(scores - top)
    total = jnp.sum(terms, axis=1, keepdims=True)
    log_ref[0, 0] = top + jnp.log(total)
    weights = (terms * (1.0 / total)).astype(BF16)
    out = gathered(dot(weights, in_window(v_ref, dp, span)), rows).astype(BF16)
    out_ref[...] = out
    attn[:, pl.ds(pl.multiple_of(h * out.shape[1], out.shape[1]), out.shape[1])] = out

    def own_copies(batch):
        return [
            pltpu.make_async_copy(line.own.at[batch], line.whole.at[ep, batch], own_sem.at[i, batch])
            for i, line in enumerate(lines)
        ]

    for batch in range(micro):

        @pl.when((m == batch) & (h == final))
        def _(batch=batch):
            for earlier in range(batch):
                hop(earlier, batch - earlier)
            residual = tokens_ref[...].astype(F32) + dot(attn[...], wo_ref[...])
            res_ref[...] = residual
            normed = (residual * rms_scale(residual) * gain_ref[...]).astype(BF16)
            normed_ref[...] = normed
            normed_own[batch] = normed
            hit = hit_ref[...] > 0.0
            logits = jnp.where(hit, dot(router_ref[...], normed, ((1,), (1,))), MASKED)
            terms = jnp.exp(logits - jnp.max(logits, axis=0, keepdims=True))
            terms = jnp.where(hit, terms, 0.0)
            probs = terms / jnp.sum(terms, axis=0, keepdims=True)
            probs_ref[...] = probs
            marked_own[batch] = jnp.where(hit, probs, -1.0)
            hop(batch, 0)
            for copy in own_copies(batch):
                copy.start()
            if batch == micro - 1:
                for t in range(1, ne + micro - 1):
                    for each in range(micro):
                        s = t + micro - 1 - each
                        if s < ne:
                            hop(each, s)
                for each in range(micro):
                    for line in lines:
                        line.wait_sends(each)
                    for copy in own_copies(each):
                        copy.wait()
                cot_line.wait_sends(0)
                cot_copy.wait()


def attention_specs(micro, rows, nd):
    pairs = KV_HEADS // 2
    mine = pl.BlockSpec((rows, 4 * HEAD_DIM), lambda m, h, *_: (m, h))
    theirs = pl.BlockSpec((nd, rows, 2 * HEAD_DIM), lambda m, h, *_: (0, m, h))
    column = pl.BlockSpec((rows, 1), lambda m, h, *_: (m, 0))
    logs = pl.BlockSpec((1, 1, 4 * rows, 1), lambda m, h, *_: (m, h, 0, 0))
    log_shape = jax.ShapeDtypeStruct((micro, pairs, 4 * rows, 1), F32)
    return (micro, pairs), mine, theirs, column, logs, log_shape


def attend(
    starts, queries, keys, values, tokens, w_out, gain, router, hit, cot, late, micro, rows, ne, collective
):
    nd, width = keys.shape[0], tokens.shape[1]
    grid, mine, theirs, column, logs, log_shape = attention_specs(micro, rows, nd)
    one = pl.Buffered(1)
    whole = lambda v: pl.BlockSpec(v.shape, lambda m, h: (0, 0), pipeline_mode=one)
    wide = pl.BlockSpec((rows, width), lambda m, h: (m, 0))
    chosen = pl.BlockSpec((hit.shape[0], rows), lambda m, h: (0, m))
    every = micro * rows
    return pl.pallas_call(
        functools.partial(attend_body, nd // 2 + 1, ne, nd, micro),
        grid=grid,
        in_specs=[column, mine, theirs, theirs, wide, whole(w_out), whole(gain), whole(router)]
        + [chosen, ANY],
        out_specs=[mine, logs, wide, wide, chosen, ANY, ANY, ANY],
        out_shape=[
            jax.ShapeDtypeStruct(queries.shape, BF16),
            log_shape,
            jax.ShapeDtypeStruct((every, width), F32),
            jax.ShapeDtypeStruct((every, width), BF16),
            jax.ShapeDtypeStruct(hit.shape, F32),
            jax.ShapeDtypeStruct((ne, micro, rows, width), BF16),
            jax.ShapeDtypeStruct((ne, micro, hit.shape[0], rows), F32),
            jax.ShapeDtypeStruct((ne, 1, late, width), BF16),
        ],
        scratch_shapes=[
            pltpu.VMEM((rows, width), BF16),
            pltpu.VMEM((micro, rows, width), BF16),
            pltpu.VMEM((micro, hit.shape[0], rows), F32),
            DMA((2, micro)),
            DMA((2, micro, 2, ne - 1)),
            DMA((2, micro, 2, ne - 1)),
            DMA,
            DMA((1, 2, ne - 1)),
            DMA((1, 2, ne - 1)),
        ],
        compiler_params=pltpu.CompilerParams(
            vmem_limit_bytes=60 * 2**20, collective_id=collective, has_side_effects=True
        ),
        cost_estimate=cost(50),
    )(starts, queries, keys, values, tokens, w_out, gain, router, hit, cot)


def attend_back_body(span, ne, nd, micro, skip, full, orders, *refs):
    refs = list(refs)

    def take(n):
        return [refs.pop(0) for _ in range(n)]

    starts_ref, q_ref, k_ref, v_ref, log_ref, tables_ref = take(6)
    cot_ref, dots_ref, probs_ref, grad_ref, residual_ref, gain_ref, normed_ref, attn_ref = take(8)
    wo_ref, router_ref, mix_ref = take(3)
    n = len(orders)
    sources, extras = take(n), take(n)
    dq_ref, res_out, wo_out, router_out, gain_out, dk_out, dv_out, mix_out = take(8)
    outs = take(n)
    grads, mix_held, mix_in = take(3)
    kv_held, kv_in = take(2), take(2)
    held, more, landing = take(n), take(n), take(n)
    load_sem, out_sem, send_sem, recv_sem, kv_send, kv_recv, kv_out, mix_sem, line_send, line_recv = refs
    ep, dp = lax.axis_index("ep"), lax.axis_index("dp")
    step = pl.program_id(0) * pl.num_programs(1) + pl.program_id(1)
    final = pl.num_programs(0) * pl.num_programs(1) - 1
    sums = []
    for a in range(n):
        part = pl.ds(skip, sources[a].shape[1] - skip)
        loads = [
            pltpu.make_async_copy(src.at[:, part], dst, load_sem.at[a, i])
            for i, (src, dst) in enumerate(((sources[a], held[a]), (extras[a], more[a])))
        ]
        sums.append(
            PairSum(
                dp, orders[a], loads, held[a], more[a], landing[a], send_sem.at[a], recv_sem.at[a]
            )
        )
    batch_sums = [
        [
            PairSum(
                dp,
                full[i],
                [],
                kv_held[i].at[m],
                None,
                kv_in[i].at[m],
                kv_send.at[i, m],
                kv_recv.at[i, m],
            )
            for i in range(2)
        ]
        for m in range(micro)
    ]
    lines = [
        LineSum(ep, ne, mix_held.at[m], mix_in.at[m], line_send.at[m], line_recv.at[m])
        for m in range(micro)
    ]
    count = q_ref.shape[0]
    line_loads = [
        pltpu.make_async_copy(
            mix_ref.at[:, pl.ds(m * count, count)], mix_held.at[m], mix_sem.at[0, m]
        )
        for m in range(micro)
    ]
    turns = bit_count(nd)

    def batch_step(m, t):
        if t <= turns:
            for each in batch_sums[m]:
                each.step(t)

    def line_step(m, t):
        if t < ne:
            lines[m].step(t)

    @pl.when(step == 0)
    def _():
        for copy in line_loads:
            copy.start()
        for each in sums:
            each.load()
        greet(ep, dp, ne, nd)
        for m in range(micro):
            line_loads[m].wait()
            line_step(m, 0)
        for each in sums:
            each.step(0)
        for i in range(2):
            kv_held[i][...] = jnp.zeros_like(kv_held[i])
        rows = q_ref.shape[0]
        pairs = [dots_ref[:, :, m, :].reshape(-1, rows) for m in range(micro)]
        pair = jnp.concatenate(pairs, axis=1)
        probs = probs_ref[...]
        grad_logits = probs * (pair - jnp.sum(probs * pair, axis=0, keepdims=True))
        high = grad_logits.astype(BF16)
        low = (grad_logits - high.astype(F32)).astype(BF16)
        normed = normed_ref[...]
        router_out[...] = dot(high, normed) + dot(low, normed)
        router = router_ref[...]
        grad_normed = (
            grad_ref[...].astype(F32)
            + dot(high, router, ((0,), (0,)))
            + dot(low, router, ((0,), (0,)))
        )
        residual = residual_ref[...]
        r = rms_scale(residual)
        gain_out[...] = jnp.sum(grad_normed * residual * r, axis=0, keepdims=True)
        scaled = grad_normed * gain_ref[...]
        mean = jnp.mean(scaled * residual, axis=1, keepdims=True)
        grad_residual = cot_ref[...].astype(F32) + r * scaled - residual * (r * r * r) * mean
        res_out[...] = grad_residual
        low_res = grad_residual.astype(BF16)
        tile = 256
        for c in range(0, wo_ref.shape[1], tile):
            y = dot(attn_ref[...], low_res[:, c : c + tile], ((0,), (0,))).astype(BF16)
            a, at = c // wo_out.shape[4], c % wo_out.shape[4]
            share = wo_out.shape[3]
            for e in range(ne):
                for d in range(nd):
                    i = (e * nd + d) * share
                    slot = slot_of(full[a % 2], d)
                    wo_out[a, slot, e, :, at : at + tile] = y[i : i + share]
        for c in range(0, wo_ref.shape[0], tile):
            grads[c // tile] = dot(low_res, wo_ref[c : c + tile, :], ((1,), (1,))).astype(BF16)

    rows = q_ref.shape[0]
    q = spread(q_ref[...].astype(F32) * SCALE).astype(BF16)
    mine = pl.ds(pl.multiple_of(pl.program_id(0) * rows, rows), rows)
    g = spread(grads[pl.program_id(1), mine, :].astype(F32)).astype(BF16)
    k, v = in_window(k_ref, dp, span), in_window(v_ref, dp, span)
    scores = window_scores(dp, span, rows, starts_ref, q, k)
    probs = jnp.exp(scores - log_ref[0, 0])
    grad_probs = dot(g, v, ((1,), (1,)))
    total = jnp.sum(probs * grad_probs, axis=1, keepdims=True)
    grad_scores = (probs * (grad_probs - total)).astype(BF16)
    dq = gathered(dot(grad_scores, k) * SCALE, rows)
    cosine, sine = tables_ref[0], -tables_ref[1]
    for i in range(0, dq.shape[1], 128):
        dq_ref[:, i : i + 128] = turn(dq[:, i : i + 128], cosine, sine).astype(BF16)
    here = pl.ds(window_of(dp, span), span)
    head = pl.program_id(1)
    at = pl.ds(pl.multiple_of(head * 2 * HEAD_DIM, 2 * HEAD_DIM), 2 * HEAD_DIM)
    batch = pl.program_id(0)
    dk = dot(grad_scores, q, ((0,), (0,))).astype(BF16)
    kv_held[0][batch, here, :, at] = dk.reshape(span, rows, dk.shape[1])
    dv = dot(probs.astype(BF16), g, ((0,), (0,))).astype(BF16)
    kv_held[1][batch, here, :, at] = dv.reshape(span, rows, dv.shape[1])

    heads = pl.num_programs(1)
    for m in range(micro):

        @pl.when((batch == m) & (head == heads - 1))
        def _(m=m):
            batch_step(m, 0)

        if m > 0:

            @pl.when((batch == m) & (head == 0))
            def _(m=m):
                batch_step(m - 1, 1)

    @pl.when(step == final // 4 + 1)
    def _():
        line_step(0, 1)

    @pl.when(step == final // 2 + 2)
    def _():
        line_step(1, 1)

    @pl.when(step == final)
    def _():
        copies = []

        def leave(copy):
            copy.start()
            copies.append(copy)

        line_step(0, 2)
        last = micro - 1
        batch_step(last - 1, 2)
        for t in range(1, max([len(order) for order in orders] + [0]) + 1):
            for each in sums:
                each.step(t)
        for a, each in enumerate(sums):
            leave(pltpu.make_async_copy(each.own(), outs[a], out_sem.at[a]))
        batch_step(last, 1)
        line_step(1, 2)
        for t in range(3, turns + 1):
            batch_step(last - 1, t)
        batch_step(last, 2)
        for t in range(3, ne):
            line_step(0, t)
            line_step(1, t)
        for t in range(3, turns + 1):
            batch_step(last, t)
        for m in range(micro):
            own = pl.ds(m * rows, rows)
            for i, out in enumerate((dk_out, dv_out)):
                leave(pltpu.make_async_copy(batch_sums[m][i].own(), out.at[own], kv_out.at[i, m]))
            leave(pltpu.make_async_copy(lines[m].own(), mix_out.at[own], mix_sem.at[1, m]))
        for each in sums + lines + sum(batch_sums, []):
            each.wait_sends()
        for copy in copies:
            copy.wait()


def attend_back(
    starts,
    queries,
    keys,
    values,
    logs_in,
    tables,
    cot,
    dots,
    probs,
    grad_normed,
    residual,
    gain,
    normed,
    attn,
    w_out,
    router,
    mix,
    sums,
    full,
    skip,
    collective,
):
    nd, ne, micro, rows = keys.shape[0], dots.shape[0], dots.shape[2], dots.shape[3]
    every, width = residual.shape
    grid, mine, theirs, column, logs, _ = attention_specs(micro, rows, nd)
    one = pl.Buffered(1)
    whole = lambda v: pl.BlockSpec(v.shape, lambda m, h: (0,) * len(v.shape), pipeline_mode=one)
    n = len(sums)
    shapes = [(v.shape[0], v.shape[1] - skip) + v.shape[2:] for v, _, _ in sums]
    deep = max([s[0] - 1 for s in shapes] + [1])
    some = max(n, 1)
    kv_width = keys.shape[2]
    wo_shape = (width // kv_width, nd, ne, w_out.shape[0] // (ne * nd), kv_width)
    before = [cot, dots, probs, grad_normed, residual, gain, normed, attn, w_out, router]
    after = [
        jax.ShapeDtypeStruct((every, width), F32),
        jax.ShapeDtypeStruct(wo_shape, BF16),
        jax.ShapeDtypeStruct(router.shape, F32),
        jax.ShapeDtypeStruct((1, width), F32),
    ]
    tile = 4 * HEAD_DIM
    return pl.pallas_call(
        functools.partial(
            attend_back_body,
            nd // 2 + 1,
            ne,
            nd,
            micro,
            skip,
            tuple(map(tuple, full)),
            tuple(tuple(order) for _, order, _ in sums),
        ),
        grid=grid,
        in_specs=[column, mine, theirs, theirs, logs, whole(tables)]
        + [whole(v) for v in before]
        + [ANY] * (2 * n + 1),
        out_specs=[mine] + [whole(v) for v in after] + [ANY] * (n + 3),
        out_shape=[jax.ShapeDtypeStruct(queries.shape, BF16)]
        + after
        + [jax.ShapeDtypeStruct((every, keys.shape[2]), BF16)] * 2
        + [jax.ShapeDtypeStruct((every, width), BF16)]
        + [jax.ShapeDtypeStruct(s[1:], BF16) for s in shapes],
        scratch_shapes=[
            pltpu.VMEM((w_out.shape[0] // tile, every, tile), BF16),
            pltpu.VMEM((micro, ne, rows, width), BF16),
            pltpu.VMEM((micro, 2, ne, rows, width), BF16),
        ]
        + [pltpu.VMEM((micro, nd, rows, keys.shape[2]), BF16)] * 2
        + [pltpu.VMEM((micro, nd - 1, rows, keys.shape[2]), BF16)] * 2
        + [pltpu.VMEM(s, BF16) for s in shapes] * 2
        + [pltpu.VMEM((s[0] - 1,) + s[1:], BF16) for s in shapes]
        + [
            DMA((some, 2)),
            DMA((some,)),
            DMA((some, deep)),
            DMA((some, deep)),
            DMA((2, micro, nd - 1)),
            DMA((2, micro, nd - 1)),
            DMA((2, micro)),
            DMA((2, micro)),
            DMA((micro, 2, ne)),
            DMA((micro, 2, ne)),
        ],
        compiler_params=pltpu.CompilerParams(
            vmem_limit_bytes=63 * 2**20, collective_id=collective, has_side_effects=True
        ),
        cost_estimate=cost(40),
    )(
        starts,
        queries,
        keys,
        values,
        logs_in,
        tables,
        *before,
        mix,
        *[v for v, _, _ in sums],
        *[extra for _, _, extra in sums],
    )


def finish_body(ne, nd, orders, n_out, *refs):
    refs = list(refs)

    def take(n):
        return [refs.pop(0) for _ in range(n)]

    n_ref, dq_ref, dk_ref, dv_ref, tables_ref, tokens_ref, gain_ref, router_ref, gain_two = take(9)
    res_ref, wq_ref, wk_ref, wv_ref, wo_ref = take(5)
    (tok_out,) = take(1)
    count = 2 * n_out + 3
    outs, held, pair_in, line_in = take(count), take(count), take(count), take(count)
    dk_turned, wq, wk, wv, res = take(5)
    load_sem, own_sem, out_sem, dp_send, dp_recv, ep_send, ep_recv = refs
    ep, dp = lax.axis_index("ep"), lax.axis_index("dp")
    columns = held[0].shape[3]
    own = [
        pltpu.make_async_copy(src, dst, own_sem.at[i])
        for i, (src, dst) in enumerate(
            ((wq_ref, wq), (wk_ref, wk), (wv_ref, wv), (res_ref, res))
        )
    ]
    sums = []
    for a in range(count):
        loads = []
        if a < n_out:
            loads = [pltpu.make_async_copy(wo_ref.at[a], held[a], load_sem.at[a])]
        sums.append(
            PairSum(
                dp,
                orders[a % 2],
                loads,
                held[a],
                None,
                pair_in[a],
                dp_send.at[a],
                dp_recv.at[a],
                major=True,
            )
        )
    spreads = [
        SpreadSum(ep, ne, sums[a].own(), line_in[a], ep_send.at[a], ep_recv.at[a])
        for a in range(count)
    ]
    early, made, small = sums[:n_out], sums[n_out:-1], sums[-1]
    queries, others = made[:n_out], made[n_out:]
    for each in early:
        each.load()
    for copy in own:
        copy.start()
    greet(ep, dp, ne, nd)
    turns = bit_count(nd)

    def steps(group, t):
        for each in group:
            if t <= turns:
                each.step(t)

    def spread_steps(group, t):
        for each in group:
            spreads[sums.index(each)].step(t)

    steps(early, 0)

    normed = n_ref[...]
    cosine, sine = (repeated(tables_ref[i], normed.shape[1]) for i in range(2))
    sine = -sine
    for i in range(0, dk_ref.shape[1], 128):
        part = dk_ref[:, i : i + 128].astype(F32)
        dk_turned[:, i : i + 128] = turn(part, cosine, sine).astype(BF16)
    tile = 256

    def product(grad, first, each):
        share = each.held.shape[2]
        for c in range(0, each.held.shape[3], tile):
            y = dot(normed, grad[:, first + c : first + c + tile]).astype(BF16)
            for e in range(ne):
                for d in range(nd):
                    r = (e * nd + d) * share
                    each.held[slot_of(each.order, d), e, :, c : c + tile] = y[r : r + share]
        each.step(0)

    for i, each in enumerate(made):
        if i < n_out:
            product(dq_ref, i * columns, each)
        else:
            product((dk_turned, dv_ref)[i - n_out], 0, each)
        if i == 0:
            steps(early, 1)
        if i == 2:
            steps(queries, 1)
    for copy in own:
        copy.wait()
    back = dot(dq_ref[...], wq[...], ((1,), (1,)))
    steps(early, 2)
    steps(others, 1)
    back = back + dot(dk_turned[...], wk[...], ((1,), (1,)))
    back = back + dot(dv_ref[...], wv[...], ((1,), (1,)))
    x = tokens_ref[...].astype(F32)
    r = rms_scale(x)
    scaled = back * gain_ref[...]
    tok_out[...] = (
        res[...] + r * scaled - x * (r * r * r) * jnp.mean(scaled * x, axis=1, keepdims=True)
    )
    for t in range(3, turns + 1):
        steps(early, t)
    spread_steps(early, 0)
    one_row = jnp.sum(back * x * r, axis=0, keepdims=True)
    blank = jnp.zeros((held[-1].shape[3] - EXPERTS - 2, x.shape[1]), F32)
    column = jnp.concatenate([router_ref[...], one_row, gain_two[...], blank], axis=0).T
    share = held[-1].shape[2]
    for e in range(ne):
        for d in range(nd):
            i = (e * nd + d) * share
            held[-1][slot_of(small.order, d), e] = column[i : i + share].astype(BF16)
    steps([small], 0)
    steps(queries, 2)
    steps([small], 1)
    for t in range(3, turns + 1):
        steps(queries, t)
    spread_steps(queries, 0)
    steps(others + [small], 2)
    for t in range(3, turns + 1):
        steps(others + [small], t)
    spread_steps(others + [small], 0)
    spread_steps(early, 1)
    spread_steps(queries, 1)
    spread_steps(others + [small], 1)
    copies = []
    for a in range(count):
        copies.append(pltpu.make_async_copy(spreads[a].own(), outs[a], out_sem.at[a]))
        copies[-1].start()
    for each in sums + spreads:
        each.wait_sends()
    for copy in copies:
        copy.wait()


def finish(
    ne,
    nd,
    orders,
    normed,
    grads,
    tables,
    tokens,
    gain,
    grad_residual,
    weights,
    w_out,
    router_grad,
    gain_two_grad,
):
    rows, width = tokens.shape
    share = width // (ne * nd)
    columns = weights[1].shape[1]
    n_out = width // columns
    count = 2 * n_out + 3
    wide = [columns] * (count - 1) + [128]
    return pl.pallas_call(
        functools.partial(finish_body, ne, nd, tuple(map(tuple, orders)), n_out),
        out_shape=[jax.ShapeDtypeStruct((rows, width), F32)]
        + [jax.ShapeDtypeStruct((share, c), BF16) for c in wide],
        in_specs=[VMEM] * 9 + [ANY] * 5,
        out_specs=[VMEM] + [ANY] * count,
        scratch_shapes=[pltpu.VMEM((nd, ne, share, c), BF16) for c in wide]
        + [pltpu.VMEM((nd - 1, ne, share, c), BF16) for c in wide]
        + [pltpu.VMEM((ne - 1, share, c), BF16) for c in wide]
        + [pltpu.VMEM(grads[1].shape, BF16)]
        + [pltpu.VMEM(w.shape, BF16) for w in weights]
        + [pltpu.VMEM((rows, width), F32)]
        + [
            DMA((count,)),
            DMA((4,)),
            DMA((count,)),
            DMA((count, bit_count(nd))),
            DMA((count, bit_count(nd))),
            DMA((count, ne - 1)),
            DMA((count, ne - 1)),
        ],
        compiler_params=pltpu.CompilerParams(
            vmem_limit_bytes=60 * 2**20, collective_id=4, has_side_effects=True
        ),
        cost_estimate=cost(45),
    )(
        normed,
        *grads,
        tables,
        tokens,
        gain,
        router_grad,
        gain_two_grad,
        grad_residual,
        *weights,
        w_out,
    )


def results_body(share, n_out, groups, *refs):
    refs = list(refs)

    def take(n):
        return [refs.pop(0) for _ in range(n)]

    residual_ref, mix_ref = take(2)
    halves = [take(groups) for _ in range(2)]
    dense = take(2 * n_out + 3)
    out_ref, d_out, d_query, d_key, d_value, router, gain_one, gain_two = take(8)
    gate, up, down = refs
    e = pl.program_id(0)

    @pl.when(e == 0)
    def _():
        out_ref[...] = (residual_ref[...] + mix_ref[...].astype(F32)).astype(BF16)
        width = dense[0].shape[1]
        for i in range(n_out):
            d_out[:, i * width : (i + 1) * width] = dense[i][...].astype(F32)
            d_query[:, i * width : (i + 1) * width] = dense[n_out + i][...].astype(F32)
        d_key[...] = dense[2 * n_out][...].astype(F32)
        d_value[...] = dense[2 * n_out + 1][...].astype(F32)
        small = dense[-1][...].astype(F32)
        router[...] = small[:, :EXPERTS]
        turned = small.T
        gain_one[...] = turned[EXPERTS : EXPERTS + 1]
        gain_two[...] = turned[EXPERTS + 1 : EXPERTS + 2]

    k = 0
    for first, second in zip(*halves):
        for m in range(first.shape[0]):

            @pl.when(e == k)
            def _(first=first, second=second, m=m):
                over = first.shape[1] - share
                gate[0] = first[m, :share].astype(F32)
                up[0, :over] = first[m, share:].astype(F32)
                up[0, over:] = second[m, : share - over].astype(F32)
                piece, columns = down.shape[1], second.shape[2]
                for j in range(down.shape[2] // columns):
                    at = share - over + j * piece
                    down[0, :, j * columns : (j + 1) * columns] = second[
                        m, at : at + piece
                    ].astype(F32)

            k += 1


def results(residual, mix, grads, dense, n_out, share, w_gate, w_down, nd, rows_share):
    rows, width = residual.shape
    n_exp, _, inner = w_gate.shape
    piece = w_down.shape[1] // nd
    ins = [residual, *mix, *grads[0], *grads[1], *dense]
    kv = dense[-2].shape[1]
    same = lambda v: pl.BlockSpec(v, lambda e: (0,) * len(v))
    outs = [
        ((rows, width), BF16),
        ((rows_share, width), F32),
        ((rows_share, width), F32),
        ((rows_share, kv), F32),
        ((rows_share, kv), F32),
        ((rows_share, EXPERTS), F32),
        ((1, rows_share), F32),
        ((1, rows_share), F32),
    ]
    experts_out = [((n_exp, share, inner), F32)] * 2 + [((n_exp, piece, width), F32)]
    return pl.pallas_call(
        functools.partial(results_body, share, n_out, len(grads[0])),
        grid=(n_exp,),
        out_shape=[jax.ShapeDtypeStruct(*v) for v in outs + experts_out],
        in_specs=[same(v.shape) for v in ins],
        out_specs=[same(v[0]) for v in outs]
        + [pl.BlockSpec((1,) + v[0][1:], lambda e: (e, 0, 0)) for v in experts_out],
        compiler_params=pltpu.CompilerParams(vmem_limit_bytes=60 * 2**20),
        cost_estimate=cost(6),
    )(*ins)


def per_device(
    tokens,
    segments,
    routes,
    first_gain,
    w_query,
    w_key,
    w_value,
    w_out,
    second_gain,
    w_router,
    w_gate,
    w_up,
    w_down,
    cotangent,
):
    micro, rows, width = tokens.shape
    ne, nd = lax.axis_size("ep"), lax.axis_size("dp")
    kv_width = KV_HEADS * HEAD_DIM
    every = micro * rows

    halfway = HEAD_DIM // 2
    frequency = ROPE_BASE ** (-(np.arange(halfway) * 2.0 / HEAD_DIM))
    angles = np.arange(nd * rows)[:, None] * frequency[None, :]
    lanes = 2 * HEAD_DIM // halfway
    sign = np.where(np.arange(2 * HEAD_DIM) % HEAD_DIM < halfway, -1.0, 1.0)
    tables = np.stack([np.tile(np.cos(angles), lanes), np.tile(np.sin(angles), lanes) * sign])
    tokens_flat = tokens.reshape(every, width)
    gain_one = first_gain.reshape(1, width)
    cot_own = cotangent.reshape(every, width)
    late = rows // 4
    normed_one, query_rot, tables, starts, key_all, value_all, cot_first = project(
        tokens_flat,
        gain_one,
        segments.reshape(micro, rows),
        jnp.asarray(tables, F32),
        w_query,
        w_key,
        w_value,
        cot_own[None],
        every - late,
        ne,
        nd,
        0,
    )
    routing = routes.reshape(every, routes.shape[2])
    hit = jnp.any(
        jnp.arange(EXPERTS, dtype=jnp.int32)[:, None, None] == routing[None], axis=2
    ).astype(F32)
    router = w_router.T
    attn_low, logs, residual, normed_two, gate_probs, normed_all, marked_all, cot_last = attend(
        starts,
        query_rot,
        key_all,
        value_all,
        tokens_flat,
        w_out,
        second_gain.reshape(1, width),
        router,
        hit,
        cot_own[None],
        late,
        micro,
        rows,
        ne,
        1,
    )
    orders = [order[:-1][::-1] for order in gather_orders(nd)]
    mix, grad_in, pair_dots, *grads = experts(
        normed_all.reshape(ne * every, width),
        [cot.reshape(ne, -1, width) for cot in (cot_first, cot_last)],
        marked_all.reshape(ne * micro, EXPERTS, rows),
        w_gate,
        w_up,
        w_down,
        micro,
        rows,
        ne,
        nd,
        6,
    )
    kept, landed, last = grads[:2], grads[2:4], grads[4:]
    height = kept[0].shape[2]
    halves = [(slice(None), slice(i * height, (i + 1) * height)) for i in range(2)]
    skip = min(2, kept[0].shape[1])
    more = kept[0].shape[1] > skip
    head = (slice(None), slice(0, skip))
    *grads, grad_back, dots_all = reduce(
        ne,
        nd,
        [(last[k], orders[i], halves[i], None, False) for k in range(2) for i in range(2)]
        + [(kept[i], orders[i][1:], head, landed[i], False) for i in range(2)],
        ((grad_in.reshape(ne, every, width), None),),
        (pair_dots,),
        2,
        40,
    )
    grads_last, grads_head = grads[:4], grads[4:]
    mix = mix.reshape(ne, every, width)
    full = [[0] + order for order in orders]
    (
        grad_query,
        grad_residual,
        grad_w_out,
        grad_router,
        grad_gain_two,
        grad_key,
        grad_value,
        mix_own,
        *grads_more,
    ) = attend_back(
        starts,
        query_rot,
        key_all,
        value_all,
        logs,
        tables,
        cot_own,
        dots_all,
        gate_probs,
        grad_back,
        residual,
        second_gain.reshape(1, width),
        normed_two,
        attn_low,
        w_out,
        router,
        mix,
        [(kept[i], orders[i][1:], landed[i]) for i in range(2)] if more else [],
        full,
        skip,
        5,
    )
    grad_tokens, *dense = finish(
        ne,
        nd,
        full,
        normed_one,
        (grad_query, grad_key, grad_value),
        tables,
        tokens_flat,
        gain_one,
        grad_residual,
        (w_query, w_key, w_value),
        grad_w_out,
        grad_router,
        grad_gain_two,
    )
    (
        output,
        d_out,
        d_query,
        d_key,
        d_value,
        d_router,
        d_gain_one,
        d_gain_two,
        d_gate,
        d_up,
        d_down,
    ) = results(
        residual,
        (mix_own,),
        [
            [grads_head[i]]
            + ([grads_more[i]] if more else [])
            + [grads_last[i][None], grads_last[2 + i][None]]
            for i in range(2)
        ],
        dense,
        width // kv_width,
        width // nd,
        w_gate,
        w_down,
        nd,
        width // (ne * nd),
    )
    return (
        output.reshape(tokens.shape),
        grad_tokens.reshape(tokens.shape),
        d_gain_one.reshape(-1),
        d_query,
        d_key,
        d_value,
        d_out,
        d_gain_two.reshape(-1),
        d_router,
        d_gate,
        d_up,
        d_down,
    )


def solution(mesh):
    in_specs = (
        P(None, ("ep", "dp"), None),
        P(None, "ep", "dp"),
        P(None, ("ep", "dp"), None),
        P(),
        P(),
        P(),
        P(),
        P(),
        P(),
        P(),
        P("ep", None, None),
        P("ep", None, None),
        P("ep", None, None),
        P(None, ("ep", "dp"), None),
    )
    out_specs = (
        P(None, ("ep", "dp"), None),
        P(None, ("ep", "dp"), None),
        P(("ep", "dp")),
        P(("ep", "dp"), None),
        P(("ep", "dp"), None),
        P(("ep", "dp"), None),
        P(("ep", "dp"), None),
        P(("ep", "dp")),
        P(("ep", "dp"), None),
        P("ep", "dp", None),
        P("ep", "dp", None),
        P("ep", "dp", None),
    )
    return jax.shard_map(
        per_device, mesh=mesh, in_specs=in_specs, out_specs=out_specs, check_vma=False
    )
```
